32 devices in a mesh: dp: 8 (over z, core), tensor: 4 (over y, x).
Axes of the slice: x: 2, y: 2, z: 4, core: 2. Of those that a mesh axis runs over, the one named last changes fastest.
Arguments:
- tokens: bfloat16 [8192, 2048], P(('dp', 'tensor')), may hold values from -6 to 6
- attn_gain: bfloat16 [2048], P('dp'), may hold values from 0.099609375 to 1.8984375
- query_weight: bfloat16 [2048, 2048], P('dp', 'tensor'), may hold values from -0.1875 to 0.1875
- key_weight: bfloat16 [2048, 2048], P('dp', 'tensor'), may hold values from -0.125 to 0.125
- value_weight: bfloat16 [2048, 2048], P('dp', 'tensor'), may hold values from -0.125 to 0.125
- output_weight: bfloat16 [2048, 2048], P('tensor', 'dp'), may hold values from -0.75 to 0.75
- ffn_gain: bfloat16 [2048], P('dp'), may hold values from 0.099609375 to 1.8984375
- gate_weight: bfloat16 [2048, 8192], P('dp', 'tensor'), may hold values from -0.125 to 0.125
- up_weight: bfloat16 [2048, 8192], P('dp', 'tensor'), may hold values from -0.125 to 0.125
- down_weight: bfloat16 [8192, 2048], P('tensor', 'dp'), may hold values from -0.0625 to 0.0625
- cotangent: bfloat16 [8192, 2048], P(('dp', 'tensor')), may hold values from -6 to 6
Outputs:
- layer_out: bfloat16 [8192, 2048], P(('dp', 'tensor'))
- input_grad: float32 [8192, 2048], P(('dp', 'tensor'))
- attn_gain_grad: float32 [2048], P('dp')
- query_grad: float32 [2048, 2048], P('dp', 'tensor')
- key_grad: float32 [2048, 2048], P('dp', 'tensor')
- value_grad: float32 [2048, 2048], P('dp', 'tensor')
- output_grad: float32 [2048, 2048], P('tensor', 'dp')
- ffn_gain_grad: float32 [2048], P('dp')
- gate_grad: float32 [2048, 8192], P('dp', 'tensor')
- up_grad: float32 [2048, 8192], P('dp', 'tensor')
- down_grad: float32 [8192, 2048], P('tensor', 'dp')
The draws below stay inside these ranges and needn't reach their ends.
All inputs are finite; a program needn't handle non-finite values.
Results may differ from the reference program's by a relative error of at most 0.02.
Values may be sent and summed in bfloat16 or wider, within the bound.
No kernel may reach another device: no remote copies, remote signals or barrier semaphores. Data moves between devices by JAX's collectives and lax.ppermute only.
A program may use at most 192 MiB of HBM per device.

```python
import jax
import jax.numpy as jnp
from jax import lax

D = 2048
HEADS = 32
HEAD_DIM = 64
FF = 8192
SEQ = 512
SEQS_DP = 2
TOKENS = 8192
N_DP = 8


def with_spikes(array, rng, source, target, blocks, factor):
    owner, partner = [(jnp.arange(array.shape[axis_at]) // (array.shape[axis_at] // blocks)).reshape([-1 if axis == axis_at else 1 for axis in range(array.ndim)]) for axis_at in (source, target)]
    chosen = jax.random.permutation(rng, blocks)[partner]
    strong = (owner == chosen) | (owner == (partner + blocks // 2) % blocks)
    return jnp.where(strong, factor * array, array)


def block_scale(rng, dims, shards, smallest, high):
    loudness, own = 1.0, jax.random.fold_in(rng, 6)
    for position, blocks in shards:
        steps = jnp.exp(jax.random.uniform(jax.random.fold_in(own, position), (blocks,), jnp.float32, smallest / len(shards), high / len(shards)))
        loudness = loudness * jnp.repeat(steps, dims[position] // blocks).reshape([-1 if axis == position else 1 for axis in range(len(dims))])
    return loudness


def centred(own_key, shape, spread, reach, shards=(), kind=jnp.bfloat16):
    values = spread * jax.random.normal(own_key, shape, jnp.float32)
    if shards:
        values = values * block_scale(own_key, shape, shards, -0.22, 0.18)
    return jnp.clip(values, -reach, reach).astype(kind)


def noise_with(stream_key, extent, spread, reach, split, heavy, held_as=jnp.bfloat16):
    values = spread * jax.random.normal(stream_key, extent, jnp.float32)
    if split:
        values = values * block_scale(stream_key, extent, split, -0.22, 0.18)
    return jnp.clip(with_spikes(values, jax.random.fold_in(stream_key, 3), *heavy), -reach, reach).astype(held_as)


def setup_inputs(seed: int = 0) -> dict:
    arg_keys = jax.random.split(jax.random.key(seed), 12)
    tokens = centred(arg_keys[0], (TOKENS, D), 1.0, 6.0, ((0, 32),))
    attn_gain = jnp.clip(1.0 + 0.18 * jax.random.normal(arg_keys[1], (D,), jnp.float32), 0.099609375, 1.8984375).astype(jnp.bfloat16)
    query_weight = centred(arg_keys[2], (D, D), (D // 2) ** -0.5, 0.1875, ((0, 8), (1, 4)))
    key_weight = centred(arg_keys[3], (D, D), D ** -0.5, 0.125, ((0, 8), (1, 4)))
    value_weight = centred(arg_keys[4], (D, D), D ** -0.5, 0.125, ((0, 8), (1, 4)))
    output_weight = centred(arg_keys[5], (D, D), (D // 32) ** -0.5, 0.75, ((0, 4), (1, 8)))
    ffn_gain = jnp.clip(1.0 + 0.18 * jax.random.normal(arg_keys[6], (D,), jnp.float32), 0.099609375, 1.8984375).astype(jnp.bfloat16)
    gate_weight = centred(arg_keys[7], (D, FF), D ** -0.5, 0.125, ((0, 8), (1, 4)))
    up_weight = centred(arg_keys[8], (D, FF), D ** -0.5, 0.125, ((0, 8), (1, 4)))
    down_weight = centred(arg_keys[9], (FF, D), FF ** -0.5, 0.0625, ((0, 4), (1, 8)))
    cotangent = noise_with(arg_keys[10], (TOKENS, D), 1.0, 6.0, ((0, 32),), (0, 1, 32, 2.75))
    return dict(tokens=tokens, attn_gain=attn_gain, query_weight=query_weight, key_weight=key_weight, value_weight=value_weight, output_weight=output_weight, ffn_gain=ffn_gain, gate_weight=gate_weight, up_weight=up_weight, down_weight=down_weight, cotangent=cotangent)


@jax.custom_vjp
def low(v):
    return lax.optimization_barrier(v.astype(jnp.bfloat16)).astype(jnp.float32)

@jax.custom_vjp
def low_back(v):
    return v

def low_keep(v):
    return (low(v), None)

def low_pass(kept, grad):
    return (grad,)

def back_keep(v):
    return (v, None)

def back_low(kept, grad):
    return (low(grad),)
low.defvjp(low_keep, low_pass)
low_back.defvjp(back_keep, back_low)
EPS = 1e-05
THETA = 130000.0

def matmul(left, right):
    return jnp.dot(left, right, precision=lax.Precision.HIGHEST)

def rope_tables(length, head_dim):
    half = head_dim // 2
    freq = THETA ** (-2.0 * jnp.arange(half, dtype=jnp.float32) / head_dim)
    angle = jnp.arange(length, dtype=jnp.float32)[:, None] * freq[None, :]
    cosine = jnp.concatenate([jnp.cos(angle), jnp.cos(angle)], axis=1)
    sine = jnp.concatenate([jnp.sin(angle), jnp.sin(angle)], axis=1)
    return (cosine, sine)

def rotate(values, cosine, sine):
    half = values.shape[-1] // 2
    turned = jnp.concatenate([-values[..., half:], values[..., :half]], axis=-1)
    return values * cosine + turned * sine

def rms_norm(values, gain):
    scale = lax.rsqrt(lax.optimization_barrier(jnp.mean(values * values, axis=-1, keepdims=True)) + EPS)
    return values * scale * gain

def layer(inputs, attn_gain, query_weight, key_weight, value_weight, output_weight, ffn_gain, gate_weight, up_weight, down_weight):
    rows = inputs.shape[0]
    seqs = rows // SEQ

    def to_heads(values):
        return values.reshape(seqs, SEQ, HEADS, HEAD_DIM).transpose(0, 2, 1, 3)
    normed = low(rms_norm(inputs, attn_gain))
    cosine, sine = rope_tables(SEQ, HEAD_DIM)
    queries = low(rotate(to_heads(low_back(matmul(normed, query_weight))), cosine, sine))
    keys = low(rotate(to_heads(low_back(matmul(normed, key_weight))), cosine, sine))
    values = to_heads(low(low_back(matmul(normed, value_weight))))
    factor = HEAD_DIM ** (-0.5)
    scores = low_back(jnp.einsum('shqd,shkd->shqk', queries, keys, precision=lax.Precision.HIGHEST) * factor)
    causal = jnp.arange(SEQ)[:, None] >= jnp.arange(SEQ)[None, :]
    scores = jnp.where(causal, scores, -1e+30)
    probs = low(jax.nn.softmax(scores, axis=-1))
    mixed = jnp.einsum('shqk,shkd->shqd', probs, values, precision=lax.Precision.HIGHEST)
    mixed = low(low_back(mixed.transpose(0, 2, 1, 3).reshape(rows, HEADS * HEAD_DIM)))
    middle = inputs + low_back(matmul(mixed, output_weight))
    second = low(rms_norm(middle, ffn_gain))
    gate = low_back(matmul(second, gate_weight))
    upward = low_back(matmul(second, up_weight))
    hidden = low(jax.nn.silu(gate) * upward)
    return middle + low_back(matmul(hidden, down_weight))

def reference(tokens, attn_gain, query_weight, key_weight, value_weight, output_weight, ffn_gain, gate_weight, up_weight, down_weight, cotangent):
    weights = tuple((w.astype(jnp.float32) for w in (attn_gain, query_weight, key_weight, value_weight, output_weight, ffn_gain, gate_weight, up_weight, down_weight)))
    group_rows = SEQS_DP * SEQ
    inputs = tokens.astype(jnp.float32).reshape(N_DP, group_rows, D)
    grads_in = cotangent.astype(jnp.float32).reshape(N_DP, group_rows, D)

    def step(totals, pair):
        block, block_grad = pair
        result, pull = jax.vjp(layer, block, *weights)
        pulled = pull(block_grad)
        return (tuple((t + g for t, g in zip(totals, pulled[1:]))), (result, pulled[0]))
    zeros = tuple((jnp.zeros_like(w) for w in weights))
    totals, (results, input_grads) = lax.scan(step, zeros, (inputs, grads_in))
    return (results.reshape(TOKENS, D).astype(jnp.bfloat16), input_grads.reshape(TOKENS, D), totals[0], totals[1], totals[2], totals[3], totals[4], totals[5], totals[6], totals[7], totals[8])
```

```python
import jax
import jax.numpy as jnp
import numpy as np
from jax import lax
from jax.sharding import PartitionSpec as P

HEAD_DIM = 64
SEQ = 512
EPS = 1e-05
THETA = 130000.0
BF16 = jnp.bfloat16
F32 = jnp.float32


def ring_order(chips):
    evens = list(range(0, chips, 2))
    odds = list(range(1, chips, 2))
    return [0] + odds + evens[:0:-1]


class Ring:
    def __init__(self, size):
        self.size = size
        self.chips = size // 2
        order = ring_order(self.chips)
        after = {order[i]: order[(i + 1) % self.chips] for i in range(self.chips)}
        place = {chip: i for i, chip in enumerate(order)}
        self.forward = [(2 * c + k, 2 * after[c] + k) for c in range(self.chips) for k in (0, 1)]
        self.swap = [(i, i ^ 1) for i in range(size)]
        table = []
        for i in range(size):
            chip, core = i // 2, i % 2
            line = [order[(place[chip] - k) % self.chips] for k in range(self.chips)]
            table.append([2 * c + core for c in line] + [2 * c + 1 - core for c in line])
        self.table = np.array(table, np.int32)
        self.inverse = np.argsort(self.table, axis=1).astype(np.int32)

    def gather(self, piece):
        own = [piece]
        for _ in range(self.chips - 1):
            own.append(lax.ppermute(own[-1], "dp", self.forward))
        other = [lax.ppermute(part, "dp", self.swap) for part in own]
        return jnp.concatenate(own + other, axis=0)

    def scatter(self, make):
        theirs = make(1)
        got = lax.ppermute(theirs, "dp", self.swap)
        mine = make(0).astype(F32) + got.astype(F32)
        blocks = mine.reshape(self.chips, -1, mine.shape[-1])
        run = blocks[1 % self.chips]
        for k in range(1, self.chips):
            run = lax.ppermute(run.astype(BF16), "dp", self.forward).astype(F32)
            run = run + blocks[(k + 1) % self.chips]
        return run


def reorder(values, line, blocks):
    width = values.shape[-1] // blocks
    return jnp.concatenate(
        [lax.dynamic_slice_in_dim(values, line[j] * width, width, axis=-1) for j in range(blocks)],
        axis=-1,
    )


def rope_tables(length, head_dim):
    half = head_dim // 2
    freq = THETA ** (-2.0 * jnp.arange(half, dtype=jnp.float32) / head_dim)
    angle = jnp.arange(length, dtype=jnp.float32)[:, None] * freq[None, :]
    cosine = jnp.concatenate([jnp.cos(angle), jnp.cos(angle)], axis=1)
    sine = jnp.concatenate([jnp.sin(angle), jnp.sin(angle)], axis=1)
    return (cosine, sine)


def rotate(values, cosine, sine):
    half = values.shape[-1] // 2
    turned = jnp.concatenate([-values[..., half:], values[..., :half]], axis=-1)
    return values * cosine + turned * sine


def unrotate(grads, cosine, sine):
    half = grads.shape[-1] // 2
    turned = grads * sine
    back = jnp.concatenate([turned[..., half:], -turned[..., :half]], axis=-1)
    return grads * cosine + back


def row_scale(values):
    return lax.rsqrt(jnp.mean(values * values, axis=-1, keepdims=True) + EPS)


def norm_back(grad, values, scale, gain):
    normed = values * scale
    scaled = grad * gain
    inner = jnp.mean(scaled * normed, axis=-1, keepdims=True)
    return scale * (scaled - normed * inner)


def times(left, right):
    return jnp.dot(left, right, preferred_element_type=F32)


def times_trans(left, right):
    return lax.dot_general(left, right, (((1,), (1,)), ((), ())), preferred_element_type=F32)


def trans_times(left, right):
    return lax.dot_general(left, right, (((0,), (0,)), ((), ())), preferred_element_type=F32)


def causal_scores(queries, keys):
    scores = jnp.einsum(
        "hqd,hkd->hqk", queries, keys, preferred_element_type=F32
    ) * HEAD_DIM ** (-0.5)
    length = scores.shape[-1]
    causal = jnp.arange(length)[:, None] >= jnp.arange(length)[None, :]
    return jnp.where(causal, scores, -1e30)


def attend(queries, keys, values):
    scores = causal_scores(queries, keys)
    top = jnp.max(scores, axis=-1, keepdims=True)
    expo = jnp.exp(scores - top)
    total = jnp.sum(expo, axis=-1, keepdims=True)
    probs = (expo / total).astype(BF16)
    mixed = jnp.einsum("hqk,hkd->hqd", probs, values, preferred_element_type=F32)
    return (mixed.astype(BF16), top + jnp.log(total))


def attend_back(queries, keys, values, grad_mixed, logsum):
    probs = jnp.exp(causal_scores(queries, keys) - logsum)
    value_part = jnp.einsum(
        "hqk,hqd->hkd", probs.astype(BF16), grad_mixed, preferred_element_type=F32
    )
    prob_grad = jnp.einsum("hqd,hkd->hqk", grad_mixed, values, preferred_element_type=F32)
    delta = jnp.sum(probs * prob_grad, axis=-1, keepdims=True)
    score_grad = (probs * (prob_grad - delta)).astype(BF16)
    factor = HEAD_DIM ** (-0.5)
    query_part = jnp.einsum("hqk,hkd->hqd", score_grad, keys, preferred_element_type=F32) * factor
    key_part = jnp.einsum("hqk,hqd->hkd", score_grad, queries, preferred_element_type=F32) * factor
    return (query_part, key_part, value_part)


def local(
    ring,
    tokens,
    attn_gain,
    query_weight,
    key_weight,
    value_weight,
    output_weight,
    ffn_gain,
    gate_weight,
    up_weight,
    down_weight,
    cotangent,
):
    me = lax.axis_index("dp")
    line = jnp.asarray(ring.table)[me]
    back = jnp.asarray(ring.inverse)[me]
    model = tokens.shape[-1]
    heads_here = query_weight.shape[1]

    attn_piece = jnp.concatenate(
        [query_weight, key_weight, value_weight, output_weight.T], axis=1
    )
    w_attn = ring.gather(attn_piece)
    w_qkv, w_out = w_attn[:, : 3 * heads_here], w_attn[:, 3 * heads_here :]
    w_gate = ring.gather(gate_weight)
    w_up = ring.gather(up_weight)
    w_down = ring.gather(down_weight.T)

    gains = lax.all_gather(jnp.stack([attn_gain, ffn_gain]), "dp", axis=0)
    gains = jnp.take(gains, line, axis=0).transpose(1, 0, 2).reshape(2, model).astype(F32)
    gain_one, gain_two = gains[0], gains[1]

    def gather_rows(values):
        return lax.all_gather(values, "tensor", axis=0, tiled=True)

    def scatter_rows(values):
        return lax.psum_scatter(
            values.astype(BF16), "tensor", scatter_dimension=0, tiled=True
        ).astype(F32)

    tokens = reorder(tokens, line, ring.size)
    cotangent = reorder(cotangent, line, ring.size)
    inputs = tokens.astype(F32)
    scale_one = row_scale(inputs)
    normed = (inputs * scale_one * gain_one).astype(BF16)
    group_one = gather_rows(normed)
    grad_rows = gather_rows(cotangent)
    all_rows = group_one.shape[0]
    seqs = all_rows // SEQ
    head_count = heads_here // HEAD_DIM

    def to_heads(values):
        return (
            values.reshape(seqs, SEQ, head_count, HEAD_DIM)
            .transpose(0, 2, 1, 3)
            .reshape(seqs * head_count, SEQ, HEAD_DIM)
        )

    def to_rows(values):
        return (
            values.reshape(seqs, head_count, SEQ, HEAD_DIM)
            .transpose(0, 2, 1, 3)
            .reshape(all_rows, head_count * HEAD_DIM)
        )

    cosine, sine = rope_tables(SEQ, HEAD_DIM)
    linear = times(group_one, w_qkv)
    q_heads = rotate(to_heads(linear[:, :heads_here]), cosine, sine).astype(BF16)
    k_heads = rotate(to_heads(linear[:, heads_here : 2 * heads_here]), cosine, sine).astype(BF16)
    v_heads = to_heads(linear[:, 2 * heads_here :].astype(BF16))
    mixed_heads, logsum = attend(q_heads, k_heads, v_heads)
    mixed_rows = to_rows(mixed_heads)
    middle = inputs + scatter_rows(times_trans(mixed_rows, w_out))
    scale_two = row_scale(middle)
    second = (middle * scale_two * gain_two).astype(BF16)
    group_two = gather_rows(second)
    gate = times(group_two, w_gate)
    upward = times(group_two, w_up)
    sigm = jax.nn.sigmoid(gate)
    silu_gate = gate * sigm
    hidden = (silu_gate * upward).astype(BF16)

    half = model // 2

    def part(values, which):
        return values[:, which * half : (which + 1) * half]

    down_sum = ring.scatter(lambda h: trans_times(part(grad_rows, h), hidden).astype(BF16))
    hidden_grad = times(grad_rows, w_down)
    layer_out = (middle + scatter_rows(times_trans(hidden, w_down))).astype(BF16)
    gate_back = (hidden_grad * upward * sigm * (1.0 + gate * (1.0 - sigm))).astype(BF16)
    up_back = (hidden_grad * silu_gate).astype(BF16)
    gate_sum = ring.scatter(lambda h: trans_times(part(group_two, h), gate_back).astype(BF16))
    up_sum = ring.scatter(lambda h: trans_times(part(group_two, h), up_back).astype(BF16))
    second_grad = scatter_rows(times_trans(gate_back, w_gate) + times_trans(up_back, w_up))
    middle_grad = cotangent.astype(F32) + norm_back(second_grad, middle, scale_two, gain_two)
    attn_grad_rows = gather_rows(middle_grad.astype(BF16))
    mixed_grad = times(attn_grad_rows, w_out).astype(BF16)
    query_heads, key_heads, value_heads = attend_back(
        q_heads, k_heads, v_heads, to_heads(mixed_grad), logsum
    )
    qkv_back = jnp.concatenate(
        [
            to_rows(unrotate(query_heads, cosine, sine)).astype(BF16),
            to_rows(unrotate(key_heads, cosine, sine)).astype(BF16),
            to_rows(value_heads).astype(BF16),
        ],
        axis=1,
    )

    def attn_part(h):
        return jnp.concatenate(
            [
                trans_times(part(group_one, h), qkv_back).astype(BF16),
                trans_times(part(attn_grad_rows, h), mixed_rows).astype(BF16),
            ],
            axis=1,
        )

    attn_sum = ring.scatter(attn_part)
    first_grad = scatter_rows(times_trans(qkv_back, w_qkv))
    input_grad = middle_grad + norm_back(first_grad, inputs, scale_one, gain_one)

    query_sum = attn_sum[:, :heads_here]
    key_sum = attn_sum[:, heads_here : 2 * heads_here]
    value_sum = attn_sum[:, 2 * heads_here : 3 * heads_here]
    output_sum = attn_sum[:, 3 * heads_here :].T

    def inner(weight, grad):
        return jnp.sum(weight.astype(F32) * grad, axis=1)

    gain_one_part = (
        inner(query_weight, query_sum) + inner(key_weight, key_sum) + inner(value_weight, value_sum)
    ) / attn_gain.astype(F32)
    gain_two_part = (inner(gate_weight, gate_sum) + inner(up_weight, up_sum)) / ffn_gain.astype(F32)
    gain_one_total, gain_two_total = lax.psum((gain_one_part, gain_two_part), "tensor")
    return (
        reorder(layer_out, back, ring.size),
        reorder(input_grad, back, ring.size),
        gain_one_total,
        query_sum,
        key_sum,
        value_sum,
        output_sum,
        gain_two_total,
        gate_sum,
        up_sum,
        down_sum.T,
    )


def solution(mesh):
    in_specs = (
        P(("dp", "tensor"), None),
        P("dp"),
        P("dp", "tensor"),
        P("dp", "tensor"),
        P("dp", "tensor"),
        P("tensor", "dp"),
        P("dp"),
        P("dp", "tensor"),
        P("dp", "tensor"),
        P("tensor", "dp"),
        P(("dp", "tensor"), None),
    )
    out_specs = (
        P(("dp", "tensor"), None),
        P(("dp", "tensor"), None),
        P("dp"),
        P("dp", "tensor"),
        P("dp", "tensor"),
        P("dp", "tensor"),
        P("tensor", "dp"),
        P("dp"),
        P("dp", "tensor"),
        P("dp", "tensor"),
        P("tensor", "dp"),
    )
    ring = Ring(mesh.shape["dp"])

    def run(*arrays):
        return local(ring, *arrays)

    return jax.shard_map(run, mesh=mesh, in_specs=in_specs, out_specs=out_specs, check_vma=False)
```

```python
import functools

import jax
import jax.numpy as jnp
import numpy as np
from jax import lax
from jax.experimental import pallas as pl
from jax.experimental.pallas import tpu as pltpu
from jax.sharding import PartitionSpec as P

HEAD_DIM = 64
SEQ = 512
EPS = 1e-05
THETA = 130000.0
BF16 = jnp.bfloat16
F32 = jnp.float32
FACTOR = HEAD_DIM**-0.5
PAIR = 2 * HEAD_DIM
HALF_SEQ = SEQ // 2


def ring_order(chips):
    evens = list(range(0, chips, 2))
    odds = list(range(1, chips, 2))
    return [0] + odds + evens[:0:-1]


def after(value, *others):
    return lax.optimization_barrier((value,) + others)[0]


class Ring:
    def __init__(self, size):
        self.size = size
        self.chips = size // 2
        order = ring_order(self.chips)
        follow = {order[i]: order[(i + 1) % self.chips] for i in range(self.chips)}
        place = {chip: i for i, chip in enumerate(order)}
        self.forward = [(2 * c + k, 2 * follow[c] + k) for c in range(self.chips) for k in (0, 1)]
        self.swap = [(i, i ^ 1) for i in range(size)]
        table = []
        for i in range(size):
            chip, core = i // 2, i % 2
            line = [order[(place[chip] - k) % self.chips] for k in range(self.chips)]
            table.append([2 * c + core for c in line] + [2 * c + 1 - core for c in line])
        self.table = np.array(table, np.int32)

    def step(self, value):
        return lax.ppermute(value, "dp", self.forward)

    def other(self, value):
        return lax.ppermute(value, "dp", self.swap)

    def gather(self, groups):
        own, sent = {}, []
        for group in groups:
            for name, piece in group:
                own[name] = [piece]
            for _ in range(self.chips - 1):
                for name, _ in group:
                    held = own[name][-1]
                    if len(sent) >= len(group):
                        held = after(held, sent[-len(group)])
                    own[name].append(self.step(held))
                    sent.append(own[name][-1])
        return {name: own[name] + [self.other(p) for p in own[name]] for name in own}


class Sums:
    def __init__(self, ring):
        self.ring = ring
        self.sent = []

    def add(self, mine):
        chips = self.ring.chips
        blocks = [m.reshape(chips, -1, m.shape[-1]) for m in mine]
        run = [b[1 % chips].astype(F32) for b in blocks]
        for k in range(1, chips):
            for i in range(len(run)):
                held = run[i].astype(BF16)
                if len(self.sent) >= len(run):
                    held = after(held, self.sent[-len(run)])
                got = self.ring.step(held)
                self.sent.append(got)
                run[i] = got.astype(F32) + blocks[i][(k + 1) % chips].astype(F32)
        return run


def nn(left, right):
    return lax.dot_general(left, right, (((1,), (0,)), ((), ())), preferred_element_type=F32)


def nt(left, right):
    return lax.dot_general(left, right, (((1,), (1,)), ((), ())), preferred_element_type=F32)


def tn(left, right):
    return lax.dot_general(left, right, (((0,), (0,)), ((), ())), preferred_element_type=F32)


def call(body, grid, ins, outs, shapes, flops, limit, scratch=(), prefetch=0, moved=0):
    return pl.pallas_call(
        body,
        grid_spec=pltpu.PrefetchScalarGridSpec(
            num_scalar_prefetch=prefetch,
            grid=grid,
            in_specs=ins,
            out_specs=outs,
            scratch_shapes=list(scratch),
        ),
        out_shape=[jax.ShapeDtypeStruct(s, t) for s, t in shapes],
        compiler_params=pltpu.CompilerParams(
            vmem_limit_bytes=limit << 20, dimension_semantics=("arbitrary",) * len(grid)
        ),
        cost_estimate=pl.CostEstimate(flops=flops, bytes_accessed=moved, transcendentals=0),
    )


def whole(shape):
    return pl.BlockSpec(shape, lambda *_: (0,) * len(shape))


def place(line_ref, j, width):
    return pl.ds(pl.multiple_of(line_ref[j] * width, 128), width)


def cut(width, j):
    return slice(j * width, (j + 1) * width)


def scale_of(values):
    return lax.rsqrt(jnp.mean(values * values, axis=-1, keepdims=True) + EPS)


def norm_body(blocks, line_ref, x_ref, gain_ref, out_ref):
    width = x_ref.shape[1] // blocks
    scale = scale_of(x_ref[...].astype(F32))
    for j in range(blocks):
        part = x_ref[:, place(line_ref, j, width)].astype(F32)
        gain = gain_ref[0:1, cut(width, j)]
        out_ref[:, cut(width, j)] = (part * scale * gain).astype(BF16)


def order_body(blocks, line_ref, x_ref, out_ref):
    width = x_ref.shape[1] // blocks
    for j in range(blocks):
        out_ref[:, cut(width, j)] = x_ref[:, place(line_ref, j, width)]


def middle_body(blocks, line_ref, x_ref, part_ref, gain_ref, middle_ref, out_ref):
    width = x_ref.shape[1] // blocks
    for j in range(blocks):
        here = x_ref[:, place(line_ref, j, width)].astype(F32)
        middle_ref[:, cut(width, j)] = here + part_ref[:, cut(width, j)].astype(F32)
    middle = middle_ref[...]
    out_ref[...] = (middle * scale_of(middle) * gain_ref[1:2, :]).astype(BF16)


def result_body(blocks, line_ref, middle_ref, part_ref, out_ref):
    width = middle_ref.shape[1] // blocks
    for j in range(blocks):
        total = middle_ref[:, cut(width, j)] + part_ref[:, cut(width, j)].astype(F32)
        out_ref[:, place(line_ref, j, width)] = total.astype(BF16)


def second_back_body(blocks, line_ref, dy_ref, grad_ref, middle_ref, gain_ref, out_ref, low_ref):
    width = dy_ref.shape[1] // blocks
    middle = middle_ref[...]
    scale = scale_of(middle)
    normed = middle * scale
    scaled = grad_ref[...].astype(F32) * gain_ref[1:2, :]
    back = scale * (scaled - normed * jnp.mean(scaled * normed, axis=-1, keepdims=True))
    for j in range(blocks):
        here = dy_ref[:, place(line_ref, j, width)].astype(F32) + back[:, cut(width, j)]
        out_ref[:, cut(width, j)] = here
        low_ref[:, cut(width, j)] = here.astype(BF16)


def first_back_body(blocks, line_ref, x_ref, grad_ref, above_ref, gain_ref, out_ref):
    width = x_ref.shape[1] // blocks
    scale = scale_of(x_ref[...].astype(F32))
    normed = jnp.concatenate(
        [x_ref[:, place(line_ref, j, width)].astype(F32) for j in range(blocks)], axis=1
    ) * scale
    scaled = grad_ref[...].astype(F32) * gain_ref[0:1, :]
    back = scale * (scaled - normed * jnp.mean(scaled * normed, axis=-1, keepdims=True))
    total = above_ref[...] + back
    for j in range(blocks):
        out_ref[:, place(line_ref, j, width)] = total[:, cut(width, j)]


def by_rows(body, line, arrays, kinds, tile=128):
    rows, width = arrays[0].shape
    tile = min(tile, rows)
    row = pl.BlockSpec((tile, width), lambda i, *_: (i, 0))
    moved = sum(a.size * a.dtype.itemsize for a in arrays)
    return call(
        functools.partial(body, line.shape[0]),
        (rows // tile,),
        [row if a.shape[0] == rows else whole(a.shape) for a in arrays],
        [row] * len(kinds),
        [((rows, width), kind) for kind in kinds],
        flops=20 * rows * width,
        limit=40,
        prefetch=1,
        moved=moved + rows * width * 4 * len(kinds),
    )(line, *arrays)


def rope_tables():
    half = HEAD_DIM // 2
    freq = THETA ** (-2.0 * jnp.arange(half, dtype=F32) / HEAD_DIM)
    angle = jnp.arange(SEQ, dtype=F32)[:, None] * freq[None, :]
    cosine, sine = jnp.cos(angle), jnp.sin(angle)
    return (
        jnp.concatenate([cosine] * (PAIR // half), axis=1),
        jnp.concatenate([-sine, sine] * (PAIR // HEAD_DIM), axis=1),
    )


def turn(values):
    half = HEAD_DIM // 2
    width = values.shape[-1]
    lane = lax.broadcasted_iota(jnp.int32, values.shape, 1) % HEAD_DIM
    return jnp.where(
        lane < half, pltpu.roll(values, width - half, 1), pltpu.roll(values, half, 1)
    )


def joined(refs):
    return jnp.concatenate([r[...] for r in refs], axis=0)


def qkv_body(n, x_ref, cos_ref, sin_ref, *refs):
    weights, outs = refs[: 3 * n], refs[3 * n :]
    rows = x_ref.shape[0]
    tile = outs[0].shape[1]
    for i in range(3):
        weight = joined(weights[i * n : (i + 1) * n])
        for s in range(rows // SEQ):
            span = slice(s * SEQ, (s + 1) * SEQ)
            product = nn(x_ref[span, :], weight)
            if i == 2:
                outs[i][span, :] = product.astype(BF16)
                continue
            for t in range(tile // PAIR):
                here = product[:, t * PAIR : (t + 1) * PAIR]
                turned = here * cos_ref[...] + turn(here) * sin_ref[...]
                outs[i][span, t * PAIR : (t + 1) * PAIR] = turned.astype(BF16)


def project(x, tables, query, key, value):
    rows, model = x.shape
    n, width = len(query), query[0].shape[1]
    tile = min(256, width)
    piece = pl.BlockSpec((model // n, tile), lambda j: (0, j))
    out = pl.BlockSpec((rows, tile), lambda j: (0, j))
    return call(
        functools.partial(qkv_body, n),
        (width // tile,),
        [whole(x.shape), whole((SEQ, PAIR)), whole((SEQ, PAIR))] + [piece] * (3 * n),
        [out] * 3,
        [((rows, width), BF16)] * 3,
        flops=6 * rows * model * width,
        limit=48,
        moved=2 * (rows * model + 3 * model * width + 3 * rows * width),
    )(x, *tables, *query, *key, *value)


def gate_body(n, x_ref, *refs):
    gate_w, up_w = refs[:n], refs[n : 2 * n]
    hidden_ref, slope_ref, silu_ref = refs[2 * n :]
    gate_weight, up_weight = joined(gate_w), joined(up_w)
    for s in range(x_ref.shape[0] // SEQ):
        span = slice(s * SEQ, (s + 1) * SEQ)
        gate = nn(x_ref[span, :], gate_weight)
        up = nn(x_ref[span, :], up_weight)
        sigm = jax.nn.sigmoid(gate)
        silu = gate * sigm
        hidden_ref[span, :] = (silu * up).astype(BF16)
        silu_ref[span, :] = silu.astype(BF16)
        slope_ref[span, :] = (up * sigm * (1.0 + gate * (1.0 - sigm))).astype(BF16)


def gate_up(x, gate, up):
    rows, model = x.shape
    n, width = len(gate), gate[0].shape[1]
    tile = min(256, width)
    piece = pl.BlockSpec((model // n, tile), lambda j: (0, j))
    out = pl.BlockSpec((rows, tile), lambda j: (0, j))
    return call(
        functools.partial(gate_body, n),
        (width // tile,),
        [whole(x.shape)] + [piece] * (2 * n),
        [out] * 3,
        [((rows, width), BF16)] * 3,
        flops=4 * rows * model * width,
        limit=48,
        moved=2 * (rows * model + 2 * model * width + 3 * rows * width),
    )(x, *gate, *up)


def hidden_back_body(n, steps, g_ref, *refs):
    first, second = refs[:n], refs[n : 2 * n]
    slope_ref, silu_ref, gate_ref, up_ref = refs[2 * n :]

    def work(weights):
        weight = joined(weights)
        for s in range(g_ref.shape[0] // SEQ):
            span = slice(s * SEQ, (s + 1) * SEQ)
            grad = nn(g_ref[span, :], weight)
            gate_ref[span, :] = (grad * slope_ref[span, :].astype(F32)).astype(BF16)
            up_ref[span, :] = (grad * silu_ref[span, :].astype(F32)).astype(BF16)

    @pl.when(pl.program_id(0) < steps)
    def _():
        work(first)

    @pl.when(pl.program_id(0) >= steps)
    def _():
        work(second)


def hidden_back(grads, first, second, slope, silu):
    rows, model = grads.shape
    n, width = len(first), first[0].shape[1]
    tile = min(256, width)
    steps = width // tile
    early = pl.BlockSpec((model // n, tile), lambda j: (0, jnp.minimum(j, steps - 1)))
    late = pl.BlockSpec((model // n, tile), lambda j: (0, jnp.maximum(j - steps, 0)))
    out = pl.BlockSpec((rows, tile), lambda j: (0, j))
    return call(
        functools.partial(hidden_back_body, n, steps),
        (2 * steps,),
        [whole(grads.shape)] + [early] * n + [late] * n + [out] * 2,
        [out] * 2,
        [((rows, 2 * width), BF16)] * 2,
        flops=4 * rows * model * width,
        limit=48,
        moved=2 * (rows * model + 2 * model * width + 8 * rows * width),
    )(grads, *first, *second, slope, silu)


def mixed_back_body(n, g_ref, *refs):
    weight = joined(refs[:n])
    refs[n][...] = nn(g_ref[...], weight).astype(BF16)


def mixed_back(grads, out):
    rows, model = grads.shape
    n, width = len(out), out[0].shape[1]
    tile = min(256, width)
    piece = pl.BlockSpec((model // n, tile), lambda j: (0, j))
    return call(
        functools.partial(mixed_back_body, n),
        (width // tile,),
        [whole(grads.shape)] + [piece] * n,
        [pl.BlockSpec((rows, tile), lambda j: (0, j))],
        [((rows, width), BF16)],
        flops=2 * rows * model * width,
        limit=48,
        moved=2 * (rows * model + model * width + rows * width),
    )(grads, *out)[0]


def trans_body(n, parts, steps, *refs):
    lefts = refs[:parts]
    weights = [refs[parts + p * n : parts + (p + 1) * n] for p in range(parts)]
    out_ref = refs[parts * (n + 1)]
    total_ref = refs[parts * (n + 1) + 1]
    k = pl.program_id(0)
    width = weights[0][0].shape[0]
    for j in range(n):
        here = nt(lefts[0][...], weights[0][j][...])
        for p in range(1, parts):
            here += nt(lefts[p][...], weights[p][j][...])
        if steps == 1:
            out_ref[:, cut(width, j)] = here.astype(BF16)
            continue

        @pl.when(k == 0)
        def _():
            total_ref[:, cut(width, j)] = here

        @pl.when((k > 0) & (k < steps - 1))
        def _():
            total_ref[:, cut(width, j)] += here

        @pl.when(k == steps - 1)
        def _():
            out_ref[:, cut(width, j)] = (total_ref[:, cut(width, j)] + here).astype(BF16)


def times_trans(parts, tile):
    rows = parts[0][0].shape[0]
    n = len(parts[0][2])
    piece_rows, width = parts[0][2][0].shape
    tile = min(tile, width)
    steps = width // tile
    ins = []
    for _, start, _ in parts:
        ins.append(pl.BlockSpec((rows, tile), functools.partial(lambda b, k: (0, b + k), start // tile)))
    ins += [pl.BlockSpec((piece_rows, tile), lambda k: (0, k))] * (n * len(parts))
    model = n * piece_rows
    return call(
        functools.partial(trans_body, n, len(parts), steps),
        (steps,),
        ins,
        [whole((rows, model))],
        [((rows, model), BF16)],
        flops=2 * rows * model * width * len(parts),
        limit=56,
        scratch=[pltpu.VMEM((rows, model), F32)],
        moved=2 * (rows * model + len(parts) * (rows + model) * width),
    )(*[left for left, _, _ in parts], *[w for _, _, pieces in parts for w in pieces])[0]


def causal(scores):
    past = scores.shape[0] - HALF_SEQ
    key = lax.broadcasted_iota(jnp.int32, (HALF_SEQ, HALF_SEQ), 0)
    query = lax.broadcasted_iota(jnp.int32, (HALF_SEQ, HALF_SEQ), 1)
    last = jnp.where(key <= query, scores[past:], -1e30)
    return last if past == 0 else jnp.concatenate([scores[:past], last], axis=0)


def head_of(h):
    return slice(h * HEAD_DIM, (h + 1) * HEAD_DIM)


def span_of(b):
    return slice(b * HALF_SEQ, (b + 1) * HALF_SEQ)


def attend_body(q_ref, k_ref, v_ref, out_ref, sum_ref):
    values = v_ref[...].astype(F32).T.astype(BF16)
    heads = []
    for h in range(2):
        blocks = []
        for b in range(2):
            reach = (b + 1) * HALF_SEQ
            query = q_ref[span_of(b), head_of(h)] * BF16(FACTOR)
            scores = causal(nt(k_ref[:reach, head_of(h)], query))
            top = jnp.max(scores, axis=0, keepdims=True)
            expo = jnp.exp(scores - top)
            total = jnp.sum(expo, axis=0, keepdims=True)
            mixed = nn(values[head_of(h), :reach], expo.astype(BF16))
            blocks.append(mixed * (1.0 / total))
            sum_ref[0, 0, h : h + 1, span_of(b)] = top + jnp.log(total)
        heads.append(jnp.concatenate(blocks, axis=1))
    out_ref[...] = jnp.concatenate(heads, axis=0).T.astype(BF16)


def attend(query, key, value):
    rows, width = query.shape
    seqs, pairs = rows // SEQ, width // PAIR
    tile = pl.BlockSpec((SEQ, PAIR), lambda s, p: (s, p))
    return call(
        attend_body,
        (seqs, pairs),
        [tile] * 3,
        [tile, pl.BlockSpec((1, 1, 2, SEQ), lambda s, p: (s, p, 0, 0))],
        [((rows, width), BF16), ((seqs, pairs, 2, SEQ), F32)],
        flops=16 * rows * width * SEQ,
        limit=40,
        moved=8 * rows * width,
    )(query, key, value)


def attend_back_body(q_ref, k_ref, v_ref, g_ref, sum_ref, cos_ref, sin_ref, dq_ref, dk_ref, dv_ref):
    keys = k_ref[...].astype(F32).T.astype(BF16)
    dq_heads, dk_heads, dv_heads = [], [], []
    for h in range(2):
        dq, dk, dv = [], [], []
        for b in range(2):
            reach = (b + 1) * HALF_SEQ
            query = q_ref[span_of(b), head_of(h)]
            grad = g_ref[span_of(b), head_of(h)]
            scores = causal(nt(k_ref[:reach, head_of(h)], query * BF16(FACTOR)))
            probs = jnp.exp(scores - sum_ref[0, 0, h : h + 1, span_of(b)])
            probs_grad = nt(v_ref[:reach, head_of(h)], grad)
            inner = jnp.sum(probs * probs_grad, axis=0, keepdims=True)
            score_grad = (probs * (probs_grad - inner)).astype(BF16)
            dv.append(nn(probs.astype(BF16), grad))
            dk.append(nn(score_grad, query))
            dq.append(nn(keys[head_of(h), :reach], score_grad))
        for parts, heads in ((dk, dk_heads), (dv, dv_heads)):
            heads.append(
                jnp.concatenate([parts[1][:HALF_SEQ] + parts[0], parts[1][HALF_SEQ:]], axis=0)
            )
        dq_heads.append(jnp.concatenate(dq, axis=1))
    dq = jnp.concatenate(dq_heads, axis=0).T * FACTOR
    dk = jnp.concatenate(dk_heads, axis=1) * FACTOR
    cosine, sine = cos_ref[...], sin_ref[...]
    dq_ref[...] = (dq * cosine - turn(dq) * sine).astype(BF16)
    dk_ref[...] = (dk * cosine - turn(dk) * sine).astype(BF16)
    dv_ref[...] = jnp.concatenate(dv_heads, axis=1).astype(BF16)


def attend_back(query, key, value, grad, logsum, tables):
    rows, width = query.shape
    seqs, pairs = rows // SEQ, width // PAIR
    tile = pl.BlockSpec((SEQ, PAIR), lambda s, p: (s, p))
    return call(
        attend_back_body,
        (seqs, pairs),
        [tile] * 4
        + [pl.BlockSpec((1, 1, 2, SEQ), lambda s, p: (s, p, 0, 0))]
        + [whole((SEQ, PAIR))] * 2,
        [tile] * 3,
        [((rows, width), BF16)] * 3,
        flops=40 * rows * width * SEQ,
        limit=40,
        moved=14 * rows * width,
    )(query, key, value, grad, logsum, *tables)


def local(
    ring,
    tokens,
    attn_gain,
    query_weight,
    key_weight,
    value_weight,
    output_weight,
    ffn_gain,
    gate_weight,
    up_weight,
    down_weight,
    cotangent,
):
    line = jnp.asarray(ring.table)[lax.axis_index("dp")]
    model = tokens.shape[1]
    half = model // 2

    def gather_rows(values):
        return lax.all_gather(values, "tensor", axis=0, tiled=True)

    def scatter_rows(values):
        return lax.psum_scatter(values, "tensor", scatter_dimension=0, tiled=True)

    down_turned = down_weight.T
    here = down_turned.shape[1] // 2
    weights = ring.gather(
        [
            [("gains", jnp.stack([attn_gain, ffn_gain]))],
            [
                ("query", query_weight),
                ("key", key_weight),
                ("value", value_weight),
                ("output", output_weight.T),
            ],
            [("gate", gate_weight), ("up", up_weight)],
            [("down_a", down_turned[:, :here]), ("down_b", down_turned[:, here:])],
        ]
    )
    gains = jnp.concatenate(weights["gains"], axis=1).astype(F32)
    tables = rope_tables()
    sums = Sums(ring)

    all_tokens = gather_rows(tokens)
    all_grads = gather_rows(after(cotangent, all_tokens))
    group_one = by_rows(norm_body, line, [all_tokens, gains], [BF16], tile=256)[0]
    query, key, value = project(
        group_one, tables, weights["query"], weights["key"], weights["value"]
    )
    mixed, logsum = attend(query, key, value)
    attended = scatter_rows(times_trans([(mixed, 0, weights["output"])], 256))
    grad_rows = by_rows(order_body, line, [after(all_grads, mixed)], [BF16], tile=256)[0]
    middle, second = by_rows(middle_body, line, [tokens, attended, gains], [F32, BF16])
    group_two = gather_rows(second)
    hidden, slope, silu = gate_up(group_two, weights["gate"], weights["up"])

    def halves(values):
        return values[:, :half], values[:, half:]

    grads_mine, grads_theirs = halves(grad_rows)
    theirs_a = tn(grads_theirs, hidden[:, :here]).astype(BF16)
    theirs_b = tn(grads_theirs, hidden[:, here:]).astype(BF16)
    got_a, got_b = ring.other(theirs_a), ring.other(theirs_b)
    mine_a = tn(grads_mine, hidden[:, :here]) + got_a.astype(F32)
    mine_b = tn(grads_mine, hidden[:, here:]) + got_b.astype(F32)
    down_a, down_b = sums.add([mine_a, mine_b])

    gate_grad, up_grad = hidden_back(
        after(grad_rows, theirs_a, theirs_b), weights["down_a"], weights["down_b"], slope, silu
    )
    second_part = times_trans(
        [(gate_grad, 0, weights["gate"]), (up_grad, 0, weights["up"])], 512
    )
    second_grad = scatter_rows(second_part)
    two_mine, two_theirs = halves(after(group_two, second_part))
    gate_theirs = tn(two_theirs, gate_grad).astype(BF16)
    up_theirs = tn(two_theirs, up_grad).astype(BF16)
    gate_got, up_got = ring.other(gate_theirs), ring.other(up_theirs)
    gate_mine = tn(two_mine, gate_grad) + gate_got.astype(F32)
    up_mine = tn(two_mine, up_grad) + up_got.astype(F32)
    gate_sum, up_sum = sums.add([gate_mine, up_mine])

    middle_grad, low_grad = by_rows(
        second_back_body, line, [cotangent, second_grad, middle, gains], [F32, BF16]
    )
    attn_grads = gather_rows(low_grad)
    result_part = scatter_rows(
        times_trans(
            [
                (after(hidden, low_grad), 0, weights["down_a"]),
                (after(hidden, low_grad), here, weights["down_b"]),
            ],
            512,
        )
    )
    layer_out = by_rows(result_body, line, [middle, result_part], [BF16])[0]

    mixed_grad = mixed_back(attn_grads, weights["output"])
    query_back, key_back, value_back = attend_back(query, key, value, mixed_grad, logsum, tables)
    one_mine, one_theirs = halves(group_one)
    attn_mine, attn_theirs = halves(attn_grads)
    pairs = [
        (one_mine, one_theirs, query_back),
        (one_mine, one_theirs, key_back),
        (one_mine, one_theirs, value_back),
        (attn_mine, attn_theirs, mixed),
    ]
    theirs = [tn(left, right).astype(BF16) for _, left, right in pairs]
    got = [ring.other(value) for value in theirs]
    mine = [tn(left, right) + g.astype(F32) for (left, _, right), g in zip(pairs, got)]
    query_sum, key_sum, value_sum, output_sum = sums.add(mine)
    first_grad = scatter_rows(
        times_trans(
            [
                (query_back, 0, weights["query"]),
                (key_back, 0, weights["key"]),
                (value_back, 0, weights["value"]),
            ],
            256,
        )
    )
    input_grad = by_rows(
        first_back_body, line, [tokens, first_grad, middle_grad, gains], [F32]
    )[0]

    def inner(weight, grad):
        return jnp.sum(weight.astype(F32) * grad, axis=1)

    gain_one_part = (
        inner(query_weight, query_sum) + inner(key_weight, key_sum) + inner(value_weight, value_sum)
    ) / attn_gain.astype(F32)
    gain_two_part = (inner(gate_weight, gate_sum) + inner(up_weight, up_sum)) / ffn_gain.astype(F32)
    gain_one_total, gain_two_total = lax.psum((gain_one_part, gain_two_part), "tensor")
    return (
        layer_out,
        input_grad,
        gain_one_total,
        query_sum,
        key_sum,
        value_sum,
        output_sum.T,
        gain_two_total,
        gate_sum,
        up_sum,
        jnp.concatenate([down_a, down_b], axis=1).T,
    )


def solution(mesh):
    in_specs = (
        P(("dp", "tensor"), None),
        P("dp"),
        P("dp", "tensor"),
        P("dp", "tensor"),
        P("dp", "tensor"),
        P("tensor", "dp"),
        P("dp"),
        P("dp", "tensor"),
        P("dp", "tensor"),
        P("tensor", "dp"),
        P(("dp", "tensor"), None),
    )
    out_specs = (
        P(("dp", "tensor"), None),
        P(("dp", "tensor"), None),
        P("dp"),
        P("dp", "tensor"),
        P("dp", "tensor"),
        P("dp", "tensor"),
        P("tensor", "dp"),
        P("dp"),
        P("dp", "tensor"),
        P("dp", "tensor"),
        P("tensor", "dp"),
    )
    ring = Ring(mesh.shape["dp"])

    def run(*arrays):
        return local(ring, *arrays)

    return jax.shard_map(run, mesh=mesh, in_specs=in_specs, out_specs=out_specs, check_vma=False)
```

```python
import functools

import jax
import jax.numpy as jnp
import numpy as np
from jax import lax
from jax.experimental import pallas as pl
from jax.experimental.pallas import tpu as pltpu
from jax.sharding import PartitionSpec as P

HEAD_DIM = 64
SEQ = 512
EPS = 1e-05
THETA = 130000.0
BF16 = jnp.bfloat16
F32 = jnp.float32
FACTOR = HEAD_DIM**-0.5
PAIR = 2 * HEAD_DIM
HALF_SEQ = SEQ // 2


def ring_order(chips):
    evens = list(range(0, chips, 2))
    odds = list(range(1, chips, 2))
    return [0] + odds + evens[:0:-1]


def after(value, *others):
    return lax.optimization_barrier((value,) + others)[0]


class Ring:
    def __init__(self, size):
        self.size = size
        self.chips = size // 2
        order = ring_order(self.chips)
        follow = {order[i]: order[(i + 1) % self.chips] for i in range(self.chips)}
        place = {chip: i for i, chip in enumerate(order)}
        self.forward = [(2 * c + k, 2 * follow[c] + k) for c in range(self.chips) for k in (0, 1)]
        self.swap = [(i, i ^ 1) for i in range(size)]
        table = []
        for i in range(size):
            chip, core = i // 2, i % 2
            line = [order[(place[chip] - k) % self.chips] for k in range(self.chips)]
            table.append([2 * c + core for c in line] + [2 * c + 1 - core for c in line])
        self.table = np.array(table, np.int32)

    def step(self, value):
        return lax.ppermute(value, "dp", self.forward)

    def other(self, value):
        return lax.ppermute(value, "dp", self.swap)

    def gather(self, groups):
        own, behind = {}, []
        for group in groups:
            for name, piece in group:
                own[name] = [piece]
            for _ in range(self.chips - 1):
                for name, _ in group:
                    held = own[name][-1]
                    own[name].append(self.step(after(held, *behind) if behind else held))
                behind = []
            behind = [own[name][-2] for name, _ in group]
        return {name: own[name] + [self.other(p) for p in own[name]] for name in own}


class Sums:
    def __init__(self, ring, mine):
        self.ring = ring
        self.blocks = [m.reshape(ring.chips, -1, m.shape[-1]) for m in mine]
        self.held = [b[1 % ring.chips] for b in self.blocks]
        self.k = 0

    def step(self):
        self.k += 1
        last = self.k == self.ring.chips - 1
        got = [self.ring.step(h) for h in self.held]
        block = (self.k + 1) % self.ring.chips
        totals = [g.astype(F32) + b[block].astype(F32) for g, b in zip(got, self.blocks)]
        self.held = totals if last else [t.astype(BF16) for t in totals]
        return self.held

    def finish(self):
        while self.k < self.ring.chips - 1:
            self.step()
        return self.held


def nn(left, right):
    return lax.dot_general(left, right, (((1,), (0,)), ((), ())), preferred_element_type=F32)


def nt(left, right):
    return lax.dot_general(left, right, (((1,), (1,)), ((), ())), preferred_element_type=F32)


def tn(left, right):
    return lax.dot_general(left, right, (((0,), (0,)), ((), ())), preferred_element_type=F32)


VMEM_LIMIT = 56 << 20
COST_SHARE = 8


def call(body, grid, ins, outs, shapes, flops, scratch=(), prefetch=0, moved=0):
    return pl.pallas_call(
        body,
        grid_spec=pltpu.PrefetchScalarGridSpec(
            num_scalar_prefetch=prefetch,
            grid=grid,
            in_specs=ins,
            out_specs=outs,
            scratch_shapes=list(scratch),
        ),
        out_shape=[jax.ShapeDtypeStruct(s, t) for s, t in shapes],
        compiler_params=pltpu.CompilerParams(
            vmem_limit_bytes=VMEM_LIMIT, dimension_semantics=("arbitrary",) * len(grid)
        ),
        cost_estimate=pl.CostEstimate(
            flops=flops // COST_SHARE, bytes_accessed=moved // COST_SHARE, transcendentals=0
        ),
    )


def whole(shape):
    return pl.BlockSpec(shape, lambda *_: (0,) * len(shape))


def place(line_ref, j, width):
    return pl.ds(pl.multiple_of(line_ref[j] * width, 128), width)


def cut(width, j):
    return slice(j * width, (j + 1) * width)


def scale_of(values):
    return lax.rsqrt(jnp.mean(values * values, axis=-1, keepdims=True) + EPS)


def norm_body(blocks, line_ref, x_ref, gain_ref, out_ref):
    width = x_ref.shape[1] // blocks
    scale = scale_of(x_ref[...].astype(F32))
    for j in range(blocks):
        part = x_ref[:, place(line_ref, j, width)].astype(F32)
        gain = gain_ref[0:1, cut(width, j)]
        out_ref[:, cut(width, j)] = (part * scale * gain).astype(BF16)


def order_body(blocks, line_ref, x_ref, out_ref):
    width = x_ref.shape[1] // blocks
    for j in range(blocks):
        out_ref[:, cut(width, j)] = x_ref[:, place(line_ref, j, width)]


def middle_body(blocks, line_ref, x_ref, part_ref, gain_ref, middle_ref, out_ref):
    width = x_ref.shape[1] // blocks
    for j in range(blocks):
        here = x_ref[:, place(line_ref, j, width)].astype(F32)
        middle_ref[:, cut(width, j)] = here + part_ref[:, cut(width, j)].astype(F32)
    middle = middle_ref[...]
    out_ref[...] = (middle * scale_of(middle) * gain_ref[1:2, :]).astype(BF16)


def result_body(blocks, line_ref, middle_ref, part_ref, out_ref):
    width = middle_ref.shape[1] // blocks
    for j in range(blocks):
        total = middle_ref[:, cut(width, j)] + part_ref[:, cut(width, j)].astype(F32)
        out_ref[:, place(line_ref, j, width)] = total.astype(BF16)


def second_back_body(blocks, line_ref, dy_ref, grad_ref, middle_ref, gain_ref, out_ref, low_ref):
    width = dy_ref.shape[1] // blocks
    middle = middle_ref[...]
    scale = scale_of(middle)
    normed = middle * scale
    scaled = grad_ref[...].astype(F32) * gain_ref[1:2, :]
    back = scale * (scaled - normed * jnp.mean(scaled * normed, axis=-1, keepdims=True))
    for j in range(blocks):
        here = dy_ref[:, place(line_ref, j, width)].astype(F32) + back[:, cut(width, j)]
        out_ref[:, cut(width, j)] = here
        low_ref[:, cut(width, j)] = here.astype(BF16)


def first_back_body(blocks, line_ref, x_ref, grad_ref, above_ref, gain_ref, out_ref):
    width = x_ref.shape[1] // blocks
    scale = scale_of(x_ref[...].astype(F32))
    normed = jnp.concatenate(
        [x_ref[:, place(line_ref, j, width)].astype(F32) for j in range(blocks)], axis=1
    ) * scale
    scaled = grad_ref[...].astype(F32) * gain_ref[0:1, :]
    back = scale * (scaled - normed * jnp.mean(scaled * normed, axis=-1, keepdims=True))
    total = above_ref[...] + back
    for j in range(blocks):
        out_ref[:, place(line_ref, j, width)] = total[:, cut(width, j)]


def by_rows(body, line, arrays, kinds, tile=128):
    rows, width = arrays[0].shape
    tile = min(tile, rows)
    row = pl.BlockSpec((tile, width), lambda i, *_: (i, 0))
    moved = sum(a.size * a.dtype.itemsize for a in arrays)
    return call(
        functools.partial(body, line.shape[0]),
        (rows // tile,),
        [row if a.shape[0] == rows else whole(a.shape) for a in arrays],
        [row] * len(kinds),
        [((rows, width), kind) for kind in kinds],
        flops=20 * rows * width,
        prefetch=1,
        moved=moved + rows * width * 4 * len(kinds),
    )(line, *arrays)


def rope_tables():
    half = HEAD_DIM // 2
    freq = THETA ** (-2.0 * jnp.arange(half, dtype=F32) / HEAD_DIM)
    angle = jnp.arange(SEQ, dtype=F32)[:, None] * freq[None, :]
    cosine, sine = jnp.cos(angle), jnp.sin(angle)
    return (
        jnp.concatenate([cosine] * (PAIR // half), axis=1),
        jnp.concatenate([-sine, sine] * (PAIR // HEAD_DIM), axis=1),
    )


def turn(values):
    half = HEAD_DIM // 2
    width = values.shape[-1]
    lane = lax.broadcasted_iota(jnp.int32, values.shape, 1) % HEAD_DIM
    return jnp.where(
        lane < half, pltpu.roll(values, width - half, 1), pltpu.roll(values, half, 1)
    )


def joined(refs):
    return jnp.concatenate([r[...] for r in refs], axis=0)


def qkv_body(n, x_ref, cos_ref, sin_ref, *refs):
    weights, outs = refs[: 3 * n], refs[3 * n :]
    rows = x_ref.shape[0]
    tile = outs[0].shape[1]
    for i in range(3):
        weight = joined(weights[i * n : (i + 1) * n])
        for s in range(rows // SEQ):
            span = slice(s * SEQ, (s + 1) * SEQ)
            product = nn(x_ref[span, :], weight)
            if i == 2:
                outs[i][span, :] = product.astype(BF16)
                continue
            for t in range(tile // PAIR):
                here = product[:, t * PAIR : (t + 1) * PAIR]
                turned = here * cos_ref[...] + turn(here) * sin_ref[...]
                outs[i][span, t * PAIR : (t + 1) * PAIR] = turned.astype(BF16)


def project(x, tables, query, key, value):
    rows, model = x.shape
    n, width = len(query), query[0].shape[1]
    tile = min(256, width)
    piece = pl.BlockSpec((model // n, tile), lambda j: (0, j))
    out = pl.BlockSpec((rows, tile), lambda j: (0, j))
    return call(
        functools.partial(qkv_body, n),
        (width // tile,),
        [whole(x.shape), whole((SEQ, PAIR)), whole((SEQ, PAIR))] + [piece] * (3 * n),
        [out] * 3,
        [((rows, width), BF16)] * 3,
        flops=6 * rows * model * width,
        moved=2 * (rows * model + 3 * model * width + 3 * rows * width),
    )(x, *tables, *query, *key, *value)


def gate_body(n, x_ref, *refs):
    gate_w, up_w = refs[:n], refs[n : 2 * n]
    hidden_ref, slope_ref, silu_ref = refs[2 * n :]
    gate_weight, up_weight = joined(gate_w), joined(up_w)
    for s in range(x_ref.shape[0] // SEQ):
        span = slice(s * SEQ, (s + 1) * SEQ)
        gate = nn(x_ref[span, :], gate_weight)
        up = nn(x_ref[span, :], up_weight)
        sigm = jax.nn.sigmoid(gate)
        silu = gate * sigm
        hidden_ref[span, :] = (silu * up).astype(BF16)
        silu_ref[span, :] = silu.astype(BF16)
        slope_ref[span, :] = (up * sigm * (1.0 + gate * (1.0 - sigm))).astype(BF16)


def gate_up(x, gate, up):
    rows, model = x.shape
    n, width = len(gate), gate[0].shape[1]
    tile = min(256, width)
    piece = pl.BlockSpec((model // n, tile), lambda j: (0, j))
    out = pl.BlockSpec((rows, tile), lambda j: (0, j))
    return call(
        functools.partial(gate_body, n),
        (width // tile,),
        [whole(x.shape)] + [piece] * (2 * n),
        [out] * 3,
        [((rows, width), BF16)] * 3,
        flops=4 * rows * model * width,
        moved=2 * (rows * model + 2 * model * width + 3 * rows * width),
    )(x, *gate, *up)


def hidden_back_body(n, steps, g_ref, *refs):
    first, second = refs[:n], refs[n : 2 * n]
    slope_ref, silu_ref, gate_ref, up_ref = refs[2 * n :]

    def work(weights):
        weight = joined(weights)
        for s in range(g_ref.shape[0] // SEQ):
            span = slice(s * SEQ, (s + 1) * SEQ)
            grad = nn(g_ref[span, :], weight)
            gate_ref[span, :] = (grad * slope_ref[span, :].astype(F32)).astype(BF16)
            up_ref[span, :] = (grad * silu_ref[span, :].astype(F32)).astype(BF16)

    @pl.when(pl.program_id(0) < steps)
    def _():
        work(first)

    @pl.when(pl.program_id(0) >= steps)
    def _():
        work(second)


def hidden_back(grads, first, second, slope, silu):
    rows, model = grads.shape
    n, width = len(first), first[0].shape[1]
    tile = min(256, width)
    steps = width // tile
    early = pl.BlockSpec((model // n, tile), lambda j: (0, jnp.minimum(j, steps - 1)))
    late = pl.BlockSpec((model // n, tile), lambda j: (0, jnp.maximum(j - steps, 0)))
    out = pl.BlockSpec((rows, tile), lambda j: (0, j))
    return call(
        functools.partial(hidden_back_body, n, steps),
        (2 * steps,),
        [whole(grads.shape)] + [early] * n + [late] * n + [out] * 2,
        [out] * 2,
        [((rows, 2 * width), BF16)] * 2,
        flops=4 * rows * model * width,
        moved=2 * (rows * model + 2 * model * width + 8 * rows * width),
    )(grads, *first, *second, slope, silu)


def mixed_back_body(n, g_ref, *refs):
    weight = joined(refs[:n])
    refs[n][...] = nn(g_ref[...], weight).astype(BF16)


def mixed_back(grads, out):
    rows, model = grads.shape
    n, width = len(out), out[0].shape[1]
    tile = min(256, width)
    piece = pl.BlockSpec((model // n, tile), lambda j: (0, j))
    return call(
        functools.partial(mixed_back_body, n),
        (width // tile,),
        [whole(grads.shape)] + [piece] * n,
        [pl.BlockSpec((rows, tile), lambda j: (0, j))],
        [((rows, width), BF16)],
        flops=2 * rows * model * width,
        moved=2 * (rows * model + model * width + rows * width),
    )(grads, *out)[0]


def trans_body(n, parts, *refs):
    lefts = refs[:parts]
    pieces = refs[parts : parts * (n + 1)]
    out_ref, held, sems = refs[parts * (n + 1) :]
    j = pl.program_id(0)
    width = held.shape[3]

    def copy(i, p, slot):
        source = pieces[p * n + i]
        return pltpu.make_async_copy(source, held.at[slot, p], sems.at[slot, p])

    def fetch(step, slot):
        for i in range(n):

            @pl.when(step == i)
            def _():
                for p in range(parts):
                    copy(i, p, slot).start()

    @pl.when(j == 0)
    def _():
        fetch(j, 0)

    @pl.when(j + 1 < n)
    def _():
        fetch(j + 1, (j + 1) % 2)

    slot = j % 2
    for p in range(parts):
        copy(0, p, slot).wait()
    rows = out_ref.shape[0]
    for s in range(rows // SEQ):
        span = slice(s * SEQ, (s + 1) * SEQ)
        total = nt(lefts[0][span, :], held[slot, 0])
        for p in range(1, parts):
            total += nt(lefts[p][span, :], held[slot, p])
        out_ref[span, :] = total.astype(BF16)


def times_trans(parts):
    rows = parts[0][0].shape[0]
    n = len(parts[0][2])
    piece_rows, width = parts[0][2][0].shape
    model = n * piece_rows
    ins = [
        pl.BlockSpec((rows, width), functools.partial(lambda b, j: (0, b), start // width))
        for _, start, _ in parts
    ]
    ins += [pl.BlockSpec(memory_space=pl.ANY)] * (n * len(parts))
    return call(
        functools.partial(trans_body, n, len(parts)),
        (n,),
        ins,
        [pl.BlockSpec((rows, piece_rows), lambda j: (0, j))],
        [((rows, model), BF16)],
        flops=2 * rows * model * width * len(parts),
        scratch=[
            pltpu.VMEM((2, len(parts), piece_rows, width), BF16),
            pltpu.SemaphoreType.DMA((2, len(parts))),
        ],
        moved=2 * (rows * model + len(parts) * (rows + model) * width),
    )(*[left for left, _, _ in parts], *[w for _, _, pieces in parts for w in pieces])[0]


def grad_body(parts, got, left_ref, *refs):
    rights, gots, outs = refs[:parts], refs[parts : parts * (1 + got)], refs[parts * (1 + got) :]
    turned = outs[parts]

    @pl.when(pl.program_id(0) == 0)
    def _():
        turned[...] = left_ref[...].T

    for i in range(parts):
        total = nn(turned[...], rights[i][...])
        if got:
            total += gots[i][...].astype(F32)
        outs[i][...] = total.astype(BF16)


def weight_grads(left, which, rights, gots=()):
    rows, model = left.shape
    half = model // 2
    parts = len(rights)
    width = rights[0][2]
    tile = min(512, width)
    out = pl.BlockSpec((half, tile), lambda j: (0, j))
    ins = [pl.BlockSpec((rows, half), lambda j: (0, which))]
    for _, start, _ in rights:
        ins.append(
            pl.BlockSpec((rows, tile), functools.partial(lambda b, j: (0, b + j), start // tile))
        )
    return call(
        functools.partial(grad_body, parts, 1 if gots else 0),
        (width // tile,),
        ins + [out] * len(gots),
        [out] * parts,
        [((half, width), BF16)] * parts,
        flops=2 * rows * half * width * parts,
        scratch=[pltpu.VMEM((half, rows), BF16)],
        moved=2 * (rows * half + parts * (rows + half) * width),
    )(left, *[right for right, _, _ in rights], *gots)


def causal(scores):
    past = scores.shape[0] - HALF_SEQ
    key = lax.broadcasted_iota(jnp.int32, (HALF_SEQ, HALF_SEQ), 0)
    query = lax.broadcasted_iota(jnp.int32, (HALF_SEQ, HALF_SEQ), 1)
    last = jnp.where(key <= query, scores[past:], -1e30)
    return last if past == 0 else jnp.concatenate([scores[:past], last], axis=0)


def head_of(h):
    return slice(h * HEAD_DIM, (h + 1) * HEAD_DIM)


def span_of(b):
    return slice(b * HALF_SEQ, (b + 1) * HALF_SEQ)


def attend_body(q_ref, k_ref, v_ref, out_ref, sum_ref):
    values = v_ref[...].astype(F32).T.astype(BF16)
    heads = []
    for h in range(2):
        blocks = []
        for b in range(2):
            reach = (b + 1) * HALF_SEQ
            query = q_ref[span_of(b), head_of(h)] * BF16(FACTOR)
            scores = causal(nt(k_ref[:reach, head_of(h)], query))
            top = jnp.max(scores, axis=0, keepdims=True)
            expo = jnp.exp(scores - top)
            total = jnp.sum(expo, axis=0, keepdims=True)
            mixed = nn(values[head_of(h), :reach], expo.astype(BF16))
            blocks.append(mixed * (1.0 / total))
            sum_ref[0, 0, h : h + 1, span_of(b)] = top + jnp.log(total)
        heads.append(jnp.concatenate(blocks, axis=1))
    out_ref[...] = jnp.concatenate(heads, axis=0).T.astype(BF16)


def attend(query, key, value):
    rows, width = query.shape
    seqs, pairs = rows // SEQ, width // PAIR
    tile = pl.BlockSpec((SEQ, PAIR), lambda s, p: (s, p))
    return call(
        attend_body,
        (seqs, pairs),
        [tile] * 3,
        [tile, pl.BlockSpec((1, 1, 2, SEQ), lambda s, p: (s, p, 0, 0))],
        [((rows, width), BF16), ((seqs, pairs, 2, SEQ), F32)],
        flops=16 * rows * width * SEQ,
        moved=8 * rows * width,
    )(query, key, value)


def attend_back_body(q_ref, k_ref, v_ref, g_ref, sum_ref, cos_ref, sin_ref, dq_ref, dk_ref, dv_ref):
    keys = k_ref[...].astype(F32).T.astype(BF16)
    dq_heads, dk_heads, dv_heads = [], [], []
    for h in range(2):
        dq, dk, dv = [], [], []
        for b in range(2):
            reach = (b + 1) * HALF_SEQ
            query = q_ref[span_of(b), head_of(h)]
            grad = g_ref[span_of(b), head_of(h)]
            scores = causal(nt(k_ref[:reach, head_of(h)], query * BF16(FACTOR)))
            probs = jnp.exp(scores - sum_ref[0, 0, h : h + 1, span_of(b)])
            probs_grad = nt(v_ref[:reach, head_of(h)], grad)
            inner = jnp.sum(probs * probs_grad, axis=0, keepdims=True)
            score_grad = (probs * (probs_grad - inner)).astype(BF16)
            dv.append(nn(probs.astype(BF16), grad))
            dk.append(nn(score_grad, query))
            dq.append(nn(keys[head_of(h), :reach], score_grad))
        for parts, heads in ((dk, dk_heads), (dv, dv_heads)):
            heads.append(
                jnp.concatenate([parts[1][:HALF_SEQ] + parts[0], parts[1][HALF_SEQ:]], axis=0)
            )
        dq_heads.append(jnp.concatenate(dq, axis=1))
    dq = jnp.concatenate(dq_heads, axis=0).T * FACTOR
    dk = jnp.concatenate(dk_heads, axis=1) * FACTOR
    cosine, sine = cos_ref[...], sin_ref[...]
    dq_ref[...] = (dq * cosine - turn(dq) * sine).astype(BF16)
    dk_ref[...] = (dk * cosine - turn(dk) * sine).astype(BF16)
    dv_ref[...] = jnp.concatenate(dv_heads, axis=1).astype(BF16)


def attend_back(query, key, value, grad, logsum, tables):
    rows, width = query.shape
    seqs, pairs = rows // SEQ, width // PAIR
    tile = pl.BlockSpec((SEQ, PAIR), lambda s, p: (s, p))
    return call(
        attend_back_body,
        (seqs, pairs),
        [tile] * 4
        + [pl.BlockSpec((1, 1, 2, SEQ), lambda s, p: (s, p, 0, 0))]
        + [whole((SEQ, PAIR))] * 2,
        [tile] * 3,
        [((rows, width), BF16)] * 3,
        flops=40 * rows * width * SEQ,
        moved=14 * rows * width,
    )(query, key, value, grad, logsum, *tables)


def local(
    ring,
    tokens,
    attn_gain,
    query_weight,
    key_weight,
    value_weight,
    output_weight,
    ffn_gain,
    gate_weight,
    up_weight,
    down_weight,
    cotangent,
):
    line = jnp.asarray(ring.table)[lax.axis_index("dp")]

    def gather_rows(values):
        return lax.all_gather(values, "tensor", axis=0, tiled=True)

    def scatter_rows(values):
        return lax.psum_scatter(values, "tensor", scatter_dimension=0, tiled=True)

    here = down_weight.shape[0] // 2
    weights = ring.gather(
        [
            [
                ("query", query_weight),
                ("key", key_weight),
                ("value", value_weight),
                ("output", output_weight.T),
                ("gains", jnp.stack([attn_gain, ffn_gain])),
            ],
            [("gate", gate_weight), ("up", up_weight)],
            [("down_a", down_weight[:here].T), ("down_b", down_weight[here:].T)],
        ]
    )
    gains = jnp.concatenate(weights["gains"], axis=1).astype(F32)
    tables = rope_tables()

    all_tokens = gather_rows(tokens)
    all_grads = gather_rows(after(cotangent, all_tokens))
    group_one = by_rows(norm_body, line, [all_tokens, gains], [BF16], tile=256)[0]
    query, key, value = project(
        group_one, tables, weights["query"], weights["key"], weights["value"]
    )
    mixed, logsum = attend(query, key, value)
    attended = scatter_rows(times_trans([(mixed, 0, weights["output"])]))
    grad_rows = by_rows(order_body, line, [after(all_grads, mixed)], [BF16], tile=256)[0]
    attended = after(attended, weights["gate"][1], weights["up"][1], grad_rows)
    middle, second = by_rows(middle_body, line, [tokens, attended, gains], [F32, BF16])
    group_two = gather_rows(second)
    hidden, slope, silu = gate_up(group_two, weights["gate"], weights["up"])

    hiddens = [(hidden, 0, here), (hidden, here, here)]
    theirs = weight_grads(grad_rows, 1, hiddens)
    got = [ring.other(value) for value in theirs]
    mine = weight_grads(grad_rows, 0, hiddens, got)
    downs = Sums(ring, mine)
    gate_grad, up_grad = hidden_back(
        after(grad_rows, *mine), weights["down_a"], weights["down_b"], slope, silu
    )
    second_part = times_trans(
        [(after(gate_grad, *downs.step()), 0, weights["gate"]), (up_grad, 0, weights["up"])]
    )
    second_grad = scatter_rows(second_part)
    backs = [(gate_grad, 0, 2 * here), (up_grad, 0, 2 * here)]
    theirs = weight_grads(after(group_two, second_part, *downs.step()), 1, backs)
    got = [ring.other(value) for value in theirs]
    mine = weight_grads(group_two, 0, backs, got)
    lifts = Sums(ring, mine)

    down_a, down_b = downs.finish()
    middle_grad, low_grad = by_rows(
        second_back_body,
        line,
        [cotangent, after(second_grad, down_a, down_b, *mine), middle, gains],
        [F32, BF16],
    )
    attn_grads = gather_rows(low_grad)
    late = after(hidden, low_grad)
    result_part = times_trans([(late, 0, weights["down_a"]), (late, here, weights["down_b"])])

    mixed_grad = mixed_back(
        after(attn_grads, result_part, *lifts.step()), weights["output"]
    )
    result_part = scatter_rows(after(result_part, mixed_grad))
    query_back, key_back, value_back = attend_back(query, key, value, mixed_grad, logsum, tables)
    own = query_weight.shape[1]
    backs = [(query_back, 0, own), (key_back, 0, own), (value_back, 0, own)]
    outs = [(mixed, 0, own)]
    lifted = lifts.step()
    theirs = weight_grads(after(group_one, *lifted), 1, backs) + weight_grads(attn_grads, 1, outs)
    got = [ring.other(value) for value in theirs]
    mine = weight_grads(group_one, 0, backs, got[:3]) + weight_grads(attn_grads, 0, outs, got[3:])
    tails = Sums(ring, mine)
    first_grad = scatter_rows(
        times_trans(
            [
                (after(query_back, *mine), 0, weights["query"]),
                (key_back, 0, weights["key"]),
                (value_back, 0, weights["value"]),
            ]
        )
    )
    gate_sum, up_sum = lifts.finish()
    query_sum, key_sum, value_sum, output_sum = tails.finish()
    layer_out = by_rows(result_body, line, [middle, result_part], [BF16])[0]
    input_grad = by_rows(
        first_back_body, line, [tokens, first_grad, middle_grad, gains], [F32]
    )[0]

    def inner(weight, grad):
        return jnp.sum(weight.astype(F32) * grad, axis=1)

    gain_one_part = (
        inner(query_weight, query_sum) + inner(key_weight, key_sum) + inner(value_weight, value_sum)
    ) / attn_gain.astype(F32)
    gain_two_part = (inner(gate_weight, gate_sum) + inner(up_weight, up_sum)) / ffn_gain.astype(F32)
    gain_one_total, gain_two_total = lax.psum((gain_one_part, gain_two_part), "tensor")
    return (
        layer_out,
        input_grad,
        gain_one_total,
        query_sum,
        key_sum,
        value_sum,
        output_sum.T,
        gain_two_total,
        gate_sum,
        up_sum,
        jnp.concatenate([down_a, down_b], axis=1).T,
    )


def solution(mesh):
    in_specs = (
        P(("dp", "tensor"), None),
        P("dp"),
        P("dp", "tensor"),
        P("dp", "tensor"),
        P("dp", "tensor"),
        P("tensor", "dp"),
        P("dp"),
        P("dp", "tensor"),
        P("dp", "tensor"),
        P("tensor", "dp"),
        P(("dp", "tensor"), None),
    )
    out_specs = (
        P(("dp", "tensor"), None),
        P(("dp", "tensor"), None),
        P("dp"),
        P("dp", "tensor"),
        P("dp", "tensor"),
        P("dp", "tensor"),
        P("tensor", "dp"),
        P("dp"),
        P("dp", "tensor"),
        P("dp", "tensor"),
        P("tensor", "dp"),
    )
    ring = Ring(mesh.shape["dp"])

    def run(*arrays):
        return local(ring, *arrays)

    return jax.shard_map(run, mesh=mesh, in_specs=in_specs, out_specs=out_specs, check_vma=False)
```

```python
import functools

import jax
import jax.numpy as jnp
import numpy as np
from jax import lax
from jax.experimental import pallas as pl
from jax.experimental.pallas import tpu as pltpu
from jax.sharding import PartitionSpec as P

HEAD_DIM = 64
SEQ = 512
EPS = 1e-05
THETA = 130000.0
BF16 = jnp.bfloat16
F32 = jnp.float32
FACTOR = HEAD_DIM**-0.5
PAIR = 2 * HEAD_DIM
HALF_SEQ = SEQ // 2


def ring_order(chips):
    evens = list(range(0, chips, 2))
    odds = list(range(1, chips, 2))
    return [0] + odds + evens[:0:-1]


class Chain:
    def __init__(self):
        self.last = ()

    def tie(self, value):
        return lax.optimization_barrier((value, *self.last))[0]

    def then(self, *values):
        self.last = values

    def gate(self, *values):
        values = lax.optimization_barrier((*values, *self.last))[: len(values)]
        self.last = values[:1]
        return values


class Ring:
    def __init__(self, size):
        self.size = size
        self.chips = size // 2
        order = ring_order(self.chips)
        follow = {order[i]: order[(i + 1) % self.chips] for i in range(self.chips)}
        place = {chip: i for i, chip in enumerate(order)}
        self.forward = [(2 * c + k, 2 * follow[c] + k) for c in range(self.chips) for k in (0, 1)]
        self.swap = [(i, i ^ 1) for i in range(size)]
        table = []
        for i in range(size):
            chip, core = i // 2, i % 2
            line = [order[(place[chip] - k) % self.chips] for k in range(self.chips)]
            table.append([2 * c + core for c in line] + [2 * c + 1 - core for c in line])
        self.table = np.array(table, np.int32)

    def step(self, value):
        return lax.ppermute(value, "dp", self.forward)

    def other(self, value):
        return lax.ppermute(value, "dp", self.swap)


class Gather:
    def __init__(self, ring, chain, *pieces):
        self.ring, self.chain = ring, chain
        self.own = [[piece] for piece in pieces]
        self.others = [[] for _ in pieces]
        self.flying = None

    def start(self):
        for own, others in zip(self.own, self.others):
            others.append(self.ring.other(own[-1]))
        if len(self.own[0]) < self.ring.chips:
            self.flying = [self.ring.step(own[-1]) for own in self.own]
        else:
            self.flying = None

    def end(self):
        for own, got in zip(self.own, self.chain.gate(*self.flying)):
            own.append(got)
        self.start()

    def finish(self):
        while self.flying:
            self.end()
        return [own + others for own, others in zip(self.own, self.others)]


class Sums:
    def __init__(self, ring, chain, *mine):
        self.ring, self.chain = ring, chain
        self.blocks = [m.reshape(ring.chips, -1, m.shape[-1]) for m in mine]
        self.held = [b[1 % ring.chips] for b in self.blocks]
        self.k = 0
        self.start()

    def start(self):
        self.flying = [self.ring.step(h) for h in self.held]
        self.k += 1

    def end(self):
        last = self.k == self.ring.chips - 1
        block = (self.k + 1) % self.ring.chips
        got = self.chain.gate(*self.flying)
        totals = [g.astype(F32) + b[block].astype(F32) for g, b in zip(got, self.blocks)]
        self.held = totals if last else [t.astype(BF16) for t in totals]
        self.chain.then(*self.held)
        if last:
            self.flying = None
        else:
            self.start()

    def finish(self):
        while self.flying:
            self.end()
        return self.held


class Group:
    def __init__(self, links, axes):
        self.links, self.axes = links, axes
        self.bits = len(links)
        self.size = 1 << self.bits
        self.orders = (list(range(self.bits)), list(range(self.bits))[::-1])

    def send(self, value, bit):
        return lax.ppermute(value, self.axes, self.links[bit])


class Spread:
    def __init__(self, group, chain, halves):
        self.group, self.chain = group, chain
        self.held = [{0: half} for half in halves]
        self.wave, self.flying = 0, {}
        self.fresh = [[0] for _ in halves]
        self.start()

    def start(self):
        for h, order in enumerate(self.group.orders):
            for k in self.fresh[h]:
                used = [i for i, bit in enumerate(order) if k >> bit & 1]
                for i in range(max(used, default=-1) + 1, len(order)):
                    block = self.group.send(self.held[h][k], order[i])
                    self.flying[h, k | 1 << order[i]] = (block, i)

    def end(self):
        self.wave += 1
        last = self.wave == self.group.bits
        keys = [
            key
            for key, (_, i) in self.flying.items()
            if last or (i < self.group.bits - 1 and bin(key[1]).count("1") == self.wave)
        ]
        got = self.chain.gate(*[self.flying.pop(key)[0] for key in keys])
        self.fresh = [[], []]
        for (h, k), block in zip(keys, got):
            self.held[h][k] = block
            self.fresh[h].append(k)
        if not last:
            self.start()

    def finish(self):
        while self.wave < self.group.bits:
            self.end()
        return [[held[k] for k in range(self.group.size)] for held in self.held]


class Fold:
    def __init__(self, group, chain, halves):
        self.group, self.chain = group, chain
        self.held = [list(half) for half in halves]
        self.parts = [[half[0]] for half in halves]
        self.wave, self.flying = 0, []
        self.start()

    def start(self):
        place = self.group.bits - 1 - self.wave
        for h, order in enumerate(self.group.orders):
            bit = order[place]
            later = sum(1 << b for b in order[place + 1 :])
            for k in reversed(range(self.group.size)):
                if k >> bit & 1 and not k & later:
                    self.flying.append((h, k ^ 1 << bit, self.group.send(self.held[h][k], bit)))

    def end(self):
        self.wave += 1
        last = self.wave == self.group.bits
        now = [f for f in self.flying if last or f[1]]
        self.flying = [f for f in self.flying if not (last or f[1])]
        got = self.chain.gate(*[block for _, _, block in now])
        for (h, k, _), block in zip(now, got):
            if k:
                total = self.held[h][k].astype(F32) + block.astype(F32)
                self.held[h][k] = total.astype(BF16)
            else:
                self.parts[h].append(block)
        if not last:
            self.start()

    def finish(self):
        while self.wave < self.group.bits:
            self.end()
        return self.parts


def nn(left, right):
    return lax.dot_general(left, right, (((1,), (0,)), ((), ())), preferred_element_type=F32)


def nt(left, right):
    return lax.dot_general(left, right, (((1,), (1,)), ((), ())), preferred_element_type=F32)


def tn(left, right):
    return lax.dot_general(left, right, (((0,), (0,)), ((), ())), preferred_element_type=F32)


VMEM_LIMIT = 56 << 20
COST_SHARE = 16


def call(body, grid, ins, outs, shapes, flops, scratch=(), prefetch=0, moved=0):
    return pl.pallas_call(
        body,
        grid_spec=pltpu.PrefetchScalarGridSpec(
            num_scalar_prefetch=prefetch,
            grid=grid,
            in_specs=ins,
            out_specs=outs,
            scratch_shapes=list(scratch),
        ),
        out_shape=[jax.ShapeDtypeStruct(s, t) for s, t in shapes],
        compiler_params=pltpu.CompilerParams(
            vmem_limit_bytes=VMEM_LIMIT, dimension_semantics=("arbitrary",) * len(grid)
        ),
        cost_estimate=pl.CostEstimate(
            flops=flops // COST_SHARE, bytes_accessed=moved // COST_SHARE, transcendentals=0
        ),
    )


def whole(shape):
    return pl.BlockSpec(shape, lambda *_: (0,) * len(shape))


def place(line_ref, j, width):
    return pl.ds(pl.multiple_of(line_ref[j] * width, 128), width)


def cut(width, j):
    return slice(j * width, (j + 1) * width)


def scale_of(values):
    return lax.rsqrt(jnp.mean(values * values, axis=-1, keepdims=True) + EPS)


def norm_body(blocks, n, line_ref, gain_ref, *refs):
    out_ref = refs[2 * n]
    width = out_ref.shape[1] // blocks
    half = out_ref.shape[1] // 2

    for k in range(n):

        @pl.when(pl.program_id(0) == k)
        def _():
            whole_ref = refs[2 * n + 1]
            whole_ref[:, :half] = refs[k][...]
            whole_ref[:, half:] = refs[n + k][...]

    x_ref = refs[2 * n + 1]
    scale = scale_of(x_ref[...].astype(F32))
    for j in range(blocks):
        part = x_ref[:, place(line_ref, j, width)].astype(F32)
        gain = gain_ref[0:1, cut(width, j)]
        out_ref[:, cut(width, j)] = (part * scale * gain).astype(BF16)


def order_body(blocks, n, line_ref, gain_ref, *refs):
    out_ref, whole_ref = refs[2 * n :]
    width = out_ref.shape[1] // blocks
    half = out_ref.shape[1] // 2

    for k in range(n):

        @pl.when(pl.program_id(0) == k)
        def _():
            whole_ref[:, :half] = refs[k][...]
            whole_ref[:, half:] = refs[n + k][...]

    for j in range(blocks):
        out_ref[:, cut(width, j)] = whole_ref[:, place(line_ref, j, width)]


def ordered(body, line, gains, halves):
    first, second = halves
    n = len(first)
    rows, half = first[0].shape
    model = 2 * half
    return call(
        functools.partial(body, line.shape[0], n),
        (n,),
        [whole(gains.shape)] + [whole((rows, half))] * (2 * n),
        [pl.BlockSpec((rows, model), lambda k, *_: (k, 0))],
        [((n * rows, model), BF16)],
        flops=20 * n * rows * model,
        scratch=[pltpu.VMEM((rows, model), BF16)],
        prefetch=1,
        moved=4 * n * rows * model,
    )(line, gains, *first, *second)[0]


def added(refs, span):
    total = refs[0][span, :].astype(F32)
    for ref in refs[1:]:
        total += ref[span, :].astype(F32)
    return total


def middle_body(blocks, m, line_ref, x_ref, gain_ref, *refs):
    middle_ref, low_ref, high_ref = refs[2 * m :]
    width = x_ref.shape[1] // blocks
    half = x_ref.shape[1] // 2
    span = slice(None)
    middle_ref[:, :half] = added(refs[:m], span)
    middle_ref[:, half:] = added(refs[m : 2 * m], span)
    for j in range(blocks):
        here = x_ref[:, place(line_ref, j, width)].astype(F32)
        middle_ref[:, cut(width, j)] += here
    middle = middle_ref[...]
    normed = (middle * scale_of(middle) * gain_ref[1:2, :]).astype(BF16)
    low_ref[...] = normed[:, :half]
    high_ref[...] = normed[:, half:]


def result_body(blocks, m, line_ref, middle_ref, gain_ref, *refs):
    out_ref = refs[2 * m]
    width = middle_ref.shape[1] // blocks
    span = slice(None)
    total = middle_ref[...] + jnp.concatenate(
        [added(refs[:m], span), added(refs[m : 2 * m], span)], axis=1
    )
    for j in range(blocks):
        out_ref[:, place(line_ref, j, width)] = total[:, cut(width, j)].astype(BF16)


def second_back_body(blocks, m, line_ref, dy_ref, gain_ref, *refs):
    middle_ref, out_ref, low_ref, high_ref = refs[2 * m :]
    width = dy_ref.shape[1] // blocks
    half = dy_ref.shape[1] // 2
    span = slice(None)
    grad = jnp.concatenate([added(refs[:m], span), added(refs[m : 2 * m], span)], axis=1)
    middle = middle_ref[...]
    scale = scale_of(middle)
    normed = middle * scale
    scaled = grad * gain_ref[1:2, :]
    out_ref[...] = scale * (scaled - normed * jnp.mean(scaled * normed, axis=-1, keepdims=True))
    for j in range(blocks):
        out_ref[:, cut(width, j)] += dy_ref[:, place(line_ref, j, width)].astype(F32)
    low_ref[...] = out_ref[:, :half].astype(BF16)
    high_ref[...] = out_ref[:, half:].astype(BF16)


def first_back_body(blocks, m, line_ref, x_ref, gain_ref, *refs):
    above_ref, out_ref = refs[2 * m :]
    width = x_ref.shape[1] // blocks
    span = slice(None)
    scale = scale_of(x_ref[...].astype(F32))
    normed = jnp.concatenate(
        [x_ref[:, place(line_ref, j, width)].astype(F32) for j in range(blocks)], axis=1
    ) * scale
    grad = jnp.concatenate([added(refs[:m], span), added(refs[m : 2 * m], span)], axis=1)
    scaled = grad * gain_ref[0:1, :]
    back = scale * (scaled - normed * jnp.mean(scaled * normed, axis=-1, keepdims=True))
    total = above_ref[...] + back
    for j in range(blocks):
        out_ref[:, place(line_ref, j, width)] = total[:, cut(width, j)]


def by_rows(body, line, first, gains, parts, more, kinds):
    rows, model = first.shape
    half = model // 2
    tile = min(128, rows)
    row = pl.BlockSpec((tile, model), lambda i, *_: (i, 0))
    slim = pl.BlockSpec((tile, half), lambda i, *_: (i, 0))
    m = len(parts[0])
    return call(
        functools.partial(body, line.shape[0], m),
        (rows // tile,),
        [row, whole(gains.shape)] + [slim] * (2 * m) + [row] * len(more),
        [slim if narrow else row for _, narrow in kinds],
        [((rows, half if narrow else model), kind) for kind, narrow in kinds],
        flops=20 * rows * model,
        prefetch=1,
        moved=rows * model * (2 * m + 4 * len(kinds)),
    )(line, first, gains, *parts[0], *parts[1], *more)


def rope_tables(place):
    half = HEAD_DIM // 2
    freq = THETA ** (-2.0 * jnp.arange(half, dtype=F32) / HEAD_DIM)
    angle = place.astype(F32)[:, None] * freq[None, :]
    cosine, sine = jnp.cos(angle), jnp.sin(angle)
    return (
        jnp.concatenate([cosine] * (PAIR // half), axis=1),
        jnp.concatenate([-sine, sine] * (PAIR // HEAD_DIM), axis=1),
    )


def turn(values):
    half = HEAD_DIM // 2
    width = values.shape[-1]
    lane = lax.broadcasted_iota(jnp.int32, values.shape, 1) % HEAD_DIM
    return jnp.where(
        lane < half, pltpu.roll(values, width - half, 1), pltpu.roll(values, half, 1)
    )


def joined(refs):
    return jnp.concatenate([r[...] for r in refs], axis=0)


def qkv_body(n, x_ref, cos_ref, sin_ref, *refs):
    weights, outs = refs[: 3 * n], refs[3 * n :]
    rows = x_ref.shape[0]
    tile = outs[0].shape[1]
    for i in range(3):
        weight = joined(weights[i * n : (i + 1) * n])
        for s in range(rows // SEQ):
            span = slice(s * SEQ, (s + 1) * SEQ)
            product = nn(x_ref[span, :], weight)
            if i == 2:
                outs[i][span, :] = product.astype(BF16)
                continue
            for t in range(tile // PAIR):
                here = product[:, t * PAIR : (t + 1) * PAIR]
                turned = here * cos_ref[...] + turn(here) * sin_ref[...]
                outs[i][span, t * PAIR : (t + 1) * PAIR] = turned.astype(BF16)


def project(x, tables, query, key, value):
    rows, model = x.shape
    n, width = len(query), query[0].shape[1]
    tile = min(256, width)
    piece = pl.BlockSpec((model // n, tile), lambda j: (0, j))
    out = pl.BlockSpec((rows, tile), lambda j: (0, j))
    return call(
        functools.partial(qkv_body, n),
        (width // tile,),
        [whole(x.shape), whole((SEQ, PAIR)), whole((SEQ, PAIR))] + [piece] * (3 * n),
        [out] * 3,
        [((rows, width), BF16)] * 3,
        flops=6 * rows * model * width,
        moved=2 * (rows * model + 3 * model * width + 3 * rows * width),
    )(x, *tables, *query, *key, *value)


def collect(pieces, held, sem):
    n = len(pieces) // 2
    rows, half = pieces[0].shape
    copies = []
    for h in range(2):
        for k in range(n):
            target = held.at[pl.ds(k * rows, rows), pl.ds(h * half, half)]
            copies.append(pltpu.make_async_copy(pieces[h * n + k], target, sem.at[h * n + k]))
    for copy in copies:
        copy.start()
    for copy in copies:
        copy.wait()


def rows_specs(halves):
    n = 2 * len(halves[0])
    rows, half = halves[0][0].shape
    scratch = [
        pltpu.VMEM((len(halves[0]) * rows, 2 * half), BF16),
        pltpu.SemaphoreType.DMA((n,)),
    ]
    return [pl.BlockSpec(memory_space=pl.ANY)] * n, scratch


def gate_body(n, m, *refs):
    gate_w, up_w = refs[m : m + n], refs[m + n : m + 2 * n]
    hidden_ref, slope_ref, silu_ref, x_ref, sem = refs[m + 2 * n :]

    @pl.when(pl.program_id(0) == 0)
    def _():
        collect(refs[:m], x_ref, sem)

    gate_weight, up_weight = joined(gate_w), joined(up_w)
    for s in range(x_ref.shape[0] // SEQ):
        span = slice(s * SEQ, (s + 1) * SEQ)
        gate = nn(x_ref[span, :], gate_weight)
        up = nn(x_ref[span, :], up_weight)
        sigm = jax.nn.sigmoid(gate)
        silu = gate * sigm
        hidden_ref[span, :] = (silu * up).astype(BF16)
        silu_ref[span, :] = silu.astype(BF16)
        slope_ref[span, :] = (up * sigm * (1.0 + gate * (1.0 - sigm))).astype(BF16)


def gate_up(halves, gate, up):
    specs, scratch = rows_specs(halves)
    rows, model = scratch[0].shape
    n, width = len(gate), gate[0].shape[1]
    tile = min(256, width)
    piece = pl.BlockSpec((model // n, tile), lambda j: (0, j))
    out = pl.BlockSpec((rows, tile), lambda j: (0, j))
    return call(
        functools.partial(gate_body, n, len(specs)),
        (width // tile,),
        specs + [piece] * (2 * n),
        [out] * 3,
        [((rows, width), BF16)] * 3,
        flops=4 * rows * model * width,
        scratch=scratch,
        moved=2 * (rows * model + 2 * model * width + 3 * rows * width),
    )(*halves[0], *halves[1], *gate, *up)


def hidden_back_body(n, steps, g_ref, *refs):
    first, second = refs[:n], refs[n : 2 * n]
    slope_ref, silu_ref, gate_ref, up_ref = refs[2 * n :]

    def work(weights):
        weight = joined(weights)
        for s in range(g_ref.shape[0] // SEQ):
            span = slice(s * SEQ, (s + 1) * SEQ)
            grad = nn(g_ref[span, :], weight)
            gate_ref[span, :] = (grad * slope_ref[span, :].astype(F32)).astype(BF16)
            up_ref[span, :] = (grad * silu_ref[span, :].astype(F32)).astype(BF16)

    @pl.when(pl.program_id(0) < steps)
    def _():
        work(first)

    @pl.when(pl.program_id(0) >= steps)
    def _():
        work(second)


def hidden_back(grads, first, second, slope, silu):
    rows, model = grads.shape
    n, width = len(first), first[0].shape[1]
    tile = min(256, width)
    steps = width // tile
    early = pl.BlockSpec((model // n, tile), lambda j: (0, jnp.minimum(j, steps - 1)))
    late = pl.BlockSpec((model // n, tile), lambda j: (0, jnp.maximum(j - steps, 0)))
    out = pl.BlockSpec((rows, tile), lambda j: (0, j))
    return call(
        functools.partial(hidden_back_body, n, steps),
        (2 * steps,),
        [whole(grads.shape)] + [early] * n + [late] * n + [out] * 2,
        [out] * 2,
        [((rows, 2 * width), BF16)] * 2,
        flops=4 * rows * model * width,
        moved=2 * (rows * model + 2 * model * width + 8 * rows * width),
    )(grads, *first, *second, slope, silu)


def mixed_back_body(n, m, *refs):
    out_ref, x_ref, sem = refs[m + n :]

    @pl.when(pl.program_id(0) == 0)
    def _():
        collect(refs[:m], x_ref, sem)

    out_ref[...] = nn(x_ref[...], joined(refs[m : m + n])).astype(BF16)


def mixed_back(halves, out):
    specs, scratch = rows_specs(halves)
    rows, model = scratch[0].shape
    n, width = len(out), out[0].shape[1]
    tile = min(256, width)
    piece = pl.BlockSpec((model // n, tile), lambda j: (0, j))
    return call(
        functools.partial(mixed_back_body, n, len(specs)),
        (width // tile,),
        specs + [piece] * n,
        [pl.BlockSpec((rows, tile), lambda j: (0, j))],
        [((rows, width), BF16)],
        flops=2 * rows * model * width,
        scratch=scratch,
        moved=2 * (rows * model + model * width + rows * width),
    )(*halves[0], *halves[1], *out)[0]


def trans_body(n, parts, blocks, *refs):
    lefts = refs[:parts]
    pieces = refs[parts : parts * (n + 1)]
    outs = refs[parts * (n + 1) : -2]
    held, sems = refs[-2:]
    j = pl.program_id(0)
    width = held.shape[3]

    def copy(i, p, slot):
        source = pieces[p * n + i]
        return pltpu.make_async_copy(source, held.at[slot, p], sems.at[slot, p])

    def fetch(step, slot):
        for i in range(n):

            @pl.when(step == i)
            def _():
                for p in range(parts):
                    copy(i, p, slot).start()

    @pl.when(j == 0)
    def _():
        fetch(j, 0)

    @pl.when(j + 1 < n)
    def _():
        fetch(j + 1, (j + 1) % 2)

    slot = j % 2
    for p in range(parts):
        copy(0, p, slot).wait()
    rows = outs[0].shape[0]
    for s in range(blocks * rows // SEQ):
        span = slice(s * SEQ, (s + 1) * SEQ)
        total = nt(lefts[0][span, :], held[slot, 0])
        for p in range(1, parts):
            total += nt(lefts[p][span, :], held[slot, p])
        total = total.astype(BF16)
        for h in range(2):

            @pl.when((j >= n // 2) == (h == 1))
            def _():
                for i in range(SEQ // rows):
                    outs[h * blocks + s * (SEQ // rows) + i][...] = total[cut(rows, i)]


def times_trans(parts, blocks):
    rows = parts[0][0].shape[0]
    n = len(parts[0][2])
    piece_rows, width = parts[0][2][0].shape
    model = n * piece_rows
    ins = [
        pl.BlockSpec((rows, width), functools.partial(lambda b, j: (0, b), start // width))
        for _, start, _ in parts
    ]
    ins += [pl.BlockSpec(memory_space=pl.ANY)] * (n * len(parts))
    outs = call(
        functools.partial(trans_body, n, len(parts), blocks),
        (n,),
        ins,
        [pl.BlockSpec((rows // blocks, piece_rows), lambda j: (0, jnp.minimum(j, n // 2 - 1)))] * blocks
        + [pl.BlockSpec((rows // blocks, piece_rows), lambda j: (0, jnp.maximum(j - n // 2, 0)))] * blocks,
        [((rows // blocks, model // 2), BF16)] * (2 * blocks),
        flops=2 * rows * model * width * len(parts),
        scratch=[
            pltpu.VMEM((2, len(parts), piece_rows, width), BF16),
            pltpu.SemaphoreType.DMA((2, len(parts))),
        ],
        moved=2 * (rows * model + len(parts) * (rows + model) * width),
    )(*[left for left, _, _ in parts], *[w for _, _, pieces in parts for w in pieces])
    return outs[:blocks], outs[blocks:]


def grad_body(parts, got, blocks, *refs):
    lefts, refs = refs[:blocks], refs[blocks:]
    rights, gots, outs = refs[:parts], refs[parts : parts * (1 + got)], refs[parts * (1 + got) :]
    turned = outs[parts]
    rows = lefts[0].shape[0]

    @pl.when(pl.program_id(0) == 0)
    def _():
        for k in range(blocks):
            turned[:, cut(rows, k)] = lefts[k][...].T

    for i in range(parts):
        total = nn(turned[...], rights[i][...])
        if got:
            total += gots[i][...].astype(F32)
        outs[i][...] = total.astype(BF16)


def weight_grads(left, which, rights, gots=()):
    rows = rights[0][0].shape[0]
    parts = len(rights)
    width = rights[0][2]
    tile = min(512, width)
    if isinstance(left, (list, tuple)):
        lefts = left[which]
        blocks, half = len(lefts), lefts[0].shape[1]
        ins = [whole(lefts[0].shape)] * blocks
    else:
        blocks, half = 1, left.shape[1] // 2
        lefts = [left]
        ins = [pl.BlockSpec((rows, half), lambda j: (0, which))]
    out = pl.BlockSpec((half, tile), lambda j: (0, j))
    for _, start, _ in rights:
        ins.append(
            pl.BlockSpec((rows, tile), functools.partial(lambda b, j: (0, b + j), start // tile))
        )
    return call(
        functools.partial(grad_body, parts, 1 if gots else 0, blocks),
        (width // tile,),
        ins + [out] * len(gots),
        [out] * parts,
        [((half, width), BF16)] * parts,
        flops=2 * rows * half * width * parts,
        scratch=[pltpu.VMEM((half, rows), BF16)],
        moved=2 * (rows * half + parts * (rows + half) * width),
    )(*lefts, *[right for right, _, _ in rights], *gots)


def causal(scores):
    past = scores.shape[0] - HALF_SEQ
    key = lax.broadcasted_iota(jnp.int32, (HALF_SEQ, HALF_SEQ), 0)
    query = lax.broadcasted_iota(jnp.int32, (HALF_SEQ, HALF_SEQ), 1)
    last = jnp.where(key <= query, scores[past:], -1e30)
    return last if past == 0 else jnp.concatenate([scores[:past], last], axis=0)


def head_of(h):
    return slice(h * HEAD_DIM, (h + 1) * HEAD_DIM)


def span_of(b):
    return slice(b * HALF_SEQ, (b + 1) * HALF_SEQ)


def in_place(shift_ref, ref, count):
    rows = SEQ // count
    spans = [pl.ds(pl.multiple_of((i ^ shift_ref[0]) * rows, rows), rows) for i in range(count)]
    return jnp.concatenate([ref[span, :] for span in spans], axis=0)


def put_back(shift_ref, ref, count, values):
    rows = SEQ // count
    for i in range(count):
        ref[pl.ds(pl.multiple_of((i ^ shift_ref[0]) * rows, rows), rows), :] = values[cut(rows, i)]


def attend_body(count, shift_ref, q_ref, k_ref, v_ref, out_ref, sum_ref):
    queries, keys = in_place(shift_ref, q_ref, count), in_place(shift_ref, k_ref, count)
    values = in_place(shift_ref, v_ref, count).astype(F32).T.astype(BF16)
    heads = []
    for h in range(2):
        blocks = []
        for b in range(2):
            reach = (b + 1) * HALF_SEQ
            query = queries[span_of(b), head_of(h)] * BF16(FACTOR)
            scores = causal(nt(keys[:reach, head_of(h)], query))
            top = jnp.max(scores, axis=0, keepdims=True)
            expo = jnp.exp(scores - top)
            total = jnp.sum(expo, axis=0, keepdims=True)
            mixed = nn(values[head_of(h), :reach], expo.astype(BF16))
            blocks.append(mixed * (1.0 / total))
            sum_ref[0, 0, h : h + 1, span_of(b)] = top + jnp.log(total)
        heads.append(jnp.concatenate(blocks, axis=1))
    put_back(shift_ref, out_ref, count, jnp.concatenate(heads, axis=0).T.astype(BF16))


def attend(shift, count, query, key, value):
    rows, width = query.shape
    seqs, pairs = rows // SEQ, width // PAIR
    tile = pl.BlockSpec((SEQ, PAIR), lambda s, p, _: (s, p))
    return call(
        functools.partial(attend_body, count),
        (seqs, pairs),
        [tile] * 3,
        [tile, pl.BlockSpec((1, 1, 2, SEQ), lambda s, p, _: (s, p, 0, 0))],
        [((rows, width), BF16), ((seqs, pairs, 2, SEQ), F32)],
        flops=16 * rows * width * SEQ,
        prefetch=1,
        moved=8 * rows * width,
    )(shift, query, key, value)


def attend_back_body(
    count, shift_ref, q_ref, k_ref, v_ref, g_ref, sum_ref, cos_ref, sin_ref, dq_ref, dk_ref, dv_ref
):
    queries, keys, values, grads = (
        in_place(shift_ref, ref, count) for ref in (q_ref, k_ref, v_ref, g_ref)
    )
    turned = keys.astype(F32).T.astype(BF16)
    dq_heads, dk_heads, dv_heads = [], [], []
    for h in range(2):
        dq, dk, dv = [], [], []
        for b in range(2):
            reach = (b + 1) * HALF_SEQ
            query = queries[span_of(b), head_of(h)]
            grad = grads[span_of(b), head_of(h)]
            scores = causal(nt(keys[:reach, head_of(h)], query * BF16(FACTOR)))
            probs = jnp.exp(scores - sum_ref[0, 0, h : h + 1, span_of(b)])
            probs_grad = nt(values[:reach, head_of(h)], grad)
            inner = jnp.sum(probs * probs_grad, axis=0, keepdims=True)
            score_grad = (probs * (probs_grad - inner)).astype(BF16)
            dv.append(nn(probs.astype(BF16), grad))
            dk.append(nn(score_grad, query))
            dq.append(nn(turned[head_of(h), :reach], score_grad))
        for parts, heads in ((dk, dk_heads), (dv, dv_heads)):
            heads.append(
                jnp.concatenate([parts[1][:HALF_SEQ] + parts[0], parts[1][HALF_SEQ:]], axis=0)
            )
        dq_heads.append(jnp.concatenate(dq, axis=1))
    dq = jnp.concatenate(dq_heads, axis=0).T * FACTOR
    dk = jnp.concatenate(dk_heads, axis=1) * FACTOR
    dv = jnp.concatenate(dv_heads, axis=1).astype(BF16)
    cosine, sine = cos_ref[...], sin_ref[...]
    put_back(shift_ref, dq_ref, count, (dq * cosine - turn(dq) * sine).astype(BF16))
    put_back(shift_ref, dk_ref, count, (dk * cosine - turn(dk) * sine).astype(BF16))
    put_back(shift_ref, dv_ref, count, dv)


def attend_back(shift, count, query, key, value, grad, logsum, tables):
    rows, width = query.shape
    seqs, pairs = rows // SEQ, width // PAIR
    tile = pl.BlockSpec((SEQ, PAIR), lambda s, p, _: (s, p))
    return call(
        functools.partial(attend_back_body, count),
        (seqs, pairs),
        [tile] * 4
        + [pl.BlockSpec((1, 1, 2, SEQ), lambda s, p, _: (s, p, 0, 0))]
        + [whole((SEQ, PAIR))] * 2,
        [tile] * 3,
        [((rows, width), BF16)] * 3,
        flops=40 * rows * width * SEQ,
        prefetch=1,
        moved=14 * rows * width,
    )(shift, query, key, value, grad, logsum, *tables)


def local(
    ring,
    group,
    tokens,
    attn_gain,
    query_weight,
    key_weight,
    value_weight,
    output_weight,
    ffn_gain,
    gate_weight,
    up_weight,
    down_weight,
    cotangent,
):
    line = jnp.asarray(ring.table)[lax.axis_index("dp")]
    rows, model = tokens.shape
    count = SEQ // rows
    blocks = group.size
    shift = lax.axis_index("tensor") % count
    row = jnp.arange(SEQ, dtype=jnp.int32)
    places = rope_tables(row)
    tables = rope_tables((row // rows ^ shift) * rows + row % rows)
    shift = jnp.reshape(shift, (1,)).astype(jnp.int32)
    here = down_weight.shape[0] // 2
    own = query_weight.shape[1]
    chain = Chain()

    def halves(values):
        return values[:, : model // 2], values[:, model // 2 :]

    spread = Spread(group, chain, halves(tokens))
    attn = Gather(
        ring,
        chain,
        query_weight,
        key_weight,
        value_weight,
        output_weight.T,
        jnp.stack([attn_gain, ffn_gain]),
    )
    attn.start()
    spread.end()
    attn.end()
    all_tokens = spread.finish()
    spread = Spread(group, chain, [chain.tie(half) for half in halves(cotangent)])
    while len(attn.own[0]) < ring.chips - 1:
        attn.end()
    gate = Gather(ring, chain, chain.tie(gate_weight))
    gate.start()
    spread.end()
    w_query, w_key, w_value, w_output, gains = attn.finish()
    up = Gather(ring, chain, chain.tie(up_weight))
    up.start()
    gains = jnp.concatenate(gains, axis=1).astype(F32)

    group_one = ordered(norm_body, line, chain.tie(gains), all_tokens)
    chain.then(group_one)
    query, key, value = project(group_one, tables, w_query, w_key, w_value)
    mixed, logsum = attend(shift, count, query, key, value)
    chain.then(mixed)
    gate.end()
    out_part = times_trans([(chain.tie(mixed), 0, w_output)], blocks)
    chain.then(*out_part[0], *out_part[1])
    up.end()
    fold = Fold(group, chain, [[chain.tie(v) for v in half] for half in out_part])
    all_grads = spread.finish()
    grad_rows = ordered(order_body, line, chain.tie(gains), all_grads)
    chain.then(grad_rows)
    fold.end()
    gate.end()
    attended = fold.finish()
    middle, *second = by_rows(
        middle_body, line, chain.tie(tokens), gains, attended, [], [(F32, 0), (BF16, 1), (BF16, 1)]
    )
    chain.then(*second)
    spread = Spread(group, chain, second)
    up.end()
    spread.end()
    (w_gate,) = gate.finish()
    down_one = Gather(ring, chain, chain.tie(down_weight[:here].T))
    down_one.start()
    group_two = spread.finish()
    (w_up,) = up.finish()
    down_two = Gather(ring, chain, chain.tie(down_weight[here:].T))
    down_two.start()
    group_two[0][0] = chain.tie(group_two[0][0])
    hidden, slope, silu = gate_up(group_two, w_gate, w_up)
    chain.then(hidden)
    down_one.end()
    down_two.end()

    hiddens = [(hidden, 0, here), (hidden, here, here)]
    theirs = weight_grads(chain.tie(grad_rows), 1, hiddens)
    got = [ring.other(value) for value in theirs]
    chain.then(*theirs)
    down_one.end()
    mine = weight_grads(chain.tie(grad_rows), 0, hiddens, got)
    chain.then(*mine)
    down_two.end()
    downs = Sums(ring, chain, *[chain.tie(value) for value in mine])
    (w_down_one,), (w_down_two,) = down_one.finish(), down_two.finish()
    gate_grad, up_grad = hidden_back(chain.tie(grad_rows), w_down_one, w_down_two, slope, silu)
    chain.then(gate_grad, up_grad)
    downs.end()
    second_part = times_trans([(chain.tie(gate_grad), 0, w_gate), (up_grad, 0, w_up)], blocks)
    chain.then(*second_part[0], *second_part[1])
    downs.end()
    fold = Fold(group, chain, [[chain.tie(v) for v in half] for half in second_part])
    backs = [(gate_grad, 0, 2 * here), (up_grad, 0, 2 * here)]
    theirs = weight_grads(group_two, 1, [(chain.tie(gate_grad), 0, 2 * here), backs[1]])
    got = [ring.other(value) for value in theirs]
    chain.then(*theirs)
    fold.end()
    mine = weight_grads(group_two, 0, [(chain.tie(gate_grad), 0, 2 * here), backs[1]], got)
    chain.then(*mine)
    gates, ups = Sums(ring, chain, mine[0]), Sums(ring, chain, mine[1])
    down_a, down_b = downs.finish()
    second_grad = fold.finish()
    middle_grad, *low_grad = by_rows(
        second_back_body,
        line,
        chain.tie(cotangent),
        gains,
        second_grad,
        [middle],
        [(F32, 0), (BF16, 1), (BF16, 1)],
    )
    chain.then(*low_grad)
    spread = Spread(group, chain, low_grad)
    result_part = times_trans(
        [(chain.tie(hidden), 0, w_down_one), (hidden, here, w_down_two)], blocks
    )
    chain.then(*result_part[0], *result_part[1])
    spread.end()
    gates.end()
    attn_grads = spread.finish()
    fold = Fold(group, chain, [[chain.tie(v) for v in half] for half in result_part])
    ups.end()

    attn_grads[0][0] = chain.tie(attn_grads[0][0])
    mixed_grad = mixed_back(attn_grads, w_output)
    query_back, key_back, value_back = attend_back(
        shift, count, query, key, value, mixed_grad, logsum, places
    )
    chain.then(query_back)
    fold.end()
    gates.end()
    backs = [(query_back, 0, own), (key_back, 0, own), (value_back, 0, own)]
    outs = [(mixed, 0, own)]
    theirs = weight_grads(chain.tie(group_one), 1, backs) + weight_grads(attn_grads, 1, outs)
    got = [ring.other(value) for value in theirs]
    chain.then(*theirs)
    ups.end()
    mine = weight_grads(chain.tie(group_one), 0, backs, got[:3])
    mine += weight_grads(attn_grads, 0, outs, got[3:])
    chain.then(*mine)
    result_part = fold.finish()
    (gate_sum,) = gates.finish()
    tails = Sums(ring, chain, *[chain.tie(value) for value in mine])
    first_part = times_trans(
        [(chain.tie(query_back), 0, w_query), (key_back, 0, w_key), (value_back, 0, w_value)], blocks
    )
    chain.then(*first_part[0], *first_part[1])
    (up_sum,) = ups.finish()
    fold = Fold(group, chain, [[chain.tie(v) for v in half] for half in first_part])
    (layer_out,) = by_rows(
        result_body, line, chain.tie(middle), gains, result_part, [], [(BF16, 0)]
    )
    chain.then(layer_out)
    fold.end()
    tails.end()
    first_grad = fold.finish()
    (input_grad,) = by_rows(
        first_back_body, line, chain.tie(tokens), gains, first_grad, [middle_grad], [(F32, 0)]
    )
    chain.then(input_grad)
    query_sum, key_sum, value_sum, output_sum = tails.finish()

    def inner(weight, grad):
        return jnp.sum(weight.astype(F32) * grad, axis=1)

    gain_one_part = (
        inner(query_weight, query_sum) + inner(key_weight, key_sum) + inner(value_weight, value_sum)
    ) / attn_gain.astype(F32)
    gain_two_part = (inner(gate_weight, gate_sum) + inner(up_weight, up_sum)) / ffn_gain.astype(F32)
    gain_one_total, gain_two_total = lax.psum((gain_one_part, gain_two_part), "tensor")
    return (
        layer_out,
        input_grad,
        gain_one_total,
        query_sum,
        key_sum,
        value_sum,
        output_sum.T,
        gain_two_total,
        gate_sum,
        up_sum,
        jnp.concatenate([down_a, down_b], axis=1).T,
    )


def solution(mesh):
    in_specs = (
        P(("dp", "tensor"), None),
        P("dp"),
        P("dp", "tensor"),
        P("dp", "tensor"),
        P("dp", "tensor"),
        P("tensor", "dp"),
        P("dp"),
        P("dp", "tensor"),
        P("dp", "tensor"),
        P("tensor", "dp"),
        P(("dp", "tensor"), None),
    )
    out_specs = (
        P(("dp", "tensor"), None),
        P(("dp", "tensor"), None),
        P("dp"),
        P("dp", "tensor"),
        P("dp", "tensor"),
        P("dp", "tensor"),
        P("tensor", "dp"),
        P("dp"),
        P("dp", "tensor"),
        P("dp", "tensor"),
        P("tensor", "dp"),
    )
    ring = Ring(mesh.shape["dp"])
    size = mesh.shape["tensor"]
    links = [[(i, i ^ 1 << b) for i in range(size)] for b in range(size.bit_length() - 1)]
    group = Group(links, "tensor")

    def run(*arrays):
        return local(ring, group, *arrays)

    return jax.shard_map(run, mesh=mesh, in_specs=in_specs, out_specs=out_specs, check_vma=False)
```

```python
import functools

import jax
import jax.numpy as jnp
import numpy as np
from jax import lax
from jax.experimental import pallas as pl
from jax.experimental.pallas import tpu as pltpu
from jax.sharding import PartitionSpec as P

HEAD_DIM = 64
SEQ = 512
EPS = 1e-05
THETA = 130000.0
BF16 = jnp.bfloat16
F32 = jnp.float32
FACTOR = HEAD_DIM**-0.5
PAIR = 2 * HEAD_DIM
HALF_SEQ = SEQ // 2


def ring_order(chips):
    evens = list(range(0, chips, 2))
    odds = list(range(1, chips, 2))
    return [0] + odds + evens[:0:-1]


class Chain:
    def __init__(self):
        self.last = ()

    def tie(self, value):
        return lax.optimization_barrier((value, *self.last))[0]

    def then(self, *values):
        self.last = values

    def gate(self, *values):
        values = lax.optimization_barrier((*values, *self.last))[: len(values)]
        self.last = values[:1]
        return values


class Ring:
    def __init__(self, size):
        self.size = size
        self.chips = size // 2
        order = ring_order(self.chips)
        follow = {order[i]: order[(i + 1) % self.chips] for i in range(self.chips)}
        place = {chip: i for i, chip in enumerate(order)}
        self.forward = [(2 * c + k, 2 * follow[c] + k) for c in range(self.chips) for k in (0, 1)]
        self.swap = [(i, i ^ 1) for i in range(size)]
        table = []
        for i in range(size):
            chip, core = i // 2, i % 2
            line = [order[(place[chip] - k) % self.chips] for k in range(self.chips)]
            table.append([2 * c + core for c in line] + [2 * c + 1 - core for c in line])
        self.table = np.array(table, np.int32)

    def step(self, value):
        return lax.ppermute(value, "dp", self.forward)

    def other(self, value):
        return lax.ppermute(value, "dp", self.swap)


class Gather:
    def __init__(self, ring, chain, piece):
        self.ring, self.chain = ring, chain
        self.own, self.others = [piece], []
        self.left = ring.chips - 1
        self.start()

    def start(self):
        self.flying = self.ring.step(self.own[-1]) if self.left else None
        self.others.append(self.ring.other(self.own[-1]))

    def down_to(self, left):
        while self.left > left:
            self.left -= 1
            got, self.others[-1] = self.chain.gate(self.flying, self.others[-1])
            self.own.append(got)
            self.start()

    def pieces(self):
        self.down_to(0)
        return self.own + self.others


class Sums:
    def __init__(self, ring, chain, mine):
        self.ring, self.chain = ring, chain
        self.blocks = mine.reshape(ring.chips, -1, mine.shape[-1])
        self.held = self.blocks[1 % ring.chips]
        self.left = ring.chips - 1
        self.flying = ring.step(self.held)

    def down_to(self, left):
        while self.left > left:
            self.left -= 1
            (got,) = self.chain.gate(self.flying)
            block = self.blocks[(self.ring.chips - self.left) % self.ring.chips]
            total = got.astype(F32) + block.astype(F32)
            self.held = total.astype(BF16) if self.left else total
            self.chain.then(self.held)
            if self.left:
                self.flying = self.ring.step(self.held)

    def total(self):
        self.down_to(0)
        return self.held


class Group:
    def __init__(self, links, axes):
        self.links, self.axes = links, axes
        self.bits = len(links)
        self.size = 1 << self.bits
        self.orders = (list(range(self.bits)), list(range(self.bits))[::-1])

    def send(self, value, bit):
        return lax.ppermute(value, self.axes, self.links[bit])

    def messages(self):
        found = []
        for order in self.orders:
            found.append([])
            for top in reversed(range(self.bits)):
                found[-1].append(
                    [
                        1 << order[top] | sum(1 << order[p] for p in range(top) if v >> p & 1)
                        for v in range(1 << top)
                    ]
                )
        return found


class Spread:
    def __init__(self, group, chain, rows):
        self.group, self.chain = group, chain
        self.held = {0: [rows]}
        self.wave = 0
        self.flying = {(1 << b, None): group.send(rows, b) for b in range(group.bits)}

    def end(self):
        self.wave += 1
        got = self.chain.gate(*self.flying.values())
        fresh = list(zip(self.flying, got))
        self.flying = {}
        for (k, h), block in fresh:
            if h is None:
                self.held[k] = [block]
            else:
                self.held.setdefault(k, [None, None])[h] = block
        if self.wave == self.group.bits:
            return
        for (k, h), block in fresh:
            for way, order in enumerate(self.group.orders):
                if h is not None and h != way:
                    continue
                half = block.shape[1] // 2
                top = max(i for i, bit in enumerate(order) if k >> bit & 1)
                for i in range(top + 1, len(order)):
                    part = block if h is not None else block[:, way * half : (way + 1) * half]
                    self.flying[k | 1 << order[i], way] = self.group.send(part, order[i])

    def blocks(self):
        while self.wave < self.group.bits:
            self.end()
        return [self.held[k] for k in range(self.group.size)]


class Fold:
    def __init__(self, group, chain, own, sent):
        self.group, self.chain = group, chain
        self.rows = own[0].shape[0]
        self.sent = [list(half) for half in sent]
        self.parts = [[half] for half in own]
        self.wave = 0
        self.start()

    def start(self):
        self.flying = [
            self.group.send(self.sent[h][self.wave], order[self.group.bits - 1 - self.wave])
            for h, order in enumerate(self.group.orders)
        ]

    def end(self):
        got = self.chain.gate(*self.flying)
        self.wave += 1
        for h, block in enumerate(got):
            self.parts[h].append(block)
            for wave in range(self.wave, self.group.bits):
                first = self.rows << (self.group.bits - 1 - wave)
                more = block[first : 2 * first].astype(F32)
                self.sent[h][wave] = (self.sent[h][wave].astype(F32) + more).astype(BF16)
        if self.wave < self.group.bits:
            self.start()

    def total(self):
        while self.wave < self.group.bits:
            self.end()
        return self.parts


class Weight:
    def __init__(self, pieces, rows, start, width):
        self.pieces, self.rows, self.start, self.width = pieces, rows, start, width
        self.model = len(pieces) * rows

    def tiles(self, tile):
        first = self.start // tile
        return [pl.BlockSpec((self.rows, tile), lambda j: (0, first + j))] * len(self.pieces)


def nn(left, right):
    return lax.dot_general(left, right, (((1,), (0,)), ((), ())), preferred_element_type=F32)


def nt(left, right):
    return lax.dot_general(left, right, (((1,), (1,)), ((), ())), preferred_element_type=F32)


def tn(left, right):
    return lax.dot_general(left, right, (((0,), (0,)), ((), ())), preferred_element_type=F32)


VMEM_LIMIT = 56 << 20
COST_SHARE = 16


def call(body, grid, ins, outs, shapes, flops, scratch=(), prefetch=0, moved=0):
    return pl.pallas_call(
        body,
        grid_spec=pltpu.PrefetchScalarGridSpec(
            num_scalar_prefetch=prefetch,
            grid=grid,
            in_specs=ins,
            out_specs=outs,
            scratch_shapes=list(scratch),
        ),
        out_shape=[jax.ShapeDtypeStruct(s, t) for s, t in shapes],
        compiler_params=pltpu.CompilerParams(
            vmem_limit_bytes=VMEM_LIMIT, dimension_semantics=("arbitrary",) * len(grid)
        ),
        cost_estimate=pl.CostEstimate(
            flops=flops // COST_SHARE, bytes_accessed=moved // COST_SHARE, transcendentals=0
        ),
    )


def whole(shape):
    return pl.BlockSpec(shape, lambda *_: (0,) * len(shape))


def place(line_ref, j, width):
    return pl.ds(pl.multiple_of(line_ref[j] * width, 128), width)


def cut(width, j):
    return slice(j * width, (j + 1) * width)


def scale_of(values):
    return lax.rsqrt(jnp.mean(values * values, axis=-1, keepdims=True) + EPS)


def fetch_blocks(counts, refs, held, sems, k, slot, wait):
    first = 0
    for i, count in enumerate(counts):
        copies = []
        half = held.shape[2] // count
        for h in range(count):
            target = held.at[slot, :, pl.ds(h * half, half)]
            copies.append(pltpu.make_async_copy(refs[first + h], target, sems.at[slot, h]))
        first += count

        @pl.when(k == i)
        def _():
            for copy in copies:
                copy.wait() if wait else copy.start()


def fetched(counts, refs, held, sems):
    k = pl.program_id(0)

    @pl.when(k == 0)
    def _():
        fetch_blocks(counts, refs, held, sems, k, 0, False)

    fetch_blocks(counts, refs, held, sems, k + 1, (k + 1) % 2, False)
    fetch_blocks(counts, refs, held, sems, k, k % 2, True)
    return held.at[k % 2]


def norm_body(blocks, counts, line_ref, gain_ref, *refs):
    out_ref, held, sems = refs[sum(counts) :]
    x_ref = fetched(counts, refs, held, sems)
    width = out_ref.shape[1] // blocks
    scale = scale_of(x_ref[...].astype(F32))
    for j in range(blocks):
        part = x_ref[:, place(line_ref, j, width)].astype(F32)
        gain = gain_ref[0:1, cut(width, j)]
        out_ref[:, cut(width, j)] = (part * scale * gain).astype(BF16)


def order_body(blocks, counts, line_ref, gain_ref, *refs):
    out_ref, held, sems = refs[sum(counts) :]
    x_ref = fetched(counts, refs, held, sems)
    width = out_ref.shape[1] // blocks
    for j in range(blocks):
        out_ref[:, cut(width, j)] = x_ref[:, place(line_ref, j, width)]


def ordered(body, line, gains, held):
    counts = [len(block) for block in held]
    rows, model = held[0][0].shape
    n = len(held)
    return call(
        functools.partial(body, line.shape[0], counts),
        (n,),
        [whole(gains.shape)] + [pl.BlockSpec(memory_space=pl.ANY)] * sum(counts),
        [pl.BlockSpec((rows, model), lambda k, *_: (k, 0))],
        [((n * rows, model), BF16)],
        flops=20 * n * rows * model,
        scratch=[pltpu.VMEM((2, rows, model), BF16), pltpu.SemaphoreType.DMA((2, 2))],
        prefetch=1,
        moved=4 * n * rows * model,
    )(line, gains, *[array for block in held for array in block])[0]


def added(refs, span):
    total = refs[0][span, :].astype(F32)
    for ref in refs[1:]:
        total += ref[span, :].astype(F32)
    return total


def middle_body(blocks, m, line_ref, x_ref, gain_ref, *refs):
    middle_ref, out_ref = refs[2 * m :]
    width = x_ref.shape[1] // blocks
    half = x_ref.shape[1] // 2
    span = slice(None)
    middle_ref[:, :half] = added(refs[:m], span)
    middle_ref[:, half:] = added(refs[m : 2 * m], span)
    for j in range(blocks):
        here = x_ref[:, place(line_ref, j, width)].astype(F32)
        middle_ref[:, cut(width, j)] += here
    middle = middle_ref[...]
    out_ref[...] = (middle * scale_of(middle) * gain_ref[1:2, :]).astype(BF16)


def result_body(blocks, m, line_ref, middle_ref, gain_ref, *refs):
    out_ref = refs[2 * m]
    width = middle_ref.shape[1] // blocks
    span = slice(None)
    total = middle_ref[...] + jnp.concatenate(
        [added(refs[:m], span), added(refs[m : 2 * m], span)], axis=1
    )
    for j in range(blocks):
        out_ref[:, place(line_ref, j, width)] = total[:, cut(width, j)].astype(BF16)


def second_back_body(blocks, m, line_ref, dy_ref, gain_ref, *refs):
    middle_ref, out_ref, low_ref = refs[2 * m :]
    width = dy_ref.shape[1] // blocks
    span = slice(None)
    grad = jnp.concatenate([added(refs[:m], span), added(refs[m : 2 * m], span)], axis=1)
    middle = middle_ref[...]
    scale = scale_of(middle)
    normed = middle * scale
    scaled = grad * gain_ref[1:2, :]
    out_ref[...] = scale * (scaled - normed * jnp.mean(scaled * normed, axis=-1, keepdims=True))
    for j in range(blocks):
        out_ref[:, cut(width, j)] += dy_ref[:, place(line_ref, j, width)].astype(F32)
    low_ref[...] = out_ref[...].astype(BF16)


def first_back_body(blocks, m, line_ref, x_ref, gain_ref, *refs):
    above_ref, out_ref = refs[2 * m :]
    width = x_ref.shape[1] // blocks
    span = slice(None)
    scale = scale_of(x_ref[...].astype(F32))
    normed = jnp.concatenate(
        [x_ref[:, place(line_ref, j, width)].astype(F32) for j in range(blocks)], axis=1
    ) * scale
    grad = jnp.concatenate([added(refs[:m], span), added(refs[m : 2 * m], span)], axis=1)
    scaled = grad * gain_ref[0:1, :]
    back = scale * (scaled - normed * jnp.mean(scaled * normed, axis=-1, keepdims=True))
    total = above_ref[...] + back
    for j in range(blocks):
        out_ref[:, place(line_ref, j, width)] = total[:, cut(width, j)]


def by_rows(body, line, first, gains, parts, more, kinds):
    rows, model = first.shape
    half = model // 2
    tile = min(128, rows)
    row = pl.BlockSpec((tile, model), lambda i, *_: (i, 0))
    slim = pl.BlockSpec((tile, half), lambda i, *_: (i, 0))
    m = len(parts[0])
    return call(
        functools.partial(body, line.shape[0], m),
        (rows // tile,),
        [row, whole(gains.shape)] + [slim] * (2 * m) + [row] * len(more),
        [row] * len(kinds),
        [((rows, model), kind) for kind in kinds],
        flops=20 * rows * model,
        prefetch=1,
        moved=rows * model * (2 * m + 4 * len(kinds)),
    )(line, first, gains, *parts[0], *parts[1], *more)


def rope_tables(place):
    half = HEAD_DIM // 2
    freq = THETA ** (-2.0 * jnp.arange(half, dtype=F32) / HEAD_DIM)
    angle = place.astype(F32)[:, None] * freq[None, :]
    cosine, sine = jnp.cos(angle), jnp.sin(angle)
    return (
        jnp.concatenate([cosine] * (PAIR // half), axis=1),
        jnp.concatenate([-sine, sine] * (PAIR // HEAD_DIM), axis=1),
    )


def turn(values):
    half = HEAD_DIM // 2
    width = values.shape[-1]
    lane = lax.broadcasted_iota(jnp.int32, values.shape, 1) % HEAD_DIM
    return jnp.where(
        lane < half, pltpu.roll(values, width - half, 1), pltpu.roll(values, half, 1)
    )


def joined(refs):
    return jnp.concatenate([r[...] for r in refs], axis=0)


def qkv_body(n, x_ref, cos_ref, sin_ref, *refs):
    weights, outs = refs[: 3 * n], refs[3 * n :]
    rows = x_ref.shape[0]
    tile = outs[0].shape[1]
    for i in range(3):
        weight = joined(weights[i * n : (i + 1) * n])
        for s in range(rows // SEQ):
            span = slice(s * SEQ, (s + 1) * SEQ)
            product = nn(x_ref[span, :], weight)
            if i == 2:
                outs[i][span, :] = product.astype(BF16)
                continue
            for t in range(tile // PAIR):
                here = product[:, t * PAIR : (t + 1) * PAIR]
                turned = here * cos_ref[...] + turn(here) * sin_ref[...]
                outs[i][span, t * PAIR : (t + 1) * PAIR] = turned.astype(BF16)


def project(x, tables, query, key, value):
    rows, model = x.shape
    n, width = len(query.pieces), query.width
    tile = min(256, width)
    out = pl.BlockSpec((rows, tile), lambda j: (0, j))
    return call(
        functools.partial(qkv_body, n),
        (width // tile,),
        [whole(x.shape), whole((SEQ, PAIR)), whole((SEQ, PAIR))]
        + query.tiles(tile)
        + key.tiles(tile)
        + value.tiles(tile),
        [out] * 3,
        [((rows, width), BF16)] * 3,
        flops=6 * rows * model * width,
        moved=2 * (rows * model + 3 * model * width + 3 * rows * width),
    )(x, *tables, *query.pieces, *key.pieces, *value.pieces)


def collect(counts, refs, held, sems):
    rows = held.shape[0] // len(counts)
    copies = []
    for k, count in enumerate(counts):
        half = held.shape[1] // count
        for h in range(count):
            target = held.at[pl.ds(k * rows, rows), pl.ds(h * half, half)]
            i = len(copies)
            copies.append(pltpu.make_async_copy(refs[i], target, sems.at[i]))
    for copy in copies:
        copy.start()
    for copy in copies:
        copy.wait()


def gate_body(n, counts, *refs):
    m = sum(counts)
    gate_w, up_w = refs[m : m + n], refs[m + n : m + 2 * n]
    hidden_ref, slope_ref, silu_ref, x_ref, sems = refs[m + 2 * n :]

    @pl.when(pl.program_id(0) == 0)
    def _():
        collect(counts, refs, x_ref, sems)

    gate_weight, up_weight = joined(gate_w), joined(up_w)
    for s in range(x_ref.shape[0] // SEQ):
        span = slice(s * SEQ, (s + 1) * SEQ)
        gate = nn(x_ref[span, :], gate_weight)
        up = nn(x_ref[span, :], up_weight)
        sigm = jax.nn.sigmoid(gate)
        silu = gate * sigm
        hidden_ref[span, :] = (silu * up).astype(BF16)
        silu_ref[span, :] = silu.astype(BF16)
        slope_ref[span, :] = (up * sigm * (1.0 + gate * (1.0 - sigm))).astype(BF16)


def collected(held):
    counts = [len(block) for block in held]
    rows, model = held[0][0].shape
    scratch = [
        pltpu.VMEM((len(held) * rows, model), BF16),
        pltpu.SemaphoreType.DMA((sum(counts),)),
    ]
    arrays = [array for block in held for array in block]
    return counts, arrays, [pl.BlockSpec(memory_space=pl.ANY)] * len(arrays), scratch


def gate_up(held, gate, up):
    counts, arrays, specs, scratch = collected(held)
    rows, model = scratch[0].shape
    n, width = len(gate.pieces), gate.width
    tile = min(256, width)
    out = pl.BlockSpec((rows, tile), lambda j: (0, j))
    return call(
        functools.partial(gate_body, n, counts),
        (width // tile,),
        specs + gate.tiles(tile) + up.tiles(tile),
        [out] * 3,
        [((rows, width), BF16)] * 3,
        flops=4 * rows * model * width,
        scratch=scratch,
        moved=2 * (rows * model + 2 * model * width + 3 * rows * width),
    )(*arrays, *gate.pieces, *up.pieces)


def hidden_back_body(n, g_ref, *refs):
    weight = joined(refs[:n])
    slope_ref, silu_ref, gate_ref, up_ref = refs[n:]
    for s in range(g_ref.shape[0] // SEQ):
        span = slice(s * SEQ, (s + 1) * SEQ)
        grad = nn(g_ref[span, :], weight)
        gate_ref[span, :] = (grad * slope_ref[span, :].astype(F32)).astype(BF16)
        up_ref[span, :] = (grad * silu_ref[span, :].astype(F32)).astype(BF16)


def hidden_back(grads, down, slope, silu):
    rows, model = grads.shape
    n, width = len(down.pieces), down.width
    tile = min(256, width)
    out = pl.BlockSpec((rows, tile), lambda j: (0, j))
    return call(
        functools.partial(hidden_back_body, n),
        (width // tile,),
        [whole(grads.shape)] + down.tiles(tile) + [out] * 2,
        [out] * 2,
        [((rows, width), BF16)] * 2,
        flops=2 * rows * model * width,
        moved=2 * (rows * model + model * width + 4 * rows * width),
    )(grads, *down.pieces, slope, silu)


def mixed_back_body(n, counts, *refs):
    m = sum(counts)
    out_ref, x_ref, sems = refs[m + n :]

    @pl.when(pl.program_id(0) == 0)
    def _():
        collect(counts, refs, x_ref, sems)

    out_ref[...] = nn(x_ref[...], joined(refs[m : m + n])).astype(BF16)


def mixed_back(held, out):
    counts, arrays, specs, scratch = collected(held)
    rows, model = scratch[0].shape
    n, width = len(out.pieces), out.width
    tile = min(256, width)
    return call(
        functools.partial(mixed_back_body, n, counts),
        (width // tile,),
        specs + out.tiles(tile),
        [pl.BlockSpec((rows, tile), lambda j: (0, j))],
        [((rows, width), BF16)],
        flops=2 * rows * model * width,
        scratch=scratch,
        moved=2 * (rows * model + model * width + rows * width),
    )(*arrays, *out.pieces)[0]


def trans_body(n, starts, targets, *refs):
    parts, blocks = len(starts), len(targets[0])
    lefts = refs[:parts]
    pieces = refs[parts : parts * (n + 1)]
    outs = refs[parts * (n + 1) : -4]
    held, ready, sems, out_sems = refs[-4:]
    j = pl.program_id(0)
    depth, width = held.shape[2:]
    rows = ready.shape[1] // blocks

    def copy(i, p, slot):
        source = pieces[p * n + i].at[pl.ds(0, depth), pl.ds(starts[p], width)]
        return pltpu.make_async_copy(source, held.at[slot, p], sems.at[slot, p])

    def fetch(step, slot):
        for i in range(n):

            @pl.when(step == i)
            def _():
                for p in range(parts):
                    copy(i, p, slot).start()

    def leave(slot, k, array, first, column):
        target = outs[array].at[pl.ds(first, rows), pl.ds(column, depth)]
        source = ready.at[slot, pl.ds(k * rows, rows), :]
        return pltpu.make_async_copy(source, target, out_sems.at[slot, k])

    def left(slot):
        for k in range(blocks):
            leave(slot, k, 0, 0, 0).wait()

    @pl.when(j == 0)
    def _():
        fetch(j, 0)

    @pl.when(j + 1 < n)
    def _():
        fetch(j + 1, (j + 1) % 2)

    slot = j % 2
    for p in range(parts):
        copy(0, p, slot).wait()

    @pl.when(j >= 2)
    def _():
        left(slot)

    for s in range(blocks * rows // SEQ):
        span = slice(s * SEQ, (s + 1) * SEQ)
        total = nt(lefts[0][span, :], held[slot, 0])
        for p in range(1, parts):
            total += nt(lefts[p][span, :], held[slot, p])
        ready[slot, span, :] = total.astype(BF16)
    column = pl.multiple_of(j % (n // 2) * depth, 128)
    for h in range(2):

        @pl.when((j >= n // 2) == (h == 1))
        def _():
            for k, (array, first) in enumerate(targets[h]):
                leave(slot, k, array, first, column).start()

    @pl.when(j == n - 1)
    def _():
        left(1 - slot)
        left(slot)


def times_trans(parts, group):
    weights = [weight for _, weight in parts]
    n, depth, width = len(weights[0].pieces), weights[0].rows, weights[0].width
    rows = parts[0][0].shape[0]
    half = weights[0].model // 2
    size = rows // group.size
    messages = group.messages()
    shapes = [((size, half), BF16)] * 2
    targets = [{0: (0, 0)}, {0: (1, 0)}]
    for h in range(2):
        for keys in messages[h]:
            for i, k in enumerate(keys):
                targets[h][k] = (len(shapes), i * size)
            shapes.append(((len(keys) * size, half), BF16))
    targets = [[t[k] for k in range(group.size)] for t in targets]
    anywhere = pl.BlockSpec(memory_space=pl.ANY)
    outs = call(
        functools.partial(trans_body, n, [weight.start for weight in weights], targets),
        (n,),
        [whole((rows, width))] * len(parts) + [anywhere] * (n * len(parts)),
        [anywhere] * len(shapes),
        shapes,
        flops=4 * rows * half * width * len(parts),
        scratch=[
            pltpu.VMEM((2, len(parts), depth, width), BF16),
            pltpu.VMEM((2, rows, depth), BF16),
            pltpu.SemaphoreType.DMA((2, len(parts))),
            pltpu.SemaphoreType.DMA((2, group.size)),
        ],
        moved=2 * (2 * rows * half + len(parts) * (rows + 2 * half) * width),
    )(*[left for left, _ in parts], *[piece for weight in weights for piece in weight.pieces])
    m = group.bits
    return outs[:2], [outs[2 : 2 + m], outs[2 + m :]]


def grad_body(parts, got, blocks, steps, *refs):
    lefts, refs = refs[:blocks], refs[blocks:]
    rights, refs = refs[:parts], refs[parts:]
    got_ref = refs[0] if got else None
    out_ref, turned = refs[got:]
    j = pl.program_id(0)

    @pl.when(j == 0)
    def _():
        rows = turned.shape[1] // blocks
        for k in range(blocks):
            turned[:, cut(rows, k)] = lefts[k][...].T

    for i in range(parts):

        @pl.when((j >= i * steps) & (j < (i + 1) * steps))
        def _():
            total = nn(turned[...], rights[i][...])
            if got:
                total += got_ref[...].astype(F32)
            out_ref[...] = total.astype(BF16)


def weight_grads(left, which, rights, got=None):
    rows, width = rights[0].shape
    parts = len(rights)
    tile = min(512, width)
    steps = width // tile
    if isinstance(left, list):
        lefts = [block[0] if len(block) == 1 else block[which] for block in left]
        half = left[0][0].shape[1] // 2
        places = [which if len(block) == 1 else 0 for block in left]
    else:
        lefts, places, half = [left], [which], left.shape[1] // 2
    blocks = len(lefts)
    ins = [
        pl.BlockSpec((rows // blocks, half), functools.partial(lambda at, j: (0, at), at))
        for at in places
    ]
    for i in range(parts):
        ins.append(
            pl.BlockSpec(
                (rows, tile),
                functools.partial(
                    lambda first, j: (0, jnp.clip(j - first, 0, steps - 1)), i * steps
                ),
            )
        )
    out = pl.BlockSpec((half, tile), lambda j: (0, j))
    more = [] if got is None else [got]
    return call(
        functools.partial(grad_body, parts, len(more), blocks, steps),
        (parts * steps,),
        ins + [out] * len(more),
        [out],
        [((half, parts * width), BF16)],
        flops=2 * rows * half * width * parts,
        scratch=[pltpu.VMEM((half, rows), BF16)],
        moved=2 * (rows * half + parts * (rows + half) * width),
    )(*lefts, *rights, *more)[0]


def causal(scores):
    past = scores.shape[0] - HALF_SEQ
    key = lax.broadcasted_iota(jnp.int32, (HALF_SEQ, HALF_SEQ), 0)
    query = lax.broadcasted_iota(jnp.int32, (HALF_SEQ, HALF_SEQ), 1)
    last = jnp.where(key <= query, scores[past:], -1e30)
    return last if past == 0 else jnp.concatenate([scores[:past], last], axis=0)


def head_of(h):
    return slice(h * HEAD_DIM, (h + 1) * HEAD_DIM)


def span_of(b):
    return slice(b * HALF_SEQ, (b + 1) * HALF_SEQ)


def in_place(shift_ref, ref, count):
    rows = SEQ // count
    spans = [pl.ds(pl.multiple_of((i ^ shift_ref[0]) * rows, rows), rows) for i in range(count)]
    return jnp.concatenate([ref[span, :] for span in spans], axis=0)


def put_back(shift_ref, ref, count, values):
    rows = SEQ // count
    for i in range(count):
        ref[pl.ds(pl.multiple_of((i ^ shift_ref[0]) * rows, rows), rows), :] = values[cut(rows, i)]


def attend_body(count, shift_ref, q_ref, k_ref, v_ref, out_ref, sum_ref):
    queries, keys = in_place(shift_ref, q_ref, count), in_place(shift_ref, k_ref, count)
    values = in_place(shift_ref, v_ref, count).astype(F32).T.astype(BF16)
    heads = []
    for h in range(2):
        blocks = []
        for b in range(2):
            reach = (b + 1) * HALF_SEQ
            query = queries[span_of(b), head_of(h)] * BF16(FACTOR)
            scores = causal(nt(keys[:reach, head_of(h)], query))
            top = jnp.max(scores, axis=0, keepdims=True)
            expo = jnp.exp(scores - top)
            total = jnp.sum(expo, axis=0, keepdims=True)
            mixed = nn(values[head_of(h), :reach], expo.astype(BF16))
            blocks.append(mixed * (1.0 / total))
            sum_ref[0, 0, h : h + 1, span_of(b)] = top + jnp.log(total)
        heads.append(jnp.concatenate(blocks, axis=1))
    put_back(shift_ref, out_ref, count, jnp.concatenate(heads, axis=0).T.astype(BF16))


def attend(shift, count, query, key, value):
    rows, width = query.shape
    seqs, pairs = rows // SEQ, width // PAIR
    tile = pl.BlockSpec((SEQ, PAIR), lambda s, p, _: (s, p))
    return call(
        functools.partial(attend_body, count),
        (seqs, pairs),
        [tile] * 3,
        [tile, pl.BlockSpec((1, 1, 2, SEQ), lambda s, p, _: (s, p, 0, 0))],
        [((rows, width), BF16), ((seqs, pairs, 2, SEQ), F32)],
        flops=16 * rows * width * SEQ,
        prefetch=1,
        moved=8 * rows * width,
    )(shift, query, key, value)


def attend_back_body(
    count, shift_ref, q_ref, k_ref, v_ref, g_ref, sum_ref, cos_ref, sin_ref, dq_ref, dk_ref, dv_ref
):
    queries, keys, values, grads = (
        in_place(shift_ref, ref, count) for ref in (q_ref, k_ref, v_ref, g_ref)
    )
    turned = keys.astype(F32).T.astype(BF16)
    dq_heads, dk_heads, dv_heads = [], [], []
    for h in range(2):
        dq, dk, dv = [], [], []
        for b in range(2):
            reach = (b + 1) * HALF_SEQ
            query = queries[span_of(b), head_of(h)]
            grad = grads[span_of(b), head_of(h)]
            scores = causal(nt(keys[:reach, head_of(h)], query * BF16(FACTOR)))
            probs = jnp.exp(scores - sum_ref[0, 0, h : h + 1, span_of(b)])
            probs_grad = nt(values[:reach, head_of(h)], grad)
            inner = jnp.sum(probs * probs_grad, axis=0, keepdims=True)
            score_grad = (probs * (probs_grad - inner)).astype(BF16)
            dv.append(nn(probs.astype(BF16), grad))
            dk.append(nn(score_grad, query))
            dq.append(nn(turned[head_of(h), :reach], score_grad))
        for parts, heads in ((dk, dk_heads), (dv, dv_heads)):
            heads.append(
                jnp.concatenate([parts[1][:HALF_SEQ] + parts[0], parts[1][HALF_SEQ:]], axis=0)
            )
        dq_heads.append(jnp.concatenate(dq, axis=1))
    dq = jnp.concatenate(dq_heads, axis=0).T * FACTOR
    dk = jnp.concatenate(dk_heads, axis=1) * FACTOR
    dv = jnp.concatenate(dv_heads, axis=1).astype(BF16)
    cosine, sine = cos_ref[...], sin_ref[...]
    put_back(shift_ref, dq_ref, count, (dq * cosine - turn(dq) * sine).astype(BF16))
    put_back(shift_ref, dk_ref, count, (dk * cosine - turn(dk) * sine).astype(BF16))
    put_back(shift_ref, dv_ref, count, dv)


def attend_back(shift, count, query, key, value, grad, logsum, tables):
    rows, width = query.shape
    seqs, pairs = rows // SEQ, width // PAIR
    tile = pl.BlockSpec((SEQ, PAIR), lambda s, p, _: (s, p))
    return call(
        functools.partial(attend_back_body, count),
        (seqs, pairs),
        [tile] * 4
        + [pl.BlockSpec((1, 1, 2, SEQ), lambda s, p, _: (s, p, 0, 0))]
        + [whole((SEQ, PAIR))] * 2,
        [tile] * 3,
        [((rows, width), BF16)] * 3,
        flops=40 * rows * width * SEQ,
        prefetch=1,
        moved=14 * rows * width,
    )(shift, query, key, value, grad, logsum, *tables)


def local(
    ring,
    group,
    tokens,
    attn_gain,
    query_weight,
    key_weight,
    value_weight,
    output_weight,
    ffn_gain,
    gate_weight,
    up_weight,
    down_weight,
    cotangent,
):
    line = jnp.asarray(ring.table)[lax.axis_index("dp")]
    rows, model = tokens.shape
    count = SEQ // rows
    shift = lax.axis_index("tensor") % count
    row = jnp.arange(SEQ, dtype=jnp.int32)
    places = rope_tables(row)
    tables = rope_tables((row // rows ^ shift) * rows + row % rows)
    shift = jnp.reshape(shift, (1,)).astype(jnp.int32)
    depth, own = query_weight.shape
    hidden_units = gate_weight.shape[1]
    chain = Chain()

    def gather(piece):
        return Gather(ring, chain, chain.tie(piece))

    def sums(mine):
        return Sums(ring, chain, chain.tie(mine))

    def spread_of(values):
        return Spread(group, chain, chain.tie(values))

    def fold_of(part):
        own_part, sent = part
        return Fold(group, chain, own_part, [[chain.tie(v) for v in half] for half in sent])

    def grads_of(left, rights):
        theirs = weight_grads(left, 1, [chain.tie(rights[0]), *rights[1:]])
        chain.then(theirs)
        got = ring.other(theirs)

        def mine():
            value = weight_grads(left, 0, [chain.tie(rights[0]), *rights[1:]], got)
            chain.then(value)
            return sums(value)

        return mine

    spread = spread_of(tokens)
    extra = jnp.concatenate(
        [attn_gain, ffn_gain, jnp.zeros((2 * (own - depth),), BF16)]
    )
    extra = jnp.broadcast_to(extra, (16, 2 * own))
    qk = gather(
        jnp.concatenate([jnp.concatenate([query_weight, key_weight], axis=1), extra], axis=0)
    )
    vo = gather(jnp.concatenate([value_weight, output_weight.T], axis=1))
    qk.down_to(2)
    vo.down_to(2)
    spread.end()
    qk.down_to(1)
    all_tokens = spread.blocks()
    spread = spread_of(cotangent)
    vo.down_to(1)
    gate = gather(gate_weight)
    qk = qk.pieces()
    spread.end()
    vo = vo.pieces()
    up = gather(up_weight)
    w_query, w_key = Weight(qk, depth, 0, own), Weight(qk, depth, own, own)
    w_value, w_output = Weight(vo, depth, 0, own), Weight(vo, depth, own, own)
    gains = jnp.concatenate(
        [piece[depth : depth + 1, : 2 * depth].reshape(2, depth) for piece in qk], axis=1
    ).astype(F32)

    group_one = ordered(norm_body, line, chain.tie(gains), all_tokens)
    chain.then(group_one)
    query, key, value = project(group_one, tables, w_query, w_key, w_value)
    mixed, logsum = attend(shift, count, query, key, value)
    chain.then(mixed)
    all_grads = spread.blocks()
    gate.down_to(2)
    out_part = times_trans([(chain.tie(mixed), w_output)], group)
    chain.then(*out_part[0])
    up.down_to(2)
    fold = fold_of(out_part)
    grad_rows = ordered(order_body, line, chain.tie(gains), all_grads)
    chain.then(grad_rows)
    fold.end()
    gate.down_to(1)
    attended = fold.total()
    middle, second = by_rows(
        middle_body, line, chain.tie(tokens), gains, attended, [], [F32, BF16]
    )
    chain.then(second)
    spread = spread_of(second)
    up.down_to(1)
    spread.end()
    w_gate = Weight(gate.pieces(), depth, 0, hidden_units)
    down = gather(down_weight.T)
    group_two = spread.blocks()
    w_up = Weight(up.pieces(), depth, 0, hidden_units)
    group_two[0] = [chain.tie(group_two[0][0])]
    hidden, slope, silu = gate_up(group_two, w_gate, w_up)
    chain.then(hidden)
    down.down_to(2)

    mine = grads_of(grad_rows, [hidden])
    down_sum = mine()
    w_down = Weight(down.pieces(), depth, 0, hidden_units)
    gate_grad, up_grad = hidden_back(chain.tie(grad_rows), w_down, slope, silu)
    chain.then(gate_grad, up_grad)
    down_sum.down_to(2)
    second_part = times_trans([(chain.tie(gate_grad), w_gate), (up_grad, w_up)], group)
    chain.then(*second_part[0])
    fold = fold_of(second_part)
    down_sum.down_to(1)
    mine_gate = grads_of(group_two, [gate_grad])
    mine_up = grads_of(group_two, [up_grad])
    gate_sum = mine_gate()
    down_sum = down_sum.total()
    fold.end()
    up_sum = mine_up()
    second_grad = fold.total()
    middle_grad, low_grad = by_rows(
        second_back_body, line, chain.tie(cotangent), gains, second_grad, [middle], [F32, BF16]
    )
    chain.then(low_grad)
    spread = spread_of(low_grad)
    result_part = times_trans([(chain.tie(hidden), w_down)], group)
    chain.then(*result_part[0])
    gate_sum.down_to(2)
    spread.end()
    up_sum.down_to(2)
    attn_grads = spread.blocks()
    fold = fold_of(result_part)

    attn_grads[0] = [chain.tie(attn_grads[0][0])]
    mixed_grad = mixed_back(attn_grads, w_output)
    query_back, key_back, value_back = attend_back(
        shift, count, query, key, value, mixed_grad, logsum, places
    )
    chain.then(query_back)
    gate_sum.down_to(1)
    fold.end()
    mine_out = grads_of(attn_grads, [mixed])
    mine_qkv = grads_of(group_one, [query_back, key_back, value_back])
    up_sum.down_to(1)
    result_part = fold.total()
    qkv_sum = mine_qkv()
    out_sum = mine_out()
    gate_sum = gate_sum.total()
    first_part = times_trans(
        [(chain.tie(query_back), w_query), (key_back, w_key), (value_back, w_value)], group
    )
    chain.then(*first_part[0])
    fold = fold_of(first_part)
    (layer_out,) = by_rows(result_body, line, chain.tie(middle), gains, result_part, [], [BF16])
    chain.then(layer_out)
    up_sum = up_sum.total()
    fold.end()
    qkv_sum.down_to(2)
    out_sum.down_to(2)
    first_grad = fold.total()
    (input_grad,) = by_rows(
        first_back_body, line, chain.tie(tokens), gains, first_grad, [middle_grad], [F32]
    )
    chain.then(input_grad)
    qkv_sum.down_to(1)
    out_sum.down_to(1)
    qkv_sum = qkv_sum.total()
    query_sum, key_sum, value_sum = [qkv_sum[:, cut(own, i)] for i in range(3)]

    def inner(weight, grad):
        return jnp.sum(weight.astype(F32) * grad, axis=1)

    gain_one_part = (
        inner(query_weight, query_sum) + inner(key_weight, key_sum) + inner(value_weight, value_sum)
    ) / attn_gain.astype(F32)
    gain_two_part = (inner(gate_weight, gate_sum) + inner(up_weight, up_sum)) / ffn_gain.astype(F32)
    gain_one_total, gain_two_total = lax.psum((gain_one_part, gain_two_part), "tensor")
    chain.then(gain_one_total)
    out_sum = out_sum.total()
    return (
        layer_out,
        input_grad,
        gain_one_total,
        query_sum,
        key_sum,
        value_sum,
        out_sum.T,
        gain_two_total,
        gate_sum,
        up_sum,
        down_sum.T,
    )


def solution(mesh):
    in_specs = (
        P(("dp", "tensor"), None),
        P("dp"),
        P("dp", "tensor"),
        P("dp", "tensor"),
        P("dp", "tensor"),
        P("tensor", "dp"),
        P("dp"),
        P("dp", "tensor"),
        P("dp", "tensor"),
        P("tensor", "dp"),
        P(("dp", "tensor"), None),
    )
    out_specs = (
        P(("dp", "tensor"), None),
        P(("dp", "tensor"), None),
        P("dp"),
        P("dp", "tensor"),
        P("dp", "tensor"),
        P("dp", "tensor"),
        P("tensor", "dp"),
        P("dp"),
        P("dp", "tensor"),
        P("dp", "tensor"),
        P("tensor", "dp"),
    )
    ring = Ring(mesh.shape["dp"])
    size = mesh.shape["tensor"]
    links = [[(i, i ^ 1 << b) for i in range(size)] for b in range(size.bit_length() - 1)]
    group = Group(links, "tensor")

    def run(*arrays):
        return local(ring, group, *arrays)

    return jax.shard_map(run, mesh=mesh, in_specs=in_specs, out_specs=out_specs, check_vma=False)
```

```python
import functools

import jax
import jax.numpy as jnp
import numpy as np
from jax import lax
from jax.experimental import pallas as pl
from jax.experimental.pallas import tpu as pltpu
from jax.sharding import PartitionSpec as P

HEAD_DIM = 64
SEQ = 512
EPS = 1e-05
THETA = 130000.0
BF16 = jnp.bfloat16
F32 = jnp.float32
FACTOR = HEAD_DIM**-0.5
PAIR = 2 * HEAD_DIM
HALF_SEQ = SEQ // 2
VMEM_LIMIT = 58 << 20
COST_SHARE = 16


class Chain:
    def __init__(self):
        self.token = jnp.zeros((8, 128), F32)
        self.swaps, self.asked = [], []

    def join(self, *values):
        *values, self.token = lax.optimization_barrier((*values, self.token))
        return values

    def gate(self, *values):
        swaps, self.swaps = self.swaps, []
        asked, self.asked = self.asked, []
        joined = self.join(
            *values, *[held[i] for held, i in swaps], *[source for source, _, _, _ in asked]
        )
        for (held, i), value in zip(swaps, joined[len(values) :]):
            held[i] = value
        for (_, held, i, swap), value in zip(asked, joined[len(values) + len(swaps) :]):
            held[i] = swap(value)
            self.swaps.append((held, i))
        return joined[: len(values)]

    def end(self, *transfers):
        counts = [len(t.flying) for t in transfers]
        got = self.gate(*[value for t in transfers for value in t.flying])
        for t, count in zip(transfers, counts):
            t.go_on(got[:count])
            got = got[count:]

    def ask(self, source, held, i, swap):
        self.asked.append((source, held, i, swap))

    def flush(self):
        for source, held, i, swap in self.asked:
            held[i] = swap(source)
        self.asked = []

    def call(self, body, grid, ins, outs, shapes, flops, scratch=(), prefetch=0, moved=0):
        first = prefetch + len(ins)
        second = first + 1 + len(outs)
        anywhere = pl.BlockSpec(memory_space=pl.ANY)

        def wrapped(*refs):
            body(*refs[:first], *refs[first + 1 : second], *refs[second + 1 :])

        run = pl.pallas_call(
            wrapped,
            grid_spec=pltpu.PrefetchScalarGridSpec(
                num_scalar_prefetch=prefetch,
                grid=grid,
                in_specs=[*ins, anywhere],
                out_specs=[*outs, anywhere],
                scratch_shapes=list(scratch),
            ),
            out_shape=[jax.ShapeDtypeStruct(s, t) for s, t in [*shapes, ((8, 128), F32)]],
            compiler_params=pltpu.CompilerParams(
                vmem_limit_bytes=VMEM_LIMIT, dimension_semantics=("arbitrary",) * len(grid)
            ),
            cost_estimate=pl.CostEstimate(
                flops=flops // COST_SHARE, bytes_accessed=moved // COST_SHARE, transcendentals=0
            ),
        )

        def with_token(*args):
            *results, self.token = run(*args, self.token)
            return results

        return with_token


class Chips:
    def __init__(self, size):
        self.bits = (size // 2).bit_length() - 1
        self.size = size
        self.swap = [(i, i ^ 1) for i in range(size)]
        self.links = [
            [(i, i ^ 2 << self.bits - 1 - p) for i in range(size)] for p in range(self.bits)
        ]
        flips = [
            sum(1 << self.bits - 1 - p for p in range(self.bits) if v >> p & 1)
            for v in range(1 << self.bits)
        ]
        table = [[i ^ 2 * f for f in flips] + [i ^ 2 * f ^ 1 for f in flips] for i in range(size)]
        self.table = np.array(table, np.int32)

    def send(self, value, p):
        return lax.ppermute(value, "dp", self.links[p])

    def other(self, value):
        return lax.ppermute(value, "dp", self.swap)


class Gather:
    def __init__(self, chips, chain, piece):
        self.chips, self.chain = chips, chain
        self.own = [piece] + [None] * (2**chips.bits - 1)
        self.others = list(self.own)
        self.ask(0)
        self.keys = [1 << p for p in range(chips.bits)]
        self.flying = [chips.send(piece, p) for p in range(chips.bits)]

    def ask(self, v):
        self.chain.ask(self.own[v], self.others, v, self.chips.other)

    def go_on(self, got):
        keys, self.keys, self.flying = self.keys, [], []
        for v, piece in zip(keys, got):
            self.own[v] = piece
            for p in range(v.bit_length(), self.chips.bits):
                self.keys.append(v | 1 << p)
                self.flying.append(self.chips.send(piece, p))
        for v in keys:
            self.ask(v)

    def pieces(self):
        while self.flying:
            self.chain.end(self)
        self.chain.flush()
        return self.own + self.others


class Sums:
    def __init__(self, chips, chain, mine):
        self.chips, self.chain = chips, chain
        self.parts = [mine[0]]
        mine = list(mine[1:])
        self.direct, self.passed = [], []
        for p in range(chips.bits):
            self.direct.append(mine.pop(0))
            self.passed.append(mine.pop(0) if p else None)
        self.p = chips.bits - 1
        self.kinds = [self.p]
        self.flying = [chips.send(self.passed[self.p], self.p)]

    def go_on(self, got):
        rows = self.parts[0].shape[0]
        kinds, self.kinds, self.flying = self.kinds, [], []
        if self.p < 0:
            self.last.append(got[0])
            return
        for kind, block in zip(kinds, got):
            if kind == "direct":
                self.parts.append(block)
            elif kind == "half":
                self.last = [block]
            else:
                add = lambda held, first: (
                    held.astype(F32) + block[first * rows : first * rows + held.shape[0]].astype(F32)
                ).astype(BF16)
                for q in range(kind):
                    self.direct[q] = add(self.direct[q], (1 << q) - 1)
                    if q:
                        self.passed[q] = add(self.passed[q], 1 << q)
        p, self.p = self.p, self.p - 1
        if p > 0:
            self.send("direct", self.direct[p], p)
        if p > 1:
            self.send(p - 1, self.passed[p - 1], p - 1)
        half = self.direct[0].shape[1] // 2
        if p == 1:
            self.send("half", self.direct[0][:, :half], 0)
        if p == 0:
            self.send("last", self.direct[0][:, half:], 0)

    def send(self, kind, value, p):
        (value,) = self.chain.join(value)
        self.kinds.append(kind)
        self.flying.append(self.chips.send(value, p))

    def total(self):
        while self.flying:
            self.chain.end(self)
        total = self.parts[0].astype(F32)
        for part in self.parts[1:]:
            total = total + part.astype(F32)
        half = total.shape[1] // 2
        return jnp.concatenate(
            [total[:, :half] + self.last[0].astype(F32), total[:, half:] + self.last[1].astype(F32)],
            axis=1,
        )


class Group:
    def __init__(self, links, axes):
        self.links, self.axes = links, axes
        self.bits = len(links)
        self.size = 1 << self.bits
        self.orders = (list(range(self.bits)), list(range(self.bits))[::-1])

    def send(self, value, bit):
        return lax.ppermute(value, self.axes, self.links[bit])

    def messages(self):
        found = []
        for order in self.orders:
            found.append([])
            for top in reversed(range(self.bits)):
                found[-1].append(
                    [
                        1 << order[top] | sum(1 << order[p] for p in range(top) if v >> p & 1)
                        for v in range(1 << top)
                    ]
                )
        return found


class Spread:
    def __init__(self, group, chain, rows):
        self.group, self.chain = group, chain
        self.held = {0: [rows]}
        self.keys = [(1 << b, None) for b in range(group.bits)]
        self.flying = [group.send(rows, b) for b in range(group.bits)]

    def go_on(self, got):
        fresh = list(zip(self.keys, got))
        self.keys, self.flying = [], []
        for (k, h), block in fresh:
            if h is None:
                self.held[k] = [block]
            else:
                self.held.setdefault(k, [None, None])[h] = block
        for (k, h), block in fresh:
            for way, order in enumerate(self.group.orders):
                if h is not None and h != way:
                    continue
                half = block.shape[1] // 2
                top = max(i for i, bit in enumerate(order) if k >> bit & 1)
                for i in range(top + 1, len(order)):
                    part = block if h is not None else block[:, way * half : (way + 1) * half]
                    self.keys.append((k | 1 << order[i], way))
                    self.flying.append(self.group.send(part, order[i]))

    def blocks(self):
        while self.flying:
            self.chain.end(self)
        return [self.held[k] for k in range(self.group.size)]


class Fold:
    def __init__(self, group, chain, own, sent):
        self.group, self.chain = group, chain
        self.rows = own[0].shape[0]
        self.sent = [list(half) for half in sent]
        self.parts = [[half] for half in own]
        self.wave = 0
        self.start()

    def start(self):
        self.flying = [
            self.group.send(self.sent[h][self.wave], order[self.group.bits - 1 - self.wave])
            for h, order in enumerate(self.group.orders)
        ]

    def go_on(self, got):
        self.wave += 1
        self.flying = []
        for h, block in enumerate(got):
            self.parts[h].append(block)
            for wave in range(self.wave, self.group.bits):
                first = self.rows << (self.group.bits - 1 - wave)
                more = block[first : 2 * first].astype(F32)
                self.sent[h][wave] = (self.sent[h][wave].astype(F32) + more).astype(BF16)
        if self.wave < self.group.bits:
            now = self.chain.join(*[sent[self.wave] for sent in self.sent])
            for sent, value in zip(self.sent, now):
                sent[self.wave] = value
            self.start()

    def total(self):
        while self.flying:
            self.chain.end(self)
        return self.parts


class Weight:
    def __init__(self, pieces, rows, start, width):
        self.pieces, self.rows, self.start, self.width = pieces, rows, start, width
        self.model = len(pieces) * rows

    def tiles(self, tile):
        first = self.start // tile
        return [pl.BlockSpec((self.rows, tile), lambda j: (0, first + j))] * len(self.pieces)


def nn(left, right):
    return lax.dot_general(left, right, (((1,), (0,)), ((), ())), preferred_element_type=F32)


def nt(left, right):
    return lax.dot_general(left, right, (((1,), (1,)), ((), ())), preferred_element_type=F32)


def tn(left, right):
    return lax.dot_general(left, right, (((0,), (0,)), ((), ())), preferred_element_type=F32)


def whole(shape):
    return pl.BlockSpec(shape, lambda *_: (0,) * len(shape))


def place(line_ref, j, width):
    return pl.ds(pl.multiple_of(line_ref[j] * width, 128), width)


def cut(width, j):
    return slice(j * width, (j + 1) * width)


def scale_of(values):
    return lax.rsqrt(jnp.mean(values * values, axis=-1, keepdims=True) + EPS)


def fetch_blocks(counts, refs, held, sems, k, slot, wait):
    first = 0
    for i, count in enumerate(counts):
        copies = []
        half = held.shape[2] // count
        for h in range(count):
            target = held.at[slot, :, pl.ds(h * half, half)]
            copies.append(pltpu.make_async_copy(refs[first + h], target, sems.at[slot, h]))
        first += count

        @pl.when(k == i)
        def _():
            for copy in copies:
                copy.wait() if wait else copy.start()


def fetched(counts, refs, held, sems):
    k = pl.program_id(0)

    @pl.when(k == 0)
    def _():
        fetch_blocks(counts, refs, held, sems, k, 0, False)

    fetch_blocks(counts, refs, held, sems, k + 1, (k + 1) % 2, False)
    fetch_blocks(counts, refs, held, sems, k, k % 2, True)
    return held.at[k % 2]


def norm_body(blocks, counts, line_ref, gain_ref, *refs):
    out_ref, held, sems = refs[sum(counts) :]
    x_ref = fetched(counts, refs, held, sems)
    width = out_ref.shape[1] // blocks
    scale = scale_of(x_ref[...].astype(F32))
    for j in range(blocks):
        part = x_ref[:, place(line_ref, j, width)].astype(F32)
        gain = gain_ref[0:1, cut(width, j)]
        out_ref[:, cut(width, j)] = (part * scale * gain).astype(BF16)


def order_body(blocks, counts, line_ref, gain_ref, *refs):
    out_ref, held, sems = refs[sum(counts) :]
    x_ref = fetched(counts, refs, held, sems)
    width = out_ref.shape[1] // blocks
    for j in range(blocks):
        out_ref[:, cut(width, j)] = x_ref[:, place(line_ref, j, width)]


def ordered(chain, body, line, gains, held):
    counts = [len(block) for block in held]
    rows, model = held[0][0].shape
    n = len(held)
    return chain.call(
        functools.partial(body, line.shape[0], counts),
        (n,),
        [whole(gains.shape)] + [pl.BlockSpec(memory_space=pl.ANY)] * sum(counts),
        [pl.BlockSpec((rows, model), lambda k, *_: (k, 0))],
        [((n * rows, model), BF16)],
        flops=20 * n * rows * model,
        scratch=[pltpu.VMEM((2, rows, model), BF16), pltpu.SemaphoreType.DMA((2, 2))],
        prefetch=1,
        moved=4 * n * rows * model,
    )(line, gains, *[array for block in held for array in block])[0]


def added(refs, span):
    total = refs[0][span, :].astype(F32)
    for ref in refs[1:]:
        total += ref[span, :].astype(F32)
    return total


def middle_body(blocks, m, line_ref, x_ref, gain_ref, *refs):
    middle_ref, out_ref = refs[2 * m :]
    width = x_ref.shape[1] // blocks
    half = x_ref.shape[1] // 2
    span = slice(None)
    middle_ref[:, :half] = added(refs[:m], span)
    middle_ref[:, half:] = added(refs[m : 2 * m], span)
    for j in range(blocks):
        here = x_ref[:, place(line_ref, j, width)].astype(F32)
        middle_ref[:, cut(width, j)] += here
    middle = middle_ref[...]
    out_ref[...] = (middle * scale_of(middle) * gain_ref[1:2, :]).astype(BF16)


def result_body(blocks, m, line_ref, middle_ref, gain_ref, *refs):
    out_ref = refs[2 * m]
    width = middle_ref.shape[1] // blocks
    span = slice(None)
    total = middle_ref[...] + jnp.concatenate(
        [added(refs[:m], span), added(refs[m : 2 * m], span)], axis=1
    )
    for j in range(blocks):
        out_ref[:, place(line_ref, j, width)] = total[:, cut(width, j)].astype(BF16)


def second_back_body(blocks, m, line_ref, dy_ref, gain_ref, *refs):
    middle_ref, out_ref, low_ref = refs[2 * m :]
    width = dy_ref.shape[1] // blocks
    span = slice(None)
    grad = jnp.concatenate([added(refs[:m], span), added(refs[m : 2 * m], span)], axis=1)
    middle = middle_ref[...]
    scale = scale_of(middle)
    normed = middle * scale
    scaled = grad * gain_ref[1:2, :]
    out_ref[...] = scale * (scaled - normed * jnp.mean(scaled * normed, axis=-1, keepdims=True))
    for j in range(blocks):
        out_ref[:, cut(width, j)] += dy_ref[:, place(line_ref, j, width)].astype(F32)
    low_ref[...] = out_ref[...].astype(BF16)


def first_back_body(blocks, m, line_ref, x_ref, gain_ref, *refs):
    above_ref, out_ref = refs[2 * m :]
    width = x_ref.shape[1] // blocks
    span = slice(None)
    scale = scale_of(x_ref[...].astype(F32))
    normed = jnp.concatenate(
        [x_ref[:, place(line_ref, j, width)].astype(F32) for j in range(blocks)], axis=1
    ) * scale
    grad = jnp.concatenate([added(refs[:m], span), added(refs[m : 2 * m], span)], axis=1)
    scaled = grad * gain_ref[0:1, :]
    back = scale * (scaled - normed * jnp.mean(scaled * normed, axis=-1, keepdims=True))
    total = above_ref[...] + back
    for j in range(blocks):
        out_ref[:, place(line_ref, j, width)] = total[:, cut(width, j)]


def by_rows(chain, body, line, first, gains, parts, more, kinds):
    rows, model = first.shape
    half = model // 2
    tile = min(128, rows)
    row = pl.BlockSpec((tile, model), lambda i, *_: (i, 0))
    slim = pl.BlockSpec((tile, half), lambda i, *_: (i, 0))
    m = len(parts[0])
    return chain.call(
        functools.partial(body, line.shape[0], m),
        (rows // tile,),
        [row, whole(gains.shape)] + [slim] * (2 * m) + [row] * len(more),
        [row] * len(kinds),
        [((rows, model), kind) for kind in kinds],
        flops=20 * rows * model,
        prefetch=1,
        moved=rows * model * (2 * m + 4 * len(kinds)),
    )(line, first, gains, *parts[0], *parts[1], *more)


def rope_tables(place):
    half = HEAD_DIM // 2
    freq = THETA ** (-2.0 * jnp.arange(half, dtype=F32) / HEAD_DIM)
    angle = place.astype(F32)[:, None] * freq[None, :]
    cosine, sine = jnp.cos(angle), jnp.sin(angle)
    return (
        jnp.concatenate([cosine] * (PAIR // half), axis=1),
        jnp.concatenate([-sine, sine] * (PAIR // HEAD_DIM), axis=1),
    )


def turn(values):
    half = HEAD_DIM // 2
    width = values.shape[-1]
    lane = lax.broadcasted_iota(jnp.int32, values.shape, 1) % HEAD_DIM
    return jnp.where(
        lane < half, pltpu.roll(values, width - half, 1), pltpu.roll(values, half, 1)
    )


def joined(refs):
    return jnp.concatenate([r[...] for r in refs], axis=0)


def qkv_body(n, x_ref, cos_ref, sin_ref, *refs):
    weights, outs = refs[: 3 * n], refs[3 * n :]
    rows = x_ref.shape[0]
    tile = outs[0].shape[1]
    for i in range(3):
        weight = joined(weights[i * n : (i + 1) * n])
        for s in range(rows // SEQ):
            span = slice(s * SEQ, (s + 1) * SEQ)
            product = nn(x_ref[span, :], weight)
            if i == 2:
                outs[i][span, :] = product.astype(BF16)
                continue
            for t in range(tile // PAIR):
                here = product[:, t * PAIR : (t + 1) * PAIR]
                turned = here * cos_ref[...] + turn(here) * sin_ref[...]
                outs[i][span, t * PAIR : (t + 1) * PAIR] = turned.astype(BF16)


def project(chain, x, tables, query, key, value):
    rows, model = x.shape
    n, width = len(query.pieces), query.width
    tile = min(256, width)
    out = pl.BlockSpec((rows, tile), lambda j: (0, j))
    return chain.call(
        functools.partial(qkv_body, n),
        (width // tile,),
        [whole(x.shape), whole((SEQ, PAIR)), whole((SEQ, PAIR))]
        + query.tiles(tile)
        + key.tiles(tile)
        + value.tiles(tile),
        [out] * 3,
        [((rows, width), BF16)] * 3,
        flops=6 * rows * model * width,
        moved=2 * (rows * model + 3 * model * width + 3 * rows * width),
    )(x, *tables, *query.pieces, *key.pieces, *value.pieces)


def collect(counts, refs, held, sems):
    rows = held.shape[0] // len(counts)
    copies = []
    for k, count in enumerate(counts):
        half = held.shape[1] // count
        for h in range(count):
            target = held.at[pl.ds(k * rows, rows), pl.ds(h * half, half)]
            i = len(copies)
            copies.append(pltpu.make_async_copy(refs[i], target, sems.at[i]))
    for copy in copies:
        copy.start()
    for copy in copies:
        copy.wait()


def gate_body(n, counts, *refs):
    m = sum(counts)
    gate_w, up_w = refs[m : m + n], refs[m + n : m + 2 * n]
    hidden_ref, slope_ref, silu_ref, x_ref, sems = refs[m + 2 * n :]

    @pl.when(pl.program_id(0) == 0)
    def _():
        collect(counts, refs, x_ref, sems)

    gate_weight, up_weight = joined(gate_w), joined(up_w)
    for s in range(x_ref.shape[0] // SEQ):
        span = slice(s * SEQ, (s + 1) * SEQ)
        gate = nn(x_ref[span, :], gate_weight)
        up = nn(x_ref[span, :], up_weight)
        sigm = jax.nn.sigmoid(gate)
        silu = gate * sigm
        hidden_ref[span, :] = (silu * up).astype(BF16)
        silu_ref[span, :] = silu.astype(BF16)
        slope_ref[span, :] = (up * sigm * (1.0 + gate * (1.0 - sigm))).astype(BF16)


def collected(held):
    counts = [len(block) for block in held]
    rows, model = held[0][0].shape
    scratch = [
        pltpu.VMEM((len(held) * rows, model), BF16),
        pltpu.SemaphoreType.DMA((sum(counts),)),
    ]
    arrays = [array for block in held for array in block]
    return counts, arrays, [pl.BlockSpec(memory_space=pl.ANY)] * len(arrays), scratch


def gate_up(chain, held, gate, up):
    counts, arrays, specs, scratch = collected(held)
    rows, model = scratch[0].shape
    n, width = len(gate.pieces), gate.width
    tile = min(256, width)
    out = pl.BlockSpec((rows, tile), lambda j: (0, j))
    return chain.call(
        functools.partial(gate_body, n, counts),
        (width // tile,),
        specs + gate.tiles(tile) + up.tiles(tile),
        [out] * 3,
        [((rows, width), BF16)] * 3,
        flops=4 * rows * model * width,
        scratch=scratch,
        moved=2 * (rows * model + 2 * model * width + 3 * rows * width),
    )(*arrays, *gate.pieces, *up.pieces)


def hidden_back_body(n, g_ref, *refs):
    weight = joined(refs[:n])
    slope_ref, silu_ref, gate_ref, up_ref = refs[n:]
    for s in range(g_ref.shape[0] // SEQ):
        span = slice(s * SEQ, (s + 1) * SEQ)
        grad = nn(g_ref[span, :], weight)
        gate_ref[span, :] = (grad * slope_ref[span, :].astype(F32)).astype(BF16)
        up_ref[span, :] = (grad * silu_ref[span, :].astype(F32)).astype(BF16)


def hidden_back(chain, grads, down, slope, silu):
    rows, model = grads.shape
    n, width = len(down.pieces), down.width
    tile = min(256, width)
    out = pl.BlockSpec((rows, tile), lambda j: (0, j))
    return chain.call(
        functools.partial(hidden_back_body, n),
        (width // tile,),
        [whole(grads.shape)] + down.tiles(tile) + [out] * 2,
        [out] * 2,
        [((rows, width), BF16)] * 2,
        flops=2 * rows * model * width,
        moved=2 * (rows * model + model * width + 4 * rows * width),
    )(grads, *down.pieces, slope, silu)


def mixed_back_body(n, counts, *refs):
    m = sum(counts)
    out_ref, x_ref, sems = refs[m + n :]

    @pl.when(pl.program_id(0) == 0)
    def _():
        collect(counts, refs, x_ref, sems)

    out_ref[...] = nn(x_ref[...], joined(refs[m : m + n])).astype(BF16)


def mixed_back(chain, held, out):
    counts, arrays, specs, scratch = collected(held)
    rows, model = scratch[0].shape
    n, width = len(out.pieces), out.width
    tile = min(256, width)
    return chain.call(
        functools.partial(mixed_back_body, n, counts),
        (width // tile,),
        specs + out.tiles(tile),
        [pl.BlockSpec((rows, tile), lambda j: (0, j))],
        [((rows, width), BF16)],
        flops=2 * rows * model * width,
        scratch=scratch,
        moved=2 * (rows * model + model * width + rows * width),
    )(*arrays, *out.pieces)[0]


def trans_body(n, starts, targets, *refs):
    parts, blocks = len(starts), len(targets[0])
    lefts = refs[:parts]
    pieces = refs[parts : parts * (n + 1)]
    outs = refs[parts * (n + 1) : -4]
    held, ready, sems, out_sems = refs[-4:]
    j = pl.program_id(0)
    depth, width = held.shape[2:]
    rows = ready.shape[1] // blocks

    def copy(i, p, slot):
        source = pieces[p * n + i].at[pl.ds(0, depth), pl.ds(starts[p], width)]
        return pltpu.make_async_copy(source, held.at[slot, p], sems.at[slot, p])

    def fetch(step, slot):
        for i in range(n):

            @pl.when(step == i)
            def _():
                for p in range(parts):
                    copy(i, p, slot).start()

    def leave(slot, k, array, first, column):
        target = outs[array].at[pl.ds(first, rows), pl.ds(column, depth)]
        source = ready.at[slot, pl.ds(k * rows, rows), :]
        return pltpu.make_async_copy(source, target, out_sems.at[slot, k])

    def left(slot):
        for k in range(blocks):
            leave(slot, k, 0, 0, 0).wait()

    @pl.when(j == 0)
    def _():
        fetch(j, 0)

    @pl.when(j + 1 < n)
    def _():
        fetch(j + 1, (j + 1) % 2)

    slot = j % 2
    for p in range(parts):
        copy(0, p, slot).wait()

    @pl.when(j >= 2)
    def _():
        left(slot)

    for s in range(blocks * rows // SEQ):
        span = slice(s * SEQ, (s + 1) * SEQ)
        total = nt(lefts[0][span, :], held[slot, 0])
        for p in range(1, parts):
            total += nt(lefts[p][span, :], held[slot, p])
        ready[slot, span, :] = total.astype(BF16)
    column = pl.multiple_of(j % (n // 2) * depth, 128)
    for h in range(2):

        @pl.when((j >= n // 2) == (h == 1))
        def _():
            for k, (array, first) in enumerate(targets[h]):
                leave(slot, k, array, first, column).start()

    @pl.when(j == n - 1)
    def _():
        left(1 - slot)
        left(slot)


def times_trans(chain, parts, group):
    weights = [weight for _, weight in parts]
    n, depth, width = len(weights[0].pieces), weights[0].rows, weights[0].width
    rows = parts[0][0].shape[0]
    half = weights[0].model // 2
    size = rows // group.size
    messages = group.messages()
    shapes = [((size, half), BF16)] * 2
    targets = [{0: (0, 0)}, {0: (1, 0)}]
    for h in range(2):
        for keys in messages[h]:
            for i, k in enumerate(keys):
                targets[h][k] = (len(shapes), i * size)
            shapes.append(((len(keys) * size, half), BF16))
    targets = [[t[k] for k in range(group.size)] for t in targets]
    anywhere = pl.BlockSpec(memory_space=pl.ANY)
    outs = chain.call(
        functools.partial(trans_body, n, [weight.start for weight in weights], targets),
        (n,),
        [whole((rows, width))] * len(parts) + [anywhere] * (n * len(parts)),
        [anywhere] * len(shapes),
        shapes,
        flops=4 * rows * half * width * len(parts),
        scratch=[
            pltpu.VMEM((2, len(parts), depth, width), BF16),
            pltpu.VMEM((2, rows, depth), BF16),
            pltpu.SemaphoreType.DMA((2, len(parts))),
            pltpu.SemaphoreType.DMA((2, group.size)),
        ],
        moved=2 * (2 * rows * half + len(parts) * (rows + 2 * half) * width),
    )(*[left for left, _ in parts], *[piece for weight in weights for piece in weight.pieces])
    m = group.bits
    return outs[:2], [outs[2 : 2 + m], outs[2 + m :]]


def grad_body(parts, got, blocks, steps, *refs):
    lefts, refs = refs[:blocks], refs[blocks:]
    rights, refs = refs[:parts], refs[parts:]
    got_ref = refs[0] if got else None
    outs, turned = refs[got:-1], refs[-1]
    j = pl.program_id(0)

    @pl.when(j == 0)
    def _():
        rows = turned.shape[1] // blocks
        for k in range(blocks):
            turned[:, cut(rows, k)] = lefts[k][...].T

    for i in range(parts):

        @pl.when((j >= i * steps) & (j < (i + 1) * steps))
        def _():
            total = nn(turned[...], rights[i][...])
            if got:
                total += got_ref[...].astype(F32)
            total = total.astype(BF16)
            first = 0
            for out_ref in outs:
                count = out_ref.shape[0]
                out_ref[...] = total[first : first + count]
                first += count


def weight_grads(chain, left, which, rights, got=None, bits=0):
    rows, width = rights[0].shape
    parts = len(rights)
    tile = min(512, width)
    steps = width // tile
    if isinstance(left, list):
        lefts = [block[0] if len(block) == 1 else block[which] for block in left]
        half = left[0][0].shape[1] // 2
        places = [which if len(block) == 1 else 0 for block in left]
    else:
        lefts, places, half = [left], [which], left.shape[1] // 2
    blocks = len(lefts)
    ins = [
        pl.BlockSpec((rows // blocks, half), functools.partial(lambda at, j: (0, at), at))
        for at in places
    ]
    for i in range(parts):
        ins.append(
            pl.BlockSpec(
                (rows, tile),
                functools.partial(
                    lambda first, j: (0, jnp.clip(j - first, 0, steps - 1)), i * steps
                ),
            )
        )
    column = lambda j: (0, j)
    more = [] if got is None else [got]
    sizes = [half >> bits]
    for p in range(bits):
        sizes += [sizes[0], ((1 << p) - 1) * sizes[0]] if p else [sizes[0]]
    return chain.call(
        functools.partial(grad_body, parts, len(more), blocks, steps),
        (parts * steps,),
        ins + [pl.BlockSpec((half, tile), column)] * len(more),
        [pl.BlockSpec((size, tile), column) for size in sizes],
        [((size, parts * width), BF16) for size in sizes],
        flops=2 * rows * half * width * parts,
        scratch=[pltpu.VMEM((half, rows), BF16)],
        moved=2 * (rows * half + parts * (rows + half) * width),
    )(*lefts, *rights, *more)


def causal(scores):
    past = scores.shape[0] - HALF_SEQ
    key = lax.broadcasted_iota(jnp.int32, (HALF_SEQ, HALF_SEQ), 0)
    query = lax.broadcasted_iota(jnp.int32, (HALF_SEQ, HALF_SEQ), 1)
    last = jnp.where(key <= query, scores[past:], -1e30)
    return last if past == 0 else jnp.concatenate([scores[:past], last], axis=0)


def head_of(h):
    return slice(h * HEAD_DIM, (h + 1) * HEAD_DIM)


def span_of(b):
    return slice(b * HALF_SEQ, (b + 1) * HALF_SEQ)


def in_place(shift_ref, ref, count):
    rows = SEQ // count
    spans = [pl.ds(pl.multiple_of((i ^ shift_ref[0]) * rows, rows), rows) for i in range(count)]
    return jnp.concatenate([ref[span, :] for span in spans], axis=0)


def put_back(shift_ref, ref, count, values):
    rows = SEQ // count
    for i in range(count):
        ref[pl.ds(pl.multiple_of((i ^ shift_ref[0]) * rows, rows), rows), :] = values[cut(rows, i)]


def attend_body(count, shift_ref, q_ref, k_ref, v_ref, out_ref, sum_ref):
    queries, keys = in_place(shift_ref, q_ref, count), in_place(shift_ref, k_ref, count)
    values = in_place(shift_ref, v_ref, count).astype(F32).T.astype(BF16)
    heads = []
    for h in range(2):
        blocks = []
        for b in range(2):
            reach = (b + 1) * HALF_SEQ
            query = queries[span_of(b), head_of(h)] * BF16(FACTOR)
            scores = causal(nt(keys[:reach, head_of(h)], query))
            top = jnp.max(scores, axis=0, keepdims=True)
            expo = jnp.exp(scores - top)
            total = jnp.sum(expo, axis=0, keepdims=True)
            mixed = nn(values[head_of(h), :reach], expo.astype(BF16))
            blocks.append(mixed * (1.0 / total))
            sum_ref[0, 0, h : h + 1, span_of(b)] = top + jnp.log(total)
        heads.append(jnp.concatenate(blocks, axis=1))
    put_back(shift_ref, out_ref, count, jnp.concatenate(heads, axis=0).T.astype(BF16))


def attend(chain, shift, count, query, key, value):
    rows, width = query.shape
    seqs, pairs = rows // SEQ, width // PAIR
    tile = pl.BlockSpec((SEQ, PAIR), lambda s, p, _: (s, p))
    return chain.call(
        functools.partial(attend_body, count),
        (seqs, pairs),
        [tile] * 3,
        [tile, pl.BlockSpec((1, 1, 2, SEQ), lambda s, p, _: (s, p, 0, 0))],
        [((rows, width), BF16), ((seqs, pairs, 2, SEQ), F32)],
        flops=16 * rows * width * SEQ,
        prefetch=1,
        moved=8 * rows * width,
    )(shift, query, key, value)


def attend_back_body(
    count, shift_ref, q_ref, k_ref, v_ref, g_ref, sum_ref, cos_ref, sin_ref, dq_ref, dk_ref, dv_ref
):
    queries, keys, values, grads = (
        in_place(shift_ref, ref, count) for ref in (q_ref, k_ref, v_ref, g_ref)
    )
    turned = keys.astype(F32).T.astype(BF16)
    dq_heads, dk_heads, dv_heads = [], [], []
    for h in range(2):
        dq, dk, dv = [], [], []
        for b in range(2):
            reach = (b + 1) * HALF_SEQ
            query = queries[span_of(b), head_of(h)]
            grad = grads[span_of(b), head_of(h)]
            scores = causal(nt(keys[:reach, head_of(h)], query * BF16(FACTOR)))
            probs = jnp.exp(scores - sum_ref[0, 0, h : h + 1, span_of(b)])
            probs_grad = nt(values[:reach, head_of(h)], grad)
            inner = jnp.sum(probs * probs_grad, axis=0, keepdims=True)
            score_grad = (probs * (probs_grad - inner)).astype(BF16)
            dv.append(nn(probs.astype(BF16), grad))
            dk.append(nn(score_grad, query))
            dq.append(nn(turned[head_of(h), :reach], score_grad))
        for parts, heads in ((dk, dk_heads), (dv, dv_heads)):
            heads.append(
                jnp.concatenate([parts[1][:HALF_SEQ] + parts[0], parts[1][HALF_SEQ:]], axis=0)
            )
        dq_heads.append(jnp.concatenate(dq, axis=1))
    dq = jnp.concatenate(dq_heads, axis=0).T * FACTOR
    dk = jnp.concatenate(dk_heads, axis=1) * FACTOR
    dv = jnp.concatenate(dv_heads, axis=1).astype(BF16)
    cosine, sine = cos_ref[...], sin_ref[...]
    put_back(shift_ref, dq_ref, count, (dq * cosine - turn(dq) * sine).astype(BF16))
    put_back(shift_ref, dk_ref, count, (dk * cosine - turn(dk) * sine).astype(BF16))
    put_back(shift_ref, dv_ref, count, dv)


def attend_back(chain, shift, count, query, key, value, grad, logsum, tables):
    rows, width = query.shape
    seqs, pairs = rows // SEQ, width // PAIR
    tile = pl.BlockSpec((SEQ, PAIR), lambda s, p, _: (s, p))
    return chain.call(
        functools.partial(attend_back_body, count),
        (seqs, pairs),
        [tile] * 4
        + [pl.BlockSpec((1, 1, 2, SEQ), lambda s, p, _: (s, p, 0, 0))]
        + [whole((SEQ, PAIR))] * 2,
        [tile] * 3,
        [((rows, width), BF16)] * 3,
        flops=40 * rows * width * SEQ,
        prefetch=1,
        moved=14 * rows * width,
    )(shift, query, key, value, grad, logsum, *tables)


def local(
    chips,
    group,
    tokens,
    attn_gain,
    query_weight,
    key_weight,
    value_weight,
    output_weight,
    ffn_gain,
    gate_weight,
    up_weight,
    down_weight,
    cotangent,
):
    line = jnp.asarray(chips.table)[lax.axis_index("dp")]
    rows, model = tokens.shape
    count = SEQ // rows
    shift = lax.axis_index("tensor") % count
    row = jnp.arange(SEQ, dtype=jnp.int32)
    places = rope_tables(row)
    tables = rope_tables((row // rows ^ shift) * rows + row % rows)
    shift = jnp.reshape(shift, (1,)).astype(jnp.int32)
    depth, own = query_weight.shape
    hidden_units = gate_weight.shape[1]
    chain = Chain()

    def gather(piece):
        return Gather(chips, chain, chain.join(piece)[0])

    def spread_of(values):
        return Spread(group, chain, chain.join(values)[0])

    def fold_of(part):
        own_part, sent = part
        sent = chain.join(*sent[0], *sent[1])
        return Fold(group, chain, own_part, [sent[: group.bits], sent[group.bits :]])

    def grads_of(left, rights):
        got = [None]
        chain.ask(weight_grads(chain, left, 1, rights)[0], got, 0, chips.other)

        def mine():
            if got[0] is None:
                chain.flush()
            return Sums(chips, chain, weight_grads(chain, left, 0, rights, got[0], chips.bits))

        return mine

    extra = jnp.concatenate([attn_gain, ffn_gain, jnp.zeros((4 * own - 2 * depth,), BF16)])
    attn = jnp.concatenate([query_weight, key_weight, value_weight, output_weight.T], axis=1)
    attn = gather(jnp.concatenate([attn, jnp.broadcast_to(extra, (16, 4 * own))], axis=0))
    spread = spread_of(tokens)
    chain.end(attn, spread)
    chain.end(attn, spread)
    all_tokens = spread.blocks()
    attn = attn.pieces()
    gate = gather(gate_weight)
    spread = spread_of(cotangent)
    w_query, w_key, w_value, w_output = [Weight(attn, depth, i * own, own) for i in range(4)]
    gains = jnp.concatenate(
        [piece[depth : depth + 1, : 2 * depth].reshape(2, depth) for piece in attn], axis=1
    ).astype(F32)

    group_one = ordered(chain, norm_body, line, gains, all_tokens)
    query, key, value = project(chain, group_one, tables, w_query, w_key, w_value)
    mixed, logsum = attend(chain, shift, count, query, key, value)
    chain.end(spread)
    out_part = times_trans(chain, [(mixed, w_output)], group)
    chain.end(gate, spread)
    fold = fold_of(out_part)
    up = gather(up_weight)
    grad_rows = ordered(chain, order_body, line, gains, spread.blocks())
    chain.end(fold)
    chain.end(up, fold)
    attended = fold.total()
    middle, second = by_rows(
        chain, middle_body, line, tokens, gains, attended, [], [F32, BF16]
    )
    spread = spread_of(second)
    chain.end(gate, spread)
    chain.end(up, spread)
    w_gate = Weight(gate.pieces(), depth, 0, hidden_units)
    group_two = spread.blocks()
    w_up = Weight(up.pieces(), depth, 0, hidden_units)
    down = gather(down_weight.T)
    hidden, slope, silu = gate_up(chain, group_two, w_gate, w_up)

    mine = grads_of(grad_rows, [hidden])
    chain.end(down)
    down_sum = mine()
    w_down = Weight(down.pieces(), depth, 0, hidden_units)
    gate_grad, up_grad = hidden_back(chain, grad_rows, w_down, slope, silu)
    chain.end(down_sum)
    second_part = times_trans(chain, [(gate_grad, w_gate), (up_grad, w_up)], group)
    fold = fold_of(second_part)
    mine_gate = grads_of(group_two, [gate_grad])
    chain.end(down_sum)
    mine_up = grads_of(group_two, [up_grad])
    chain.end(fold)
    gate_sum = mine_gate()
    chain.end(down_sum, fold)
    second_grad = fold.total()
    middle_grad, low_grad = by_rows(
        chain, second_back_body, line, cotangent, gains, second_grad, [middle], [F32, BF16]
    )
    spread = spread_of(low_grad)
    up_sum = mine_up()
    chain.end(gate_sum, spread)
    result_part = times_trans(chain, [(hidden, w_down)], group)
    attn_grads = spread.blocks()
    down_sum = down_sum.total()

    mixed_grad = mixed_back(chain, attn_grads, w_output)
    fold = fold_of(result_part)
    query_back, key_back, value_back = attend_back(
        chain, shift, count, query, key, value, mixed_grad, logsum, places
    )
    chain.end(gate_sum)
    mine = grads_of(group_one, [query_back, key_back, value_back])
    chain.end(fold)
    chain.end(up_sum)
    qkv_sum = mine()
    result_part = fold.total()
    gate_sum = gate_sum.total()
    first_part = times_trans(
        chain, [(query_back, w_query), (key_back, w_key), (value_back, w_value)], group
    )
    fold = fold_of(first_part)
    mine = grads_of(attn_grads, [mixed])
    chain.end(up_sum, fold)
    out_sum = mine()
    (layer_out,) = by_rows(chain, result_body, line, middle, gains, result_part, [], [BF16])
    chain.end(fold)
    first_grad = fold.total()
    (input_grad,) = by_rows(
        chain, first_back_body, line, tokens, gains, first_grad, [middle_grad], [F32]
    )
    chain.end(up_sum, qkv_sum)
    up_sum = up_sum.total()
    chain.end(qkv_sum, out_sum)
    qkv_sum = qkv_sum.total()
    query_sum, key_sum, value_sum = [qkv_sum[:, cut(own, i)] for i in range(3)]

    def inner(weight, grad):
        return jnp.sum(weight.astype(F32) * grad, axis=1)

    gain_one_part = (
        inner(query_weight, query_sum) + inner(key_weight, key_sum) + inner(value_weight, value_sum)
    ) / attn_gain.astype(F32)
    gain_two_part = (inner(gate_weight, gate_sum) + inner(up_weight, up_sum)) / ffn_gain.astype(F32)
    gain_one_total, gain_two_total = lax.psum((gain_one_part, gain_two_part), "tensor")
    (gain_one_total,) = chain.join(gain_one_total)
    out_sum = out_sum.total()
    return (
        layer_out,
        input_grad,
        gain_one_total,
        query_sum,
        key_sum,
        value_sum,
        out_sum.T,
        gain_two_total,
        gate_sum,
        up_sum,
        down_sum.T,
    )


def solution(mesh):
    in_specs = (
        P(("dp", "tensor"), None),
        P("dp"),
        P("dp", "tensor"),
        P("dp", "tensor"),
        P("dp", "tensor"),
        P("tensor", "dp"),
        P("dp"),
        P("dp", "tensor"),
        P("dp", "tensor"),
        P("tensor", "dp"),
        P(("dp", "tensor"), None),
    )
    out_specs = (
        P(("dp", "tensor"), None),
        P(("dp", "tensor"), None),
        P("dp"),
        P("dp", "tensor"),
        P("dp", "tensor"),
        P("dp", "tensor"),
        P("tensor", "dp"),
        P("dp"),
        P("dp", "tensor"),
        P("dp", "tensor"),
        P("tensor", "dp"),
    )
    chips = Chips(mesh.shape["dp"])
    size = mesh.shape["tensor"]
    links = [[(i, i ^ 1 << b) for i in range(size)] for b in range(size.bit_length() - 1)]
    group = Group(links, "tensor")

    def run(*arrays):
        return local(chips, group, *arrays)

    return jax.shard_map(run, mesh=mesh, in_specs=in_specs, out_specs=out_specs, check_vma=False)
```

```python
import functools

import jax
import jax.numpy as jnp
import numpy as np
from jax import lax
from jax.experimental import pallas as pl
from jax.experimental.pallas import tpu as pltpu
from jax.sharding import PartitionSpec as P

HEAD_DIM = 64
SEQ = 512
EPS = 1e-05
THETA = 130000.0
BF16 = jnp.bfloat16
F32 = jnp.float32
FACTOR = HEAD_DIM**-0.5
PAIR = 2 * HEAD_DIM
HALF_SEQ = SEQ // 2
VMEM_LIMIT = 58 << 20
COST_SHARE = 16


class Chain:
    def __init__(self):
        self.token = jnp.zeros((8, 128), F32)
        self.swaps, self.asked = [], []

    def join(self, *values):
        *values, self.token = lax.optimization_barrier((*values, self.token))
        return values

    def gate(self, *values):
        swaps, self.swaps = self.swaps, []
        asked, self.asked = self.asked, []
        joined = self.join(
            *values, *[held[i] for held, i in swaps], *[source for source, _, _, _ in asked]
        )
        for (held, i), value in zip(swaps, joined[len(values) :]):
            held[i] = value
        for (_, held, i, swap), value in zip(asked, joined[len(values) + len(swaps) :]):
            held[i] = swap(value)
            self.swaps.append((held, i))
        return joined[: len(values)]

    def end(self, *transfers):
        counts = [len(t.flying) for t in transfers]
        got = self.gate(*[value for t in transfers for value in t.flying])
        for t, count in zip(transfers, counts):
            t.go_on(got[:count])
            got = got[count:]

    def ask(self, source, held, i, swap):
        self.asked.append((source, held, i, swap))

    def flush(self):
        for source, held, i, swap in self.asked:
            held[i] = swap(source)
        self.asked = []

    def call(self, body, grid, ins, outs, shapes, flops, scratch=(), prefetch=0, moved=0):
        first = prefetch + len(ins)
        second = first + 1 + len(outs)
        anywhere = pl.BlockSpec(memory_space=pl.ANY)

        def wrapped(*refs):
            body(*refs[:first], *refs[first + 1 : second], *refs[second + 1 :])

        run = pl.pallas_call(
            wrapped,
            grid_spec=pltpu.PrefetchScalarGridSpec(
                num_scalar_prefetch=prefetch,
                grid=grid,
                in_specs=[*ins, anywhere],
                out_specs=[*outs, anywhere],
                scratch_shapes=list(scratch),
            ),
            out_shape=[jax.ShapeDtypeStruct(s, t) for s, t in [*shapes, ((8, 128), F32)]],
            compiler_params=pltpu.CompilerParams(
                vmem_limit_bytes=VMEM_LIMIT, dimension_semantics=("arbitrary",) * len(grid)
            ),
            cost_estimate=pl.CostEstimate(
                flops=flops // COST_SHARE, bytes_accessed=moved // COST_SHARE, transcendentals=0
            ),
        )

        def with_token(*args):
            *results, self.token = run(*args, self.token)
            return results

        return with_token


class Chips:
    def __init__(self, size):
        self.bits = (size // 2).bit_length() - 1
        self.size = size
        self.swap = [(i, i ^ 1) for i in range(size)]
        self.links = [
            [(i, i ^ 2 << self.bits - 1 - p) for i in range(size)] for p in range(self.bits)
        ]
        flips = [
            sum(1 << self.bits - 1 - p for p in range(self.bits) if v >> p & 1)
            for v in range(1 << self.bits)
        ]
        table = [[i ^ 2 * f for f in flips] + [i ^ 2 * f ^ 1 for f in flips] for i in range(size)]
        self.table = np.array(table, np.int32)

    def send(self, value, p):
        return lax.ppermute(value, "dp", self.links[p])

    def other(self, value):
        return lax.ppermute(value, "dp", self.swap)


class Gather:
    def __init__(self, chips, chain, piece):
        self.chips, self.chain = chips, chain
        self.own = [piece] + [None] * (2**chips.bits - 1)
        self.others = list(self.own)
        self.ask(0)
        self.keys = [1 << p for p in range(chips.bits)]
        self.flying = [chips.send(piece, p) for p in range(chips.bits)]

    def ask(self, v):
        self.chain.ask(self.own[v], self.others, v, self.chips.other)

    def go_on(self, got):
        keys, self.keys, self.flying = self.keys, [], []
        for v, piece in zip(keys, got):
            self.own[v] = piece
            for p in range(v.bit_length(), self.chips.bits):
                self.keys.append(v | 1 << p)
                self.flying.append(self.chips.send(piece, p))
        for v in keys:
            self.ask(v)

    def pieces(self):
        while self.flying:
            self.chain.end(self)
        self.chain.flush()
        return self.own + self.others


class Sums:
    def __init__(self, chips, chain, mine):
        self.chips, self.chain = chips, chain
        self.parts = [mine[0]]
        mine = list(mine[1:])
        self.direct, self.passed = [], []
        for p in range(chips.bits):
            self.direct.append(mine.pop(0))
            self.passed.append(mine.pop(0) if p else None)
        self.p = chips.bits - 1
        self.kinds = [self.p]
        self.flying = [chips.send(self.passed[self.p], self.p)]

    def go_on(self, got):
        rows = self.parts[0].shape[0]
        kinds, self.kinds, self.flying = self.kinds, [], []
        if self.p < 0:
            self.last.append(got[0])
            return
        for kind, block in zip(kinds, got):
            if kind == "direct":
                self.parts.append(block)
            elif kind == "half":
                self.last = [block]
            else:
                add = lambda held, first: (
                    held.astype(F32) + block[first * rows : first * rows + held.shape[0]].astype(F32)
                ).astype(BF16)
                for q in range(kind):
                    self.direct[q] = add(self.direct[q], (1 << q) - 1)
                    if q:
                        self.passed[q] = add(self.passed[q], 1 << q)
        p, self.p = self.p, self.p - 1
        if p > 0:
            self.send("direct", self.direct[p], p)
        if p > 1:
            self.send(p - 1, self.passed[p - 1], p - 1)
        half = self.direct[0].shape[1] // 2
        if p == 1:
            self.send("half", self.direct[0][:, :half], 0)
        if p == 0:
            self.send("last", self.direct[0][:, half:], 0)

    def send(self, kind, value, p):
        (value,) = self.chain.join(value)
        self.kinds.append(kind)
        self.flying.append(self.chips.send(value, p))

    def total(self):
        while self.flying:
            self.chain.end(self)
        total = self.parts[0].astype(F32)
        for part in self.parts[1:]:
            total = total + part.astype(F32)
        half = total.shape[1] // 2
        return jnp.concatenate(
            [total[:, :half] + self.last[0].astype(F32), total[:, half:] + self.last[1].astype(F32)],
            axis=1,
        )


class Group:
    def __init__(self, links, axes):
        self.links, self.axes = links, axes
        self.bits = len(links)
        self.size = 1 << self.bits
        self.orders = (list(range(self.bits)), list(range(self.bits))[::-1])

    def send(self, value, bit):
        return lax.ppermute(value, self.axes, self.links[bit])

    def messages(self):
        found = []
        for order in self.orders:
            found.append([])
            for top in reversed(range(self.bits)):
                found[-1].append(
                    [
                        1 << order[top] | sum(1 << order[p] for p in range(top) if v >> p & 1)
                        for v in range(1 << top)
                    ]
                )
        return found


class Spread:
    def __init__(self, group, chain, rows):
        self.group, self.chain = group, chain
        self.held = {0: [rows]}
        self.keys = [(1 << b, None) for b in range(group.bits)]
        self.flying = [group.send(rows, b) for b in range(group.bits)]

    def go_on(self, got):
        fresh = list(zip(self.keys, got))
        self.keys, self.flying = [], []
        for (k, h), block in fresh:
            if h is None:
                self.held[k] = [block]
            else:
                self.held.setdefault(k, [None, None])[h] = block
        for (k, h), block in fresh:
            for way, order in enumerate(self.group.orders):
                if h is not None and h != way:
                    continue
                half = block.shape[1] // 2
                top = max(i for i, bit in enumerate(order) if k >> bit & 1)
                for i in range(top + 1, len(order)):
                    part = block if h is not None else block[:, way * half : (way + 1) * half]
                    self.keys.append((k | 1 << order[i], way))
                    self.flying.append(self.group.send(part, order[i]))

    def blocks(self):
        while self.flying:
            self.chain.end(self)
        return [self.held[k] for k in range(self.group.size)]


class Fold:
    def __init__(self, group, chain, own, sent):
        self.group, self.chain = group, chain
        self.rows = own[0].shape[0]
        self.sent = [list(half) for half in sent]
        self.parts = [[half] for half in own]
        self.wave = 0
        self.start()

    def start(self):
        self.flying = [
            self.group.send(self.sent[h][self.wave], order[self.group.bits - 1 - self.wave])
            for h, order in enumerate(self.group.orders)
        ]

    def go_on(self, got):
        self.wave += 1
        self.flying = []
        for h, block in enumerate(got):
            self.parts[h].append(block)
            for wave in range(self.wave, self.group.bits):
                first = self.rows << (self.group.bits - 1 - wave)
                more = block[first : 2 * first].astype(F32)
                self.sent[h][wave] = (self.sent[h][wave].astype(F32) + more).astype(BF16)
        if self.wave < self.group.bits:
            now = self.chain.join(*[sent[self.wave] for sent in self.sent])
            for sent, value in zip(self.sent, now):
                sent[self.wave] = value
            self.start()

    def total(self):
        while self.flying:
            self.chain.end(self)
        return self.parts


class Weight:
    def __init__(self, pieces, rows, start, width):
        self.pieces, self.rows, self.start, self.width = pieces, rows, start, width
        self.model = len(pieces) * rows if len(pieces) > 1 else pieces[0].shape[0]

    def tiles(self, tile):
        first = self.start // tile
        return [pl.BlockSpec((self.rows, tile), lambda j: (0, first + j))] * len(self.pieces)


def nn(left, right):
    return lax.dot_general(left, right, (((1,), (0,)), ((), ())), preferred_element_type=F32)


def nt(left, right):
    return lax.dot_general(left, right, (((1,), (1,)), ((), ())), preferred_element_type=F32)


def tn(left, right):
    return lax.dot_general(left, right, (((0,), (0,)), ((), ())), preferred_element_type=F32)


def whole(shape):
    return pl.BlockSpec(shape, lambda *_: (0,) * len(shape))


def place(line_ref, j, width):
    return pl.ds(pl.multiple_of(line_ref[j] * width, 128), width)


def cut(width, j):
    return slice(j * width, (j + 1) * width)


def scale_of(values):
    return lax.rsqrt(jnp.mean(values * values, axis=-1, keepdims=True) + EPS)


def fetch_blocks(counts, refs, held, sems, k, slot, wait):
    first = 0
    for i, count in enumerate(counts):
        copies = []
        half = held.shape[2] // count
        for h in range(count):
            target = held.at[slot, :, pl.ds(h * half, half)]
            copies.append(pltpu.make_async_copy(refs[first + h], target, sems.at[slot, h]))
        first += count

        @pl.when(k == i)
        def _():
            for copy in copies:
                copy.wait() if wait else copy.start()


def fetched(counts, refs, held, sems):
    k = pl.program_id(0)

    @pl.when(k == 0)
    def _():
        fetch_blocks(counts, refs, held, sems, k, 0, False)

    fetch_blocks(counts, refs, held, sems, k + 1, (k + 1) % 2, False)
    fetch_blocks(counts, refs, held, sems, k, k % 2, True)
    return held.at[k % 2]


def norm_body(blocks, counts, line_ref, gain_ref, *refs):
    out_ref, held, sems = refs[sum(counts) :]
    x_ref = fetched(counts, refs, held, sems)
    width = out_ref.shape[1] // blocks
    scale = scale_of(x_ref[...].astype(F32))
    for j in range(blocks):
        part = x_ref[:, place(line_ref, j, width)].astype(F32)
        gain = gain_ref[0:1, cut(width, j)]
        out_ref[:, cut(width, j)] = (part * scale * gain).astype(BF16)


def order_body(blocks, counts, line_ref, gain_ref, *refs):
    out_ref, held, sems = refs[sum(counts) :]
    x_ref = fetched(counts, refs, held, sems)
    width = out_ref.shape[1] // blocks
    for j in range(blocks):
        out_ref[:, cut(width, j)] = x_ref[:, place(line_ref, j, width)]


def ordered(chain, body, line, gains, held):
    counts = [len(block) for block in held]
    rows, model = held[0][0].shape
    n = len(held)
    return chain.call(
        functools.partial(body, line.shape[0], counts),
        (n,),
        [whole(gains.shape)] + [pl.BlockSpec(memory_space=pl.ANY)] * sum(counts),
        [pl.BlockSpec((rows, model), lambda k, *_: (k, 0))],
        [((n * rows, model), BF16)],
        flops=20 * n * rows * model,
        scratch=[pltpu.VMEM((2, rows, model), BF16), pltpu.SemaphoreType.DMA((2, 2))],
        prefetch=1,
        moved=4 * n * rows * model,
    )(line, gains, *[array for block in held for array in block])[0]


def added(refs, span):
    total = refs[0][span, :].astype(F32)
    for ref in refs[1:]:
        total += ref[span, :].astype(F32)
    return total


def middle_body(blocks, m, line_ref, x_ref, gain_ref, *refs):
    middle_ref, out_ref = refs[2 * m :]
    width = x_ref.shape[1] // blocks
    half = x_ref.shape[1] // 2
    span = slice(None)
    middle_ref[:, :half] = added(refs[:m], span)
    middle_ref[:, half:] = added(refs[m : 2 * m], span)
    for j in range(blocks):
        here = x_ref[:, place(line_ref, j, width)].astype(F32)
        middle_ref[:, cut(width, j)] += here
    middle = middle_ref[...]
    normed = (middle * scale_of(middle) * gain_ref[1:2, :]).astype(BF16)
    for j in range(blocks):
        out_ref[:, place(line_ref, j, width)] = normed[:, cut(width, j)]


def result_body(blocks, m, line_ref, middle_ref, gain_ref, *refs):
    out_ref = refs[2 * m]
    width = middle_ref.shape[1] // blocks
    span = slice(None)
    total = middle_ref[...] + jnp.concatenate(
        [added(refs[:m], span), added(refs[m : 2 * m], span)], axis=1
    )
    for j in range(blocks):
        out_ref[:, place(line_ref, j, width)] = total[:, cut(width, j)].astype(BF16)


def second_back_body(blocks, m, line_ref, dy_ref, gain_ref, *refs):
    middle_ref, out_ref, low_ref = refs[2 * m :]
    width = dy_ref.shape[1] // blocks
    half = dy_ref.shape[1] // 2
    span = slice(None)
    low_ref[:, :half] = added(refs[:m], span).astype(BF16)
    low_ref[:, half:] = added(refs[m : 2 * m], span).astype(BF16)
    grad = jnp.concatenate(
        [low_ref[:, place(line_ref, j, width)] for j in range(blocks)], axis=1
    ).astype(F32)
    middle = middle_ref[...]
    scale = scale_of(middle)
    normed = middle * scale
    scaled = grad * gain_ref[1:2, :]
    out_ref[...] = scale * (scaled - normed * jnp.mean(scaled * normed, axis=-1, keepdims=True))
    for j in range(blocks):
        out_ref[:, cut(width, j)] += dy_ref[:, place(line_ref, j, width)].astype(F32)
    low_ref[...] = out_ref[...].astype(BF16)


def first_back_body(blocks, m, line_ref, x_ref, gain_ref, *refs):
    above_ref, out_ref = refs[2 * m :]
    width = x_ref.shape[1] // blocks
    span = slice(None)
    scale = scale_of(x_ref[...].astype(F32))
    normed = jnp.concatenate(
        [x_ref[:, place(line_ref, j, width)].astype(F32) for j in range(blocks)], axis=1
    ) * scale
    grad = jnp.concatenate([added(refs[:m], span), added(refs[m : 2 * m], span)], axis=1)
    scaled = grad * gain_ref[0:1, :]
    back = scale * (scaled - normed * jnp.mean(scaled * normed, axis=-1, keepdims=True))
    total = above_ref[...] + back
    for j in range(blocks):
        out_ref[:, place(line_ref, j, width)] = total[:, cut(width, j)]


def by_rows(chain, body, line, first, gains, parts, more, kinds):
    rows, model = first.shape
    half = model // 2
    tile = min(128, rows)
    row = pl.BlockSpec((tile, model), lambda i, *_: (i, 0))
    slim = pl.BlockSpec((tile, half), lambda i, *_: (i, 0))
    m = len(parts[0])
    return chain.call(
        functools.partial(body, line.shape[0], m),
        (rows // tile,),
        [row, whole(gains.shape)] + [slim] * (2 * m) + [row] * len(more),
        [row] * len(kinds),
        [((rows, model), kind) for kind in kinds],
        flops=20 * rows * model,
        prefetch=1,
        moved=rows * model * (2 * m + 4 * len(kinds)),
    )(line, first, gains, *parts[0], *parts[1], *more)


def rope_tables(place):
    half = HEAD_DIM // 2
    freq = THETA ** (-2.0 * jnp.arange(half, dtype=F32) / HEAD_DIM)
    angle = place.astype(F32)[:, None] * freq[None, :]
    cosine, sine = jnp.cos(angle), jnp.sin(angle)
    return (
        jnp.concatenate([cosine] * (PAIR // half), axis=1),
        jnp.concatenate([-sine, sine] * (PAIR // HEAD_DIM), axis=1),
    )


def turn(values):
    half = HEAD_DIM // 2
    width = values.shape[-1]
    lane = lax.broadcasted_iota(jnp.int32, values.shape, 1) % HEAD_DIM
    return jnp.where(
        lane < half, pltpu.roll(values, width - half, 1), pltpu.roll(values, half, 1)
    )


def joined(refs):
    return jnp.concatenate([r[...] for r in refs], axis=0)


def qkv_body(n, x_ref, cos_ref, sin_ref, *refs):
    weights, outs = refs[: 3 * n], refs[3 * n :]
    rows = x_ref.shape[0]
    tile = outs[0].shape[1]
    for i in range(3):
        weight = joined(weights[i * n : (i + 1) * n])
        for s in range(rows // SEQ):
            span = slice(s * SEQ, (s + 1) * SEQ)
            product = nn(x_ref[span, :], weight)
            if i == 2:
                outs[i][span, :] = product.astype(BF16)
                continue
            for t in range(tile // PAIR):
                here = product[:, t * PAIR : (t + 1) * PAIR]
                turned = here * cos_ref[...] + turn(here) * sin_ref[...]
                outs[i][span, t * PAIR : (t + 1) * PAIR] = turned.astype(BF16)


def project(chain, x, tables, query, key, value):
    rows, model = x.shape
    n, width = len(query.pieces), query.width
    tile = min(256, width)
    out = pl.BlockSpec((rows, tile), lambda j: (0, j))
    return chain.call(
        functools.partial(qkv_body, n),
        (width // tile,),
        [whole(x.shape), whole((SEQ, PAIR)), whole((SEQ, PAIR))]
        + query.tiles(tile)
        + key.tiles(tile)
        + value.tiles(tile),
        [out] * 3,
        [((rows, width), BF16)] * 3,
        flops=6 * rows * model * width,
        moved=2 * (rows * model + 3 * model * width + 3 * rows * width),
    )(x, *tables, *query.pieces, *key.pieces, *value.pieces)


def collect(counts, refs, held, sems):
    rows = held.shape[0] // len(counts)
    copies = []
    for k, count in enumerate(counts):
        half = held.shape[1] // count
        for h in range(count):
            target = held.at[pl.ds(k * rows, rows), pl.ds(h * half, half)]
            i = len(copies)
            copies.append(pltpu.make_async_copy(refs[i], target, sems.at[i]))
    for copy in copies:
        copy.start()
    for copy in copies:
        copy.wait()


def gate_body(counts, *refs):
    m = sum(counts)
    gate_ref, up_ref, hidden_ref, slope_ref, silu_ref, x_ref, sems = refs[m:]

    @pl.when(pl.program_id(0) == 0)
    def _():
        collect(counts, refs, x_ref, sems)

    for s in range(x_ref.shape[0] // SEQ):
        span = slice(s * SEQ, (s + 1) * SEQ)
        gate = nn(x_ref[span, :], gate_ref[...])
        up = nn(x_ref[span, :], up_ref[...])
        sigm = jax.nn.sigmoid(gate)
        silu = gate * sigm
        hidden_ref[span, :] = (silu * up).astype(BF16)
        silu_ref[span, :] = silu.astype(BF16)
        slope_ref[span, :] = (up * sigm * (1.0 + gate * (1.0 - sigm))).astype(BF16)


def collected(held):
    counts = [len(block) for block in held]
    rows, model = held[0][0].shape
    scratch = [
        pltpu.VMEM((len(held) * rows, model), BF16),
        pltpu.SemaphoreType.DMA((sum(counts),)),
    ]
    arrays = [array for block in held for array in block]
    return counts, arrays, [pl.BlockSpec(memory_space=pl.ANY)] * len(arrays), scratch


def gate_up(chain, held, gate, up):
    counts, arrays, specs, scratch = collected(held)
    rows, model = scratch[0].shape
    width = gate.shape[1]
    tile = min(256, width)
    out = pl.BlockSpec((rows, tile), lambda j: (0, j))
    return chain.call(
        functools.partial(gate_body, counts),
        (width // tile,),
        specs + [pl.BlockSpec((model, tile), lambda j: (0, j))] * 2,
        [out] * 3,
        [((rows, width), BF16)] * 3,
        flops=4 * rows * model * width,
        scratch=scratch,
        moved=2 * (rows * model + 2 * model * width + 3 * rows * width),
    )(*arrays, gate, up)


def hidden_back_body(n, g_ref, *refs):
    weight = joined(refs[:n])
    slope_ref, silu_ref, gate_ref, up_ref = refs[n:]
    for s in range(g_ref.shape[0] // SEQ):
        span = slice(s * SEQ, (s + 1) * SEQ)
        grad = nn(g_ref[span, :], weight)
        gate_ref[span, :] = (grad * slope_ref[span, :].astype(F32)).astype(BF16)
        up_ref[span, :] = (grad * silu_ref[span, :].astype(F32)).astype(BF16)


def hidden_back(chain, grads, down, slope, silu):
    rows, model = grads.shape
    n, width = len(down.pieces), down.width
    tile = min(256, width)
    out = pl.BlockSpec((rows, tile), lambda j: (0, j))
    return chain.call(
        functools.partial(hidden_back_body, n),
        (width // tile,),
        [whole(grads.shape)] + down.tiles(tile) + [out] * 2,
        [out] * 2,
        [((rows, width), BF16)] * 2,
        flops=2 * rows * model * width,
        moved=2 * (rows * model + model * width + 4 * rows * width),
    )(grads, *down.pieces, slope, silu)


def mixed_back_body(n, counts, *refs):
    m = sum(counts)
    out_ref, x_ref, sems = refs[m + n :]

    @pl.when(pl.program_id(0) == 0)
    def _():
        collect(counts, refs, x_ref, sems)

    out_ref[...] = nn(x_ref[...], joined(refs[m : m + n])).astype(BF16)


def mixed_back(chain, held, out):
    counts, arrays, specs, scratch = collected(held)
    rows, model = scratch[0].shape
    n, width = len(out.pieces), out.width
    tile = min(256, width)
    return chain.call(
        functools.partial(mixed_back_body, n, counts),
        (width // tile,),
        specs + out.tiles(tile),
        [pl.BlockSpec((rows, tile), lambda j: (0, j))],
        [((rows, width), BF16)],
        flops=2 * rows * model * width,
        scratch=scratch,
        moved=2 * (rows * model + model * width + rows * width),
    )(*arrays, *out.pieces)[0]


def trans_body(n, starts, count, targets, *refs):
    parts, blocks = len(starts), len(targets[0])
    lefts = refs[:parts]
    pieces, outs = refs[parts : parts + count], refs[parts + count : -4]
    held, ready, sems, out_sems = refs[-4:]
    j = pl.program_id(0)
    depth, width = held.shape[2:]
    rows = ready.shape[1] // blocks

    def copy(i, p, slot):
        source = pieces[p * n + i].at[pl.ds(0, depth), pl.ds(starts[p], width)]
        return pltpu.make_async_copy(source, held.at[slot, p], sems.at[slot, p])

    def whole_copy(step, p, slot):
        first = pl.multiple_of(step * depth, depth)
        source = pieces[p].at[pl.ds(first, depth), pl.ds(starts[p], width)]
        return pltpu.make_async_copy(source, held.at[slot, p], sems.at[slot, p])

    def fetch(step, slot):
        if count == parts:
            for p in range(parts):
                whole_copy(step, p, slot).start()
            return
        for i in range(n):

            @pl.when(step == i)
            def _():
                for p in range(parts):
                    copy(i, p, slot).start()

    def leave(slot, k, array, first, column):
        target = outs[array].at[pl.ds(first, rows), pl.ds(column, depth)]
        source = ready.at[slot, pl.ds(k * rows, rows), :]
        return pltpu.make_async_copy(source, target, out_sems.at[slot, k])

    def left(slot):
        for k in range(blocks):
            leave(slot, k, 0, 0, 0).wait()

    @pl.when(j == 0)
    def _():
        fetch(j, 0)

    @pl.when(j + 1 < n)
    def _():
        fetch(j + 1, (j + 1) % 2)

    slot = j % 2
    for p in range(parts):
        (whole_copy if count == parts else copy)(0, p, slot).wait()

    @pl.when(j >= 2)
    def _():
        left(slot)

    for s in range(blocks * rows // SEQ):
        span = slice(s * SEQ, (s + 1) * SEQ)
        total = nt(lefts[0][span, :], held[slot, 0])
        for p in range(1, parts):
            total += nt(lefts[p][span, :], held[slot, p])
        ready[slot, span, :] = total.astype(BF16)
    column = pl.multiple_of(j % (n // 2) * depth, 128)
    for h in range(2):

        @pl.when((j >= n // 2) == (h == 1))
        def _():
            for k, (array, first) in enumerate(targets[h]):
                leave(slot, k, array, first, column).start()

    @pl.when(j == n - 1)
    def _():
        left(1 - slot)
        left(slot)


def times_trans(chain, parts, group):
    weights = [weight for _, weight in parts]
    depth, width = weights[0].rows, weights[0].width
    n = weights[0].model // depth
    pieces = [piece for weight in weights for piece in weight.pieces]
    rows = parts[0][0].shape[0]
    half = weights[0].model // 2
    size = rows // group.size
    messages = group.messages()
    shapes = [((size, half), BF16)] * 2
    targets = [{0: (0, 0)}, {0: (1, 0)}]
    for h in range(2):
        for keys in messages[h]:
            for i, k in enumerate(keys):
                targets[h][k] = (len(shapes), i * size)
            shapes.append(((len(keys) * size, half), BF16))
    targets = [[t[k] for k in range(group.size)] for t in targets]
    anywhere = pl.BlockSpec(memory_space=pl.ANY)
    outs = chain.call(
        functools.partial(
            trans_body, n, [weight.start for weight in weights], len(pieces), targets
        ),
        (n,),
        [whole((rows, width))] * len(parts) + [anywhere] * len(pieces),
        [anywhere] * len(shapes),
        shapes,
        flops=4 * rows * half * width * len(parts),
        scratch=[
            pltpu.VMEM((2, len(parts), depth, width), BF16),
            pltpu.VMEM((2, rows, depth), BF16),
            pltpu.SemaphoreType.DMA((2, len(parts))),
            pltpu.SemaphoreType.DMA((2, group.size)),
        ],
        moved=2 * (2 * rows * half + len(parts) * (rows + 2 * half) * width),
    )(*[left for left, _ in parts], *pieces)
    m = group.bits
    return outs[:2], [outs[2 : 2 + m], outs[2 + m :]]


def grad_body(parts, got, blocks, steps, *refs):
    lefts, refs = refs[:blocks], refs[blocks:]
    rights, refs = refs[:parts], refs[parts:]
    got_ref = refs[0] if got else None
    outs, turned = refs[got:-1], refs[-1]
    j = pl.program_id(0)

    @pl.when(j == 0)
    def _():
        rows = turned.shape[1] // blocks
        for k in range(blocks):
            turned[:, cut(rows, k)] = lefts[k][...].T

    for i in range(parts):

        @pl.when((j >= i * steps) & (j < (i + 1) * steps))
        def _():
            total = nn(turned[...], rights[i][...])
            if got:
                total += got_ref[...].astype(F32)
            total = total.astype(BF16)
            first = 0
            for out_ref in outs:
                count = out_ref.shape[0]
                out_ref[...] = total[first : first + count]
                first += count


def weight_grads(chain, left, which, rights, got=None, bits=0):
    rows, width = rights[0].shape
    parts = len(rights)
    tile = min(512, width)
    steps = width // tile
    if isinstance(left, list):
        lefts = [block[0] if len(block) == 1 else block[which] for block in left]
        half = left[0][0].shape[1] // 2
        places = [which if len(block) == 1 else 0 for block in left]
    else:
        lefts, places, half = [left], [which], left.shape[1] // 2
    blocks = len(lefts)
    ins = [
        pl.BlockSpec((rows // blocks, half), functools.partial(lambda at, j: (0, at), at))
        for at in places
    ]
    for i in range(parts):
        ins.append(
            pl.BlockSpec(
                (rows, tile),
                functools.partial(
                    lambda first, j: (0, jnp.clip(j - first, 0, steps - 1)), i * steps
                ),
            )
        )
    column = lambda j: (0, j)
    more = [] if got is None else [got]
    sizes = [half >> bits]
    for p in range(bits):
        sizes += [sizes[0], ((1 << p) - 1) * sizes[0]] if p else [sizes[0]]
    return chain.call(
        functools.partial(grad_body, parts, len(more), blocks, steps),
        (parts * steps,),
        ins + [pl.BlockSpec((half, tile), column)] * len(more),
        [pl.BlockSpec((size, tile), column) for size in sizes],
        [((size, parts * width), BF16) for size in sizes],
        flops=2 * rows * half * width * parts,
        scratch=[pltpu.VMEM((half, rows), BF16)],
        moved=2 * (rows * half + parts * (rows + half) * width),
    )(*lefts, *rights, *more)


def full_grad_body(counts, *refs):
    right_ref, out_ref, turned, held, sems = refs[sum(counts) :]

    @pl.when(pl.program_id(0) == 0)
    def _():
        collect(counts, refs, held, sems)
        rows = held.shape[0] // len(counts)
        for k in range(len(counts)):
            turned[:, cut(rows, k)] = held[cut(rows, k), :].T

    half = out_ref.shape[0] // 2
    for h in range(2):
        span = slice(h * half, (h + 1) * half)
        out_ref[span, :] = nn(turned[span, :], right_ref[...]).astype(BF16)


def full_grad(chain, left, right):
    counts, arrays, specs, scratch = collected(left)
    rows, model = scratch[0].shape
    width = right.shape[1]
    tile = min(512, width)
    return chain.call(
        functools.partial(full_grad_body, counts),
        (width // tile,),
        specs + [pl.BlockSpec((rows, tile), lambda j: (0, j))],
        [pl.BlockSpec((model, tile), lambda j: (0, j))],
        [((model, width), BF16)],
        flops=2 * rows * model * width,
        scratch=[pltpu.VMEM((model, rows), BF16)] + scratch,
        moved=2 * (rows * model + (rows + model) * width),
    )(*arrays, right)[0]


def causal(scores):
    past = scores.shape[0] - HALF_SEQ
    key = lax.broadcasted_iota(jnp.int32, (HALF_SEQ, HALF_SEQ), 0)
    query = lax.broadcasted_iota(jnp.int32, (HALF_SEQ, HALF_SEQ), 1)
    last = jnp.where(key <= query, scores[past:], -1e30)
    return last if past == 0 else jnp.concatenate([scores[:past], last], axis=0)


def head_of(h):
    return slice(h * HEAD_DIM, (h + 1) * HEAD_DIM)


def span_of(b):
    return slice(b * HALF_SEQ, (b + 1) * HALF_SEQ)


def in_place(shift_ref, ref, count):
    rows = SEQ // count
    spans = [pl.ds(pl.multiple_of((i ^ shift_ref[0]) * rows, rows), rows) for i in range(count)]
    return jnp.concatenate([ref[span, :] for span in spans], axis=0)


def put_back(shift_ref, ref, count, values):
    rows = SEQ // count
    for i in range(count):
        ref[pl.ds(pl.multiple_of((i ^ shift_ref[0]) * rows, rows), rows), :] = values[cut(rows, i)]


def attend_body(count, shift_ref, q_ref, k_ref, v_ref, out_ref, sum_ref):
    queries, keys = in_place(shift_ref, q_ref, count), in_place(shift_ref, k_ref, count)
    values = in_place(shift_ref, v_ref, count).astype(F32).T.astype(BF16)
    heads = []
    for h in range(2):
        blocks = []
        for b in range(2):
            reach = (b + 1) * HALF_SEQ
            query = queries[span_of(b), head_of(h)] * BF16(FACTOR)
            scores = causal(nt(keys[:reach, head_of(h)], query))
            top = jnp.max(scores, axis=0, keepdims=True)
            expo = jnp.exp(scores - top)
            total = jnp.sum(expo, axis=0, keepdims=True)
            mixed = nn(values[head_of(h), :reach], expo.astype(BF16))
            blocks.append(mixed * (1.0 / total))
            sum_ref[0, 0, h : h + 1, span_of(b)] = top + jnp.log(total)
        heads.append(jnp.concatenate(blocks, axis=1))
    put_back(shift_ref, out_ref, count, jnp.concatenate(heads, axis=0).T.astype(BF16))


def attend(chain, shift, count, query, key, value):
    rows, width = query.shape
    seqs, pairs = rows // SEQ, width // PAIR
    tile = pl.BlockSpec((SEQ, PAIR), lambda s, p, _: (s, p))
    return chain.call(
        functools.partial(attend_body, count),
        (seqs, pairs),
        [tile] * 3,
        [tile, pl.BlockSpec((1, 1, 2, SEQ), lambda s, p, _: (s, p, 0, 0))],
        [((rows, width), BF16), ((seqs, pairs, 2, SEQ), F32)],
        flops=16 * rows * width * SEQ,
        prefetch=1,
        moved=8 * rows * width,
    )(shift, query, key, value)


def attend_back_body(
    count, shift_ref, q_ref, k_ref, v_ref, g_ref, sum_ref, cos_ref, sin_ref, dq_ref, dk_ref, dv_ref
):
    queries, keys, values, grads = (
        in_place(shift_ref, ref, count) for ref in (q_ref, k_ref, v_ref, g_ref)
    )
    turned = keys.astype(F32).T.astype(BF16)
    dq_heads, dk_heads, dv_heads = [], [], []
    for h in range(2):
        dq, dk, dv = [], [], []
        for b in range(2):
            reach = (b + 1) * HALF_SEQ
            query = queries[span_of(b), head_of(h)]
            grad = grads[span_of(b), head_of(h)]
            scores = causal(nt(keys[:reach, head_of(h)], query * BF16(FACTOR)))
            probs = jnp.exp(scores - sum_ref[0, 0, h : h + 1, span_of(b)])
            probs_grad = nt(values[:reach, head_of(h)], grad)
            inner = jnp.sum(probs * probs_grad, axis=0, keepdims=True)
            score_grad = (probs * (probs_grad - inner)).astype(BF16)
            dv.append(nn(probs.astype(BF16), grad))
            dk.append(nn(score_grad, query))
            dq.append(nn(turned[head_of(h), :reach], score_grad))
        for parts, heads in ((dk, dk_heads), (dv, dv_heads)):
            heads.append(
                jnp.concatenate([parts[1][:HALF_SEQ] + parts[0], parts[1][HALF_SEQ:]], axis=0)
            )
        dq_heads.append(jnp.concatenate(dq, axis=1))
    dq = jnp.concatenate(dq_heads, axis=0).T * FACTOR
    dk = jnp.concatenate(dk_heads, axis=1) * FACTOR
    dv = jnp.concatenate(dv_heads, axis=1).astype(BF16)
    cosine, sine = cos_ref[...], sin_ref[...]
    put_back(shift_ref, dq_ref, count, (dq * cosine - turn(dq) * sine).astype(BF16))
    put_back(shift_ref, dk_ref, count, (dk * cosine - turn(dk) * sine).astype(BF16))
    put_back(shift_ref, dv_ref, count, dv)


def attend_back(chain, shift, count, query, key, value, grad, logsum, tables):
    rows, width = query.shape
    seqs, pairs = rows // SEQ, width // PAIR
    tile = pl.BlockSpec((SEQ, PAIR), lambda s, p, _: (s, p))
    return chain.call(
        functools.partial(attend_back_body, count),
        (seqs, pairs),
        [tile] * 4
        + [pl.BlockSpec((1, 1, 2, SEQ), lambda s, p, _: (s, p, 0, 0))]
        + [whole((SEQ, PAIR))] * 2,
        [tile] * 3,
        [((rows, width), BF16)] * 3,
        flops=40 * rows * width * SEQ,
        prefetch=1,
        moved=14 * rows * width,
    )(shift, query, key, value, grad, logsum, *tables)


def local(
    chips,
    group,
    tokens,
    attn_gain,
    query_weight,
    key_weight,
    value_weight,
    output_weight,
    ffn_gain,
    gate_weight,
    up_weight,
    down_weight,
    cotangent,
):
    line = jnp.asarray(chips.table)[lax.axis_index("dp")]
    rows, model = tokens.shape
    count = SEQ // rows
    shift = lax.axis_index("tensor") % count
    row = jnp.arange(SEQ, dtype=jnp.int32)
    places = rope_tables(row)
    tables = rope_tables((row // rows ^ shift) * rows + row % rows)
    shift = jnp.reshape(shift, (1,)).astype(jnp.int32)
    depth, own = query_weight.shape
    hidden_units = gate_weight.shape[1]
    chain = Chain()

    def gather(piece):
        return Gather(chips, chain, chain.join(piece)[0])

    def spread_of(values):
        return Spread(group, chain, chain.join(values)[0])

    def fold_of(part):
        own_part, sent = part
        sent = chain.join(*sent[0], *sent[1])
        return Fold(group, chain, own_part, [sent[: group.bits], sent[group.bits :]])

    def grads_of(left, rights):
        got = [None]
        chain.ask(weight_grads(chain, left, 1, rights)[0], got, 0, chips.other)

        def mine():
            if got[0] is None:
                chain.flush()
            return Sums(chips, chain, weight_grads(chain, left, 0, rights, got[0], chips.bits))

        return mine

    def gather_whole(weight):
        return lax.all_gather(chain.join(weight)[0], "dp", axis=0, tiled=True)

    def sum_whole(grad):
        return lax.psum_scatter(grad, "dp", scatter_dimension=0, tiled=True).astype(F32)

    extra = jnp.concatenate([attn_gain, ffn_gain, jnp.zeros((4 * own - 2 * depth,), BF16)])
    attn = jnp.concatenate([query_weight, key_weight, value_weight, output_weight.T], axis=1)
    attn = gather(jnp.concatenate([attn, jnp.broadcast_to(extra, (16, 4 * own))], axis=0))
    spread = spread_of(tokens)
    chain.end(attn, spread)
    all_gate = gather_whole(gate_weight)
    chain.end(attn, spread)
    all_tokens = spread.blocks()
    attn = attn.pieces()
    spread = spread_of(cotangent)
    w_query, w_key, w_value, w_output = [Weight(attn, depth, i * own, own) for i in range(4)]
    gains = jnp.concatenate(
        [piece[depth : depth + 1, : 2 * depth].reshape(2, depth) for piece in attn], axis=1
    ).astype(F32)

    group_one = ordered(chain, norm_body, line, gains, all_tokens)
    all_up = gather_whole(up_weight)
    query, key, value = project(chain, group_one, tables, w_query, w_key, w_value)
    mixed, logsum = attend(chain, shift, count, query, key, value)
    chain.end(spread)
    out_part = times_trans(chain, [(mixed, w_output)], group)
    fold = fold_of(out_part)
    chain.end(spread)
    grad_rows = ordered(chain, order_body, line, gains, spread.blocks())
    chain.end(fold)
    attended = fold.total()
    middle, second = by_rows(
        chain, middle_body, line, tokens, gains, attended, [], [F32, BF16]
    )
    spread = spread_of(second)
    down = gather(down_weight.T)
    chain.end(spread)
    group_two = spread.blocks()
    w_gate = Weight([all_gate], depth, 0, hidden_units)
    w_up = Weight([all_up], depth, 0, hidden_units)
    hidden, slope, silu = gate_up(chain, group_two, all_gate, all_up)

    chain.end(down)
    mine = grads_of(grad_rows, [hidden])
    down_sum = mine()
    w_down = Weight(down.pieces(), depth, 0, hidden_units)
    gate_grad, up_grad = hidden_back(chain, grad_rows, w_down, slope, silu)
    chain.end(down_sum)
    second_part = times_trans(chain, [(gate_grad, w_gate), (up_grad, w_up)], group)
    fold = fold_of(second_part)
    gate_sum = sum_whole(full_grad(chain, group_two, gate_grad))
    chain.end(fold, down_sum)
    up_sum = sum_whole(full_grad(chain, group_two, up_grad))
    second_grad = fold.total()
    middle_grad, low_grad = by_rows(
        chain, second_back_body, line, cotangent, gains, second_grad, [middle], [F32, BF16]
    )
    spread = spread_of(low_grad)
    result_part = times_trans(chain, [(hidden, w_down)], group)
    chain.end(spread, down_sum)
    attn_grads = spread.blocks()
    down_sum = down_sum.total()

    mixed_grad = mixed_back(chain, attn_grads, w_output)
    fold = fold_of(result_part)
    query_back, key_back, value_back = attend_back(
        chain, shift, count, query, key, value, mixed_grad, logsum, places
    )
    mine = grads_of(group_one, [query_back, key_back, value_back])
    chain.end(fold)
    mine_out = grads_of(attn_grads, [mixed])
    qkv_sum = mine()
    result_part = fold.total()
    first_part = times_trans(
        chain, [(query_back, w_query), (key_back, w_key), (value_back, w_value)], group
    )
    fold = fold_of(first_part)
    out_sum = mine_out()
    (layer_out,) = by_rows(chain, result_body, line, middle, gains, result_part, [], [BF16])
    chain.end(fold, qkv_sum)
    first_grad = fold.total()
    (input_grad,) = by_rows(
        chain, first_back_body, line, tokens, gains, first_grad, [middle_grad], [F32]
    )
    chain.end(qkv_sum, out_sum)
    qkv_sum = qkv_sum.total()
    query_sum, key_sum, value_sum = [qkv_sum[:, cut(own, i)] for i in range(3)]

    def inner(weight, grad):
        return jnp.sum(weight.astype(F32) * grad, axis=1)

    gain_one_part = (
        inner(query_weight, query_sum) + inner(key_weight, key_sum) + inner(value_weight, value_sum)
    ) / attn_gain.astype(F32)
    gain_two_part = (inner(gate_weight, gate_sum) + inner(up_weight, up_sum)) / ffn_gain.astype(F32)
    gain_one_total, gain_two_total = lax.psum((gain_one_part, gain_two_part), "tensor")
    (gain_one_total,) = chain.join(gain_one_total)
    out_sum = out_sum.total()
    return (
        layer_out,
        input_grad,
        gain_one_total,
        query_sum,
        key_sum,
        value_sum,
        out_sum.T,
        gain_two_total,
        gate_sum,
        up_sum,
        down_sum.T,
    )


def solution(mesh):
    in_specs = (
        P(("dp", "tensor"), None),
        P("dp"),
        P("dp", "tensor"),
        P("dp", "tensor"),
        P("dp", "tensor"),
        P("tensor", "dp"),
        P("dp"),
        P("dp", "tensor"),
        P("dp", "tensor"),
        P("tensor", "dp"),
        P(("dp", "tensor"), None),
    )
    out_specs = (
        P(("dp", "tensor"), None),
        P(("dp", "tensor"), None),
        P("dp"),
        P("dp", "tensor"),
        P("dp", "tensor"),
        P("dp", "tensor"),
        P("tensor", "dp"),
        P("dp"),
        P("dp", "tensor"),
        P("dp", "tensor"),
        P("tensor", "dp"),
    )
    chips = Chips(mesh.shape["dp"])
    size = mesh.shape["tensor"]
    links = [[(i, i ^ 1 << b) for i in range(size)] for b in range(size.bit_length() - 1)]
    group = Group(links, "tensor")

    def run(*arrays):
        return local(chips, group, *arrays)

    return jax.shard_map(run, mesh=mesh, in_specs=in_specs, out_specs=out_specs, check_vma=False)
```

```python
import functools

import jax
import jax.numpy as jnp
import numpy as np
from jax import lax
from jax.experimental import pallas as pl
from jax.experimental.pallas import tpu as pltpu
from jax.sharding import PartitionSpec as P

HEAD_DIM = 64
SEQ = 512
EPS = 1e-05
THETA = 130000.0
BF16 = jnp.bfloat16
F32 = jnp.float32
FACTOR = HEAD_DIM**-0.5
PAIR = 2 * HEAD_DIM
HALF_SEQ = SEQ // 2
VMEM_LIMIT = 58 << 20
COST_SHARE = 16


class Chain:
    def __init__(self):
        self.token = jnp.zeros((8, 128), F32)
        self.swaps, self.asked = [], []

    def join(self, *values):
        *values, self.token = lax.optimization_barrier((*values, self.token))
        return values

    def gate(self, *values):
        swaps, self.swaps = self.swaps, []
        asked, self.asked = self.asked, []
        joined = self.join(
            *values, *[held[i] for held, i in swaps], *[source for source, _, _, _ in asked]
        )
        for (held, i), value in zip(swaps, joined[len(values) :]):
            held[i] = value
        for (_, held, i, swap), value in zip(asked, joined[len(values) + len(swaps) :]):
            held[i] = swap(value)
            self.swaps.append((held, i))
        return joined[: len(values)]

    def end(self, *transfers):
        counts = [len(t.flying) for t in transfers]
        got = self.gate(*[value for t in transfers for value in t.flying])
        for t, count in zip(transfers, counts):
            t.go_on(got[:count])
            got = got[count:]

    def ask(self, source, held, i, swap):
        self.asked.append((source, held, i, swap))

    def flush(self):
        for source, held, i, swap in self.asked:
            held[i] = swap(source)
        self.asked = []

    def call(self, body, grid, ins, outs, shapes, flops, scratch=(), prefetch=0, moved=0):
        first = prefetch + len(ins)
        second = first + 1 + len(outs)
        anywhere = pl.BlockSpec(memory_space=pl.ANY)

        def wrapped(*refs):
            body(*refs[:first], *refs[first + 1 : second], *refs[second + 1 :])

        run = pl.pallas_call(
            wrapped,
            grid_spec=pltpu.PrefetchScalarGridSpec(
                num_scalar_prefetch=prefetch,
                grid=grid,
                in_specs=[*ins, anywhere],
                out_specs=[*outs, anywhere],
                scratch_shapes=list(scratch),
            ),
            out_shape=[jax.ShapeDtypeStruct(s, t) for s, t in [*shapes, ((8, 128), F32)]],
            compiler_params=pltpu.CompilerParams(
                vmem_limit_bytes=VMEM_LIMIT, dimension_semantics=("arbitrary",) * len(grid)
            ),
            cost_estimate=pl.CostEstimate(
                flops=flops // COST_SHARE, bytes_accessed=moved // COST_SHARE, transcendentals=0
            ),
        )

        def with_token(*args):
            *results, self.token = run(*args, self.token)
            return results

        return with_token


class Chips:
    def __init__(self, size):
        self.bits = (size // 2).bit_length() - 1
        self.size = size
        self.swap = [(i, i ^ 1) for i in range(size)]
        self.links = [
            [(i, i ^ 2 << self.bits - 1 - p) for i in range(size)] for p in range(self.bits)
        ]
        flips = [
            sum(1 << self.bits - 1 - p for p in range(self.bits) if v >> p & 1)
            for v in range(1 << self.bits)
        ]
        table = [[i ^ 2 * f for f in flips] + [i ^ 2 * f ^ 1 for f in flips] for i in range(size)]
        self.table = np.array(table, np.int32)

    def send(self, value, p):
        return lax.ppermute(value, "dp", self.links[p])

    def other(self, value):
        return lax.ppermute(value, "dp", self.swap)


class Gather:
    def __init__(self, chips, chain, piece):
        self.chips, self.chain = chips, chain
        self.own = [piece] + [None] * (2**chips.bits - 1)
        self.others = list(self.own)
        self.ask(0)
        self.keys = [1 << p for p in range(chips.bits)]
        self.flying = [chips.send(piece, p) for p in range(chips.bits)]

    def ask(self, v):
        self.chain.ask(self.own[v], self.others, v, self.chips.other)

    def go_on(self, got):
        keys, self.keys, self.flying = self.keys, [], []
        for v, piece in zip(keys, got):
            self.own[v] = piece
            for p in range(v.bit_length(), self.chips.bits):
                self.keys.append(v | 1 << p)
                self.flying.append(self.chips.send(piece, p))
        for v in keys:
            self.ask(v)

    def pieces(self):
        while self.flying:
            self.chain.end(self)
        self.chain.flush()
        return self.own + self.others


class Sums:
    def __init__(self, chips, chain, mine):
        self.chips, self.chain = chips, chain
        self.parts = [mine[0]]
        mine = list(mine[1:])
        self.direct, self.passed = [], []
        for p in range(chips.bits):
            self.direct.append(mine.pop(0))
            self.passed.append(mine.pop(0) if p else None)
        self.p = chips.bits - 1
        self.kinds = [self.p]
        self.flying = [chips.send(self.passed[self.p], self.p)]

    def go_on(self, got):
        rows = self.parts[0].shape[0]
        kinds, self.kinds, self.flying = self.kinds, [], []
        if self.p < 0:
            self.last.append(got[0])
            return
        for kind, block in zip(kinds, got):
            if kind == "direct":
                self.parts.append(block)
            elif kind == "half":
                self.last = [block]
            else:
                add = lambda held, first: (
                    held.astype(F32) + block[first * rows : first * rows + held.shape[0]].astype(F32)
                ).astype(BF16)
                for q in range(kind):
                    self.direct[q] = add(self.direct[q], (1 << q) - 1)
                    if q:
                        self.passed[q] = add(self.passed[q], 1 << q)
        p, self.p = self.p, self.p - 1
        if p > 0:
            self.send("direct", self.direct[p], p)
        if p > 1:
            self.send(p - 1, self.passed[p - 1], p - 1)
        half = self.direct[0].shape[1] // 2
        if p == 1:
            self.send("half", self.direct[0][:, :half], 0)
        if p == 0:
            self.send("last", self.direct[0][:, half:], 0)

    def send(self, kind, value, p):
        (value,) = self.chain.join(value)
        self.kinds.append(kind)
        self.flying.append(self.chips.send(value, p))

    def total(self):
        while self.flying:
            self.chain.end(self)
        total = self.parts[0].astype(F32)
        for part in self.parts[1:]:
            total = total + part.astype(F32)
        half = total.shape[1] // 2
        return jnp.concatenate(
            [total[:, :half] + self.last[0].astype(F32), total[:, half:] + self.last[1].astype(F32)],
            axis=1,
        )


class Group:
    def __init__(self, links, axes):
        self.links, self.axes = links, axes
        self.bits = len(links)
        self.size = 1 << self.bits
        self.orders = (list(range(self.bits)), list(range(self.bits))[::-1])

    def send(self, value, bit):
        return lax.ppermute(value, self.axes, self.links[bit])

    def messages(self):
        found = []
        for order in self.orders:
            found.append([])
            for top in reversed(range(self.bits)):
                found[-1].append(
                    [
                        1 << order[top] | sum(1 << order[p] for p in range(top) if v >> p & 1)
                        for v in range(1 << top)
                    ]
                )
        return found


class Spread:
    def __init__(self, group, chain, rows):
        self.group, self.chain = group, chain
        self.held = {0: [rows]}
        self.keys = [(1 << b, None) for b in range(group.bits)]
        self.flying = [group.send(rows, b) for b in range(group.bits)]

    def go_on(self, got):
        fresh = list(zip(self.keys, got))
        self.keys, self.flying = [], []
        for (k, h), block in fresh:
            if h is None:
                self.held[k] = [block]
            else:
                self.held.setdefault(k, [None, None])[h] = block
        for (k, h), block in fresh:
            for way, order in enumerate(self.group.orders):
                if h is not None and h != way:
                    continue
                half = block.shape[1] // 2
                top = max(i for i, bit in enumerate(order) if k >> bit & 1)
                for i in range(top + 1, len(order)):
                    part = block if h is not None else block[:, way * half : (way + 1) * half]
                    self.keys.append((k | 1 << order[i], way))
                    self.flying.append(self.group.send(part, order[i]))

    def blocks(self):
        while self.flying:
            self.chain.end(self)
        return [self.held[k] for k in range(self.group.size)]


class Fold:
    def __init__(self, group, chain, own, sent):
        self.group, self.chain = group, chain
        self.rows = own[0].shape[0]
        self.sent = [list(half) for half in sent]
        self.parts = [[half] for half in own]
        self.wave = 0
        self.start()

    def start(self):
        self.flying = [
            self.group.send(self.sent[h][self.wave], order[self.group.bits - 1 - self.wave])
            for h, order in enumerate(self.group.orders)
        ]

    def go_on(self, got):
        self.wave += 1
        self.flying = []
        for h, block in enumerate(got):
            self.parts[h].append(block)
            for wave in range(self.wave, self.group.bits):
                first = self.rows << (self.group.bits - 1 - wave)
                more = block[first : 2 * first].astype(F32)
                self.sent[h][wave] = (self.sent[h][wave].astype(F32) + more).astype(BF16)
        if self.wave < self.group.bits:
            now = self.chain.join(*[sent[self.wave] for sent in self.sent])
            for sent, value in zip(self.sent, now):
                sent[self.wave] = value
            self.start()

    def total(self):
        while self.flying:
            self.chain.end(self)
        return self.parts


class Weight:
    def __init__(self, pieces, rows, start, width):
        self.pieces, self.rows, self.start, self.width = pieces, rows, start, width
        self.model = len(pieces) * rows if len(pieces) > 1 else pieces[0].shape[0]

    def tiles(self, tile):
        first = self.start // tile
        return [pl.BlockSpec((self.rows, tile), lambda j: (0, first + j))] * len(self.pieces)


def nn(left, right):
    return lax.dot_general(left, right, (((1,), (0,)), ((), ())), preferred_element_type=F32)


def nt(left, right):
    return lax.dot_general(left, right, (((1,), (1,)), ((), ())), preferred_element_type=F32)


def tn(left, right):
    return lax.dot_general(left, right, (((0,), (0,)), ((), ())), preferred_element_type=F32)


def whole(shape):
    return pl.BlockSpec(shape, lambda *_: (0,) * len(shape))


def place(line_ref, j, width):
    return pl.ds(pl.multiple_of(line_ref[j] * width, 128), width)


def cut(width, j):
    return slice(j * width, (j + 1) * width)


def scale_of(values):
    return lax.rsqrt(jnp.mean(values * values, axis=-1, keepdims=True) + EPS)


def fetch_blocks(counts, refs, held, sems, k, slot, wait):
    first = 0
    for i, count in enumerate(counts):
        copies = []
        half = held.shape[2] // count
        for h in range(count):
            target = held.at[slot, :, pl.ds(h * half, half)]
            copies.append(pltpu.make_async_copy(refs[first + h], target, sems.at[slot, h]))
        first += count

        @pl.when(k == i)
        def _():
            for copy in copies:
                copy.wait() if wait else copy.start()


def fetched(counts, refs, held, sems):
    k = pl.program_id(0)

    @pl.when(k == 0)
    def _():
        fetch_blocks(counts, refs, held, sems, k, 0, False)

    fetch_blocks(counts, refs, held, sems, k + 1, (k + 1) % 2, False)
    fetch_blocks(counts, refs, held, sems, k, k % 2, True)
    return held.at[k % 2]


def norm_body(blocks, counts, line_ref, gain_ref, *refs):
    out_ref, held, sems = refs[sum(counts) :]
    x_ref = fetched(counts, refs, held, sems)
    width = out_ref.shape[1] // blocks
    scale = scale_of(x_ref[...].astype(F32))
    for j in range(blocks):
        part = x_ref[:, place(line_ref, j, width)].astype(F32)
        gain = gain_ref[0:1, cut(width, j)]
        out_ref[:, cut(width, j)] = (part * scale * gain).astype(BF16)


def order_body(blocks, counts, line_ref, gain_ref, *refs):
    out_ref, held, sems = refs[sum(counts) :]
    x_ref = fetched(counts, refs, held, sems)
    width = out_ref.shape[1] // blocks
    for j in range(blocks):
        out_ref[:, cut(width, j)] = x_ref[:, place(line_ref, j, width)]


def ordered(chain, body, line, gains, held):
    counts = [len(block) for block in held]
    rows, model = held[0][0].shape
    n = len(held)
    return chain.call(
        functools.partial(body, line.shape[0], counts),
        (n,),
        [whole(gains.shape)] + [pl.BlockSpec(memory_space=pl.ANY)] * sum(counts),
        [pl.BlockSpec((rows, model), lambda k, *_: (k, 0))],
        [((n * rows, model), BF16)],
        flops=20 * n * rows * model,
        scratch=[pltpu.VMEM((2, rows, model), BF16), pltpu.SemaphoreType.DMA((2, 2))],
        prefetch=1,
        moved=4 * n * rows * model,
    )(line, gains, *[array for block in held for array in block])[0]


def added(refs, span):
    total = refs[0][span, :].astype(F32)
    for ref in refs[1:]:
        total += ref[span, :].astype(F32)
    return total


def middle_body(blocks, m, line_ref, x_ref, gain_ref, *refs):
    middle_ref, out_ref = refs[2 * m :]
    width = x_ref.shape[1] // blocks
    half = x_ref.shape[1] // 2
    span = slice(None)
    middle_ref[:, :half] = added(refs[:m], span)
    middle_ref[:, half:] = added(refs[m : 2 * m], span)
    for j in range(blocks):
        here = x_ref[:, place(line_ref, j, width)].astype(F32)
        middle_ref[:, cut(width, j)] += here
    middle = middle_ref[...]
    normed = (middle * scale_of(middle) * gain_ref[1:2, :]).astype(BF16)
    for j in range(blocks):
        out_ref[:, place(line_ref, j, width)] = normed[:, cut(width, j)]


def result_body(blocks, m, line_ref, middle_ref, gain_ref, *refs):
    out_ref = refs[2 * m]
    width = middle_ref.shape[1] // blocks
    span = slice(None)
    total = middle_ref[...] + jnp.concatenate(
        [added(refs[:m], span), added(refs[m : 2 * m], span)], axis=1
    )
    for j in range(blocks):
        out_ref[:, place(line_ref, j, width)] = total[:, cut(width, j)].astype(BF16)


def second_back_body(blocks, m, line_ref, dy_ref, gain_ref, *refs):
    middle_ref, out_ref, low_ref = refs[2 * m :]
    width = dy_ref.shape[1] // blocks
    half = dy_ref.shape[1] // 2
    span = slice(None)
    low_ref[:, :half] = added(refs[:m], span).astype(BF16)
    low_ref[:, half:] = added(refs[m : 2 * m], span).astype(BF16)
    grad = jnp.concatenate(
        [low_ref[:, place(line_ref, j, width)] for j in range(blocks)], axis=1
    ).astype(F32)
    middle = middle_ref[...]
    scale = scale_of(middle)
    normed = middle * scale
    scaled = grad * gain_ref[1:2, :]
    out_ref[...] = scale * (scaled - normed * jnp.mean(scaled * normed, axis=-1, keepdims=True))
    for j in range(blocks):
        out_ref[:, cut(width, j)] += dy_ref[:, place(line_ref, j, width)].astype(F32)
    low_ref[...] = out_ref[...].astype(BF16)


def first_back_body(blocks, m, line_ref, x_ref, gain_ref, *refs):
    above_ref, out_ref = refs[2 * m :]
    width = x_ref.shape[1] // blocks
    span = slice(None)
    scale = scale_of(x_ref[...].astype(F32))
    normed = jnp.concatenate(
        [x_ref[:, place(line_ref, j, width)].astype(F32) for j in range(blocks)], axis=1
    ) * scale
    grad = jnp.concatenate([added(refs[:m], span), added(refs[m : 2 * m], span)], axis=1)
    scaled = grad * gain_ref[0:1, :]
    back = scale * (scaled - normed * jnp.mean(scaled * normed, axis=-1, keepdims=True))
    total = above_ref[...] + back
    for j in range(blocks):
        out_ref[:, place(line_ref, j, width)] = total[:, cut(width, j)]


def by_rows(chain, body, line, first, gains, parts, more, kinds):
    rows, model = first.shape
    half = model // 2
    tile = min(128, rows)
    row = pl.BlockSpec((tile, model), lambda i, *_: (i, 0))
    slim = pl.BlockSpec((tile, half), lambda i, *_: (i, 0))
    m = len(parts[0])
    return chain.call(
        functools.partial(body, line.shape[0], m),
        (rows // tile,),
        [row, whole(gains.shape)] + [slim] * (2 * m) + [row] * len(more),
        [row] * len(kinds),
        [((rows, model), kind) for kind in kinds],
        flops=20 * rows * model,
        prefetch=1,
        moved=rows * model * (2 * m + 4 * len(kinds)),
    )(line, first, gains, *parts[0], *parts[1], *more)


def rope_tables(place):
    half = HEAD_DIM // 2
    freq = THETA ** (-2.0 * jnp.arange(half, dtype=F32) / HEAD_DIM)
    angle = place.astype(F32)[:, None] * freq[None, :]
    cosine, sine = jnp.cos(angle), jnp.sin(angle)
    return (
        jnp.concatenate([cosine] * (PAIR // half), axis=1),
        jnp.concatenate([-sine, sine] * (PAIR // HEAD_DIM), axis=1),
    )


def turn(values):
    half = HEAD_DIM // 2
    width = values.shape[-1]
    lane = lax.broadcasted_iota(jnp.int32, values.shape, 1) % HEAD_DIM
    return jnp.where(
        lane < half, pltpu.roll(values, width - half, 1), pltpu.roll(values, half, 1)
    )


def joined(refs):
    return jnp.concatenate([r[...] for r in refs], axis=0)


def qkv_body(n, x_ref, cos_ref, sin_ref, *refs):
    weights, outs = refs[: 3 * n], refs[3 * n :]
    rows = x_ref.shape[0]
    tile = outs[0].shape[1]
    for i in range(3):
        weight = joined(weights[i * n : (i + 1) * n])
        for s in range(rows // SEQ):
            span = slice(s * SEQ, (s + 1) * SEQ)
            product = nn(x_ref[span, :], weight)
            if i == 2:
                outs[i][span, :] = product.astype(BF16)
                continue
            for t in range(tile // PAIR):
                here = product[:, t * PAIR : (t + 1) * PAIR]
                turned = here * cos_ref[...] + turn(here) * sin_ref[...]
                outs[i][span, t * PAIR : (t + 1) * PAIR] = turned.astype(BF16)


def project(chain, x, tables, query, key, value):
    rows, model = x.shape
    n, width = len(query.pieces), query.width
    tile = min(256, width)
    out = pl.BlockSpec((rows, tile), lambda j: (0, j))
    return chain.call(
        functools.partial(qkv_body, n),
        (width // tile,),
        [whole(x.shape), whole((SEQ, PAIR)), whole((SEQ, PAIR))]
        + query.tiles(tile)
        + key.tiles(tile)
        + value.tiles(tile),
        [out] * 3,
        [((rows, width), BF16)] * 3,
        flops=6 * rows * model * width,
        moved=2 * (rows * model + 3 * model * width + 3 * rows * width),
    )(x, *tables, *query.pieces, *key.pieces, *value.pieces)


def collect(counts, refs, held, sems):
    rows = held.shape[0] // len(counts)
    copies = []
    for k, count in enumerate(counts):
        half = held.shape[1] // count
        for h in range(count):
            target = held.at[pl.ds(k * rows, rows), pl.ds(h * half, half)]
            i = len(copies)
            copies.append(pltpu.make_async_copy(refs[i], target, sems.at[i]))
    for copy in copies:
        copy.start()
    for copy in copies:
        copy.wait()


def gate_body(counts, *refs):
    m = sum(counts)
    gate_ref, up_ref, hidden_ref, slope_ref, silu_ref, x_ref, sems = refs[m:]

    @pl.when(pl.program_id(0) == 0)
    def _():
        collect(counts, refs, x_ref, sems)

    for s in range(x_ref.shape[0] // SEQ):
        span = slice(s * SEQ, (s + 1) * SEQ)
        gate = nn(x_ref[span, :], gate_ref[...])
        up = nn(x_ref[span, :], up_ref[...])
        sigm = jax.nn.sigmoid(gate)
        silu = gate * sigm
        hidden_ref[span, :] = (silu * up).astype(BF16)
        silu_ref[span, :] = silu.astype(BF16)
        slope_ref[span, :] = (up * sigm * (1.0 + gate * (1.0 - sigm))).astype(BF16)


def collected(held):
    counts = [len(block) for block in held]
    rows, model = held[0][0].shape
    scratch = [
        pltpu.VMEM((len(held) * rows, model), BF16),
        pltpu.SemaphoreType.DMA((sum(counts),)),
    ]
    arrays = [array for block in held for array in block]
    return counts, arrays, [pl.BlockSpec(memory_space=pl.ANY)] * len(arrays), scratch


def gate_up(chain, held, gate, up):
    counts, arrays, specs, scratch = collected(held)
    rows, model = scratch[0].shape
    width = gate.shape[1]
    tile = min(256, width)
    out = pl.BlockSpec((rows, tile), lambda j: (0, j))
    return chain.call(
        functools.partial(gate_body, counts),
        (width // tile,),
        specs + [pl.BlockSpec((model, tile), lambda j: (0, j))] * 2,
        [out] * 3,
        [((rows, width), BF16)] * 3,
        flops=4 * rows * model * width,
        scratch=scratch,
        moved=2 * (rows * model + 2 * model * width + 3 * rows * width),
    )(*arrays, gate, up)


def hidden_back_body(n, g_ref, *refs):
    weight = joined(refs[:n])
    slope_ref, silu_ref, gate_ref, up_ref = refs[n:]
    for s in range(g_ref.shape[0] // SEQ):
        span = slice(s * SEQ, (s + 1) * SEQ)
        grad = nn(g_ref[span, :], weight)
        gate_ref[span, :] = (grad * slope_ref[span, :].astype(F32)).astype(BF16)
        up_ref[span, :] = (grad * silu_ref[span, :].astype(F32)).astype(BF16)


def hidden_back(chain, grads, down, slope, silu):
    rows, model = grads.shape
    n, width = len(down.pieces), down.width
    tile = min(256, width)
    out = pl.BlockSpec((rows, tile), lambda j: (0, j))
    return chain.call(
        functools.partial(hidden_back_body, n),
        (width // tile,),
        [whole(grads.shape)] + down.tiles(tile) + [out] * 2,
        [out] * 2,
        [((rows, width), BF16)] * 2,
        flops=2 * rows * model * width,
        moved=2 * (rows * model + model * width + 4 * rows * width),
    )(grads, *down.pieces, slope, silu)


def mixed_back_body(n, counts, *refs):
    m = sum(counts)
    out_ref, x_ref, sems = refs[m + n :]

    @pl.when(pl.program_id(0) == 0)
    def _():
        collect(counts, refs, x_ref, sems)

    out_ref[...] = nn(x_ref[...], joined(refs[m : m + n])).astype(BF16)


def mixed_back(chain, held, out):
    counts, arrays, specs, scratch = collected(held)
    rows, model = scratch[0].shape
    n, width = len(out.pieces), out.width
    tile = min(256, width)
    return chain.call(
        functools.partial(mixed_back_body, n, counts),
        (width // tile,),
        specs + out.tiles(tile),
        [pl.BlockSpec((rows, tile), lambda j: (0, j))],
        [((rows, width), BF16)],
        flops=2 * rows * model * width,
        scratch=scratch,
        moved=2 * (rows * model + model * width + rows * width),
    )(*arrays, *out.pieces)[0]


def trans_body(n, starts, count, targets, *refs):
    parts, blocks = len(starts), len(targets[0])
    lefts = refs[:parts]
    pieces, outs = refs[parts : parts + count], refs[parts + count : -4]
    held, ready, sems, out_sems = refs[-4:]
    j = pl.program_id(0)
    depth, width = held.shape[2:]
    rows = ready.shape[1] // blocks

    def copy(i, p, slot):
        source = pieces[p * n + i].at[pl.ds(0, depth), pl.ds(starts[p], width)]
        return pltpu.make_async_copy(source, held.at[slot, p], sems.at[slot, p])

    def whole_copy(step, p, slot):
        first = pl.multiple_of(step * depth, depth)
        source = pieces[p].at[pl.ds(first, depth), pl.ds(starts[p], width)]
        return pltpu.make_async_copy(source, held.at[slot, p], sems.at[slot, p])

    def fetch(step, slot):
        if count == parts:
            for p in range(parts):
                whole_copy(step, p, slot).start()
            return
        for i in range(n):

            @pl.when(step == i)
            def _():
                for p in range(parts):
                    copy(i, p, slot).start()

    def leave(slot, k, array, first, column):
        target = outs[array].at[pl.ds(first, rows), pl.ds(column, depth)]
        source = ready.at[slot, pl.ds(k * rows, rows), :]
        return pltpu.make_async_copy(source, target, out_sems.at[slot, k])

    def left(slot):
        for k in range(blocks):
            leave(slot, k, 0, 0, 0).wait()

    @pl.when(j == 0)
    def _():
        fetch(j, 0)

    @pl.when(j + 1 < n)
    def _():
        fetch(j + 1, (j + 1) % 2)

    slot = j % 2
    for p in range(parts):
        (whole_copy if count == parts else copy)(0, p, slot).wait()

    @pl.when(j >= 2)
    def _():
        left(slot)

    for s in range(blocks * rows // SEQ):
        span = slice(s * SEQ, (s + 1) * SEQ)
        total = nt(lefts[0][span, :], held[slot, 0])
        for p in range(1, parts):
            total += nt(lefts[p][span, :], held[slot, p])
        ready[slot, span, :] = total.astype(BF16)
    column = pl.multiple_of(j % (n // 2) * depth, 128)
    for h in range(2):

        @pl.when((j >= n // 2) == (h == 1))
        def _():
            for k, (array, first) in enumerate(targets[h]):
                leave(slot, k, array, first, column).start()

    @pl.when(j == n - 1)
    def _():
        left(1 - slot)
        left(slot)


def times_trans(chain, parts, group):
    weights = [weight for _, weight in parts]
    depth, width = weights[0].rows, weights[0].width
    n = weights[0].model // depth
    pieces = [piece for weight in weights for piece in weight.pieces]
    rows = parts[0][0].shape[0]
    half = weights[0].model // 2
    size = rows // group.size
    messages = group.messages()
    shapes = [((size, half), BF16)] * 2
    targets = [{0: (0, 0)}, {0: (1, 0)}]
    for h in range(2):
        for keys in messages[h]:
            for i, k in enumerate(keys):
                targets[h][k] = (len(shapes), i * size)
            shapes.append(((len(keys) * size, half), BF16))
    targets = [[t[k] for k in range(group.size)] for t in targets]
    anywhere = pl.BlockSpec(memory_space=pl.ANY)
    outs = chain.call(
        functools.partial(
            trans_body, n, [weight.start for weight in weights], len(pieces), targets
        ),
        (n,),
        [whole((rows, width))] * len(parts) + [anywhere] * len(pieces),
        [anywhere] * len(shapes),
        shapes,
        flops=4 * rows * half * width * len(parts),
        scratch=[
            pltpu.VMEM((2, len(parts), depth, width), BF16),
            pltpu.VMEM((2, rows, depth), BF16),
            pltpu.SemaphoreType.DMA((2, len(parts))),
            pltpu.SemaphoreType.DMA((2, group.size)),
        ],
        moved=2 * (2 * rows * half + len(parts) * (rows + 2 * half) * width),
    )(*[left for left, _ in parts], *pieces)
    m = group.bits
    return outs[:2], [outs[2 : 2 + m], outs[2 + m :]]


def grad_body(parts, got, blocks, steps, *refs):
    lefts, refs = refs[:blocks], refs[blocks:]
    rights, refs = refs[:parts], refs[parts:]
    got_ref = refs[0] if got else None
    outs, turned = refs[got:-1], refs[-1]
    j = pl.program_id(0)

    @pl.when(j == 0)
    def _():
        rows = turned.shape[1] // blocks
        for k in range(blocks):
            turned[:, cut(rows, k)] = lefts[k][...].T

    for i in range(parts):

        @pl.when((j >= i * steps) & (j < (i + 1) * steps))
        def _():
            total = nn(turned[...], rights[i][...])
            if got:
                total += got_ref[...].astype(F32)
            total = total.astype(BF16)
            first = 0
            for out_ref in outs:
                count = out_ref.shape[0]
                out_ref[...] = total[first : first + count]
                first += count


def weight_grads(chain, left, which, rights, got=None, bits=0):
    rows, width = rights[0].shape
    parts = len(rights)
    tile = min(512, width)
    steps = width // tile
    if isinstance(left, list):
        lefts = [block[0] if len(block) == 1 else block[which] for block in left]
        half = left[0][0].shape[1] // 2
        places = [which if len(block) == 1 else 0 for block in left]
    else:
        lefts, places, half = [left], [which], left.shape[1] // 2
    blocks = len(lefts)
    ins = [
        pl.BlockSpec((rows // blocks, half), functools.partial(lambda at, j: (0, at), at))
        for at in places
    ]
    for i in range(parts):
        ins.append(
            pl.BlockSpec(
                (rows, tile),
                functools.partial(
                    lambda first, j: (0, jnp.clip(j - first, 0, steps - 1)), i * steps
                ),
            )
        )
    column = lambda j: (0, j)
    more = [] if got is None else [got]
    sizes = [half >> bits]
    for p in range(bits):
        sizes += [sizes[0], ((1 << p) - 1) * sizes[0]] if p else [sizes[0]]
    return chain.call(
        functools.partial(grad_body, parts, len(more), blocks, steps),
        (parts * steps,),
        ins + [pl.BlockSpec((half, tile), column)] * len(more),
        [pl.BlockSpec((size, tile), column) for size in sizes],
        [((size, parts * width), BF16) for size in sizes],
        flops=2 * rows * half * width * parts,
        scratch=[pltpu.VMEM((half, rows), BF16)],
        moved=2 * (rows * half + parts * (rows + half) * width),
    )(*lefts, *rights, *more)


def full_grad_body(parts, tiles, line_ref, *refs):
    lefts = []
    for counts, _, _ in parts:
        lefts.append(refs[: sum(counts)])
        refs = refs[sum(counts) :]
    rights, (out_ref, turned, held, sems) = refs[:-4], refs[-4:]
    j = pl.program_id(0)
    depth = out_ref.shape[0] // line_ref.shape[0]
    n = 0
    for (counts, first, count), left in zip(parts, lefts):

        @pl.when(j == first)
        def _():
            collect(counts, left, held, sems)
            rows = held.shape[0] // len(counts)
            for k in range(len(counts)):
                turned[:, cut(rows, k)] = held[cut(rows, k), :].T

        for i in range(count):

            @pl.when((j >= first + i * tiles) & (j < first + (i + 1) * tiles))
            def _():
                half = out_ref.shape[0] // 2
                for h in range(2):
                    total = nn(turned[h * half : (h + 1) * half, :], rights[n + i][...])
                    total = total.astype(BF16)
                    for b in range(half // depth):
                        place_of = pl.multiple_of(line_ref[h * half // depth + b] * depth, 128)
                        out_ref[pl.ds(place_of, depth), :] = total[cut(depth, b)]

        n += count


def full_grad(chain, line, parts):
    arrays, specs, where, rights = [], [], [], []
    width = parts[0][1][0].shape[1]
    tile = min(512, width)
    tiles = width // tile
    most = 0
    for left, more in parts:
        left = left if isinstance(left, list) else [[left]]
        counts, blocks, anywhere, scratch = collected(left)
        where.append((counts, len(rights) * tiles, len(more)))
        arrays += blocks
        specs += anywhere
        rights += more
        most = max(most, len(blocks))
    rows, model = scratch[0].shape
    for i in range(len(rights)):
        index = lambda first, j, *_: (0, jnp.clip(j - first, 0, tiles - 1))
        specs.append(pl.BlockSpec((rows, tile), functools.partial(index, i * tiles)))
    return chain.call(
        functools.partial(full_grad_body, where, tiles),
        (len(rights) * tiles,),
        specs,
        [pl.BlockSpec((model, tile), lambda j, *_: (0, j))],
        [((model, len(rights) * width), BF16)],
        flops=2 * rows * model * width * len(rights),
        scratch=[
            pltpu.VMEM((model, rows), BF16),
            pltpu.VMEM((rows, model), BF16),
            pltpu.SemaphoreType.DMA((most,)),
        ],
        prefetch=1,
        moved=2 * (rows * model + (rows + model) * width * len(rights)),
    )(line, *arrays, *rights)[0]


def causal(scores):
    past = scores.shape[0] - HALF_SEQ
    key = lax.broadcasted_iota(jnp.int32, (HALF_SEQ, HALF_SEQ), 0)
    query = lax.broadcasted_iota(jnp.int32, (HALF_SEQ, HALF_SEQ), 1)
    last = jnp.where(key <= query, scores[past:], -1e30)
    return last if past == 0 else jnp.concatenate([scores[:past], last], axis=0)


def head_of(h):
    return slice(h * HEAD_DIM, (h + 1) * HEAD_DIM)


def span_of(b):
    return slice(b * HALF_SEQ, (b + 1) * HALF_SEQ)


def in_place(shift_ref, ref, count):
    rows = SEQ // count
    spans = [pl.ds(pl.multiple_of((i ^ shift_ref[0]) * rows, rows), rows) for i in range(count)]
    return jnp.concatenate([ref[span, :] for span in spans], axis=0)


def put_back(shift_ref, ref, count, values):
    rows = SEQ // count
    for i in range(count):
        ref[pl.ds(pl.multiple_of((i ^ shift_ref[0]) * rows, rows), rows), :] = values[cut(rows, i)]


def attend_body(count, shift_ref, q_ref, k_ref, v_ref, out_ref, sum_ref):
    queries, keys = in_place(shift_ref, q_ref, count), in_place(shift_ref, k_ref, count)
    values = in_place(shift_ref, v_ref, count).astype(F32).T.astype(BF16)
    heads = []
    for h in range(2):
        blocks = []
        for b in range(2):
            reach = (b + 1) * HALF_SEQ
            query = queries[span_of(b), head_of(h)] * BF16(FACTOR)
            scores = causal(nt(keys[:reach, head_of(h)], query))
            top = jnp.max(scores, axis=0, keepdims=True)
            expo = jnp.exp(scores - top)
            total = jnp.sum(expo, axis=0, keepdims=True)
            mixed = nn(values[head_of(h), :reach], expo.astype(BF16))
            blocks.append(mixed * (1.0 / total))
            sum_ref[0, 0, h : h + 1, span_of(b)] = top + jnp.log(total)
        heads.append(jnp.concatenate(blocks, axis=1))
    put_back(shift_ref, out_ref, count, jnp.concatenate(heads, axis=0).T.astype(BF16))


def attend(chain, shift, count, query, key, value):
    rows, width = query.shape
    seqs, pairs = rows // SEQ, width // PAIR
    tile = pl.BlockSpec((SEQ, PAIR), lambda s, p, _: (s, p))
    return chain.call(
        functools.partial(attend_body, count),
        (seqs, pairs),
        [tile] * 3,
        [tile, pl.BlockSpec((1, 1, 2, SEQ), lambda s, p, _: (s, p, 0, 0))],
        [((rows, width), BF16), ((seqs, pairs, 2, SEQ), F32)],
        flops=16 * rows * width * SEQ,
        prefetch=1,
        moved=8 * rows * width,
    )(shift, query, key, value)


def attend_back_body(
    count, shift_ref, q_ref, k_ref, v_ref, g_ref, sum_ref, cos_ref, sin_ref, dq_ref, dk_ref, dv_ref
):
    queries, keys, values, grads = (
        in_place(shift_ref, ref, count) for ref in (q_ref, k_ref, v_ref, g_ref)
    )
    turned = keys.astype(F32).T.astype(BF16)
    dq_heads, dk_heads, dv_heads = [], [], []
    for h in range(2):
        dq, dk, dv = [], [], []
        for b in range(2):
            reach = (b + 1) * HALF_SEQ
            query = queries[span_of(b), head_of(h)]
            grad = grads[span_of(b), head_of(h)]
            scores = causal(nt(keys[:reach, head_of(h)], query * BF16(FACTOR)))
            probs = jnp.exp(scores - sum_ref[0, 0, h : h + 1, span_of(b)])
            probs_grad = nt(values[:reach, head_of(h)], grad)
            inner = jnp.sum(probs * probs_grad, axis=0, keepdims=True)
            score_grad = (probs * (probs_grad - inner)).astype(BF16)
            dv.append(nn(probs.astype(BF16), grad))
            dk.append(nn(score_grad, query))
            dq.append(nn(turned[head_of(h), :reach], score_grad))
        for parts, heads in ((dk, dk_heads), (dv, dv_heads)):
            heads.append(
                jnp.concatenate([parts[1][:HALF_SEQ] + parts[0], parts[1][HALF_SEQ:]], axis=0)
            )
        dq_heads.append(jnp.concatenate(dq, axis=1))
    dq = jnp.concatenate(dq_heads, axis=0).T * FACTOR
    dk = jnp.concatenate(dk_heads, axis=1) * FACTOR
    dv = jnp.concatenate(dv_heads, axis=1).astype(BF16)
    cosine, sine = cos_ref[...], sin_ref[...]
    put_back(shift_ref, dq_ref, count, (dq * cosine - turn(dq) * sine).astype(BF16))
    put_back(shift_ref, dk_ref, count, (dk * cosine - turn(dk) * sine).astype(BF16))
    put_back(shift_ref, dv_ref, count, dv)


def attend_back(chain, shift, count, query, key, value, grad, logsum, tables):
    rows, width = query.shape
    seqs, pairs = rows // SEQ, width // PAIR
    tile = pl.BlockSpec((SEQ, PAIR), lambda s, p, _: (s, p))
    return chain.call(
        functools.partial(attend_back_body, count),
        (seqs, pairs),
        [tile] * 4
        + [pl.BlockSpec((1, 1, 2, SEQ), lambda s, p, _: (s, p, 0, 0))]
        + [whole((SEQ, PAIR))] * 2,
        [tile] * 3,
        [((rows, width), BF16)] * 3,
        flops=40 * rows * width * SEQ,
        prefetch=1,
        moved=14 * rows * width,
    )(shift, query, key, value, grad, logsum, *tables)


def local(
    chips,
    group,
    tokens,
    attn_gain,
    query_weight,
    key_weight,
    value_weight,
    output_weight,
    ffn_gain,
    gate_weight,
    up_weight,
    down_weight,
    cotangent,
):
    line = jnp.asarray(chips.table)[lax.axis_index("dp")]
    rows, model = tokens.shape
    count = SEQ // rows
    shift = lax.axis_index("tensor") % count
    row = jnp.arange(SEQ, dtype=jnp.int32)
    places = rope_tables(row)
    tables = rope_tables((row // rows ^ shift) * rows + row % rows)
    shift = jnp.reshape(shift, (1,)).astype(jnp.int32)
    depth, own = query_weight.shape
    hidden_units = gate_weight.shape[1]
    chain = Chain()

    def gather(piece):
        return Gather(chips, chain, chain.join(piece)[0])

    def spread_of(values):
        return Spread(group, chain, chain.join(values)[0])

    def fold_of(part):
        own_part, sent = part
        sent = chain.join(*sent[0], *sent[1])
        return Fold(group, chain, own_part, [sent[: group.bits], sent[group.bits :]])

    def grads_of(left, rights):
        got = [None]
        chain.ask(weight_grads(chain, left, 1, rights)[0], got, 0, chips.other)

        def mine():
            if got[0] is None:
                chain.flush()
            return Sums(chips, chain, weight_grads(chain, left, 0, rights, got[0], chips.bits))

        return mine

    def gather_whole(weight):
        return lax.all_gather(chain.join(weight)[0], "dp", axis=0, tiled=True)

    def sum_whole(grad):
        return lax.psum_scatter(grad, "dp", scatter_dimension=0, tiled=True).astype(F32)

    straight = jnp.arange(chips.size, dtype=jnp.int32)
    extra = jnp.concatenate([attn_gain, ffn_gain, jnp.zeros((4 * own - 2 * depth,), BF16)])
    attn = jnp.concatenate([query_weight, key_weight, value_weight, output_weight.T], axis=1)
    attn = gather(jnp.concatenate([attn, jnp.broadcast_to(extra, (16, 4 * own))], axis=0))
    spread = spread_of(tokens)
    chain.end(attn, spread)
    chain.end(attn, spread)
    all_tokens = spread.blocks()
    attn = attn.pieces()
    all_gate = gather_whole(gate_weight)
    spread = spread_of(cotangent)
    w_query, w_key, w_value, w_output = [Weight(attn, depth, i * own, own) for i in range(4)]
    gains = jnp.concatenate(
        [piece[depth : depth + 1, : 2 * depth].reshape(2, depth) for piece in attn], axis=1
    ).astype(F32)

    group_one = ordered(chain, norm_body, line, gains, all_tokens)
    all_up = gather_whole(up_weight)
    down = gather(down_weight.T)
    query, key, value = project(chain, group_one, tables, w_query, w_key, w_value)
    mixed, logsum = attend(chain, shift, count, query, key, value)
    chain.end(spread)
    out_part = times_trans(chain, [(mixed, w_output)], group)
    all_grads = spread.blocks()
    fold = fold_of(out_part)
    grad_rows = ordered(chain, order_body, line, gains, all_grads)
    chain.end(fold)
    attended = fold.total()
    middle, second = by_rows(
        chain, middle_body, line, tokens, gains, attended, [], [F32, BF16]
    )
    spread = spread_of(second)
    chain.end(spread)
    group_two = spread.blocks()
    second_rows = ordered(chain, order_body, line, gains, group_two)
    w_gate = Weight([all_gate], depth, 0, hidden_units)
    w_up = Weight([all_up], depth, 0, hidden_units)
    hidden, slope, silu = gate_up(chain, group_two, all_gate, all_up)

    chain.end(down)
    down_sum = sum_whole(full_grad(chain, straight, [(all_grads, [hidden])]))
    w_down = Weight(down.pieces(), depth, 0, hidden_units)
    gate_grad, up_grad = hidden_back(chain, grad_rows, w_down, slope, silu)
    second_part = times_trans(chain, [(gate_grad, w_gate), (up_grad, w_up)], group)
    fold = fold_of(second_part)
    up_sum = sum_whole(full_grad(chain, straight, [(group_two, [up_grad])]))
    mine = grads_of(second_rows, [gate_grad])
    chain.end(fold)
    gate_sum = mine()
    second_grad = fold.total()
    middle_grad, low_grad = by_rows(
        chain, second_back_body, line, cotangent, gains, second_grad, [middle], [F32, BF16]
    )
    spread = spread_of(low_grad)
    result_part = times_trans(chain, [(hidden, w_down)], group)
    chain.end(spread)
    attn_grads = spread.blocks()

    mixed_grad = mixed_back(chain, attn_grads, w_output)
    fold = fold_of(result_part)
    query_back, key_back, value_back = attend_back(
        chain, shift, count, query, key, value, mixed_grad, logsum, places
    )
    chain.end(fold)
    attn_sum = sum_whole(
        full_grad(
            chain,
            line,
            [(group_one, [query_back, key_back, value_back]), (attn_grads, [mixed])],
        )
    )
    result_part = fold.total()
    first_part = times_trans(
        chain, [(query_back, w_query), (key_back, w_key), (value_back, w_value)], group
    )
    chain.end(gate_sum)
    fold = fold_of(first_part)
    (layer_out,) = by_rows(chain, result_body, line, middle, gains, result_part, [], [BF16])
    chain.end(fold)
    first_grad = fold.total()
    (input_grad,) = by_rows(
        chain, first_back_body, line, tokens, gains, first_grad, [middle_grad], [F32]
    )
    query_sum, key_sum, value_sum, out_sum = [attn_sum[:, cut(own, i)] for i in range(4)]
    gate_sum = gate_sum.total()

    def inner(weight, grad):
        return jnp.sum(weight.astype(F32) * grad, axis=1)

    gain_one_part = (
        inner(query_weight, query_sum) + inner(key_weight, key_sum) + inner(value_weight, value_sum)
    ) / attn_gain.astype(F32)
    gain_two_part = (inner(gate_weight, gate_sum) + inner(up_weight, up_sum)) / ffn_gain.astype(F32)
    gain_one_total, gain_two_total = lax.psum((gain_one_part, gain_two_part), "tensor")
    return (
        layer_out,
        input_grad,
        gain_one_total,
        query_sum,
        key_sum,
        value_sum,
        out_sum.T,
        gain_two_total,
        gate_sum,
        up_sum,
        down_sum.T,
    )


def solution(mesh):
    in_specs = (
        P(("dp", "tensor"), None),
        P("dp"),
        P("dp", "tensor"),
        P("dp", "tensor"),
        P("dp", "tensor"),
        P("tensor", "dp"),
        P("dp"),
        P("dp", "tensor"),
        P("dp", "tensor"),
        P("tensor", "dp"),
        P(("dp", "tensor"), None),
    )
    out_specs = (
        P(("dp", "tensor"), None),
        P(("dp", "tensor"), None),
        P("dp"),
        P("dp", "tensor"),
        P("dp", "tensor"),
        P("dp", "tensor"),
        P("tensor", "dp"),
        P("dp"),
        P("dp", "tensor"),
        P("dp", "tensor"),
        P("tensor", "dp"),
    )
    chips = Chips(mesh.shape["dp"])
    size = mesh.shape["tensor"]
    links = [[(i, i ^ 1 << b) for i in range(size)] for b in range(size.bit_length() - 1)]
    group = Group(links, "tensor")

    def run(*arrays):
        return local(chips, group, *arrays)

    return jax.shard_map(run, mesh=mesh, in_specs=in_specs, out_specs=out_specs, check_vma=False)
```

```python
import functools

import jax
import jax.numpy as jnp
import numpy as np
from jax import lax
from jax.experimental import pallas as pl
from jax.experimental.pallas import tpu as pltpu
from jax.sharding import PartitionSpec as P

HEAD_DIM = 64
SEQ = 512
EPS = 1e-05
THETA = 130000.0
BF16 = jnp.bfloat16
F32 = jnp.float32
FACTOR = HEAD_DIM**-0.5
PAIR = 2 * HEAD_DIM
HALF_SEQ = SEQ // 2
VMEM_LIMIT = 58 << 20
COST_SHARE = 4096


class Chain:
    def __init__(self):
        self.token = jnp.zeros((8, 128), F32)
        self.swaps, self.asked = [], []

    def join(self, *values):
        *values, self.token = lax.optimization_barrier((*values, self.token))
        return values

    def gate(self, *values):
        swaps, self.swaps = self.swaps, []
        asked, self.asked = self.asked, []
        joined = self.join(
            *values, *[held[i] for held, i in swaps], *[source for source, _, _, _ in asked]
        )
        for (held, i), value in zip(swaps, joined[len(values) :]):
            held[i] = value
        for (_, held, i, swap), value in zip(asked, joined[len(values) + len(swaps) :]):
            held[i] = swap(value)
            self.swaps.append((held, i))
        return joined[: len(values)]

    def end(self, *transfers):
        counts = [len(t.flying) for t in transfers]
        got = self.gate(*[value for t in transfers for value in t.flying])
        for t, count in zip(transfers, counts):
            t.go_on(got[:count])
            got = got[count:]

    def ask(self, source, held, i, swap):
        self.asked.append((source, held, i, swap))

    def flush(self):
        for source, held, i, swap in self.asked:
            held[i] = swap(source)
        self.asked = []

    def call(self, body, grid, ins, outs, shapes, flops, scratch=(), prefetch=0, moved=0):
        first = prefetch + len(ins)
        second = first + 1 + len(outs)
        anywhere = pl.BlockSpec(memory_space=pl.ANY)

        def wrapped(*refs):
            body(*refs[:first], *refs[first + 1 : second], *refs[second + 1 :])

        run = pl.pallas_call(
            wrapped,
            grid_spec=pltpu.PrefetchScalarGridSpec(
                num_scalar_prefetch=prefetch,
                grid=grid,
                in_specs=[*ins, anywhere],
                out_specs=[*outs, anywhere],
                scratch_shapes=list(scratch),
            ),
            out_shape=[jax.ShapeDtypeStruct(s, t) for s, t in [*shapes, ((8, 128), F32)]],
            compiler_params=pltpu.CompilerParams(
                vmem_limit_bytes=VMEM_LIMIT, dimension_semantics=("arbitrary",) * len(grid)
            ),
            cost_estimate=pl.CostEstimate(
                flops=flops // COST_SHARE, bytes_accessed=moved // COST_SHARE, transcendentals=0
            ),
        )

        def with_token(*args):
            *results, self.token = run(*args, self.token)
            return results

        return with_token


class Chips:
    def __init__(self, size):
        self.bits = (size // 2).bit_length() - 1
        self.size = size
        self.swap = [(i, i ^ 1) for i in range(size)]
        self.links = [
            [(i, i ^ 2 << self.bits - 1 - p) for i in range(size)] for p in range(self.bits)
        ]
        flips = [
            sum(1 << self.bits - 1 - p for p in range(self.bits) if v >> p & 1)
            for v in range(1 << self.bits)
        ]
        table = [[i ^ 2 * f for f in flips] + [i ^ 2 * f ^ 1 for f in flips] for i in range(size)]
        self.table = np.array(table, np.int32)

    def send(self, value, p):
        return lax.ppermute(value, "dp", self.links[p])

    def other(self, value):
        return lax.ppermute(value, "dp", self.swap)


class Gather:
    def __init__(self, chips, chain, piece):
        self.chips, self.chain = chips, chain
        self.own = [piece] + [None] * (2**chips.bits - 1)
        self.others = list(self.own)
        self.ask(0)
        self.keys = [1 << p for p in range(chips.bits)]
        self.flying = [chips.send(piece, p) for p in range(chips.bits)]

    def ask(self, v):
        self.chain.ask(self.own[v], self.others, v, self.chips.other)

    def go_on(self, got):
        keys, self.keys, self.flying = self.keys, [], []
        for v, piece in zip(keys, got):
            self.own[v] = piece
            for p in range(v.bit_length(), self.chips.bits):
                self.keys.append(v | 1 << p)
                self.flying.append(self.chips.send(piece, p))
        for v in keys:
            self.ask(v)

    def pieces(self):
        while self.flying:
            self.chain.end(self)
        self.chain.flush()
        return self.own + self.others


class Sums:
    def __init__(self, chips, chain, mine, apart=False):
        self.chips, self.chain, self.apart = chips, chain, apart
        self.parts = [mine[0]]
        mine = list(mine[1:])
        self.direct, self.passed = [], []
        for p in range(chips.bits):
            self.direct.append(mine.pop(0))
            self.passed.append(mine.pop(0) if p else None)
        self.p = chips.bits - 1
        self.kinds = [self.p]
        self.flying = [chips.send(self.passed[self.p], self.p)]

    def go_on(self, got):
        rows = self.parts[0].shape[0]
        kinds, self.kinds, self.flying = self.kinds, [], []
        for kind, block in zip(kinds, got):
            if kind is None:
                self.parts.append(block)
                continue
            add = lambda held, first: (
                held.astype(F32) + block[first * rows : first * rows + held.shape[0]].astype(F32)
            ).astype(BF16)
            for q in range(kind):
                self.direct[q] = add(self.direct[q], (1 << q) - 1)
                if q:
                    self.passed[q] = add(self.passed[q], 1 << q)
        p, self.p = self.p, self.p - 1
        if p > 0:
            self.send(None, self.direct[p], p)
        if p > 1:
            self.send(p - 1, self.passed[p - 1], p - 1)
        if p == (0 if self.apart else 1):
            self.send(None, self.direct[0], 0)

    def send(self, kind, value, p):
        (value,) = self.chain.join(value)
        self.kinds.append(kind)
        self.flying.append(self.chips.send(value, p))

    def total(self):
        while self.flying:
            self.chain.end(self)
        total = self.parts[0].astype(F32)
        for part in self.parts[1:]:
            total = total + part.astype(F32)
        return total


class Group:
    def __init__(self, links, axes):
        self.links, self.axes = links, axes
        self.bits = len(links)
        self.size = 1 << self.bits
        self.orders = (list(range(self.bits)), list(range(self.bits))[::-1])

    def send(self, value, bit):
        return lax.ppermute(value, self.axes, self.links[bit])

    def messages(self):
        found = []
        for order in self.orders:
            found.append([])
            for top in reversed(range(self.bits)):
                found[-1].append(
                    [
                        1 << order[top] | sum(1 << order[p] for p in range(top) if v >> p & 1)
                        for v in range(1 << top)
                    ]
                )
        return found


class Spread:
    def __init__(self, group, chain, rows):
        self.group, self.chain = group, chain
        self.held = {0: [rows]}
        self.later = None
        self.keys = [(1 << b, None) for b in range(group.bits)]
        self.flying = [group.send(rows, b) for b in range(group.bits)]

    def go_on(self, got):
        fresh = list(zip(self.keys, got))
        self.keys, self.flying = [], []
        for (k, h), block in fresh:
            if h is None:
                self.held[k] = [block]
            else:
                self.held.setdefault(k, [None, None])[h] = block
        for (k, h), block in fresh:
            for way, order in enumerate(self.group.orders):
                if h is not None and h != way:
                    continue
                half = block.shape[1] // 2
                top = max(i for i, bit in enumerate(order) if k >> bit & 1)
                for i in range(top + 1, len(order)):
                    part = block if h is not None else block[:, way * half : (way + 1) * half]
                    self.keys.append((k | 1 << order[i], way))
                    if self.later is not None:
                        self.later.append((part, order[i]))
                    else:
                        self.flying.append(self.group.send(part, order[i]))

    def resume(self):
        later, self.later = self.later, None
        parts = self.chain.join(*[part for part, _ in later])
        self.flying = [self.group.send(part, bit) for part, (_, bit) in zip(parts, later)]

    def blocks(self):
        while self.flying:
            self.chain.end(self)
        return [self.held[k] for k in range(self.group.size)]


class Fold:
    def __init__(self, group, chain, own, sent):
        self.group, self.chain = group, chain
        self.rows = own[0].shape[0]
        self.sent = [list(half) for half in sent]
        self.parts = [[half] for half in own]
        self.wave = 0
        self.start()

    def start(self):
        self.flying = [
            self.group.send(self.sent[h][self.wave], order[self.group.bits - 1 - self.wave])
            for h, order in enumerate(self.group.orders)
        ]

    def go_on(self, got):
        self.wave += 1
        self.flying = []
        for h, block in enumerate(got):
            self.parts[h].append(block)
            for wave in range(self.wave, self.group.bits):
                first = self.rows << (self.group.bits - 1 - wave)
                more = block[first : 2 * first].astype(F32)
                self.sent[h][wave] = (self.sent[h][wave].astype(F32) + more).astype(BF16)
        if self.wave < self.group.bits:
            now = self.chain.join(*[sent[self.wave] for sent in self.sent])
            for sent, value in zip(self.sent, now):
                sent[self.wave] = value
            self.start()

    def total(self):
        while self.flying:
            self.chain.end(self)
        return self.parts


class Weight:
    def __init__(self, pieces, rows, start, width):
        self.pieces, self.rows, self.start, self.width = pieces, rows, start, width
        self.model = len(pieces) * rows

    def tiles(self, tile):
        first = self.start // tile
        return [pl.BlockSpec((self.rows, tile), lambda j: (0, first + j))] * len(self.pieces)


def nn(left, right):
    return lax.dot_general(left, right, (((1,), (0,)), ((), ())), preferred_element_type=F32)


def nt(left, right):
    return lax.dot_general(left, right, (((1,), (1,)), ((), ())), preferred_element_type=F32)


def tn(left, right):
    return lax.dot_general(left, right, (((0,), (0,)), ((), ())), preferred_element_type=F32)


def whole(shape):
    return pl.BlockSpec(shape, lambda *_: (0,) * len(shape))


def place(line_ref, j, width):
    return pl.ds(pl.multiple_of(line_ref[j] * width, 128), width)


def cut(width, j):
    return slice(j * width, (j + 1) * width)


def scale_of(values):
    return lax.rsqrt(jnp.mean(values * values, axis=-1, keepdims=True) + EPS)


def fetch_blocks(counts, refs, held, sems, k, slot, wait):
    first = 0
    for i, count in enumerate(counts):
        copies = []
        half = held.shape[2] // count
        for h in range(count):
            target = held.at[slot, :, pl.ds(h * half, half)]
            copies.append(pltpu.make_async_copy(refs[first + h], target, sems.at[slot, h]))
        first += count

        @pl.when(k == i)
        def _():
            for copy in copies:
                copy.wait() if wait else copy.start()


def fetched(counts, refs, held, sems):
    k = pl.program_id(0)

    @pl.when(k == 0)
    def _():
        fetch_blocks(counts, refs, held, sems, k, 0, False)

    fetch_blocks(counts, refs, held, sems, k + 1, (k + 1) % 2, False)
    fetch_blocks(counts, refs, held, sems, k, k % 2, True)
    return held.at[k % 2]


def norm_body(blocks, counts, line_ref, gain_ref, *refs):
    out_ref, held, sems = refs[sum(counts) :]
    x_ref = fetched(counts, refs, held, sems)
    width = out_ref.shape[1] // blocks
    scale = scale_of(x_ref[...].astype(F32))
    for j in range(blocks):
        part = x_ref[:, place(line_ref, j, width)].astype(F32)
        gain = gain_ref[0:1, cut(width, j)]
        out_ref[:, cut(width, j)] = (part * scale * gain).astype(BF16)


def order_body(blocks, counts, line_ref, gain_ref, *refs):
    out_ref, held, sems = refs[sum(counts) :]
    x_ref = fetched(counts, refs, held, sems)
    width = out_ref.shape[1] // blocks
    for j in range(blocks):
        out_ref[:, cut(width, j)] = x_ref[:, place(line_ref, j, width)]


def ordered(chain, body, line, gains, held):
    counts = [len(block) for block in held]
    rows, model = held[0][0].shape
    n = len(held)
    return chain.call(
        functools.partial(body, line.shape[0], counts),
        (n,),
        [whole(gains.shape)] + [pl.BlockSpec(memory_space=pl.ANY)] * sum(counts),
        [pl.BlockSpec((rows, model), lambda k, *_: (k, 0))],
        [((n * rows, model), BF16)],
        flops=20 * n * rows * model,
        scratch=[pltpu.VMEM((2, rows, model), BF16), pltpu.SemaphoreType.DMA((2, 2))],
        prefetch=1,
        moved=4 * n * rows * model,
    )(line, gains, *[array for block in held for array in block])[0]


def added(refs, span):
    total = refs[0][span, :].astype(F32)
    for ref in refs[1:]:
        total += ref[span, :].astype(F32)
    return total


def middle_body(blocks, m, line_ref, x_ref, gain_ref, *refs):
    middle_ref, out_ref = refs[2 * m :]
    width = x_ref.shape[1] // blocks
    half = x_ref.shape[1] // 2
    span = slice(None)
    middle_ref[:, :half] = added(refs[:m], span)
    middle_ref[:, half:] = added(refs[m : 2 * m], span)
    for j in range(blocks):
        here = x_ref[:, place(line_ref, j, width)].astype(F32)
        middle_ref[:, cut(width, j)] += here
    middle = middle_ref[...]
    out_ref[...] = (middle * scale_of(middle) * gain_ref[1:2, :]).astype(BF16)


def result_body(blocks, m, line_ref, middle_ref, gain_ref, *refs):
    out_ref = refs[2 * m]
    width = middle_ref.shape[1] // blocks
    span = slice(None)
    total = middle_ref[...] + jnp.concatenate(
        [added(refs[:m], span), added(refs[m : 2 * m], span)], axis=1
    )
    for j in range(blocks):
        out_ref[:, place(line_ref, j, width)] = total[:, cut(width, j)].astype(BF16)


def second_back_body(blocks, m, line_ref, dy_ref, gain_ref, *refs):
    middle_ref, out_ref, low_ref = refs[2 * m :]
    width = dy_ref.shape[1] // blocks
    span = slice(None)
    grad = jnp.concatenate([added(refs[:m], span), added(refs[m : 2 * m], span)], axis=1)
    middle = middle_ref[...]
    scale = scale_of(middle)
    normed = middle * scale
    scaled = grad * gain_ref[1:2, :]
    out_ref[...] = scale * (scaled - normed * jnp.mean(scaled * normed, axis=-1, keepdims=True))
    for j in range(blocks):
        out_ref[:, cut(width, j)] += dy_ref[:, place(line_ref, j, width)].astype(F32)
    low_ref[...] = out_ref[...].astype(BF16)


def first_back_body(blocks, m, line_ref, x_ref, gain_ref, *refs):
    above_ref, out_ref = refs[2 * m :]
    width = x_ref.shape[1] // blocks
    span = slice(None)
    scale = scale_of(x_ref[...].astype(F32))
    normed = jnp.concatenate(
        [x_ref[:, place(line_ref, j, width)].astype(F32) for j in range(blocks)], axis=1
    ) * scale
    grad = jnp.concatenate([added(refs[:m], span), added(refs[m : 2 * m], span)], axis=1)
    scaled = grad * gain_ref[0:1, :]
    back = scale * (scaled - normed * jnp.mean(scaled * normed, axis=-1, keepdims=True))
    total = above_ref[...] + back
    for j in range(blocks):
        out_ref[:, place(line_ref, j, width)] = total[:, cut(width, j)]


def by_rows(chain, body, line, first, gains, parts, more, kinds):
    rows, model = first.shape
    half = model // 2
    tile = min(128, rows)
    row = pl.BlockSpec((tile, model), lambda i, *_: (i, 0))
    slim = pl.BlockSpec((tile, half), lambda i, *_: (i, 0))
    m = len(parts[0])
    return chain.call(
        functools.partial(body, line.shape[0], m),
        (rows // tile,),
        [row, whole(gains.shape)] + [slim] * (2 * m) + [row] * len(more),
        [row] * len(kinds),
        [((rows, model), kind) for kind in kinds],
        flops=20 * rows * model,
        prefetch=1,
        moved=rows * model * (2 * m + 4 * len(kinds)),
    )(line, first, gains, *parts[0], *parts[1], *more)


def rope_tables(place):
    half = HEAD_DIM // 2
    freq = THETA ** (-2.0 * jnp.arange(half, dtype=F32) / HEAD_DIM)
    angle = place.astype(F32)[:, None] * freq[None, :]
    cosine, sine = jnp.cos(angle), jnp.sin(angle)
    return (
        jnp.concatenate([cosine] * (PAIR // half), axis=1),
        jnp.concatenate([-sine, sine] * (PAIR // HEAD_DIM), axis=1),
    )


def turn(values):
    half = HEAD_DIM // 2
    width = values.shape[-1]
    lane = lax.broadcasted_iota(jnp.int32, values.shape, 1) % HEAD_DIM
    return jnp.where(
        lane < half, pltpu.roll(values, width - half, 1), pltpu.roll(values, half, 1)
    )


def joined(refs):
    return jnp.concatenate([r[...] for r in refs], axis=0)


def qkv_body(n, x_ref, cos_ref, sin_ref, *refs):
    weights, outs = refs[: 3 * n], refs[3 * n :]
    rows = x_ref.shape[0]
    tile = outs[0].shape[1]
    for i in range(3):
        weight = joined(weights[i * n : (i + 1) * n])
        for s in range(rows // SEQ):
            span = slice(s * SEQ, (s + 1) * SEQ)
            product = nn(x_ref[span, :], weight)
            if i == 2:
                outs[i][span, :] = product.astype(BF16)
                continue
            for t in range(tile // PAIR):
                here = product[:, t * PAIR : (t + 1) * PAIR]
                turned = here * cos_ref[...] + turn(here) * sin_ref[...]
                outs[i][span, t * PAIR : (t + 1) * PAIR] = turned.astype(BF16)


def project(chain, x, tables, query, key, value):
    rows, model = x.shape
    n, width = len(query.pieces), query.width
    tile = min(256, width)
    out = pl.BlockSpec((rows, tile), lambda j: (0, j))
    return chain.call(
        functools.partial(qkv_body, n),
        (width // tile,),
        [whole(x.shape), whole((SEQ, PAIR)), whole((SEQ, PAIR))]
        + query.tiles(tile)
        + key.tiles(tile)
        + value.tiles(tile),
        [out] * 3,
        [((rows, width), BF16)] * 3,
        flops=6 * rows * model * width,
        moved=2 * (rows * model + 3 * model * width + 3 * rows * width),
    )(x, *tables, *query.pieces, *key.pieces, *value.pieces)


def collect(counts, refs, held, sems):
    rows = held.shape[0] // len(counts)
    copies = []
    for k, count in enumerate(counts):
        half = held.shape[1] // count
        for h in range(count):
            target = held.at[pl.ds(k * rows, rows), pl.ds(h * half, half)]
            i = len(copies)
            copies.append(pltpu.make_async_copy(refs[i], target, sems.at[i]))
    for copy in copies:
        copy.start()
    for copy in copies:
        copy.wait()


def gate_body(n, counts, *refs):
    m = sum(counts)
    gate_w, up_w = refs[m : m + n], refs[m + n : m + 2 * n]
    hidden_ref, slope_ref, silu_ref, x_ref, sems = refs[m + 2 * n :]

    @pl.when(pl.program_id(0) == 0)
    def _():
        collect(counts, refs, x_ref, sems)

    gate_weight, up_weight = joined(gate_w), joined(up_w)
    for s in range(x_ref.shape[0] // SEQ):
        span = slice(s * SEQ, (s + 1) * SEQ)
        gate = nn(x_ref[span, :], gate_weight)
        up = nn(x_ref[span, :], up_weight)
        sigm = jax.nn.sigmoid(gate)
        silu = gate * sigm
        hidden_ref[span, :] = (silu * up).astype(BF16)
        silu_ref[span, :] = silu.astype(BF16)
        slope_ref[span, :] = (up * sigm * (1.0 + gate * (1.0 - sigm))).astype(BF16)


def collected(held):
    counts = [len(block) for block in held]
    rows, model = held[0][0].shape
    scratch = [
        pltpu.VMEM((len(held) * rows, model), BF16),
        pltpu.SemaphoreType.DMA((sum(counts),)),
    ]
    arrays = [array for block in held for array in block]
    return counts, arrays, [pl.BlockSpec(memory_space=pl.ANY)] * len(arrays), scratch


def gate_up(chain, held, gate, up):
    counts, arrays, specs, scratch = collected(held)
    rows, model = scratch[0].shape
    n, width = len(gate.pieces), gate.width
    tile = min(256, width)
    out = pl.BlockSpec((rows, tile), lambda j: (0, j))
    return chain.call(
        functools.partial(gate_body, n, counts),
        (width // tile,),
        specs + gate.tiles(tile) + up.tiles(tile),
        [out] * 3,
        [((rows, width), BF16)] * 3,
        flops=4 * rows * model * width,
        scratch=scratch,
        moved=2 * (rows * model + 2 * model * width + 3 * rows * width),
    )(*arrays, *gate.pieces, *up.pieces)


def hidden_back_body(n, g_ref, *refs):
    weight = joined(refs[:n])
    slope_ref, silu_ref, gate_ref, up_ref = refs[n:]
    for s in range(g_ref.shape[0] // SEQ):
        span = slice(s * SEQ, (s + 1) * SEQ)
        grad = nn(g_ref[span, :], weight)
        gate_ref[span, :] = (grad * slope_ref[span, :].astype(F32)).astype(BF16)
        up_ref[span, :] = (grad * silu_ref[span, :].astype(F32)).astype(BF16)


def hidden_back(chain, grads, down, slope, silu):
    rows, model = grads.shape
    n, width = len(down.pieces), down.width
    tile = min(256, width)
    out = pl.BlockSpec((rows, tile), lambda j: (0, j))
    return chain.call(
        functools.partial(hidden_back_body, n),
        (width // tile,),
        [whole(grads.shape)] + down.tiles(tile) + [out] * 2,
        [out] * 2,
        [((rows, width), BF16)] * 2,
        flops=2 * rows * model * width,
        moved=2 * (rows * model + model * width + 4 * rows * width),
    )(grads, *down.pieces, slope, silu)


def mixed_back_body(n, counts, *refs):
    m = sum(counts)
    out_ref, x_ref, sems = refs[m + n :]

    @pl.when(pl.program_id(0) == 0)
    def _():
        collect(counts, refs, x_ref, sems)

    out_ref[...] = nn(x_ref[...], joined(refs[m : m + n])).astype(BF16)


def mixed_back(chain, held, out):
    counts, arrays, specs, scratch = collected(held)
    rows, model = scratch[0].shape
    n, width = len(out.pieces), out.width
    tile = min(256, width)
    return chain.call(
        functools.partial(mixed_back_body, n, counts),
        (width // tile,),
        specs + out.tiles(tile),
        [pl.BlockSpec((rows, tile), lambda j: (0, j))],
        [((rows, width), BF16)],
        flops=2 * rows * model * width,
        scratch=scratch,
        moved=2 * (rows * model + model * width + rows * width),
    )(*arrays, *out.pieces)[0]


def trans_body(n, starts, targets, *refs):
    parts, blocks = len(starts), len(targets[0])
    lefts = refs[:parts]
    pieces = refs[parts : parts * (n + 1)]
    outs = refs[parts * (n + 1) : -4]
    held, ready, sems, out_sems = refs[-4:]
    j = pl.program_id(0)
    depth, width = held.shape[2:]
    rows = ready.shape[1] // blocks

    def copy(i, p, slot):
        source = pieces[p * n + i].at[pl.ds(0, depth), pl.ds(starts[p], width)]
        return pltpu.make_async_copy(source, held.at[slot, p], sems.at[slot, p])

    def fetch(step, slot):
        for i in range(n):

            @pl.when(step == i)
            def _():
                for p in range(parts):
                    copy(i, p, slot).start()

    def leave(slot, k, array, first, column):
        target = outs[array].at[pl.ds(first, rows), pl.ds(column, depth)]
        source = ready.at[slot, pl.ds(k * rows, rows), :]
        return pltpu.make_async_copy(source, target, out_sems.at[slot, k])

    def left(slot):
        for k in range(blocks):
            leave(slot, k, 0, 0, 0).wait()

    @pl.when(j == 0)
    def _():
        fetch(j, 0)

    @pl.when(j + 1 < n)
    def _():
        fetch(j + 1, (j + 1) % 2)

    slot = j % 2
    for p in range(parts):
        copy(0, p, slot).wait()

    @pl.when(j >= 2)
    def _():
        left(slot)

    for s in range(blocks * rows // SEQ):
        span = slice(s * SEQ, (s + 1) * SEQ)
        total = nt(lefts[0][span, :], held[slot, 0])
        for p in range(1, parts):
            total += nt(lefts[p][span, :], held[slot, p])
        ready[slot, span, :] = total.astype(BF16)
    column = pl.multiple_of(j % (n // 2) * depth, 128)
    for h in range(2):

        @pl.when((j >= n // 2) == (h == 1))
        def _():
            for k, (array, first) in enumerate(targets[h]):
                leave(slot, k, array, first, column).start()

    @pl.when(j == n - 1)
    def _():
        left(1 - slot)
        left(slot)


def times_trans(chain, parts, group):
    weights = [weight for _, weight in parts]
    n, depth, width = len(weights[0].pieces), weights[0].rows, weights[0].width
    rows = parts[0][0].shape[0]
    half = weights[0].model // 2
    size = rows // group.size
    messages = group.messages()
    shapes = [((size, half), BF16)] * 2
    targets = [{0: (0, 0)}, {0: (1, 0)}]
    for h in range(2):
        for keys in messages[h]:
            for i, k in enumerate(keys):
                targets[h][k] = (len(shapes), i * size)
            shapes.append(((len(keys) * size, half), BF16))
    targets = [[t[k] for k in range(group.size)] for t in targets]
    anywhere = pl.BlockSpec(memory_space=pl.ANY)
    outs = chain.call(
        functools.partial(trans_body, n, [weight.start for weight in weights], targets),
        (n,),
        [whole((rows, width))] * len(parts) + [anywhere] * (n * len(parts)),
        [anywhere] * len(shapes),
        shapes,
        flops=4 * rows * half * width * len(parts),
        scratch=[
            pltpu.VMEM((2, len(parts), depth, width), BF16),
            pltpu.VMEM((2, rows, depth), BF16),
            pltpu.SemaphoreType.DMA((2, len(parts))),
            pltpu.SemaphoreType.DMA((2, group.size)),
        ],
        moved=2 * (2 * rows * half + len(parts) * (rows + 2 * half) * width),
    )(*[left for left, _ in parts], *[piece for weight in weights for piece in weight.pieces])
    m = group.bits
    return outs[:2], [outs[2 : 2 + m], outs[2 + m :]]


def grad_body(parts, got, blocks, steps, *refs):
    lefts, refs = refs[:blocks], refs[blocks:]
    rights, refs = refs[:parts], refs[parts:]
    got_ref = refs[0] if got else None
    outs, turned = refs[got:-1], refs[-1]
    j = pl.program_id(0)

    @pl.when(j == 0)
    def _():
        rows = turned.shape[1] // blocks
        for k in range(blocks):
            turned[:, cut(rows, k)] = lefts[k][...].T

    for i in range(parts):

        @pl.when((j >= i * steps) & (j < (i + 1) * steps))
        def _():
            total = nn(turned[...], rights[i][...])
            if got:
                total += got_ref[...].astype(F32)
            total = total.astype(BF16)
            first = 0
            for out_ref in outs:
                count = out_ref.shape[0]
                out_ref[...] = total[first : first + count]
                first += count


def weight_grads(chain, left, which, rights, got=None, bits=0):
    rows, width = rights[0].shape
    parts = len(rights)
    tile = min(512, width)
    steps = width // tile
    if isinstance(left, list):
        lefts = [block[0] if len(block) == 1 else block[which] for block in left]
        half = left[0][0].shape[1] // 2
        places = [which if len(block) == 1 else 0 for block in left]
    else:
        lefts, places, half = [left], [which], left.shape[1] // 2
    blocks = len(lefts)
    ins = [
        pl.BlockSpec((rows // blocks, half), functools.partial(lambda at, j: (0, at), at))
        for at in places
    ]
    for i in range(parts):
        ins.append(
            pl.BlockSpec(
                (rows, tile),
                functools.partial(
                    lambda first, j: (0, jnp.clip(j - first, 0, steps - 1)), i * steps
                ),
            )
        )
    column = lambda j: (0, j)
    more = [] if got is None else [got]
    sizes = [half >> bits]
    for p in range(bits):
        sizes += [sizes[0], ((1 << p) - 1) * sizes[0]] if p else [sizes[0]]
    return chain.call(
        functools.partial(grad_body, parts, len(more), blocks, steps),
        (parts * steps,),
        ins + [pl.BlockSpec((half, tile), column)] * len(more),
        [pl.BlockSpec((size, tile), column) for size in sizes],
        [((size, parts * width), BF16) for size in sizes],
        flops=2 * rows * half * width * parts,
        scratch=[pltpu.VMEM((half, rows), BF16)],
        moved=2 * (rows * half + parts * (rows + half) * width),
    )(*lefts, *rights, *more)


def causal(scores):
    past = scores.shape[0] - HALF_SEQ
    key = lax.broadcasted_iota(jnp.int32, (HALF_SEQ, HALF_SEQ), 0)
    query = lax.broadcasted_iota(jnp.int32, (HALF_SEQ, HALF_SEQ), 1)
    last = jnp.where(key <= query, scores[past:], -1e30)
    return last if past == 0 else jnp.concatenate([scores[:past], last], axis=0)


def head_of(h):
    return slice(h * HEAD_DIM, (h + 1) * HEAD_DIM)


def span_of(b):
    return slice(b * HALF_SEQ, (b + 1) * HALF_SEQ)


def in_place(shift_ref, ref, count):
    rows = SEQ // count
    spans = [pl.ds(pl.multiple_of((i ^ shift_ref[0]) * rows, rows), rows) for i in range(count)]
    return jnp.concatenate([ref[span, :] for span in spans], axis=0)


def put_back(shift_ref, ref, count, values):
    rows = SEQ // count
    for i in range(count):
        ref[pl.ds(pl.multiple_of((i ^ shift_ref[0]) * rows, rows), rows), :] = values[cut(rows, i)]


def attend_body(count, shift_ref, q_ref, k_ref, v_ref, out_ref, sum_ref):
    queries, keys = in_place(shift_ref, q_ref, count), in_place(shift_ref, k_ref, count)
    values = in_place(shift_ref, v_ref, count).astype(F32).T.astype(BF16)
    heads = []
    for h in range(2):
        blocks = []
        for b in range(2):
            reach = (b + 1) * HALF_SEQ
            query = queries[span_of(b), head_of(h)] * BF16(FACTOR)
            scores = causal(nt(keys[:reach, head_of(h)], query))
            top = jnp.max(scores, axis=0, keepdims=True)
            expo = jnp.exp(scores - top)
            total = jnp.sum(expo, axis=0, keepdims=True)
            mixed = nn(values[head_of(h), :reach], expo.astype(BF16))
            blocks.append(mixed * (1.0 / total))
            sum_ref[0, 0, h : h + 1, span_of(b)] = top + jnp.log(total)
        heads.append(jnp.concatenate(blocks, axis=1))
    put_back(shift_ref, out_ref, count, jnp.concatenate(heads, axis=0).T.astype(BF16))


def attend(chain, shift, count, query, key, value):
    rows, width = query.shape
    seqs, pairs = rows // SEQ, width // PAIR
    tile = pl.BlockSpec((SEQ, PAIR), lambda s, p, _: (s, p))
    return chain.call(
        functools.partial(attend_body, count),
        (seqs, pairs),
        [tile] * 3,
        [tile, pl.BlockSpec((1, 1, 2, SEQ), lambda s, p, _: (s, p, 0, 0))],
        [((rows, width), BF16), ((seqs, pairs, 2, SEQ), F32)],
        flops=16 * rows * width * SEQ,
        prefetch=1,
        moved=8 * rows * width,
    )(shift, query, key, value)


def attend_back_body(
    count, shift_ref, q_ref, k_ref, v_ref, g_ref, sum_ref, cos_ref, sin_ref, dq_ref, dk_ref, dv_ref
):
    queries, keys, values, grads = (
        in_place(shift_ref, ref, count) for ref in (q_ref, k_ref, v_ref, g_ref)
    )
    turned = keys.astype(F32).T.astype(BF16)
    dq_heads, dk_heads, dv_heads = [], [], []
    for h in range(2):
        dq, dk, dv = [], [], []
        for b in range(2):
            reach = (b + 1) * HALF_SEQ
            query = queries[span_of(b), head_of(h)]
            grad = grads[span_of(b), head_of(h)]
            scores = causal(nt(keys[:reach, head_of(h)], query * BF16(FACTOR)))
            probs = jnp.exp(scores - sum_ref[0, 0, h : h + 1, span_of(b)])
            probs_grad = nt(values[:reach, head_of(h)], grad)
            inner = jnp.sum(probs * probs_grad, axis=0, keepdims=True)
            score_grad = (probs * (probs_grad - inner)).astype(BF16)
            dv.append(nn(probs.astype(BF16), grad))
            dk.append(nn(score_grad, query))
            dq.append(nn(turned[head_of(h), :reach], score_grad))
        for parts, heads in ((dk, dk_heads), (dv, dv_heads)):
            heads.append(
                jnp.concatenate([parts[1][:HALF_SEQ] + parts[0], parts[1][HALF_SEQ:]], axis=0)
            )
        dq_heads.append(jnp.concatenate(dq, axis=1))
    dq = jnp.concatenate(dq_heads, axis=0).T * FACTOR
    dk = jnp.concatenate(dk_heads, axis=1) * FACTOR
    dv = jnp.concatenate(dv_heads, axis=1).astype(BF16)
    cosine, sine = cos_ref[...], sin_ref[...]
    put_back(shift_ref, dq_ref, count, (dq * cosine - turn(dq) * sine).astype(BF16))
    put_back(shift_ref, dk_ref, count, (dk * cosine - turn(dk) * sine).astype(BF16))
    put_back(shift_ref, dv_ref, count, dv)


def attend_back(chain, shift, count, query, key, value, grad, logsum, tables):
    rows, width = query.shape
    seqs, pairs = rows // SEQ, width // PAIR
    tile = pl.BlockSpec((SEQ, PAIR), lambda s, p, _: (s, p))
    return chain.call(
        functools.partial(attend_back_body, count),
        (seqs, pairs),
        [tile] * 4
        + [pl.BlockSpec((1, 1, 2, SEQ), lambda s, p, _: (s, p, 0, 0))]
        + [whole((SEQ, PAIR))] * 2,
        [tile] * 3,
        [((rows, width), BF16)] * 3,
        flops=40 * rows * width * SEQ,
        prefetch=1,
        moved=14 * rows * width,
    )(shift, query, key, value, grad, logsum, *tables)


def local(
    chips,
    group,
    tokens,
    attn_gain,
    query_weight,
    key_weight,
    value_weight,
    output_weight,
    ffn_gain,
    gate_weight,
    up_weight,
    down_weight,
    cotangent,
):
    line = jnp.asarray(chips.table)[lax.axis_index("dp")]
    rows, model = tokens.shape
    count = SEQ // rows
    shift = lax.axis_index("tensor") % count
    row = jnp.arange(SEQ, dtype=jnp.int32)
    places = rope_tables(row)
    tables = rope_tables((row // rows ^ shift) * rows + row % rows)
    shift = jnp.reshape(shift, (1,)).astype(jnp.int32)
    depth, own = query_weight.shape
    hidden_units = gate_weight.shape[1]
    chain = Chain()

    def gather(piece):
        return Gather(chips, chain, chain.join(piece)[0])

    def spread_of(values):
        return Spread(group, chain, chain.join(values)[0])

    def fold_of(part):
        own_part, sent = part
        sent = chain.join(*sent[0], *sent[1])
        return Fold(group, chain, own_part, [sent[: group.bits], sent[group.bits :]])

    def grads_of(left, rights):
        got = [None]
        chain.ask(weight_grads(chain, left, 1, rights)[0], got, 0, chips.other)

        def mine(apart=False):
            if got[0] is None:
                chain.flush()
            blocks = weight_grads(chain, left, 0, rights, got[0], chips.bits)
            return Sums(chips, chain, blocks, apart)

        return mine

    extra = jnp.concatenate([attn_gain, ffn_gain, jnp.zeros((4 * own - 2 * depth,), BF16)])
    attn = jnp.concatenate([query_weight, key_weight, value_weight, output_weight.T], axis=1)
    attn = gather(jnp.concatenate([attn, jnp.broadcast_to(extra, (16, 4 * own))], axis=0))
    spread = spread_of(tokens)
    grads_spread = spread_of(cotangent)
    grads_spread.later = []
    chain.end(attn, spread, grads_spread)
    chain.end(attn, spread)
    all_tokens = spread.blocks()
    attn = attn.pieces()
    pair = gather(jnp.concatenate([gate_weight, up_weight], axis=1))
    w_query, w_key, w_value, w_output = [Weight(attn, depth, i * own, own) for i in range(4)]
    gains = jnp.concatenate(
        [piece[depth : depth + 1, : 2 * depth].reshape(2, depth) for piece in attn], axis=1
    ).astype(F32)

    group_one = ordered(chain, norm_body, line, gains, all_tokens)
    query, key, value = project(chain, group_one, tables, w_query, w_key, w_value)
    mixed, logsum = attend(chain, shift, count, query, key, value)
    out_part = times_trans(chain, [(mixed, w_output)], group)
    fold = fold_of(out_part)
    chain.end(fold, pair)
    chain.end(fold)
    attended = fold.total()
    middle, second = by_rows(
        chain, middle_body, line, tokens, gains, attended, [], [F32, BF16]
    )
    spread = spread_of(second)
    chain.end(spread, pair)
    pair = pair.pieces()
    down = gather(down_weight.T)
    chain.end(spread)
    group_two = spread.blocks()
    grads_spread.resume()
    w_gate = Weight(pair, depth, 0, hidden_units)
    w_up = Weight(pair, depth, hidden_units, hidden_units)
    hidden, slope, silu = gate_up(chain, group_two, w_gate, w_up)

    chain.end(down, grads_spread)
    grad_rows = ordered(chain, order_body, line, gains, grads_spread.blocks())
    mine = grads_of(grad_rows, [hidden])
    down_sum = mine()
    w_down = Weight(down.pieces(), depth, 0, hidden_units)
    gate_grad, up_grad = hidden_back(chain, grad_rows, w_down, slope, silu)
    mine_gate = grads_of(group_two, [gate_grad])
    chain.end(down_sum)
    second_part = times_trans(chain, [(gate_grad, w_gate), (up_grad, w_up)], group)
    mine_up = grads_of(group_two, [up_grad])
    gate_sum = mine_gate()
    chain.end(down_sum)
    fold = fold_of(second_part)
    up_sum = mine_up(True)
    chain.end(gate_sum, fold)
    result_part = times_trans(chain, [(hidden, w_down)], group)
    chain.end(up_sum, fold)
    second_grad = fold.total()
    middle_grad, low_grad = by_rows(
        chain, second_back_body, line, cotangent, gains, second_grad, [middle], [F32, BF16]
    )
    spread = spread_of(low_grad)
    chain.end(spread)
    attn_grads = spread.blocks()
    down_sum = down_sum.total()

    mixed_grad = mixed_back(chain, attn_grads, w_output)
    chain.end(gate_sum)
    fold = fold_of(result_part)
    query_back, key_back, value_back = attend_back(
        chain, shift, count, query, key, value, mixed_grad, logsum, places
    )
    mine_qkv = grads_of(group_one, [query_back, key_back, value_back])
    chain.end(up_sum, fold)
    mine_out = grads_of(attn_grads, [mixed])
    qkv_sum = mine_qkv()
    out_sum = mine_out()
    first_part = times_trans(
        chain, [(query_back, w_query), (key_back, w_key), (value_back, w_value)], group
    )
    gate_sum = gate_sum.total()
    chain.end(up_sum, qkv_sum, out_sum, fold)
    result_part = fold.total()
    fold = fold_of(first_part)
    (layer_out,) = by_rows(chain, result_body, line, middle, gains, result_part, [], [BF16])
    up_sum = up_sum.total()
    chain.end(fold)
    chain.end(fold, qkv_sum)
    first_grad = fold.total()
    (input_grad,) = by_rows(
        chain, first_back_body, line, tokens, gains, first_grad, [middle_grad], [F32]
    )
    qkv_sum = qkv_sum.total()
    query_sum, key_sum, value_sum = [qkv_sum[:, cut(own, i)] for i in range(3)]

    def inner(weight, grad):
        return jnp.sum(weight.astype(F32) * grad, axis=1)

    gain_one_part = (
        inner(query_weight, query_sum) + inner(key_weight, key_sum) + inner(value_weight, value_sum)
    ) / attn_gain.astype(F32)
    gain_two_part = (inner(gate_weight, gate_sum) + inner(up_weight, up_sum)) / ffn_gain.astype(F32)
    gain_one_total, gain_two_total = lax.psum((gain_one_part, gain_two_part), "tensor")
    (gain_one_total,) = chain.join(gain_one_total)
    out_sum = out_sum.total()
    return (
        layer_out,
        input_grad,
        gain_one_total,
        query_sum,
        key_sum,
        value_sum,
        out_sum.T,
        gain_two_total,
        gate_sum,
        up_sum,
        down_sum.T,
    )


def solution(mesh):
    in_specs = (
        P(("dp", "tensor"), None),
        P("dp"),
        P("dp", "tensor"),
        P("dp", "tensor"),
        P("dp", "tensor"),
        P("tensor", "dp"),
        P("dp"),
        P("dp", "tensor"),
        P("dp", "tensor"),
        P("tensor", "dp"),
        P(("dp", "tensor"), None),
    )
    out_specs = (
        P(("dp", "tensor"), None),
        P(("dp", "tensor"), None),
        P("dp"),
        P("dp", "tensor"),
        P("dp", "tensor"),
        P("dp", "tensor"),
        P("tensor", "dp"),
        P("dp"),
        P("dp", "tensor"),
        P("dp", "tensor"),
        P("tensor", "dp"),
    )
    chips = Chips(mesh.shape["dp"])
    size = mesh.shape["tensor"]
    links = [[(i, i ^ 1 << b) for i in range(size)] for b in range(size.bit_length() - 1)]
    group = Group(links, "tensor")

    def run(*arrays):
        return local(chips, group, *arrays)

    return jax.shard_map(run, mesh=mesh, in_specs=in_specs, out_specs=out_specs, check_vma=False)
```

```python
import functools

import jax
import jax.numpy as jnp
import numpy as np
from jax import lax
from jax.experimental import pallas as pl
from jax.experimental.pallas import tpu as pltpu
from jax.sharding import PartitionSpec as P

HEAD_DIM = 64
SEQ = 512
EPS = 1e-05
THETA = 130000.0
BF16 = jnp.bfloat16
F32 = jnp.float32
FACTOR = HEAD_DIM**-0.5
PAIR = 2 * HEAD_DIM
HALF_SEQ = SEQ // 2
VMEM_LIMIT = 58 << 20
COST_SHARE = 4096


class Chain:
    def __init__(self):
        self.token = jnp.zeros((8, 128), F32)
        self.swaps, self.asked = [], []

    def join(self, *values):
        *values, self.token = lax.optimization_barrier((*values, self.token))
        return values

    def gate(self, *values):
        swaps, self.swaps = self.swaps, []
        asked, self.asked = self.asked, []
        joined = self.join(
            *values, *[held[i] for held, i in swaps], *[source for source, _, _, _ in asked]
        )
        for (held, i), value in zip(swaps, joined[len(values) :]):
            held[i] = value
        for (_, held, i, swap), value in zip(asked, joined[len(values) + len(swaps) :]):
            held[i] = swap(value)
            self.swaps.append((held, i))
        return joined[: len(values)]

    def end(self, *transfers):
        counts = [len(t.flying) for t in transfers]
        got = self.gate(*[value for t in transfers for value in t.flying])
        for t, count in zip(transfers, counts):
            t.go_on(got[:count])
            got = got[count:]

    def ask(self, source, held, i, swap):
        self.asked.append((source, held, i, swap))

    def flush(self):
        for source, held, i, swap in self.asked:
            held[i] = swap(source)
        self.asked = []

    def call(self, body, grid, ins, outs, shapes, flops, scratch=(), prefetch=0, moved=0):
        first = prefetch + len(ins)
        second = first + 1 + len(outs)
        anywhere = pl.BlockSpec(memory_space=pl.ANY)

        def wrapped(*refs):
            body(*refs[:first], *refs[first + 1 : second], *refs[second + 1 :])

        run = pl.pallas_call(
            wrapped,
            grid_spec=pltpu.PrefetchScalarGridSpec(
                num_scalar_prefetch=prefetch,
                grid=grid,
                in_specs=[*ins, anywhere],
                out_specs=[*outs, anywhere],
                scratch_shapes=list(scratch),
            ),
            out_shape=[jax.ShapeDtypeStruct(s, t) for s, t in [*shapes, ((8, 128), F32)]],
            compiler_params=pltpu.CompilerParams(
                vmem_limit_bytes=VMEM_LIMIT, dimension_semantics=("arbitrary",) * len(grid)
            ),
            cost_estimate=pl.CostEstimate(
                flops=flops // COST_SHARE, bytes_accessed=moved // COST_SHARE, transcendentals=0
            ),
        )

        def with_token(*args):
            *results, self.token = run(*args, self.token)
            return results

        return with_token


class Chips:
    def __init__(self, size):
        self.bits = (size // 2).bit_length() - 1
        self.size = size
        self.swap = [(i, i ^ 1) for i in range(size)]
        self.links = [
            [(i, i ^ 2 << self.bits - 1 - p) for i in range(size)] for p in range(self.bits)
        ]
        flips = [
            sum(1 << self.bits - 1 - p for p in range(self.bits) if v >> p & 1)
            for v in range(1 << self.bits)
        ]
        table = [[i ^ 2 * f for f in flips] + [i ^ 2 * f ^ 1 for f in flips] for i in range(size)]
        self.table = np.array(table, np.int32)

    def send(self, value, p):
        return lax.ppermute(value, "dp", self.links[p])

    def other(self, value):
        return lax.ppermute(value, "dp", self.swap)


class Gather:
    def __init__(self, chips, chain, piece):
        self.chips, self.chain = chips, chain
        self.own = [piece] + [None] * (2**chips.bits - 1)
        self.others = list(self.own)
        self.ask(0)
        self.keys = [1 << p for p in range(chips.bits)]
        self.flying = [chips.send(piece, p) for p in range(chips.bits)]

    def ask(self, v):
        self.chain.ask(self.own[v], self.others, v, self.chips.other)

    def go_on(self, got):
        keys, self.keys, self.flying = self.keys, [], []
        for v, piece in zip(keys, got):
            self.own[v] = piece
            for p in range(v.bit_length(), self.chips.bits):
                self.keys.append(v | 1 << p)
                self.flying.append(self.chips.send(piece, p))
        for v in keys:
            self.ask(v)

    def pieces(self):
        while self.flying:
            self.chain.end(self)
        self.chain.flush()
        return self.own + self.others


class Sums:
    def __init__(self, chips, chain, mine, apart=False):
        self.chips, self.chain, self.apart = chips, chain, apart
        self.parts = [mine[0]]
        mine = list(mine[1:])
        self.direct, self.passed = [], []
        for p in range(chips.bits):
            self.direct.append(mine.pop(0))
            self.passed.append(mine.pop(0) if p else None)
        self.p = chips.bits - 1
        self.kinds = [self.p]
        self.flying = [chips.send(self.passed[self.p], self.p)]

    def go_on(self, got):
        rows = self.parts[0].shape[0]
        kinds, self.kinds, self.flying = self.kinds, [], []
        for kind, block in zip(kinds, got):
            if kind is None:
                self.parts.append(block)
                continue
            add = lambda held, first: (
                held.astype(F32) + block[first * rows : first * rows + held.shape[0]].astype(F32)
            ).astype(BF16)
            for q in range(kind):
                self.direct[q] = add(self.direct[q], (1 << q) - 1)
                if q:
                    self.passed[q] = add(self.passed[q], 1 << q)
        p, self.p = self.p, self.p - 1
        if p > 0:
            self.send(None, self.direct[p], p)
        if p > 1:
            self.send(p - 1, self.passed[p - 1], p - 1)
        if p == (0 if self.apart else 1):
            self.send(None, self.direct[0], 0)

    def send(self, kind, value, p):
        (value,) = self.chain.join(value)
        self.kinds.append(kind)
        self.flying.append(self.chips.send(value, p))

    def terms(self):
        while self.flying:
            self.chain.end(self)
        return self.parts


class Group:
    def __init__(self, links, axes):
        self.links, self.axes = links, axes
        self.bits = len(links)
        self.size = 1 << self.bits
        self.orders = (list(range(self.bits)), list(range(self.bits))[::-1])

    def send(self, value, bit):
        return lax.ppermute(value, self.axes, self.links[bit])

    def messages(self):
        found = []
        for order in self.orders:
            found.append([])
            for top in reversed(range(self.bits)):
                found[-1].append(
                    [
                        1 << order[top] | sum(1 << order[p] for p in range(top) if v >> p & 1)
                        for v in range(1 << top)
                    ]
                )
        return found


class Spread:
    def __init__(self, group, chain, rows):
        self.group, self.chain = group, chain
        self.held = {0: [rows]}
        self.later = None
        self.keys = [(1 << b, None) for b in range(group.bits)]
        self.flying = [group.send(rows, b) for b in range(group.bits)]

    def go_on(self, got):
        fresh = list(zip(self.keys, got))
        self.keys, self.flying = [], []
        for (k, h), block in fresh:
            if h is None:
                self.held[k] = [block]
            else:
                self.held.setdefault(k, [None, None])[h] = block
        for (k, h), block in fresh:
            for way, order in enumerate(self.group.orders):
                if h is not None and h != way:
                    continue
                half = block.shape[1] // 2
                top = max(i for i, bit in enumerate(order) if k >> bit & 1)
                for i in range(top + 1, len(order)):
                    part = block if h is not None else block[:, way * half : (way + 1) * half]
                    self.keys.append((k | 1 << order[i], way))
                    if self.later is not None:
                        self.later.append((part, order[i]))
                    else:
                        self.flying.append(self.group.send(part, order[i]))

    def resume(self):
        later, self.later = self.later, None
        parts = self.chain.join(*[part for part, _ in later])
        self.flying = [self.group.send(part, bit) for part, (_, bit) in zip(parts, later)]

    def blocks(self):
        while self.flying:
            self.chain.end(self)
        return [self.held[k] for k in range(self.group.size)]


class Fold:
    def __init__(self, group, chain, own, sent):
        self.group, self.chain = group, chain
        self.rows = own[0].shape[0]
        self.sent = [list(half) for half in sent]
        self.parts = [[half] for half in own]
        self.wave = 0
        self.start()

    def start(self):
        self.flying = [
            self.group.send(self.sent[h][self.wave], order[self.group.bits - 1 - self.wave])
            for h, order in enumerate(self.group.orders)
        ]

    def go_on(self, got):
        self.wave += 1
        self.flying = []
        for h, block in enumerate(got):
            self.parts[h].append(block)
            for wave in range(self.wave, self.group.bits):
                first = self.rows << (self.group.bits - 1 - wave)
                more = block[first : 2 * first].astype(F32)
                self.sent[h][wave] = (self.sent[h][wave].astype(F32) + more).astype(BF16)
        if self.wave < self.group.bits:
            now = self.chain.join(*[sent[self.wave] for sent in self.sent])
            for sent, value in zip(self.sent, now):
                sent[self.wave] = value
            self.start()

    def total(self):
        while self.flying:
            self.chain.end(self)
        return self.parts


class Weight:
    def __init__(self, pieces, rows, start, width):
        self.pieces, self.rows, self.start, self.width = pieces, rows, start, width
        self.model = len(pieces) * rows

    def tiles(self, tile):
        first = self.start // tile
        return [pl.BlockSpec((self.rows, tile), lambda j: (0, first + j))] * len(self.pieces)


def nn(left, right):
    return lax.dot_general(left, right, (((1,), (0,)), ((), ())), preferred_element_type=F32)


def nt(left, right):
    return lax.dot_general(left, right, (((1,), (1,)), ((), ())), preferred_element_type=F32)


def tn(left, right):
    return lax.dot_general(left, right, (((0,), (0,)), ((), ())), preferred_element_type=F32)


def whole(shape):
    return pl.BlockSpec(shape, lambda *_: (0,) * len(shape))


def place(line_ref, j, width):
    return pl.ds(pl.multiple_of(line_ref[j] * width, 128), width)


def cut(width, j):
    return slice(j * width, (j + 1) * width)


def scale_of(values):
    return lax.rsqrt(jnp.mean(values * values, axis=-1, keepdims=True) + EPS)


def fetch_blocks(counts, refs, held, sems, k, slot, wait):
    first = 0
    for i, count in enumerate(counts):
        copies = []
        half = held.shape[2] // count
        for h in range(count):
            target = held.at[slot, :, pl.ds(h * half, half)]
            copies.append(pltpu.make_async_copy(refs[first + h], target, sems.at[slot, h]))
        first += count

        @pl.when(k == i)
        def _():
            for copy in copies:
                copy.wait() if wait else copy.start()


def fetched(counts, refs, held, sems):
    k = pl.program_id(0)

    @pl.when(k == 0)
    def _():
        fetch_blocks(counts, refs, held, sems, k, 0, False)

    fetch_blocks(counts, refs, held, sems, k + 1, (k + 1) % 2, False)
    fetch_blocks(counts, refs, held, sems, k, k % 2, True)
    return held.at[k % 2]


def norm_body(blocks, counts, line_ref, gain_ref, *refs):
    out_ref, held, sems = refs[sum(counts) :]
    x_ref = fetched(counts, refs, held, sems)
    width = out_ref.shape[1] // blocks
    scale = scale_of(x_ref[...].astype(F32))
    for j in range(blocks):
        part = x_ref[:, place(line_ref, j, width)].astype(F32)
        gain = gain_ref[0:1, cut(width, j)]
        out_ref[:, cut(width, j)] = (part * scale * gain).astype(BF16)


def order_body(blocks, counts, line_ref, gain_ref, *refs):
    out_ref, held, sems = refs[sum(counts) :]
    x_ref = fetched(counts, refs, held, sems)
    width = out_ref.shape[1] // blocks
    for j in range(blocks):
        out_ref[:, cut(width, j)] = x_ref[:, place(line_ref, j, width)]


def ordered(chain, body, line, gains, held):
    counts = [len(block) for block in held]
    rows, model = held[0][0].shape
    n = len(held)
    return chain.call(
        functools.partial(body, line.shape[0], counts),
        (n,),
        [whole(gains.shape)] + [pl.BlockSpec(memory_space=pl.ANY)] * sum(counts),
        [pl.BlockSpec((rows, model), lambda k, *_: (k, 0))],
        [((n * rows, model), BF16)],
        flops=20 * n * rows * model,
        scratch=[pltpu.VMEM((2, rows, model), BF16), pltpu.SemaphoreType.DMA((2, 2))],
        prefetch=1,
        moved=4 * n * rows * model,
    )(line, gains, *[array for block in held for array in block])[0]


def added(refs, span):
    total = refs[0][span, :].astype(F32)
    for ref in refs[1:]:
        total += ref[span, :].astype(F32)
    return total


def middle_body(blocks, m, line_ref, x_ref, gain_ref, *refs):
    middle_ref, out_ref = refs[2 * m :]
    width = x_ref.shape[1] // blocks
    half = x_ref.shape[1] // 2
    span = slice(None)
    middle_ref[:, :half] = added(refs[:m], span)
    middle_ref[:, half:] = added(refs[m : 2 * m], span)
    for j in range(blocks):
        here = x_ref[:, place(line_ref, j, width)].astype(F32)
        middle_ref[:, cut(width, j)] += here
    middle = middle_ref[...]
    out_ref[...] = (middle * scale_of(middle) * gain_ref[1:2, :]).astype(BF16)


def result_body(blocks, m, line_ref, middle_ref, gain_ref, *refs):
    out_ref = refs[2 * m]
    width = middle_ref.shape[1] // blocks
    span = slice(None)
    total = middle_ref[...] + jnp.concatenate(
        [added(refs[:m], span), added(refs[m : 2 * m], span)], axis=1
    )
    for j in range(blocks):
        out_ref[:, place(line_ref, j, width)] = total[:, cut(width, j)].astype(BF16)


def second_back_body(blocks, m, line_ref, dy_ref, gain_ref, *refs):
    middle_ref, out_ref, low_ref = refs[2 * m :]
    width = dy_ref.shape[1] // blocks
    span = slice(None)
    grad = jnp.concatenate([added(refs[:m], span), added(refs[m : 2 * m], span)], axis=1)
    middle = middle_ref[...]
    scale = scale_of(middle)
    normed = middle * scale
    scaled = grad * gain_ref[1:2, :]
    out_ref[...] = scale * (scaled - normed * jnp.mean(scaled * normed, axis=-1, keepdims=True))
    for j in range(blocks):
        out_ref[:, cut(width, j)] += dy_ref[:, place(line_ref, j, width)].astype(F32)
    low_ref[...] = out_ref[...].astype(BF16)


def first_back_body(blocks, m, line_ref, x_ref, gain_ref, *refs):
    above_ref, out_ref = refs[2 * m :]
    width = x_ref.shape[1] // blocks
    span = slice(None)
    scale = scale_of(x_ref[...].astype(F32))
    normed = jnp.concatenate(
        [x_ref[:, place(line_ref, j, width)].astype(F32) for j in range(blocks)], axis=1
    ) * scale
    grad = jnp.concatenate([added(refs[:m], span), added(refs[m : 2 * m], span)], axis=1)
    scaled = grad * gain_ref[0:1, :]
    back = scale * (scaled - normed * jnp.mean(scaled * normed, axis=-1, keepdims=True))
    total = above_ref[...] + back
    for j in range(blocks):
        out_ref[:, place(line_ref, j, width)] = total[:, cut(width, j)]


def by_rows(chain, body, line, first, gains, parts, more, kinds):
    rows, model = first.shape
    half = model // 2
    tile = min(128, rows)
    row = pl.BlockSpec((tile, model), lambda i, *_: (i, 0))
    slim = pl.BlockSpec((tile, half), lambda i, *_: (i, 0))
    m = len(parts[0])
    return chain.call(
        functools.partial(body, line.shape[0], m),
        (rows // tile,),
        [row, whole(gains.shape)] + [slim] * (2 * m) + [row] * len(more),
        [row] * len(kinds),
        [((rows, model), kind) for kind in kinds],
        flops=20 * rows * model,
        prefetch=1,
        moved=rows * model * (2 * m + 4 * len(kinds)),
    )(line, first, gains, *parts[0], *parts[1], *more)


def finish_body(m, n, *refs):
    total = added(refs[:m], slice(None))
    weights, outs = refs[m : m + n], refs[m + n :]
    if not n:
        outs[0][...] = total.T
        return
    width = weights[0].shape[1]
    inner = jnp.zeros((total.shape[0], 1), F32)
    for i in range(n):
        part = total[:, cut(width, i)]
        outs[i][...] = part
        inner += jnp.sum(weights[i][...].astype(F32) * part, axis=1, keepdims=True)
    outs[n][...] = jnp.broadcast_to(inner, outs[n].shape)


def finish(chain, terms, weights=()):
    rows, columns = terms[0].shape
    tile = min(128, rows)
    row = pl.BlockSpec((tile, columns), lambda i: (i, 0))
    n = len(weights)
    if n:
        slim = pl.BlockSpec((tile, columns // n), lambda i: (i, 0))
        outs = [slim] * n + [pl.BlockSpec((tile, 128), lambda i: (i, 0))]
        shapes = [((rows, columns // n), F32)] * n + [((rows, 128), F32)]
    else:
        slim = None
        outs = [pl.BlockSpec((columns, tile), lambda i: (0, i))]
        shapes = [((columns, rows), F32)]
    results = chain.call(
        functools.partial(finish_body, len(terms), n),
        (rows // tile,),
        [row] * len(terms) + [slim] * n,
        outs,
        shapes,
        flops=4 * rows * columns,
        moved=rows * columns * 12,
    )(*terms, *weights)
    if n:
        results[n] = results[n][:, 0]
    return results


def rope_tables(place):
    half = HEAD_DIM // 2
    freq = THETA ** (-2.0 * jnp.arange(half, dtype=F32) / HEAD_DIM)
    angle = place.astype(F32)[:, None] * freq[None, :]
    cosine, sine = jnp.cos(angle), jnp.sin(angle)
    return (
        jnp.concatenate([cosine] * (PAIR // half), axis=1),
        jnp.concatenate([-sine, sine] * (PAIR // HEAD_DIM), axis=1),
    )


def turn(values):
    half = HEAD_DIM // 2
    width = values.shape[-1]
    lane = lax.broadcasted_iota(jnp.int32, values.shape, 1) % HEAD_DIM
    return jnp.where(
        lane < half, pltpu.roll(values, width - half, 1), pltpu.roll(values, half, 1)
    )


def joined(refs):
    return jnp.concatenate([r[...] for r in refs], axis=0)


def qkv_body(n, x_ref, cos_ref, sin_ref, *refs):
    weights, outs = refs[: 3 * n], refs[3 * n :]
    rows = x_ref.shape[0]
    tile = outs[0].shape[1]
    for i in range(3):
        weight = joined(weights[i * n : (i + 1) * n])
        for s in range(rows // SEQ):
            span = slice(s * SEQ, (s + 1) * SEQ)
            product = nn(x_ref[span, :], weight)
            if i == 2:
                outs[i][span, :] = product.astype(BF16)
                continue
            for t in range(tile // PAIR):
                here = product[:, t * PAIR : (t + 1) * PAIR]
                turned = here * cos_ref[...] + turn(here) * sin_ref[...]
                outs[i][span, t * PAIR : (t + 1) * PAIR] = turned.astype(BF16)


def project(chain, x, tables, query, key, value):
    rows, model = x.shape
    n, width = len(query.pieces), query.width
    tile = min(256, width)
    out = pl.BlockSpec((rows, tile), lambda j: (0, j))
    return chain.call(
        functools.partial(qkv_body, n),
        (width // tile,),
        [whole(x.shape), whole((SEQ, PAIR)), whole((SEQ, PAIR))]
        + query.tiles(tile)
        + key.tiles(tile)
        + value.tiles(tile),
        [out] * 3,
        [((rows, width), BF16)] * 3,
        flops=6 * rows * model * width,
        moved=2 * (rows * model + 3 * model * width + 3 * rows * width),
    )(x, *tables, *query.pieces, *key.pieces, *value.pieces)


def collect(counts, refs, held, sems):
    rows = held.shape[0] // len(counts)
    copies = []
    for k, count in enumerate(counts):
        half = held.shape[1] // count
        for h in range(count):
            target = held.at[pl.ds(k * rows, rows), pl.ds(h * half, half)]
            i = len(copies)
            copies.append(pltpu.make_async_copy(refs[i], target, sems.at[i]))
    for copy in copies:
        copy.start()
    for copy in copies:
        copy.wait()


def gate_body(n, counts, *refs):
    m = sum(counts)
    gate_w, up_w = refs[m : m + n], refs[m + n : m + 2 * n]
    hidden_ref, slope_ref, silu_ref, x_ref, sems = refs[m + 2 * n :]

    @pl.when(pl.program_id(0) == 0)
    def _():
        collect(counts, refs, x_ref, sems)

    gate_weight, up_weight = joined(gate_w), joined(up_w)
    for s in range(x_ref.shape[0] // SEQ):
        span = slice(s * SEQ, (s + 1) * SEQ)
        gate = nn(x_ref[span, :], gate_weight)
        up = nn(x_ref[span, :], up_weight)
        sigm = jax.nn.sigmoid(gate)
        silu = gate * sigm
        hidden_ref[span, :] = (silu * up).astype(BF16)
        silu_ref[span, :] = silu.astype(BF16)
        slope_ref[span, :] = (up * sigm * (1.0 + gate * (1.0 - sigm))).astype(BF16)


def collected(held):
    counts = [len(block) for block in held]
    rows, model = held[0][0].shape
    scratch = [
        pltpu.VMEM((len(held) * rows, model), BF16),
        pltpu.SemaphoreType.DMA((sum(counts),)),
    ]
    arrays = [array for block in held for array in block]
    return counts, arrays, [pl.BlockSpec(memory_space=pl.ANY)] * len(arrays), scratch


def gate_up(chain, held, gate, up):
    counts, arrays, specs, scratch = collected(held)
    rows, model = scratch[0].shape
    n, width = len(gate.pieces), gate.width
    tile = min(256, width)
    out = pl.BlockSpec((rows, tile), lambda j: (0, j))
    return chain.call(
        functools.partial(gate_body, n, counts),
        (width // tile,),
        specs + gate.tiles(tile) + up.tiles(tile),
        [out] * 3,
        [((rows, width), BF16)] * 3,
        flops=4 * rows * model * width,
        scratch=scratch,
        moved=2 * (rows * model + 2 * model * width + 3 * rows * width),
    )(*arrays, *gate.pieces, *up.pieces)


def hidden_back_body(n, g_ref, *refs):
    weight = joined(refs[:n])
    slope_ref, silu_ref, gate_ref, up_ref = refs[n:]
    for s in range(g_ref.shape[0] // SEQ):
        span = slice(s * SEQ, (s + 1) * SEQ)
        grad = nn(g_ref[span, :], weight)
        gate_ref[span, :] = (grad * slope_ref[span, :].astype(F32)).astype(BF16)
        up_ref[span, :] = (grad * silu_ref[span, :].astype(F32)).astype(BF16)


def hidden_back(chain, grads, down, slope, silu):
    rows, model = grads.shape
    n, width = len(down.pieces), down.width
    tile = min(256, width)
    out = pl.BlockSpec((rows, tile), lambda j: (0, j))
    return chain.call(
        functools.partial(hidden_back_body, n),
        (width // tile,),
        [whole(grads.shape)] + down.tiles(tile) + [out] * 2,
        [out] * 2,
        [((rows, width), BF16)] * 2,
        flops=2 * rows * model * width,
        moved=2 * (rows * model + model * width + 4 * rows * width),
    )(grads, *down.pieces, slope, silu)


def mixed_back_body(n, counts, *refs):
    m = sum(counts)
    out_ref, x_ref, sems = refs[m + n :]

    @pl.when(pl.program_id(0) == 0)
    def _():
        collect(counts, refs, x_ref, sems)

    out_ref[...] = nn(x_ref[...], joined(refs[m : m + n])).astype(BF16)


def mixed_back(chain, held, out):
    counts, arrays, specs, scratch = collected(held)
    rows, model = scratch[0].shape
    n, width = len(out.pieces), out.width
    tile = min(256, width)
    return chain.call(
        functools.partial(mixed_back_body, n, counts),
        (width // tile,),
        specs + out.tiles(tile),
        [pl.BlockSpec((rows, tile), lambda j: (0, j))],
        [((rows, width), BF16)],
        flops=2 * rows * model * width,
        scratch=scratch,
        moved=2 * (rows * model + model * width + rows * width),
    )(*arrays, *out.pieces)[0]


def trans_body(n, starts, targets, *refs):
    parts, blocks = len(starts), len(targets[0])
    lefts = refs[:parts]
    pieces = refs[parts : parts * (n + 1)]
    outs = refs[parts * (n + 1) : -4]
    held, ready, sems, out_sems = refs[-4:]
    j = pl.program_id(0)
    depth, width = held.shape[2:]
    rows = ready.shape[1] // blocks

    def copy(i, p, slot):
        source = pieces[p * n + i].at[pl.ds(0, depth), pl.ds(starts[p], width)]
        return pltpu.make_async_copy(source, held.at[slot, p], sems.at[slot, p])

    def fetch(step, slot):
        for i in range(n):

            @pl.when(step == i)
            def _():
                for p in range(parts):
                    copy(i, p, slot).start()

    def leave(slot, k, array, first, column):
        target = outs[array].at[pl.ds(first, rows), pl.ds(column, depth)]
        source = ready.at[slot, pl.ds(k * rows, rows), :]
        return pltpu.make_async_copy(source, target, out_sems.at[slot, k])

    def left(slot):
        for k in range(blocks):
            leave(slot, k, 0, 0, 0).wait()

    @pl.when(j == 0)
    def _():
        fetch(j, 0)

    @pl.when(j + 1 < n)
    def _():
        fetch(j + 1, (j + 1) % 2)

    slot = j % 2
    for p in range(parts):
        copy(0, p, slot).wait()

    @pl.when(j >= 2)
    def _():
        left(slot)

    for s in range(blocks * rows // SEQ):
        span = slice(s * SEQ, (s + 1) * SEQ)
        total = nt(lefts[0][span, :], held[slot, 0])
        for p in range(1, parts):
            total += nt(lefts[p][span, :], held[slot, p])
        ready[slot, span, :] = total.astype(BF16)
    column = pl.multiple_of(j % (n // 2) * depth, 128)
    for h in range(2):

        @pl.when((j >= n // 2) == (h == 1))
        def _():
            for k, (array, first) in enumerate(targets[h]):
                leave(slot, k, array, first, column).start()

    @pl.when(j == n - 1)
    def _():
        left(1 - slot)
        left(slot)


def times_trans(chain, parts, group):
    weights = [weight for _, weight in parts]
    n, depth, width = len(weights[0].pieces), weights[0].rows, weights[0].width
    rows = parts[0][0].shape[0]
    half = weights[0].model // 2
    size = rows // group.size
    messages = group.messages()
    shapes = [((size, half), BF16)] * 2
    targets = [{0: (0, 0)}, {0: (1, 0)}]
    for h in range(2):
        for keys in messages[h]:
            for i, k in enumerate(keys):
                targets[h][k] = (len(shapes), i * size)
            shapes.append(((len(keys) * size, half), BF16))
    targets = [[t[k] for k in range(group.size)] for t in targets]
    anywhere = pl.BlockSpec(memory_space=pl.ANY)
    outs = chain.call(
        functools.partial(trans_body, n, [weight.start for weight in weights], targets),
        (n,),
        [whole((rows, width))] * len(parts) + [anywhere] * (n * len(parts)),
        [anywhere] * len(shapes),
        shapes,
        flops=4 * rows * half * width * len(parts),
        scratch=[
            pltpu.VMEM((2, len(parts), depth, width), BF16),
            pltpu.VMEM((2, rows, depth), BF16),
            pltpu.SemaphoreType.DMA((2, len(parts))),
            pltpu.SemaphoreType.DMA((2, group.size)),
        ],
        moved=2 * (2 * rows * half + len(parts) * (rows + 2 * half) * width),
    )(*[left for left, _ in parts], *[piece for weight in weights for piece in weight.pieces])
    m = group.bits
    return outs[:2], [outs[2 : 2 + m], outs[2 + m :]]


def grad_body(parts, got, blocks, steps, *refs):
    lefts, refs = refs[:blocks], refs[blocks:]
    rights, refs = refs[:parts], refs[parts:]
    got_ref = refs[0] if got else None
    outs, turned = refs[got:-1], refs[-1]
    j = pl.program_id(0)

    @pl.when(j == 0)
    def _():
        rows = turned.shape[1] // blocks
        for k in range(blocks):
            turned[:, cut(rows, k)] = lefts[k][...].T

    for i in range(parts):

        @pl.when((j >= i * steps) & (j < (i + 1) * steps))
        def _():
            total = nn(turned[...], rights[i][...])
            if got:
                total += got_ref[...].astype(F32)
            total = total.astype(BF16)
            first = 0
            for out_ref in outs:
                count = out_ref.shape[0]
                out_ref[...] = total[first : first + count]
                first += count


def weight_grads(chain, left, which, rights, got=None, bits=0):
    rows, width = rights[0].shape
    parts = len(rights)
    tile = min(512, width)
    steps = width // tile
    if isinstance(left, list):
        lefts = [block[0] if len(block) == 1 else block[which] for block in left]
        half = left[0][0].shape[1] // 2
        places = [which if len(block) == 1 else 0 for block in left]
    else:
        lefts, places, half = [left], [which], left.shape[1] // 2
    blocks = len(lefts)
    ins = [
        pl.BlockSpec((rows // blocks, half), functools.partial(lambda at, j: (0, at), at))
        for at in places
    ]
    for i in range(parts):
        ins.append(
            pl.BlockSpec(
                (rows, tile),
                functools.partial(
                    lambda first, j: (0, jnp.clip(j - first, 0, steps - 1)), i * steps
                ),
            )
        )
    column = lambda j: (0, j)
    more = [] if got is None else [got]
    sizes = [half >> bits]
    for p in range(bits):
        sizes += [sizes[0], ((1 << p) - 1) * sizes[0]] if p else [sizes[0]]
    return chain.call(
        functools.partial(grad_body, parts, len(more), blocks, steps),
        (parts * steps,),
        ins + [pl.BlockSpec((half, tile), column)] * len(more),
        [pl.BlockSpec((size, tile), column) for size in sizes],
        [((size, parts * width), BF16) for size in sizes],
        flops=2 * rows * half * width * parts,
        scratch=[pltpu.VMEM((half, rows), BF16)],
        moved=2 * (rows * half + parts * (rows + half) * width),
    )(*lefts, *rights, *more)


def causal(scores):
    past = scores.shape[0] - HALF_SEQ
    key = lax.broadcasted_iota(jnp.int32, (HALF_SEQ, HALF_SEQ), 0)
    query = lax.broadcasted_iota(jnp.int32, (HALF_SEQ, HALF_SEQ), 1)
    last = jnp.where(key <= query, scores[past:], -1e30)
    return last if past == 0 else jnp.concatenate([scores[:past], last], axis=0)


def head_of(h):
    return slice(h * HEAD_DIM, (h + 1) * HEAD_DIM)


def span_of(b):
    return slice(b * HALF_SEQ, (b + 1) * HALF_SEQ)


def in_place(shift_ref, ref, count):
    rows = SEQ // count
    spans = [pl.ds(pl.multiple_of((i ^ shift_ref[0]) * rows, rows), rows) for i in range(count)]
    return jnp.concatenate([ref[span, :] for span in spans], axis=0)


def put_back(shift_ref, ref, count, values):
    rows = SEQ // count
    for i in range(count):
        ref[pl.ds(pl.multiple_of((i ^ shift_ref[0]) * rows, rows), rows), :] = values[cut(rows, i)]


def attend_body(count, shift_ref, q_ref, k_ref, v_ref, out_ref, sum_ref):
    queries, keys = in_place(shift_ref, q_ref, count), in_place(shift_ref, k_ref, count)
    values = in_place(shift_ref, v_ref, count).astype(F32).T.astype(BF16)
    heads = []
    for h in range(2):
        blocks = []
        for b in range(2):
            reach = (b + 1) * HALF_SEQ
            query = queries[span_of(b), head_of(h)] * BF16(FACTOR)
            scores = causal(nt(keys[:reach, head_of(h)], query))
            top = jnp.max(scores, axis=0, keepdims=True)
            expo = jnp.exp(scores - top)
            total = jnp.sum(expo, axis=0, keepdims=True)
            mixed = nn(values[head_of(h), :reach], expo.astype(BF16))
            blocks.append(mixed * (1.0 / total))
            sum_ref[0, 0, h : h + 1, span_of(b)] = top + jnp.log(total)
        heads.append(jnp.concatenate(blocks, axis=1))
    put_back(shift_ref, out_ref, count, jnp.concatenate(heads, axis=0).T.astype(BF16))


def attend(chain, shift, count, query, key, value):
    rows, width = query.shape
    seqs, pairs = rows // SEQ, width // PAIR
    tile = pl.BlockSpec((SEQ, PAIR), lambda s, p, _: (s, p))
    return chain.call(
        functools.partial(attend_body, count),
        (seqs, pairs),
        [tile] * 3,
        [tile, pl.BlockSpec((1, 1, 2, SEQ), lambda s, p, _: (s, p, 0, 0))],
        [((rows, width), BF16), ((seqs, pairs, 2, SEQ), F32)],
        flops=16 * rows * width * SEQ,
        prefetch=1,
        moved=8 * rows * width,
    )(shift, query, key, value)


def attend_back_body(
    count, shift_ref, q_ref, k_ref, v_ref, g_ref, sum_ref, cos_ref, sin_ref, dq_ref, dk_ref, dv_ref
):
    queries, keys, values, grads = (
        in_place(shift_ref, ref, count) for ref in (q_ref, k_ref, v_ref, g_ref)
    )
    turned = keys.astype(F32).T.astype(BF16)
    dq_heads, dk_heads, dv_heads = [], [], []
    for h in range(2):
        dq, dk, dv = [], [], []
        for b in range(2):
            reach = (b + 1) * HALF_SEQ
            query = queries[span_of(b), head_of(h)]
            grad = grads[span_of(b), head_of(h)]
            scores = causal(nt(keys[:reach, head_of(h)], query * BF16(FACTOR)))
            probs = jnp.exp(scores - sum_ref[0, 0, h : h + 1, span_of(b)])
            probs_grad = nt(values[:reach, head_of(h)], grad)
            inner = jnp.sum(probs * probs_grad, axis=0, keepdims=True)
            score_grad = (probs * (probs_grad - inner)).astype(BF16)
            dv.append(nn(probs.astype(BF16), grad))
            dk.append(nn(score_grad, query))
            dq.append(nn(turned[head_of(h), :reach], score_grad))
        for parts, heads in ((dk, dk_heads), (dv, dv_heads)):
            heads.append(
                jnp.concatenate([parts[1][:HALF_SEQ] + parts[0], parts[1][HALF_SEQ:]], axis=0)
            )
        dq_heads.append(jnp.concatenate(dq, axis=1))
    dq = jnp.concatenate(dq_heads, axis=0).T * FACTOR
    dk = jnp.concatenate(dk_heads, axis=1) * FACTOR
    dv = jnp.concatenate(dv_heads, axis=1).astype(BF16)
    cosine, sine = cos_ref[...], sin_ref[...]
    put_back(shift_ref, dq_ref, count, (dq * cosine - turn(dq) * sine).astype(BF16))
    put_back(shift_ref, dk_ref, count, (dk * cosine - turn(dk) * sine).astype(BF16))
    put_back(shift_ref, dv_ref, count, dv)


def attend_back(chain, shift, count, query, key, value, grad, logsum, tables):
    rows, width = query.shape
    seqs, pairs = rows // SEQ, width // PAIR
    tile = pl.BlockSpec((SEQ, PAIR), lambda s, p, _: (s, p))
    return chain.call(
        functools.partial(attend_back_body, count),
        (seqs, pairs),
        [tile] * 4
        + [pl.BlockSpec((1, 1, 2, SEQ), lambda s, p, _: (s, p, 0, 0))]
        + [whole((SEQ, PAIR))] * 2,
        [tile] * 3,
        [((rows, width), BF16)] * 3,
        flops=40 * rows * width * SEQ,
        prefetch=1,
        moved=14 * rows * width,
    )(shift, query, key, value, grad, logsum, *tables)


def local(
    chips,
    group,
    tokens,
    attn_gain,
    query_weight,
    key_weight,
    value_weight,
    output_weight,
    ffn_gain,
    gate_weight,
    up_weight,
    down_weight,
    cotangent,
):
    line = jnp.asarray(chips.table)[lax.axis_index("dp")]
    rows, model = tokens.shape
    count = SEQ // rows
    shift = lax.axis_index("tensor") % count
    row = jnp.arange(SEQ, dtype=jnp.int32)
    places = rope_tables(row)
    tables = rope_tables((row // rows ^ shift) * rows + row % rows)
    shift = jnp.reshape(shift, (1,)).astype(jnp.int32)
    depth, own = query_weight.shape
    hidden_units = gate_weight.shape[1]
    chain = Chain()

    def gather(piece):
        return Gather(chips, chain, chain.join(piece)[0])

    def spread_of(values):
        return Spread(group, chain, chain.join(values)[0])

    def fold_of(part):
        own_part, sent = part
        sent = chain.join(*sent[0], *sent[1])
        return Fold(group, chain, own_part, [sent[: group.bits], sent[group.bits :]])

    def grads_of(left, rights):
        got = [None]
        chain.ask(weight_grads(chain, left, 1, rights)[0], got, 0, chips.other)

        def mine(apart=False):
            if got[0] is None:
                chain.flush()
            blocks = weight_grads(chain, left, 0, rights, got[0], chips.bits)
            return Sums(chips, chain, blocks, apart)

        return mine

    extra = jnp.concatenate([attn_gain, ffn_gain, jnp.zeros((4 * own - 2 * depth,), BF16)])
    attn = jnp.concatenate([query_weight, key_weight, value_weight, output_weight.T], axis=1)
    attn = gather(jnp.concatenate([attn, jnp.broadcast_to(extra, (16, 4 * own))], axis=0))
    spread = spread_of(tokens)
    grads_spread = spread_of(cotangent)
    grads_spread.later = []
    (down_turned,) = chain.join(down_weight.T)
    chain.end(attn, spread, grads_spread)
    chain.end(attn, spread)
    all_tokens = spread.blocks()
    attn = attn.pieces()
    pair = gather(jnp.concatenate([gate_weight, up_weight], axis=1))
    w_query, w_key, w_value, w_output = [Weight(attn, depth, i * own, own) for i in range(4)]
    gains = jnp.concatenate(
        [piece[depth : depth + 1, : 2 * depth].reshape(2, depth) for piece in attn], axis=1
    ).astype(F32)

    group_one = ordered(chain, norm_body, line, gains, all_tokens)
    grads_spread.resume()
    query, key, value = project(chain, group_one, tables, w_query, w_key, w_value)
    mixed, logsum = attend(chain, shift, count, query, key, value)
    out_part = times_trans(chain, [(mixed, w_output)], group)
    fold = fold_of(out_part)
    chain.end(fold, pair, grads_spread)
    grad_rows = ordered(chain, order_body, line, gains, grads_spread.blocks())
    chain.end(fold)
    attended = fold.total()
    middle, second = by_rows(
        chain, middle_body, line, tokens, gains, attended, [], [F32, BF16]
    )
    spread = spread_of(second)
    chain.end(spread, pair)
    pair = pair.pieces()
    down = gather(down_turned)
    chain.end(spread)
    group_two = spread.blocks()
    w_gate = Weight(pair, depth, 0, hidden_units)
    w_up = Weight(pair, depth, hidden_units, hidden_units)
    hidden, slope, silu = gate_up(chain, group_two, w_gate, w_up)

    mine = grads_of(grad_rows, [hidden])
    chain.end(down)
    down_sum = mine()
    w_down = Weight(down.pieces(), depth, 0, hidden_units)
    gate_grad, up_grad = hidden_back(chain, grad_rows, w_down, slope, silu)
    mine_gate = grads_of(group_two, [gate_grad])
    chain.end(down_sum)
    second_part = times_trans(chain, [(gate_grad, w_gate), (up_grad, w_up)], group)
    mine_up = grads_of(group_two, [up_grad])
    gate_sum = mine_gate()
    chain.end(down_sum)
    fold = fold_of(second_part)
    up_sum = mine_up(True)
    chain.end(gate_sum, fold)
    result_part = times_trans(chain, [(hidden, w_down)], group)
    chain.end(fold)
    second_grad = fold.total()
    middle_grad, low_grad = by_rows(
        chain, second_back_body, line, cotangent, gains, second_grad, [middle], [F32, BF16]
    )
    spread = spread_of(low_grad)
    chain.end(up_sum)
    (down_sum,) = finish(chain, down_sum.terms())
    chain.end(spread)
    attn_grads = spread.blocks()

    mixed_grad = mixed_back(chain, attn_grads, w_output)
    mine_out = grads_of(attn_grads, [mixed])
    chain.end(gate_sum)
    fold = fold_of(result_part)
    query_back, key_back, value_back = attend_back(
        chain, shift, count, query, key, value, mixed_grad, logsum, places
    )
    mine_qkv = grads_of(group_one, [query_back, key_back, value_back])
    chain.end(up_sum, fold)
    qkv_sum = mine_qkv()
    out_sum = mine_out()
    first_part = times_trans(
        chain, [(query_back, w_query), (key_back, w_key), (value_back, w_value)], group
    )
    gate_sum, gate_inner = finish(chain, gate_sum.terms(), [gate_weight])
    chain.end(up_sum, qkv_sum, fold)
    result_part = fold.total()
    fold = fold_of(first_part)
    (layer_out,) = by_rows(chain, result_body, line, middle, gains, result_part, [], [BF16])
    chain.end(fold)
    up_sum, up_inner = finish(chain, up_sum.terms(), [up_weight])
    first_grad = fold.total()
    (input_grad,) = by_rows(
        chain, first_back_body, line, tokens, gains, first_grad, [middle_grad], [F32]
    )
    chain.end(qkv_sum, out_sum)
    query_sum, key_sum, value_sum, qkv_inner = finish(
        chain, qkv_sum.terms(), [query_weight, key_weight, value_weight]
    )
    gain_one_total, gain_two_total = lax.psum(
        (
            qkv_inner / attn_gain.astype(F32),
            (gate_inner + up_inner) / ffn_gain.astype(F32),
        ),
        "tensor",
    )
    (gain_one_total,) = chain.join(gain_one_total)
    (out_sum,) = finish(chain, out_sum.terms())
    return (
        layer_out,
        input_grad,
        gain_one_total,
        query_sum,
        key_sum,
        value_sum,
        out_sum,
        gain_two_total,
        gate_sum,
        up_sum,
        down_sum,
    )


def solution(mesh):
    in_specs = (
        P(("dp", "tensor"), None),
        P("dp"),
        P("dp", "tensor"),
        P("dp", "tensor"),
        P("dp", "tensor"),
        P("tensor", "dp"),
        P("dp"),
        P("dp", "tensor"),
        P("dp", "tensor"),
        P("tensor", "dp"),
        P(("dp", "tensor"), None),
    )
    out_specs = (
        P(("dp", "tensor"), None),
        P(("dp", "tensor"), None),
        P("dp"),
        P("dp", "tensor"),
        P("dp", "tensor"),
        P("dp", "tensor"),
        P("tensor", "dp"),
        P("dp"),
        P("dp", "tensor"),
        P("dp", "tensor"),
        P("tensor", "dp"),
    )
    chips = Chips(mesh.shape["dp"])
    size = mesh.shape["tensor"]
    links = [[(i, i ^ 1 << b) for i in range(size)] for b in range(size.bit_length() - 1)]
    group = Group(links, "tensor")

    def run(*arrays):
        return local(chips, group, *arrays)

    return jax.shard_map(run, mesh=mesh, in_specs=in_specs, out_specs=out_specs, check_vma=False)
```

```python
import functools

import jax
import jax.numpy as jnp
import numpy as np
from jax import lax
from jax.experimental import pallas as pl
from jax.experimental.pallas import tpu as pltpu
from jax.sharding import PartitionSpec as P

HEAD_DIM = 64
SEQ = 512
EPS = 1e-05
THETA = 130000.0
BF16 = jnp.bfloat16
F32 = jnp.float32
FACTOR = HEAD_DIM**-0.5
PAIR = 2 * HEAD_DIM
HALF_SEQ = SEQ // 2
VMEM_LIMIT = 58 << 20
COST_SHARE = 4096


class Chain:
    def __init__(self):
        self.token = jnp.zeros((8, 128), F32)
        self.swaps, self.asked = [], []

    def join(self, *values):
        *values, self.token = lax.optimization_barrier((*values, self.token))
        return values

    def gate(self, *values):
        swaps, self.swaps = self.swaps, []
        asked, self.asked = self.asked, []
        joined = self.join(
            *values, *[held[i] for held, i in swaps], *[source for source, _, _, _ in asked]
        )
        for (held, i), value in zip(swaps, joined[len(values) :]):
            held[i] = value
        for (_, held, i, swap), value in zip(asked, joined[len(values) + len(swaps) :]):
            held[i] = swap(value)
            self.swaps.append((held, i))
        return joined[: len(values)]

    def end(self, *transfers):
        counts = [len(t.flying) for t in transfers]
        got = self.gate(*[value for t in transfers for value in t.flying])
        for t, count in zip(transfers, counts):
            t.go_on(got[:count])
            got = got[count:]

    def ask(self, source, held, i, swap):
        self.asked.append((source, held, i, swap))

    def flush(self):
        for source, held, i, swap in self.asked:
            held[i] = swap(source)
        self.asked = []

    def call(self, body, grid, ins, outs, shapes, flops, scratch=(), prefetch=0, moved=0):
        first = prefetch + len(ins)
        second = first + 1 + len(outs)
        anywhere = pl.BlockSpec(memory_space=pl.ANY)

        def wrapped(*refs):
            body(*refs[:first], *refs[first + 1 : second], *refs[second + 1 :])

        run = pl.pallas_call(
            wrapped,
            grid_spec=pltpu.PrefetchScalarGridSpec(
                num_scalar_prefetch=prefetch,
                grid=grid,
                in_specs=[*ins, anywhere],
                out_specs=[*outs, anywhere],
                scratch_shapes=list(scratch),
            ),
            out_shape=[jax.ShapeDtypeStruct(s, t) for s, t in [*shapes, ((8, 128), F32)]],
            compiler_params=pltpu.CompilerParams(
                vmem_limit_bytes=VMEM_LIMIT, dimension_semantics=("arbitrary",) * len(grid)
            ),
            cost_estimate=pl.CostEstimate(
                flops=flops // COST_SHARE, bytes_accessed=moved // COST_SHARE, transcendentals=0
            ),
        )

        def with_token(*args):
            *results, self.token = run(*args, self.token)
            return results

        return with_token


class Chips:
    def __init__(self, size):
        self.bits = (size // 2).bit_length() - 1
        self.size = size
        self.swap = [(i, i ^ 1) for i in range(size)]
        self.links = [
            [(i, i ^ 2 << self.bits - 1 - p) for i in range(size)] for p in range(self.bits)
        ]
        flips = [
            sum(1 << self.bits - 1 - p for p in range(self.bits) if v >> p & 1)
            for v in range(1 << self.bits)
        ]
        table = [[i ^ 2 * f for f in flips] + [i ^ 2 * f ^ 1 for f in flips] for i in range(size)]
        self.table = np.array(table, np.int32)

    def send(self, value, p):
        return lax.ppermute(value, "dp", self.links[p])

    def other(self, value):
        return lax.ppermute(value, "dp", self.swap)


class Gather:
    def __init__(self, chips, chain, piece):
        self.chips, self.chain = chips, chain
        self.own = [piece] + [None] * (2**chips.bits - 1)
        self.others = list(self.own)
        self.ask(0)
        self.keys = [1 << p for p in range(chips.bits)]
        self.flying = [chips.send(piece, p) for p in range(chips.bits)]

    def ask(self, v):
        self.chain.ask(self.own[v], self.others, v, self.chips.other)

    def go_on(self, got):
        keys, self.keys, self.flying = self.keys, [], []
        for v, piece in zip(keys, got):
            self.own[v] = piece
            for p in range(v.bit_length(), self.chips.bits):
                self.keys.append(v | 1 << p)
                self.flying.append(self.chips.send(piece, p))
        for v in keys:
            self.ask(v)

    def pieces(self):
        while self.flying:
            self.chain.end(self)
        self.chain.flush()
        return self.own + self.others


class Sums:
    def __init__(self, chips, chain, mine, apart=False):
        self.chips, self.chain, self.apart = chips, chain, apart
        self.parts = [mine[0]]
        mine = list(mine[1:])
        self.direct, self.passed = [], []
        for p in range(chips.bits):
            self.direct.append(mine.pop(0))
            self.passed.append(mine.pop(0) if p else None)
        self.p = chips.bits - 1
        self.kinds = [self.p]
        self.flying = [chips.send(self.passed[self.p], self.p)]

    def go_on(self, got):
        rows = self.parts[0].shape[0]
        kinds, self.kinds, self.flying = self.kinds, [], []
        for kind, block in zip(kinds, got):
            if kind is None:
                self.parts.append(block)
                continue
            add = lambda held, first: (
                held.astype(F32) + block[first * rows : first * rows + held.shape[0]].astype(F32)
            ).astype(BF16)
            for q in range(kind):
                self.direct[q] = add(self.direct[q], (1 << q) - 1)
                if q:
                    self.passed[q] = add(self.passed[q], 1 << q)
        p, self.p = self.p, self.p - 1
        if p > 0:
            self.send(None, self.direct[p], p)
        if p > 1:
            self.send(p - 1, self.passed[p - 1], p - 1)
        if p == (0 if self.apart else 1):
            self.send(None, self.direct[0], 0)

    def send(self, kind, value, p):
        self.kinds.append(kind)
        self.flying.append(self.chips.send(value, p))

    def terms(self):
        while self.flying:
            self.chain.end(self)
        return self.parts


class Group:
    def __init__(self, links, axes):
        self.links, self.axes = links, axes
        self.bits = len(links)
        self.size = 1 << self.bits
        self.orders = (list(range(self.bits)), list(range(self.bits))[::-1])

    def send(self, value, bit):
        return lax.ppermute(value, self.axes, self.links[bit])

    def messages(self):
        found = []
        for order in self.orders:
            found.append([])
            for top in reversed(range(self.bits)):
                found[-1].append(
                    [
                        1 << order[top] | sum(1 << order[p] for p in range(top) if v >> p & 1)
                        for v in range(1 << top)
                    ]
                )
        return found


class Spread:
    def __init__(self, group, chain, rows):
        self.group, self.chain = group, chain
        self.held = {0: [rows]}
        self.later = None
        self.keys = [(1 << b, None) for b in range(group.bits)]
        self.flying = [group.send(rows, b) for b in range(group.bits)]

    def go_on(self, got):
        fresh = list(zip(self.keys, got))
        self.keys, self.flying = [], []
        for (k, h), block in fresh:
            if h is None:
                self.held[k] = [block]
            else:
                self.held.setdefault(k, [None, None])[h] = block
        for (k, h), block in fresh:
            for way, order in enumerate(self.group.orders):
                if h is not None and h != way:
                    continue
                half = block.shape[1] // 2
                top = max(i for i, bit in enumerate(order) if k >> bit & 1)
                for i in range(top + 1, len(order)):
                    part = block if h is not None else block[:, way * half : (way + 1) * half]
                    self.keys.append((k | 1 << order[i], way))
                    if self.later is not None:
                        self.later.append((part, order[i]))
                    else:
                        self.flying.append(self.group.send(part, order[i]))

    def resume(self):
        later, self.later = self.later, None
        parts = self.chain.join(*[part for part, _ in later])
        self.flying = [self.group.send(part, bit) for part, (_, bit) in zip(parts, later)]

    def blocks(self):
        while self.flying:
            self.chain.end(self)
        return [self.held[k] for k in range(self.group.size)]


class Fold:
    def __init__(self, group, chain, own, sent):
        self.group, self.chain = group, chain
        self.rows = own[0].shape[0]
        self.sent = [list(half) for half in sent]
        self.parts = [[half] for half in own]
        self.wave = 0
        self.start()

    def start(self):
        self.flying = [
            self.group.send(self.sent[h][self.wave], order[self.group.bits - 1 - self.wave])
            for h, order in enumerate(self.group.orders)
        ]

    def go_on(self, got):
        self.wave += 1
        self.flying = []
        for h, block in enumerate(got):
            self.parts[h].append(block)
            for wave in range(self.wave, self.group.bits):
                first = self.rows << (self.group.bits - 1 - wave)
                more = block[first : 2 * first].astype(F32)
                self.sent[h][wave] = (self.sent[h][wave].astype(F32) + more).astype(BF16)
        if self.wave < self.group.bits:
            now = self.chain.join(*[sent[self.wave] for sent in self.sent])
            for sent, value in zip(self.sent, now):
                sent[self.wave] = value
            self.start()

    def total(self):
        while self.flying:
            self.chain.end(self)
        return self.parts


class Weight:
    def __init__(self, pieces, rows, start, width):
        self.pieces, self.rows, self.start, self.width = pieces, rows, start, width
        self.model = len(pieces) * rows

    def tiles(self, tile):
        first = self.start // tile
        return [pl.BlockSpec((self.rows, tile), lambda j: (0, first + j))] * len(self.pieces)


def nn(left, right):
    return lax.dot_general(left, right, (((1,), (0,)), ((), ())), preferred_element_type=F32)


def nt(left, right):
    return lax.dot_general(left, right, (((1,), (1,)), ((), ())), preferred_element_type=F32)


def tn(left, right):
    return lax.dot_general(left, right, (((0,), (0,)), ((), ())), preferred_element_type=F32)


def whole(shape):
    return pl.BlockSpec(shape, lambda *_: (0,) * len(shape))


def place(line_ref, j, width):
    return pl.ds(pl.multiple_of(line_ref[j] * width, 128), width)


def cut(width, j):
    return slice(j * width, (j + 1) * width)


def scale_of(values):
    return lax.rsqrt(jnp.mean(values * values, axis=-1, keepdims=True) + EPS)


def fetch_blocks(counts, refs, held, sems, k, slot, wait):
    first = 0
    for i, count in enumerate(counts):
        copies = []
        half = held.shape[2] // count
        for h in range(count):
            target = held.at[slot, :, pl.ds(h * half, half)]
            copies.append(pltpu.make_async_copy(refs[first + h], target, sems.at[slot, h]))
        first += count

        @pl.when(k == i)
        def _():
            for copy in copies:
                copy.wait() if wait else copy.start()


def fetched(counts, refs, held, sems):
    k = pl.program_id(0)

    @pl.when(k == 0)
    def _():
        fetch_blocks(counts, refs, held, sems, k, 0, False)

    fetch_blocks(counts, refs, held, sems, k + 1, (k + 1) % 2, False)
    fetch_blocks(counts, refs, held, sems, k, k % 2, True)
    return held.at[k % 2]


def norm_body(blocks, counts, line_ref, gain_ref, *refs):
    out_ref, held, sems = refs[sum(counts) :]
    x_ref = fetched(counts, refs, held, sems)
    width = out_ref.shape[1] // blocks
    scale = scale_of(x_ref[...].astype(F32))
    for j in range(blocks):
        part = x_ref[:, place(line_ref, j, width)].astype(F32)
        gain = gain_ref[0:1, cut(width, j)]
        out_ref[:, cut(width, j)] = (part * scale * gain).astype(BF16)


def order_body(blocks, counts, line_ref, gain_ref, *refs):
    out_ref, held, sems = refs[sum(counts) :]
    x_ref = fetched(counts, refs, held, sems)
    width = out_ref.shape[1] // blocks
    for j in range(blocks):
        out_ref[:, cut(width, j)] = x_ref[:, place(line_ref, j, width)]


def ordered(chain, body, line, gains, held):
    counts = [len(block) for block in held]
    rows, model = held[0][0].shape
    n = len(held)
    return chain.call(
        functools.partial(body, line.shape[0], counts),
        (n,),
        [whole(gains.shape)] + [pl.BlockSpec(memory_space=pl.ANY)] * sum(counts),
        [pl.BlockSpec((rows, model), lambda k, *_: (k, 0))],
        [((n * rows, model), BF16)],
        flops=20 * n * rows * model,
        scratch=[pltpu.VMEM((2, rows, model), BF16), pltpu.SemaphoreType.DMA((2, 2))],
        prefetch=1,
        moved=4 * n * rows * model,
    )(line, gains, *[array for block in held for array in block])[0]


def added(refs, span):
    total = refs[0][span, :].astype(F32)
    for ref in refs[1:]:
        total += ref[span, :].astype(F32)
    return total


def middle_body(blocks, m, line_ref, x_ref, gain_ref, *refs):
    middle_ref, out_ref = refs[2 * m :]
    width = x_ref.shape[1] // blocks
    half = x_ref.shape[1] // 2
    span = slice(None)
    middle_ref[:, :half] = added(refs[:m], span)
    middle_ref[:, half:] = added(refs[m : 2 * m], span)
    for j in range(blocks):
        here = x_ref[:, place(line_ref, j, width)].astype(F32)
        middle_ref[:, cut(width, j)] += here
    middle = middle_ref[...]
    out_ref[...] = (middle * scale_of(middle) * gain_ref[1:2, :]).astype(BF16)


def result_body(blocks, m, line_ref, middle_ref, gain_ref, *refs):
    out_ref = refs[2 * m]
    width = middle_ref.shape[1] // blocks
    span = slice(None)
    total = middle_ref[...] + jnp.concatenate(
        [added(refs[:m], span), added(refs[m : 2 * m], span)], axis=1
    )
    for j in range(blocks):
        out_ref[:, place(line_ref, j, width)] = total[:, cut(width, j)].astype(BF16)


def second_back_body(blocks, m, line_ref, dy_ref, gain_ref, *refs):
    middle_ref, out_ref, low_ref = refs[2 * m :]
    width = dy_ref.shape[1] // blocks
    span = slice(None)
    grad = jnp.concatenate([added(refs[:m], span), added(refs[m : 2 * m], span)], axis=1)
    middle = middle_ref[...]
    scale = scale_of(middle)
    normed = middle * scale
    scaled = grad * gain_ref[1:2, :]
    out_ref[...] = scale * (scaled - normed * jnp.mean(scaled * normed, axis=-1, keepdims=True))
    for j in range(blocks):
        out_ref[:, cut(width, j)] += dy_ref[:, place(line_ref, j, width)].astype(F32)
    low_ref[...] = out_ref[...].astype(BF16)


def first_back_body(blocks, m, line_ref, x_ref, gain_ref, *refs):
    above_ref, out_ref = refs[2 * m :]
    width = x_ref.shape[1] // blocks
    span = slice(None)
    scale = scale_of(x_ref[...].astype(F32))
    normed = jnp.concatenate(
        [x_ref[:, place(line_ref, j, width)].astype(F32) for j in range(blocks)], axis=1
    ) * scale
    grad = jnp.concatenate([added(refs[:m], span), added(refs[m : 2 * m], span)], axis=1)
    scaled = grad * gain_ref[0:1, :]
    back = scale * (scaled - normed * jnp.mean(scaled * normed, axis=-1, keepdims=True))
    total = above_ref[...] + back
    for j in range(blocks):
        out_ref[:, place(line_ref, j, width)] = total[:, cut(width, j)]


def by_rows(chain, body, line, first, gains, parts, more, kinds):
    rows, model = first.shape
    half = model // 2
    tile = min(128, rows)
    row = pl.BlockSpec((tile, model), lambda i, *_: (i, 0))
    slim = pl.BlockSpec((tile, half), lambda i, *_: (i, 0))
    m = len(parts[0])
    return chain.call(
        functools.partial(body, line.shape[0], m),
        (rows // tile,),
        [row, whole(gains.shape)] + [slim] * (2 * m) + [row] * len(more),
        [row] * len(kinds),
        [((rows, model), kind) for kind in kinds],
        flops=20 * rows * model,
        prefetch=1,
        moved=rows * model * (2 * m + 4 * len(kinds)),
    )(line, first, gains, *parts[0], *parts[1], *more)


def finish_body(m, n, *refs):
    total = added(refs[:m], slice(None))
    weights, outs = refs[m : m + n], refs[m + n :]
    if not n:
        outs[0][...] = total.T
        return
    width = weights[0].shape[1]
    inner = jnp.zeros((total.shape[0], 1), F32)
    for i in range(n):
        part = total[:, cut(width, i)]
        outs[i][...] = part
        inner += jnp.sum(weights[i][...].astype(F32) * part, axis=1, keepdims=True)
    outs[n][...] = jnp.broadcast_to(inner, outs[n].shape)


def finish(chain, terms, weights=()):
    rows, columns = terms[0].shape
    tile = min(128, rows)
    row = pl.BlockSpec((tile, columns), lambda i: (i, 0))
    n = len(weights)
    if n:
        slim = pl.BlockSpec((tile, columns // n), lambda i: (i, 0))
        outs = [slim] * n + [pl.BlockSpec((tile, 128), lambda i: (i, 0))]
        shapes = [((rows, columns // n), F32)] * n + [((rows, 128), F32)]
    else:
        slim = None
        outs = [pl.BlockSpec((columns, tile), lambda i: (0, i))]
        shapes = [((columns, rows), F32)]
    results = chain.call(
        functools.partial(finish_body, len(terms), n),
        (rows // tile,),
        [row] * len(terms) + [slim] * n,
        outs,
        shapes,
        flops=4 * rows * columns,
        moved=rows * columns * 12,
    )(*terms, *weights)
    if n:
        results[n] = results[n][:, 0]
    return results


def rope_tables(place):
    half = HEAD_DIM // 2
    freq = THETA ** (-2.0 * jnp.arange(half, dtype=F32) / HEAD_DIM)
    angle = place.astype(F32)[:, None] * freq[None, :]
    cosine, sine = jnp.cos(angle), jnp.sin(angle)
    return (
        jnp.concatenate([cosine] * (PAIR // half), axis=1),
        jnp.concatenate([-sine, sine] * (PAIR // HEAD_DIM), axis=1),
    )


def turn(values):
    half = HEAD_DIM // 2
    width = values.shape[-1]
    lane = lax.broadcasted_iota(jnp.int32, values.shape, 1) % HEAD_DIM
    return jnp.where(
        lane < half, pltpu.roll(values, width - half, 1), pltpu.roll(values, half, 1)
    )


def joined(refs):
    return jnp.concatenate([r[...] for r in refs], axis=0)


def qkv_body(n, x_ref, cos_ref, sin_ref, *refs):
    weights, outs = refs[: 3 * n], refs[3 * n :]
    rows = x_ref.shape[0]
    tile = outs[0].shape[1]
    for i in range(3):
        weight = joined(weights[i * n : (i + 1) * n])
        for s in range(rows // SEQ):
            span = slice(s * SEQ, (s + 1) * SEQ)
            product = nn(x_ref[span, :], weight)
            if i == 2:
                outs[i][span, :] = product.astype(BF16)
                continue
            for t in range(tile // PAIR):
                here = product[:, t * PAIR : (t + 1) * PAIR]
                turned = here * cos_ref[...] + turn(here) * sin_ref[...]
                outs[i][span, t * PAIR : (t + 1) * PAIR] = turned.astype(BF16)


def project(chain, x, tables, query, key, value):
    rows, model = x.shape
    n, width = len(query.pieces), query.width
    tile = min(256, width)
    out = pl.BlockSpec((rows, tile), lambda j: (0, j))
    return chain.call(
        functools.partial(qkv_body, n),
        (width // tile,),
        [whole(x.shape), whole((SEQ, PAIR)), whole((SEQ, PAIR))]
        + query.tiles(tile)
        + key.tiles(tile)
        + value.tiles(tile),
        [out] * 3,
        [((rows, width), BF16)] * 3,
        flops=6 * rows * model * width,
        moved=2 * (rows * model + 3 * model * width + 3 * rows * width),
    )(x, *tables, *query.pieces, *key.pieces, *value.pieces)


def collect(counts, refs, held, sems):
    rows = held.shape[0] // len(counts)
    copies = []
    for k, count in enumerate(counts):
        half = held.shape[1] // count
        for h in range(count):
            target = held.at[pl.ds(k * rows, rows), pl.ds(h * half, half)]
            i = len(copies)
            copies.append(pltpu.make_async_copy(refs[i], target, sems.at[i]))
    for copy in copies:
        copy.start()
    for copy in copies:
        copy.wait()


def gate_body(n, counts, *refs):
    m = sum(counts)
    gate_w, up_w = refs[m : m + n], refs[m + n : m + 2 * n]
    hidden_ref, slope_ref, silu_ref, x_ref, sems = refs[m + 2 * n :]

    @pl.when(pl.program_id(0) == 0)
    def _():
        collect(counts, refs, x_ref, sems)

    gate_weight, up_weight = joined(gate_w), joined(up_w)
    for s in range(x_ref.shape[0] // SEQ):
        span = slice(s * SEQ, (s + 1) * SEQ)
        gate = nn(x_ref[span, :], gate_weight)
        up = nn(x_ref[span, :], up_weight)
        sigm = jax.nn.sigmoid(gate)
        silu = gate * sigm
        hidden_ref[span, :] = (silu * up).astype(BF16)
        silu_ref[span, :] = silu.astype(BF16)
        slope_ref[span, :] = (up * sigm * (1.0 + gate * (1.0 - sigm))).astype(BF16)


def collected(held):
    counts = [len(block) for block in held]
    rows, model = held[0][0].shape
    scratch = [
        pltpu.VMEM((len(held) * rows, model), BF16),
        pltpu.SemaphoreType.DMA((sum(counts),)),
    ]
    arrays = [array for block in held for array in block]
    return counts, arrays, [pl.BlockSpec(memory_space=pl.ANY)] * len(arrays), scratch


def gate_up(chain, held, gate, up):
    counts, arrays, specs, scratch = collected(held)
    rows, model = scratch[0].shape
    n, width = len(gate.pieces), gate.width
    tile = min(256, width)
    out = pl.BlockSpec((rows, tile), lambda j: (0, j))
    return chain.call(
        functools.partial(gate_body, n, counts),
        (width // tile,),
        specs + gate.tiles(tile) + up.tiles(tile),
        [out] * 3,
        [((rows, width), BF16)] * 3,
        flops=4 * rows * model * width,
        scratch=scratch,
        moved=2 * (rows * model + 2 * model * width + 3 * rows * width),
    )(*arrays, *gate.pieces, *up.pieces)


def hidden_back_body(n, g_ref, *refs):
    weight = joined(refs[:n])
    slope_ref, silu_ref, gate_ref, up_ref = refs[n:]
    for s in range(g_ref.shape[0] // SEQ):
        span = slice(s * SEQ, (s + 1) * SEQ)
        grad = nn(g_ref[span, :], weight)
        gate_ref[span, :] = (grad * slope_ref[span, :].astype(F32)).astype(BF16)
        up_ref[span, :] = (grad * silu_ref[span, :].astype(F32)).astype(BF16)


def hidden_back(chain, grads, down, slope, silu):
    rows, model = grads.shape
    n, width = len(down.pieces), down.width
    tile = min(256, width)
    out = pl.BlockSpec((rows, tile), lambda j: (0, j))
    return chain.call(
        functools.partial(hidden_back_body, n),
        (width // tile,),
        [whole(grads.shape)] + down.tiles(tile) + [out] * 2,
        [out] * 2,
        [((rows, width), BF16)] * 2,
        flops=2 * rows * model * width,
        moved=2 * (rows * model + model * width + 4 * rows * width),
    )(grads, *down.pieces, slope, silu)


def mixed_back_body(n, counts, *refs):
    m = sum(counts)
    out_ref, x_ref, sems = refs[m + n :]

    @pl.when(pl.program_id(0) == 0)
    def _():
        collect(counts, refs, x_ref, sems)

    out_ref[...] = nn(x_ref[...], joined(refs[m : m + n])).astype(BF16)


def mixed_back(chain, held, out):
    counts, arrays, specs, scratch = collected(held)
    rows, model = scratch[0].shape
    n, width = len(out.pieces), out.width
    tile = min(256, width)
    return chain.call(
        functools.partial(mixed_back_body, n, counts),
        (width // tile,),
        specs + out.tiles(tile),
        [pl.BlockSpec((rows, tile), lambda j: (0, j))],
        [((rows, width), BF16)],
        flops=2 * rows * model * width,
        scratch=scratch,
        moved=2 * (rows * model + model * width + rows * width),
    )(*arrays, *out.pieces)[0]


def trans_body(n, starts, targets, *refs):
    parts, blocks = len(starts), len(targets[0])
    lefts = refs[:parts]
    pieces = refs[parts : parts * (n + 1)]
    outs = refs[parts * (n + 1) : -4]
    held, ready, sems, out_sems = refs[-4:]
    j = pl.program_id(0)
    depth, width = held.shape[2:]
    rows = ready.shape[1] // blocks

    def copy(i, p, slot):
        source = pieces[p * n + i].at[pl.ds(0, depth), pl.ds(starts[p], width)]
        return pltpu.make_async_copy(source, held.at[slot, p], sems.at[slot, p])

    def fetch(step, slot):
        for i in range(n):

            @pl.when(step == i)
            def _():
                for p in range(parts):
                    copy(i, p, slot).start()

    def leave(slot, k, array, first, column):
        target = outs[array].at[pl.ds(first, rows), pl.ds(column, depth)]
        source = ready.at[slot, pl.ds(k * rows, rows), :]
        return pltpu.make_async_copy(source, target, out_sems.at[slot, k])

    def left(slot):
        for k in range(blocks):
            leave(slot, k, 0, 0, 0).wait()

    @pl.when(j == 0)
    def _():
        fetch(j, 0)

    @pl.when(j + 1 < n)
    def _():
        fetch(j + 1, (j + 1) % 2)

    slot = j % 2
    for p in range(parts):
        copy(0, p, slot).wait()

    @pl.when(j >= 2)
    def _():
        left(slot)

    for s in range(blocks * rows // SEQ):
        span = slice(s * SEQ, (s + 1) * SEQ)
        total = nt(lefts[0][span, :], held[slot, 0])
        for p in range(1, parts):
            total += nt(lefts[p][span, :], held[slot, p])
        ready[slot, span, :] = total.astype(BF16)
    column = pl.multiple_of(j % (n // 2) * depth, 128)
    for h in range(2):

        @pl.when((j >= n // 2) == (h == 1))
        def _():
            for k, (array, first) in enumerate(targets[h]):
                leave(slot, k, array, first, column).start()

    @pl.when(j == n - 1)
    def _():
        left(1 - slot)
        left(slot)


def times_trans(chain, parts, group):
    weights = [weight for _, weight in parts]
    n, depth, width = len(weights[0].pieces), weights[0].rows, weights[0].width
    rows = parts[0][0].shape[0]
    half = weights[0].model // 2
    size = rows // group.size
    messages = group.messages()
    shapes = [((size, half), BF16)] * 2
    targets = [{0: (0, 0)}, {0: (1, 0)}]
    for h in range(2):
        for keys in messages[h]:
            for i, k in enumerate(keys):
                targets[h][k] = (len(shapes), i * size)
            shapes.append(((len(keys) * size, half), BF16))
    targets = [[t[k] for k in range(group.size)] for t in targets]
    anywhere = pl.BlockSpec(memory_space=pl.ANY)
    outs = chain.call(
        functools.partial(trans_body, n, [weight.start for weight in weights], targets),
        (n,),
        [whole((rows, width))] * len(parts) + [anywhere] * (n * len(parts)),
        [anywhere] * len(shapes),
        shapes,
        flops=4 * rows * half * width * len(parts),
        scratch=[
            pltpu.VMEM((2, len(parts), depth, width), BF16),
            pltpu.VMEM((2, rows, depth), BF16),
            pltpu.SemaphoreType.DMA((2, len(parts))),
            pltpu.SemaphoreType.DMA((2, group.size)),
        ],
        moved=2 * (2 * rows * half + len(parts) * (rows + 2 * half) * width),
    )(*[left for left, _ in parts], *[piece for weight in weights for piece in weight.pieces])
    m = group.bits
    return outs[:2], [outs[2 : 2 + m], outs[2 + m :]]


def grad_body(parts, got, blocks, steps, *refs):
    lefts, refs = refs[:blocks], refs[blocks:]
    rights, refs = refs[:parts], refs[parts:]
    got_ref = refs[0] if got else None
    outs, turned = refs[got:-1], refs[-1]
    j = pl.program_id(0)

    @pl.when(j == 0)
    def _():
        rows = turned.shape[1] // blocks
        for k in range(blocks):
            turned[:, cut(rows, k)] = lefts[k][...].T

    for i in range(parts):

        @pl.when((j >= i * steps) & (j < (i + 1) * steps))
        def _():
            total = nn(turned[...], rights[i][...])
            if got:
                total += got_ref[...].astype(F32)
            total = total.astype(BF16)
            first = 0
            for out_ref in outs:
                count = out_ref.shape[0]
                out_ref[...] = total[first : first + count]
                first += count


def weight_grads(chain, left, which, rights, got=None, bits=0):
    rows, width = rights[0].shape
    parts = len(rights)
    tile = min(512, width)
    steps = width // tile
    if isinstance(left, list):
        lefts = [block[0] if len(block) == 1 else block[which] for block in left]
        half = left[0][0].shape[1] // 2
        places = [which if len(block) == 1 else 0 for block in left]
    else:
        lefts, places, half = [left], [which], left.shape[1] // 2
    blocks = len(lefts)
    ins = [
        pl.BlockSpec((rows // blocks, half), functools.partial(lambda at, j: (0, at), at))
        for at in places
    ]
    for i in range(parts):
        ins.append(
            pl.BlockSpec(
                (rows, tile),
                functools.partial(
                    lambda first, j: (0, jnp.clip(j - first, 0, steps - 1)), i * steps
                ),
            )
        )
    column = lambda j: (0, j)
    more = [] if got is None else [got]
    sizes = [half >> bits]
    for p in range(bits):
        sizes += [sizes[0], ((1 << p) - 1) * sizes[0]] if p else [sizes[0]]
    return chain.call(
        functools.partial(grad_body, parts, len(more), blocks, steps),
        (parts * steps,),
        ins + [pl.BlockSpec((half, tile), column)] * len(more),
        [pl.BlockSpec((size, tile), column) for size in sizes],
        [((size, parts * width), BF16) for size in sizes],
        flops=2 * rows * half * width * parts,
        scratch=[pltpu.VMEM((half, rows), BF16)],
        moved=2 * (rows * half + parts * (rows + half) * width),
    )(*lefts, *rights, *more)


def causal(scores):
    past = scores.shape[0] - HALF_SEQ
    key = lax.broadcasted_iota(jnp.int32, (HALF_SEQ, HALF_SEQ), 0)
    query = lax.broadcasted_iota(jnp.int32, (HALF_SEQ, HALF_SEQ), 1)
    last = jnp.where(key <= query, scores[past:], -1e30)
    return last if past == 0 else jnp.concatenate([scores[:past], last], axis=0)


def head_of(h):
    return slice(h * HEAD_DIM, (h + 1) * HEAD_DIM)


def span_of(b):
    return slice(b * HALF_SEQ, (b + 1) * HALF_SEQ)


def in_place(shift_ref, ref, count):
    rows = SEQ // count
    spans = [pl.ds(pl.multiple_of((i ^ shift_ref[0]) * rows, rows), rows) for i in range(count)]
    return jnp.concatenate([ref[span, :] for span in spans], axis=0)


def put_back(shift_ref, ref, count, values):
    rows = SEQ // count
    for i in range(count):
        ref[pl.ds(pl.multiple_of((i ^ shift_ref[0]) * rows, rows), rows), :] = values[cut(rows, i)]


def attend_body(count, shift_ref, q_ref, k_ref, v_ref, out_ref, sum_ref):
    queries, keys = in_place(shift_ref, q_ref, count), in_place(shift_ref, k_ref, count)
    values = in_place(shift_ref, v_ref, count).astype(F32).T.astype(BF16)
    heads = []
    for h in range(2):
        blocks = []
        for b in range(2):
            reach = (b + 1) * HALF_SEQ
            query = queries[span_of(b), head_of(h)] * BF16(FACTOR)
            scores = causal(nt(keys[:reach, head_of(h)], query))
            top = jnp.max(scores, axis=0, keepdims=True)
            expo = jnp.exp(scores - top)
            total = jnp.sum(expo, axis=0, keepdims=True)
            mixed = nn(values[head_of(h), :reach], expo.astype(BF16))
            blocks.append(mixed * (1.0 / total))
            sum_ref[0, 0, h : h + 1, span_of(b)] = top + jnp.log(total)
        heads.append(jnp.concatenate(blocks, axis=1))
    put_back(shift_ref, out_ref, count, jnp.concatenate(heads, axis=0).T.astype(BF16))


def attend(chain, shift, count, query, key, value):
    rows, width = query.shape
    seqs, pairs = rows // SEQ, width // PAIR
    tile = pl.BlockSpec((SEQ, PAIR), lambda s, p, _: (s, p))
    return chain.call(
        functools.partial(attend_body, count),
        (seqs, pairs),
        [tile] * 3,
        [tile, pl.BlockSpec((1, 1, 2, SEQ), lambda s, p, _: (s, p, 0, 0))],
        [((rows, width), BF16), ((seqs, pairs, 2, SEQ), F32)],
        flops=16 * rows * width * SEQ,
        prefetch=1,
        moved=8 * rows * width,
    )(shift, query, key, value)


def attend_back_body(
    count, shift_ref, q_ref, k_ref, v_ref, g_ref, sum_ref, cos_ref, sin_ref, dq_ref, dk_ref, dv_ref
):
    queries, keys, values, grads = (
        in_place(shift_ref, ref, count) for ref in (q_ref, k_ref, v_ref, g_ref)
    )
    turned = keys.astype(F32).T.astype(BF16)
    dq_heads, dk_heads, dv_heads = [], [], []
    for h in range(2):
        dq, dk, dv = [], [], []
        for b in range(2):
            reach = (b + 1) * HALF_SEQ
            query = queries[span_of(b), head_of(h)]
            grad = grads[span_of(b), head_of(h)]
            scores = causal(nt(keys[:reach, head_of(h)], query * BF16(FACTOR)))
            probs = jnp.exp(scores - sum_ref[0, 0, h : h + 1, span_of(b)])
            probs_grad = nt(values[:reach, head_of(h)], grad)
            inner = jnp.sum(probs * probs_grad, axis=0, keepdims=True)
            score_grad = (probs * (probs_grad - inner)).astype(BF16)
            dv.append(nn(probs.astype(BF16), grad))
            dk.append(nn(score_grad, query))
            dq.append(nn(turned[head_of(h), :reach], score_grad))
        for parts, heads in ((dk, dk_heads), (dv, dv_heads)):
            heads.append(
                jnp.concatenate([parts[1][:HALF_SEQ] + parts[0], parts[1][HALF_SEQ:]], axis=0)
            )
        dq_heads.append(jnp.concatenate(dq, axis=1))
    dq = jnp.concatenate(dq_heads, axis=0).T * FACTOR
    dk = jnp.concatenate(dk_heads, axis=1) * FACTOR
    dv = jnp.concatenate(dv_heads, axis=1).astype(BF16)
    cosine, sine = cos_ref[...], sin_ref[...]
    put_back(shift_ref, dq_ref, count, (dq * cosine - turn(dq) * sine).astype(BF16))
    put_back(shift_ref, dk_ref, count, (dk * cosine - turn(dk) * sine).astype(BF16))
    put_back(shift_ref, dv_ref, count, dv)


def attend_back(chain, shift, count, query, key, value, grad, logsum, tables):
    rows, width = query.shape
    seqs, pairs = rows // SEQ, width // PAIR
    tile = pl.BlockSpec((SEQ, PAIR), lambda s, p, _: (s, p))
    return chain.call(
        functools.partial(attend_back_body, count),
        (seqs, pairs),
        [tile] * 4
        + [pl.BlockSpec((1, 1, 2, SEQ), lambda s, p, _: (s, p, 0, 0))]
        + [whole((SEQ, PAIR))] * 2,
        [tile] * 3,
        [((rows, width), BF16)] * 3,
        flops=40 * rows * width * SEQ,
        prefetch=1,
        moved=14 * rows * width,
    )(shift, query, key, value, grad, logsum, *tables)


def local(
    chips,
    group,
    tokens,
    attn_gain,
    query_weight,
    key_weight,
    value_weight,
    output_weight,
    ffn_gain,
    gate_weight,
    up_weight,
    down_weight,
    cotangent,
):
    line = jnp.asarray(chips.table)[lax.axis_index("dp")]
    rows, model = tokens.shape
    count = SEQ // rows
    shift = lax.axis_index("tensor") % count
    row = jnp.arange(SEQ, dtype=jnp.int32)
    places = rope_tables(row)
    tables = rope_tables((row // rows ^ shift) * rows + row % rows)
    shift = jnp.reshape(shift, (1,)).astype(jnp.int32)
    early = (*places, *tables, line, shift)
    depth, own = query_weight.shape
    hidden_units = gate_weight.shape[1]
    chain = Chain()

    def gather(piece):
        return Gather(chips, chain, chain.join(piece)[0])

    def spread_of(values):
        return Spread(group, chain, chain.join(values)[0])

    def fold_of(part):
        own_part, sent = part
        sent = chain.join(*sent[0], *sent[1])
        return Fold(group, chain, own_part, [sent[: group.bits], sent[group.bits :]])

    def grads_of(left, rights):
        got = [None]
        chain.ask(weight_grads(chain, left, 1, rights)[0], got, 0, chips.other)

        def mine(apart=False):
            if got[0] is None:
                chain.flush()
            blocks = weight_grads(chain, left, 0, rights, got[0], chips.bits)
            return Sums(chips, chain, blocks, apart)

        return mine

    extra = jnp.concatenate([attn_gain, ffn_gain, jnp.zeros((4 * own - 2 * depth,), BF16)])
    attn = jnp.concatenate([query_weight, key_weight, value_weight, output_weight.T], axis=1)
    attn = gather(jnp.concatenate([attn, jnp.broadcast_to(extra, (16, 4 * own))], axis=0))
    spread = spread_of(tokens)
    grads_spread = spread_of(cotangent)
    grads_spread.later = []
    down_turned, *early = chain.join(down_weight.T, *early)
    places, tables, line, shift = early[:2], early[2:4], early[4], early[5]
    chain.end(attn, spread, grads_spread)
    chain.end(attn, spread)
    all_tokens = spread.blocks()
    attn = attn.pieces()
    pair = gather(jnp.concatenate([gate_weight, up_weight], axis=1))
    w_query, w_key, w_value, w_output = [Weight(attn, depth, i * own, own) for i in range(4)]
    gains = jnp.concatenate(
        [piece[depth : depth + 1, : 2 * depth].reshape(2, depth) for piece in attn], axis=1
    ).astype(F32)

    group_one = ordered(chain, norm_body, line, gains, all_tokens)
    grads_spread.resume()
    query, key, value = project(chain, group_one, tables, w_query, w_key, w_value)
    mixed, logsum = attend(chain, shift, count, query, key, value)
    out_part = times_trans(chain, [(mixed, w_output)], group)
    fold = fold_of(out_part)
    chain.end(fold, pair, grads_spread)
    grad_rows = ordered(chain, order_body, line, gains, grads_spread.blocks())
    chain.end(fold)
    attended = fold.total()
    middle, second = by_rows(
        chain, middle_body, line, tokens, gains, attended, [], [F32, BF16]
    )
    spread = spread_of(second)
    chain.end(spread, pair)
    pair = pair.pieces()
    down = gather(down_turned)
    chain.end(spread)
    group_two = spread.blocks()
    w_gate = Weight(pair, depth, 0, hidden_units)
    w_up = Weight(pair, depth, hidden_units, hidden_units)
    hidden, slope, silu = gate_up(chain, group_two, w_gate, w_up)

    mine = grads_of(grad_rows, [hidden])
    chain.end(down)
    chain.flush()
    down_sum = mine()
    w_down = Weight(down.pieces(), depth, 0, hidden_units)
    gate_grad, up_grad = hidden_back(chain, grad_rows, w_down, slope, silu)
    mine_gate = grads_of(group_two, [gate_grad])
    chain.end(down_sum)
    second_part = times_trans(chain, [(gate_grad, w_gate), (up_grad, w_up)], group)
    mine_up = grads_of(group_two, [up_grad])
    gate_sum = mine_gate()
    chain.end(down_sum)
    fold = fold_of(second_part)
    up_sum = mine_up()
    chain.end(gate_sum, fold)
    result_part = times_trans(chain, [(hidden, w_down)], group)
    chain.end(fold)
    second_grad = fold.total()
    middle_grad, low_grad = by_rows(
        chain, second_back_body, line, cotangent, gains, second_grad, [middle], [F32, BF16]
    )
    spread = spread_of(low_grad)
    chain.end(up_sum)
    (down_sum,) = finish(chain, down_sum.terms())
    chain.end(spread)
    attn_grads = spread.blocks()

    mixed_grad = mixed_back(chain, attn_grads, w_output)
    mine_out = grads_of(attn_grads, [mixed])
    chain.end(gate_sum)
    fold = fold_of(result_part)
    query_back, key_back, value_back = attend_back(
        chain, shift, count, query, key, value, mixed_grad, logsum, places
    )
    first_part = times_trans(
        chain, [(query_back, w_query), (key_back, w_key), (value_back, w_value)], group
    )
    out_sum = mine_out()
    mine_qkv = grads_of(group_one, [query_back, key_back, value_back])
    chain.end(up_sum, out_sum, fold)
    qkv_sum = mine_qkv()
    chain.end(out_sum, fold)
    result_part = fold.total()
    fold = fold_of(first_part)
    (layer_out,) = by_rows(chain, result_body, line, middle, gains, result_part, [], [BF16])
    gate_sum, gate_inner = finish(chain, gate_sum.terms(), [gate_weight])
    chain.end(qkv_sum, fold)
    up_sum, up_inner = finish(chain, up_sum.terms(), [up_weight])
    chain.end(fold)
    first_grad = fold.total()
    (input_grad,) = by_rows(
        chain, first_back_body, line, tokens, gains, first_grad, [middle_grad], [F32]
    )
    (out_sum,) = finish(chain, out_sum.terms())
    chain.end(qkv_sum)
    query_sum, key_sum, value_sum, qkv_inner = finish(
        chain, qkv_sum.terms(), [query_weight, key_weight, value_weight]
    )
    gain_one_total, gain_two_total = lax.psum(
        (
            qkv_inner / attn_gain.astype(F32),
            (gate_inner + up_inner) / ffn_gain.astype(F32),
        ),
        "tensor",
    )
    return (
        layer_out,
        input_grad,
        gain_one_total,
        query_sum,
        key_sum,
        value_sum,
        out_sum,
        gain_two_total,
        gate_sum,
        up_sum,
        down_sum,
    )


def solution(mesh):
    in_specs = (
        P(("dp", "tensor"), None),
        P("dp"),
        P("dp", "tensor"),
        P("dp", "tensor"),
        P("dp", "tensor"),
        P("tensor", "dp"),
        P("dp"),
        P("dp", "tensor"),
        P("dp", "tensor"),
        P("tensor", "dp"),
        P(("dp", "tensor"), None),
    )
    out_specs = (
        P(("dp", "tensor"), None),
        P(("dp", "tensor"), None),
        P("dp"),
        P("dp", "tensor"),
        P("dp", "tensor"),
        P("dp", "tensor"),
        P("tensor", "dp"),
        P("dp"),
        P("dp", "tensor"),
        P("dp", "tensor"),
        P("tensor", "dp"),
    )
    chips = Chips(mesh.shape["dp"])
    size = mesh.shape["tensor"]
    links = [[(i, i ^ 1 << b) for i in range(size)] for b in range(size.bit_length() - 1)]
    group = Group(links, "tensor")

    def run(*arrays):
        return local(chips, group, *arrays)

    return jax.shard_map(run, mesh=mesh, in_specs=in_specs, out_specs=out_specs, check_vma=False)
```

```python
import functools

import jax
import jax.numpy as jnp
import numpy as np
from jax import lax
from jax.experimental import pallas as pl
from jax.experimental.pallas import tpu as pltpu
from jax.sharding import PartitionSpec as P

HEAD_DIM = 64
SEQ = 512
EPS = 1e-05
THETA = 130000.0
BF16 = jnp.bfloat16
F32 = jnp.float32
FACTOR = HEAD_DIM**-0.5
PAIR = 2 * HEAD_DIM
HALF_SEQ = SEQ // 2
VMEM_LIMIT = 58 << 20
COST_SHARE = 4096


class Chain:
    def __init__(self):
        self.token = jnp.zeros((8, 128), F32)
        self.swaps, self.asked = [], []

    def join(self, *values):
        *values, self.token = lax.optimization_barrier((*values, self.token))
        return values

    def gate(self, *values):
        swaps, self.swaps = self.swaps, []
        asked, self.asked = self.asked, []
        joined = self.join(
            *values, *[held[i] for held, i in swaps], *[source for source, _, _, _ in asked]
        )
        for (held, i), value in zip(swaps, joined[len(values) :]):
            held[i] = value
        for (_, held, i, swap), value in zip(asked, joined[len(values) + len(swaps) :]):
            held[i] = swap(value)
            self.swaps.append((held, i))
        return joined[: len(values)]

    def end(self, *transfers):
        counts = [len(t.flying) for t in transfers]
        got = self.gate(*[value for t in transfers for value in t.flying])
        for t, count in zip(transfers, counts):
            if count:
                t.go_on(got[:count])
            got = got[count:]

    def ask(self, source, held, i, swap):
        self.asked.append((source, held, i, swap))

    def flush(self):
        for source, held, i, swap in self.asked:
            held[i] = swap(source)
        self.asked = []

    def call(self, body, grid, ins, outs, shapes, flops, scratch=(), prefetch=0, moved=0):
        first = prefetch + len(ins)
        second = first + 1 + len(outs)
        anywhere = pl.BlockSpec(memory_space=pl.ANY)

        def wrapped(*refs):
            body(*refs[:first], *refs[first + 1 : second], *refs[second + 1 :])

        run = pl.pallas_call(
            wrapped,
            grid_spec=pltpu.PrefetchScalarGridSpec(
                num_scalar_prefetch=prefetch,
                grid=grid,
                in_specs=[*ins, anywhere],
                out_specs=[*outs, anywhere],
                scratch_shapes=list(scratch),
            ),
            out_shape=[jax.ShapeDtypeStruct(s, t) for s, t in [*shapes, ((8, 128), F32)]],
            compiler_params=pltpu.CompilerParams(
                vmem_limit_bytes=VMEM_LIMIT, dimension_semantics=("arbitrary",) * len(grid)
            ),
            cost_estimate=pl.CostEstimate(
                flops=flops // COST_SHARE, bytes_accessed=moved // COST_SHARE, transcendentals=0
            ),
        )

        def with_token(*args):
            *results, self.token = run(*args, self.token)
            return results

        return with_token


class Chips:
    def __init__(self, size):
        self.bits = (size // 2).bit_length() - 1
        self.size = size
        self.swap = [(i, i ^ 1) for i in range(size)]
        self.links = [
            [(i, i ^ 2 << self.bits - 1 - p) for i in range(size)] for p in range(self.bits)
        ]
        flips = [
            sum(1 << self.bits - 1 - p for p in range(self.bits) if v >> p & 1)
            for v in range(1 << self.bits)
        ]
        table = [[i ^ 2 * f for f in flips] + [i ^ 2 * f ^ 1 for f in flips] for i in range(size)]
        self.table = np.array(table, np.int32)

    def send(self, value, p):
        return lax.ppermute(value, "dp", self.links[p])

    def other(self, value):
        return lax.ppermute(value, "dp", self.swap)


class Gather:
    def __init__(self, chips, chain, piece):
        self.chips, self.chain = chips, chain
        self.own = [piece] + [None] * (2**chips.bits - 1)
        self.others = list(self.own)
        self.ask(0)
        self.keys = [1 << p for p in range(chips.bits)]
        self.flying = [chips.send(piece, p) for p in range(chips.bits)]

    def ask(self, v):
        self.chain.ask(self.own[v], self.others, v, self.chips.other)

    def go_on(self, got):
        keys, self.keys, self.flying = self.keys, [], []
        for v, piece in zip(keys, got):
            self.own[v] = piece
            for p in range(v.bit_length(), self.chips.bits):
                self.keys.append(v | 1 << p)
                self.flying.append(self.chips.send(piece, p))
        for v in keys:
            self.ask(v)

    def pieces(self):
        while self.flying:
            self.chain.end(self)
        self.chain.flush()
        return self.own + self.others


class Sums:
    def __init__(self, chips, chain, mine, apart=False, hold=False):
        self.chips, self.chain, self.apart, self.hold = chips, chain, apart, hold
        self.todo = []
        self.parts = [mine[0]]
        mine = list(mine[1:])
        self.direct, self.passed = [], []
        for p in range(chips.bits):
            self.direct.append(mine.pop(0))
            self.passed.append(mine.pop(0) if p else None)
        self.p = chips.bits - 1
        self.kinds = [self.p]
        self.flying = [chips.send(self.passed[self.p], self.p)]

    def go_on(self, got):
        rows = self.parts[0].shape[0]
        kinds, self.kinds, self.flying = self.kinds, [], []
        for kind, block in zip(kinds, got):
            if kind is None:
                self.parts.append(block)
                continue
            add = lambda held, first: (
                held.astype(F32) + block[first * rows : first * rows + held.shape[0]].astype(F32)
            ).astype(BF16)
            for q in range(kind):
                self.direct[q] = add(self.direct[q], (1 << q) - 1)
                if q:
                    self.passed[q] = add(self.passed[q], 1 << q)
        p, self.p = self.p, self.p - 1
        if p > 0:
            self.todo.append((None, self.direct[p], p))
        if p > 1:
            self.todo.append((p - 1, self.passed[p - 1], p - 1))
        if p == (0 if self.apart else 1):
            self.todo.append((None, self.direct[0], 0))
        if not self.hold:
            self.resume()

    def resume(self):
        todo, self.todo = self.todo, []
        values = self.chain.join(*[value for _, value, _ in todo])
        for (kind, _, p), value in zip(todo, values):
            self.kinds.append(kind)
            self.flying.append(self.chips.send(value, p))

    def terms(self):
        while self.flying or self.todo:
            if self.todo:
                self.resume()
            self.chain.end(self)
        return self.parts


class Group:
    def __init__(self, links, axes):
        self.links, self.axes = links, axes
        self.bits = len(links)
        self.size = 1 << self.bits
        self.orders = (list(range(self.bits)), list(range(self.bits))[::-1])

    def send(self, value, bit):
        return lax.ppermute(value, self.axes, self.links[bit])

    def messages(self):
        found = []
        for order in self.orders:
            found.append([])
            for top in reversed(range(self.bits)):
                found[-1].append(
                    [
                        1 << order[top] | sum(1 << order[p] for p in range(top) if v >> p & 1)
                        for v in range(1 << top)
                    ]
                )
        return found


class Spread:
    def __init__(self, group, chain, rows):
        self.group, self.chain = group, chain
        self.held = {0: [rows]}
        self.later = None
        self.keys = [(1 << b, None) for b in range(group.bits)]
        self.flying = [group.send(rows, b) for b in range(group.bits)]

    def go_on(self, got):
        fresh = list(zip(self.keys, got))
        self.keys, self.flying = [], []
        for (k, h), block in fresh:
            if h is None:
                self.held[k] = [block]
            else:
                self.held.setdefault(k, [None, None])[h] = block
        for (k, h), block in fresh:
            for way, order in enumerate(self.group.orders):
                if h is not None and h != way:
                    continue
                half = block.shape[1] // 2
                top = max(i for i, bit in enumerate(order) if k >> bit & 1)
                for i in range(top + 1, len(order)):
                    part = block if h is not None else block[:, way * half : (way + 1) * half]
                    self.keys.append((k | 1 << order[i], way))
                    if self.later is not None:
                        self.later.append((part, order[i]))
                    else:
                        self.flying.append(self.group.send(part, order[i]))

        if self.later:
            parts = self.chain.join(*[part for part, _ in self.later])
            self.later = [(part, bit) for part, (_, bit) in zip(parts, self.later)]

    def resume(self):
        later, self.later = self.later, None
        parts = self.chain.join(*[part for part, _ in later])
        self.flying = [self.group.send(part, bit) for part, (_, bit) in zip(parts, later)]

    def blocks(self):
        while self.flying:
            self.chain.end(self)
        return [self.held[k] for k in range(self.group.size)]


class Fold:
    def __init__(self, group, chain, own, sent):
        self.group, self.chain = group, chain
        self.rows = own[0].shape[0]
        self.sent = [list(half) for half in sent]
        self.parts = [[half] for half in own]
        self.wave = 0
        self.start()

    def start(self):
        self.flying = [
            self.group.send(self.sent[h][self.wave], order[self.group.bits - 1 - self.wave])
            for h, order in enumerate(self.group.orders)
        ]

    def go_on(self, got):
        self.wave += 1
        self.flying = []
        for h, block in enumerate(got):
            self.parts[h].append(block)
            for wave in range(self.wave, self.group.bits):
                first = self.rows << (self.group.bits - 1 - wave)
                more = block[first : 2 * first].astype(F32)
                self.sent[h][wave] = (self.sent[h][wave].astype(F32) + more).astype(BF16)
        if self.wave < self.group.bits:
            now = self.chain.join(*[sent[self.wave] for sent in self.sent])
            for sent, value in zip(self.sent, now):
                sent[self.wave] = value
            self.start()

    def total(self):
        while self.flying:
            self.chain.end(self)
        return self.parts


class Weight:
    def __init__(self, pieces, rows, start, width):
        self.pieces, self.rows, self.start, self.width = pieces, rows, start, width
        self.model = len(pieces) * rows

    def tiles(self, tile):
        first = self.start // tile
        return [pl.BlockSpec((self.rows, tile), lambda j: (0, first + j))] * len(self.pieces)


def nn(left, right):
    return lax.dot_general(left, right, (((1,), (0,)), ((), ())), preferred_element_type=F32)


def nt(left, right):
    return lax.dot_general(left, right, (((1,), (1,)), ((), ())), preferred_element_type=F32)


def tn(left, right):
    return lax.dot_general(left, right, (((0,), (0,)), ((), ())), preferred_element_type=F32)


def whole(shape):
    return pl.BlockSpec(shape, lambda *_: (0,) * len(shape))


def place(line_ref, j, width):
    return pl.ds(pl.multiple_of(line_ref[j] * width, 128), width)


def cut(width, j):
    return slice(j * width, (j + 1) * width)


def scale_of(values):
    return lax.rsqrt(jnp.mean(values * values, axis=-1, keepdims=True) + EPS)


def fetch_blocks(counts, refs, held, sems, k, slot, wait):
    first = 0
    for i, count in enumerate(counts):
        copies = []
        half = held.shape[2] // count
        for h in range(count):
            target = held.at[slot, :, pl.ds(h * half, half)]
            copies.append(pltpu.make_async_copy(refs[first + h], target, sems.at[slot, h]))
        first += count

        @pl.when(k == i)
        def _():
            for copy in copies:
                copy.wait() if wait else copy.start()


def fetched(counts, refs, held, sems):
    k = pl.program_id(0)

    @pl.when(k == 0)
    def _():
        fetch_blocks(counts, refs, held, sems, k, 0, False)

    fetch_blocks(counts, refs, held, sems, k + 1, (k + 1) % 2, False)
    fetch_blocks(counts, refs, held, sems, k, k % 2, True)
    return held.at[k % 2]


def norm_body(blocks, counts, line_ref, gain_ref, *refs):
    out_ref, held, sems = refs[sum(counts) :]
    x_ref = fetched(counts, refs, held, sems)
    width = out_ref.shape[1] // blocks
    scale = scale_of(x_ref[...].astype(F32))
    for j in range(blocks):
        part = x_ref[:, place(line_ref, j, width)].astype(F32)
        gain = gain_ref[0:1, cut(width, j)]
        out_ref[:, cut(width, j)] = (part * scale * gain).astype(BF16)


def order_body(blocks, counts, line_ref, gain_ref, *refs):
    out_ref, held, sems = refs[sum(counts) :]
    x_ref = fetched(counts, refs, held, sems)
    width = out_ref.shape[1] // blocks
    for j in range(blocks):
        out_ref[:, cut(width, j)] = x_ref[:, place(line_ref, j, width)]


def ordered(chain, body, line, gains, held):
    counts = [len(block) for block in held]
    rows, model = held[0][0].shape
    n = len(held)
    return chain.call(
        functools.partial(body, line.shape[0], counts),
        (n,),
        [whole(gains.shape)] + [pl.BlockSpec(memory_space=pl.ANY)] * sum(counts),
        [pl.BlockSpec((rows, model), lambda k, *_: (k, 0))],
        [((n * rows, model), BF16)],
        flops=20 * n * rows * model,
        scratch=[pltpu.VMEM((2, rows, model), BF16), pltpu.SemaphoreType.DMA((2, 2))],
        prefetch=1,
        moved=4 * n * rows * model,
    )(line, gains, *[array for block in held for array in block])[0]


def added(refs, span):
    total = refs[0][span, :].astype(F32)
    for ref in refs[1:]:
        total += ref[span, :].astype(F32)
    return total


def middle_body(blocks, m, line_ref, x_ref, gain_ref, *refs):
    middle_ref, out_ref = refs[2 * m :]
    width = x_ref.shape[1] // blocks
    half = x_ref.shape[1] // 2
    span = slice(None)
    middle_ref[:, :half] = added(refs[:m], span)
    middle_ref[:, half:] = added(refs[m : 2 * m], span)
    for j in range(blocks):
        here = x_ref[:, place(line_ref, j, width)].astype(F32)
        middle_ref[:, cut(width, j)] += here
    middle = middle_ref[...]
    out_ref[...] = (middle * scale_of(middle) * gain_ref[1:2, :]).astype(BF16)


def result_body(blocks, m, line_ref, middle_ref, gain_ref, *refs):
    out_ref = refs[2 * m]
    width = middle_ref.shape[1] // blocks
    span = slice(None)
    total = middle_ref[...] + jnp.concatenate(
        [added(refs[:m], span), added(refs[m : 2 * m], span)], axis=1
    )
    for j in range(blocks):
        out_ref[:, place(line_ref, j, width)] = total[:, cut(width, j)].astype(BF16)


def second_back_body(blocks, m, line_ref, dy_ref, gain_ref, *refs):
    middle_ref, out_ref, low_ref = refs[2 * m :]
    width = dy_ref.shape[1] // blocks
    span = slice(None)
    grad = jnp.concatenate([added(refs[:m], span), added(refs[m : 2 * m], span)], axis=1)
    middle = middle_ref[...]
    scale = scale_of(middle)
    normed = middle * scale
    scaled = grad * gain_ref[1:2, :]
    out_ref[...] = scale * (scaled - normed * jnp.mean(scaled * normed, axis=-1, keepdims=True))
    for j in range(blocks):
        out_ref[:, cut(width, j)] += dy_ref[:, place(line_ref, j, width)].astype(F32)
    low_ref[...] = out_ref[...].astype(BF16)


def first_back_body(blocks, m, line_ref, x_ref, gain_ref, *refs):
    above_ref, out_ref = refs[2 * m :]
    width = x_ref.shape[1] // blocks
    span = slice(None)
    scale = scale_of(x_ref[...].astype(F32))
    normed = jnp.concatenate(
        [x_ref[:, place(line_ref, j, width)].astype(F32) for j in range(blocks)], axis=1
    ) * scale
    grad = jnp.concatenate([added(refs[:m], span), added(refs[m : 2 * m], span)], axis=1)
    scaled = grad * gain_ref[0:1, :]
    back = scale * (scaled - normed * jnp.mean(scaled * normed, axis=-1, keepdims=True))
    total = above_ref[...] + back
    for j in range(blocks):
        out_ref[:, place(line_ref, j, width)] = total[:, cut(width, j)]


def by_rows(chain, body, line, first, gains, parts, more, kinds):
    rows, model = first.shape
    half = model // 2
    tile = min(128, rows)
    row = pl.BlockSpec((tile, model), lambda i, *_: (i, 0))
    slim = pl.BlockSpec((tile, half), lambda i, *_: (i, 0))
    m = len(parts[0])
    return chain.call(
        functools.partial(body, line.shape[0], m),
        (rows // tile,),
        [row, whole(gains.shape)] + [slim] * (2 * m) + [row] * len(more),
        [row] * len(kinds),
        [((rows, model), kind) for kind in kinds],
        flops=20 * rows * model,
        prefetch=1,
        moved=rows * model * (2 * m + 4 * len(kinds)),
    )(line, first, gains, *parts[0], *parts[1], *more)


def finish_body(m, n, *refs):
    total = added(refs[:m], slice(None))
    weights, outs = refs[m : m + n], refs[m + n :]
    if not n:
        outs[0][...] = total.T
        return
    width = weights[0].shape[1]
    inner = jnp.zeros((total.shape[0], 1), F32)
    for i in range(n):
        part = total[:, cut(width, i)]
        outs[i][...] = part
        inner += jnp.sum(weights[i][...].astype(F32) * part, axis=1, keepdims=True)
    outs[n][...] = jnp.broadcast_to(inner, outs[n].shape)


def finish(chain, terms, weights=()):
    rows, columns = terms[0].shape
    tile = min(128, rows)
    row = pl.BlockSpec((tile, columns), lambda i: (i, 0))
    n = len(weights)
    if n:
        slim = pl.BlockSpec((tile, columns // n), lambda i: (i, 0))
        outs = [slim] * n + [pl.BlockSpec((tile, 128), lambda i: (i, 0))]
        shapes = [((rows, columns // n), F32)] * n + [((rows, 128), F32)]
    else:
        slim = None
        outs = [pl.BlockSpec((columns, tile), lambda i: (0, i))]
        shapes = [((columns, rows), F32)]
    results = chain.call(
        functools.partial(finish_body, len(terms), n),
        (rows // tile,),
        [row] * len(terms) + [slim] * n,
        outs,
        shapes,
        flops=4 * rows * columns,
        moved=rows * columns * 12,
    )(*terms, *weights)
    if n:
        results[n] = results[n][:, 0]
    return results


def rope_tables(place):
    half = HEAD_DIM // 2
    freq = THETA ** (-2.0 * jnp.arange(half, dtype=F32) / HEAD_DIM)
    angle = place.astype(F32)[:, None] * freq[None, :]
    cosine, sine = jnp.cos(angle), jnp.sin(angle)
    return (
        jnp.concatenate([cosine] * (PAIR // half), axis=1),
        jnp.concatenate([-sine, sine] * (PAIR // HEAD_DIM), axis=1),
    )


def turn(values):
    half = HEAD_DIM // 2
    width = values.shape[-1]
    lane = lax.broadcasted_iota(jnp.int32, values.shape, 1) % HEAD_DIM
    return jnp.where(
        lane < half, pltpu.roll(values, width - half, 1), pltpu.roll(values, half, 1)
    )


def joined(refs):
    return jnp.concatenate([r[...] for r in refs], axis=0)


def qkv_body(n, x_ref, cos_ref, sin_ref, *refs):
    weights, outs = refs[: 3 * n], refs[3 * n :]
    rows = x_ref.shape[0]
    tile = outs[0].shape[1]
    for i in range(3):
        weight = joined(weights[i * n : (i + 1) * n])
        for s in range(rows // SEQ):
            span = slice(s * SEQ, (s + 1) * SEQ)
            product = nn(x_ref[span, :], weight)
            if i == 2:
                outs[i][span, :] = product.astype(BF16)
                continue
            for t in range(tile // PAIR):
                here = product[:, t * PAIR : (t + 1) * PAIR]
                turned = here * cos_ref[...] + turn(here) * sin_ref[...]
                outs[i][span, t * PAIR : (t + 1) * PAIR] = turned.astype(BF16)


def project(chain, x, tables, query, key, value):
    rows, model = x.shape
    n, width = len(query.pieces), query.width
    tile = min(256, width)
    out = pl.BlockSpec((rows, tile), lambda j: (0, j))
    return chain.call(
        functools.partial(qkv_body, n),
        (width // tile,),
        [whole(x.shape), whole((SEQ, PAIR)), whole((SEQ, PAIR))]
        + query.tiles(tile)
        + key.tiles(tile)
        + value.tiles(tile),
        [out] * 3,
        [((rows, width), BF16)] * 3,
        flops=6 * rows * model * width,
        moved=2 * (rows * model + 3 * model * width + 3 * rows * width),
    )(x, *tables, *query.pieces, *key.pieces, *value.pieces)


def collect(counts, refs, held, sems):
    rows = held.shape[0] // len(counts)
    copies = []
    for k, count in enumerate(counts):
        half = held.shape[1] // count
        for h in range(count):
            target = held.at[pl.ds(k * rows, rows), pl.ds(h * half, half)]
            i = len(copies)
            copies.append(pltpu.make_async_copy(refs[i], target, sems.at[i]))
    for copy in copies:
        copy.start()
    for copy in copies:
        copy.wait()


def gate_body(n, counts, *refs):
    m = sum(counts)
    gate_w, up_w = refs[m : m + n], refs[m + n : m + 2 * n]
    hidden_ref, slope_ref, silu_ref, x_ref, sems = refs[m + 2 * n :]

    @pl.when(pl.program_id(0) == 0)
    def _():
        collect(counts, refs, x_ref, sems)

    gate_weight, up_weight = joined(gate_w), joined(up_w)
    for s in range(x_ref.shape[0] // SEQ):
        span = slice(s * SEQ, (s + 1) * SEQ)
        gate = nn(x_ref[span, :], gate_weight)
        up = nn(x_ref[span, :], up_weight)
        sigm = jax.nn.sigmoid(gate)
        silu = gate * sigm
        hidden_ref[span, :] = (silu * up).astype(BF16)
        silu_ref[span, :] = silu.astype(BF16)
        slope_ref[span, :] = (up * sigm * (1.0 + gate * (1.0 - sigm))).astype(BF16)


def collected(held):
    counts = [len(block) for block in held]
    rows, model = held[0][0].shape
    scratch = [
        pltpu.VMEM((len(held) * rows, model), BF16),
        pltpu.SemaphoreType.DMA((sum(counts),)),
    ]
    arrays = [array for block in held for array in block]
    return counts, arrays, [pl.BlockSpec(memory_space=pl.ANY)] * len(arrays), scratch


def gate_up(chain, held, gate, up):
    counts, arrays, specs, scratch = collected(held)
    rows, model = scratch[0].shape
    n, width = len(gate.pieces), gate.width
    tile = min(256, width)
    out = pl.BlockSpec((rows, tile), lambda j: (0, j))
    return chain.call(
        functools.partial(gate_body, n, counts),
        (width // tile,),
        specs + gate.tiles(tile) + up.tiles(tile),
        [out] * 3,
        [((rows, width), BF16)] * 3,
        flops=4 * rows * model * width,
        scratch=scratch,
        moved=2 * (rows * model + 2 * model * width + 3 * rows * width),
    )(*arrays, *gate.pieces, *up.pieces)


def hidden_back_body(n, g_ref, *refs):
    weight = joined(refs[:n])
    slope_ref, silu_ref, gate_ref, up_ref = refs[n:]
    for s in range(g_ref.shape[0] // SEQ):
        span = slice(s * SEQ, (s + 1) * SEQ)
        grad = nn(g_ref[span, :], weight)
        gate_ref[span, :] = (grad * slope_ref[span, :].astype(F32)).astype(BF16)
        up_ref[span, :] = (grad * silu_ref[span, :].astype(F32)).astype(BF16)


def hidden_back(chain, grads, down, slope, silu):
    rows, model = grads.shape
    n, width = len(down.pieces), down.width
    tile = min(256, width)
    out = pl.BlockSpec((rows, tile), lambda j: (0, j))
    return chain.call(
        functools.partial(hidden_back_body, n),
        (width // tile,),
        [whole(grads.shape)] + down.tiles(tile) + [out] * 2,
        [out] * 2,
        [((rows, width), BF16)] * 2,
        flops=2 * rows * model * width,
        moved=2 * (rows * model + model * width + 4 * rows * width),
    )(grads, *down.pieces, slope, silu)


def mixed_back_body(n, counts, *refs):
    m = sum(counts)
    out_ref, x_ref, sems = refs[m + n :]

    @pl.when(pl.program_id(0) == 0)
    def _():
        collect(counts, refs, x_ref, sems)

    out_ref[...] = nn(x_ref[...], joined(refs[m : m + n])).astype(BF16)


def mixed_back(chain, held, out):
    counts, arrays, specs, scratch = collected(held)
    rows, model = scratch[0].shape
    n, width = len(out.pieces), out.width
    tile = min(256, width)
    return chain.call(
        functools.partial(mixed_back_body, n, counts),
        (width // tile,),
        specs + out.tiles(tile),
        [pl.BlockSpec((rows, tile), lambda j: (0, j))],
        [((rows, width), BF16)],
        flops=2 * rows * model * width,
        scratch=scratch,
        moved=2 * (rows * model + model * width + rows * width),
    )(*arrays, *out.pieces)[0]


def trans_body(n, starts, targets, *refs):
    parts, blocks = len(starts), len(targets[0])
    lefts = refs[:parts]
    pieces = refs[parts : parts * (n + 1)]
    outs = refs[parts * (n + 1) : -4]
    held, ready, sems, out_sems = refs[-4:]
    j = pl.program_id(0)
    depth, width = held.shape[2:]
    rows = ready.shape[1] // blocks

    def copy(i, p, slot):
        source = pieces[p * n + i].at[pl.ds(0, depth), pl.ds(starts[p], width)]
        return pltpu.make_async_copy(source, held.at[slot, p], sems.at[slot, p])

    def fetch(step, slot):
        for i in range(n):

            @pl.when(step == i)
            def _():
                for p in range(parts):
                    copy(i, p, slot).start()

    def leave(slot, k, array, first, column):
        target = outs[array].at[pl.ds(first, rows), pl.ds(column, depth)]
        source = ready.at[slot, pl.ds(k * rows, rows), :]
        return pltpu.make_async_copy(source, target, out_sems.at[slot, k])

    def left(slot):
        for k in range(blocks):
            leave(slot, k, 0, 0, 0).wait()

    @pl.when(j == 0)
    def _():
        fetch(j, 0)

    @pl.when(j + 1 < n)
    def _():
        fetch(j + 1, (j + 1) % 2)

    slot = j % 2
    for p in range(parts):
        copy(0, p, slot).wait()

    @pl.when(j >= 2)
    def _():
        left(slot)

    for s in range(blocks * rows // SEQ):
        span = slice(s * SEQ, (s + 1) * SEQ)
        total = nt(lefts[0][span, :], held[slot, 0])
        for p in range(1, parts):
            total += nt(lefts[p][span, :], held[slot, p])
        ready[slot, span, :] = total.astype(BF16)
    column = pl.multiple_of(j % (n // 2) * depth, 128)
    for h in range(2):

        @pl.when((j >= n // 2) == (h == 1))
        def _():
            for k, (array, first) in enumerate(targets[h]):
                leave(slot, k, array, first, column).start()

    @pl.when(j == n - 1)
    def _():
        left(1 - slot)
        left(slot)


def times_trans(chain, parts, group):
    weights = [weight for _, weight in parts]
    n, depth, width = len(weights[0].pieces), weights[0].rows, weights[0].width
    rows = parts[0][0].shape[0]
    half = weights[0].model // 2
    size = rows // group.size
    messages = group.messages()
    shapes = [((size, half), BF16)] * 2
    targets = [{0: (0, 0)}, {0: (1, 0)}]
    for h in range(2):
        for keys in messages[h]:
            for i, k in enumerate(keys):
                targets[h][k] = (len(shapes), i * size)
            shapes.append(((len(keys) * size, half), BF16))
    targets = [[t[k] for k in range(group.size)] for t in targets]
    anywhere = pl.BlockSpec(memory_space=pl.ANY)
    outs = chain.call(
        functools.partial(trans_body, n, [weight.start for weight in weights], targets),
        (n,),
        [whole((rows, width))] * len(parts) + [anywhere] * (n * len(parts)),
        [anywhere] * len(shapes),
        shapes,
        flops=4 * rows * half * width * len(parts),
        scratch=[
            pltpu.VMEM((2, len(parts), depth, width), BF16),
            pltpu.VMEM((2, rows, depth), BF16),
            pltpu.SemaphoreType.DMA((2, len(parts))),
            pltpu.SemaphoreType.DMA((2, group.size)),
        ],
        moved=2 * (2 * rows * half + len(parts) * (rows + 2 * half) * width),
    )(*[left for left, _ in parts], *[piece for weight in weights for piece in weight.pieces])
    m = group.bits
    return outs[:2], [outs[2 : 2 + m], outs[2 + m :]]


def grad_body(parts, got, blocks, steps, *refs):
    lefts, refs = refs[:blocks], refs[blocks:]
    rights, refs = refs[:parts], refs[parts:]
    got_ref = refs[0] if got else None
    outs, turned = refs[got:-1], refs[-1]
    j = pl.program_id(0)

    @pl.when(j == 0)
    def _():
        rows = turned.shape[1] // blocks
        for k in range(blocks):
            turned[:, cut(rows, k)] = lefts[k][...].T

    for i in range(parts):

        @pl.when((j >= i * steps) & (j < (i + 1) * steps))
        def _():
            total = nn(turned[...], rights[i][...])
            if got:
                total += got_ref[...].astype(F32)
            total = total.astype(BF16)
            first = 0
            for out_ref in outs:
                count = out_ref.shape[0]
                out_ref[...] = total[first : first + count]
                first += count


def weight_grads(chain, left, which, rights, got=None, bits=0):
    rows, width = rights[0].shape
    parts = len(rights)
    tile = min(512, width)
    steps = width // tile
    if isinstance(left, list):
        lefts = [block[0] if len(block) == 1 else block[which] for block in left]
        half = left[0][0].shape[1] // 2
        places = [which if len(block) == 1 else 0 for block in left]
    else:
        lefts, places, half = [left], [which], left.shape[1] // 2
    blocks = len(lefts)
    ins = [
        pl.BlockSpec((rows // blocks, half), functools.partial(lambda at, j: (0, at), at))
        for at in places
    ]
    for i in range(parts):
        ins.append(
            pl.BlockSpec(
                (rows, tile),
                functools.partial(
                    lambda first, j: (0, jnp.clip(j - first, 0, steps - 1)), i * steps
                ),
            )
        )
    column = lambda j: (0, j)
    more = [] if got is None else [got]
    sizes = [half >> bits]
    for p in range(bits):
        sizes += [sizes[0], ((1 << p) - 1) * sizes[0]] if p else [sizes[0]]
    return chain.call(
        functools.partial(grad_body, parts, len(more), blocks, steps),
        (parts * steps,),
        ins + [pl.BlockSpec((half, tile), column)] * len(more),
        [pl.BlockSpec((size, tile), column) for size in sizes],
        [((size, parts * width), BF16) for size in sizes],
        flops=2 * rows * half * width * parts,
        scratch=[pltpu.VMEM((half, rows), BF16)],
        moved=2 * (rows * half + parts * (rows + half) * width),
    )(*lefts, *rights, *more)


def causal(scores):
    past = scores.shape[0] - HALF_SEQ
    key = lax.broadcasted_iota(jnp.int32, (HALF_SEQ, HALF_SEQ), 0)
    query = lax.broadcasted_iota(jnp.int32, (HALF_SEQ, HALF_SEQ), 1)
    last = jnp.where(key <= query, scores[past:], -1e30)
    return last if past == 0 else jnp.concatenate([scores[:past], last], axis=0)


def head_of(h):
    return slice(h * HEAD_DIM, (h + 1) * HEAD_DIM)


def span_of(b):
    return slice(b * HALF_SEQ, (b + 1) * HALF_SEQ)


def in_place(shift_ref, ref, count):
    rows = SEQ // count
    spans = [pl.ds(pl.multiple_of((i ^ shift_ref[0]) * rows, rows), rows) for i in range(count)]
    return jnp.concatenate([ref[span, :] for span in spans], axis=0)


def put_back(shift_ref, ref, count, values):
    rows = SEQ // count
    for i in range(count):
        ref[pl.ds(pl.multiple_of((i ^ shift_ref[0]) * rows, rows), rows), :] = values[cut(rows, i)]


def attend_body(count, shift_ref, q_ref, k_ref, v_ref, out_ref, sum_ref):
    queries, keys = in_place(shift_ref, q_ref, count), in_place(shift_ref, k_ref, count)
    values = in_place(shift_ref, v_ref, count).astype(F32).T.astype(BF16)
    heads = []
    for h in range(2):
        blocks = []
        for b in range(2):
            reach = (b + 1) * HALF_SEQ
            query = queries[span_of(b), head_of(h)] * BF16(FACTOR)
            scores = causal(nt(keys[:reach, head_of(h)], query))
            top = jnp.max(scores, axis=0, keepdims=True)
            expo = jnp.exp(scores - top)
            total = jnp.sum(expo, axis=0, keepdims=True)
            mixed = nn(values[head_of(h), :reach], expo.astype(BF16))
            blocks.append(mixed * (1.0 / total))
            sum_ref[0, 0, h : h + 1, span_of(b)] = top + jnp.log(total)
        heads.append(jnp.concatenate(blocks, axis=1))
    put_back(shift_ref, out_ref, count, jnp.concatenate(heads, axis=0).T.astype(BF16))


def attend(chain, shift, count, query, key, value):
    rows, width = query.shape
    seqs, pairs = rows // SEQ, width // PAIR
    tile = pl.BlockSpec((SEQ, PAIR), lambda s, p, _: (s, p))
    return chain.call(
        functools.partial(attend_body, count),
        (seqs, pairs),
        [tile] * 3,
        [tile, pl.BlockSpec((1, 1, 2, SEQ), lambda s, p, _: (s, p, 0, 0))],
        [((rows, width), BF16), ((seqs, pairs, 2, SEQ), F32)],
        flops=16 * rows * width * SEQ,
        prefetch=1,
        moved=8 * rows * width,
    )(shift, query, key, value)


def attend_back_body(
    count, shift_ref, q_ref, k_ref, v_ref, g_ref, sum_ref, cos_ref, sin_ref, dq_ref, dk_ref, dv_ref
):
    queries, keys, values, grads = (
        in_place(shift_ref, ref, count) for ref in (q_ref, k_ref, v_ref, g_ref)
    )
    turned = keys.astype(F32).T.astype(BF16)
    dq_heads, dk_heads, dv_heads = [], [], []
    for h in range(2):
        dq, dk, dv = [], [], []
        for b in range(2):
            reach = (b + 1) * HALF_SEQ
            query = queries[span_of(b), head_of(h)]
            grad = grads[span_of(b), head_of(h)]
            scores = causal(nt(keys[:reach, head_of(h)], query * BF16(FACTOR)))
            probs = jnp.exp(scores - sum_ref[0, 0, h : h + 1, span_of(b)])
            probs_grad = nt(values[:reach, head_of(h)], grad)
            inner = jnp.sum(probs * probs_grad, axis=0, keepdims=True)
            score_grad = (probs * (probs_grad - inner)).astype(BF16)
            dv.append(nn(probs.astype(BF16), grad))
            dk.append(nn(score_grad, query))
            dq.append(nn(turned[head_of(h), :reach], score_grad))
        for parts, heads in ((dk, dk_heads), (dv, dv_heads)):
            heads.append(
                jnp.concatenate([parts[1][:HALF_SEQ] + parts[0], parts[1][HALF_SEQ:]], axis=0)
            )
        dq_heads.append(jnp.concatenate(dq, axis=1))
    dq = jnp.concatenate(dq_heads, axis=0).T * FACTOR
    dk = jnp.concatenate(dk_heads, axis=1) * FACTOR
    dv = jnp.concatenate(dv_heads, axis=1).astype(BF16)
    cosine, sine = cos_ref[...], sin_ref[...]
    put_back(shift_ref, dq_ref, count, (dq * cosine - turn(dq) * sine).astype(BF16))
    put_back(shift_ref, dk_ref, count, (dk * cosine - turn(dk) * sine).astype(BF16))
    put_back(shift_ref, dv_ref, count, dv)


def attend_back(chain, shift, count, query, key, value, grad, logsum, tables):
    rows, width = query.shape
    seqs, pairs = rows // SEQ, width // PAIR
    tile = pl.BlockSpec((SEQ, PAIR), lambda s, p, _: (s, p))
    return chain.call(
        functools.partial(attend_back_body, count),
        (seqs, pairs),
        [tile] * 4
        + [pl.BlockSpec((1, 1, 2, SEQ), lambda s, p, _: (s, p, 0, 0))]
        + [whole((SEQ, PAIR))] * 2,
        [tile] * 3,
        [((rows, width), BF16)] * 3,
        flops=40 * rows * width * SEQ,
        prefetch=1,
        moved=14 * rows * width,
    )(shift, query, key, value, grad, logsum, *tables)


def local(
    chips,
    group,
    tokens,
    attn_gain,
    query_weight,
    key_weight,
    value_weight,
    output_weight,
    ffn_gain,
    gate_weight,
    up_weight,
    down_weight,
    cotangent,
):
    line = jnp.asarray(chips.table)[lax.axis_index("dp")]
    rows, model = tokens.shape
    count = SEQ // rows
    shift = lax.axis_index("tensor") % count
    row = jnp.arange(SEQ, dtype=jnp.int32)
    places = rope_tables(row)
    tables = rope_tables((row // rows ^ shift) * rows + row % rows)
    shift = jnp.reshape(shift, (1,)).astype(jnp.int32)
    early = (*places, *tables, line, shift)
    depth, own = query_weight.shape
    hidden_units = gate_weight.shape[1]
    chain = Chain()

    def gather(piece):
        return Gather(chips, chain, chain.join(piece)[0])

    def spread_of(values):
        return Spread(group, chain, chain.join(values)[0])

    def fold_of(part):
        own_part, sent = part
        sent = chain.join(*sent[0], *sent[1])
        return Fold(group, chain, own_part, [sent[: group.bits], sent[group.bits :]])

    def grads_of(left, rights):
        got = [None]
        chain.ask(weight_grads(chain, left, 1, rights)[0], got, 0, chips.other)

        def mine(**how):
            if got[0] is None:
                chain.flush()
            blocks = weight_grads(chain, left, 0, rights, got[0], chips.bits)
            return Sums(chips, chain, blocks, **how)

        return mine

    extra = jnp.concatenate([attn_gain, ffn_gain, jnp.zeros((4 * own - 2 * depth,), BF16)])
    attn = jnp.concatenate([query_weight, key_weight, value_weight, output_weight.T], axis=1)
    attn = gather(jnp.concatenate([attn, jnp.broadcast_to(extra, (16, 4 * own))], axis=0))
    spread = spread_of(tokens)
    grads_spread = spread_of(cotangent)
    grads_spread.later = []
    down_turned, *early = chain.join(down_weight.T, *early)
    places, tables, line, shift = early[:2], early[2:4], early[4], early[5]
    chain.end(attn, spread, grads_spread)
    chain.end(attn, spread)
    all_tokens = spread.blocks()
    attn = attn.pieces()
    pair = gather(jnp.concatenate([gate_weight, up_weight], axis=1))
    w_query, w_key, w_value, w_output = [Weight(attn, depth, i * own, own) for i in range(4)]
    gains = jnp.concatenate(
        [piece[depth : depth + 1, : 2 * depth].reshape(2, depth) for piece in attn], axis=1
    ).astype(F32)

    group_one = ordered(chain, norm_body, line, gains, all_tokens)
    grads_spread.resume()
    query, key, value = project(chain, group_one, tables, w_query, w_key, w_value)
    mixed, logsum = attend(chain, shift, count, query, key, value)
    out_part = times_trans(chain, [(mixed, w_output)], group)
    fold = fold_of(out_part)
    chain.end(fold, pair, grads_spread)
    grad_rows = ordered(chain, order_body, line, gains, grads_spread.blocks())
    chain.end(fold)
    attended = fold.total()
    middle, second = by_rows(
        chain, middle_body, line, tokens, gains, attended, [], [F32, BF16]
    )
    spread = spread_of(second)
    chain.end(spread, pair)
    pair = pair.pieces()
    down = gather(down_turned)
    chain.end(spread)
    group_two = spread.blocks()
    w_gate = Weight(pair, depth, 0, hidden_units)
    w_up = Weight(pair, depth, hidden_units, hidden_units)
    hidden, slope, silu = gate_up(chain, group_two, w_gate, w_up)

    mine = grads_of(grad_rows, [hidden])
    chain.end(down)
    chain.flush()
    down_sum = mine()
    w_down = Weight(down.pieces(), depth, 0, hidden_units)
    gate_grad, up_grad = hidden_back(chain, grad_rows, w_down, slope, silu)
    mine_gate = grads_of(group_two, [gate_grad])
    chain.end(down_sum)
    second_part = times_trans(chain, [(gate_grad, w_gate), (up_grad, w_up)], group)
    mine_up = grads_of(group_two, [up_grad])
    gate_sum = mine_gate(hold=True)
    chain.end(down_sum)
    fold = fold_of(second_part)
    up_sum = mine_up(apart=True)
    chain.end(gate_sum, fold)
    result_part = times_trans(chain, [(hidden, w_down)], group)
    chain.end(fold)
    second_grad = fold.total()
    middle_grad, low_grad = by_rows(
        chain, second_back_body, line, cotangent, gains, second_grad, [middle], [F32, BF16]
    )
    spread = spread_of(low_grad)
    chain.end(up_sum)
    gate_sum.resume()
    (down_sum,) = finish(chain, down_sum.terms())
    chain.end(spread)
    attn_grads = spread.blocks()

    mixed_grad = mixed_back(chain, attn_grads, w_output)
    mine_out = grads_of(attn_grads, [mixed])
    chain.end(gate_sum)
    fold = fold_of(result_part)
    query_back, key_back, value_back = attend_back(
        chain, shift, count, query, key, value, mixed_grad, logsum, places
    )
    chain.end(up_sum, fold)
    mine_qkv = grads_of(group_one, [query_back, key_back, value_back])
    chain.flush()
    first_part = times_trans(
        chain, [(query_back, w_query), (key_back, w_key), (value_back, w_value)], group
    )
    qkv_sum = mine_qkv()
    out_sum = mine_out()
    gate_sum, gate_inner = finish(chain, gate_sum.terms(), [gate_weight])
    chain.end(up_sum, qkv_sum, fold)
    result_part = fold.total()
    fold = fold_of(first_part)
    (layer_out,) = by_rows(chain, result_body, line, middle, gains, result_part, [], [BF16])
    up_sum, up_inner = finish(chain, up_sum.terms(), [up_weight])
    chain.end(qkv_sum, out_sum, fold)
    query_sum, key_sum, value_sum, qkv_inner = finish(
        chain, qkv_sum.terms(), [query_weight, key_weight, value_weight]
    )
    gain_one_total, gain_two_total = lax.psum(
        (
            qkv_inner / attn_gain.astype(F32),
            (gate_inner + up_inner) / ffn_gain.astype(F32),
        ),
        "tensor",
    )
    (gain_one_total,) = chain.join(gain_one_total)
    first_grad = fold.total()
    (input_grad,) = by_rows(
        chain, first_back_body, line, tokens, gains, first_grad, [middle_grad], [F32]
    )
    (out_sum,) = finish(chain, out_sum.terms())
    return (
        layer_out,
        input_grad,
        gain_one_total,
        query_sum,
        key_sum,
        value_sum,
        out_sum,
        gain_two_total,
        gate_sum,
        up_sum,
        down_sum,
    )


def solution(mesh):
    in_specs = (
        P(("dp", "tensor"), None),
        P("dp"),
        P("dp", "tensor"),
        P("dp", "tensor"),
        P("dp", "tensor"),
        P("tensor", "dp"),
        P("dp"),
        P("dp", "tensor"),
        P("dp", "tensor"),
        P("tensor", "dp"),
        P(("dp", "tensor"), None),
    )
    out_specs = (
        P(("dp", "tensor"), None),
        P(("dp", "tensor"), None),
        P("dp"),
        P("dp", "tensor"),
        P("dp", "tensor"),
        P("dp", "tensor"),
        P("tensor", "dp"),
        P("dp"),
        P("dp", "tensor"),
        P("dp", "tensor"),
        P("tensor", "dp"),
    )
    chips = Chips(mesh.shape["dp"])
    size = mesh.shape["tensor"]
    links = [[(i, i ^ 1 << b) for i in range(size)] for b in range(size.bit_length() - 1)]
    group = Group(links, "tensor")

    def run(*arrays):
        return local(chips, group, *arrays)

    return jax.shard_map(run, mesh=mesh, in_specs=in_specs, out_specs=out_specs, check_vma=False)
```

```python
import functools

import jax
import jax.numpy as jnp
import numpy as np
from jax import lax
from jax.experimental import pallas as pl
from jax.experimental.pallas import tpu as pltpu
from jax.sharding import PartitionSpec as P

HEAD_DIM = 64
SEQ = 512
EPS = 1e-05
THETA = 130000.0
BF16 = jnp.bfloat16
F32 = jnp.float32
FACTOR = HEAD_DIM**-0.5
PAIR = 2 * HEAD_DIM
HALF_SEQ = SEQ // 2
VMEM_LIMIT = 58 << 20
COST_SHARE = 4096


class Chain:
    def __init__(self):
        self.token = jnp.zeros((8, 128), F32)
        self.swaps, self.asked = [], []

    def join(self, *values):
        *values, self.token = lax.optimization_barrier((*values, self.token))
        return values

    def gate(self, *values):
        swaps, self.swaps = self.swaps, []
        asked, self.asked = self.asked, []
        joined = self.join(
            *values, *[held[i] for held, i in swaps], *[source for source, _, _, _ in asked]
        )
        for (held, i), value in zip(swaps, joined[len(values) :]):
            held[i] = value
        for (_, held, i, swap), value in zip(asked, joined[len(values) + len(swaps) :]):
            held[i] = swap(value)
            self.swaps.append((held, i))
        return joined[: len(values)]

    def end(self, *transfers):
        counts = [len(t.flying) for t in transfers]
        got = self.gate(*[value for t in transfers for value in t.flying])
        for t, count in zip(transfers, counts):
            if count:
                t.go_on(got[:count])
            got = got[count:]

    def ask(self, source, held, i, swap):
        self.asked.append((source, held, i, swap))

    def flush(self):
        for source, held, i, swap in self.asked:
            held[i] = swap(source)
        self.asked = []

    def call(self, body, grid, ins, outs, shapes, flops, scratch=(), prefetch=0, moved=0):
        first = prefetch + len(ins)
        second = first + 1 + len(outs)
        anywhere = pl.BlockSpec(memory_space=pl.ANY)

        def wrapped(*refs):
            body(*refs[:first], *refs[first + 1 : second], *refs[second + 1 :])

        run = pl.pallas_call(
            wrapped,
            grid_spec=pltpu.PrefetchScalarGridSpec(
                num_scalar_prefetch=prefetch,
                grid=grid,
                in_specs=[*ins, anywhere],
                out_specs=[*outs, anywhere],
                scratch_shapes=list(scratch),
            ),
            out_shape=[jax.ShapeDtypeStruct(s, t) for s, t in [*shapes, ((8, 128), F32)]],
            compiler_params=pltpu.CompilerParams(
                vmem_limit_bytes=VMEM_LIMIT, dimension_semantics=("arbitrary",) * len(grid)
            ),
            cost_estimate=pl.CostEstimate(
                flops=flops // COST_SHARE, bytes_accessed=moved // COST_SHARE, transcendentals=0
            ),
        )

        def with_token(*args):
            *results, self.token = run(*args, self.token)
            return results

        return with_token


class Chips:
    def __init__(self, size):
        self.bits = (size // 2).bit_length() - 1
        self.size = size
        self.swap = [(i, i ^ 1) for i in range(size)]
        self.links = [
            [(i, i ^ 2 << self.bits - 1 - p) for i in range(size)] for p in range(self.bits)
        ]
        flips = [
            sum(1 << self.bits - 1 - p for p in range(self.bits) if v >> p & 1)
            for v in range(1 << self.bits)
        ]
        table = [[i ^ 2 * f for f in flips] + [i ^ 2 * f ^ 1 for f in flips] for i in range(size)]
        self.table = np.array(table, np.int32)

    def send(self, value, p):
        return lax.ppermute(value, "dp", self.links[p])

    def other(self, value):
        return lax.ppermute(value, "dp", self.swap)


class Gather:
    def __init__(self, chips, chain, piece):
        self.chips, self.chain = chips, chain
        self.own = [piece] + [None] * (2**chips.bits - 1)
        self.others = list(self.own)
        self.ask(0)
        self.keys = [1 << p for p in range(chips.bits)]
        self.flying = [chips.send(piece, p) for p in range(chips.bits)]

    def ask(self, v):
        self.chain.ask(self.own[v], self.others, v, self.chips.other)

    def go_on(self, got):
        keys, self.keys, self.flying = self.keys, [], []
        for v, piece in zip(keys, got):
            self.own[v] = piece
            for p in range(v.bit_length(), self.chips.bits):
                self.keys.append(v | 1 << p)
                self.flying.append(self.chips.send(piece, p))
        for v in keys:
            self.ask(v)

    def pieces(self):
        while self.flying:
            self.chain.end(self)
        self.chain.flush()
        return self.own + self.others


class Sums:
    def __init__(self, chips, chain, mine, apart=False, hold=False):
        self.chips, self.chain, self.apart, self.hold = chips, chain, apart, hold
        self.todo = []
        self.parts = [mine[0]]
        mine = list(mine[1:])
        self.direct, self.passed = [], []
        for p in range(chips.bits):
            self.direct.append(mine.pop(0))
            self.passed.append(mine.pop(0) if p else None)
        self.p = chips.bits - 1
        self.kinds = [self.p]
        self.flying = [chips.send(self.passed[self.p], self.p)]

    def go_on(self, got):
        rows = self.parts[0].shape[0]
        kinds, self.kinds, self.flying = self.kinds, [], []
        if self.p == 0:
            self.parts += got
            return
        for kind, block in zip(kinds, got):
            if kind is None:
                self.parts.append(block)
                continue
            add = lambda held, first: (
                held.astype(F32) + block[first * rows : first * rows + held.shape[0]].astype(F32)
            ).astype(BF16)
            for q in range(kind):
                self.direct[q] = add(self.direct[q], (1 << q) - 1)
                if q:
                    self.passed[q] = add(self.passed[q], 1 << q)
        p, self.p = self.p, self.p - 1
        if p > 0:
            self.todo.append((None, self.direct[p], p))
        if p > 1:
            self.todo.append((p - 1, self.passed[p - 1], p - 1))
        if p == 1 and not self.apart:
            self.todo.append((None, self.direct[0], 0))
        if not self.hold:
            self.resume()

    def resume(self):
        todo, self.todo = self.todo, []
        values = self.chain.join(*[value for _, value, _ in todo])
        for (kind, _, p), value in zip(todo, values):
            self.kinds.append(kind)
            self.flying.append(self.chips.send(value, p))

    def send_half(self, i):
        while self.p > 0:
            self.chain.end(self)
        width = self.direct[0].shape[1] // 2
        (value,) = self.chain.join(self.direct[0][:, i * width : (i + 1) * width])
        self.kinds.append(None)
        self.flying.append(self.chips.send(value, 0))

    def terms(self):
        while self.flying or self.todo:
            if self.todo:
                self.resume()
            self.chain.end(self)
        return sorted(self.parts, key=lambda part: -part.shape[1])


class Group:
    def __init__(self, links, axes):
        self.links, self.axes = links, axes
        self.bits = len(links)
        self.size = 1 << self.bits
        self.orders = (list(range(self.bits)), list(range(self.bits))[::-1])

    def send(self, value, bit):
        return lax.ppermute(value, self.axes, self.links[bit])

    def messages(self):
        found = []
        for order in self.orders:
            found.append([])
            for top in reversed(range(self.bits)):
                found[-1].append(
                    [
                        1 << order[top] | sum(1 << order[p] for p in range(top) if v >> p & 1)
                        for v in range(1 << top)
                    ]
                )
        return found


class Spread:
    def __init__(self, group, chain, rows):
        self.group, self.chain = group, chain
        self.held = {0: [rows]}
        self.later = None
        self.keys = [(1 << b, None) for b in range(group.bits)]
        self.flying = [group.send(rows, b) for b in range(group.bits)]

    def go_on(self, got):
        fresh = list(zip(self.keys, got))
        self.keys, self.flying = [], []
        for (k, h), block in fresh:
            if h is None:
                self.held[k] = [block]
            else:
                self.held.setdefault(k, [None, None])[h] = block
        for (k, h), block in fresh:
            for way, order in enumerate(self.group.orders):
                if h is not None and h != way:
                    continue
                half = block.shape[1] // 2
                top = max(i for i, bit in enumerate(order) if k >> bit & 1)
                for i in range(top + 1, len(order)):
                    part = block if h is not None else block[:, way * half : (way + 1) * half]
                    self.keys.append((k | 1 << order[i], way))
                    if self.later is not None:
                        self.later.append((part, order[i]))
                    else:
                        self.flying.append(self.group.send(part, order[i]))

        if self.later:
            parts = self.chain.join(*[part for part, _ in self.later])
            self.later = [(part, bit) for part, (_, bit) in zip(parts, self.later)]

    def resume(self):
        later, self.later = self.later, None
        parts = self.chain.join(*[part for part, _ in later])
        self.flying = [self.group.send(part, bit) for part, (_, bit) in zip(parts, later)]

    def blocks(self):
        while self.flying:
            self.chain.end(self)
        return [self.held[k] for k in range(self.group.size)]


class Fold:
    def __init__(self, group, chain, own, sent):
        self.group, self.chain = group, chain
        self.rows = own[0].shape[0]
        self.sent = [list(half) for half in sent]
        self.parts = [[half] for half in own]
        self.wave = 0
        self.start()

    def start(self):
        self.flying = [
            self.group.send(self.sent[h][self.wave], order[self.group.bits - 1 - self.wave])
            for h, order in enumerate(self.group.orders)
        ]

    def go_on(self, got):
        self.wave += 1
        self.flying = []
        for h, block in enumerate(got):
            self.parts[h].append(block)
            for wave in range(self.wave, self.group.bits):
                first = self.rows << (self.group.bits - 1 - wave)
                more = block[first : 2 * first].astype(F32)
                self.sent[h][wave] = (self.sent[h][wave].astype(F32) + more).astype(BF16)
        if self.wave < self.group.bits:
            now = self.chain.join(*[sent[self.wave] for sent in self.sent])
            for sent, value in zip(self.sent, now):
                sent[self.wave] = value
            self.start()

    def total(self):
        while self.flying:
            self.chain.end(self)
        return self.parts


class Weight:
    def __init__(self, pieces, rows, start, width):
        self.pieces, self.rows, self.start, self.width = pieces, rows, start, width
        self.model = len(pieces) * rows

    def tiles(self, tile):
        first = self.start // tile
        return [pl.BlockSpec((self.rows, tile), lambda j: (0, first + j))] * len(self.pieces)


def nn(left, right):
    return lax.dot_general(left, right, (((1,), (0,)), ((), ())), preferred_element_type=F32)


def nt(left, right):
    return lax.dot_general(left, right, (((1,), (1,)), ((), ())), preferred_element_type=F32)


def tn(left, right):
    return lax.dot_general(left, right, (((0,), (0,)), ((), ())), preferred_element_type=F32)


def whole(shape):
    return pl.BlockSpec(shape, lambda *_: (0,) * len(shape))


def place(line_ref, j, width):
    return pl.ds(pl.multiple_of(line_ref[j] * width, 128), width)


def cut(width, j):
    return slice(j * width, (j + 1) * width)


def scale_of(values):
    return lax.rsqrt(jnp.mean(values * values, axis=-1, keepdims=True) + EPS)


def fetch_blocks(counts, refs, held, sems, k, slot, wait):
    first = 0
    for i, count in enumerate(counts):
        copies = []
        half = held.shape[2] // count
        for h in range(count):
            target = held.at[slot, :, pl.ds(h * half, half)]
            copies.append(pltpu.make_async_copy(refs[first + h], target, sems.at[slot, h]))
        first += count

        @pl.when(k == i)
        def _():
            for copy in copies:
                copy.wait() if wait else copy.start()


def fetched(counts, refs, held, sems):
    k = pl.program_id(0)

    @pl.when(k == 0)
    def _():
        fetch_blocks(counts, refs, held, sems, k, 0, False)

    fetch_blocks(counts, refs, held, sems, k + 1, (k + 1) % 2, False)
    fetch_blocks(counts, refs, held, sems, k, k % 2, True)
    return held.at[k % 2]


def norm_body(blocks, counts, line_ref, gain_ref, *refs):
    out_ref, held, sems = refs[sum(counts) :]
    x_ref = fetched(counts, refs, held, sems)
    width = out_ref.shape[1] // blocks
    scale = scale_of(x_ref[...].astype(F32))
    for j in range(blocks):
        part = x_ref[:, place(line_ref, j, width)].astype(F32)
        gain = gain_ref[0:1, cut(width, j)]
        out_ref[:, cut(width, j)] = (part * scale * gain).astype(BF16)


def order_body(blocks, counts, line_ref, gain_ref, *refs):
    out_ref, held, sems = refs[sum(counts) :]
    x_ref = fetched(counts, refs, held, sems)
    width = out_ref.shape[1] // blocks
    for j in range(blocks):
        out_ref[:, cut(width, j)] = x_ref[:, place(line_ref, j, width)]


def ordered(chain, body, line, gains, held):
    counts = [len(block) for block in held]
    rows, model = held[0][0].shape
    n = len(held)
    return chain.call(
        functools.partial(body, line.shape[0], counts),
        (n,),
        [whole(gains.shape)] + [pl.BlockSpec(memory_space=pl.ANY)] * sum(counts),
        [pl.BlockSpec((rows, model), lambda k, *_: (k, 0))],
        [((n * rows, model), BF16)],
        flops=20 * n * rows * model,
        scratch=[pltpu.VMEM((2, rows, model), BF16), pltpu.SemaphoreType.DMA((2, 2))],
        prefetch=1,
        moved=4 * n * rows * model,
    )(line, gains, *[array for block in held for array in block])[0]


def added(refs, span):
    total = refs[0][span, :].astype(F32)
    for ref in refs[1:]:
        total += ref[span, :].astype(F32)
    return total


def middle_body(blocks, m, line_ref, x_ref, gain_ref, *refs):
    middle_ref, out_ref = refs[2 * m :]
    width = x_ref.shape[1] // blocks
    half = x_ref.shape[1] // 2
    span = slice(None)
    middle_ref[:, :half] = added(refs[:m], span)
    middle_ref[:, half:] = added(refs[m : 2 * m], span)
    for j in range(blocks):
        here = x_ref[:, place(line_ref, j, width)].astype(F32)
        middle_ref[:, cut(width, j)] += here
    middle = middle_ref[...]
    out_ref[...] = (middle * scale_of(middle) * gain_ref[1:2, :]).astype(BF16)


def result_body(blocks, m, line_ref, middle_ref, gain_ref, *refs):
    out_ref = refs[2 * m]
    width = middle_ref.shape[1] // blocks
    span = slice(None)
    total = middle_ref[...] + jnp.concatenate(
        [added(refs[:m], span), added(refs[m : 2 * m], span)], axis=1
    )
    for j in range(blocks):
        out_ref[:, place(line_ref, j, width)] = total[:, cut(width, j)].astype(BF16)


def second_back_body(blocks, m, line_ref, dy_ref, gain_ref, *refs):
    middle_ref, out_ref, low_ref = refs[2 * m :]
    width = dy_ref.shape[1] // blocks
    span = slice(None)
    grad = jnp.concatenate([added(refs[:m], span), added(refs[m : 2 * m], span)], axis=1)
    middle = middle_ref[...]
    scale = scale_of(middle)
    normed = middle * scale
    scaled = grad * gain_ref[1:2, :]
    out_ref[...] = scale * (scaled - normed * jnp.mean(scaled * normed, axis=-1, keepdims=True))
    for j in range(blocks):
        out_ref[:, cut(width, j)] += dy_ref[:, place(line_ref, j, width)].astype(F32)
    low_ref[...] = out_ref[...].astype(BF16)


def first_back_body(blocks, m, line_ref, x_ref, gain_ref, *refs):
    above_ref, out_ref = refs[2 * m :]
    width = x_ref.shape[1] // blocks
    span = slice(None)
    scale = scale_of(x_ref[...].astype(F32))
    normed = jnp.concatenate(
        [x_ref[:, place(line_ref, j, width)].astype(F32) for j in range(blocks)], axis=1
    ) * scale
    grad = jnp.concatenate([added(refs[:m], span), added(refs[m : 2 * m], span)], axis=1)
    scaled = grad * gain_ref[0:1, :]
    back = scale * (scaled - normed * jnp.mean(scaled * normed, axis=-1, keepdims=True))
    total = above_ref[...] + back
    for j in range(blocks):
        out_ref[:, place(line_ref, j, width)] = total[:, cut(width, j)]


def by_rows(chain, body, line, first, gains, parts, more, kinds):
    rows, model = first.shape
    half = model // 2
    tile = min(128, rows)
    row = pl.BlockSpec((tile, model), lambda i, *_: (i, 0))
    slim = pl.BlockSpec((tile, half), lambda i, *_: (i, 0))
    m = len(parts[0])
    return chain.call(
        functools.partial(body, line.shape[0], m),
        (rows // tile,),
        [row, whole(gains.shape)] + [slim] * (2 * m) + [row] * len(more),
        [row] * len(kinds),
        [((rows, model), kind) for kind in kinds],
        flops=20 * rows * model,
        prefetch=1,
        moved=rows * model * (2 * m + 4 * len(kinds)),
    )(line, first, gains, *parts[0], *parts[1], *more)


def finish_body(m, halves, n, *refs):
    total = added(refs[:m], slice(None))
    if halves:
        total += jnp.concatenate([ref[...].astype(F32) for ref in refs[m : m + halves]], axis=1)
    m += halves
    weights, outs = refs[m : m + n], refs[m + n :]
    if not n:
        outs[0][...] = total.T
        return
    width = weights[0].shape[1]
    inner = jnp.zeros((total.shape[0], 1), F32)
    for i in range(n):
        part = total[:, cut(width, i)]
        outs[i][...] = part
        inner += jnp.sum(weights[i][...].astype(F32) * part, axis=1, keepdims=True)
    outs[n][...] = jnp.broadcast_to(inner, outs[n].shape)


def finish(chain, terms, weights=()):
    rows, columns = terms[0].shape
    tile = min(128, rows)
    row = pl.BlockSpec((tile, columns), lambda i: (i, 0))
    n = len(weights)
    halves = sum(1 for term in terms if term.shape[1] < columns)
    half = [pl.BlockSpec((tile, columns // 2), lambda i: (i, 0))] * halves
    if n:
        slim = pl.BlockSpec((tile, columns // n), lambda i: (i, 0))
        outs = [slim] * n + [pl.BlockSpec((tile, 128), lambda i: (i, 0))]
        shapes = [((rows, columns // n), F32)] * n + [((rows, 128), F32)]
    else:
        slim = None
        outs = [pl.BlockSpec((columns, tile), lambda i: (0, i))]
        shapes = [((columns, rows), F32)]
    results = chain.call(
        functools.partial(finish_body, len(terms) - halves, halves, n),
        (rows // tile,),
        [row] * (len(terms) - halves) + half + [slim] * n,
        outs,
        shapes,
        flops=4 * rows * columns,
        moved=rows * columns * 12,
    )(*terms, *weights)
    if n:
        results[n] = results[n][:, 0]
    return results


def rope_tables(place):
    half = HEAD_DIM // 2
    freq = THETA ** (-2.0 * jnp.arange(half, dtype=F32) / HEAD_DIM)
    angle = place.astype(F32)[:, None] * freq[None, :]
    cosine, sine = jnp.cos(angle), jnp.sin(angle)
    return (
        jnp.concatenate([cosine] * (PAIR // half), axis=1),
        jnp.concatenate([-sine, sine] * (PAIR // HEAD_DIM), axis=1),
    )


def turn(values):
    half = HEAD_DIM // 2
    width = values.shape[-1]
    lane = lax.broadcasted_iota(jnp.int32, values.shape, 1) % HEAD_DIM
    return jnp.where(
        lane < half, pltpu.roll(values, width - half, 1), pltpu.roll(values, half, 1)
    )


def joined(refs):
    return jnp.concatenate([r[...] for r in refs], axis=0)


def qkv_body(n, x_ref, cos_ref, sin_ref, *refs):
    weights, outs = refs[: 3 * n], refs[3 * n :]
    rows = x_ref.shape[0]
    tile = outs[0].shape[1]
    for i in range(3):
        weight = joined(weights[i * n : (i + 1) * n])
        for s in range(rows // SEQ):
            span = slice(s * SEQ, (s + 1) * SEQ)
            product = nn(x_ref[span, :], weight)
            if i == 2:
                outs[i][span, :] = product.astype(BF16)
                continue
            for t in range(tile // PAIR):
                here = product[:, t * PAIR : (t + 1) * PAIR]
                turned = here * cos_ref[...] + turn(here) * sin_ref[...]
                outs[i][span, t * PAIR : (t + 1) * PAIR] = turned.astype(BF16)


def project(chain, x, tables, query, key, value):
    rows, model = x.shape
    n, width = len(query.pieces), query.width
    tile = min(256, width)
    out = pl.BlockSpec((rows, tile), lambda j: (0, j))
    return chain.call(
        functools.partial(qkv_body, n),
        (width // tile,),
        [whole(x.shape), whole((SEQ, PAIR)), whole((SEQ, PAIR))]
        + query.tiles(tile)
        + key.tiles(tile)
        + value.tiles(tile),
        [out] * 3,
        [((rows, width), BF16)] * 3,
        flops=6 * rows * model * width,
        moved=2 * (rows * model + 3 * model * width + 3 * rows * width),
    )(x, *tables, *query.pieces, *key.pieces, *value.pieces)


def collect(counts, refs, held, sems):
    rows = held.shape[0] // len(counts)
    copies = []
    for k, count in enumerate(counts):
        half = held.shape[1] // count
        for h in range(count):
            target = held.at[pl.ds(k * rows, rows), pl.ds(h * half, half)]
            i = len(copies)
            copies.append(pltpu.make_async_copy(refs[i], target, sems.at[i]))
    for copy in copies:
        copy.start()
    for copy in copies:
        copy.wait()


def gate_body(n, counts, *refs):
    m = sum(counts)
    gate_w, up_w = refs[m : m + n], refs[m + n : m + 2 * n]
    hidden_ref, slope_ref, silu_ref, x_ref, sems = refs[m + 2 * n :]

    @pl.when(pl.program_id(0) == 0)
    def _():
        collect(counts, refs, x_ref, sems)

    gate_weight, up_weight = joined(gate_w), joined(up_w)
    for s in range(x_ref.shape[0] // SEQ):
        span = slice(s * SEQ, (s + 1) * SEQ)
        gate = nn(x_ref[span, :], gate_weight)
        up = nn(x_ref[span, :], up_weight)
        sigm = jax.nn.sigmoid(gate)
        silu = gate * sigm
        hidden_ref[span, :] = (silu * up).astype(BF16)
        silu_ref[span, :] = silu.astype(BF16)
        slope_ref[span, :] = (up * sigm * (1.0 + gate * (1.0 - sigm))).astype(BF16)


def collected(held):
    counts = [len(block) for block in held]
    rows, model = held[0][0].shape
    scratch = [
        pltpu.VMEM((len(held) * rows, model), BF16),
        pltpu.SemaphoreType.DMA((sum(counts),)),
    ]
    arrays = [array for block in held for array in block]
    return counts, arrays, [pl.BlockSpec(memory_space=pl.ANY)] * len(arrays), scratch


def gate_up(chain, held, gate, up):
    counts, arrays, specs, scratch = collected(held)
    rows, model = scratch[0].shape
    n, width = len(gate.pieces), gate.width
    tile = min(256, width)
    out = pl.BlockSpec((rows, tile), lambda j: (0, j))
    return chain.call(
        functools.partial(gate_body, n, counts),
        (width // tile,),
        specs + gate.tiles(tile) + up.tiles(tile),
        [out] * 3,
        [((rows, width), BF16)] * 3,
        flops=4 * rows * model * width,
        scratch=scratch,
        moved=2 * (rows * model + 2 * model * width + 3 * rows * width),
    )(*arrays, *gate.pieces, *up.pieces)


def hidden_back_body(n, g_ref, *refs):
    weight = joined(refs[:n])
    slope_ref, silu_ref, gate_ref, up_ref = refs[n:]
    for s in range(g_ref.shape[0] // SEQ):
        span = slice(s * SEQ, (s + 1) * SEQ)
        grad = nn(g_ref[span, :], weight)
        gate_ref[span, :] = (grad * slope_ref[span, :].astype(F32)).astype(BF16)
        up_ref[span, :] = (grad * silu_ref[span, :].astype(F32)).astype(BF16)


def hidden_back(chain, grads, down, slope, silu):
    rows, model = grads.shape
    n, width = len(down.pieces), down.width
    tile = min(256, width)
    out = pl.BlockSpec((rows, tile), lambda j: (0, j))
    return chain.call(
        functools.partial(hidden_back_body, n),
        (width // tile,),
        [whole(grads.shape)] + down.tiles(tile) + [out] * 2,
        [out] * 2,
        [((rows, width), BF16)] * 2,
        flops=2 * rows * model * width,
        moved=2 * (rows * model + model * width + 4 * rows * width),
    )(grads, *down.pieces, slope, silu)


def mixed_back_body(n, counts, *refs):
    m = sum(counts)
    out_ref, x_ref, sems = refs[m + n :]

    @pl.when(pl.program_id(0) == 0)
    def _():
        collect(counts, refs, x_ref, sems)

    out_ref[...] = nn(x_ref[...], joined(refs[m : m + n])).astype(BF16)


def mixed_back(chain, held, out):
    counts, arrays, specs, scratch = collected(held)
    rows, model = scratch[0].shape
    n, width = len(out.pieces), out.width
    tile = min(256, width)
    return chain.call(
        functools.partial(mixed_back_body, n, counts),
        (width // tile,),
        specs + out.tiles(tile),
        [pl.BlockSpec((rows, tile), lambda j: (0, j))],
        [((rows, width), BF16)],
        flops=2 * rows * model * width,
        scratch=scratch,
        moved=2 * (rows * model + model * width + rows * width),
    )(*arrays, *out.pieces)[0]


def trans_body(n, starts, targets, *refs):
    parts, blocks = len(starts), len(targets[0])
    lefts = refs[:parts]
    pieces = refs[parts : parts * (n + 1)]
    outs = refs[parts * (n + 1) : -4]
    held, ready, sems, out_sems = refs[-4:]
    j = pl.program_id(0)
    depth, width = held.shape[2:]
    rows = ready.shape[1] // blocks

    def copy(i, p, slot):
        source = pieces[p * n + i].at[pl.ds(0, depth), pl.ds(starts[p], width)]
        return pltpu.make_async_copy(source, held.at[slot, p], sems.at[slot, p])

    def fetch(step, slot):
        for i in range(n):

            @pl.when(step == i)
            def _():
                for p in range(parts):
                    copy(i, p, slot).start()

    def leave(slot, k, array, first, column):
        target = outs[array].at[pl.ds(first, rows), pl.ds(column, depth)]
        source = ready.at[slot, pl.ds(k * rows, rows), :]
        return pltpu.make_async_copy(source, target, out_sems.at[slot, k])

    def left(slot):
        for k in range(blocks):
            leave(slot, k, 0, 0, 0).wait()

    @pl.when(j == 0)
    def _():
        fetch(j, 0)

    @pl.when(j + 1 < n)
    def _():
        fetch(j + 1, (j + 1) % 2)

    slot = j % 2
    for p in range(parts):
        copy(0, p, slot).wait()

    @pl.when(j >= 2)
    def _():
        left(slot)

    for s in range(blocks * rows // SEQ):
        span = slice(s * SEQ, (s + 1) * SEQ)
        total = nt(lefts[0][span, :], held[slot, 0])
        for p in range(1, parts):
            total += nt(lefts[p][span, :], held[slot, p])
        ready[slot, span, :] = total.astype(BF16)
    column = pl.multiple_of(j % (n // 2) * depth, 128)
    for h in range(2):

        @pl.when((j >= n // 2) == (h == 1))
        def _():
            for k, (array, first) in enumerate(targets[h]):
                leave(slot, k, array, first, column).start()

    @pl.when(j == n - 1)
    def _():
        left(1 - slot)
        left(slot)


def times_trans(chain, parts, group):
    weights = [weight for _, weight in parts]
    n, depth, width = len(weights[0].pieces), weights[0].rows, weights[0].width
    rows = parts[0][0].shape[0]
    half = weights[0].model // 2
    size = rows // group.size
    messages = group.messages()
    shapes = [((size, half), BF16)] * 2
    targets = [{0: (0, 0)}, {0: (1, 0)}]
    for h in range(2):
        for keys in messages[h]:
            for i, k in enumerate(keys):
                targets[h][k] = (len(shapes), i * size)
            shapes.append(((len(keys) * size, half), BF16))
    targets = [[t[k] for k in range(group.size)] for t in targets]
    anywhere = pl.BlockSpec(memory_space=pl.ANY)
    outs = chain.call(
        functools.partial(trans_body, n, [weight.start for weight in weights], targets),
        (n,),
        [whole((rows, width))] * len(parts) + [anywhere] * (n * len(parts)),
        [anywhere] * len(shapes),
        shapes,
        flops=4 * rows * half * width * len(parts),
        scratch=[
            pltpu.VMEM((2, len(parts), depth, width), BF16),
            pltpu.VMEM((2, rows, depth), BF16),
            pltpu.SemaphoreType.DMA((2, len(parts))),
            pltpu.SemaphoreType.DMA((2, group.size)),
        ],
        moved=2 * (2 * rows * half + len(parts) * (rows + 2 * half) * width),
    )(*[left for left, _ in parts], *[piece for weight in weights for piece in weight.pieces])
    m = group.bits
    return outs[:2], [outs[2 : 2 + m], outs[2 + m :]]


def grad_body(parts, got, blocks, steps, *refs):
    lefts, refs = refs[:blocks], refs[blocks:]
    rights, refs = refs[:parts], refs[parts:]
    got_ref = refs[0] if got else None
    outs, turned = refs[got:-1], refs[-1]
    j = pl.program_id(0)

    @pl.when(j == 0)
    def _():
        rows = turned.shape[1] // blocks
        for k in range(blocks):
            turned[:, cut(rows, k)] = lefts[k][...].T

    for i in range(parts):

        @pl.when((j >= i * steps) & (j < (i + 1) * steps))
        def _():
            total = nn(turned[...], rights[i][...])
            if got:
                total += got_ref[...].astype(F32)
            total = total.astype(BF16)
            first = 0
            for out_ref in outs:
                count = out_ref.shape[0]
                out_ref[...] = total[first : first + count]
                first += count


def weight_grads(chain, left, which, rights, got=None, bits=0):
    rows, width = rights[0].shape
    parts = len(rights)
    tile = min(512, width)
    steps = width // tile
    if isinstance(left, list):
        lefts = [block[0] if len(block) == 1 else block[which] for block in left]
        half = left[0][0].shape[1] // 2
        places = [which if len(block) == 1 else 0 for block in left]
    else:
        lefts, places, half = [left], [which], left.shape[1] // 2
    blocks = len(lefts)
    ins = [
        pl.BlockSpec((rows // blocks, half), functools.partial(lambda at, j: (0, at), at))
        for at in places
    ]
    for i in range(parts):
        ins.append(
            pl.BlockSpec(
                (rows, tile),
                functools.partial(
                    lambda first, j: (0, jnp.clip(j - first, 0, steps - 1)), i * steps
                ),
            )
        )
    column = lambda j: (0, j)
    more = [] if got is None else [got]
    sizes = [half >> bits]
    for p in range(bits):
        sizes += [sizes[0], ((1 << p) - 1) * sizes[0]] if p else [sizes[0]]
    return chain.call(
        functools.partial(grad_body, parts, len(more), blocks, steps),
        (parts * steps,),
        ins + [pl.BlockSpec((half, tile), column)] * len(more),
        [pl.BlockSpec((size, tile), column) for size in sizes],
        [((size, parts * width), BF16) for size in sizes],
        flops=2 * rows * half * width * parts,
        scratch=[pltpu.VMEM((half, rows), BF16)],
        moved=2 * (rows * half + parts * (rows + half) * width),
    )(*lefts, *rights, *more)


def causal(scores):
    past = scores.shape[0] - HALF_SEQ
    key = lax.broadcasted_iota(jnp.int32, (HALF_SEQ, HALF_SEQ), 0)
    query = lax.broadcasted_iota(jnp.int32, (HALF_SEQ, HALF_SEQ), 1)
    last = jnp.where(key <= query, scores[past:], -1e30)
    return last if past == 0 else jnp.concatenate([scores[:past], last], axis=0)


def head_of(h):
    return slice(h * HEAD_DIM, (h + 1) * HEAD_DIM)


def span_of(b):
    return slice(b * HALF_SEQ, (b + 1) * HALF_SEQ)


def in_place(shift_ref, ref, count):
    rows = SEQ // count
    spans = [pl.ds(pl.multiple_of((i ^ shift_ref[0]) * rows, rows), rows) for i in range(count)]
    return jnp.concatenate([ref[span, :] for span in spans], axis=0)


def put_back(shift_ref, ref, count, values):
    rows = SEQ // count
    for i in range(count):
        ref[pl.ds(pl.multiple_of((i ^ shift_ref[0]) * rows, rows), rows), :] = values[cut(rows, i)]


def attend_body(count, shift_ref, q_ref, k_ref, v_ref, out_ref, sum_ref):
    queries, keys = in_place(shift_ref, q_ref, count), in_place(shift_ref, k_ref, count)
    values = in_place(shift_ref, v_ref, count).astype(F32).T.astype(BF16)
    heads = []
    for h in range(2):
        blocks = []
        for b in range(2):
            reach = (b + 1) * HALF_SEQ
            query = queries[span_of(b), head_of(h)] * BF16(FACTOR)
            scores = causal(nt(keys[:reach, head_of(h)], query))
            top = jnp.max(scores, axis=0, keepdims=True)
            expo = jnp.exp(scores - top)
            total = jnp.sum(expo, axis=0, keepdims=True)
            mixed = nn(values[head_of(h), :reach], expo.astype(BF16))
            blocks.append(mixed * (1.0 / total))
            sum_ref[0, 0, h : h + 1, span_of(b)] = top + jnp.log(total)
        heads.append(jnp.concatenate(blocks, axis=1))
    put_back(shift_ref, out_ref, count, jnp.concatenate(heads, axis=0).T.astype(BF16))


def attend(chain, shift, count, query, key, value):
    rows, width = query.shape
    seqs, pairs = rows // SEQ, width // PAIR
    tile = pl.BlockSpec((SEQ, PAIR), lambda s, p, _: (s, p))
    return chain.call(
        functools.partial(attend_body, count),
        (seqs, pairs),
        [tile] * 3,
        [tile, pl.BlockSpec((1, 1, 2, SEQ), lambda s, p, _: (s, p, 0, 0))],
        [((rows, width), BF16), ((seqs, pairs, 2, SEQ), F32)],
        flops=16 * rows * width * SEQ,
        prefetch=1,
        moved=8 * rows * width,
    )(shift, query, key, value)


def attend_back_body(
    count, shift_ref, q_ref, k_ref, v_ref, g_ref, sum_ref, cos_ref, sin_ref, dq_ref, dk_ref, dv_ref
):
    queries, keys, values, grads = (
        in_place(shift_ref, ref, count) for ref in (q_ref, k_ref, v_ref, g_ref)
    )
    turned = keys.astype(F32).T.astype(BF16)
    dq_heads, dk_heads, dv_heads = [], [], []
    for h in range(2):
        dq, dk, dv = [], [], []
        for b in range(2):
            reach = (b + 1) * HALF_SEQ
            query = queries[span_of(b), head_of(h)]
            grad = grads[span_of(b), head_of(h)]
            scores = causal(nt(keys[:reach, head_of(h)], query * BF16(FACTOR)))
            probs = jnp.exp(scores - sum_ref[0, 0, h : h + 1, span_of(b)])
            probs_grad = nt(values[:reach, head_of(h)], grad)
            inner = jnp.sum(probs * probs_grad, axis=0, keepdims=True)
            score_grad = (probs * (probs_grad - inner)).astype(BF16)
            dv.append(nn(probs.astype(BF16), grad))
            dk.append(nn(score_grad, query))
            dq.append(nn(turned[head_of(h), :reach], score_grad))
        for parts, heads in ((dk, dk_heads), (dv, dv_heads)):
            heads.append(
                jnp.concatenate([parts[1][:HALF_SEQ] + parts[0], parts[1][HALF_SEQ:]], axis=0)
            )
        dq_heads.append(jnp.concatenate(dq, axis=1))
    dq = jnp.concatenate(dq_heads, axis=0).T * FACTOR
    dk = jnp.concatenate(dk_heads, axis=1) * FACTOR
    dv = jnp.concatenate(dv_heads, axis=1).astype(BF16)
    cosine, sine = cos_ref[...], sin_ref[...]
    put_back(shift_ref, dq_ref, count, (dq * cosine - turn(dq) * sine).astype(BF16))
    put_back(shift_ref, dk_ref, count, (dk * cosine - turn(dk) * sine).astype(BF16))
    put_back(shift_ref, dv_ref, count, dv)


def attend_back(chain, shift, count, query, key, value, grad, logsum, tables):
    rows, width = query.shape
    seqs, pairs = rows // SEQ, width // PAIR
    tile = pl.BlockSpec((SEQ, PAIR), lambda s, p, _: (s, p))
    return chain.call(
        functools.partial(attend_back_body, count),
        (seqs, pairs),
        [tile] * 4
        + [pl.BlockSpec((1, 1, 2, SEQ), lambda s, p, _: (s, p, 0, 0))]
        + [whole((SEQ, PAIR))] * 2,
        [tile] * 3,
        [((rows, width), BF16)] * 3,
        flops=40 * rows * width * SEQ,
        prefetch=1,
        moved=14 * rows * width,
    )(shift, query, key, value, grad, logsum, *tables)


def local(
    chips,
    group,
    tokens,
    attn_gain,
    query_weight,
    key_weight,
    value_weight,
    output_weight,
    ffn_gain,
    gate_weight,
    up_weight,
    down_weight,
    cotangent,
):
    line = jnp.asarray(chips.table)[lax.axis_index("dp")]
    rows, model = tokens.shape
    count = SEQ // rows
    shift = lax.axis_index("tensor") % count
    row = jnp.arange(SEQ, dtype=jnp.int32)
    places = rope_tables(row)
    tables = rope_tables((row // rows ^ shift) * rows + row % rows)
    shift = jnp.reshape(shift, (1,)).astype(jnp.int32)
    early = (*places, *tables, line, shift)
    depth, own = query_weight.shape
    hidden_units = gate_weight.shape[1]
    chain = Chain()

    def gather(piece):
        return Gather(chips, chain, chain.join(piece)[0])

    def spread_of(values):
        return Spread(group, chain, chain.join(values)[0])

    def fold_of(part):
        own_part, sent = part
        sent = chain.join(*sent[0], *sent[1])
        return Fold(group, chain, own_part, [sent[: group.bits], sent[group.bits :]])

    def grads_of(left, rights):
        got = [None]
        chain.ask(weight_grads(chain, left, 1, rights)[0], got, 0, chips.other)

        def mine(**how):
            if got[0] is None:
                chain.flush()
            blocks = weight_grads(chain, left, 0, rights, got[0], chips.bits)
            return Sums(chips, chain, blocks, **how)

        return mine

    extra = jnp.concatenate([attn_gain, ffn_gain, jnp.zeros((4 * own - 2 * depth,), BF16)])
    attn = jnp.concatenate([query_weight, key_weight, value_weight, output_weight.T], axis=1)
    attn = gather(jnp.concatenate([attn, jnp.broadcast_to(extra, (16, 4 * own))], axis=0))
    spread = spread_of(tokens)
    grads_spread = spread_of(cotangent)
    grads_spread.later = []
    down_turned, *early = chain.join(down_weight.T, *early)
    places, tables, line, shift = early[:2], early[2:4], early[4], early[5]
    chain.end(attn, spread, grads_spread)
    chain.end(attn, spread)
    all_tokens = spread.blocks()
    attn = attn.pieces()
    pair = gather(jnp.concatenate([gate_weight, up_weight], axis=1))
    w_query, w_key, w_value, w_output = [Weight(attn, depth, i * own, own) for i in range(4)]
    gains = jnp.concatenate(
        [piece[depth : depth + 1, : 2 * depth].reshape(2, depth) for piece in attn], axis=1
    ).astype(F32)

    group_one = ordered(chain, norm_body, line, gains, all_tokens)
    grads_spread.resume()
    query, key, value = project(chain, group_one, tables, w_query, w_key, w_value)
    mixed, logsum = attend(chain, shift, count, query, key, value)
    out_part = times_trans(chain, [(mixed, w_output)], group)
    fold = fold_of(out_part)
    chain.end(fold, pair, grads_spread)
    grad_rows = ordered(chain, order_body, line, gains, grads_spread.blocks())
    chain.end(fold)
    attended = fold.total()
    middle, second = by_rows(
        chain, middle_body, line, tokens, gains, attended, [], [F32, BF16]
    )
    spread = spread_of(second)
    chain.end(spread, pair)
    pair = pair.pieces()
    down = gather(down_turned)
    chain.end(spread)
    group_two = spread.blocks()
    w_gate = Weight(pair, depth, 0, hidden_units)
    w_up = Weight(pair, depth, hidden_units, hidden_units)
    hidden, slope, silu = gate_up(chain, group_two, w_gate, w_up)

    mine = grads_of(grad_rows, [hidden])
    chain.end(down)
    chain.flush()
    down_sum = mine()
    w_down = Weight(down.pieces(), depth, 0, hidden_units)
    gate_grad, up_grad = hidden_back(chain, grad_rows, w_down, slope, silu)
    mine_gate = grads_of(group_two, [gate_grad])
    chain.end(down_sum)
    second_part = times_trans(chain, [(gate_grad, w_gate), (up_grad, w_up)], group)
    mine_up = grads_of(group_two, [up_grad])
    gate_sum = mine_gate(hold=True)
    chain.end(down_sum)
    fold = fold_of(second_part)
    up_sum = mine_up(apart=True)
    chain.end(gate_sum, fold)
    result_part = times_trans(chain, [(hidden, w_down)], group)
    chain.end(fold)
    second_grad = fold.total()
    middle_grad, low_grad = by_rows(
        chain, second_back_body, line, cotangent, gains, second_grad, [middle], [F32, BF16]
    )
    spread = spread_of(low_grad)
    chain.end(up_sum)
    gate_sum.resume()
    (down_sum,) = finish(chain, down_sum.terms())
    chain.end(spread)
    attn_grads = spread.blocks()

    mixed_grad = mixed_back(chain, attn_grads, w_output)
    mine_out = grads_of(attn_grads, [mixed])
    chain.end(gate_sum)
    up_sum.send_half(0)
    fold = fold_of(result_part)
    query_back, key_back, value_back = attend_back(
        chain, shift, count, query, key, value, mixed_grad, logsum, places
    )
    chain.end(up_sum, fold)
    up_sum.send_half(1)
    mine_qkv = grads_of(group_one, [query_back, key_back, value_back])
    chain.flush()
    first_part = times_trans(
        chain, [(query_back, w_query), (key_back, w_key), (value_back, w_value)], group
    )
    qkv_sum = mine_qkv()
    chain.end(up_sum, fold)
    result_part = fold.total()
    out_sum = mine_out(hold=True)
    (layer_out,) = by_rows(chain, result_body, line, middle, gains, result_part, [], [BF16])
    gate_sum, gate_inner = finish(chain, gate_sum.terms(), [gate_weight])
    chain.end(qkv_sum, out_sum)
    fold = fold_of(first_part)
    up_sum, up_inner = finish(chain, up_sum.terms(), [up_weight])
    chain.end(fold)
    chain.end(fold)
    first_grad = fold.total()
    (input_grad,) = by_rows(
        chain, first_back_body, line, tokens, gains, first_grad, [middle_grad], [F32]
    )
    chain.end(qkv_sum)
    out_sum.resume()
    query_sum, key_sum, value_sum, qkv_inner = finish(
        chain, qkv_sum.terms(), [query_weight, key_weight, value_weight]
    )
    gain_one_total, gain_two_total = lax.psum(
        (
            qkv_inner / attn_gain.astype(F32),
            (gate_inner + up_inner) / ffn_gain.astype(F32),
        ),
        "tensor",
    )
    (gain_one_total,) = chain.join(gain_one_total)
    (out_sum,) = finish(chain, out_sum.terms())
    return (
        layer_out,
        input_grad,
        gain_one_total,
        query_sum,
        key_sum,
        value_sum,
        out_sum,
        gain_two_total,
        gate_sum,
        up_sum,
        down_sum,
    )


def solution(mesh):
    in_specs = (
        P(("dp", "tensor"), None),
        P("dp"),
        P("dp", "tensor"),
        P("dp", "tensor"),
        P("dp", "tensor"),
        P("tensor", "dp"),
        P("dp"),
        P("dp", "tensor"),
        P("dp", "tensor"),
        P("tensor", "dp"),
        P(("dp", "tensor"), None),
    )
    out_specs = (
        P(("dp", "tensor"), None),
        P(("dp", "tensor"), None),
        P("dp"),
        P("dp", "tensor"),
        P("dp", "tensor"),
        P("dp", "tensor"),
        P("tensor", "dp"),
        P("dp"),
        P("dp", "tensor"),
        P("dp", "tensor"),
        P("tensor", "dp"),
    )
    chips = Chips(mesh.shape["dp"])
    size = mesh.shape["tensor"]
    links = [[(i, i ^ 1 << b) for i in range(size)] for b in range(size.bit_length() - 1)]
    group = Group(links, "tensor")

    def run(*arrays):
        return local(chips, group, *arrays)

    return jax.shard_map(run, mesh=mesh, in_specs=in_specs, out_specs=out_specs, check_vma=False)
```

```python
import functools

import jax
import jax.numpy as jnp
import numpy as np
from jax import lax
from jax.experimental import pallas as pl
from jax.experimental.pallas import tpu as pltpu
from jax.sharding import PartitionSpec as P

HEAD_DIM = 64
SEQ = 512
EPS = 1e-05
THETA = 130000.0
BF16 = jnp.bfloat16
F32 = jnp.float32
FACTOR = HEAD_DIM**-0.5
PAIR = 2 * HEAD_DIM
HALF_SEQ = SEQ // 2
VMEM_LIMIT = 58 << 20
COST_SHARE = 4096


class Chain:
    def __init__(self):
        self.token = jnp.zeros((8, 128), F32)
        self.swaps, self.asked = [], []

    def join(self, *values):
        *values, self.token = lax.optimization_barrier((*values, self.token))
        return values

    def gate(self, *values):
        swaps, self.swaps = self.swaps, []
        asked, self.asked = self.asked, []
        joined = self.join(
            *values, *[held[i] for held, i in swaps], *[source for source, _, _, _ in asked]
        )
        for (held, i), value in zip(swaps, joined[len(values) :]):
            held[i] = value
        for (_, held, i, swap), value in zip(asked, joined[len(values) + len(swaps) :]):
            held[i] = swap(value)
            self.swaps.append((held, i))
        return joined[: len(values)]

    def end(self, *transfers):
        counts = [len(t.flying) for t in transfers]
        got = self.gate(*[value for t in transfers for value in t.flying])
        for t, count in zip(transfers, counts):
            if count:
                t.go_on(got[:count])
            got = got[count:]

    def ask(self, source, held, i, swap):
        self.asked.append((source, held, i, swap))

    def flush(self):
        for source, held, i, swap in self.asked:
            held[i] = swap(source)
        self.asked = []

    def call(self, body, grid, ins, outs, shapes, flops, scratch=(), prefetch=0, moved=0):
        first = prefetch + len(ins)
        second = first + 1 + len(outs)
        anywhere = pl.BlockSpec(memory_space=pl.ANY)

        def wrapped(*refs):
            body(*refs[:first], *refs[first + 1 : second], *refs[second + 1 :])

        run = pl.pallas_call(
            wrapped,
            grid_spec=pltpu.PrefetchScalarGridSpec(
                num_scalar_prefetch=prefetch,
                grid=grid,
                in_specs=[*ins, anywhere],
                out_specs=[*outs, anywhere],
                scratch_shapes=list(scratch),
            ),
            out_shape=[jax.ShapeDtypeStruct(s, t) for s, t in [*shapes, ((8, 128), F32)]],
            compiler_params=pltpu.CompilerParams(
                vmem_limit_bytes=VMEM_LIMIT, dimension_semantics=("arbitrary",) * len(grid)
            ),
            cost_estimate=pl.CostEstimate(
                flops=flops // COST_SHARE, bytes_accessed=moved // COST_SHARE, transcendentals=0
            ),
        )

        def with_token(*args):
            *results, self.token = run(*args, self.token)
            return results

        return with_token


class Chips:
    def __init__(self, size):
        self.bits = (size // 2).bit_length() - 1
        self.size = size
        self.swap = [(i, i ^ 1) for i in range(size)]
        self.links = [
            [(i, i ^ 2 << self.bits - 1 - p) for i in range(size)] for p in range(self.bits)
        ]
        flips = [
            sum(1 << self.bits - 1 - p for p in range(self.bits) if v >> p & 1)
            for v in range(1 << self.bits)
        ]
        table = [[i ^ 2 * f for f in flips] + [i ^ 2 * f ^ 1 for f in flips] for i in range(size)]
        self.table = np.array(table, np.int32)

    def send(self, value, p):
        return lax.ppermute(value, "dp", self.links[p])

    def other(self, value):
        return lax.ppermute(value, "dp", self.swap)


class Gather:
    def __init__(self, chips, chain, piece):
        self.chips, self.chain = chips, chain
        self.own = [piece] + [None] * (2**chips.bits - 1)
        self.others = list(self.own)
        self.ask(0)
        self.keys = [1 << p for p in range(chips.bits)]
        self.flying = [chips.send(piece, p) for p in range(chips.bits)]

    def ask(self, v):
        self.chain.ask(self.own[v], self.others, v, self.chips.other)

    def go_on(self, got):
        keys, self.keys, self.flying = self.keys, [], []
        for v, piece in zip(keys, got):
            self.own[v] = piece
            for p in range(v.bit_length(), self.chips.bits):
                self.keys.append(v | 1 << p)
                self.flying.append(self.chips.send(piece, p))
        for v in keys:
            self.ask(v)

    def pieces(self):
        while self.flying:
            self.chain.end(self)
        self.chain.flush()
        return self.own + self.others


class Sums:
    def __init__(self, chips, chain, mine, apart=False, hold=False):
        self.chips, self.chain, self.apart, self.hold = chips, chain, apart, hold
        self.todo = []
        self.parts = [mine[0]]
        mine = list(mine[1:])
        self.direct, self.passed = [], []
        for p in range(chips.bits):
            self.direct.append(mine.pop(0))
            self.passed.append(mine.pop(0) if p else None)
        self.p = chips.bits - 1
        self.kinds = [self.p]
        self.flying = [chips.send(self.passed[self.p], self.p)]

    def go_on(self, got):
        rows = self.parts[0].shape[0]
        kinds, self.kinds, self.flying = self.kinds, [], []
        if self.p == 0:
            self.parts += got
            return
        for kind, block in zip(kinds, got):
            if kind is None:
                self.parts.append(block)
                continue
            add = lambda held, first: (
                held.astype(F32) + block[first * rows : first * rows + held.shape[0]].astype(F32)
            ).astype(BF16)
            for q in range(kind):
                self.direct[q] = add(self.direct[q], (1 << q) - 1)
                if q:
                    self.passed[q] = add(self.passed[q], 1 << q)
        p, self.p = self.p, self.p - 1
        if p > 0:
            self.todo.append((None, self.direct[p], p))
        if p > 1:
            self.todo.append((p - 1, self.passed[p - 1], p - 1))
        if p == 1 and not self.apart:
            self.todo.append((None, self.direct[0], 0))
        if not self.hold:
            self.resume()

    def resume(self):
        todo, self.todo = self.todo, []
        values = self.chain.join(*[value for _, value, _ in todo])
        for (kind, _, p), value in zip(todo, values):
            self.kinds.append(kind)
            self.flying.append(self.chips.send(value, p))

    def send_half(self, i):
        while self.p > 0:
            self.chain.end(self)
        width = self.direct[0].shape[1] // 2
        (value,) = self.chain.join(self.direct[0][:, i * width : (i + 1) * width])
        self.kinds.append(None)
        self.flying.append(self.chips.send(value, 0))

    def terms(self):
        while self.flying or self.todo:
            if self.todo:
                self.resume()
            self.chain.end(self)
        return sorted(self.parts, key=lambda part: -part.shape[1])


class Group:
    def __init__(self, links, axes):
        self.links, self.axes = links, axes
        self.bits = len(links)
        self.size = 1 << self.bits
        self.orders = (list(range(self.bits)), list(range(self.bits))[::-1])

    def send(self, value, bit):
        return lax.ppermute(value, self.axes, self.links[bit])

    def messages(self):
        found = []
        for order in self.orders:
            found.append([])
            for top in reversed(range(self.bits)):
                found[-1].append(
                    [
                        1 << order[top] | sum(1 << order[p] for p in range(top) if v >> p & 1)
                        for v in range(1 << top)
                    ]
                )
        return found


class Spread:
    def __init__(self, group, chain, rows):
        self.group, self.chain = group, chain
        self.held = {0: [rows]}
        self.later = None
        self.keys = [(1 << b, None) for b in range(group.bits)]
        self.flying = [group.send(rows, b) for b in range(group.bits)]

    def go_on(self, got):
        fresh = list(zip(self.keys, got))
        self.keys, self.flying = [], []
        for (k, h), block in fresh:
            if h is None:
                self.held[k] = [block]
            else:
                self.held.setdefault(k, [None, None])[h] = block
        for (k, h), block in fresh:
            for way, order in enumerate(self.group.orders):
                if h is not None and h != way:
                    continue
                half = block.shape[1] // 2
                top = max(i for i, bit in enumerate(order) if k >> bit & 1)
                for i in range(top + 1, len(order)):
                    part = block if h is not None else block[:, way * half : (way + 1) * half]
                    self.keys.append((k | 1 << order[i], way))
                    if self.later is not None:
                        self.later.append((part, order[i]))
                    else:
                        self.flying.append(self.group.send(part, order[i]))

        if self.later:
            parts = self.chain.join(*[part for part, _ in self.later])
            self.later = [(part, bit) for part, (_, bit) in zip(parts, self.later)]

    def resume(self):
        later, self.later = self.later, None
        parts = self.chain.join(*[part for part, _ in later])
        self.flying = [self.group.send(part, bit) for part, (_, bit) in zip(parts, later)]

    def blocks(self):
        while self.flying:
            self.chain.end(self)
        return [self.held[k] for k in range(self.group.size)]


class Fold:
    def __init__(self, group, chain, own, sent):
        self.group, self.chain = group, chain
        self.rows = own[0].shape[0]
        self.sent = [list(half) for half in sent]
        self.parts = [[half] for half in own]
        self.wave = 0
        self.start()

    def start(self):
        self.flying = [
            self.group.send(self.sent[h][self.wave], order[self.group.bits - 1 - self.wave])
            for h, order in enumerate(self.group.orders)
        ]

    def go_on(self, got):
        self.wave += 1
        self.flying = []
        for h, block in enumerate(got):
            self.parts[h].append(block)
            for wave in range(self.wave, self.group.bits):
                first = self.rows << (self.group.bits - 1 - wave)
                more = block[first : 2 * first].astype(F32)
                self.sent[h][wave] = (self.sent[h][wave].astype(F32) + more).astype(BF16)
        if self.wave < self.group.bits:
            now = self.chain.join(*[sent[self.wave] for sent in self.sent])
            for sent, value in zip(self.sent, now):
                sent[self.wave] = value
            self.start()

    def total(self):
        while self.flying:
            self.chain.end(self)
        return self.parts


class Weight:
    def __init__(self, pieces, rows, start, width):
        self.pieces, self.rows, self.start, self.width = pieces, rows, start, width
        self.model = len(pieces) * rows

    def tiles(self, tile):
        first = self.start // tile
        return [pl.BlockSpec((self.rows, tile), lambda j: (0, first + j))] * len(self.pieces)


def nn(left, right):
    return lax.dot_general(left, right, (((1,), (0,)), ((), ())), preferred_element_type=F32)


def nt(left, right):
    return lax.dot_general(left, right, (((1,), (1,)), ((), ())), preferred_element_type=F32)


def tn(left, right):
    return lax.dot_general(left, right, (((0,), (0,)), ((), ())), preferred_element_type=F32)


def whole(shape):
    return pl.BlockSpec(shape, lambda *_: (0,) * len(shape))


def place(line_ref, j, width):
    return pl.ds(pl.multiple_of(line_ref[j] * width, 128), width)


def cut(width, j):
    return slice(j * width, (j + 1) * width)


def scale_of(values):
    return lax.rsqrt(jnp.mean(values * values, axis=-1, keepdims=True) + EPS)


def fetch_blocks(counts, refs, held, sems, k, slot, wait):
    first = 0
    for i, count in enumerate(counts):
        copies = []
        half = held.shape[2] // count
        for h in range(count):
            target = held.at[slot, :, pl.ds(h * half, half)]
            copies.append(pltpu.make_async_copy(refs[first + h], target, sems.at[slot, h]))
        first += count

        @pl.when(k == i)
        def _():
            for copy in copies:
                copy.wait() if wait else copy.start()


def fetched(counts, refs, held, sems):
    k = pl.program_id(0)

    @pl.when(k == 0)
    def _():
        fetch_blocks(counts, refs, held, sems, k, 0, False)

    fetch_blocks(counts, refs, held, sems, k + 1, (k + 1) % 2, False)
    fetch_blocks(counts, refs, held, sems, k, k % 2, True)
    return held.at[k % 2]


def norm_body(blocks, counts, line_ref, gain_ref, *refs):
    out_ref, held, sems = refs[sum(counts) :]
    x_ref = fetched(counts, refs, held, sems)
    width = out_ref.shape[1] // blocks
    scale = scale_of(x_ref[...].astype(F32))
    for j in range(blocks):
        part = x_ref[:, place(line_ref, j, width)].astype(F32)
        gain = gain_ref[0:1, cut(width, j)]
        out_ref[:, cut(width, j)] = (part * scale * gain).astype(BF16)


def order_body(blocks, counts, line_ref, gain_ref, *refs):
    out_ref, held, sems = refs[sum(counts) :]
    x_ref = fetched(counts, refs, held, sems)
    width = out_ref.shape[1] // blocks
    for j in range(blocks):
        out_ref[:, cut(width, j)] = x_ref[:, place(line_ref, j, width)]


def ordered(chain, body, line, gains, held):
    counts = [len(block) for block in held]
    rows, model = held[0][0].shape
    n = len(held)
    return chain.call(
        functools.partial(body, line.shape[0], counts),
        (n,),
        [whole(gains.shape)] + [pl.BlockSpec(memory_space=pl.ANY)] * sum(counts),
        [pl.BlockSpec((rows, model), lambda k, *_: (k, 0))],
        [((n * rows, model), BF16)],
        flops=20 * n * rows * model,
        scratch=[pltpu.VMEM((2, rows, model), BF16), pltpu.SemaphoreType.DMA((2, 2))],
        prefetch=1,
        moved=4 * n * rows * model,
    )(line, gains, *[array for block in held for array in block])[0]


def added(refs, span):
    total = refs[0][span, :].astype(F32)
    for ref in refs[1:]:
        total += ref[span, :].astype(F32)
    return total


def middle_body(blocks, m, line_ref, x_ref, gain_ref, *refs):
    middle_ref, out_ref = refs[2 * m :]
    width = x_ref.shape[1] // blocks
    half = x_ref.shape[1] // 2
    span = slice(None)
    middle_ref[:, :half] = added(refs[:m], span)
    middle_ref[:, half:] = added(refs[m : 2 * m], span)
    for j in range(blocks):
        here = x_ref[:, place(line_ref, j, width)].astype(F32)
        middle_ref[:, cut(width, j)] += here
    middle = middle_ref[...]
    out_ref[...] = (middle * scale_of(middle) * gain_ref[1:2, :]).astype(BF16)


def result_body(blocks, m, line_ref, middle_ref, gain_ref, *refs):
    out_ref = refs[2 * m]
    width = middle_ref.shape[1] // blocks
    span = slice(None)
    total = middle_ref[...] + jnp.concatenate(
        [added(refs[:m], span), added(refs[m : 2 * m], span)], axis=1
    )
    for j in range(blocks):
        out_ref[:, place(line_ref, j, width)] = total[:, cut(width, j)].astype(BF16)


def second_back_body(blocks, m, line_ref, dy_ref, gain_ref, *refs):
    middle_ref, out_ref, low_ref = refs[2 * m :]
    width = dy_ref.shape[1] // blocks
    span = slice(None)
    grad = jnp.concatenate([added(refs[:m], span), added(refs[m : 2 * m], span)], axis=1)
    middle = middle_ref[...]
    scale = scale_of(middle)
    normed = middle * scale
    scaled = grad * gain_ref[1:2, :]
    out_ref[...] = scale * (scaled - normed * jnp.mean(scaled * normed, axis=-1, keepdims=True))
    for j in range(blocks):
        out_ref[:, cut(width, j)] += dy_ref[:, place(line_ref, j, width)].astype(F32)
    low_ref[...] = out_ref[...].astype(BF16)


def first_back_body(blocks, m, line_ref, x_ref, gain_ref, *refs):
    above_ref, out_ref = refs[2 * m :]
    width = x_ref.shape[1] // blocks
    span = slice(None)
    scale = scale_of(x_ref[...].astype(F32))
    normed = jnp.concatenate(
        [x_ref[:, place(line_ref, j, width)].astype(F32) for j in range(blocks)], axis=1
    ) * scale
    grad = jnp.concatenate([added(refs[:m], span), added(refs[m : 2 * m], span)], axis=1)
    scaled = grad * gain_ref[0:1, :]
    back = scale * (scaled - normed * jnp.mean(scaled * normed, axis=-1, keepdims=True))
    total = above_ref[...] + back
    for j in range(blocks):
        out_ref[:, place(line_ref, j, width)] = total[:, cut(width, j)]


def by_rows(chain, body, line, first, gains, parts, more, kinds):
    rows, model = first.shape
    half = model // 2
    tile = min(128, rows)
    row = pl.BlockSpec((tile, model), lambda i, *_: (i, 0))
    slim = pl.BlockSpec((tile, half), lambda i, *_: (i, 0))
    m = len(parts[0])
    return chain.call(
        functools.partial(body, line.shape[0], m),
        (rows // tile,),
        [row, whole(gains.shape)] + [slim] * (2 * m) + [row] * len(more),
        [row] * len(kinds),
        [((rows, model), kind) for kind in kinds],
        flops=20 * rows * model,
        prefetch=1,
        moved=rows * model * (2 * m + 4 * len(kinds)),
    )(line, first, gains, *parts[0], *parts[1], *more)


def finish_body(m, halves, n, *refs):
    total = added(refs[:m], slice(None))
    if halves:
        total += jnp.concatenate([ref[...].astype(F32) for ref in refs[m : m + halves]], axis=1)
    m += halves
    weights, outs = refs[m : m + n], refs[m + n :]
    if not n:
        outs[0][...] = total.T
        return
    width = weights[0].shape[1]
    inner = jnp.zeros((total.shape[0], 1), F32)
    for i in range(n):
        part = total[:, cut(width, i)]
        outs[i][...] = part
        inner += jnp.sum(weights[i][...].astype(F32) * part, axis=1, keepdims=True)
    outs[n][...] = jnp.broadcast_to(inner, outs[n].shape)


def finish(chain, terms, weights=()):
    rows, columns = terms[0].shape
    tile = min(128, rows)
    row = pl.BlockSpec((tile, columns), lambda i: (i, 0))
    n = len(weights)
    halves = sum(1 for term in terms if term.shape[1] < columns)
    half = [pl.BlockSpec((tile, columns // 2), lambda i: (i, 0))] * halves
    if n:
        slim = pl.BlockSpec((tile, columns // n), lambda i: (i, 0))
        outs = [slim] * n + [pl.BlockSpec((tile, 128), lambda i: (i, 0))]
        shapes = [((rows, columns // n), F32)] * n + [((rows, 128), F32)]
    else:
        slim = None
        outs = [pl.BlockSpec((columns, tile), lambda i: (0, i))]
        shapes = [((columns, rows), F32)]
    results = chain.call(
        functools.partial(finish_body, len(terms) - halves, halves, n),
        (rows // tile,),
        [row] * (len(terms) - halves) + half + [slim] * n,
        outs,
        shapes,
        flops=4 * rows * columns,
        moved=rows * columns * 12,
    )(*terms, *weights)
    if n:
        results[n] = results[n][:, 0]
    return results


def rope_tables(place):
    half = HEAD_DIM // 2
    freq = THETA ** (-2.0 * jnp.arange(half, dtype=F32) / HEAD_DIM)
    angle = place.astype(F32)[:, None] * freq[None, :]
    cosine, sine = jnp.cos(angle), jnp.sin(angle)
    return (
        jnp.concatenate([cosine] * (PAIR // half), axis=1),
        jnp.concatenate([-sine, sine] * (PAIR // HEAD_DIM), axis=1),
    )


def turn(values):
    half = HEAD_DIM // 2
    width = values.shape[-1]
    lane = lax.broadcasted_iota(jnp.int32, values.shape, 1) % HEAD_DIM
    return jnp.where(
        lane < half, pltpu.roll(values, width - half, 1), pltpu.roll(values, half, 1)
    )


def joined(refs):
    return jnp.concatenate([r[...] for r in refs], axis=0)


def qkv_body(n, x_ref, cos_ref, sin_ref, *refs):
    weights, outs = refs[: 3 * n], refs[3 * n :]
    rows = x_ref.shape[0]
    tile = outs[0].shape[1]
    for i in range(3):
        weight = joined(weights[i * n : (i + 1) * n])
        for s in range(rows // SEQ):
            span = slice(s * SEQ, (s + 1) * SEQ)
            product = nn(x_ref[span, :], weight)
            if i == 2:
                outs[i][span, :] = product.astype(BF16)
                continue
            for t in range(tile // PAIR):
                here = product[:, t * PAIR : (t + 1) * PAIR]
                turned = here * cos_ref[...] + turn(here) * sin_ref[...]
                outs[i][span, t * PAIR : (t + 1) * PAIR] = turned.astype(BF16)


def project(chain, x, tables, query, key, value):
    rows, model = x.shape
    n, width = len(query.pieces), query.width
    tile = min(256, width)
    out = pl.BlockSpec((rows, tile), lambda j: (0, j))
    return chain.call(
        functools.partial(qkv_body, n),
        (width // tile,),
        [whole(x.shape), whole((SEQ, PAIR)), whole((SEQ, PAIR))]
        + query.tiles(tile)
        + key.tiles(tile)
        + value.tiles(tile),
        [out] * 3,
        [((rows, width), BF16)] * 3,
        flops=6 * rows * model * width,
        moved=2 * (rows * model + 3 * model * width + 3 * rows * width),
    )(x, *tables, *query.pieces, *key.pieces, *value.pieces)


def collect(counts, refs, held, sems):
    rows = held.shape[0] // len(counts)
    copies = []
    for k, count in enumerate(counts):
        half = held.shape[1] // count
        for h in range(count):
            target = held.at[pl.ds(k * rows, rows), pl.ds(h * half, half)]
            i = len(copies)
            copies.append(pltpu.make_async_copy(refs[i], target, sems.at[i]))
    for copy in copies:
        copy.start()
    for copy in copies:
        copy.wait()


def gate_body(n, counts, *refs):
    m = sum(counts)
    gate_w, up_w = refs[m : m + n], refs[m + n : m + 2 * n]
    hidden_ref, slope_ref, silu_ref, x_ref, sems = refs[m + 2 * n :]

    @pl.when(pl.program_id(0) == 0)
    def _():
        collect(counts, refs, x_ref, sems)

    gate_weight, up_weight = joined(gate_w), joined(up_w)
    for s in range(x_ref.shape[0] // SEQ):
        span = slice(s * SEQ, (s + 1) * SEQ)
        gate = nn(x_ref[span, :], gate_weight)
        up = nn(x_ref[span, :], up_weight)
        sigm = jax.nn.sigmoid(gate)
        silu = gate * sigm
        hidden_ref[span, :] = (silu * up).astype(BF16)
        silu_ref[span, :] = silu.astype(BF16)
        slope_ref[span, :] = (up * sigm * (1.0 + gate * (1.0 - sigm))).astype(BF16)


def collected(held):
    counts = [len(block) for block in held]
    rows, model = held[0][0].shape
    scratch = [
        pltpu.VMEM((len(held) * rows, model), BF16),
        pltpu.SemaphoreType.DMA((sum(counts),)),
    ]
    arrays = [array for block in held for array in block]
    return counts, arrays, [pl.BlockSpec(memory_space=pl.ANY)] * len(arrays), scratch


def gate_up(chain, held, gate, up):
    counts, arrays, specs, scratch = collected(held)
    rows, model = scratch[0].shape
    n, width = len(gate.pieces), gate.width
    tile = min(256, width)
    out = pl.BlockSpec((rows, tile), lambda j: (0, j))
    return chain.call(
        functools.partial(gate_body, n, counts),
        (width // tile,),
        specs + gate.tiles(tile) + up.tiles(tile),
        [out] * 3,
        [((rows, width), BF16)] * 3,
        flops=4 * rows * model * width,
        scratch=scratch,
        moved=2 * (rows * model + 2 * model * width + 3 * rows * width),
    )(*arrays, *gate.pieces, *up.pieces)


def hidden_back_body(n, g_ref, *refs):
    weight = joined(refs[:n])
    slope_ref, silu_ref, gate_ref, up_ref = refs[n:]
    for s in range(g_ref.shape[0] // SEQ):
        span = slice(s * SEQ, (s + 1) * SEQ)
        grad = nn(g_ref[span, :], weight)
        gate_ref[span, :] = (grad * slope_ref[span, :].astype(F32)).astype(BF16)
        up_ref[span, :] = (grad * silu_ref[span, :].astype(F32)).astype(BF16)


def hidden_back(chain, grads, down, slope, silu):
    rows, model = grads.shape
    n, width = len(down.pieces), down.width
    tile = min(256, width)
    out = pl.BlockSpec((rows, tile), lambda j: (0, j))
    return chain.call(
        functools.partial(hidden_back_body, n),
        (width // tile,),
        [whole(grads.shape)] + down.tiles(tile) + [out] * 2,
        [out] * 2,
        [((rows, width), BF16)] * 2,
        flops=2 * rows * model * width,
        moved=2 * (rows * model + model * width + 4 * rows * width),
    )(grads, *down.pieces, slope, silu)


def mixed_back_body(n, counts, *refs):
    m = sum(counts)
    out_ref, x_ref, sems = refs[m + n :]

    @pl.when(pl.program_id(0) == 0)
    def _():
        collect(counts, refs, x_ref, sems)

    out_ref[...] = nn(x_ref[...], joined(refs[m : m + n])).astype(BF16)


def mixed_back(chain, held, out):
    counts, arrays, specs, scratch = collected(held)
    rows, model = scratch[0].shape
    n, width = len(out.pieces), out.width
    tile = min(256, width)
    return chain.call(
        functools.partial(mixed_back_body, n, counts),
        (width // tile,),
        specs + out.tiles(tile),
        [pl.BlockSpec((rows, tile), lambda j: (0, j))],
        [((rows, width), BF16)],
        flops=2 * rows * model * width,
        scratch=scratch,
        moved=2 * (rows * model + model * width + rows * width),
    )(*arrays, *out.pieces)[0]


def trans_body(n, starts, targets, *refs):
    parts, blocks = len(starts), len(targets[0])
    lefts = refs[:parts]
    pieces = refs[parts : parts * (n + 1)]
    outs = refs[parts * (n + 1) : -4]
    held, ready, sems, out_sems = refs[-4:]
    j = pl.program_id(0)
    depth, width = held.shape[2:]
    rows = ready.shape[1] // blocks

    def copy(i, p, slot):
        source = pieces[p * n + i].at[pl.ds(0, depth), pl.ds(starts[p], width)]
        return pltpu.make_async_copy(source, held.at[slot, p], sems.at[slot, p])

    def fetch(step, slot):
        for i in range(n):

            @pl.when(step == i)
            def _():
                for p in range(parts):
                    copy(i, p, slot).start()

    def leave(slot, k, array, first, column):
        target = outs[array].at[pl.ds(first, rows), pl.ds(column, depth)]
        source = ready.at[slot, pl.ds(k * rows, rows), :]
        return pltpu.make_async_copy(source, target, out_sems.at[slot, k])

    def left(slot):
        for k in range(blocks):
            leave(slot, k, 0, 0, 0).wait()

    @pl.when(j == 0)
    def _():
        fetch(j, 0)

    @pl.when(j + 1 < n)
    def _():
        fetch(j + 1, (j + 1) % 2)

    slot = j % 2
    for p in range(parts):
        copy(0, p, slot).wait()

    @pl.when(j >= 2)
    def _():
        left(slot)

    for s in range(blocks * rows // SEQ):
        span = slice(s * SEQ, (s + 1) * SEQ)
        total = nt(lefts[0][span, :], held[slot, 0])
        for p in range(1, parts):
            total += nt(lefts[p][span, :], held[slot, p])
        ready[slot, span, :] = total.astype(BF16)
    column = pl.multiple_of(j % (n // 2) * depth, 128)
    for h in range(2):

        @pl.when((j >= n // 2) == (h == 1))
        def _():
            for k, (array, first) in enumerate(targets[h]):
                leave(slot, k, array, first, column).start()

    @pl.when(j == n - 1)
    def _():
        left(1 - slot)
        left(slot)


def times_trans(chain, parts, group):
    weights = [weight for _, weight in parts]
    n, depth, width = len(weights[0].pieces), weights[0].rows, weights[0].width
    rows = parts[0][0].shape[0]
    half = weights[0].model // 2
    size = rows // group.size
    messages = group.messages()
    shapes = [((size, half), BF16)] * 2
    targets = [{0: (0, 0)}, {0: (1, 0)}]
    for h in range(2):
        for keys in messages[h]:
            for i, k in enumerate(keys):
                targets[h][k] = (len(shapes), i * size)
            shapes.append(((len(keys) * size, half), BF16))
    targets = [[t[k] for k in range(group.size)] for t in targets]
    anywhere = pl.BlockSpec(memory_space=pl.ANY)
    outs = chain.call(
        functools.partial(trans_body, n, [weight.start for weight in weights], targets),
        (n,),
        [whole((rows, width))] * len(parts) + [anywhere] * (n * len(parts)),
        [anywhere] * len(shapes),
        shapes,
        flops=4 * rows * half * width * len(parts),
        scratch=[
            pltpu.VMEM((2, len(parts), depth, width), BF16),
            pltpu.VMEM((2, rows, depth), BF16),
            pltpu.SemaphoreType.DMA((2, len(parts))),
            pltpu.SemaphoreType.DMA((2, group.size)),
        ],
        moved=2 * (2 * rows * half + len(parts) * (rows + 2 * half) * width),
    )(*[left for left, _ in parts], *[piece for weight in weights for piece in weight.pieces])
    m = group.bits
    return outs[:2], [outs[2 : 2 + m], outs[2 + m :]]


def grad_body(parts, got, blocks, steps, *refs):
    lefts, refs = refs[:blocks], refs[blocks:]
    rights, refs = refs[:parts], refs[parts:]
    got_ref = refs[0] if got else None
    outs, turned = refs[got:-1], refs[-1]
    j = pl.program_id(0)

    @pl.when(j == 0)
    def _():
        rows = turned.shape[1] // blocks
        for k in range(blocks):
            turned[:, cut(rows, k)] = lefts[k][...].T

    for i in range(parts):

        @pl.when((j >= i * steps) & (j < (i + 1) * steps))
        def _():
            total = nn(turned[...], rights[i][...])
            if got:
                total += got_ref[...].astype(F32)
            total = total.astype(BF16)
            first = 0
            for out_ref in outs:
                count = out_ref.shape[0]
                out_ref[...] = total[first : first + count]
                first += count


def weight_grads(chain, left, which, rights, got=None, bits=0):
    rows, width = rights[0].shape
    parts = len(rights)
    tile = min(512, width)
    steps = width // tile
    if isinstance(left, list):
        lefts = [block[0] if len(block) == 1 else block[which] for block in left]
        half = left[0][0].shape[1] // 2
        places = [which if len(block) == 1 else 0 for block in left]
    else:
        lefts, places, half = [left], [which], left.shape[1] // 2
    blocks = len(lefts)
    ins = [
        pl.BlockSpec((rows // blocks, half), functools.partial(lambda at, j: (0, at), at))
        for at in places
    ]
    for i in range(parts):
        ins.append(
            pl.BlockSpec(
                (rows, tile),
                functools.partial(
                    lambda first, j: (0, jnp.clip(j - first, 0, steps - 1)), i * steps
                ),
            )
        )
    column = lambda j: (0, j)
    more = [] if got is None else [got]
    sizes = [half >> bits]
    for p in range(bits):
        sizes += [sizes[0], ((1 << p) - 1) * sizes[0]] if p else [sizes[0]]
    return chain.call(
        functools.partial(grad_body, parts, len(more), blocks, steps),
        (parts * steps,),
        ins + [pl.BlockSpec((half, tile), column)] * len(more),
        [pl.BlockSpec((size, tile), column) for size in sizes],
        [((size, parts * width), BF16) for size in sizes],
        flops=2 * rows * half * width * parts,
        scratch=[pltpu.VMEM((half, rows), BF16)],
        moved=2 * (rows * half + parts * (rows + half) * width),
    )(*lefts, *rights, *more)


def causal(scores):
    past = scores.shape[0] - HALF_SEQ
    key = lax.broadcasted_iota(jnp.int32, (HALF_SEQ, HALF_SEQ), 0)
    query = lax.broadcasted_iota(jnp.int32, (HALF_SEQ, HALF_SEQ), 1)
    last = jnp.where(key <= query, scores[past:], -1e30)
    return last if past == 0 else jnp.concatenate([scores[:past], last], axis=0)


def head_of(h):
    return slice(h * HEAD_DIM, (h + 1) * HEAD_DIM)


def span_of(b):
    return slice(b * HALF_SEQ, (b + 1) * HALF_SEQ)


def in_place(shift_ref, ref, count):
    rows = SEQ // count
    spans = [pl.ds(pl.multiple_of((i ^ shift_ref[0]) * rows, rows), rows) for i in range(count)]
    return jnp.concatenate([ref[span, :] for span in spans], axis=0)


def put_back(shift_ref, ref, count, values):
    rows = SEQ // count
    for i in range(count):
        ref[pl.ds(pl.multiple_of((i ^ shift_ref[0]) * rows, rows), rows), :] = values[cut(rows, i)]


def attend_body(count, shift_ref, q_ref, k_ref, v_ref, out_ref, sum_ref):
    queries, keys = in_place(shift_ref, q_ref, count), in_place(shift_ref, k_ref, count)
    values = in_place(shift_ref, v_ref, count).astype(F32).T.astype(BF16)
    heads = []
    for h in range(2):
        blocks = []
        for b in range(2):
            reach = (b + 1) * HALF_SEQ
            query = queries[span_of(b), head_of(h)] * BF16(FACTOR)
            scores = causal(nt(keys[:reach, head_of(h)], query))
            top = jnp.max(scores, axis=0, keepdims=True)
            expo = jnp.exp(scores - top)
            total = jnp.sum(expo, axis=0, keepdims=True)
            mixed = nn(values[head_of(h), :reach], expo.astype(BF16))
            blocks.append(mixed * (1.0 / total))
            sum_ref[0, 0, h : h + 1, span_of(b)] = top + jnp.log(total)
        heads.append(jnp.concatenate(blocks, axis=1))
    put_back(shift_ref, out_ref, count, jnp.concatenate(heads, axis=0).T.astype(BF16))


def attend(chain, shift, count, query, key, value):
    rows, width = query.shape
    seqs, pairs = rows // SEQ, width // PAIR
    tile = pl.BlockSpec((SEQ, PAIR), lambda s, p, _: (s, p))
    return chain.call(
        functools.partial(attend_body, count),
        (seqs, pairs),
        [tile] * 3,
        [tile, pl.BlockSpec((1, 1, 2, SEQ), lambda s, p, _: (s, p, 0, 0))],
        [((rows, width), BF16), ((seqs, pairs, 2, SEQ), F32)],
        flops=16 * rows * width * SEQ,
        prefetch=1,
        moved=8 * rows * width,
    )(shift, query, key, value)


def attend_back_body(
    count, shift_ref, q_ref, k_ref, v_ref, g_ref, sum_ref, cos_ref, sin_ref, dq_ref, dk_ref, dv_ref
):
    queries, keys, values, grads = (
        in_place(shift_ref, ref, count) for ref in (q_ref, k_ref, v_ref, g_ref)
    )
    turned = keys.astype(F32).T.astype(BF16)
    dq_heads, dk_heads, dv_heads = [], [], []
    for h in range(2):
        dq, dk, dv = [], [], []
        for b in range(2):
            reach = (b + 1) * HALF_SEQ
            query = queries[span_of(b), head_of(h)]
            grad = grads[span_of(b), head_of(h)]
            scores = causal(nt(keys[:reach, head_of(h)], query * BF16(FACTOR)))
            probs = jnp.exp(scores - sum_ref[0, 0, h : h + 1, span_of(b)])
            probs_grad = nt(values[:reach, head_of(h)], grad)
            inner = jnp.sum(probs * probs_grad, axis=0, keepdims=True)
            score_grad = (probs * (probs_grad - inner)).astype(BF16)
            dv.append(nn(probs.astype(BF16), grad))
            dk.append(nn(score_grad, query))
            dq.append(nn(turned[head_of(h), :reach], score_grad))
        for parts, heads in ((dk, dk_heads), (dv, dv_heads)):
            heads.append(
                jnp.concatenate([parts[1][:HALF_SEQ] + parts[0], parts[1][HALF_SEQ:]], axis=0)
            )
        dq_heads.append(jnp.concatenate(dq, axis=1))
    dq = jnp.concatenate(dq_heads, axis=0).T * FACTOR
    dk = jnp.concatenate(dk_heads, axis=1) * FACTOR
    dv = jnp.concatenate(dv_heads, axis=1).astype(BF16)
    cosine, sine = cos_ref[...], sin_ref[...]
    put_back(shift_ref, dq_ref, count, (dq * cosine - turn(dq) * sine).astype(BF16))
    put_back(shift_ref, dk_ref, count, (dk * cosine - turn(dk) * sine).astype(BF16))
    put_back(shift_ref, dv_ref, count, dv)


def attend_back(chain, shift, count, query, key, value, grad, logsum, tables):
    rows, width = query.shape
    seqs, pairs = rows // SEQ, width // PAIR
    tile = pl.BlockSpec((SEQ, PAIR), lambda s, p, _: (s, p))
    return chain.call(
        functools.partial(attend_back_body, count),
        (seqs, pairs),
        [tile] * 4
        + [pl.BlockSpec((1, 1, 2, SEQ), lambda s, p, _: (s, p, 0, 0))]
        + [whole((SEQ, PAIR))] * 2,
        [tile] * 3,
        [((rows, width), BF16)] * 3,
        flops=40 * rows * width * SEQ,
        prefetch=1,
        moved=14 * rows * width,
    )(shift, query, key, value, grad, logsum, *tables)


def local(
    chips,
    group,
    tokens,
    attn_gain,
    query_weight,
    key_weight,
    value_weight,
    output_weight,
    ffn_gain,
    gate_weight,
    up_weight,
    down_weight,
    cotangent,
):
    line = jnp.asarray(chips.table)[lax.axis_index("dp")]
    rows, model = tokens.shape
    count = SEQ // rows
    shift = lax.axis_index("tensor") % count
    row = jnp.arange(SEQ, dtype=jnp.int32)
    places = rope_tables(row)
    tables = rope_tables((row // rows ^ shift) * rows + row % rows)
    shift = jnp.reshape(shift, (1,)).astype(jnp.int32)
    early = (*places, *tables, line, shift)
    depth, own = query_weight.shape
    hidden_units = gate_weight.shape[1]
    chain = Chain()

    def gather(piece):
        return Gather(chips, chain, chain.join(piece)[0])

    def spread_of(values):
        return Spread(group, chain, chain.join(values)[0])

    def fold_of(part):
        own_part, sent = part
        sent = chain.join(*sent[0], *sent[1])
        return Fold(group, chain, own_part, [sent[: group.bits], sent[group.bits :]])

    def grads_of(left, rights):
        got = [None]
        chain.ask(weight_grads(chain, left, 1, rights)[0], got, 0, chips.other)

        def mine(**how):
            if got[0] is None:
                chain.flush()
            blocks = weight_grads(chain, left, 0, rights, got[0], chips.bits)
            return Sums(chips, chain, blocks, **how)

        return mine

    extra = jnp.concatenate([attn_gain, ffn_gain, jnp.zeros((4 * own - 2 * depth,), BF16)])
    attn = jnp.concatenate([query_weight, key_weight, value_weight, output_weight.T], axis=1)
    attn = gather(jnp.concatenate([attn, jnp.broadcast_to(extra, (16, 4 * own))], axis=0))
    spread = spread_of(tokens)
    grads_spread = spread_of(cotangent)
    grads_spread.later = []
    down_turned, *early = chain.join(down_weight.T, *early)
    places, tables, line, shift = early[:2], early[2:4], early[4], early[5]
    chain.end(attn, spread, grads_spread)
    chain.end(attn, spread)
    all_tokens = spread.blocks()
    attn = attn.pieces()
    pair = gather(jnp.concatenate([gate_weight, up_weight], axis=1))
    w_query, w_key, w_value, w_output = [Weight(attn, depth, i * own, own) for i in range(4)]
    gains = jnp.concatenate(
        [piece[depth : depth + 1, : 2 * depth].reshape(2, depth) for piece in attn], axis=1
    ).astype(F32)

    group_one = ordered(chain, norm_body, line, gains, all_tokens)
    grads_spread.resume()
    query, key, value = project(chain, group_one, tables, w_query, w_key, w_value)
    mixed, logsum = attend(chain, shift, count, query, key, value)
    out_part = times_trans(chain, [(mixed, w_output)], group)
    fold = fold_of(out_part)
    chain.end(fold, pair, grads_spread)
    grad_rows = ordered(chain, order_body, line, gains, grads_spread.blocks())
    chain.end(fold)
    attended = fold.total()
    middle, second = by_rows(
        chain, middle_body, line, tokens, gains, attended, [], [F32, BF16]
    )
    spread = spread_of(second)
    chain.end(spread, pair)
    pair = pair.pieces()
    down = gather(down_turned)
    chain.end(spread)
    group_two = spread.blocks()
    w_gate = Weight(pair, depth, 0, hidden_units)
    w_up = Weight(pair, depth, hidden_units, hidden_units)
    hidden, slope, silu = gate_up(chain, group_two, w_gate, w_up)

    mine = grads_of(grad_rows, [hidden])
    chain.end(down)
    chain.flush()
    down_sum = mine()
    w_down = Weight(down.pieces(), depth, 0, hidden_units)
    gate_grad, up_grad = hidden_back(chain, grad_rows, w_down, slope, silu)
    mine_gate = grads_of(group_two, [gate_grad])
    chain.end(down_sum)
    second_part = times_trans(chain, [(gate_grad, w_gate), (up_grad, w_up)], group)
    mine_up = grads_of(group_two, [up_grad])
    gate_sum = mine_gate(hold=True)
    chain.end(down_sum)
    fold = fold_of(second_part)
    up_sum = mine_up(apart=True)
    chain.end(gate_sum, fold)
    result_part = times_trans(chain, [(hidden, w_down)], group)
    chain.end(fold)
    second_grad = fold.total()
    middle_grad, low_grad = by_rows(
        chain, second_back_body, line, cotangent, gains, second_grad, [middle], [F32, BF16]
    )
    spread = spread_of(low_grad)
    chain.end(up_sum)
    gate_sum.resume()
    (down_sum,) = finish(chain, down_sum.terms())
    chain.end(spread)
    attn_grads = spread.blocks()

    mixed_grad = mixed_back(chain, attn_grads, w_output)
    mine_out = grads_of(attn_grads, [mixed])
    chain.end(gate_sum)
    up_sum.send_half(0)
    fold = fold_of(result_part)
    query_back, key_back, value_back = attend_back(
        chain, shift, count, query, key, value, mixed_grad, logsum, places
    )
    mine_qkv = grads_of(group_one, [query_back, key_back, value_back])
    chain.end(up_sum, fold)
    up_sum.send_half(1)
    out_sum = mine_out(hold=True)
    qkv_sum = mine_qkv()
    first_part = times_trans(
        chain, [(query_back, w_query), (key_back, w_key), (value_back, w_value)], group
    )
    chain.end(up_sum, fold, out_sum)
    result_part = fold.total()
    (layer_out,) = by_rows(chain, result_body, line, middle, gains, result_part, [], [BF16])
    gate_sum, gate_inner = finish(chain, gate_sum.terms(), [gate_weight])
    chain.end(qkv_sum)
    fold = fold_of(first_part)
    out_sum.resume()
    up_sum, up_inner = finish(chain, up_sum.terms(), [up_weight])
    chain.end(fold)
    chain.end(fold)
    first_grad = fold.total()
    (input_grad,) = by_rows(
        chain, first_back_body, line, tokens, gains, first_grad, [middle_grad], [F32]
    )
    chain.end(qkv_sum)
    query_sum, key_sum, value_sum, qkv_inner = finish(
        chain, qkv_sum.terms(), [query_weight, key_weight, value_weight]
    )
    gain_one_total, gain_two_total = lax.psum(
        (
            qkv_inner / attn_gain.astype(F32),
            (gate_inner + up_inner) / ffn_gain.astype(F32),
        ),
        "tensor",
    )
    (gain_one_total,) = chain.join(gain_one_total)
    (out_sum,) = finish(chain, out_sum.terms())
    return (
        layer_out,
        input_grad,
        gain_one_total,
        query_sum,
        key_sum,
        value_sum,
        out_sum,
        gain_two_total,
        gate_sum,
        up_sum,
        down_sum,
    )


def solution(mesh):
    in_specs = (
        P(("dp", "tensor"), None),
        P("dp"),
        P("dp", "tensor"),
        P("dp", "tensor"),
        P("dp", "tensor"),
        P("tensor", "dp"),
        P("dp"),
        P("dp", "tensor"),
        P("dp", "tensor"),
        P("tensor", "dp"),
        P(("dp", "tensor"), None),
    )
    out_specs = (
        P(("dp", "tensor"), None),
        P(("dp", "tensor"), None),
        P("dp"),
        P("dp", "tensor"),
        P("dp", "tensor"),
        P("dp", "tensor"),
        P("tensor", "dp"),
        P("dp"),
        P("dp", "tensor"),
        P("dp", "tensor"),
        P("tensor", "dp"),
    )
    chips = Chips(mesh.shape["dp"])
    size = mesh.shape["tensor"]
    links = [[(i, i ^ 1 << b) for i in range(size)] for b in range(size.bit_length() - 1)]
    group = Group(links, "tensor")

    def run(*arrays):
        return local(chips, group, *arrays)

    return jax.shard_map(run, mesh=mesh, in_specs=in_specs, out_specs=out_specs, check_vma=False)
```

```python
import functools

import jax
import jax.numpy as jnp
import numpy as np
from jax import lax
from jax.experimental import pallas as pl
from jax.experimental.pallas import tpu as pltpu
from jax.sharding import PartitionSpec as P

HEAD_DIM = 64
SEQ = 512
EPS = 1e-05
THETA = 130000.0
BF16 = jnp.bfloat16
F32 = jnp.float32
FACTOR = HEAD_DIM**-0.5
PAIR = 2 * HEAD_DIM
HALF_SEQ = SEQ // 2
VMEM_LIMIT = 58 << 20
COST_SHARE = 4096


class Chain:
    def __init__(self):
        self.token = jnp.zeros((8, 128), F32)
        self.swaps, self.asked = [], []

    def join(self, *values):
        *values, self.token = lax.optimization_barrier((*values, self.token))
        return values

    def gate(self, *values):
        swaps, self.swaps = self.swaps, []
        asked, self.asked = self.asked, []
        joined = self.join(
            *values, *[held[i] for held, i in swaps], *[source for source, _, _, _ in asked]
        )
        for (held, i), value in zip(swaps, joined[len(values) :]):
            held[i] = value
        for (_, held, i, swap), value in zip(asked, joined[len(values) + len(swaps) :]):
            held[i] = swap(value)
            self.swaps.append((held, i))
        return joined[: len(values)]

    def end(self, *transfers):
        counts = [len(t.flying) for t in transfers]
        got = self.gate(*[value for t in transfers for value in t.flying])
        for t, count in zip(transfers, counts):
            if count:
                t.go_on(got[:count])
            got = got[count:]

    def ask(self, source, held, i, swap):
        self.asked.append((source, held, i, swap))

    def flush(self):
        for source, held, i, swap in self.asked:
            held[i] = swap(source)
        self.asked = []

    def call(self, body, grid, ins, outs, shapes, flops, scratch=(), prefetch=0, moved=0):
        first = prefetch + len(ins)
        second = first + 1 + len(outs)
        anywhere = pl.BlockSpec(memory_space=pl.ANY)

        def wrapped(*refs):
            body(*refs[:first], *refs[first + 1 : second], *refs[second + 1 :])

        run = pl.pallas_call(
            wrapped,
            grid_spec=pltpu.PrefetchScalarGridSpec(
                num_scalar_prefetch=prefetch,
                grid=grid,
                in_specs=[*ins, anywhere],
                out_specs=[*outs, anywhere],
                scratch_shapes=list(scratch),
            ),
            out_shape=[jax.ShapeDtypeStruct(s, t) for s, t in [*shapes, ((8, 128), F32)]],
            compiler_params=pltpu.CompilerParams(
                vmem_limit_bytes=VMEM_LIMIT, dimension_semantics=("arbitrary",) * len(grid)
            ),
            cost_estimate=pl.CostEstimate(
                flops=flops // COST_SHARE, bytes_accessed=moved // COST_SHARE, transcendentals=0
            ),
        )

        def with_token(*args):
            *results, self.token = run(*args, self.token)
            return results

        return with_token


class Chips:
    def __init__(self, size):
        self.bits = (size // 2).bit_length() - 1
        self.size = size
        self.swap = [(i, i ^ 1) for i in range(size)]
        self.links = [
            [(i, i ^ 2 << self.bits - 1 - p) for i in range(size)] for p in range(self.bits)
        ]
        flips = [
            sum(1 << self.bits - 1 - p for p in range(self.bits) if v >> p & 1)
            for v in range(1 << self.bits)
        ]
        table = [[i ^ 2 * f for f in flips] + [i ^ 2 * f ^ 1 for f in flips] for i in range(size)]
        self.table = np.array(table, np.int32)

    def send(self, value, p):
        return lax.ppermute(value, "dp", self.links[p])

    def other(self, value):
        return lax.ppermute(value, "dp", self.swap)


class Gather:
    def __init__(self, chips, chain, piece):
        self.chips, self.chain = chips, chain
        self.own = [piece] + [None] * (2**chips.bits - 1)
        self.others = list(self.own)
        self.ask(0)
        self.keys = [1 << p for p in range(chips.bits)]
        self.flying = [chips.send(piece, p) for p in range(chips.bits)]

    def ask(self, v):
        self.chain.ask(self.own[v], self.others, v, self.chips.other)

    def go_on(self, got):
        keys, self.keys, self.flying = self.keys, [], []
        for v, piece in zip(keys, got):
            self.own[v] = piece
            for p in range(v.bit_length(), self.chips.bits):
                self.keys.append(v | 1 << p)
                self.flying.append(self.chips.send(piece, p))
        for v in keys:
            self.ask(v)

    def pieces(self):
        while self.flying:
            self.chain.end(self)
        self.chain.flush()
        return self.own + self.others


class Sums:
    def __init__(self, chips, chain, mine, apart=False, hold=False):
        self.chips, self.chain, self.apart, self.hold = chips, chain, apart, hold
        self.todo = []
        self.parts = [mine[0]]
        mine = list(mine[1:])
        self.direct, self.passed = [], []
        for p in range(chips.bits):
            self.direct.append(mine.pop(0))
            self.passed.append(mine.pop(0) if p else None)
        self.p = chips.bits - 1
        self.kinds = [self.p]
        self.flying = [chips.send(self.passed[self.p], self.p)]

    def go_on(self, got):
        rows = self.parts[0].shape[0]
        kinds, self.kinds, self.flying = self.kinds, [], []
        if self.p == 0:
            self.parts += got
            return
        for kind, block in zip(kinds, got):
            if kind is None:
                self.parts.append(block)
                continue
            add = lambda held, first: (
                held.astype(F32) + block[first * rows : first * rows + held.shape[0]].astype(F32)
            ).astype(BF16)
            for q in range(kind):
                self.direct[q] = add(self.direct[q], (1 << q) - 1)
                if q:
                    self.passed[q] = add(self.passed[q], 1 << q)
        p, self.p = self.p, self.p - 1
        if p > 0:
            self.todo.append((None, self.direct[p], p))
        if p > 1:
            self.todo.append((p - 1, self.passed[p - 1], p - 1))
        if p == 1 and not self.apart:
            self.todo.append((None, self.direct[0], 0))
        if not self.hold:
            self.resume()

    def resume(self):
        todo, self.todo = self.todo, []
        values = self.chain.join(*[value for _, value, _ in todo])
        for (kind, _, p), value in zip(todo, values):
            self.kinds.append(kind)
            self.flying.append(self.chips.send(value, p))

    def send_half(self, i):
        while self.p > 0:
            self.chain.end(self)
        width = self.direct[0].shape[1] // 2
        (value,) = self.chain.join(self.direct[0][:, i * width : (i + 1) * width])
        self.kinds.append(None)
        self.flying.append(self.chips.send(value, 0))

    def terms(self):
        while self.flying or self.todo:
            if self.todo:
                self.resume()
            self.chain.end(self)
        return sorted(self.parts, key=lambda part: -part.shape[1])


class Group:
    def __init__(self, links, axes):
        self.links, self.axes = links, axes
        self.bits = len(links)
        self.size = 1 << self.bits
        self.orders = (list(range(self.bits)), list(range(self.bits))[::-1])

    def send(self, value, bit):
        return lax.ppermute(value, self.axes, self.links[bit])

    def messages(self):
        found = []
        for order in self.orders:
            found.append([])
            for top in reversed(range(self.bits)):
                found[-1].append(
                    [
                        1 << order[top] | sum(1 << order[p] for p in range(top) if v >> p & 1)
                        for v in range(1 << top)
                    ]
                )
        return found


class Spread:
    def __init__(self, group, chain, rows):
        self.group, self.chain = group, chain
        self.held = {0: [rows]}
        self.later = None
        self.keys = [(1 << b, None) for b in range(group.bits)]
        self.flying = [group.send(rows, b) for b in range(group.bits)]

    def go_on(self, got):
        fresh = list(zip(self.keys, got))
        self.keys, self.flying = [], []
        for (k, h), block in fresh:
            if h is None:
                self.held[k] = [block]
            else:
                self.held.setdefault(k, [None, None])[h] = block
        for (k, h), block in fresh:
            for way, order in enumerate(self.group.orders):
                if h is not None and h != way:
                    continue
                half = block.shape[1] // 2
                top = max(i for i, bit in enumerate(order) if k >> bit & 1)
                for i in range(top + 1, len(order)):
                    part = block if h is not None else block[:, way * half : (way + 1) * half]
                    self.keys.append((k | 1 << order[i], way))
                    if self.later is not None:
                        self.later.append((part, order[i]))
                    else:
                        self.flying.append(self.group.send(part, order[i]))

        if self.later:
            parts = self.chain.join(*[part for part, _ in self.later])
            self.later = [(part, bit) for part, (_, bit) in zip(parts, self.later)]

    def resume(self):
        later, self.later = self.later, None
        parts = self.chain.join(*[part for part, _ in later])
        self.flying = [self.group.send(part, bit) for part, (_, bit) in zip(parts, later)]

    def blocks(self):
        while self.flying:
            self.chain.end(self)
        return [self.held[k] for k in range(self.group.size)]


class Fold:
    def __init__(self, group, chain, own, sent):
        self.group, self.chain = group, chain
        self.rows = own[0].shape[0]
        self.sent = [list(half) for half in sent]
        self.parts = [[half] for half in own]
        self.wave = 0
        self.start()

    def start(self):
        self.flying = [
            self.group.send(self.sent[h][self.wave], order[self.group.bits - 1 - self.wave])
            for h, order in enumerate(self.group.orders)
        ]

    def go_on(self, got):
        self.wave += 1
        self.flying = []
        for h, block in enumerate(got):
            self.parts[h].append(block)
            for wave in range(self.wave, self.group.bits):
                first = self.rows << (self.group.bits - 1 - wave)
                more = block[first : 2 * first].astype(F32)
                self.sent[h][wave] = (self.sent[h][wave].astype(F32) + more).astype(BF16)
        if self.wave < self.group.bits:
            now = self.chain.join(*[sent[self.wave] for sent in self.sent])
            for sent, value in zip(self.sent, now):
                sent[self.wave] = value
            self.start()

    def total(self):
        while self.flying:
            self.chain.end(self)
        return self.parts


class Weight:
    def __init__(self, pieces, rows, start, width):
        self.pieces, self.rows, self.start, self.width = pieces, rows, start, width
        self.model = len(pieces) * rows

    def tiles(self, tile):
        first = self.start // tile
        return [pl.BlockSpec((self.rows, tile), lambda j: (0, first + j))] * len(self.pieces)


def nn(left, right):
    return lax.dot_general(left, right, (((1,), (0,)), ((), ())), preferred_element_type=F32)


def nt(left, right):
    return lax.dot_general(left, right, (((1,), (1,)), ((), ())), preferred_element_type=F32)


def tn(left, right):
    return lax.dot_general(left, right, (((0,), (0,)), ((), ())), preferred_element_type=F32)


def whole(shape):
    return pl.BlockSpec(shape, lambda *_: (0,) * len(shape))


def place(line_ref, j, width):
    return pl.ds(pl.multiple_of(line_ref[j] * width, 128), width)


def cut(width, j):
    return slice(j * width, (j + 1) * width)


def scale_of(values):
    return lax.rsqrt(jnp.mean(values * values, axis=-1, keepdims=True) + EPS)


def fetch_blocks(counts, refs, held, sems, k, slot, wait):
    first = 0
    for i, count in enumerate(counts):
        copies = []
        half = held.shape[2] // count
        for h in range(count):
            target = held.at[slot, :, pl.ds(h * half, half)]
            copies.append(pltpu.make_async_copy(refs[first + h], target, sems.at[slot, h]))
        first += count

        @pl.when(k == i)
        def _():
            for copy in copies:
                copy.wait() if wait else copy.start()


def fetched(counts, refs, held, sems):
    k = pl.program_id(0)

    @pl.when(k == 0)
    def _():
        fetch_blocks(counts, refs, held, sems, k, 0, False)

    fetch_blocks(counts, refs, held, sems, k + 1, (k + 1) % 2, False)
    fetch_blocks(counts, refs, held, sems, k, k % 2, True)
    return held.at[k % 2]


def norm_body(blocks, counts, line_ref, gain_ref, *refs):
    out_ref, held, sems = refs[sum(counts) :]
    x_ref = fetched(counts, refs, held, sems)
    width = out_ref.shape[1] // blocks
    scale = scale_of(x_ref[...].astype(F32))
    for j in range(blocks):
        part = x_ref[:, place(line_ref, j, width)].astype(F32)
        gain = gain_ref[0:1, cut(width, j)]
        out_ref[:, cut(width, j)] = (part * scale * gain).astype(BF16)


def order_body(blocks, counts, line_ref, gain_ref, *refs):
    out_ref, held, sems = refs[sum(counts) :]
    x_ref = fetched(counts, refs, held, sems)
    width = out_ref.shape[1] // blocks
    for j in range(blocks):
        out_ref[:, cut(width, j)] = x_ref[:, place(line_ref, j, width)]


def ordered(chain, body, line, gains, held):
    counts = [len(block) for block in held]
    rows, model = held[0][0].shape
    n = len(held)
    return chain.call(
        functools.partial(body, line.shape[0], counts),
        (n,),
        [whole(gains.shape)] + [pl.BlockSpec(memory_space=pl.ANY)] * sum(counts),
        [pl.BlockSpec((rows, model), lambda k, *_: (k, 0))],
        [((n * rows, model), BF16)],
        flops=20 * n * rows * model,
        scratch=[pltpu.VMEM((2, rows, model), BF16), pltpu.SemaphoreType.DMA((2, 2))],
        prefetch=1,
        moved=4 * n * rows * model,
    )(line, gains, *[array for block in held for array in block])[0]


def added(refs, span):
    total = refs[0][span, :].astype(F32)
    for ref in refs[1:]:
        total += ref[span, :].astype(F32)
    return total


def middle_body(blocks, m, line_ref, x_ref, gain_ref, *refs):
    middle_ref, out_ref = refs[2 * m :]
    width = x_ref.shape[1] // blocks
    half = x_ref.shape[1] // 2
    span = slice(None)
    middle_ref[:, :half] = added(refs[:m], span)
    middle_ref[:, half:] = added(refs[m : 2 * m], span)
    for j in range(blocks):
        here = x_ref[:, place(line_ref, j, width)].astype(F32)
        middle_ref[:, cut(width, j)] += here
    middle = middle_ref[...]
    out_ref[...] = (middle * scale_of(middle) * gain_ref[1:2, :]).astype(BF16)


def result_body(blocks, m, line_ref, middle_ref, gain_ref, *refs):
    out_ref = refs[2 * m]
    width = middle_ref.shape[1] // blocks
    span = slice(None)
    total = middle_ref[...] + jnp.concatenate(
        [added(refs[:m], span), added(refs[m : 2 * m], span)], axis=1
    )
    for j in range(blocks):
        out_ref[:, place(line_ref, j, width)] = total[:, cut(width, j)].astype(BF16)


def second_back_body(blocks, m, line_ref, dy_ref, gain_ref, *refs):
    middle_ref, out_ref, low_ref = refs[2 * m :]
    width = dy_ref.shape[1] // blocks
    span = slice(None)
    grad = jnp.concatenate([added(refs[:m], span), added(refs[m : 2 * m], span)], axis=1)
    middle = middle_ref[...]
    scale = scale_of(middle)
    normed = middle * scale
    scaled = grad * gain_ref[1:2, :]
    out_ref[...] = scale * (scaled - normed * jnp.mean(scaled * normed, axis=-1, keepdims=True))
    for j in range(blocks):
        out_ref[:, cut(width, j)] += dy_ref[:, place(line_ref, j, width)].astype(F32)
    low_ref[...] = out_ref[...].astype(BF16)


def first_back_body(blocks, m, line_ref, x_ref, gain_ref, *refs):
    above_ref, out_ref = refs[2 * m :]
    width = x_ref.shape[1] // blocks
    span = slice(None)
    scale = scale_of(x_ref[...].astype(F32))
    normed = jnp.concatenate(
        [x_ref[:, place(line_ref, j, width)].astype(F32) for j in range(blocks)], axis=1
    ) * scale
    grad = jnp.concatenate([added(refs[:m], span), added(refs[m : 2 * m], span)], axis=1)
    scaled = grad * gain_ref[0:1, :]
    back = scale * (scaled - normed * jnp.mean(scaled * normed, axis=-1, keepdims=True))
    total = above_ref[...] + back
    for j in range(blocks):
        out_ref[:, place(line_ref, j, width)] = total[:, cut(width, j)]


def by_rows(chain, body, line, first, gains, parts, more, kinds):
    rows, model = first.shape
    half = model // 2
    tile = min(128, rows)
    row = pl.BlockSpec((tile, model), lambda i, *_: (i, 0))
    slim = pl.BlockSpec((tile, half), lambda i, *_: (i, 0))
    m = len(parts[0])
    return chain.call(
        functools.partial(body, line.shape[0], m),
        (rows // tile,),
        [row, whole(gains.shape)] + [slim] * (2 * m) + [row] * len(more),
        [row] * len(kinds),
        [((rows, model), kind) for kind in kinds],
        flops=20 * rows * model,
        prefetch=1,
        moved=rows * model * (2 * m + 4 * len(kinds)),
    )(line, first, gains, *parts[0], *parts[1], *more)


def finish_body(m, halves, n, *refs):
    total = added(refs[:m], slice(None))
    if halves:
        total += jnp.concatenate([ref[...].astype(F32) for ref in refs[m : m + halves]], axis=1)
    m += halves
    weights, outs = refs[m : m + n], refs[m + n :]
    if not n:
        outs[0][...] = total.T
        return
    width = weights[0].shape[1]
    inner = jnp.zeros((total.shape[0], 1), F32)
    for i in range(n):
        part = total[:, cut(width, i)]
        outs[i][...] = part
        inner += jnp.sum(weights[i][...].astype(F32) * part, axis=1, keepdims=True)
    outs[n][...] = jnp.broadcast_to(inner, outs[n].shape)


def finish(chain, terms, weights=()):
    rows, columns = terms[0].shape
    tile = min(128, rows)
    row = pl.BlockSpec((tile, columns), lambda i: (i, 0))
    n = len(weights)
    halves = sum(1 for term in terms if term.shape[1] < columns)
    half = [pl.BlockSpec((tile, columns // 2), lambda i: (i, 0))] * halves
    if n:
        slim = pl.BlockSpec((tile, columns // n), lambda i: (i, 0))
        outs = [slim] * n + [pl.BlockSpec((tile, 128), lambda i: (i, 0))]
        shapes = [((rows, columns // n), F32)] * n + [((rows, 128), F32)]
    else:
        slim = None
        outs = [pl.BlockSpec((columns, tile), lambda i: (0, i))]
        shapes = [((columns, rows), F32)]
    results = chain.call(
        functools.partial(finish_body, len(terms) - halves, halves, n),
        (rows // tile,),
        [row] * (len(terms) - halves) + half + [slim] * n,
        outs,
        shapes,
        flops=4 * rows * columns,
        moved=rows * columns * 12,
    )(*terms, *weights)
    if n:
        results[n] = results[n][:, 0]
    return results


def rope_tables(place):
    half = HEAD_DIM // 2
    freq = THETA ** (-2.0 * jnp.arange(half, dtype=F32) / HEAD_DIM)
    angle = place.astype(F32)[:, None] * freq[None, :]
    cosine, sine = jnp.cos(angle), jnp.sin(angle)
    return (
        jnp.concatenate([cosine] * (PAIR // half), axis=1),
        jnp.concatenate([-sine, sine] * (PAIR // HEAD_DIM), axis=1),
    )


def turn(values):
    half = HEAD_DIM // 2
    width = values.shape[-1]
    lane = lax.broadcasted_iota(jnp.int32, values.shape, 1) % HEAD_DIM
    return jnp.where(
        lane < half, pltpu.roll(values, width - half, 1), pltpu.roll(values, half, 1)
    )


def joined(refs):
    return jnp.concatenate([r[...] for r in refs], axis=0)


def qkv_body(n, x_ref, cos_ref, sin_ref, *refs):
    weights, outs = refs[: 3 * n], refs[3 * n :]
    rows = x_ref.shape[0]
    tile = outs[0].shape[1]
    for i in range(3):
        weight = joined(weights[i * n : (i + 1) * n])
        for s in range(rows // SEQ):
            span = slice(s * SEQ, (s + 1) * SEQ)
            product = nn(x_ref[span, :], weight)
            if i == 2:
                outs[i][span, :] = product.astype(BF16)
                continue
            for t in range(tile // PAIR):
                here = product[:, t * PAIR : (t + 1) * PAIR]
                turned = here * cos_ref[...] + turn(here) * sin_ref[...]
                outs[i][span, t * PAIR : (t + 1) * PAIR] = turned.astype(BF16)


def project(chain, x, tables, query, key, value):
    rows, model = x.shape
    n, width = len(query.pieces), query.width
    tile = min(256, width)
    out = pl.BlockSpec((rows, tile), lambda j: (0, j))
    return chain.call(
        functools.partial(qkv_body, n),
        (width // tile,),
        [whole(x.shape), whole((SEQ, PAIR)), whole((SEQ, PAIR))]
        + query.tiles(tile)
        + key.tiles(tile)
        + value.tiles(tile),
        [out] * 3,
        [((rows, width), BF16)] * 3,
        flops=6 * rows * model * width,
        moved=2 * (rows * model + 3 * model * width + 3 * rows * width),
    )(x, *tables, *query.pieces, *key.pieces, *value.pieces)


def collect(counts, refs, held, sems):
    rows = held.shape[0] // len(counts)
    copies = []
    for k, count in enumerate(counts):
        half = held.shape[1] // count
        for h in range(count):
            target = held.at[pl.ds(k * rows, rows), pl.ds(h * half, half)]
            i = len(copies)
            copies.append(pltpu.make_async_copy(refs[i], target, sems.at[i]))
    for copy in copies:
        copy.start()
    for copy in copies:
        copy.wait()


def gate_body(n, counts, *refs):
    m = sum(counts)
    gate_w, up_w = refs[m : m + n], refs[m + n : m + 2 * n]
    hidden_ref, slope_ref, silu_ref, x_ref, sems = refs[m + 2 * n :]

    @pl.when(pl.program_id(0) == 0)
    def _():
        collect(counts, refs, x_ref, sems)

    gate_weight, up_weight = joined(gate_w), joined(up_w)
    for s in range(x_ref.shape[0] // SEQ):
        span = slice(s * SEQ, (s + 1) * SEQ)
        gate = nn(x_ref[span, :], gate_weight)
        up = nn(x_ref[span, :], up_weight)
        sigm = jax.nn.sigmoid(gate)
        silu = gate * sigm
        hidden_ref[span, :] = (silu * up).astype(BF16)
        silu_ref[span, :] = silu.astype(BF16)
        slope_ref[span, :] = (up * sigm * (1.0 + gate * (1.0 - sigm))).astype(BF16)


def collected(held):
    counts = [len(block) for block in held]
    rows, model = held[0][0].shape
    scratch = [
        pltpu.VMEM((len(held) * rows, model), BF16),
        pltpu.SemaphoreType.DMA((sum(counts),)),
    ]
    arrays = [array for block in held for array in block]
    return counts, arrays, [pl.BlockSpec(memory_space=pl.ANY)] * len(arrays), scratch


def gate_up(chain, held, gate, up):
    counts, arrays, specs, scratch = collected(held)
    rows, model = scratch[0].shape
    n, width = len(gate.pieces), gate.width
    tile = min(256, width)
    out = pl.BlockSpec((rows, tile), lambda j: (0, j))
    return chain.call(
        functools.partial(gate_body, n, counts),
        (width // tile,),
        specs + gate.tiles(tile) + up.tiles(tile),
        [out] * 3,
        [((rows, width), BF16)] * 3,
        flops=4 * rows * model * width,
        scratch=scratch,
        moved=2 * (rows * model + 2 * model * width + 3 * rows * width),
    )(*arrays, *gate.pieces, *up.pieces)


def hidden_back_body(n, g_ref, *refs):
    weight = joined(refs[:n])
    slope_ref, silu_ref, gate_ref, up_ref = refs[n:]
    for s in range(g_ref.shape[0] // SEQ):
        span = slice(s * SEQ, (s + 1) * SEQ)
        grad = nn(g_ref[span, :], weight)
        gate_ref[span, :] = (grad * slope_ref[span, :].astype(F32)).astype(BF16)
        up_ref[span, :] = (grad * silu_ref[span, :].astype(F32)).astype(BF16)


def hidden_back(chain, grads, down, slope, silu):
    rows, model = grads.shape
    n, width = len(down.pieces), down.width
    tile = min(256, width)
    out = pl.BlockSpec((rows, tile), lambda j: (0, j))
    return chain.call(
        functools.partial(hidden_back_body, n),
        (width // tile,),
        [whole(grads.shape)] + down.tiles(tile) + [out] * 2,
        [out] * 2,
        [((rows, width), BF16)] * 2,
        flops=2 * rows * model * width,
        moved=2 * (rows * model + model * width + 4 * rows * width),
    )(grads, *down.pieces, slope, silu)


def mixed_back_body(n, counts, *refs):
    m = sum(counts)
    out_ref, x_ref, sems = refs[m + n :]

    @pl.when(pl.program_id(0) == 0)
    def _():
        collect(counts, refs, x_ref, sems)

    out_ref[...] = nn(x_ref[...], joined(refs[m : m + n])).astype(BF16)


def mixed_back(chain, held, out):
    counts, arrays, specs, scratch = collected(held)
    rows, model = scratch[0].shape
    n, width = len(out.pieces), out.width
    tile = min(256, width)
    return chain.call(
        functools.partial(mixed_back_body, n, counts),
        (width // tile,),
        specs + out.tiles(tile),
        [pl.BlockSpec((rows, tile), lambda j: (0, j))],
        [((rows, width), BF16)],
        flops=2 * rows * model * width,
        scratch=scratch,
        moved=2 * (rows * model + model * width + rows * width),
    )(*arrays, *out.pieces)[0]


def trans_body(n, starts, targets, *refs):
    parts, blocks = len(starts), len(targets[0])
    lefts = refs[:parts]
    pieces = refs[parts : parts * (n + 1)]
    outs = refs[parts * (n + 1) : -4]
    held, ready, sems, out_sems = refs[-4:]
    j = pl.program_id(0)
    depth, width = held.shape[2:]
    rows = ready.shape[1] // blocks

    def copy(i, p, slot):
        source = pieces[p * n + i].at[pl.ds(0, depth), pl.ds(starts[p], width)]
        return pltpu.make_async_copy(source, held.at[slot, p], sems.at[slot, p])

    def fetch(step, slot):
        for i in range(n):

            @pl.when(step == i)
            def _():
                for p in range(parts):
                    copy(i, p, slot).start()

    def leave(slot, k, array, first, column):
        target = outs[array].at[pl.ds(first, rows), pl.ds(column, depth)]
        source = ready.at[slot, pl.ds(k * rows, rows), :]
        return pltpu.make_async_copy(source, target, out_sems.at[slot, k])

    def left(slot):
        for k in range(blocks):
            leave(slot, k, 0, 0, 0).wait()

    @pl.when(j == 0)
    def _():
        fetch(j, 0)

    @pl.when(j + 1 < n)
    def _():
        fetch(j + 1, (j + 1) % 2)

    slot = j % 2
    for p in range(parts):
        copy(0, p, slot).wait()

    @pl.when(j >= 2)
    def _():
        left(slot)

    for s in range(blocks * rows // SEQ):
        span = slice(s * SEQ, (s + 1) * SEQ)
        total = nt(lefts[0][span, :], held[slot, 0])
        for p in range(1, parts):
            total += nt(lefts[p][span, :], held[slot, p])
        ready[slot, span, :] = total.astype(BF16)
    column = pl.multiple_of(j % (n // 2) * depth, 128)
    for h in range(2):

        @pl.when((j >= n // 2) == (h == 1))
        def _():
            for k, (array, first) in enumerate(targets[h]):
                leave(slot, k, array, first, column).start()

    @pl.when(j == n - 1)
    def _():
        left(1 - slot)
        left(slot)


def times_trans(chain, parts, group):
    weights = [weight for _, weight in parts]
    n, depth, width = len(weights[0].pieces), weights[0].rows, weights[0].width
    rows = parts[0][0].shape[0]
    half = weights[0].model // 2
    size = rows // group.size
    messages = group.messages()
    shapes = [((size, half), BF16)] * 2
    targets = [{0: (0, 0)}, {0: (1, 0)}]
    for h in range(2):
        for keys in messages[h]:
            for i, k in enumerate(keys):
                targets[h][k] = (len(shapes), i * size)
            shapes.append(((len(keys) * size, half), BF16))
    targets = [[t[k] for k in range(group.size)] for t in targets]
    anywhere = pl.BlockSpec(memory_space=pl.ANY)
    outs = chain.call(
        functools.partial(trans_body, n, [weight.start for weight in weights], targets),
        (n,),
        [whole((rows, width))] * len(parts) + [anywhere] * (n * len(parts)),
        [anywhere] * len(shapes),
        shapes,
        flops=4 * rows * half * width * len(parts),
        scratch=[
            pltpu.VMEM((2, len(parts), depth, width), BF16),
            pltpu.VMEM((2, rows, depth), BF16),
            pltpu.SemaphoreType.DMA((2, len(parts))),
            pltpu.SemaphoreType.DMA((2, group.size)),
        ],
        moved=2 * (2 * rows * half + len(parts) * (rows + 2 * half) * width),
    )(*[left for left, _ in parts], *[piece for weight in weights for piece in weight.pieces])
    m = group.bits
    return outs[:2], [outs[2 : 2 + m], outs[2 + m :]]


def grad_body(parts, got, blocks, steps, *refs):
    lefts, refs = refs[:blocks], refs[blocks:]
    rights, refs = refs[:parts], refs[parts:]
    got_ref = refs[0] if got else None
    outs, turned = refs[got:-1], refs[-1]
    j = pl.program_id(0)

    @pl.when(j == 0)
    def _():
        rows = turned.shape[1] // blocks
        for k in range(blocks):
            turned[:, cut(rows, k)] = lefts[k][...].T

    for i in range(parts):

        @pl.when((j >= i * steps) & (j < (i + 1) * steps))
        def _():
            total = nn(turned[...], rights[i][...])
            if got:
                total += got_ref[...].astype(F32)
            total = total.astype(BF16)
            first = 0
            for out_ref in outs:
                count = out_ref.shape[0]
                out_ref[...] = total[first : first + count]
                first += count


def weight_grads(chain, left, which, rights, got=None, bits=0):
    rows, width = rights[0].shape
    parts = len(rights)
    tile = min(512, width)
    steps = width // tile
    if isinstance(left, list):
        lefts = [block[0] if len(block) == 1 else block[which] for block in left]
        half = left[0][0].shape[1] // 2
        places = [which if len(block) == 1 else 0 for block in left]
    else:
        lefts, places, half = [left], [which], left.shape[1] // 2
    blocks = len(lefts)
    ins = [
        pl.BlockSpec((rows // blocks, half), functools.partial(lambda at, j: (0, at), at))
        for at in places
    ]
    for i in range(parts):
        ins.append(
            pl.BlockSpec(
                (rows, tile),
                functools.partial(
                    lambda first, j: (0, jnp.clip(j - first, 0, steps - 1)), i * steps
                ),
            )
        )
    column = lambda j: (0, j)
    more = [] if got is None else [got]
    sizes = [half >> bits]
    for p in range(bits):
        sizes += [sizes[0], ((1 << p) - 1) * sizes[0]] if p else [sizes[0]]
    return chain.call(
        functools.partial(grad_body, parts, len(more), blocks, steps),
        (parts * steps,),
        ins + [pl.BlockSpec((half, tile), column)] * len(more),
        [pl.BlockSpec((size, tile), column) for size in sizes],
        [((size, parts * width), BF16) for size in sizes],
        flops=2 * rows * half * width * parts,
        scratch=[pltpu.VMEM((half, rows), BF16)],
        moved=2 * (rows * half + parts * (rows + half) * width),
    )(*lefts, *rights, *more)


def causal(scores):
    past = scores.shape[0] - HALF_SEQ
    key = lax.broadcasted_iota(jnp.int32, (HALF_SEQ, HALF_SEQ), 0)
    query = lax.broadcasted_iota(jnp.int32, (HALF_SEQ, HALF_SEQ), 1)
    last = jnp.where(key <= query, scores[past:], -1e30)
    return last if past == 0 else jnp.concatenate([scores[:past], last], axis=0)


def head_of(h):
    return slice(h * HEAD_DIM, (h + 1) * HEAD_DIM)


def span_of(b):
    return slice(b * HALF_SEQ, (b + 1) * HALF_SEQ)


def in_place(shift_ref, ref, count):
    rows = SEQ // count
    spans = [pl.ds(pl.multiple_of((i ^ shift_ref[0]) * rows, rows), rows) for i in range(count)]
    return jnp.concatenate([ref[span, :] for span in spans], axis=0)


def put_back(shift_ref, ref, count, values):
    rows = SEQ // count
    for i in range(count):
        ref[pl.ds(pl.multiple_of((i ^ shift_ref[0]) * rows, rows), rows), :] = values[cut(rows, i)]


def attend_body(count, shift_ref, q_ref, k_ref, v_ref, out_ref, sum_ref):
    queries, keys = in_place(shift_ref, q_ref, count), in_place(shift_ref, k_ref, count)
    values = in_place(shift_ref, v_ref, count).astype(F32).T.astype(BF16)
    heads = []
    for h in range(2):
        blocks = []
        for b in range(2):
            reach = (b + 1) * HALF_SEQ
            query = queries[span_of(b), head_of(h)] * BF16(FACTOR)
            scores = causal(nt(keys[:reach, head_of(h)], query))
            top = jnp.max(scores, axis=0, keepdims=True)
            expo = jnp.exp(scores - top)
            total = jnp.sum(expo, axis=0, keepdims=True)
            mixed = nn(values[head_of(h), :reach], expo.astype(BF16))
            blocks.append(mixed * (1.0 / total))
            sum_ref[0, 0, h : h + 1, span_of(b)] = top + jnp.log(total)
        heads.append(jnp.concatenate(blocks, axis=1))
    put_back(shift_ref, out_ref, count, jnp.concatenate(heads, axis=0).T.astype(BF16))


def attend(chain, shift, count, query, key, value):
    rows, width = query.shape
    seqs, pairs = rows // SEQ, width // PAIR
    tile = pl.BlockSpec((SEQ, PAIR), lambda s, p, _: (s, p))
    return chain.call(
        functools.partial(attend_body, count),
        (seqs, pairs),
        [tile] * 3,
        [tile, pl.BlockSpec((1, 1, 2, SEQ), lambda s, p, _: (s, p, 0, 0))],
        [((rows, width), BF16), ((seqs, pairs, 2, SEQ), F32)],
        flops=16 * rows * width * SEQ,
        prefetch=1,
        moved=8 * rows * width,
    )(shift, query, key, value)


def attend_back_body(
    count, shift_ref, q_ref, k_ref, v_ref, g_ref, sum_ref, cos_ref, sin_ref, dq_ref, dk_ref, dv_ref
):
    queries, keys, values, grads = (
        in_place(shift_ref, ref, count) for ref in (q_ref, k_ref, v_ref, g_ref)
    )
    turned = keys.astype(F32).T.astype(BF16)
    dq_heads, dk_heads, dv_heads = [], [], []
    for h in range(2):
        dq, dk, dv = [], [], []
        for b in range(2):
            reach = (b + 1) * HALF_SEQ
            query = queries[span_of(b), head_of(h)]
            grad = grads[span_of(b), head_of(h)]
            scores = causal(nt(keys[:reach, head_of(h)], query * BF16(FACTOR)))
            probs = jnp.exp(scores - sum_ref[0, 0, h : h + 1, span_of(b)])
            probs_grad = nt(values[:reach, head_of(h)], grad)
            inner = jnp.sum(probs * probs_grad, axis=0, keepdims=True)
            score_grad = (probs * (probs_grad - inner)).astype(BF16)
            dv.append(nn(probs.astype(BF16), grad))
            dk.append(nn(score_grad, query))
            dq.append(nn(turned[head_of(h), :reach], score_grad))
        for parts, heads in ((dk, dk_heads), (dv, dv_heads)):
            heads.append(
                jnp.concatenate([parts[1][:HALF_SEQ] + parts[0], parts[1][HALF_SEQ:]], axis=0)
            )
        dq_heads.append(jnp.concatenate(dq, axis=1))
    dq = jnp.concatenate(dq_heads, axis=0).T * FACTOR
    dk = jnp.concatenate(dk_heads, axis=1) * FACTOR
    dv = jnp.concatenate(dv_heads, axis=1).astype(BF16)
    cosine, sine = cos_ref[...], sin_ref[...]
    put_back(shift_ref, dq_ref, count, (dq * cosine - turn(dq) * sine).astype(BF16))
    put_back(shift_ref, dk_ref, count, (dk * cosine - turn(dk) * sine).astype(BF16))
    put_back(shift_ref, dv_ref, count, dv)


def attend_back(chain, shift, count, query, key, value, grad, logsum, tables):
    rows, width = query.shape
    seqs, pairs = rows // SEQ, width // PAIR
    tile = pl.BlockSpec((SEQ, PAIR), lambda s, p, _: (s, p))
    return chain.call(
        functools.partial(attend_back_body, count),
        (seqs, pairs),
        [tile] * 4
        + [pl.BlockSpec((1, 1, 2, SEQ), lambda s, p, _: (s, p, 0, 0))]
        + [whole((SEQ, PAIR))] * 2,
        [tile] * 3,
        [((rows, width), BF16)] * 3,
        flops=40 * rows * width * SEQ,
        prefetch=1,
        moved=14 * rows * width,
    )(shift, query, key, value, grad, logsum, *tables)


def local(
    chips,
    group,
    tokens,
    attn_gain,
    query_weight,
    key_weight,
    value_weight,
    output_weight,
    ffn_gain,
    gate_weight,
    up_weight,
    down_weight,
    cotangent,
):
    line = jnp.asarray(chips.table)[lax.axis_index("dp")]
    rows, model = tokens.shape
    count = SEQ // rows
    shift = lax.axis_index("tensor") % count
    row = jnp.arange(SEQ, dtype=jnp.int32)
    places = rope_tables(row)
    tables = rope_tables((row // rows ^ shift) * rows + row % rows)
    shift = jnp.reshape(shift, (1,)).astype(jnp.int32)
    early = (*places, *tables, line, shift)
    depth, own = query_weight.shape
    hidden_units = gate_weight.shape[1]
    chain = Chain()

    def gather(piece):
        return Gather(chips, chain, chain.join(piece)[0])

    def spread_of(values):
        return Spread(group, chain, chain.join(values)[0])

    def fold_of(part):
        own_part, sent = part
        sent = chain.join(*sent[0], *sent[1])
        return Fold(group, chain, own_part, [sent[: group.bits], sent[group.bits :]])

    def grads_of(left, rights):
        got = [None]
        chain.ask(weight_grads(chain, left, 1, rights)[0], got, 0, chips.other)

        def mine(**how):
            if got[0] is None:
                chain.flush()
            blocks = weight_grads(chain, left, 0, rights, got[0], chips.bits)
            return Sums(chips, chain, blocks, **how)

        return mine

    extra = jnp.concatenate([attn_gain, ffn_gain, jnp.zeros((4 * own - 2 * depth,), BF16)])
    attn = jnp.concatenate([query_weight, key_weight, value_weight, output_weight.T], axis=1)
    attn = gather(jnp.concatenate([attn, jnp.broadcast_to(extra, (16, 4 * own))], axis=0))
    spread = spread_of(tokens)
    grads_spread = spread_of(cotangent)
    grads_spread.later = []
    down_turned, *early = chain.join(down_weight.T, *early)
    places, tables, line, shift = early[:2], early[2:4], early[4], early[5]
    chain.end(attn, spread, grads_spread)
    chain.end(attn, spread)
    all_tokens = spread.blocks()
    attn = attn.pieces()
    pair = gather(jnp.concatenate([gate_weight, up_weight], axis=1))
    w_query, w_key, w_value, w_output = [Weight(attn, depth, i * own, own) for i in range(4)]
    gains = jnp.concatenate(
        [piece[depth : depth + 1, : 2 * depth].reshape(2, depth) for piece in attn], axis=1
    ).astype(F32)

    group_one = ordered(chain, norm_body, line, gains, all_tokens)
    grads_spread.resume()
    query, key, value = project(chain, group_one, tables, w_query, w_key, w_value)
    mixed, logsum = attend(chain, shift, count, query, key, value)
    out_part = times_trans(chain, [(mixed, w_output)], group)
    fold = fold_of(out_part)
    chain.end(fold, pair, grads_spread)
    grad_rows = ordered(chain, order_body, line, gains, grads_spread.blocks())
    chain.end(fold)
    attended = fold.total()
    middle, second = by_rows(
        chain, middle_body, line, tokens, gains, attended, [], [F32, BF16]
    )
    spread = spread_of(second)
    chain.end(spread, pair)
    pair = pair.pieces()
    down = gather(down_turned)
    chain.end(spread)
    group_two = spread.blocks()
    w_gate = Weight(pair, depth, 0, hidden_units)
    w_up = Weight(pair, depth, hidden_units, hidden_units)
    hidden, slope, silu = gate_up(chain, group_two, w_gate, w_up)

    mine = grads_of(grad_rows, [hidden])
    chain.end(down)
    chain.flush()
    down_sum = mine()
    w_down = Weight(down.pieces(), depth, 0, hidden_units)
    gate_grad, up_grad = hidden_back(chain, grad_rows, w_down, slope, silu)
    mine_gate = grads_of(group_two, [gate_grad])
    chain.end(down_sum)
    second_part = times_trans(chain, [(gate_grad, w_gate), (up_grad, w_up)], group)
    mine_up = grads_of(group_two, [up_grad])
    gate_sum = mine_gate(hold=True)
    chain.end(down_sum)
    fold = fold_of(second_part)
    up_sum = mine_up(apart=True)
    chain.end(gate_sum, fold)
    result_part = times_trans(chain, [(hidden, w_down)], group)
    chain.end(fold)
    second_grad = fold.total()
    middle_grad, low_grad = by_rows(
        chain, second_back_body, line, cotangent, gains, second_grad, [middle], [F32, BF16]
    )
    spread = spread_of(low_grad)
    chain.end(up_sum)
    gate_sum.resume()
    (down_sum,) = finish(chain, down_sum.terms())
    chain.end(spread)
    attn_grads = spread.blocks()

    mixed_grad = mixed_back(chain, attn_grads, w_output)
    mine_out = grads_of(attn_grads, [mixed])
    chain.end(gate_sum)
    up_sum.send_half(0)
    fold = fold_of(result_part)
    query_back, key_back, value_back = attend_back(
        chain, shift, count, query, key, value, mixed_grad, logsum, places
    )
    mine_qkv = grads_of(group_one, [query_back, key_back, value_back])
    chain.end(up_sum, fold)
    up_sum.send_half(1)
    out_sum = mine_out(hold=True)
    chain.end(up_sum, fold, out_sum)
    qkv_sum = mine_qkv()
    first_part = times_trans(
        chain, [(query_back, w_query), (key_back, w_key), (value_back, w_value)], group
    )
    result_part = fold.total()
    chain.end(qkv_sum)
    fold = fold_of(first_part)
    out_sum.resume()
    up_sum, up_inner = finish(chain, up_sum.terms(), [up_weight])
    gate_sum, gate_inner = finish(chain, gate_sum.terms(), [gate_weight])
    (layer_out,) = by_rows(chain, result_body, line, middle, gains, result_part, [], [BF16])
    chain.end(fold)
    chain.end(fold)
    first_grad = fold.total()
    (input_grad,) = by_rows(
        chain, first_back_body, line, tokens, gains, first_grad, [middle_grad], [F32]
    )
    chain.end(qkv_sum)
    query_sum, key_sum, value_sum, qkv_inner = finish(
        chain, qkv_sum.terms(), [query_weight, key_weight, value_weight]
    )
    gain_one_total, gain_two_total = lax.psum(
        (
            qkv_inner / attn_gain.astype(F32),
            (gate_inner + up_inner) / ffn_gain.astype(F32),
        ),
        "tensor",
    )
    (gain_one_total,) = chain.join(gain_one_total)
    (out_sum,) = finish(chain, out_sum.terms())
    return (
        layer_out,
        input_grad,
        gain_one_total,
        query_sum,
        key_sum,
        value_sum,
        out_sum,
        gain_two_total,
        gate_sum,
        up_sum,
        down_sum,
    )


def solution(mesh):
    in_specs = (
        P(("dp", "tensor"), None),
        P("dp"),
        P("dp", "tensor"),
        P("dp", "tensor"),
        P("dp", "tensor"),
        P("tensor", "dp"),
        P("dp"),
        P("dp", "tensor"),
        P("dp", "tensor"),
        P("tensor", "dp"),
        P(("dp", "tensor"), None),
    )
    out_specs = (
        P(("dp", "tensor"), None),
        P(("dp", "tensor"), None),
        P("dp"),
        P("dp", "tensor"),
        P("dp", "tensor"),
        P("dp", "tensor"),
        P("tensor", "dp"),
        P("dp"),
        P("dp", "tensor"),
        P("dp", "tensor"),
        P("tensor", "dp"),
    )
    chips = Chips(mesh.shape["dp"])
    size = mesh.shape["tensor"]
    links = [[(i, i ^ 1 << b) for i in range(size)] for b in range(size.bit_length() - 1)]
    group = Group(links, "tensor")

    def run(*arrays):
        return local(chips, group, *arrays)

    return jax.shard_map(run, mesh=mesh, in_specs=in_specs, out_specs=out_specs, check_vma=False)
```

```python
import functools

import jax
import jax.numpy as jnp
import numpy as np
from jax import lax
from jax.experimental import pallas as pl
from jax.experimental.pallas import tpu as pltpu
from jax.sharding import PartitionSpec as P

HEAD_DIM = 64
SEQ = 512
EPS = 1e-05
THETA = 130000.0
BF16 = jnp.bfloat16
F32 = jnp.float32
FACTOR = HEAD_DIM**-0.5
PAIR = 2 * HEAD_DIM
HALF_SEQ = SEQ // 2
VMEM_LIMIT = 58 << 20
COST_SHARE = 4096


class Chain:
    def __init__(self):
        self.token = jnp.zeros((8, 128), F32)
        self.swaps, self.asked = [], []

    def join(self, *values):
        *values, self.token = lax.optimization_barrier((*values, self.token))
        return values

    def gate(self, *values):
        swaps, self.swaps = self.swaps, []
        asked, self.asked = self.asked, []
        joined = self.join(
            *values, *[held[i] for held, i in swaps], *[source for source, _, _, _ in asked]
        )
        for (held, i), value in zip(swaps, joined[len(values) :]):
            held[i] = value
        for (_, held, i, swap), value in zip(asked, joined[len(values) + len(swaps) :]):
            held[i] = swap(value)
            self.swaps.append((held, i))
        return joined[: len(values)]

    def end(self, *transfers):
        counts = [len(t.flying) for t in transfers]
        got = self.gate(*[value for t in transfers for value in t.flying])
        for t, count in zip(transfers, counts):
            if count:
                t.go_on(got[:count])
            got = got[count:]

    def ask(self, source, held, i, swap):
        self.asked.append((source, held, i, swap))

    def flush(self):
        for source, held, i, swap in self.asked:
            held[i] = swap(source)
        self.asked = []

    def call(self, body, grid, ins, outs, shapes, flops, scratch=(), prefetch=0, moved=0):
        first = prefetch + len(ins)
        second = first + 1 + len(outs)
        anywhere = pl.BlockSpec(memory_space=pl.ANY)

        def wrapped(*refs):
            body(*refs[:first], *refs[first + 1 : second], *refs[second + 1 :])

        run = pl.pallas_call(
            wrapped,
            grid_spec=pltpu.PrefetchScalarGridSpec(
                num_scalar_prefetch=prefetch,
                grid=grid,
                in_specs=[*ins, anywhere],
                out_specs=[*outs, anywhere],
                scratch_shapes=list(scratch),
            ),
            out_shape=[jax.ShapeDtypeStruct(s, t) for s, t in [*shapes, ((8, 128), F32)]],
            compiler_params=pltpu.CompilerParams(
                vmem_limit_bytes=VMEM_LIMIT, dimension_semantics=("arbitrary",) * len(grid)
            ),
            cost_estimate=pl.CostEstimate(
                flops=flops // COST_SHARE, bytes_accessed=moved // COST_SHARE, transcendentals=0
            ),
        )

        def with_token(*args):
            *results, self.token = run(*args, self.token)
            return results

        return with_token


class Chips:
    def __init__(self, size):
        self.bits = (size // 2).bit_length() - 1
        self.size = size
        self.swap = [(i, i ^ 1) for i in range(size)]
        self.links = [
            [(i, i ^ 2 << self.bits - 1 - p) for i in range(size)] for p in range(self.bits)
        ]
        flips = [
            sum(1 << self.bits - 1 - p for p in range(self.bits) if v >> p & 1)
            for v in range(1 << self.bits)
        ]
        table = [[i ^ 2 * f for f in flips] + [i ^ 2 * f ^ 1 for f in flips] for i in range(size)]
        self.table = np.array(table, np.int32)

    def send(self, value, p):
        return lax.ppermute(value, "dp", self.links[p])

    def other(self, value):
        return lax.ppermute(value, "dp", self.swap)


class Gather:
    def __init__(self, chips, chain, piece):
        self.chips, self.chain = chips, chain
        self.own = [piece] + [None] * (2**chips.bits - 1)
        self.others = list(self.own)
        self.ask(0)
        self.keys = [1 << p for p in range(chips.bits)]
        self.flying = [chips.send(piece, p) for p in range(chips.bits)]

    def ask(self, v):
        self.chain.ask(self.own[v], self.others, v, self.chips.other)

    def go_on(self, got):
        keys, self.keys, self.flying = self.keys, [], []
        for v, piece in zip(keys, got):
            self.own[v] = piece
            for p in range(v.bit_length(), self.chips.bits):
                self.keys.append(v | 1 << p)
                self.flying.append(self.chips.send(piece, p))
        for v in keys:
            self.ask(v)

    def pieces(self):
        while self.flying:
            self.chain.end(self)
        self.chain.flush()
        return self.own + self.others


class Sums:
    def __init__(self, chips, chain, mine, apart=False, hold=False, cut_in_two=False):
        self.chips, self.chain, self.apart, self.hold = chips, chain, apart, hold
        self.todo = []
        self.cut_in_two = cut_in_two and chips.bits == 2
        self.parts = [mine[0]]
        mine = list(mine[1:])
        self.direct, self.passed = [], []
        for p in range(chips.bits):
            self.direct.append(mine.pop(0))
            self.passed.append(mine.pop(0) if p else None)
        self.p = chips.bits - 1
        if self.cut_in_two:
            self.kinds = [0, 1]
            self.flying = [chips.send(half, 1) for half in self.in_two(self.passed[1])]
            return
        self.kinds = [self.p]
        self.flying = [chips.send(self.passed[self.p], self.p)]

    def in_two(self, values):
        width = values.shape[1] // 2
        return values[:, :width], values[:, width:]

    def go_on(self, got):
        rows = self.parts[0].shape[0]
        kinds, self.kinds, self.flying = self.kinds, [], []
        if self.p == 0:
            self.parts += got
            return
        if self.cut_in_two:
            self.p = 0
            total = self.direct[0].astype(F32) + jnp.concatenate(got, axis=1).astype(F32)
            self.todo = [(None, self.direct[1], 1), (None, total.astype(BF16), 0)]
            self.resume()
            return
        for kind, block in zip(kinds, got):
            if kind is None:
                self.parts.append(block)
                continue
            add = lambda held, first: (
                held.astype(F32) + block[first * rows : first * rows + held.shape[0]].astype(F32)
            ).astype(BF16)
            for q in range(kind):
                self.direct[q] = add(self.direct[q], (1 << q) - 1)
                if q:
                    self.passed[q] = add(self.passed[q], 1 << q)
        p, self.p = self.p, self.p - 1
        if p > 0:
            self.todo.append((None, self.direct[p], p))
        if p > 1:
            self.todo.append((p - 1, self.passed[p - 1], p - 1))
        if p == 1 and not self.apart:
            self.todo.append((None, self.direct[0], 0))
        if not self.hold:
            self.resume()

    def resume(self):
        todo, self.todo = self.todo, []
        values = self.chain.join(*[value for _, value, _ in todo])
        for (kind, _, p), value in zip(todo, values):
            self.kinds.append(kind)
            self.flying.append(self.chips.send(value, p))

    def send_half(self, i):
        while self.p > 0:
            self.chain.end(self)
        width = self.direct[0].shape[1] // 2
        (value,) = self.chain.join(self.direct[0][:, i * width : (i + 1) * width])
        self.kinds.append(None)
        self.flying.append(self.chips.send(value, 0))

    def terms(self):
        while self.flying or self.todo:
            if self.todo:
                self.resume()
            self.chain.end(self)
        return sorted(self.parts, key=lambda part: -part.shape[1])


class Group:
    def __init__(self, links, axes):
        self.links, self.axes = links, axes
        self.bits = len(links)
        self.size = 1 << self.bits
        self.orders = (list(range(self.bits)), list(range(self.bits))[::-1])

    def send(self, value, bit):
        return lax.ppermute(value, self.axes, self.links[bit])

    def messages(self):
        found = []
        for order in self.orders:
            found.append([])
            for top in reversed(range(self.bits)):
                found[-1].append(
                    [
                        1 << order[top] | sum(1 << order[p] for p in range(top) if v >> p & 1)
                        for v in range(1 << top)
                    ]
                )
        return found


class Spread:
    def __init__(self, group, chain, rows):
        self.group, self.chain = group, chain
        self.held = {0: [rows]}
        self.later = None
        self.keys = [(1 << b, None) for b in range(group.bits)]
        self.flying = [group.send(rows, b) for b in range(group.bits)]

    def go_on(self, got):
        fresh = list(zip(self.keys, got))
        self.keys, self.flying = [], []
        for (k, h), block in fresh:
            if h is None:
                self.held[k] = [block]
            else:
                self.held.setdefault(k, [None, None])[h] = block
        for (k, h), block in fresh:
            for way, order in enumerate(self.group.orders):
                if h is not None and h != way:
                    continue
                half = block.shape[1] // 2
                top = max(i for i, bit in enumerate(order) if k >> bit & 1)
                for i in range(top + 1, len(order)):
                    part = block if h is not None else block[:, way * half : (way + 1) * half]
                    self.keys.append((k | 1 << order[i], way))
                    if self.later is not None:
                        self.later.append((part, order[i]))
                    else:
                        self.flying.append(self.group.send(part, order[i]))

        if self.later:
            parts = self.chain.join(*[part for part, _ in self.later])
            self.later = [(part, bit) for part, (_, bit) in zip(parts, self.later)]

    def resume(self):
        later, self.later = self.later, None
        parts = self.chain.join(*[part for part, _ in later])
        self.flying = [self.group.send(part, bit) for part, (_, bit) in zip(parts, later)]

    def blocks(self):
        while self.flying:
            self.chain.end(self)
        return [self.held[k] for k in range(self.group.size)]


class Fold:
    def __init__(self, group, chain, own, sent):
        self.group, self.chain = group, chain
        self.rows = own[0].shape[0]
        self.sent = [list(half) for half in sent]
        self.parts = [[half] for half in own]
        self.wave = 0
        self.start()

    def start(self):
        self.flying = [
            self.group.send(self.sent[h][self.wave], order[self.group.bits - 1 - self.wave])
            for h, order in enumerate(self.group.orders)
        ]

    def go_on(self, got):
        self.wave += 1
        self.flying = []
        for h, block in enumerate(got):
            self.parts[h].append(block)
            for wave in range(self.wave, self.group.bits):
                first = self.rows << (self.group.bits - 1 - wave)
                more = block[first : 2 * first].astype(F32)
                self.sent[h][wave] = (self.sent[h][wave].astype(F32) + more).astype(BF16)
        if self.wave < self.group.bits:
            now = self.chain.join(*[sent[self.wave] for sent in self.sent])
            for sent, value in zip(self.sent, now):
                sent[self.wave] = value
            self.start()

    def total(self):
        while self.flying:
            self.chain.end(self)
        return self.parts


class Weight:
    def __init__(self, pieces, rows, start, width):
        self.pieces, self.rows, self.start, self.width = pieces, rows, start, width
        self.model = len(pieces) * rows

    def tiles(self, tile):
        first = self.start // tile
        return [pl.BlockSpec((self.rows, tile), lambda j: (0, first + j))] * len(self.pieces)


def nn(left, right):
    return lax.dot_general(left, right, (((1,), (0,)), ((), ())), preferred_element_type=F32)


def nt(left, right):
    return lax.dot_general(left, right, (((1,), (1,)), ((), ())), preferred_element_type=F32)


def tn(left, right):
    return lax.dot_general(left, right, (((0,), (0,)), ((), ())), preferred_element_type=F32)


def whole(shape):
    return pl.BlockSpec(shape, lambda *_: (0,) * len(shape))


def place(line_ref, j, width):
    return pl.ds(pl.multiple_of(line_ref[j] * width, 128), width)


def cut(width, j):
    return slice(j * width, (j + 1) * width)


def scale_of(values):
    return lax.rsqrt(jnp.mean(values * values, axis=-1, keepdims=True) + EPS)


def fetch_blocks(counts, refs, held, sems, k, slot, wait):
    first = 0
    for i, count in enumerate(counts):
        copies = []
        half = held.shape[2] // count
        for h in range(count):
            target = held.at[slot, :, pl.ds(h * half, half)]
            copies.append(pltpu.make_async_copy(refs[first + h], target, sems.at[slot, h]))
        first += count

        @pl.when(k == i)
        def _():
            for copy in copies:
                copy.wait() if wait else copy.start()


def fetched(counts, refs, held, sems):
    k = pl.program_id(0)

    @pl.when(k == 0)
    def _():
        fetch_blocks(counts, refs, held, sems, k, 0, False)

    fetch_blocks(counts, refs, held, sems, k + 1, (k + 1) % 2, False)
    fetch_blocks(counts, refs, held, sems, k, k % 2, True)
    return held.at[k % 2]


def norm_body(blocks, counts, line_ref, gain_ref, *refs):
    out_ref, held, sems = refs[sum(counts) :]
    x_ref = fetched(counts, refs, held, sems)
    width = out_ref.shape[1] // blocks
    scale = scale_of(x_ref[...].astype(F32))
    for j in range(blocks):
        part = x_ref[:, place(line_ref, j, width)].astype(F32)
        gain = gain_ref[0:1, cut(width, j)]
        out_ref[:, cut(width, j)] = (part * scale * gain).astype(BF16)


def order_body(blocks, counts, line_ref, gain_ref, *refs):
    out_ref, held, sems = refs[sum(counts) :]
    x_ref = fetched(counts, refs, held, sems)
    width = out_ref.shape[1] // blocks
    for j in range(blocks):
        out_ref[:, cut(width, j)] = x_ref[:, place(line_ref, j, width)]


def ordered(chain, body, line, gains, held):
    counts = [len(block) for block in held]
    rows, model = held[0][0].shape
    n = len(held)
    return chain.call(
        functools.partial(body, line.shape[0], counts),
        (n,),
        [whole(gains.shape)] + [pl.BlockSpec(memory_space=pl.ANY)] * sum(counts),
        [pl.BlockSpec((rows, model), lambda k, *_: (k, 0))],
        [((n * rows, model), BF16)],
        flops=20 * n * rows * model,
        scratch=[pltpu.VMEM((2, rows, model), BF16), pltpu.SemaphoreType.DMA((2, 2))],
        prefetch=1,
        moved=4 * n * rows * model,
    )(line, gains, *[array for block in held for array in block])[0]


def added(refs, span):
    total = refs[0][span, :].astype(F32)
    for ref in refs[1:]:
        total += ref[span, :].astype(F32)
    return total


def middle_body(blocks, m, line_ref, x_ref, gain_ref, *refs):
    middle_ref, out_ref = refs[2 * m :]
    width = x_ref.shape[1] // blocks
    half = x_ref.shape[1] // 2
    span = slice(None)
    middle_ref[:, :half] = added(refs[:m], span)
    middle_ref[:, half:] = added(refs[m : 2 * m], span)
    for j in range(blocks):
        here = x_ref[:, place(line_ref, j, width)].astype(F32)
        middle_ref[:, cut(width, j)] += here
    middle = middle_ref[...]
    out_ref[...] = (middle * scale_of(middle) * gain_ref[1:2, :]).astype(BF16)


def result_body(blocks, m, line_ref, middle_ref, gain_ref, *refs):
    out_ref = refs[2 * m]
    width = middle_ref.shape[1] // blocks
    span = slice(None)
    total = middle_ref[...] + jnp.concatenate(
        [added(refs[:m], span), added(refs[m : 2 * m], span)], axis=1
    )
    for j in range(blocks):
        out_ref[:, place(line_ref, j, width)] = total[:, cut(width, j)].astype(BF16)


def second_back_body(blocks, m, line_ref, dy_ref, gain_ref, *refs):
    middle_ref, out_ref, low_ref = refs[2 * m :]
    width = dy_ref.shape[1] // blocks
    span = slice(None)
    grad = jnp.concatenate([added(refs[:m], span), added(refs[m : 2 * m], span)], axis=1)
    middle = middle_ref[...]
    scale = scale_of(middle)
    normed = middle * scale
    scaled = grad * gain_ref[1:2, :]
    out_ref[...] = scale * (scaled - normed * jnp.mean(scaled * normed, axis=-1, keepdims=True))
    for j in range(blocks):
        out_ref[:, cut(width, j)] += dy_ref[:, place(line_ref, j, width)].astype(F32)
    low_ref[...] = out_ref[...].astype(BF16)


def first_back_body(blocks, m, line_ref, x_ref, gain_ref, *refs):
    above_ref, out_ref = refs[2 * m :]
    width = x_ref.shape[1] // blocks
    span = slice(None)
    scale = scale_of(x_ref[...].astype(F32))
    normed = jnp.concatenate(
        [x_ref[:, place(line_ref, j, width)].astype(F32) for j in range(blocks)], axis=1
    ) * scale
    grad = jnp.concatenate([added(refs[:m], span), added(refs[m : 2 * m], span)], axis=1)
    scaled = grad * gain_ref[0:1, :]
    back = scale * (scaled - normed * jnp.mean(scaled * normed, axis=-1, keepdims=True))
    total = above_ref[...] + back
    for j in range(blocks):
        out_ref[:, place(line_ref, j, width)] = total[:, cut(width, j)]


def by_rows(chain, body, line, first, gains, parts, more, kinds):
    rows, model = first.shape
    half = model // 2
    tile = min(128, rows)
    row = pl.BlockSpec((tile, model), lambda i, *_: (i, 0))
    slim = pl.BlockSpec((tile, half), lambda i, *_: (i, 0))
    m = len(parts[0])
    return chain.call(
        functools.partial(body, line.shape[0], m),
        (rows // tile,),
        [row, whole(gains.shape)] + [slim] * (2 * m) + [row] * len(more),
        [row] * len(kinds),
        [((rows, model), kind) for kind in kinds],
        flops=20 * rows * model,
        prefetch=1,
        moved=rows * model * (2 * m + 4 * len(kinds)),
    )(line, first, gains, *parts[0], *parts[1], *more)


def finish_body(m, halves, n, *refs):
    total = added(refs[:m], slice(None))
    if halves:
        total += jnp.concatenate([ref[...].astype(F32) for ref in refs[m : m + halves]], axis=1)
    m += halves
    weights, outs = refs[m : m + n], refs[m + n :]
    if not n:
        outs[0][...] = total.T
        return
    width = weights[0].shape[1]
    inner = jnp.zeros((total.shape[0], 1), F32)
    for i in range(n):
        part = total[:, cut(width, i)]
        outs[i][...] = part
        inner += jnp.sum(weights[i][...].astype(F32) * part, axis=1, keepdims=True)
    outs[n][...] = jnp.broadcast_to(inner, outs[n].shape)


def finish(chain, terms, weights=()):
    rows, columns = terms[0].shape
    tile = min(128, rows)
    row = pl.BlockSpec((tile, columns), lambda i: (i, 0))
    n = len(weights)
    halves = sum(1 for term in terms if term.shape[1] < columns)
    half = [pl.BlockSpec((tile, columns // 2), lambda i: (i, 0))] * halves
    if n:
        slim = pl.BlockSpec((tile, columns // n), lambda i: (i, 0))
        outs = [slim] * n + [pl.BlockSpec((tile, 128), lambda i: (i, 0))]
        shapes = [((rows, columns // n), F32)] * n + [((rows, 128), F32)]
    else:
        slim = None
        outs = [pl.BlockSpec((columns, tile), lambda i: (0, i))]
        shapes = [((columns, rows), F32)]
    results = chain.call(
        functools.partial(finish_body, len(terms) - halves, halves, n),
        (rows // tile,),
        [row] * (len(terms) - halves) + half + [slim] * n,
        outs,
        shapes,
        flops=4 * rows * columns,
        moved=rows * columns * 12,
    )(*terms, *weights)
    if n:
        results[n] = results[n][:, 0]
    return results


def rope_tables(place):
    half = HEAD_DIM // 2
    freq = THETA ** (-2.0 * jnp.arange(half, dtype=F32) / HEAD_DIM)
    angle = place.astype(F32)[:, None] * freq[None, :]
    cosine, sine = jnp.cos(angle), jnp.sin(angle)
    return (
        jnp.concatenate([cosine] * (PAIR // half), axis=1),
        jnp.concatenate([-sine, sine] * (PAIR // HEAD_DIM), axis=1),
    )


def turn(values):
    half = HEAD_DIM // 2
    width = values.shape[-1]
    lane = lax.broadcasted_iota(jnp.int32, values.shape, 1) % HEAD_DIM
    return jnp.where(
        lane < half, pltpu.roll(values, width - half, 1), pltpu.roll(values, half, 1)
    )


def joined(refs):
    return jnp.concatenate([r[...] for r in refs], axis=0)


def qkv_body(n, x_ref, cos_ref, sin_ref, *refs):
    weights, outs = refs[: 3 * n], refs[3 * n :]
    rows = x_ref.shape[0]
    tile = outs[0].shape[1]
    for i in range(3):
        weight = joined(weights[i * n : (i + 1) * n])
        for s in range(rows // SEQ):
            span = slice(s * SEQ, (s + 1) * SEQ)
            product = nn(x_ref[span, :], weight)
            if i == 2:
                outs[i][span, :] = product.astype(BF16)
                continue
            for t in range(tile // PAIR):
                here = product[:, t * PAIR : (t + 1) * PAIR]
                turned = here * cos_ref[...] + turn(here) * sin_ref[...]
                outs[i][span, t * PAIR : (t + 1) * PAIR] = turned.astype(BF16)


def project(chain, x, tables, query, key, value):
    rows, model = x.shape
    n, width = len(query.pieces), query.width
    tile = min(256, width)
    out = pl.BlockSpec((rows, tile), lambda j: (0, j))
    return chain.call(
        functools.partial(qkv_body, n),
        (width // tile,),
        [whole(x.shape), whole((SEQ, PAIR)), whole((SEQ, PAIR))]
        + query.tiles(tile)
        + key.tiles(tile)
        + value.tiles(tile),
        [out] * 3,
        [((rows, width), BF16)] * 3,
        flops=6 * rows * model * width,
        moved=2 * (rows * model + 3 * model * width + 3 * rows * width),
    )(x, *tables, *query.pieces, *key.pieces, *value.pieces)


def collect(counts, refs, held, sems):
    rows = held.shape[0] // len(counts)
    copies = []
    for k, count in enumerate(counts):
        half = held.shape[1] // count
        for h in range(count):
            target = held.at[pl.ds(k * rows, rows), pl.ds(h * half, half)]
            i = len(copies)
            copies.append(pltpu.make_async_copy(refs[i], target, sems.at[i]))
    for copy in copies:
        copy.start()
    for copy in copies:
        copy.wait()


def gate_body(n, counts, *refs):
    m = sum(counts)
    gate_w, up_w = refs[m : m + n], refs[m + n : m + 2 * n]
    hidden_ref, slope_ref, silu_ref, x_ref, sems = refs[m + 2 * n :]

    @pl.when(pl.program_id(0) == 0)
    def _():
        collect(counts, refs, x_ref, sems)

    gate_weight, up_weight = joined(gate_w), joined(up_w)
    for s in range(x_ref.shape[0] // SEQ):
        span = slice(s * SEQ, (s + 1) * SEQ)
        gate = nn(x_ref[span, :], gate_weight)
        up = nn(x_ref[span, :], up_weight)
        sigm = jax.nn.sigmoid(gate)
        silu = gate * sigm
        hidden_ref[span, :] = (silu * up).astype(BF16)
        silu_ref[span, :] = silu.astype(BF16)
        slope_ref[span, :] = (up * sigm * (1.0 + gate * (1.0 - sigm))).astype(BF16)


def collected(held):
    counts = [len(block) for block in held]
    rows, model = held[0][0].shape
    scratch = [
        pltpu.VMEM((len(held) * rows, model), BF16),
        pltpu.SemaphoreType.DMA((sum(counts),)),
    ]
    arrays = [array for block in held for array in block]
    return counts, arrays, [pl.BlockSpec(memory_space=pl.ANY)] * len(arrays), scratch


def gate_up(chain, held, gate, up):
    counts, arrays, specs, scratch = collected(held)
    rows, model = scratch[0].shape
    n, width = len(gate.pieces), gate.width
    tile = min(256, width)
    out = pl.BlockSpec((rows, tile), lambda j: (0, j))
    return chain.call(
        functools.partial(gate_body, n, counts),
        (width // tile,),
        specs + gate.tiles(tile) + up.tiles(tile),
        [out] * 3,
        [((rows, width), BF16)] * 3,
        flops=4 * rows * model * width,
        scratch=scratch,
        moved=2 * (rows * model + 2 * model * width + 3 * rows * width),
    )(*arrays, *gate.pieces, *up.pieces)


def hidden_back_body(n, g_ref, *refs):
    weight = joined(refs[:n])
    slope_ref, silu_ref, gate_ref, up_ref = refs[n:]
    for s in range(g_ref.shape[0] // SEQ):
        span = slice(s * SEQ, (s + 1) * SEQ)
        grad = nn(g_ref[span, :], weight)
        gate_ref[span, :] = (grad * slope_ref[span, :].astype(F32)).astype(BF16)
        up_ref[span, :] = (grad * silu_ref[span, :].astype(F32)).astype(BF16)


def hidden_back(chain, grads, down, slope, silu):
    rows, model = grads.shape
    n, width = len(down.pieces), down.width
    tile = min(256, width)
    out = pl.BlockSpec((rows, tile), lambda j: (0, j))
    return chain.call(
        functools.partial(hidden_back_body, n),
        (width // tile,),
        [whole(grads.shape)] + down.tiles(tile) + [out] * 2,
        [out] * 2,
        [((rows, width), BF16)] * 2,
        flops=2 * rows * model * width,
        moved=2 * (rows * model + model * width + 4 * rows * width),
    )(grads, *down.pieces, slope, silu)


def mixed_back_body(n, counts, *refs):
    m = sum(counts)
    out_ref, x_ref, sems = refs[m + n :]

    @pl.when(pl.program_id(0) == 0)
    def _():
        collect(counts, refs, x_ref, sems)

    out_ref[...] = nn(x_ref[...], joined(refs[m : m + n])).astype(BF16)


def mixed_back(chain, held, out):
    counts, arrays, specs, scratch = collected(held)
    rows, model = scratch[0].shape
    n, width = len(out.pieces), out.width
    tile = min(256, width)
    return chain.call(
        functools.partial(mixed_back_body, n, counts),
        (width // tile,),
        specs + out.tiles(tile),
        [pl.BlockSpec((rows, tile), lambda j: (0, j))],
        [((rows, width), BF16)],
        flops=2 * rows * model * width,
        scratch=scratch,
        moved=2 * (rows * model + model * width + rows * width),
    )(*arrays, *out.pieces)[0]


def trans_body(n, starts, targets, *refs):
    parts, blocks = len(starts), len(targets[0])
    lefts = refs[:parts]
    pieces = refs[parts : parts * (n + 1)]
    outs = refs[parts * (n + 1) : -4]
    held, ready, sems, out_sems = refs[-4:]
    j = pl.program_id(0)
    depth, width = held.shape[2:]
    rows = ready.shape[1] // blocks

    def copy(i, p, slot):
        source = pieces[p * n + i].at[pl.ds(0, depth), pl.ds(starts[p], width)]
        return pltpu.make_async_copy(source, held.at[slot, p], sems.at[slot, p])

    def fetch(step, slot):
        for i in range(n):

            @pl.when(step == i)
            def _():
                for p in range(parts):
                    copy(i, p, slot).start()

    def leave(slot, k, array, first, column):
        target = outs[array].at[pl.ds(first, rows), pl.ds(column, depth)]
        source = ready.at[slot, pl.ds(k * rows, rows), :]
        return pltpu.make_async_copy(source, target, out_sems.at[slot, k])

    def left(slot):
        for k in range(blocks):
            leave(slot, k, 0, 0, 0).wait()

    @pl.when(j == 0)
    def _():
        fetch(j, 0)

    @pl.when(j + 1 < n)
    def _():
        fetch(j + 1, (j + 1) % 2)

    slot = j % 2
    for p in range(parts):
        copy(0, p, slot).wait()

    @pl.when(j >= 2)
    def _():
        left(slot)

    for s in range(blocks * rows // SEQ):
        span = slice(s * SEQ, (s + 1) * SEQ)
        total = nt(lefts[0][span, :], held[slot, 0])
        for p in range(1, parts):
            total += nt(lefts[p][span, :], held[slot, p])
        ready[slot, span, :] = total.astype(BF16)
    column = pl.multiple_of(j % (n // 2) * depth, 128)
    for h in range(2):

        @pl.when((j >= n // 2) == (h == 1))
        def _():
            for k, (array, first) in enumerate(targets[h]):
                leave(slot, k, array, first, column).start()

    @pl.when(j == n - 1)
    def _():
        left(1 - slot)
        left(slot)


def times_trans(chain, parts, group):
    weights = [weight for _, weight in parts]
    n, depth, width = len(weights[0].pieces), weights[0].rows, weights[0].width
    rows = parts[0][0].shape[0]
    half = weights[0].model // 2
    size = rows // group.size
    messages = group.messages()
    shapes = [((size, half), BF16)] * 2
    targets = [{0: (0, 0)}, {0: (1, 0)}]
    for h in range(2):
        for keys in messages[h]:
            for i, k in enumerate(keys):
                targets[h][k] = (len(shapes), i * size)
            shapes.append(((len(keys) * size, half), BF16))
    targets = [[t[k] for k in range(group.size)] for t in targets]
    anywhere = pl.BlockSpec(memory_space=pl.ANY)
    outs = chain.call(
        functools.partial(trans_body, n, [weight.start for weight in weights], targets),
        (n,),
        [whole((rows, width))] * len(parts) + [anywhere] * (n * len(parts)),
        [anywhere] * len(shapes),
        shapes,
        flops=4 * rows * half * width * len(parts),
        scratch=[
            pltpu.VMEM((2, len(parts), depth, width), BF16),
            pltpu.VMEM((2, rows, depth), BF16),
            pltpu.SemaphoreType.DMA((2, len(parts))),
            pltpu.SemaphoreType.DMA((2, group.size)),
        ],
        moved=2 * (2 * rows * half + len(parts) * (rows + 2 * half) * width),
    )(*[left for left, _ in parts], *[piece for weight in weights for piece in weight.pieces])
    m = group.bits
    return outs[:2], [outs[2 : 2 + m], outs[2 + m :]]


def grad_body(parts, got, blocks, steps, *refs):
    lefts, refs = refs[:blocks], refs[blocks:]
    rights, refs = refs[:parts], refs[parts:]
    got_ref = refs[0] if got else None
    outs, turned = refs[got:-1], refs[-1]
    j = pl.program_id(0)

    @pl.when(j == 0)
    def _():
        rows = turned.shape[1] // blocks
        for k in range(blocks):
            turned[:, cut(rows, k)] = lefts[k][...].T

    for i in range(parts):

        @pl.when((j >= i * steps) & (j < (i + 1) * steps))
        def _():
            total = nn(turned[...], rights[i][...])
            if got:
                total += got_ref[...].astype(F32)
            total = total.astype(BF16)
            first = 0
            for out_ref in outs:
                count = out_ref.shape[0]
                out_ref[...] = total[first : first + count]
                first += count


def weight_grads(chain, left, which, rights, got=None, bits=0):
    rows, width = rights[0].shape
    parts = len(rights)
    tile = min(512, width)
    steps = width // tile
    if isinstance(left, list):
        lefts = [block[0] if len(block) == 1 else block[which] for block in left]
        half = left[0][0].shape[1] // 2
        places = [which if len(block) == 1 else 0 for block in left]
    else:
        lefts, places, half = [left], [which], left.shape[1] // 2
    blocks = len(lefts)
    ins = [
        pl.BlockSpec((rows // blocks, half), functools.partial(lambda at, j: (0, at), at))
        for at in places
    ]
    for i in range(parts):
        ins.append(
            pl.BlockSpec(
                (rows, tile),
                functools.partial(
                    lambda first, j: (0, jnp.clip(j - first, 0, steps - 1)), i * steps
                ),
            )
        )
    column = lambda j: (0, j)
    more = [] if got is None else [got]
    sizes = [half >> bits]
    for p in range(bits):
        sizes += [sizes[0], ((1 << p) - 1) * sizes[0]] if p else [sizes[0]]
    return chain.call(
        functools.partial(grad_body, parts, len(more), blocks, steps),
        (parts * steps,),
        ins + [pl.BlockSpec((half, tile), column)] * len(more),
        [pl.BlockSpec((size, tile), column) for size in sizes],
        [((size, parts * width), BF16) for size in sizes],
        flops=2 * rows * half * width * parts,
        scratch=[pltpu.VMEM((half, rows), BF16)],
        moved=2 * (rows * half + parts * (rows + half) * width),
    )(*lefts, *rights, *more)


def causal(scores):
    past = scores.shape[0] - HALF_SEQ
    key = lax.broadcasted_iota(jnp.int32, (HALF_SEQ, HALF_SEQ), 0)
    query = lax.broadcasted_iota(jnp.int32, (HALF_SEQ, HALF_SEQ), 1)
    last = jnp.where(key <= query, scores[past:], -1e30)
    return last if past == 0 else jnp.concatenate([scores[:past], last], axis=0)


def head_of(h):
    return slice(h * HEAD_DIM, (h + 1) * HEAD_DIM)


def span_of(b):
    return slice(b * HALF_SEQ, (b + 1) * HALF_SEQ)


def in_place(shift_ref, ref, count):
    rows = SEQ // count
    spans = [pl.ds(pl.multiple_of((i ^ shift_ref[0]) * rows, rows), rows) for i in range(count)]
    return jnp.concatenate([ref[span, :] for span in spans], axis=0)


def put_back(shift_ref, ref, count, values):
    rows = SEQ // count
    for i in range(count):
        ref[pl.ds(pl.multiple_of((i ^ shift_ref[0]) * rows, rows), rows), :] = values[cut(rows, i)]


def attend_body(count, shift_ref, q_ref, k_ref, v_ref, out_ref, sum_ref):
    queries, keys = in_place(shift_ref, q_ref, count), in_place(shift_ref, k_ref, count)
    values = in_place(shift_ref, v_ref, count).astype(F32).T.astype(BF16)
    heads = []
    for h in range(2):
        blocks = []
        for b in range(2):
            reach = (b + 1) * HALF_SEQ
            query = queries[span_of(b), head_of(h)] * BF16(FACTOR)
            scores = causal(nt(keys[:reach, head_of(h)], query))
            top = jnp.max(scores, axis=0, keepdims=True)
            expo = jnp.exp(scores - top)
            total = jnp.sum(expo, axis=0, keepdims=True)
            mixed = nn(values[head_of(h), :reach], expo.astype(BF16))
            blocks.append(mixed * (1.0 / total))
            sum_ref[0, 0, h : h + 1, span_of(b)] = top + jnp.log(total)
        heads.append(jnp.concatenate(blocks, axis=1))
    put_back(shift_ref, out_ref, count, jnp.concatenate(heads, axis=0).T.astype(BF16))


def attend(chain, shift, count, query, key, value):
    rows, width = query.shape
    seqs, pairs = rows // SEQ, width // PAIR
    tile = pl.BlockSpec((SEQ, PAIR), lambda s, p, _: (s, p))
    return chain.call(
        functools.partial(attend_body, count),
        (seqs, pairs),
        [tile] * 3,
        [tile, pl.BlockSpec((1, 1, 2, SEQ), lambda s, p, _: (s, p, 0, 0))],
        [((rows, width), BF16), ((seqs, pairs, 2, SEQ), F32)],
        flops=16 * rows * width * SEQ,
        prefetch=1,
        moved=8 * rows * width,
    )(shift, query, key, value)


def attend_back_body(
    count, shift_ref, q_ref, k_ref, v_ref, g_ref, sum_ref, cos_ref, sin_ref, dq_ref, dk_ref, dv_ref
):
    queries, keys, values, grads = (
        in_place(shift_ref, ref, count) for ref in (q_ref, k_ref, v_ref, g_ref)
    )
    turned = keys.astype(F32).T.astype(BF16)
    dq_heads, dk_heads, dv_heads = [], [], []
    for h in range(2):
        dq, dk, dv = [], [], []
        for b in range(2):
            reach = (b + 1) * HALF_SEQ
            query = queries[span_of(b), head_of(h)]
            grad = grads[span_of(b), head_of(h)]
            scores = causal(nt(keys[:reach, head_of(h)], query * BF16(FACTOR)))
            probs = jnp.exp(scores - sum_ref[0, 0, h : h + 1, span_of(b)])
            probs_grad = nt(values[:reach, head_of(h)], grad)
            inner = jnp.sum(probs * probs_grad, axis=0, keepdims=True)
            score_grad = (probs * (probs_grad - inner)).astype(BF16)
            dv.append(nn(probs.astype(BF16), grad))
            dk.append(nn(score_grad, query))
            dq.append(nn(turned[head_of(h), :reach], score_grad))
        for parts, heads in ((dk, dk_heads), (dv, dv_heads)):
            heads.append(
                jnp.concatenate([parts[1][:HALF_SEQ] + parts[0], parts[1][HALF_SEQ:]], axis=0)
            )
        dq_heads.append(jnp.concatenate(dq, axis=1))
    dq = jnp.concatenate(dq_heads, axis=0).T * FACTOR
    dk = jnp.concatenate(dk_heads, axis=1) * FACTOR
    dv = jnp.concatenate(dv_heads, axis=1).astype(BF16)
    cosine, sine = cos_ref[...], sin_ref[...]
    put_back(shift_ref, dq_ref, count, (dq * cosine - turn(dq) * sine).astype(BF16))
    put_back(shift_ref, dk_ref, count, (dk * cosine - turn(dk) * sine).astype(BF16))
    put_back(shift_ref, dv_ref, count, dv)


def attend_back(chain, shift, count, query, key, value, grad, logsum, tables):
    rows, width = query.shape
    seqs, pairs = rows // SEQ, width // PAIR
    tile = pl.BlockSpec((SEQ, PAIR), lambda s, p, _: (s, p))
    return chain.call(
        functools.partial(attend_back_body, count),
        (seqs, pairs),
        [tile] * 4
        + [pl.BlockSpec((1, 1, 2, SEQ), lambda s, p, _: (s, p, 0, 0))]
        + [whole((SEQ, PAIR))] * 2,
        [tile] * 3,
        [((rows, width), BF16)] * 3,
        flops=40 * rows * width * SEQ,
        prefetch=1,
        moved=14 * rows * width,
    )(shift, query, key, value, grad, logsum, *tables)


def local(
    chips,
    group,
    tokens,
    attn_gain,
    query_weight,
    key_weight,
    value_weight,
    output_weight,
    ffn_gain,
    gate_weight,
    up_weight,
    down_weight,
    cotangent,
):
    line = jnp.asarray(chips.table)[lax.axis_index("dp")]
    rows, model = tokens.shape
    count = SEQ // rows
    shift = lax.axis_index("tensor") % count
    row = jnp.arange(SEQ, dtype=jnp.int32)
    places = rope_tables(row)
    tables = rope_tables((row // rows ^ shift) * rows + row % rows)
    shift = jnp.reshape(shift, (1,)).astype(jnp.int32)
    early = (*places, *tables, line, shift)
    depth, own = query_weight.shape
    hidden_units = gate_weight.shape[1]
    chain = Chain()

    def gather(piece):
        return Gather(chips, chain, chain.join(piece)[0])

    def spread_of(values):
        return Spread(group, chain, chain.join(values)[0])

    def fold_of(part):
        own_part, sent = part
        sent = chain.join(*sent[0], *sent[1])
        return Fold(group, chain, own_part, [sent[: group.bits], sent[group.bits :]])

    def grads_of(left, rights):
        got = [None]
        chain.ask(weight_grads(chain, left, 1, rights)[0], got, 0, chips.other)

        def mine(**how):
            if got[0] is None:
                chain.flush()
            blocks = weight_grads(chain, left, 0, rights, got[0], chips.bits)
            return Sums(chips, chain, blocks, **how)

        return mine

    extra = jnp.concatenate([attn_gain, ffn_gain, jnp.zeros((4 * own - 2 * depth,), BF16)])
    attn = jnp.concatenate([query_weight, key_weight, value_weight, output_weight.T], axis=1)
    attn = gather(jnp.concatenate([attn, jnp.broadcast_to(extra, (16, 4 * own))], axis=0))
    spread = spread_of(tokens)
    grads_spread = spread_of(cotangent)
    grads_spread.later = []
    down_turned, *early = chain.join(down_weight.T, *early)
    places, tables, line, shift = early[:2], early[2:4], early[4], early[5]
    chain.end(attn, spread, grads_spread)
    chain.end(attn, spread)
    all_tokens = spread.blocks()
    attn = attn.pieces()
    pair = gather(jnp.concatenate([gate_weight, up_weight], axis=1))
    w_query, w_key, w_value, w_output = [Weight(attn, depth, i * own, own) for i in range(4)]
    gains = jnp.concatenate(
        [piece[depth : depth + 1, : 2 * depth].reshape(2, depth) for piece in attn], axis=1
    ).astype(F32)

    group_one = ordered(chain, norm_body, line, gains, all_tokens)
    grads_spread.resume()
    query, key, value = project(chain, group_one, tables, w_query, w_key, w_value)
    mixed, logsum = attend(chain, shift, count, query, key, value)
    out_part = times_trans(chain, [(mixed, w_output)], group)
    fold = fold_of(out_part)
    chain.end(fold, pair, grads_spread)
    grad_rows = ordered(chain, order_body, line, gains, grads_spread.blocks())
    chain.end(fold)
    attended = fold.total()
    middle, second = by_rows(
        chain, middle_body, line, tokens, gains, attended, [], [F32, BF16]
    )
    spread = spread_of(second)
    chain.end(spread, pair)
    pair = pair.pieces()
    down = gather(down_turned)
    chain.end(spread)
    group_two = spread.blocks()
    w_gate = Weight(pair, depth, 0, hidden_units)
    w_up = Weight(pair, depth, hidden_units, hidden_units)
    hidden, slope, silu = gate_up(chain, group_two, w_gate, w_up)

    mine = grads_of(grad_rows, [hidden])
    chain.end(down)
    chain.flush()
    down_sum = mine()
    w_down = Weight(down.pieces(), depth, 0, hidden_units)
    gate_grad, up_grad = hidden_back(chain, grad_rows, w_down, slope, silu)
    mine_gate = grads_of(group_two, [gate_grad])
    chain.end(down_sum)
    second_part = times_trans(chain, [(gate_grad, w_gate), (up_grad, w_up)], group)
    mine_up = grads_of(group_two, [up_grad])
    gate_sum = mine_gate(hold=True)
    chain.end(down_sum)
    fold = fold_of(second_part)
    up_sum = mine_up(apart=True)
    chain.end(gate_sum, fold)
    result_part = times_trans(chain, [(hidden, w_down)], group)
    chain.end(fold)
    second_grad = fold.total()
    middle_grad, low_grad = by_rows(
        chain, second_back_body, line, cotangent, gains, second_grad, [middle], [F32, BF16]
    )
    spread = spread_of(low_grad)
    chain.end(up_sum)
    gate_sum.resume()
    (down_sum,) = finish(chain, down_sum.terms())
    chain.end(spread)
    attn_grads = spread.blocks()

    mixed_grad = mixed_back(chain, attn_grads, w_output)
    mine_out = grads_of(attn_grads, [mixed])
    chain.end(gate_sum)
    up_sum.send_half(0)
    fold = fold_of(result_part)
    query_back, key_back, value_back = attend_back(
        chain, shift, count, query, key, value, mixed_grad, logsum, places
    )
    mine_qkv = grads_of(group_one, [query_back, key_back, value_back])
    chain.end(up_sum, fold)
    up_sum.send_half(1)
    out_sum = mine_out(hold=True)
    qkv_sum = mine_qkv(cut_in_two=True)
    chain.end(fold, out_sum)
    result_part = fold.total()
    first_part = times_trans(
        chain, [(query_back, w_query), (key_back, w_key), (value_back, w_value)], group
    )
    chain.end(up_sum, qkv_sum)
    fold = fold_of(first_part)
    out_sum.resume()
    up_sum, up_inner = finish(chain, up_sum.terms(), [up_weight])
    gate_sum, gate_inner = finish(chain, gate_sum.terms(), [gate_weight])
    (layer_out,) = by_rows(chain, result_body, line, middle, gains, result_part, [], [BF16])
    chain.end(fold)
    chain.end(fold)
    first_grad = fold.total()
    (input_grad,) = by_rows(
        chain, first_back_body, line, tokens, gains, first_grad, [middle_grad], [F32]
    )
    chain.end(qkv_sum)
    query_sum, key_sum, value_sum, qkv_inner = finish(
        chain, qkv_sum.terms(), [query_weight, key_weight, value_weight]
    )
    gain_one_total, gain_two_total = lax.psum(
        (
            qkv_inner / attn_gain.astype(F32),
            (gate_inner + up_inner) / ffn_gain.astype(F32),
        ),
        "tensor",
    )
    (gain_one_total,) = chain.join(gain_one_total)
    (out_sum,) = finish(chain, out_sum.terms())
    return (
        layer_out,
        input_grad,
        gain_one_total,
        query_sum,
        key_sum,
        value_sum,
        out_sum,
        gain_two_total,
        gate_sum,
        up_sum,
        down_sum,
    )


def solution(mesh):
    in_specs = (
        P(("dp", "tensor"), None),
        P("dp"),
        P("dp", "tensor"),
        P("dp", "tensor"),
        P("dp", "tensor"),
        P("tensor", "dp"),
        P("dp"),
        P("dp", "tensor"),
        P("dp", "tensor"),
        P("tensor", "dp"),
        P(("dp", "tensor"), None),
    )
    out_specs = (
        P(("dp", "tensor"), None),
        P(("dp", "tensor"), None),
        P("dp"),
        P("dp", "tensor"),
        P("dp", "tensor"),
        P("dp", "tensor"),
        P("tensor", "dp"),
        P("dp"),
        P("dp", "tensor"),
        P("dp", "tensor"),
        P("tensor", "dp"),
    )
    chips = Chips(mesh.shape["dp"])
    size = mesh.shape["tensor"]
    links = [[(i, i ^ 1 << b) for i in range(size)] for b in range(size.bit_length() - 1)]
    group = Group(links, "tensor")

    def run(*arrays):
        return local(chips, group, *arrays)

    return jax.shard_map(run, mesh=mesh, in_specs=in_specs, out_specs=out_specs, check_vma=False)
```

```python
import functools

import jax
import jax.numpy as jnp
import numpy as np
from jax import lax
from jax.experimental import pallas as pl
from jax.experimental.pallas import tpu as pltpu
from jax.sharding import PartitionSpec as P

HEAD_DIM = 64
SEQ = 512
EPS = 1e-05
THETA = 130000.0
BF16 = jnp.bfloat16
F32 = jnp.float32
FACTOR = HEAD_DIM**-0.5
PAIR = 2 * HEAD_DIM
HALF_SEQ = SEQ // 2
VMEM_LIMIT = 58 << 20
COST_SHARE = 4096


class Chain:
    def __init__(self):
        self.token = jnp.zeros((8, 128), F32)
        self.swaps, self.asked = [], []

    def join(self, *values):
        *values, self.token = lax.optimization_barrier((*values, self.token))
        return values

    def gate(self, *values):
        swaps, self.swaps = self.swaps, []
        asked, self.asked = self.asked, []
        joined = self.join(
            *values, *[held[i] for held, i in swaps], *[source for source, _, _, _ in asked]
        )
        for (held, i), value in zip(swaps, joined[len(values) :]):
            held[i] = value
        for (_, held, i, swap), value in zip(asked, joined[len(values) + len(swaps) :]):
            held[i] = swap(value)
            self.swaps.append((held, i))
        return joined[: len(values)]

    def end(self, *transfers):
        counts = [len(t.flying) for t in transfers]
        got = self.gate(*[value for t in transfers for value in t.flying])
        for t, count in zip(transfers, counts):
            if count:
                t.go_on(got[:count])
            got = got[count:]

    def ask(self, source, held, i, swap):
        self.asked.append((source, held, i, swap))

    def flush(self):
        for source, held, i, swap in self.asked:
            held[i] = swap(source)
        self.asked = []

    def call(self, body, grid, ins, outs, shapes, flops, scratch=(), prefetch=0, moved=0):
        first = prefetch + len(ins)
        second = first + 1 + len(outs)
        anywhere = pl.BlockSpec(memory_space=pl.ANY)

        def wrapped(*refs):
            body(*refs[:first], *refs[first + 1 : second], *refs[second + 1 :])

        run = pl.pallas_call(
            wrapped,
            grid_spec=pltpu.PrefetchScalarGridSpec(
                num_scalar_prefetch=prefetch,
                grid=grid,
                in_specs=[*ins, anywhere],
                out_specs=[*outs, anywhere],
                scratch_shapes=list(scratch),
            ),
            out_shape=[jax.ShapeDtypeStruct(s, t) for s, t in [*shapes, ((8, 128), F32)]],
            compiler_params=pltpu.CompilerParams(
                vmem_limit_bytes=VMEM_LIMIT, dimension_semantics=("arbitrary",) * len(grid)
            ),
            cost_estimate=pl.CostEstimate(
                flops=flops // COST_SHARE, bytes_accessed=moved // COST_SHARE, transcendentals=0
            ),
        )

        def with_token(*args):
            *results, self.token = run(*args, self.token)
            return results

        return with_token


class Chips:
    def __init__(self, size):
        self.bits = (size // 2).bit_length() - 1
        self.size = size
        self.swap = [(i, i ^ 1) for i in range(size)]
        self.links = [
            [(i, i ^ 2 << self.bits - 1 - p) for i in range(size)] for p in range(self.bits)
        ]
        flips = [
            sum(1 << self.bits - 1 - p for p in range(self.bits) if v >> p & 1)
            for v in range(1 << self.bits)
        ]
        table = [[i ^ 2 * f for f in flips] + [i ^ 2 * f ^ 1 for f in flips] for i in range(size)]
        self.table = np.array(table, np.int32)

    def send(self, value, p):
        return lax.ppermute(value, "dp", self.links[p])

    def other(self, value):
        return lax.ppermute(value, "dp", self.swap)


class Gather:
    def __init__(self, chips, chain, piece):
        self.chips, self.chain = chips, chain
        self.own = [piece] + [None] * (2**chips.bits - 1)
        self.others = list(self.own)
        self.ask(0)
        self.keys = [1 << p for p in range(chips.bits)]
        self.flying = [chips.send(piece, p) for p in range(chips.bits)]

    def ask(self, v):
        self.chain.ask(self.own[v], self.others, v, self.chips.other)

    def go_on(self, got):
        keys, self.keys, self.flying = self.keys, [], []
        for v, piece in zip(keys, got):
            self.own[v] = piece
            for p in range(v.bit_length(), self.chips.bits):
                self.keys.append(v | 1 << p)
                self.flying.append(self.chips.send(piece, p))
        for v in keys:
            self.ask(v)

    def pieces(self):
        while self.flying:
            self.chain.end(self)
        self.chain.flush()
        return self.own + self.others


class Sums:
    def __init__(self, chips, chain, mine, apart=False, hold=False, cut_in_two=False):
        self.chips, self.chain, self.apart, self.hold = chips, chain, apart, hold
        self.todo = []
        self.cut_in_two = cut_in_two and chips.bits == 2
        self.parts = [mine[0]]
        mine = list(mine[1:])
        self.direct, self.passed = [], []
        for p in range(chips.bits):
            self.direct.append(mine.pop(0))
            self.passed.append(mine.pop(0) if p else None)
        self.p = chips.bits - 1
        if self.cut_in_two:
            self.kinds = [0, 1]
            self.flying = [chips.send(half, 1) for half in self.in_two(self.passed[1])]
            return
        self.kinds = [self.p]
        self.flying = [chips.send(self.passed[self.p], self.p)]

    def in_two(self, values):
        width = values.shape[1] // 2
        return values[:, :width], values[:, width:]

    def go_on(self, got):
        rows = self.parts[0].shape[0]
        kinds, self.kinds, self.flying = self.kinds, [], []
        if self.p == 0:
            self.parts += got
            return
        if self.cut_in_two:
            self.p = 0
            total = self.direct[0].astype(F32) + jnp.concatenate(got, axis=1).astype(F32)
            self.todo = [(None, self.direct[1], 1), (None, total.astype(BF16), 0)]
            self.resume()
            return
        for kind, block in zip(kinds, got):
            if kind is None:
                self.parts.append(block)
                continue
            add = lambda held, first: (
                held.astype(F32) + block[first * rows : first * rows + held.shape[0]].astype(F32)
            ).astype(BF16)
            for q in range(kind):
                self.direct[q] = add(self.direct[q], (1 << q) - 1)
                if q:
                    self.passed[q] = add(self.passed[q], 1 << q)
        p, self.p = self.p, self.p - 1
        if p > 0:
            self.todo.append((None, self.direct[p], p))
        if p > 1:
            self.todo.append((p - 1, self.passed[p - 1], p - 1))
        if p == 1 and not self.apart:
            self.todo.append((None, self.direct[0], 0))
        if not self.hold:
            self.resume()

    def resume(self):
        todo, self.todo = self.todo, []
        values = self.chain.join(*[value for _, value, _ in todo])
        for (kind, _, p), value in zip(todo, values):
            self.kinds.append(kind)
            self.flying.append(self.chips.send(value, p))

    def send_half(self, i):
        while self.p > 0:
            self.chain.end(self)
        width = self.direct[0].shape[1] // 2
        (value,) = self.chain.join(self.direct[0][:, i * width : (i + 1) * width])
        self.kinds.append(None)
        self.flying.append(self.chips.send(value, 0))

    def terms(self):
        while self.flying or self.todo:
            if self.todo:
                self.resume()
            self.chain.end(self)
        return sorted(self.parts, key=lambda part: -part.shape[1])


class Group:
    def __init__(self, links, axes):
        self.links, self.axes = links, axes
        self.bits = len(links)
        self.size = 1 << self.bits
        self.orders = (list(range(self.bits)), list(range(self.bits))[::-1])

    def send(self, value, bit):
        return lax.ppermute(value, self.axes, self.links[bit])

    def messages(self):
        found = []
        for order in self.orders:
            found.append([])
            for top in reversed(range(self.bits)):
                found[-1].append(
                    [
                        1 << order[top] | sum(1 << order[p] for p in range(top) if v >> p & 1)
                        for v in range(1 << top)
                    ]
                )
        return found


class Spread:
    def __init__(self, group, chain, rows):
        self.group, self.chain = group, chain
        self.held = {0: [rows]}
        self.later = None
        self.keys = [(1 << b, None) for b in range(group.bits)]
        self.flying = [group.send(rows, b) for b in range(group.bits)]

    def go_on(self, got):
        fresh = list(zip(self.keys, got))
        self.keys, self.flying = [], []
        for (k, h), block in fresh:
            if h is None:
                self.held[k] = [block]
            else:
                self.held.setdefault(k, [None, None])[h] = block
        for (k, h), block in fresh:
            for way, order in enumerate(self.group.orders):
                if h is not None and h != way:
                    continue
                half = block.shape[1] // 2
                top = max(i for i, bit in enumerate(order) if k >> bit & 1)
                for i in range(top + 1, len(order)):
                    part = block if h is not None else block[:, way * half : (way + 1) * half]
                    self.keys.append((k | 1 << order[i], way))
                    if self.later is not None:
                        self.later.append((part, order[i]))
                    else:
                        self.flying.append(self.group.send(part, order[i]))

        if self.later:
            parts = self.chain.join(*[part for part, _ in self.later])
            self.later = [(part, bit) for part, (_, bit) in zip(parts, self.later)]

    def resume(self):
        later, self.later = self.later, None
        parts = self.chain.join(*[part for part, _ in later])
        self.flying = [self.group.send(part, bit) for part, (_, bit) in zip(parts, later)]

    def blocks(self):
        while self.flying:
            self.chain.end(self)
        return [self.held[k] for k in range(self.group.size)]


class Fold:
    def __init__(self, group, chain, own, sent):
        self.group, self.chain = group, chain
        self.rows = own[0].shape[0]
        self.sent = [list(half) for half in sent]
        self.parts = [[half] for half in own]
        self.wave = 0
        self.start()

    def start(self):
        self.flying = [
            self.group.send(self.sent[h][self.wave], order[self.group.bits - 1 - self.wave])
            for h, order in enumerate(self.group.orders)
        ]

    def go_on(self, got):
        self.wave += 1
        self.flying = []
        for h, block in enumerate(got):
            self.parts[h].append(block)
            for wave in range(self.wave, self.group.bits):
                first = self.rows << (self.group.bits - 1 - wave)
                more = block[first : 2 * first].astype(F32)
                self.sent[h][wave] = (self.sent[h][wave].astype(F32) + more).astype(BF16)
        if self.wave < self.group.bits:
            now = self.chain.join(*[sent[self.wave] for sent in self.sent])
            for sent, value in zip(self.sent, now):
                sent[self.wave] = value
            self.start()

    def total(self):
        while self.flying:
            self.chain.end(self)
        return self.parts


class Weight:
    def __init__(self, pieces, rows, start, width):
        self.pieces, self.rows, self.start, self.width = pieces, rows, start, width
        self.model = len(pieces) * rows

    def tiles(self, tile):
        first = self.start // tile
        return [pl.BlockSpec((self.rows, tile), lambda j: (0, first + j))] * len(self.pieces)


def nn(left, right):
    return lax.dot_general(left, right, (((1,), (0,)), ((), ())), preferred_element_type=F32)


def nt(left, right):
    return lax.dot_general(left, right, (((1,), (1,)), ((), ())), preferred_element_type=F32)


def tn(left, right):
    return lax.dot_general(left, right, (((0,), (0,)), ((), ())), preferred_element_type=F32)


def whole(shape):
    return pl.BlockSpec(shape, lambda *_: (0,) * len(shape))


def place(line_ref, j, width):
    return pl.ds(pl.multiple_of(line_ref[j] * width, 128), width)


def cut(width, j):
    return slice(j * width, (j + 1) * width)


def scale_of(values):
    return lax.rsqrt(jnp.mean(values * values, axis=-1, keepdims=True) + EPS)


def fetch_blocks(counts, refs, held, sems, k, slot, wait):
    first = 0
    for i, count in enumerate(counts):
        copies = []
        half = held.shape[2] // count
        for h in range(count):
            target = held.at[slot, :, pl.ds(h * half, half)]
            copies.append(pltpu.make_async_copy(refs[first + h], target, sems.at[slot, h]))
        first += count

        @pl.when(k == i)
        def _():
            for copy in copies:
                copy.wait() if wait else copy.start()


def fetched(counts, refs, held, sems):
    k = pl.program_id(0)

    @pl.when(k == 0)
    def _():
        fetch_blocks(counts, refs, held, sems, k, 0, False)

    fetch_blocks(counts, refs, held, sems, k + 1, (k + 1) % 2, False)
    fetch_blocks(counts, refs, held, sems, k, k % 2, True)
    return held.at[k % 2]


def norm_body(blocks, counts, line_ref, gain_ref, *refs):
    out_ref, held, sems = refs[sum(counts) :]
    x_ref = fetched(counts, refs, held, sems)
    width = out_ref.shape[1] // blocks
    scale = scale_of(x_ref[...].astype(F32))
    for j in range(blocks):
        part = x_ref[:, place(line_ref, j, width)].astype(F32)
        gain = gain_ref[0:1, cut(width, j)]
        out_ref[:, cut(width, j)] = (part * scale * gain).astype(BF16)


def order_body(blocks, counts, line_ref, gain_ref, *refs):
    out_ref, held, sems = refs[sum(counts) :]
    x_ref = fetched(counts, refs, held, sems)
    width = out_ref.shape[1] // blocks
    for j in range(blocks):
        out_ref[:, cut(width, j)] = x_ref[:, place(line_ref, j, width)]


def ordered(chain, body, line, gains, held):
    counts = [len(block) for block in held]
    rows, model = held[0][0].shape
    n = len(held)
    return chain.call(
        functools.partial(body, line.shape[0], counts),
        (n,),
        [whole(gains.shape)] + [pl.BlockSpec(memory_space=pl.ANY)] * sum(counts),
        [pl.BlockSpec((rows, model), lambda k, *_: (k, 0))],
        [((n * rows, model), BF16)],
        flops=20 * n * rows * model,
        scratch=[pltpu.VMEM((2, rows, model), BF16), pltpu.SemaphoreType.DMA((2, 2))],
        prefetch=1,
        moved=4 * n * rows * model,
    )(line, gains, *[array for block in held for array in block])[0]


def added(refs, span):
    total = refs[0][span, :].astype(F32)
    for ref in refs[1:]:
        total += ref[span, :].astype(F32)
    return total


def middle_body(blocks, m, line_ref, x_ref, gain_ref, *refs):
    middle_ref, out_ref = refs[2 * m :]
    width = x_ref.shape[1] // blocks
    half = x_ref.shape[1] // 2
    span = slice(None)
    middle_ref[:, :half] = added(refs[:m], span)
    middle_ref[:, half:] = added(refs[m : 2 * m], span)
    for j in range(blocks):
        here = x_ref[:, place(line_ref, j, width)].astype(F32)
        middle_ref[:, cut(width, j)] += here
    middle = middle_ref[...]
    out_ref[...] = (middle * scale_of(middle) * gain_ref[1:2, :]).astype(BF16)


def result_body(blocks, m, line_ref, middle_ref, gain_ref, *refs):
    out_ref = refs[2 * m]
    width = middle_ref.shape[1] // blocks
    span = slice(None)
    total = middle_ref[...] + jnp.concatenate(
        [added(refs[:m], span), added(refs[m : 2 * m], span)], axis=1
    )
    for j in range(blocks):
        out_ref[:, place(line_ref, j, width)] = total[:, cut(width, j)].astype(BF16)


def second_back_body(blocks, m, line_ref, dy_ref, gain_ref, *refs):
    middle_ref, out_ref, low_ref = refs[2 * m :]
    width = dy_ref.shape[1] // blocks
    span = slice(None)
    grad = jnp.concatenate([added(refs[:m], span), added(refs[m : 2 * m], span)], axis=1)
    middle = middle_ref[...]
    scale = scale_of(middle)
    normed = middle * scale
    scaled = grad * gain_ref[1:2, :]
    out_ref[...] = scale * (scaled - normed * jnp.mean(scaled * normed, axis=-1, keepdims=True))
    for j in range(blocks):
        out_ref[:, cut(width, j)] += dy_ref[:, place(line_ref, j, width)].astype(F32)
    low_ref[...] = out_ref[...].astype(BF16)


def first_back_body(blocks, m, line_ref, x_ref, gain_ref, *refs):
    above_ref, out_ref = refs[2 * m :]
    width = x_ref.shape[1] // blocks
    span = slice(None)
    scale = scale_of(x_ref[...].astype(F32))
    normed = jnp.concatenate(
        [x_ref[:, place(line_ref, j, width)].astype(F32) for j in range(blocks)], axis=1
    ) * scale
    grad = jnp.concatenate([added(refs[:m], span), added(refs[m : 2 * m], span)], axis=1)
    scaled = grad * gain_ref[0:1, :]
    back = scale * (scaled - normed * jnp.mean(scaled * normed, axis=-1, keepdims=True))
    total = above_ref[...] + back
    for j in range(blocks):
        out_ref[:, place(line_ref, j, width)] = total[:, cut(width, j)]


def by_rows(chain, body, line, first, gains, parts, more, kinds):
    rows, model = first.shape
    half = model // 2
    tile = min(128, rows)
    row = pl.BlockSpec((tile, model), lambda i, *_: (i, 0))
    slim = pl.BlockSpec((tile, half), lambda i, *_: (i, 0))
    m = len(parts[0])
    return chain.call(
        functools.partial(body, line.shape[0], m),
        (rows // tile,),
        [row, whole(gains.shape)] + [slim] * (2 * m) + [row] * len(more),
        [row] * len(kinds),
        [((rows, model), kind) for kind in kinds],
        flops=20 * rows * model,
        prefetch=1,
        moved=rows * model * (2 * m + 4 * len(kinds)),
    )(line, first, gains, *parts[0], *parts[1], *more)


def finish_body(m, halves, n, *refs):
    total = added(refs[:m], slice(None))
    if halves:
        total += jnp.concatenate([ref[...].astype(F32) for ref in refs[m : m + halves]], axis=1)
    m += halves
    weights, outs = refs[m : m + n], refs[m + n :]
    if not n:
        outs[0][...] = total.T
        return
    width = weights[0].shape[1]
    inner = jnp.zeros((total.shape[0], 1), F32)
    for i in range(n):
        part = total[:, cut(width, i)]
        outs[i][...] = part
        inner += jnp.sum(weights[i][...].astype(F32) * part, axis=1, keepdims=True)
    outs[n][...] = jnp.broadcast_to(inner, outs[n].shape)


def finish(chain, terms, weights=()):
    rows, columns = terms[0].shape
    tile = min(128, rows)
    row = pl.BlockSpec((tile, columns), lambda i: (i, 0))
    n = len(weights)
    halves = sum(1 for term in terms if term.shape[1] < columns)
    half = [pl.BlockSpec((tile, columns // 2), lambda i: (i, 0))] * halves
    if n:
        slim = pl.BlockSpec((tile, columns // n), lambda i: (i, 0))
        outs = [slim] * n + [pl.BlockSpec((tile, 128), lambda i: (i, 0))]
        shapes = [((rows, columns // n), F32)] * n + [((rows, 128), F32)]
    else:
        slim = None
        outs = [pl.BlockSpec((columns, tile), lambda i: (0, i))]
        shapes = [((columns, rows), F32)]
    results = chain.call(
        functools.partial(finish_body, len(terms) - halves, halves, n),
        (rows // tile,),
        [row] * (len(terms) - halves) + half + [slim] * n,
        outs,
        shapes,
        flops=4 * rows * columns,
        moved=rows * columns * 12,
    )(*terms, *weights)
    if n:
        results[n] = results[n][:, 0]
    return results


def rope_tables(place):
    half = HEAD_DIM // 2
    freq = THETA ** (-2.0 * jnp.arange(half, dtype=F32) / HEAD_DIM)
    angle = place.astype(F32)[:, None] * freq[None, :]
    cosine, sine = jnp.cos(angle), jnp.sin(angle)
    return (
        jnp.concatenate([cosine] * (PAIR // half), axis=1),
        jnp.concatenate([-sine, sine] * (PAIR // HEAD_DIM), axis=1),
    )


def turn(values):
    half = HEAD_DIM // 2
    width = values.shape[-1]
    lane = lax.broadcasted_iota(jnp.int32, values.shape, 1) % HEAD_DIM
    return jnp.where(
        lane < half, pltpu.roll(values, width - half, 1), pltpu.roll(values, half, 1)
    )


def joined(refs):
    return jnp.concatenate([r[...] for r in refs], axis=0)


def qkv_body(n, x_ref, cos_ref, sin_ref, *refs):
    weights, outs = refs[: 3 * n], refs[3 * n :]
    rows = x_ref.shape[0]
    tile = outs[0].shape[1]
    for i in range(3):
        weight = joined(weights[i * n : (i + 1) * n])
        for s in range(rows // SEQ):
            span = slice(s * SEQ, (s + 1) * SEQ)
            product = nn(x_ref[span, :], weight)
            if i == 2:
                outs[i][span, :] = product.astype(BF16)
                continue
            for t in range(tile // PAIR):
                here = product[:, t * PAIR : (t + 1) * PAIR]
                turned = here * cos_ref[...] + turn(here) * sin_ref[...]
                outs[i][span, t * PAIR : (t + 1) * PAIR] = turned.astype(BF16)


def project(chain, x, tables, query, key, value):
    rows, model = x.shape
    n, width = len(query.pieces), query.width
    tile = min(256, width)
    out = pl.BlockSpec((rows, tile), lambda j: (0, j))
    return chain.call(
        functools.partial(qkv_body, n),
        (width // tile,),
        [whole(x.shape), whole((SEQ, PAIR)), whole((SEQ, PAIR))]
        + query.tiles(tile)
        + key.tiles(tile)
        + value.tiles(tile),
        [out] * 3,
        [((rows, width), BF16)] * 3,
        flops=6 * rows * model * width,
        moved=2 * (rows * model + 3 * model * width + 3 * rows * width),
    )(x, *tables, *query.pieces, *key.pieces, *value.pieces)


def collect(counts, refs, held, sems):
    rows = held.shape[0] // len(counts)
    copies = []
    for k, count in enumerate(counts):
        half = held.shape[1] // count
        for h in range(count):
            target = held.at[pl.ds(k * rows, rows), pl.ds(h * half, half)]
            i = len(copies)
            copies.append(pltpu.make_async_copy(refs[i], target, sems.at[i]))
    for copy in copies:
        copy.start()
    for copy in copies:
        copy.wait()


def gate_body(n, counts, *refs):
    m = sum(counts)
    gate_w, up_w = refs[m : m + n], refs[m + n : m + 2 * n]
    hidden_ref, slope_ref, silu_ref, x_ref, sems = refs[m + 2 * n :]

    @pl.when(pl.program_id(0) == 0)
    def _():
        collect(counts, refs, x_ref, sems)

    gate_weight, up_weight = joined(gate_w), joined(up_w)
    for s in range(x_ref.shape[0] // SEQ):
        span = slice(s * SEQ, (s + 1) * SEQ)
        gate = nn(x_ref[span, :], gate_weight)
        up = nn(x_ref[span, :], up_weight)
        sigm = jax.nn.sigmoid(gate)
        silu = gate * sigm
        hidden_ref[span, :] = (silu * up).astype(BF16)
        silu_ref[span, :] = silu.astype(BF16)
        slope_ref[span, :] = (up * sigm * (1.0 + gate * (1.0 - sigm))).astype(BF16)


def collected(held):
    counts = [len(block) for block in held]
    rows, model = held[0][0].shape
    scratch = [
        pltpu.VMEM((len(held) * rows, model), BF16),
        pltpu.SemaphoreType.DMA((sum(counts),)),
    ]
    arrays = [array for block in held for array in block]
    return counts, arrays, [pl.BlockSpec(memory_space=pl.ANY)] * len(arrays), scratch


def gate_up(chain, held, gate, up):
    counts, arrays, specs, scratch = collected(held)
    rows, model = scratch[0].shape
    n, width = len(gate.pieces), gate.width
    tile = min(256, width)
    out = pl.BlockSpec((rows, tile), lambda j: (0, j))
    return chain.call(
        functools.partial(gate_body, n, counts),
        (width // tile,),
        specs + gate.tiles(tile) + up.tiles(tile),
        [out] * 3,
        [((rows, width), BF16)] * 3,
        flops=4 * rows * model * width,
        scratch=scratch,
        moved=2 * (rows * model + 2 * model * width + 3 * rows * width),
    )(*arrays, *gate.pieces, *up.pieces)


def hidden_back_body(n, g_ref, *refs):
    weight = joined(refs[:n])
    slope_ref, silu_ref, gate_ref, up_ref = refs[n:]
    for s in range(g_ref.shape[0] // SEQ):
        span = slice(s * SEQ, (s + 1) * SEQ)
        grad = nn(g_ref[span, :], weight)
        gate_ref[span, :] = (grad * slope_ref[span, :].astype(F32)).astype(BF16)
        up_ref[span, :] = (grad * silu_ref[span, :].astype(F32)).astype(BF16)


def hidden_back(chain, grads, down, slope, silu):
    rows, model = grads.shape
    n, width = len(down.pieces), down.width
    tile = min(256, width)
    out = pl.BlockSpec((rows, tile), lambda j: (0, j))
    return chain.call(
        functools.partial(hidden_back_body, n),
        (width // tile,),
        [whole(grads.shape)] + down.tiles(tile) + [out] * 2,
        [out] * 2,
        [((rows, width), BF16)] * 2,
        flops=2 * rows * model * width,
        moved=2 * (rows * model + model * width + 4 * rows * width),
    )(grads, *down.pieces, slope, silu)


def mixed_back_body(n, counts, *refs):
    m = sum(counts)
    out_ref, x_ref, sems = refs[m + n :]

    @pl.when(pl.program_id(0) == 0)
    def _():
        collect(counts, refs, x_ref, sems)

    out_ref[...] = nn(x_ref[...], joined(refs[m : m + n])).astype(BF16)


def mixed_back(chain, held, out):
    counts, arrays, specs, scratch = collected(held)
    rows, model = scratch[0].shape
    n, width = len(out.pieces), out.width
    tile = min(256, width)
    return chain.call(
        functools.partial(mixed_back_body, n, counts),
        (width // tile,),
        specs + out.tiles(tile),
        [pl.BlockSpec((rows, tile), lambda j: (0, j))],
        [((rows, width), BF16)],
        flops=2 * rows * model * width,
        scratch=scratch,
        moved=2 * (rows * model + model * width + rows * width),
    )(*arrays, *out.pieces)[0]


def trans_body(n, starts, targets, *refs):
    parts, blocks = len(starts), len(targets[0])
    lefts = refs[:parts]
    pieces = refs[parts : parts * (n + 1)]
    outs = refs[parts * (n + 1) : -4]
    held, ready, sems, out_sems = refs[-4:]
    j = pl.program_id(0)
    depth, width = held.shape[2:]
    rows = ready.shape[1] // blocks

    def copy(i, p, slot):
        source = pieces[p * n + i].at[pl.ds(0, depth), pl.ds(starts[p], width)]
        return pltpu.make_async_copy(source, held.at[slot, p], sems.at[slot, p])

    def fetch(step, slot):
        for i in range(n):

            @pl.when(step == i)
            def _():
                for p in range(parts):
                    copy(i, p, slot).start()

    def leave(slot, k, array, first, column):
        target = outs[array].at[pl.ds(first, rows), pl.ds(column, depth)]
        source = ready.at[slot, pl.ds(k * rows, rows), :]
        return pltpu.make_async_copy(source, target, out_sems.at[slot, k])

    def left(slot):
        for k in range(blocks):
            leave(slot, k, 0, 0, 0).wait()

    @pl.when(j == 0)
    def _():
        fetch(j, 0)

    @pl.when(j + 1 < n)
    def _():
        fetch(j + 1, (j + 1) % 2)

    slot = j % 2
    for p in range(parts):
        copy(0, p, slot).wait()

    @pl.when(j >= 2)
    def _():
        left(slot)

    for s in range(blocks * rows // SEQ):
        span = slice(s * SEQ, (s + 1) * SEQ)
        total = nt(lefts[0][span, :], held[slot, 0])
        for p in range(1, parts):
            total += nt(lefts[p][span, :], held[slot, p])
        ready[slot, span, :] = total.astype(BF16)
    column = pl.multiple_of(j % (n // 2) * depth, 128)
    for h in range(2):

        @pl.when((j >= n // 2) == (h == 1))
        def _():
            for k, (array, first) in enumerate(targets[h]):
                leave(slot, k, array, first, column).start()

    @pl.when(j == n - 1)
    def _():
        left(1 - slot)
        left(slot)


def times_trans(chain, parts, group):
    weights = [weight for _, weight in parts]
    n, depth, width = len(weights[0].pieces), weights[0].rows, weights[0].width
    rows = parts[0][0].shape[0]
    half = weights[0].model // 2
    size = rows // group.size
    messages = group.messages()
    shapes = [((size, half), BF16)] * 2
    targets = [{0: (0, 0)}, {0: (1, 0)}]
    for h in range(2):
        for keys in messages[h]:
            for i, k in enumerate(keys):
                targets[h][k] = (len(shapes), i * size)
            shapes.append(((len(keys) * size, half), BF16))
    targets = [[t[k] for k in range(group.size)] for t in targets]
    anywhere = pl.BlockSpec(memory_space=pl.ANY)
    outs = chain.call(
        functools.partial(trans_body, n, [weight.start for weight in weights], targets),
        (n,),
        [whole((rows, width))] * len(parts) + [anywhere] * (n * len(parts)),
        [anywhere] * len(shapes),
        shapes,
        flops=4 * rows * half * width * len(parts),
        scratch=[
            pltpu.VMEM((2, len(parts), depth, width), BF16),
            pltpu.VMEM((2, rows, depth), BF16),
            pltpu.SemaphoreType.DMA((2, len(parts))),
            pltpu.SemaphoreType.DMA((2, group.size)),
        ],
        moved=2 * (2 * rows * half + len(parts) * (rows + 2 * half) * width),
    )(*[left for left, _ in parts], *[piece for weight in weights for piece in weight.pieces])
    m = group.bits
    return outs[:2], [outs[2 : 2 + m], outs[2 + m :]]


def turn_body(counts, *refs):
    out_ref, held, sems = refs[sum(counts) :]
    j = pl.program_id(0)
    width = out_ref.shape[0]

    @pl.when(j == 0)
    def _():
        collect(counts, refs, held, sems)

    for k in range(len(counts)):
        rows = held.shape[0] // len(counts)
        span = pl.ds(pl.multiple_of(j * width, 128), width)
        out_ref[:, cut(rows, k)] = held[cut(rows, k), span].T


def turned(chain, left):
    counts, arrays, specs, scratch = collected(left if isinstance(left, list) else [[left]])
    rows, model = scratch[0].shape
    tile = 256
    return chain.call(
        functools.partial(turn_body, counts),
        (model // tile,),
        specs,
        [pl.BlockSpec((tile, rows), lambda j: (j, 0))],
        [((model, rows), BF16)],
        flops=rows * model,
        scratch=scratch,
        moved=4 * rows * model,
    )(*arrays)[0]


def grad_body(parts, got, blocks, steps, *refs):
    lefts, refs = refs[:blocks], refs[blocks:]
    rights, refs = refs[:parts], refs[parts:]
    got_ref = refs[0] if got else None
    outs, turned_ref = refs[got:], lefts[0]
    j = pl.program_id(0)
    if blocks > 1:
        outs, turned_ref = refs[got:-1], refs[-1]

        @pl.when(j == 0)
        def _():
            rows = turned_ref.shape[1] // blocks
            for k in range(blocks):
                turned_ref[:, cut(rows, k)] = lefts[k][...].T

    for i in range(parts):

        @pl.when((j >= i * steps) & (j < (i + 1) * steps))
        def _():
            total = nn(turned_ref[...], rights[i][...])
            if got:
                total += got_ref[...].astype(F32)
            total = total.astype(BF16)
            first = 0
            for out_ref in outs:
                count = out_ref.shape[0]
                out_ref[...] = total[first : first + count]
                first += count


def weight_grads(chain, left, which, rights, got=None, bits=0):
    rows, width = rights[0].shape
    parts = len(rights)
    tile = min(512, width)
    steps = width // tile
    if isinstance(left, list):
        lefts = [block[0] if len(block) == 1 else block[which] for block in left]
        half = left[0][0].shape[1] // 2
        places = [which if len(block) == 1 else 0 for block in left]
        ins = [
            pl.BlockSpec((rows // len(left), half), functools.partial(lambda at, j: (0, at), at))
            for at in places
        ]
        scratch = [pltpu.VMEM((half, rows), BF16)]
    else:
        lefts, half = [left], left.shape[0] // 2
        ins = [pl.BlockSpec((half, rows), lambda j: (which, 0))]
        scratch = []
    for i in range(parts):
        ins.append(
            pl.BlockSpec(
                (rows, tile),
                functools.partial(
                    lambda first, j: (0, jnp.clip(j - first, 0, steps - 1)), i * steps
                ),
            )
        )
    column = lambda j: (0, j)
    more = [] if got is None else [got]
    sizes = [half >> bits]
    for p in range(bits):
        sizes += [sizes[0], ((1 << p) - 1) * sizes[0]] if p else [sizes[0]]
    return chain.call(
        functools.partial(grad_body, parts, len(more), len(lefts), steps),
        (parts * steps,),
        ins + [pl.BlockSpec((half, tile), column)] * len(more),
        [pl.BlockSpec((size, tile), column) for size in sizes],
        [((size, parts * width), BF16) for size in sizes],
        flops=2 * rows * half * width * parts,
        scratch=scratch,
        moved=2 * (rows * half + parts * (rows + half) * width),
    )(*lefts, *rights, *more)


def causal(scores):
    past = scores.shape[0] - HALF_SEQ
    key = lax.broadcasted_iota(jnp.int32, (HALF_SEQ, HALF_SEQ), 0)
    query = lax.broadcasted_iota(jnp.int32, (HALF_SEQ, HALF_SEQ), 1)
    last = jnp.where(key <= query, scores[past:], -1e30)
    return last if past == 0 else jnp.concatenate([scores[:past], last], axis=0)


def head_of(h):
    return slice(h * HEAD_DIM, (h + 1) * HEAD_DIM)


def span_of(b):
    return slice(b * HALF_SEQ, (b + 1) * HALF_SEQ)


def in_place(shift_ref, ref, count):
    rows = SEQ // count
    spans = [pl.ds(pl.multiple_of((i ^ shift_ref[0]) * rows, rows), rows) for i in range(count)]
    return jnp.concatenate([ref[span, :] for span in spans], axis=0)


def put_back(shift_ref, ref, count, values):
    rows = SEQ // count
    for i in range(count):
        ref[pl.ds(pl.multiple_of((i ^ shift_ref[0]) * rows, rows), rows), :] = values[cut(rows, i)]


def attend_body(count, shift_ref, q_ref, k_ref, v_ref, out_ref, sum_ref):
    queries, keys = in_place(shift_ref, q_ref, count), in_place(shift_ref, k_ref, count)
    values = in_place(shift_ref, v_ref, count).astype(F32).T.astype(BF16)
    heads = []
    for h in range(2):
        blocks = []
        for b in range(2):
            reach = (b + 1) * HALF_SEQ
            query = queries[span_of(b), head_of(h)] * BF16(FACTOR)
            scores = causal(nt(keys[:reach, head_of(h)], query))
            top = jnp.max(scores, axis=0, keepdims=True)
            expo = jnp.exp(scores - top)
            total = jnp.sum(expo, axis=0, keepdims=True)
            mixed = nn(values[head_of(h), :reach], expo.astype(BF16))
            blocks.append(mixed * (1.0 / total))
            sum_ref[0, 0, h : h + 1, span_of(b)] = top + jnp.log(total)
        heads.append(jnp.concatenate(blocks, axis=1))
    put_back(shift_ref, out_ref, count, jnp.concatenate(heads, axis=0).T.astype(BF16))


def attend(chain, shift, count, query, key, value):
    rows, width = query.shape
    seqs, pairs = rows // SEQ, width // PAIR
    tile = pl.BlockSpec((SEQ, PAIR), lambda s, p, _: (s, p))
    return chain.call(
        functools.partial(attend_body, count),
        (seqs, pairs),
        [tile] * 3,
        [tile, pl.BlockSpec((1, 1, 2, SEQ), lambda s, p, _: (s, p, 0, 0))],
        [((rows, width), BF16), ((seqs, pairs, 2, SEQ), F32)],
        flops=16 * rows * width * SEQ,
        prefetch=1,
        moved=8 * rows * width,
    )(shift, query, key, value)


def attend_back_body(
    count, shift_ref, q_ref, k_ref, v_ref, g_ref, sum_ref, cos_ref, sin_ref, dq_ref, dk_ref, dv_ref
):
    queries, keys, values, grads = (
        in_place(shift_ref, ref, count) for ref in (q_ref, k_ref, v_ref, g_ref)
    )
    turned = keys.astype(F32).T.astype(BF16)
    dq_heads, dk_heads, dv_heads = [], [], []
    for h in range(2):
        dq, dk, dv = [], [], []
        for b in range(2):
            reach = (b + 1) * HALF_SEQ
            query = queries[span_of(b), head_of(h)]
            grad = grads[span_of(b), head_of(h)]
            scores = causal(nt(keys[:reach, head_of(h)], query * BF16(FACTOR)))
            probs = jnp.exp(scores - sum_ref[0, 0, h : h + 1, span_of(b)])
            probs_grad = nt(values[:reach, head_of(h)], grad)
            inner = jnp.sum(probs * probs_grad, axis=0, keepdims=True)
            score_grad = (probs * (probs_grad - inner)).astype(BF16)
            dv.append(nn(probs.astype(BF16), grad))
            dk.append(nn(score_grad, query))
            dq.append(nn(turned[head_of(h), :reach], score_grad))
        for parts, heads in ((dk, dk_heads), (dv, dv_heads)):
            heads.append(
                jnp.concatenate([parts[1][:HALF_SEQ] + parts[0], parts[1][HALF_SEQ:]], axis=0)
            )
        dq_heads.append(jnp.concatenate(dq, axis=1))
    dq = jnp.concatenate(dq_heads, axis=0).T * FACTOR
    dk = jnp.concatenate(dk_heads, axis=1) * FACTOR
    dv = jnp.concatenate(dv_heads, axis=1).astype(BF16)
    cosine, sine = cos_ref[...], sin_ref[...]
    put_back(shift_ref, dq_ref, count, (dq * cosine - turn(dq) * sine).astype(BF16))
    put_back(shift_ref, dk_ref, count, (dk * cosine - turn(dk) * sine).astype(BF16))
    put_back(shift_ref, dv_ref, count, dv)


def attend_back(chain, shift, count, query, key, value, grad, logsum, tables):
    rows, width = query.shape
    seqs, pairs = rows // SEQ, width // PAIR
    tile = pl.BlockSpec((SEQ, PAIR), lambda s, p, _: (s, p))
    return chain.call(
        functools.partial(attend_back_body, count),
        (seqs, pairs),
        [tile] * 4
        + [pl.BlockSpec((1, 1, 2, SEQ), lambda s, p, _: (s, p, 0, 0))]
        + [whole((SEQ, PAIR))] * 2,
        [tile] * 3,
        [((rows, width), BF16)] * 3,
        flops=40 * rows * width * SEQ,
        prefetch=1,
        moved=14 * rows * width,
    )(shift, query, key, value, grad, logsum, *tables)


def local(
    chips,
    group,
    tokens,
    attn_gain,
    query_weight,
    key_weight,
    value_weight,
    output_weight,
    ffn_gain,
    gate_weight,
    up_weight,
    down_weight,
    cotangent,
):
    line = jnp.asarray(chips.table)[lax.axis_index("dp")]
    rows, model = tokens.shape
    count = SEQ // rows
    shift = lax.axis_index("tensor") % count
    row = jnp.arange(SEQ, dtype=jnp.int32)
    places = rope_tables(row)
    tables = rope_tables((row // rows ^ shift) * rows + row % rows)
    shift = jnp.reshape(shift, (1,)).astype(jnp.int32)
    early = (*places, *tables, line, shift)
    depth, own = query_weight.shape
    hidden_units = gate_weight.shape[1]
    chain = Chain()

    def gather(piece):
        return Gather(chips, chain, chain.join(piece)[0])

    def spread_of(values):
        return Spread(group, chain, chain.join(values)[0])

    def fold_of(part):
        own_part, sent = part
        sent = chain.join(*sent[0], *sent[1])
        return Fold(group, chain, own_part, [sent[: group.bits], sent[group.bits :]])

    def grads_of(left, rights):
        got = [None]
        chain.ask(weight_grads(chain, left, 1, rights)[0], got, 0, chips.other)

        def mine(**how):
            if got[0] is None:
                chain.flush()
            blocks = weight_grads(chain, left, 0, rights, got[0], chips.bits)
            return Sums(chips, chain, blocks, **how)

        return mine

    extra = jnp.concatenate([attn_gain, ffn_gain, jnp.zeros((4 * own - 2 * depth,), BF16)])
    attn = jnp.concatenate([query_weight, key_weight, value_weight, output_weight.T], axis=1)
    attn = gather(jnp.concatenate([attn, jnp.broadcast_to(extra, (16, 4 * own))], axis=0))
    spread = spread_of(tokens)
    grads_spread = spread_of(cotangent)
    grads_spread.later = []
    down_turned, *early = chain.join(down_weight.T, *early)
    places, tables, line, shift = early[:2], early[2:4], early[4], early[5]
    chain.end(attn, spread, grads_spread)
    chain.end(attn, spread)
    all_tokens = spread.blocks()
    attn = attn.pieces()
    pair = gather(jnp.concatenate([gate_weight, up_weight], axis=1))
    w_query, w_key, w_value, w_output = [Weight(attn, depth, i * own, own) for i in range(4)]
    gains = jnp.concatenate(
        [piece[depth : depth + 1, : 2 * depth].reshape(2, depth) for piece in attn], axis=1
    ).astype(F32)

    group_one = ordered(chain, norm_body, line, gains, all_tokens)
    grads_spread.resume()
    query, key, value = project(chain, group_one, tables, w_query, w_key, w_value)
    mixed, logsum = attend(chain, shift, count, query, key, value)
    out_part = times_trans(chain, [(mixed, w_output)], group)
    fold = fold_of(out_part)
    turned_one = turned(chain, group_one)
    chain.end(fold, pair, grads_spread)
    grad_rows = ordered(chain, order_body, line, gains, grads_spread.blocks())
    chain.end(fold)
    attended = fold.total()
    middle, second = by_rows(
        chain, middle_body, line, tokens, gains, attended, [], [F32, BF16]
    )
    spread = spread_of(second)
    turned_grads = turned(chain, grad_rows)
    chain.end(spread, pair)
    pair = pair.pieces()
    down = gather(down_turned)
    chain.end(spread)
    group_two = spread.blocks()
    w_gate = Weight(pair, depth, 0, hidden_units)
    w_up = Weight(pair, depth, hidden_units, hidden_units)
    hidden, slope, silu = gate_up(chain, group_two, w_gate, w_up)

    mine = grads_of(turned_grads, [hidden])
    chain.end(down)
    chain.flush()
    turned_two = turned(chain, group_two)
    down_sum = mine()
    w_down = Weight(down.pieces(), depth, 0, hidden_units)
    gate_grad, up_grad = hidden_back(chain, grad_rows, w_down, slope, silu)
    mine_gate = grads_of(turned_two, [gate_grad])
    chain.end(down_sum)
    second_part = times_trans(chain, [(gate_grad, w_gate), (up_grad, w_up)], group)
    mine_up = grads_of(turned_two, [up_grad])
    gate_sum = mine_gate(hold=True)
    chain.end(down_sum)
    fold = fold_of(second_part)
    up_sum = mine_up(apart=True)
    chain.end(gate_sum, fold)
    result_part = times_trans(chain, [(hidden, w_down)], group)
    chain.end(fold)
    second_grad = fold.total()
    middle_grad, low_grad = by_rows(
        chain, second_back_body, line, cotangent, gains, second_grad, [middle], [F32, BF16]
    )
    spread = spread_of(low_grad)
    chain.end(up_sum)
    gate_sum.resume()
    (down_sum,) = finish(chain, down_sum.terms())
    chain.end(spread)
    attn_grads = spread.blocks()

    mixed_grad = mixed_back(chain, attn_grads, w_output)
    mine_out = grads_of(attn_grads, [mixed])
    chain.end(gate_sum)
    up_sum.send_half(0)
    fold = fold_of(result_part)
    query_back, key_back, value_back = attend_back(
        chain, shift, count, query, key, value, mixed_grad, logsum, places
    )
    mine_qkv = grads_of(turned_one, [query_back, key_back, value_back])
    out_sum = mine_out(hold=True)
    chain.end(up_sum, fold)
    up_sum.send_half(1)
    qkv_sum = mine_qkv(cut_in_two=True)
    chain.end(fold, out_sum)
    result_part = fold.total()
    first_part = times_trans(
        chain, [(query_back, w_query), (key_back, w_key), (value_back, w_value)], group
    )
    chain.end(up_sum, qkv_sum)
    fold = fold_of(first_part)
    out_sum.resume()
    up_sum, up_inner = finish(chain, up_sum.terms(), [up_weight])
    gate_sum, gate_inner = finish(chain, gate_sum.terms(), [gate_weight])
    (layer_out,) = by_rows(chain, result_body, line, middle, gains, result_part, [], [BF16])
    chain.end(fold)
    chain.end(fold)
    first_grad = fold.total()
    (input_grad,) = by_rows(
        chain, first_back_body, line, tokens, gains, first_grad, [middle_grad], [F32]
    )
    chain.end(qkv_sum)
    query_sum, key_sum, value_sum, qkv_inner = finish(
        chain, qkv_sum.terms(), [query_weight, key_weight, value_weight]
    )
    gain_one_total, gain_two_total = lax.psum(
        (
            qkv_inner / attn_gain.astype(F32),
            (gate_inner + up_inner) / ffn_gain.astype(F32),
        ),
        "tensor",
    )
    (gain_one_total,) = chain.join(gain_one_total)
    (out_sum,) = finish(chain, out_sum.terms())
    return (
        layer_out,
        input_grad,
        gain_one_total,
        query_sum,
        key_sum,
        value_sum,
        out_sum,
        gain_two_total,
        gate_sum,
        up_sum,
        down_sum,
    )


def solution(mesh):
    in_specs = (
        P(("dp", "tensor"), None),
        P("dp"),
        P("dp", "tensor"),
        P("dp", "tensor"),
        P("dp", "tensor"),
        P("tensor", "dp"),
        P("dp"),
        P("dp", "tensor"),
        P("dp", "tensor"),
        P("tensor", "dp"),
        P(("dp", "tensor"), None),
    )
    out_specs = (
        P(("dp", "tensor"), None),
        P(("dp", "tensor"), None),
        P("dp"),
        P("dp", "tensor"),
        P("dp", "tensor"),
        P("dp", "tensor"),
        P("tensor", "dp"),
        P("dp"),
        P("dp", "tensor"),
        P("dp", "tensor"),
        P("tensor", "dp"),
    )
    chips = Chips(mesh.shape["dp"])
    size = mesh.shape["tensor"]
    links = [[(i, i ^ 1 << b) for i in range(size)] for b in range(size.bit_length() - 1)]
    group = Group(links, "tensor")

    def run(*arrays):
        return local(chips, group, *arrays)

    return jax.shard_map(run, mesh=mesh, in_specs=in_specs, out_specs=out_specs, check_vma=False)
```

```python
import functools

import jax
import jax.numpy as jnp
import numpy as np
from jax import lax
from jax.experimental import pallas as pl
from jax.experimental.pallas import tpu as pltpu
from jax.sharding import PartitionSpec as P

HEAD_DIM = 64
SEQ = 512
EPS = 1e-05
THETA = 130000.0
BF16 = jnp.bfloat16
F32 = jnp.float32
FACTOR = HEAD_DIM**-0.5
PAIR = 2 * HEAD_DIM
HALF_SEQ = SEQ // 2
VMEM_LIMIT = 58 << 20
COST_SHARE = 4096


class Chain:
    def __init__(self):
        self.token = jnp.zeros((8, 128), F32)
        self.swaps, self.asked = [], []

    def join(self, *values):
        *values, self.token = lax.optimization_barrier((*values, self.token))
        return values

    def gate(self, *values):
        swaps, self.swaps = self.swaps, []
        asked, self.asked = self.asked, []
        joined = self.join(
            *values, *[held[i] for held, i in swaps], *[source for source, _, _, _ in asked]
        )
        for (held, i), value in zip(swaps, joined[len(values) :]):
            held[i] = value
        for (_, held, i, swap), value in zip(asked, joined[len(values) + len(swaps) :]):
            held[i] = swap(value)
            self.swaps.append((held, i))
        return joined[: len(values)]

    def end(self, *transfers):
        counts = [len(t.flying) for t in transfers]
        got = self.gate(*[value for t in transfers for value in t.flying])
        for t, count in zip(transfers, counts):
            if count:
                t.go_on(got[:count])
            got = got[count:]

    def ask(self, source, held, i, swap):
        self.asked.append((source, held, i, swap))

    def flush(self):
        for source, held, i, swap in self.asked:
            held[i] = swap(source)
        self.asked = []

    def call(self, body, grid, ins, outs, shapes, flops, scratch=(), prefetch=0, moved=0):
        first = prefetch + len(ins)
        second = first + 1 + len(outs)
        anywhere = pl.BlockSpec(memory_space=pl.ANY)

        def wrapped(*refs):
            body(*refs[:first], *refs[first + 1 : second], *refs[second + 1 :])

        run = pl.pallas_call(
            wrapped,
            grid_spec=pltpu.PrefetchScalarGridSpec(
                num_scalar_prefetch=prefetch,
                grid=grid,
                in_specs=[*ins, anywhere],
                out_specs=[*outs, anywhere],
                scratch_shapes=list(scratch),
            ),
            out_shape=[jax.ShapeDtypeStruct(s, t) for s, t in [*shapes, ((8, 128), F32)]],
            compiler_params=pltpu.CompilerParams(
                vmem_limit_bytes=VMEM_LIMIT, dimension_semantics=("arbitrary",) * len(grid)
            ),
            cost_estimate=pl.CostEstimate(
                flops=flops // COST_SHARE, bytes_accessed=moved // COST_SHARE, transcendentals=0
            ),
        )

        def with_token(*args):
            *results, self.token = run(*args, self.token)
            return results

        return with_token


class Chips:
    def __init__(self, size):
        self.bits = (size // 2).bit_length() - 1
        self.size = size
        self.swap = [(i, i ^ 1) for i in range(size)]
        self.links = [
            [(i, i ^ 2 << self.bits - 1 - p) for i in range(size)] for p in range(self.bits)
        ]
        flips = [
            sum(1 << self.bits - 1 - p for p in range(self.bits) if v >> p & 1)
            for v in range(1 << self.bits)
        ]
        table = [[i ^ 2 * f for f in flips] + [i ^ 2 * f ^ 1 for f in flips] for i in range(size)]
        self.table = np.array(table, np.int32)

    def send(self, value, p):
        return lax.ppermute(value, "dp", self.links[p])

    def other(self, value):
        return lax.ppermute(value, "dp", self.swap)


class Gather:
    def __init__(self, chips, chain, piece):
        self.chips, self.chain = chips, chain
        self.own = [piece] + [None] * (2**chips.bits - 1)
        self.others = list(self.own)
        self.ask(0)
        self.keys = [1 << p for p in range(chips.bits)]
        self.flying = [chips.send(piece, p) for p in range(chips.bits)]

    def ask(self, v):
        self.chain.ask(self.own[v], self.others, v, self.chips.other)

    def go_on(self, got):
        keys, self.keys, self.flying = self.keys, [], []
        for v, piece in zip(keys, got):
            self.own[v] = piece
            for p in range(v.bit_length(), self.chips.bits):
                self.keys.append(v | 1 << p)
                self.flying.append(self.chips.send(piece, p))
        for v in keys:
            self.ask(v)

    def pieces(self):
        while self.flying:
            self.chain.end(self)
        self.chain.flush()
        return self.own + self.others


class Sums:
    def __init__(self, chips, chain, mine, apart=False, hold=False, cut_in_two=False):
        self.chips, self.chain, self.apart, self.hold = chips, chain, apart, hold
        self.todo = []
        self.cut_in_two = cut_in_two and chips.bits == 2
        self.parts = [mine[0]]
        mine = list(mine[1:])
        self.direct, self.passed = [], []
        for p in range(chips.bits):
            self.direct.append(mine.pop(0))
            self.passed.append(mine.pop(0) if p else None)
        self.p = chips.bits - 1
        if self.cut_in_two:
            self.kinds = [0, 1]
            self.flying = [chips.send(half, 1) for half in self.in_two(self.passed[1])]
            return
        self.kinds = [self.p]
        self.flying = [chips.send(self.passed[self.p], self.p)]

    def in_two(self, values):
        width = values.shape[1] // 2
        return values[:, :width], values[:, width:]

    def go_on(self, got):
        rows = self.parts[0].shape[0]
        kinds, self.kinds, self.flying = self.kinds, [], []
        if self.p == 0:
            self.parts += got
            return
        if self.cut_in_two:
            self.p = 0
            total = self.direct[0].astype(F32) + jnp.concatenate(got, axis=1).astype(F32)
            self.todo = [(None, self.direct[1], 1), (None, total.astype(BF16), 0)]
            self.resume()
            return
        for kind, block in zip(kinds, got):
            if kind is None:
                self.parts.append(block)
                continue
            add = lambda held, first: (
                held.astype(F32) + block[first * rows : first * rows + held.shape[0]].astype(F32)
            ).astype(BF16)
            for q in range(kind):
                self.direct[q] = add(self.direct[q], (1 << q) - 1)
                if q:
                    self.passed[q] = add(self.passed[q], 1 << q)
        p, self.p = self.p, self.p - 1
        if p > 0:
            self.todo.append((None, self.direct[p], p))
        if p > 1:
            self.todo.append((p - 1, self.passed[p - 1], p - 1))
        if p == 1 and not self.apart:
            self.todo.append((None, self.direct[0], 0))
        if not self.hold:
            self.resume()

    def resume(self):
        todo, self.todo = self.todo, []
        values = self.chain.join(*[value for _, value, _ in todo])
        for (kind, _, p), value in zip(todo, values):
            self.kinds.append(kind)
            self.flying.append(self.chips.send(value, p))

    def send_half(self, i):
        while self.p > 0:
            self.chain.end(self)
        width = self.direct[0].shape[1] // 2
        (value,) = self.chain.join(self.direct[0][:, i * width : (i + 1) * width])
        self.kinds.append(None)
        self.flying.append(self.chips.send(value, 0))

    def terms(self):
        while self.flying or self.todo:
            if self.todo:
                self.resume()
            self.chain.end(self)
        return sorted(self.parts, key=lambda part: -part.shape[1])


class Group:
    def __init__(self, links, axes):
        self.links, self.axes = links, axes
        self.bits = len(links)
        self.size = 1 << self.bits
        self.orders = (list(range(self.bits)), list(range(self.bits))[::-1])

    def send(self, value, bit):
        return lax.ppermute(value, self.axes, self.links[bit])

    def messages(self):
        found = []
        for order in self.orders:
            found.append([])
            for top in reversed(range(self.bits)):
                found[-1].append(
                    [
                        1 << order[top] | sum(1 << order[p] for p in range(top) if v >> p & 1)
                        for v in range(1 << top)
                    ]
                )
        return found


class Spread:
    def __init__(self, group, chain, rows):
        self.group, self.chain = group, chain
        self.held = {0: [rows]}
        self.later = None
        self.keys = [(1 << b, None) for b in range(group.bits)]
        self.flying = [group.send(rows, b) for b in range(group.bits)]

    def go_on(self, got):
        fresh = list(zip(self.keys, got))
        self.keys, self.flying = [], []
        for (k, h), block in fresh:
            if h is None:
                self.held[k] = [block]
            else:
                self.held.setdefault(k, [None, None])[h] = block
        for (k, h), block in fresh:
            for way, order in enumerate(self.group.orders):
                if h is not None and h != way:
                    continue
                half = block.shape[1] // 2
                top = max(i for i, bit in enumerate(order) if k >> bit & 1)
                for i in range(top + 1, len(order)):
                    part = block if h is not None else block[:, way * half : (way + 1) * half]
                    self.keys.append((k | 1 << order[i], way))
                    if self.later is not None:
                        self.later.append((part, order[i]))
                    else:
                        self.flying.append(self.group.send(part, order[i]))

        if self.later:
            parts = self.chain.join(*[part for part, _ in self.later])
            self.later = [(part, bit) for part, (_, bit) in zip(parts, self.later)]

    def resume(self):
        later, self.later = self.later, None
        parts = self.chain.join(*[part for part, _ in later])
        self.flying = [self.group.send(part, bit) for part, (_, bit) in zip(parts, later)]

    def blocks(self):
        while self.flying:
            self.chain.end(self)
        return [self.held[k] for k in range(self.group.size)]


class Fold:
    def __init__(self, group, chain, own, sent):
        self.group, self.chain = group, chain
        self.rows = own[0].shape[0]
        self.sent = [list(half) for half in sent]
        self.parts = [[half] for half in own]
        self.wave = 0
        self.start()

    def start(self):
        self.flying = [
            self.group.send(self.sent[h][self.wave], order[self.group.bits - 1 - self.wave])
            for h, order in enumerate(self.group.orders)
        ]

    def go_on(self, got):
        self.wave += 1
        self.flying = []
        for h, block in enumerate(got):
            self.parts[h].append(block)
        for wave in range(self.wave, self.group.bits):
            sums = add_rows(self.chain, [sent[wave] for sent in self.sent], got)
            for sent, value in zip(self.sent, sums):
                sent[wave] = value
        if self.wave < self.group.bits:
            self.start()

    def total(self):
        while self.flying:
            self.chain.end(self)
        return self.parts


class Weight:
    def __init__(self, pieces, rows, start, width):
        self.pieces, self.rows, self.start, self.width = pieces, rows, start, width
        self.model = len(pieces) * rows

    def tiles(self, tile):
        first = self.start // tile
        return [pl.BlockSpec((self.rows, tile), lambda j: (0, first + j))] * len(self.pieces)


def nn(left, right):
    return lax.dot_general(left, right, (((1,), (0,)), ((), ())), preferred_element_type=F32)


def nt(left, right):
    return lax.dot_general(left, right, (((1,), (1,)), ((), ())), preferred_element_type=F32)


def tn(left, right):
    return lax.dot_general(left, right, (((0,), (0,)), ((), ())), preferred_element_type=F32)


def whole(shape):
    return pl.BlockSpec(shape, lambda *_: (0,) * len(shape))


def place(line_ref, j, width):
    return pl.ds(pl.multiple_of(line_ref[j] * width, 128), width)


def cut(width, j):
    return slice(j * width, (j + 1) * width)


def scale_of(values):
    return lax.rsqrt(jnp.mean(values * values, axis=-1, keepdims=True) + EPS)


def fetch_blocks(counts, refs, held, sems, k, slot, wait):
    first = 0
    for i, count in enumerate(counts):
        copies = []
        half = held.shape[2] // count
        for h in range(count):
            target = held.at[slot, :, pl.ds(h * half, half)]
            copies.append(pltpu.make_async_copy(refs[first + h], target, sems.at[slot, h]))
        first += count

        @pl.when(k == i)
        def _():
            for copy in copies:
                copy.wait() if wait else copy.start()


def fetched(counts, refs, held, sems):
    k = pl.program_id(0)

    @pl.when(k == 0)
    def _():
        fetch_blocks(counts, refs, held, sems, k, 0, False)

    fetch_blocks(counts, refs, held, sems, k + 1, (k + 1) % 2, False)
    fetch_blocks(counts, refs, held, sems, k, k % 2, True)
    return held.at[k % 2]


def norm_body(blocks, counts, line_ref, gain_ref, *refs):
    out_ref, held, sems = refs[sum(counts) :]
    x_ref = fetched(counts, refs, held, sems)
    width = out_ref.shape[1] // blocks
    scale = scale_of(x_ref[...].astype(F32))
    for j in range(blocks):
        part = x_ref[:, place(line_ref, j, width)].astype(F32)
        gain = gain_ref[0:1, cut(width, j)]
        out_ref[:, cut(width, j)] = (part * scale * gain).astype(BF16)


def order_body(blocks, counts, line_ref, gain_ref, *refs):
    out_ref, held, sems = refs[sum(counts) :]
    x_ref = fetched(counts, refs, held, sems)
    width = out_ref.shape[1] // blocks
    for j in range(blocks):
        out_ref[:, cut(width, j)] = x_ref[:, place(line_ref, j, width)]


def ordered(chain, body, line, gains, held):
    counts = [len(block) for block in held]
    rows, model = held[0][0].shape
    n = len(held)
    return chain.call(
        functools.partial(body, line.shape[0], counts),
        (n,),
        [whole(gains.shape)] + [pl.BlockSpec(memory_space=pl.ANY)] * sum(counts),
        [pl.BlockSpec((rows, model), lambda k, *_: (k, 0))],
        [((n * rows, model), BF16)],
        flops=20 * n * rows * model,
        scratch=[pltpu.VMEM((2, rows, model), BF16), pltpu.SemaphoreType.DMA((2, 2))],
        prefetch=1,
        moved=4 * n * rows * model,
    )(line, gains, *[array for block in held for array in block])[0]


def added(refs, span):
    total = refs[0][span, :].astype(F32)
    for ref in refs[1:]:
        total += ref[span, :].astype(F32)
    return total


def middle_body(blocks, m, line_ref, x_ref, gain_ref, *refs):
    middle_ref, out_ref = refs[2 * m :]
    width = x_ref.shape[1] // blocks
    half = x_ref.shape[1] // 2
    span = slice(None)
    middle_ref[:, :half] = added(refs[:m], span)
    middle_ref[:, half:] = added(refs[m : 2 * m], span)
    for j in range(blocks):
        here = x_ref[:, place(line_ref, j, width)].astype(F32)
        middle_ref[:, cut(width, j)] += here
    middle = middle_ref[...]
    out_ref[...] = (middle * scale_of(middle) * gain_ref[1:2, :]).astype(BF16)


def result_body(blocks, m, line_ref, middle_ref, gain_ref, *refs):
    out_ref = refs[2 * m]
    width = middle_ref.shape[1] // blocks
    span = slice(None)
    total = middle_ref[...] + jnp.concatenate(
        [added(refs[:m], span), added(refs[m : 2 * m], span)], axis=1
    )
    for j in range(blocks):
        out_ref[:, place(line_ref, j, width)] = total[:, cut(width, j)].astype(BF16)


def second_back_body(blocks, m, line_ref, dy_ref, gain_ref, *refs):
    middle_ref, out_ref, low_ref = refs[2 * m :]
    width = dy_ref.shape[1] // blocks
    span = slice(None)
    grad = jnp.concatenate([added(refs[:m], span), added(refs[m : 2 * m], span)], axis=1)
    middle = middle_ref[...]
    scale = scale_of(middle)
    normed = middle * scale
    scaled = grad * gain_ref[1:2, :]
    out_ref[...] = scale * (scaled - normed * jnp.mean(scaled * normed, axis=-1, keepdims=True))
    for j in range(blocks):
        out_ref[:, cut(width, j)] += dy_ref[:, place(line_ref, j, width)].astype(F32)
    low_ref[...] = out_ref[...].astype(BF16)


def first_back_body(blocks, m, line_ref, x_ref, gain_ref, *refs):
    above_ref, out_ref = refs[2 * m :]
    width = x_ref.shape[1] // blocks
    span = slice(None)
    scale = scale_of(x_ref[...].astype(F32))
    normed = jnp.concatenate(
        [x_ref[:, place(line_ref, j, width)].astype(F32) for j in range(blocks)], axis=1
    ) * scale
    grad = jnp.concatenate([added(refs[:m], span), added(refs[m : 2 * m], span)], axis=1)
    scaled = grad * gain_ref[0:1, :]
    back = scale * (scaled - normed * jnp.mean(scaled * normed, axis=-1, keepdims=True))
    total = above_ref[...] + back
    for j in range(blocks):
        out_ref[:, place(line_ref, j, width)] = total[:, cut(width, j)]


def by_rows(chain, body, line, first, gains, parts, more, kinds):
    rows, model = first.shape
    half = model // 2
    tile = min(128, rows)
    row = pl.BlockSpec((tile, model), lambda i, *_: (i, 0))
    slim = pl.BlockSpec((tile, half), lambda i, *_: (i, 0))
    m = len(parts[0])
    return chain.call(
        functools.partial(body, line.shape[0], m),
        (rows // tile,),
        [row, whole(gains.shape)] + [slim] * (2 * m) + [row] * len(more),
        [row] * len(kinds),
        [((rows, model), kind) for kind in kinds],
        flops=20 * rows * model,
        prefetch=1,
        moved=rows * model * (2 * m + 4 * len(kinds)),
    )(line, first, gains, *parts[0], *parts[1], *more)


def add_rows_body(count, *refs):
    for i in range(count):
        total = refs[i][...].astype(F32) + refs[count + i][...].astype(F32)
        refs[2 * count + i][...] = total.astype(BF16)


def add_rows(chain, helds, blocks):
    rows, columns = helds[0].shape
    tile = min(128, rows)
    steps = rows // tile
    count = len(helds)
    here = pl.BlockSpec((tile, columns), lambda i: (i, 0))
    return chain.call(
        functools.partial(add_rows_body, count),
        (steps,),
        [here] * count + [pl.BlockSpec((tile, columns), lambda i: (steps + i, 0))] * count,
        [here] * count,
        [((rows, columns), BF16)] * count,
        flops=count * rows * columns,
        moved=6 * count * rows * columns,
    )(*helds, *blocks)


def finish_body(m, halves, n, *refs):
    total = added(refs[:m], slice(None))
    if halves:
        total += jnp.concatenate([ref[...].astype(F32) for ref in refs[m : m + halves]], axis=1)
    m += halves
    weights, outs = refs[m : m + n], refs[m + n :]
    if not n:
        outs[0][...] = total.T
        return
    width = weights[0].shape[1]
    inner = jnp.zeros((total.shape[0], 1), F32)
    for i in range(n):
        part = total[:, cut(width, i)]
        outs[i][...] = part
        inner += jnp.sum(weights[i][...].astype(F32) * part, axis=1, keepdims=True)
    outs[n][...] = jnp.broadcast_to(inner, outs[n].shape)


def finish(chain, terms, weights=()):
    rows, columns = terms[0].shape
    tile = min(128, rows)
    row = pl.BlockSpec((tile, columns), lambda i: (i, 0))
    n = len(weights)
    halves = sum(1 for term in terms if term.shape[1] < columns)
    half = [pl.BlockSpec((tile, columns // 2), lambda i: (i, 0))] * halves
    if n:
        slim = pl.BlockSpec((tile, columns // n), lambda i: (i, 0))
        outs = [slim] * n + [pl.BlockSpec((tile, 128), lambda i: (i, 0))]
        shapes = [((rows, columns // n), F32)] * n + [((rows, 128), F32)]
    else:
        slim = None
        outs = [pl.BlockSpec((columns, tile), lambda i: (0, i))]
        shapes = [((columns, rows), F32)]
    results = chain.call(
        functools.partial(finish_body, len(terms) - halves, halves, n),
        (rows // tile,),
        [row] * (len(terms) - halves) + half + [slim] * n,
        outs,
        shapes,
        flops=4 * rows * columns,
        moved=rows * columns * 12,
    )(*terms, *weights)
    if n:
        results[n] = results[n][:, 0]
    return results


def rope_tables(place):
    half = HEAD_DIM // 2
    freq = THETA ** (-2.0 * jnp.arange(half, dtype=F32) / HEAD_DIM)
    angle = place.astype(F32)[:, None] * freq[None, :]
    cosine, sine = jnp.cos(angle), jnp.sin(angle)
    return (
        jnp.concatenate([cosine] * (PAIR // half), axis=1),
        jnp.concatenate([-sine, sine] * (PAIR // HEAD_DIM), axis=1),
    )


def turn(values):
    half = HEAD_DIM // 2
    width = values.shape[-1]
    lane = lax.broadcasted_iota(jnp.int32, values.shape, 1) % HEAD_DIM
    return jnp.where(
        lane < half, pltpu.roll(values, width - half, 1), pltpu.roll(values, half, 1)
    )


def joined(refs):
    return jnp.concatenate([r[...] for r in refs], axis=0)


def qkv_body(n, x_ref, cos_ref, sin_ref, *refs):
    weights, outs = refs[: 3 * n], refs[3 * n :]
    rows = x_ref.shape[0]
    tile = outs[0].shape[1]
    for i in range(3):
        weight = joined(weights[i * n : (i + 1) * n])
        for s in range(rows // SEQ):
            span = slice(s * SEQ, (s + 1) * SEQ)
            product = nn(x_ref[span, :], weight)
            if i == 2:
                outs[i][span, :] = product.astype(BF16)
                continue
            for t in range(tile // PAIR):
                here = product[:, t * PAIR : (t + 1) * PAIR]
                turned = here * cos_ref[...] + turn(here) * sin_ref[...]
                outs[i][span, t * PAIR : (t + 1) * PAIR] = turned.astype(BF16)


def project(chain, x, tables, query, key, value):
    rows, model = x.shape
    n, width = len(query.pieces), query.width
    tile = min(256, width)
    out = pl.BlockSpec((rows, tile), lambda j: (0, j))
    return chain.call(
        functools.partial(qkv_body, n),
        (width // tile,),
        [whole(x.shape), whole((SEQ, PAIR)), whole((SEQ, PAIR))]
        + query.tiles(tile)
        + key.tiles(tile)
        + value.tiles(tile),
        [out] * 3,
        [((rows, width), BF16)] * 3,
        flops=6 * rows * model * width,
        moved=2 * (rows * model + 3 * model * width + 3 * rows * width),
    )(x, *tables, *query.pieces, *key.pieces, *value.pieces)


def collect(counts, refs, held, sems):
    rows = held.shape[0] // len(counts)
    copies = []
    for k, count in enumerate(counts):
        half = held.shape[1] // count
        for h in range(count):
            target = held.at[pl.ds(k * rows, rows), pl.ds(h * half, half)]
            i = len(copies)
            copies.append(pltpu.make_async_copy(refs[i], target, sems.at[i]))
    for copy in copies:
        copy.start()
    for copy in copies:
        copy.wait()


def gate_body(n, counts, *refs):
    m = sum(counts)
    gate_w, up_w = refs[m : m + n], refs[m + n : m + 2 * n]
    hidden_ref, slope_ref, silu_ref, x_ref, sems = refs[m + 2 * n :]

    @pl.when(pl.program_id(0) == 0)
    def _():
        collect(counts, refs, x_ref, sems)

    gate_weight, up_weight = joined(gate_w), joined(up_w)
    for s in range(x_ref.shape[0] // SEQ):
        span = slice(s * SEQ, (s + 1) * SEQ)
        gate = nn(x_ref[span, :], gate_weight)
        up = nn(x_ref[span, :], up_weight)
        sigm = jax.nn.sigmoid(gate)
        silu = gate * sigm
        hidden_ref[span, :] = (silu * up).astype(BF16)
        silu_ref[span, :] = silu.astype(BF16)
        slope_ref[span, :] = (up * sigm * (1.0 + gate * (1.0 - sigm))).astype(BF16)


def collected(held):
    counts = [len(block) for block in held]
    rows, model = held[0][0].shape
    scratch = [
        pltpu.VMEM((len(held) * rows, model), BF16),
        pltpu.SemaphoreType.DMA((sum(counts),)),
    ]
    arrays = [array for block in held for array in block]
    return counts, arrays, [pl.BlockSpec(memory_space=pl.ANY)] * len(arrays), scratch


def gate_up(chain, held, gate, up):
    counts, arrays, specs, scratch = collected(held)
    rows, model = scratch[0].shape
    n, width = len(gate.pieces), gate.width
    tile = min(256, width)
    out = pl.BlockSpec((rows, tile), lambda j: (0, j))
    return chain.call(
        functools.partial(gate_body, n, counts),
        (width // tile,),
        specs + gate.tiles(tile) + up.tiles(tile),
        [out] * 3,
        [((rows, width), BF16)] * 3,
        flops=4 * rows * model * width,
        scratch=scratch,
        moved=2 * (rows * model + 2 * model * width + 3 * rows * width),
    )(*arrays, *gate.pieces, *up.pieces)


def hidden_back_body(n, g_ref, *refs):
    weight = joined(refs[:n])
    slope_ref, silu_ref, gate_ref, up_ref = refs[n:]
    for s in range(g_ref.shape[0] // SEQ):
        span = slice(s * SEQ, (s + 1) * SEQ)
        grad = nn(g_ref[span, :], weight)
        gate_ref[span, :] = (grad * slope_ref[span, :].astype(F32)).astype(BF16)
        up_ref[span, :] = (grad * silu_ref[span, :].astype(F32)).astype(BF16)


def hidden_back(chain, grads, down, slope, silu):
    rows, model = grads.shape
    n, width = len(down.pieces), down.width
    tile = min(256, width)
    out = pl.BlockSpec((rows, tile), lambda j: (0, j))
    return chain.call(
        functools.partial(hidden_back_body, n),
        (width // tile,),
        [whole(grads.shape)] + down.tiles(tile) + [out] * 2,
        [out] * 2,
        [((rows, width), BF16)] * 2,
        flops=2 * rows * model * width,
        moved=2 * (rows * model + model * width + 4 * rows * width),
    )(grads, *down.pieces, slope, silu)


def mixed_back_body(n, counts, *refs):
    m = sum(counts)
    out_ref, x_ref, sems = refs[m + n :]

    @pl.when(pl.program_id(0) == 0)
    def _():
        collect(counts, refs, x_ref, sems)

    out_ref[...] = nn(x_ref[...], joined(refs[m : m + n])).astype(BF16)


def mixed_back(chain, held, out):
    counts, arrays, specs, scratch = collected(held)
    rows, model = scratch[0].shape
    n, width = len(out.pieces), out.width
    tile = min(256, width)
    return chain.call(
        functools.partial(mixed_back_body, n, counts),
        (width // tile,),
        specs + out.tiles(tile),
        [pl.BlockSpec((rows, tile), lambda j: (0, j))],
        [((rows, width), BF16)],
        flops=2 * rows * model * width,
        scratch=scratch,
        moved=2 * (rows * model + model * width + rows * width),
    )(*arrays, *out.pieces)[0]


def trans_body(n, starts, targets, *refs):
    parts, blocks = len(starts), len(targets[0])
    lefts = refs[:parts]
    pieces = refs[parts : parts * (n + 1)]
    outs = refs[parts * (n + 1) : -4]
    held, ready, sems, out_sems = refs[-4:]
    j = pl.program_id(0)
    depth, width = held.shape[2:]
    rows = ready.shape[1] // blocks

    def copy(i, p, slot):
        source = pieces[p * n + i].at[pl.ds(0, depth), pl.ds(starts[p], width)]
        return pltpu.make_async_copy(source, held.at[slot, p], sems.at[slot, p])

    def fetch(step, slot):
        for i in range(n):

            @pl.when(step == i)
            def _():
                for p in range(parts):
                    copy(i, p, slot).start()

    def leave(slot, k, array, first, column):
        target = outs[array].at[pl.ds(first, rows), pl.ds(column, depth)]
        source = ready.at[slot, pl.ds(k * rows, rows), :]
        return pltpu.make_async_copy(source, target, out_sems.at[slot, k])

    def left(slot):
        for k in range(blocks):
            leave(slot, k, 0, 0, 0).wait()

    @pl.when(j == 0)
    def _():
        fetch(j, 0)

    @pl.when(j + 1 < n)
    def _():
        fetch(j + 1, (j + 1) % 2)

    slot = j % 2
    for p in range(parts):
        copy(0, p, slot).wait()

    @pl.when(j >= 2)
    def _():
        left(slot)

    for s in range(blocks * rows // SEQ):
        span = slice(s * SEQ, (s + 1) * SEQ)
        total = nt(lefts[0][span, :], held[slot, 0])
        for p in range(1, parts):
            total += nt(lefts[p][span, :], held[slot, p])
        ready[slot, span, :] = total.astype(BF16)
    column = pl.multiple_of(j % (n // 2) * depth, 128)
    for h in range(2):

        @pl.when((j >= n // 2) == (h == 1))
        def _():
            for k, (array, first) in enumerate(targets[h]):
                leave(slot, k, array, first, column).start()

    @pl.when(j == n - 1)
    def _():
        left(1 - slot)
        left(slot)


def times_trans(chain, parts, group):
    weights = [weight for _, weight in parts]
    n, depth, width = len(weights[0].pieces), weights[0].rows, weights[0].width
    rows = parts[0][0].shape[0]
    half = weights[0].model // 2
    size = rows // group.size
    messages = group.messages()
    shapes = [((size, half), BF16)] * 2
    targets = [{0: (0, 0)}, {0: (1, 0)}]
    for h in range(2):
        for keys in messages[h]:
            for i, k in enumerate(keys):
                targets[h][k] = (len(shapes), i * size)
            shapes.append(((len(keys) * size, half), BF16))
    targets = [[t[k] for k in range(group.size)] for t in targets]
    anywhere = pl.BlockSpec(memory_space=pl.ANY)
    outs = chain.call(
        functools.partial(trans_body, n, [weight.start for weight in weights], targets),
        (n,),
        [whole((rows, width))] * len(parts) + [anywhere] * (n * len(parts)),
        [anywhere] * len(shapes),
        shapes,
        flops=4 * rows * half * width * len(parts),
        scratch=[
            pltpu.VMEM((2, len(parts), depth, width), BF16),
            pltpu.VMEM((2, rows, depth), BF16),
            pltpu.SemaphoreType.DMA((2, len(parts))),
            pltpu.SemaphoreType.DMA((2, group.size)),
        ],
        moved=2 * (2 * rows * half + len(parts) * (rows + 2 * half) * width),
    )(*[left for left, _ in parts], *[piece for weight in weights for piece in weight.pieces])
    m = group.bits
    return outs[:2], [outs[2 : 2 + m], outs[2 + m :]]


def grad_body(parts, got, blocks, steps, *refs):
    lefts, refs = refs[:blocks], refs[blocks:]
    rights, refs = refs[:parts], refs[parts:]
    got_ref = refs[0] if got else None
    outs, turned = refs[got:-1], refs[-1]
    j = pl.program_id(0)

    @pl.when(j == 0)
    def _():
        rows = turned.shape[1] // blocks
        for k in range(blocks):
            turned[:, cut(rows, k)] = lefts[k][...].T

    for i in range(parts):

        @pl.when((j >= i * steps) & (j < (i + 1) * steps))
        def _():
            total = nn(turned[...], rights[i][...])
            if got:
                total += got_ref[...].astype(F32)
            total = total.astype(BF16)
            first = 0
            for out_ref in outs:
                count = out_ref.shape[0]
                out_ref[...] = total[first : first + count]
                first += count


def weight_grads(chain, left, which, rights, got=None, bits=0):
    rows, width = rights[0].shape
    parts = len(rights)
    tile = min(512, width)
    steps = width // tile
    if isinstance(left, list):
        lefts = [block[0] if len(block) == 1 else block[which] for block in left]
        half = left[0][0].shape[1] // 2
        places = [which if len(block) == 1 else 0 for block in left]
    else:
        lefts, places, half = [left], [which], left.shape[1] // 2
    blocks = len(lefts)
    ins = [
        pl.BlockSpec((rows // blocks, half), functools.partial(lambda at, j: (0, at), at))
        for at in places
    ]
    for i in range(parts):
        ins.append(
            pl.BlockSpec(
                (rows, tile),
                functools.partial(
                    lambda first, j: (0, jnp.clip(j - first, 0, steps - 1)), i * steps
                ),
            )
        )
    column = lambda j: (0, j)
    more = [] if got is None else [got]
    sizes = [half >> bits]
    for p in range(bits):
        sizes += [sizes[0], ((1 << p) - 1) * sizes[0]] if p else [sizes[0]]
    return chain.call(
        functools.partial(grad_body, parts, len(more), blocks, steps),
        (parts * steps,),
        ins + [pl.BlockSpec((half, tile), column)] * len(more),
        [pl.BlockSpec((size, tile), column) for size in sizes],
        [((size, parts * width), BF16) for size in sizes],
        flops=2 * rows * half * width * parts,
        scratch=[pltpu.VMEM((half, rows), BF16)],
        moved=2 * (rows * half + parts * (rows + half) * width),
    )(*lefts, *rights, *more)


def causal(scores):
    past = scores.shape[0] - HALF_SEQ
    key = lax.broadcasted_iota(jnp.int32, (HALF_SEQ, HALF_SEQ), 0)
    query = lax.broadcasted_iota(jnp.int32, (HALF_SEQ, HALF_SEQ), 1)
    last = jnp.where(key <= query, scores[past:], -1e30)
    return last if past == 0 else jnp.concatenate([scores[:past], last], axis=0)


def head_of(h):
    return slice(h * HEAD_DIM, (h + 1) * HEAD_DIM)


def span_of(b):
    return slice(b * HALF_SEQ, (b + 1) * HALF_SEQ)


def in_place(shift_ref, ref, count):
    rows = SEQ // count
    spans = [pl.ds(pl.multiple_of((i ^ shift_ref[0]) * rows, rows), rows) for i in range(count)]
    return jnp.concatenate([ref[span, :] for span in spans], axis=0)


def put_back(shift_ref, ref, count, values):
    rows = SEQ // count
    for i in range(count):
        ref[pl.ds(pl.multiple_of((i ^ shift_ref[0]) * rows, rows), rows), :] = values[cut(rows, i)]


def attend_body(count, shift_ref, q_ref, k_ref, v_ref, out_ref, sum_ref):
    queries, keys = in_place(shift_ref, q_ref, count), in_place(shift_ref, k_ref, count)
    values = in_place(shift_ref, v_ref, count).astype(F32).T.astype(BF16)
    heads = []
    for h in range(2):
        blocks = []
        for b in range(2):
            reach = (b + 1) * HALF_SEQ
            query = queries[span_of(b), head_of(h)] * BF16(FACTOR)
            scores = causal(nt(keys[:reach, head_of(h)], query))
            top = jnp.max(scores, axis=0, keepdims=True)
            expo = jnp.exp(scores - top)
            total = jnp.sum(expo, axis=0, keepdims=True)
            mixed = nn(values[head_of(h), :reach], expo.astype(BF16))
            blocks.append(mixed * (1.0 / total))
            sum_ref[0, 0, h : h + 1, span_of(b)] = top + jnp.log(total)
        heads.append(jnp.concatenate(blocks, axis=1))
    put_back(shift_ref, out_ref, count, jnp.concatenate(heads, axis=0).T.astype(BF16))


def attend(chain, shift, count, query, key, value):
    rows, width = query.shape
    seqs, pairs = rows // SEQ, width // PAIR
    tile = pl.BlockSpec((SEQ, PAIR), lambda s, p, _: (s, p))
    return chain.call(
        functools.partial(attend_body, count),
        (seqs, pairs),
        [tile] * 3,
        [tile, pl.BlockSpec((1, 1, 2, SEQ), lambda s, p, _: (s, p, 0, 0))],
        [((rows, width), BF16), ((seqs, pairs, 2, SEQ), F32)],
        flops=16 * rows * width * SEQ,
        prefetch=1,
        moved=8 * rows * width,
    )(shift, query, key, value)


def attend_back_body(
    count, shift_ref, q_ref, k_ref, v_ref, g_ref, sum_ref, cos_ref, sin_ref, dq_ref, dk_ref, dv_ref
):
    queries, keys, values, grads = (
        in_place(shift_ref, ref, count) for ref in (q_ref, k_ref, v_ref, g_ref)
    )
    turned = keys.astype(F32).T.astype(BF16)
    dq_heads, dk_heads, dv_heads = [], [], []
    for h in range(2):
        dq, dk, dv = [], [], []
        for b in range(2):
            reach = (b + 1) * HALF_SEQ
            query = queries[span_of(b), head_of(h)]
            grad = grads[span_of(b), head_of(h)]
            scores = causal(nt(keys[:reach, head_of(h)], query * BF16(FACTOR)))
            probs = jnp.exp(scores - sum_ref[0, 0, h : h + 1, span_of(b)])
            probs_grad = nt(values[:reach, head_of(h)], grad)
            inner = jnp.sum(probs * probs_grad, axis=0, keepdims=True)
            score_grad = (probs * (probs_grad - inner)).astype(BF16)
            dv.append(nn(probs.astype(BF16), grad))
            dk.append(nn(score_grad, query))
            dq.append(nn(turned[head_of(h), :reach], score_grad))
        for parts, heads in ((dk, dk_heads), (dv, dv_heads)):
            heads.append(
                jnp.concatenate([parts[1][:HALF_SEQ] + parts[0], parts[1][HALF_SEQ:]], axis=0)
            )
        dq_heads.append(jnp.concatenate(dq, axis=1))
    dq = jnp.concatenate(dq_heads, axis=0).T * FACTOR
    dk = jnp.concatenate(dk_heads, axis=1) * FACTOR
    dv = jnp.concatenate(dv_heads, axis=1).astype(BF16)
    cosine, sine = cos_ref[...], sin_ref[...]
    put_back(shift_ref, dq_ref, count, (dq * cosine - turn(dq) * sine).astype(BF16))
    put_back(shift_ref, dk_ref, count, (dk * cosine - turn(dk) * sine).astype(BF16))
    put_back(shift_ref, dv_ref, count, dv)


def attend_back(chain, shift, count, query, key, value, grad, logsum, tables):
    rows, width = query.shape
    seqs, pairs = rows // SEQ, width // PAIR
    tile = pl.BlockSpec((SEQ, PAIR), lambda s, p, _: (s, p))
    return chain.call(
        functools.partial(attend_back_body, count),
        (seqs, pairs),
        [tile] * 4
        + [pl.BlockSpec((1, 1, 2, SEQ), lambda s, p, _: (s, p, 0, 0))]
        + [whole((SEQ, PAIR))] * 2,
        [tile] * 3,
        [((rows, width), BF16)] * 3,
        flops=40 * rows * width * SEQ,
        prefetch=1,
        moved=14 * rows * width,
    )(shift, query, key, value, grad, logsum, *tables)


def local(
    chips,
    group,
    tokens,
    attn_gain,
    query_weight,
    key_weight,
    value_weight,
    output_weight,
    ffn_gain,
    gate_weight,
    up_weight,
    down_weight,
    cotangent,
):
    line = jnp.asarray(chips.table)[lax.axis_index("dp")]
    rows, model = tokens.shape
    count = SEQ // rows
    shift = lax.axis_index("tensor") % count
    row = jnp.arange(SEQ, dtype=jnp.int32)
    places = rope_tables(row)
    tables = rope_tables((row // rows ^ shift) * rows + row % rows)
    shift = jnp.reshape(shift, (1,)).astype(jnp.int32)
    early = (*places, *tables, line, shift)
    depth, own = query_weight.shape
    hidden_units = gate_weight.shape[1]
    chain = Chain()

    def gather(piece):
        return Gather(chips, chain, chain.join(piece)[0])

    def spread_of(values):
        return Spread(group, chain, chain.join(values)[0])

    def fold_of(part):
        own_part, sent = part
        sent = chain.join(*sent[0], *sent[1])
        return Fold(group, chain, own_part, [sent[: group.bits], sent[group.bits :]])

    def grads_of(left, rights):
        got = [None]
        chain.ask(weight_grads(chain, left, 1, rights)[0], got, 0, chips.other)

        def mine(**how):
            if got[0] is None:
                chain.flush()
            blocks = weight_grads(chain, left, 0, rights, got[0], chips.bits)
            return Sums(chips, chain, blocks, **how)

        return mine

    extra = jnp.concatenate([attn_gain, ffn_gain, jnp.zeros((4 * own - 2 * depth,), BF16)])
    attn = jnp.concatenate([query_weight, key_weight, value_weight, output_weight.T], axis=1)
    attn = gather(jnp.concatenate([attn, jnp.broadcast_to(extra, (16, 4 * own))], axis=0))
    spread = spread_of(tokens)
    grads_spread = spread_of(cotangent)
    grads_spread.later = []
    down_turned, *early = chain.join(down_weight.T, *early)
    places, tables, line, shift = early[:2], early[2:4], early[4], early[5]
    chain.end(attn, spread, grads_spread)
    chain.end(attn, spread)
    all_tokens = spread.blocks()
    attn = attn.pieces()
    pair = gather(jnp.concatenate([gate_weight, up_weight], axis=1))
    w_query, w_key, w_value, w_output = [Weight(attn, depth, i * own, own) for i in range(4)]
    gains = jnp.concatenate(
        [piece[depth : depth + 1, : 2 * depth].reshape(2, depth) for piece in attn], axis=1
    ).astype(F32)

    group_one = ordered(chain, norm_body, line, gains, all_tokens)
    grads_spread.resume()
    query, key, value = project(chain, group_one, tables, w_query, w_key, w_value)
    mixed, logsum = attend(chain, shift, count, query, key, value)
    out_part = times_trans(chain, [(mixed, w_output)], group)
    fold = fold_of(out_part)
    chain.end(fold, pair, grads_spread)
    grad_rows = ordered(chain, order_body, line, gains, grads_spread.blocks())
    chain.end(fold)
    attended = fold.total()
    middle, second = by_rows(
        chain, middle_body, line, tokens, gains, attended, [], [F32, BF16]
    )
    spread = spread_of(second)
    chain.end(spread, pair)
    pair = pair.pieces()
    down = gather(down_turned)
    chain.end(spread)
    group_two = spread.blocks()
    w_gate = Weight(pair, depth, 0, hidden_units)
    w_up = Weight(pair, depth, hidden_units, hidden_units)
    hidden, slope, silu = gate_up(chain, group_two, w_gate, w_up)

    mine = grads_of(grad_rows, [hidden])
    chain.end(down)
    chain.flush()
    down_sum = mine()
    w_down = Weight(down.pieces(), depth, 0, hidden_units)
    gate_grad, up_grad = hidden_back(chain, grad_rows, w_down, slope, silu)
    mine_gate = grads_of(group_two, [gate_grad])
    chain.end(down_sum)
    second_part = times_trans(chain, [(gate_grad, w_gate), (up_grad, w_up)], group)
    mine_up = grads_of(group_two, [up_grad])
    gate_sum = mine_gate(hold=True)
    chain.end(down_sum)
    fold = fold_of(second_part)
    up_sum = mine_up(apart=True)
    chain.end(gate_sum, fold)
    result_part = times_trans(chain, [(hidden, w_down)], group)
    chain.end(fold)
    second_grad = fold.total()
    middle_grad, low_grad = by_rows(
        chain, second_back_body, line, cotangent, gains, second_grad, [middle], [F32, BF16]
    )
    spread = spread_of(low_grad)
    chain.end(up_sum)
    gate_sum.resume()
    (down_sum,) = finish(chain, down_sum.terms())
    chain.end(spread)
    attn_grads = spread.blocks()

    mixed_grad = mixed_back(chain, attn_grads, w_output)
    mine_out = grads_of(attn_grads, [mixed])
    chain.end(gate_sum)
    up_sum.send_half(0)
    fold = fold_of(result_part)
    query_back, key_back, value_back = attend_back(
        chain, shift, count, query, key, value, mixed_grad, logsum, places
    )
    mine_qkv = grads_of(group_one, [query_back, key_back, value_back])
    out_sum = mine_out(hold=True)
    chain.end(up_sum, fold)
    up_sum.send_half(1)
    qkv_sum = mine_qkv(cut_in_two=True)
    chain.end(fold, out_sum)
    result_part = fold.total()
    first_part = times_trans(
        chain, [(query_back, w_query), (key_back, w_key), (value_back, w_value)], group
    )
    chain.end(up_sum, qkv_sum)
    fold = fold_of(first_part)
    out_sum.resume()
    up_sum, up_inner = finish(chain, up_sum.terms(), [up_weight])
    gate_sum, gate_inner = finish(chain, gate_sum.terms(), [gate_weight])
    (layer_out,) = by_rows(chain, result_body, line, middle, gains, result_part, [], [BF16])
    chain.end(fold)
    chain.end(fold)
    first_grad = fold.total()
    (input_grad,) = by_rows(
        chain, first_back_body, line, tokens, gains, first_grad, [middle_grad], [F32]
    )
    chain.end(qkv_sum)
    query_sum, key_sum, value_sum, qkv_inner = finish(
        chain, qkv_sum.terms(), [query_weight, key_weight, value_weight]
    )
    gain_parts = jnp.stack(
        [qkv_inner / attn_gain.astype(F32), (gate_inner + up_inner) / ffn_gain.astype(F32)]
    )
    (gain_parts,) = chain.join(gain_parts)
    (out_sum,) = finish(chain, out_sum.terms())
    gain_totals = gain_parts
    for k in range(1, group.size):
        pairs = [(i, i ^ k) for i in range(group.size)]
        gain_totals += lax.ppermute(gain_parts, "tensor", pairs)
    gain_one_total, gain_two_total = gain_totals[0], gain_totals[1]
    return (
        layer_out,
        input_grad,
        gain_one_total,
        query_sum,
        key_sum,
        value_sum,
        out_sum,
        gain_two_total,
        gate_sum,
        up_sum,
        down_sum,
    )


def solution(mesh):
    in_specs = (
        P(("dp", "tensor"), None),
        P("dp"),
        P("dp", "tensor"),
        P("dp", "tensor"),
        P("dp", "tensor"),
        P("tensor", "dp"),
        P("dp"),
        P("dp", "tensor"),
        P("dp", "tensor"),
        P("tensor", "dp"),
        P(("dp", "tensor"), None),
    )
    out_specs = (
        P(("dp", "tensor"), None),
        P(("dp", "tensor"), None),
        P("dp"),
        P("dp", "tensor"),
        P("dp", "tensor"),
        P("dp", "tensor"),
        P("tensor", "dp"),
        P("dp"),
        P("dp", "tensor"),
        P("dp", "tensor"),
        P("tensor", "dp"),
    )
    chips = Chips(mesh.shape["dp"])
    size = mesh.shape["tensor"]
    links = [[(i, i ^ 1 << b) for i in range(size)] for b in range(size.bit_length() - 1)]
    group = Group(links, "tensor")

    def run(*arrays):
        return local(chips, group, *arrays)

    return jax.shard_map(run, mesh=mesh, in_specs=in_specs, out_specs=out_specs, check_vma=False)
```

```python
import functools

import jax
import jax.numpy as jnp
import numpy as np
from jax import lax
from jax.experimental import pallas as pl
from jax.experimental.pallas import tpu as pltpu
from jax.sharding import PartitionSpec as P

HEAD_DIM = 64
SEQ = 512
EPS = 1e-05
THETA = 130000.0
BF16 = jnp.bfloat16
F32 = jnp.float32
FACTOR = HEAD_DIM**-0.5
PAIR = 2 * HEAD_DIM
HALF_SEQ = SEQ // 2
VMEM_LIMIT = 58 << 20
COST_SHARE = 4096


class Chain:
    def __init__(self):
        self.token = jnp.zeros((8, 128), F32)
        self.swaps, self.asked = [], []

    def join(self, *values):
        *values, self.token = lax.optimization_barrier((*values, self.token))
        return values

    def gate(self, *values):
        swaps, self.swaps = self.swaps, []
        asked, self.asked = self.asked, []
        joined = self.join(
            *values, *[held[i] for held, i in swaps], *[source for source, _, _, _ in asked]
        )
        for (held, i), value in zip(swaps, joined[len(values) :]):
            held[i] = value
        for (_, held, i, swap), value in zip(asked, joined[len(values) + len(swaps) :]):
            held[i] = swap(value)
            self.swaps.append((held, i))
        return joined[: len(values)]

    def end(self, *transfers):
        counts = [len(t.flying) for t in transfers]
        got = self.gate(*[value for t in transfers for value in t.flying])
        for t, count in zip(transfers, counts):
            if count:
                t.go_on(got[:count])
            got = got[count:]

    def ask(self, source, held, i, swap):
        self.asked.append((source, held, i, swap))

    def flush(self):
        for source, held, i, swap in self.asked:
            held[i] = swap(source)
        self.asked = []

    def call(self, body, grid, ins, outs, shapes, flops, scratch=(), prefetch=0, moved=0):
        first = prefetch + len(ins)
        second = first + 1 + len(outs)
        anywhere = pl.BlockSpec(memory_space=pl.ANY)

        def wrapped(*refs):
            body(*refs[:first], *refs[first + 1 : second], *refs[second + 1 :])

        run = pl.pallas_call(
            wrapped,
            grid_spec=pltpu.PrefetchScalarGridSpec(
                num_scalar_prefetch=prefetch,
                grid=grid,
                in_specs=[*ins, anywhere],
                out_specs=[*outs, anywhere],
                scratch_shapes=list(scratch),
            ),
            out_shape=[jax.ShapeDtypeStruct(s, t) for s, t in [*shapes, ((8, 128), F32)]],
            compiler_params=pltpu.CompilerParams(
                vmem_limit_bytes=VMEM_LIMIT, dimension_semantics=("arbitrary",) * len(grid)
            ),
            cost_estimate=pl.CostEstimate(
                flops=flops // COST_SHARE, bytes_accessed=moved // COST_SHARE, transcendentals=0
            ),
        )

        def with_token(*args):
            *results, self.token = run(*args, self.token)
            return results

        return with_token


class Chips:
    def __init__(self, size):
        self.bits = (size // 2).bit_length() - 1
        self.size = size
        self.swap = [(i, i ^ 1) for i in range(size)]
        self.links = [
            [(i, i ^ 2 << self.bits - 1 - p) for i in range(size)] for p in range(self.bits)
        ]
        flips = [
            sum(1 << self.bits - 1 - p for p in range(self.bits) if v >> p & 1)
            for v in range(1 << self.bits)
        ]
        table = [[i ^ 2 * f for f in flips] + [i ^ 2 * f ^ 1 for f in flips] for i in range(size)]
        self.table = np.array(table, np.int32)

    def send(self, value, p):
        return lax.ppermute(value, "dp", self.links[p])

    def other(self, value):
        return lax.ppermute(value, "dp", self.swap)


class Gather:
    def __init__(self, chips, chain, piece):
        self.chips, self.chain = chips, chain
        self.own = [piece] + [None] * (2**chips.bits - 1)
        self.others = list(self.own)
        self.ask(0)
        self.keys = [1 << p for p in range(chips.bits)]
        self.flying = [chips.send(piece, p) for p in range(chips.bits)]

    def ask(self, v):
        self.chain.ask(self.own[v], self.others, v, self.chips.other)

    def go_on(self, got):
        keys, self.keys, self.flying = self.keys, [], []
        for v, piece in zip(keys, got):
            self.own[v] = piece
            for p in range(v.bit_length(), self.chips.bits):
                self.keys.append(v | 1 << p)
                self.flying.append(self.chips.send(piece, p))
        for v in keys:
            self.ask(v)

    def pieces(self):
        while self.flying:
            self.chain.end(self)
        self.chain.flush()
        return self.own + self.others


class Sums:
    def __init__(self, chips, chain, mine, apart=False, hold=False, cut_in_two=False):
        self.chips, self.chain, self.apart, self.hold = chips, chain, apart, hold
        self.todo = []
        self.cut_in_two = cut_in_two and chips.bits == 2
        self.parts = [mine[0]]
        mine = list(mine[1:])
        self.direct, self.passed = [], []
        for p in range(chips.bits):
            self.direct.append(mine.pop(0))
            self.passed.append(mine.pop(0) if p else None)
        self.p = chips.bits - 1
        if self.cut_in_two:
            self.kinds = [0, 1]
            self.flying = [chips.send(half, 1) for half in self.in_two(self.passed[1])]
            return
        self.kinds = [self.p]
        self.flying = [chips.send(self.passed[self.p], self.p)]

    def in_two(self, values):
        width = values.shape[1] // 2
        return values[:, :width], values[:, width:]

    def go_on(self, got):
        rows = self.parts[0].shape[0]
        kinds, self.kinds, self.flying = self.kinds, [], []
        if self.p == 0:
            self.parts += got
            return
        if self.cut_in_two:
            self.p = 0
            total = self.direct[0].astype(F32) + jnp.concatenate(got, axis=1).astype(F32)
            self.todo = [(None, self.direct[1], 1), (None, total.astype(BF16), 0)]
            self.resume()
            return
        for kind, block in zip(kinds, got):
            if kind is None:
                self.parts.append(block)
                continue
            add = lambda held, first: (
                held.astype(F32) + block[first * rows : first * rows + held.shape[0]].astype(F32)
            ).astype(BF16)
            for q in range(kind):
                self.direct[q] = add(self.direct[q], (1 << q) - 1)
                if q:
                    self.passed[q] = add(self.passed[q], 1 << q)
        p, self.p = self.p, self.p - 1
        if p > 0:
            self.todo.append((None, self.direct[p], p))
        if p > 1:
            self.todo.append((p - 1, self.passed[p - 1], p - 1))
        if p == 1 and not self.apart:
            self.todo.append((None, self.direct[0], 0))
        if not self.hold:
            self.resume()

    def resume(self):
        todo, self.todo = self.todo, []
        values = self.chain.join(*[value for _, value, _ in todo])
        for (kind, _, p), value in zip(todo, values):
            self.kinds.append(kind)
            self.flying.append(self.chips.send(value, p))

    def send_half(self, i):
        while self.p > 0:
            self.chain.end(self)
        width = self.direct[0].shape[1] // 2
        (value,) = self.chain.join(self.direct[0][:, i * width : (i + 1) * width])
        self.kinds.append(None)
        self.flying.append(self.chips.send(value, 0))

    def terms(self):
        while self.flying or self.todo:
            if self.todo:
                self.resume()
            self.chain.end(self)
        return sorted(self.parts, key=lambda part: -part.shape[1])


class Group:
    def __init__(self, links, axes):
        self.links, self.axes = links, axes
        self.bits = len(links)
        self.size = 1 << self.bits
        self.orders = (list(range(self.bits)), list(range(self.bits))[::-1])

    def send(self, value, bit):
        return lax.ppermute(value, self.axes, self.links[bit])

    def messages(self):
        found = []
        for order in self.orders:
            found.append([])
            for top in reversed(range(self.bits)):
                found[-1].append(
                    [
                        1 << order[top] | sum(1 << order[p] for p in range(top) if v >> p & 1)
                        for v in range(1 << top)
                    ]
                )
        return found


class Spread:
    def __init__(self, group, chain, rows):
        self.group, self.chain = group, chain
        self.held = {0: [rows]}
        self.later = None
        self.keys = [(1 << b, None) for b in range(group.bits)]
        self.flying = [group.send(rows, b) for b in range(group.bits)]

    def go_on(self, got):
        fresh = list(zip(self.keys, got))
        self.keys, self.flying = [], []
        for (k, h), block in fresh:
            if h is None:
                self.held[k] = [block]
            else:
                self.held.setdefault(k, [None, None])[h] = block
        for (k, h), block in fresh:
            for way, order in enumerate(self.group.orders):
                if h is not None and h != way:
                    continue
                half = block.shape[1] // 2
                top = max(i for i, bit in enumerate(order) if k >> bit & 1)
                for i in range(top + 1, len(order)):
                    part = block if h is not None else block[:, way * half : (way + 1) * half]
                    self.keys.append((k | 1 << order[i], way))
                    if self.later is not None:
                        self.later.append((part, order[i]))
                    else:
                        self.flying.append(self.group.send(part, order[i]))

        if self.later:
            parts = self.chain.join(*[part for part, _ in self.later])
            self.later = [(part, bit) for part, (_, bit) in zip(parts, self.later)]

    def resume(self):
        later, self.later = self.later, None
        parts = self.chain.join(*[part for part, _ in later])
        self.flying = [self.group.send(part, bit) for part, (_, bit) in zip(parts, later)]

    def blocks(self):
        while self.flying:
            self.chain.end(self)
        return [self.held[k] for k in range(self.group.size)]


class Fold:
    def __init__(self, group, chain, own, sent):
        self.group, self.chain = group, chain
        self.rows = own[0].shape[0]
        self.sent = [list(half) for half in sent]
        self.parts = [[half] for half in own]
        self.wave = 0
        self.start()

    def start(self):
        self.flying = [
            self.group.send(self.sent[h][self.wave], order[self.group.bits - 1 - self.wave])
            for h, order in enumerate(self.group.orders)
        ]

    def go_on(self, got):
        self.wave += 1
        self.flying = []
        for h, block in enumerate(got):
            self.parts[h].append(block)
        for wave in range(self.wave, self.group.bits):
            sums = add_rows(self.chain, [sent[wave] for sent in self.sent], got)
            for sent, value in zip(self.sent, sums):
                sent[wave] = value
        if self.wave < self.group.bits:
            self.start()

    def total(self):
        while self.flying:
            self.chain.end(self)
        return self.parts


class Weight:
    def __init__(self, pieces, rows, start, width):
        self.pieces, self.rows, self.start, self.width = pieces, rows, start, width
        self.model = len(pieces) * rows

    def tiles(self, tile):
        first = self.start // tile
        return [pl.BlockSpec((self.rows, tile), lambda j: (0, first + j))] * len(self.pieces)


def nn(left, right):
    return lax.dot_general(left, right, (((1,), (0,)), ((), ())), preferred_element_type=F32)


def nt(left, right):
    return lax.dot_general(left, right, (((1,), (1,)), ((), ())), preferred_element_type=F32)


def tn(left, right):
    return lax.dot_general(left, right, (((0,), (0,)), ((), ())), preferred_element_type=F32)


def whole(shape):
    return pl.BlockSpec(shape, lambda *_: (0,) * len(shape))


def place(line_ref, j, width):
    return pl.ds(pl.multiple_of(line_ref[j] * width, 128), width)


def cut(width, j):
    return slice(j * width, (j + 1) * width)


def scale_of(values):
    return lax.rsqrt(jnp.mean(values * values, axis=-1, keepdims=True) + EPS)


def fetch_blocks(counts, refs, held, sems, k, slot, wait):
    first = 0
    for i, count in enumerate(counts):
        copies = []
        half = held.shape[2] // count
        for h in range(count):
            target = held.at[slot, :, pl.ds(h * half, half)]
            copies.append(pltpu.make_async_copy(refs[first + h], target, sems.at[slot, h]))
        first += count

        @pl.when(k == i)
        def _():
            for copy in copies:
                copy.wait() if wait else copy.start()


def fetched(counts, refs, held, sems):
    k = pl.program_id(0)

    @pl.when(k == 0)
    def _():
        fetch_blocks(counts, refs, held, sems, k, 0, False)

    fetch_blocks(counts, refs, held, sems, k + 1, (k + 1) % 2, False)
    fetch_blocks(counts, refs, held, sems, k, k % 2, True)
    return held.at[k % 2]


def norm_body(blocks, counts, line_ref, gain_ref, *refs):
    out_ref, held, sems = refs[sum(counts) :]
    x_ref = fetched(counts, refs, held, sems)
    width = out_ref.shape[1] // blocks
    scale = scale_of(x_ref[...].astype(F32))
    for j in range(blocks):
        part = x_ref[:, place(line_ref, j, width)].astype(F32)
        gain = gain_ref[0:1, cut(width, j)]
        out_ref[:, cut(width, j)] = (part * scale * gain).astype(BF16)


def order_body(blocks, counts, line_ref, gain_ref, *refs):
    out_ref, held, sems = refs[sum(counts) :]
    x_ref = fetched(counts, refs, held, sems)
    width = out_ref.shape[1] // blocks
    for j in range(blocks):
        out_ref[:, cut(width, j)] = x_ref[:, place(line_ref, j, width)]


def ordered(chain, body, line, gains, held):
    counts = [len(block) for block in held]
    rows, model = held[0][0].shape
    n = len(held)
    return chain.call(
        functools.partial(body, line.shape[0], counts),
        (n,),
        [whole(gains.shape)] + [pl.BlockSpec(memory_space=pl.ANY)] * sum(counts),
        [pl.BlockSpec((rows, model), lambda k, *_: (k, 0))],
        [((n * rows, model), BF16)],
        flops=20 * n * rows * model,
        scratch=[pltpu.VMEM((2, rows, model), BF16), pltpu.SemaphoreType.DMA((2, 2))],
        prefetch=1,
        moved=4 * n * rows * model,
    )(line, gains, *[array for block in held for array in block])[0]


def added(refs, span):
    total = refs[0][span, :].astype(F32)
    for ref in refs[1:]:
        total += ref[span, :].astype(F32)
    return total


def middle_body(blocks, m, line_ref, x_ref, gain_ref, *refs):
    middle_ref, out_ref = refs[2 * m :]
    width = x_ref.shape[1] // blocks
    half = x_ref.shape[1] // 2
    span = slice(None)
    middle_ref[:, :half] = added(refs[:m], span)
    middle_ref[:, half:] = added(refs[m : 2 * m], span)
    for j in range(blocks):
        here = x_ref[:, place(line_ref, j, width)].astype(F32)
        middle_ref[:, cut(width, j)] += here
    middle = middle_ref[...]
    out_ref[...] = (middle * scale_of(middle) * gain_ref[1:2, :]).astype(BF16)


def result_body(blocks, m, line_ref, middle_ref, gain_ref, *refs):
    out_ref = refs[2 * m]
    width = middle_ref.shape[1] // blocks
    span = slice(None)
    total = middle_ref[...] + jnp.concatenate(
        [added(refs[:m], span), added(refs[m : 2 * m], span)], axis=1
    )
    for j in range(blocks):
        out_ref[:, place(line_ref, j, width)] = total[:, cut(width, j)].astype(BF16)


def second_back_body(blocks, m, line_ref, dy_ref, gain_ref, *refs):
    middle_ref, out_ref, low_ref = refs[2 * m :]
    width = dy_ref.shape[1] // blocks
    span = slice(None)
    grad = jnp.concatenate([added(refs[:m], span), added(refs[m : 2 * m], span)], axis=1)
    middle = middle_ref[...]
    scale = scale_of(middle)
    normed = middle * scale
    scaled = grad * gain_ref[1:2, :]
    out_ref[...] = scale * (scaled - normed * jnp.mean(scaled * normed, axis=-1, keepdims=True))
    for j in range(blocks):
        out_ref[:, cut(width, j)] += dy_ref[:, place(line_ref, j, width)].astype(F32)
    low_ref[...] = out_ref[...].astype(BF16)


def first_back_body(blocks, m, line_ref, x_ref, gain_ref, *refs):
    above_ref, out_ref = refs[2 * m :]
    width = x_ref.shape[1] // blocks
    span = slice(None)
    scale = scale_of(x_ref[...].astype(F32))
    normed = jnp.concatenate(
        [x_ref[:, place(line_ref, j, width)].astype(F32) for j in range(blocks)], axis=1
    ) * scale
    grad = jnp.concatenate([added(refs[:m], span), added(refs[m : 2 * m], span)], axis=1)
    scaled = grad * gain_ref[0:1, :]
    back = scale * (scaled - normed * jnp.mean(scaled * normed, axis=-1, keepdims=True))
    total = above_ref[...] + back
    for j in range(blocks):
        out_ref[:, place(line_ref, j, width)] = total[:, cut(width, j)]


def by_rows(chain, body, line, first, gains, parts, more, kinds):
    rows, model = first.shape
    half = model // 2
    tile = min(64, rows)
    row = pl.BlockSpec((tile, model), lambda i, *_: (i, 0))
    slim = pl.BlockSpec((tile, half), lambda i, *_: (i, 0))
    m = len(parts[0])
    return chain.call(
        functools.partial(body, line.shape[0], m),
        (rows // tile,),
        [row, whole(gains.shape)] + [slim] * (2 * m) + [row] * len(more),
        [row] * len(kinds),
        [((rows, model), kind) for kind in kinds],
        flops=20 * rows * model,
        prefetch=1,
        moved=rows * model * (2 * m + 4 * len(kinds)),
    )(line, first, gains, *parts[0], *parts[1], *more)


def add_rows_body(count, *refs):
    for i in range(count):
        total = refs[i][...].astype(F32) + refs[count + i][...].astype(F32)
        refs[2 * count + i][...] = total.astype(BF16)


def add_rows(chain, helds, blocks):
    rows, columns = helds[0].shape
    tile = min(64, rows)
    steps = rows // tile
    count = len(helds)
    here = pl.BlockSpec((tile, columns), lambda i: (i, 0))
    return chain.call(
        functools.partial(add_rows_body, count),
        (steps,),
        [here] * count + [pl.BlockSpec((tile, columns), lambda i: (steps + i, 0))] * count,
        [here] * count,
        [((rows, columns), BF16)] * count,
        flops=count * rows * columns,
        moved=6 * count * rows * columns,
    )(*helds, *blocks)


def finish_body(m, halves, n, *refs):
    total = added(refs[:m], slice(None))
    if halves:
        total += jnp.concatenate([ref[...].astype(F32) for ref in refs[m : m + halves]], axis=1)
    m += halves
    weights, outs = refs[m : m + n], refs[m + n :]
    if not n:
        outs[0][...] = total.T
        return
    width = weights[0].shape[1]
    inner = jnp.zeros((total.shape[0], 1), F32)
    for i in range(n):
        part = total[:, cut(width, i)]
        outs[i][...] = part
        inner += jnp.sum(weights[i][...].astype(F32) * part, axis=1, keepdims=True)
    outs[n][...] = jnp.broadcast_to(inner, outs[n].shape)


def finish(chain, terms, weights=()):
    rows, columns = terms[0].shape
    tile = min(64 if weights else 128, rows)
    row = pl.BlockSpec((tile, columns), lambda i: (i, 0))
    n = len(weights)
    halves = sum(1 for term in terms if term.shape[1] < columns)
    half = [pl.BlockSpec((tile, columns // 2), lambda i: (i, 0))] * halves
    if n:
        slim = pl.BlockSpec((tile, columns // n), lambda i: (i, 0))
        outs = [slim] * n + [pl.BlockSpec((tile, 128), lambda i: (i, 0))]
        shapes = [((rows, columns // n), F32)] * n + [((rows, 128), F32)]
    else:
        slim = None
        outs = [pl.BlockSpec((columns, tile), lambda i: (0, i))]
        shapes = [((columns, rows), F32)]
    results = chain.call(
        functools.partial(finish_body, len(terms) - halves, halves, n),
        (rows // tile,),
        [row] * (len(terms) - halves) + half + [slim] * n,
        outs,
        shapes,
        flops=4 * rows * columns,
        moved=rows * columns * 12,
    )(*terms, *weights)
    if n:
        results[n] = results[n][:, 0]
    return results


def rope_tables(place):
    half = HEAD_DIM // 2
    freq = THETA ** (-2.0 * jnp.arange(half, dtype=F32) / HEAD_DIM)
    angle = place.astype(F32)[:, None] * freq[None, :]
    cosine, sine = jnp.cos(angle), jnp.sin(angle)
    return (
        jnp.concatenate([cosine] * (PAIR // half), axis=1),
        jnp.concatenate([-sine, sine] * (PAIR // HEAD_DIM), axis=1),
    )


def turn(values):
    half = HEAD_DIM // 2
    width = values.shape[-1]
    lane = lax.broadcasted_iota(jnp.int32, values.shape, 1) % HEAD_DIM
    return jnp.where(
        lane < half, pltpu.roll(values, width - half, 1), pltpu.roll(values, half, 1)
    )


def joined(refs):
    return jnp.concatenate([r[...] for r in refs], axis=0)


def qkv_body(n, x_ref, cos_ref, sin_ref, *refs):
    weights, outs = refs[: 3 * n], refs[3 * n :]
    rows = x_ref.shape[0]
    tile = outs[0].shape[1]
    for i in range(3):
        weight = joined(weights[i * n : (i + 1) * n])
        for s in range(rows // SEQ):
            span = slice(s * SEQ, (s + 1) * SEQ)
            product = nn(x_ref[span, :], weight)
            if i == 2:
                outs[i][span, :] = product.astype(BF16)
                continue
            for t in range(tile // PAIR):
                here = product[:, t * PAIR : (t + 1) * PAIR]
                turned = here * cos_ref[...] + turn(here) * sin_ref[...]
                outs[i][span, t * PAIR : (t + 1) * PAIR] = turned.astype(BF16)


def project(chain, x, tables, query, key, value):
    rows, model = x.shape
    n, width = len(query.pieces), query.width
    tile = min(256, width)
    out = pl.BlockSpec((rows, tile), lambda j: (0, j))
    return chain.call(
        functools.partial(qkv_body, n),
        (width // tile,),
        [whole(x.shape), whole((SEQ, PAIR)), whole((SEQ, PAIR))]
        + query.tiles(tile)
        + key.tiles(tile)
        + value.tiles(tile),
        [out] * 3,
        [((rows, width), BF16)] * 3,
        flops=6 * rows * model * width,
        moved=2 * (rows * model + 3 * model * width + 3 * rows * width),
    )(x, *tables, *query.pieces, *key.pieces, *value.pieces)


def collect(counts, refs, held, sems):
    rows = held.shape[0] // len(counts)
    copies = []
    for k, count in enumerate(counts):
        half = held.shape[1] // count
        for h in range(count):
            target = held.at[pl.ds(k * rows, rows), pl.ds(h * half, half)]
            i = len(copies)
            copies.append(pltpu.make_async_copy(refs[i], target, sems.at[i]))
    for copy in copies:
        copy.start()
    for copy in copies:
        copy.wait()


def gate_body(n, counts, *refs):
    m = sum(counts)
    gate_w, up_w = refs[m : m + n], refs[m + n : m + 2 * n]
    hidden_ref, slope_ref, silu_ref, x_ref, sems = refs[m + 2 * n :]

    @pl.when(pl.program_id(0) == 0)
    def _():
        collect(counts, refs, x_ref, sems)

    gate_weight, up_weight = joined(gate_w), joined(up_w)
    for s in range(x_ref.shape[0] // SEQ):
        span = slice(s * SEQ, (s + 1) * SEQ)
        gate = nn(x_ref[span, :], gate_weight)
        up = nn(x_ref[span, :], up_weight)
        sigm = jax.nn.sigmoid(gate)
        silu = gate * sigm
        hidden_ref[span, :] = (silu * up).astype(BF16)
        silu_ref[span, :] = silu.astype(BF16)
        slope_ref[span, :] = (up * sigm * (1.0 + gate * (1.0 - sigm))).astype(BF16)


def collected(held):
    counts = [len(block) for block in held]
    rows, model = held[0][0].shape
    scratch = [
        pltpu.VMEM((len(held) * rows, model), BF16),
        pltpu.SemaphoreType.DMA((sum(counts),)),
    ]
    arrays = [array for block in held for array in block]
    return counts, arrays, [pl.BlockSpec(memory_space=pl.ANY)] * len(arrays), scratch


def gate_up(chain, held, gate, up):
    counts, arrays, specs, scratch = collected(held)
    rows, model = scratch[0].shape
    n, width = len(gate.pieces), gate.width
    tile = min(256, width)
    out = pl.BlockSpec((rows, tile), lambda j: (0, j))
    return chain.call(
        functools.partial(gate_body, n, counts),
        (width // tile,),
        specs + gate.tiles(tile) + up.tiles(tile),
        [out] * 3,
        [((rows, width), BF16)] * 3,
        flops=4 * rows * model * width,
        scratch=scratch,
        moved=2 * (rows * model + 2 * model * width + 3 * rows * width),
    )(*arrays, *gate.pieces, *up.pieces)


def hidden_back_body(n, g_ref, *refs):
    weight = joined(refs[:n])
    slope_ref, silu_ref, gate_ref, up_ref = refs[n:]
    for s in range(g_ref.shape[0] // SEQ):
        span = slice(s * SEQ, (s + 1) * SEQ)
        grad = nn(g_ref[span, :], weight)
        gate_ref[span, :] = (grad * slope_ref[span, :].astype(F32)).astype(BF16)
        up_ref[span, :] = (grad * silu_ref[span, :].astype(F32)).astype(BF16)


def hidden_back(chain, grads, down, slope, silu):
    rows, model = grads.shape
    n, width = len(down.pieces), down.width
    tile = min(256, width)
    out = pl.BlockSpec((rows, tile), lambda j: (0, j))
    return chain.call(
        functools.partial(hidden_back_body, n),
        (width // tile,),
        [whole(grads.shape)] + down.tiles(tile) + [out] * 2,
        [out] * 2,
        [((rows, width), BF16)] * 2,
        flops=2 * rows * model * width,
        moved=2 * (rows * model + model * width + 4 * rows * width),
    )(grads, *down.pieces, slope, silu)


def mixed_back_body(n, counts, *refs):
    m = sum(counts)
    out_ref, x_ref, sems = refs[m + n :]

    @pl.when(pl.program_id(0) == 0)
    def _():
        collect(counts, refs, x_ref, sems)

    out_ref[...] = nn(x_ref[...], joined(refs[m : m + n])).astype(BF16)


def mixed_back(chain, held, out):
    counts, arrays, specs, scratch = collected(held)
    rows, model = scratch[0].shape
    n, width = len(out.pieces), out.width
    tile = min(256, width)
    return chain.call(
        functools.partial(mixed_back_body, n, counts),
        (width // tile,),
        specs + out.tiles(tile),
        [pl.BlockSpec((rows, tile), lambda j: (0, j))],
        [((rows, width), BF16)],
        flops=2 * rows * model * width,
        scratch=scratch,
        moved=2 * (rows * model + model * width + rows * width),
    )(*arrays, *out.pieces)[0]


def trans_body(n, starts, targets, *refs):
    parts, blocks = len(starts), len(targets[0])
    lefts = refs[:parts]
    pieces = refs[parts : parts * (n + 1)]
    outs = refs[parts * (n + 1) : -4]
    held, ready, sems, out_sems = refs[-4:]
    j = pl.program_id(0)
    depth, width = held.shape[2:]
    rows = ready.shape[1] // blocks

    def copy(i, p, slot):
        source = pieces[p * n + i].at[pl.ds(0, depth), pl.ds(starts[p], width)]
        return pltpu.make_async_copy(source, held.at[slot, p], sems.at[slot, p])

    def fetch(step, slot):
        for i in range(n):

            @pl.when(step == i)
            def _():
                for p in range(parts):
                    copy(i, p, slot).start()

    def leave(slot, k, array, first, column):
        target = outs[array].at[pl.ds(first, rows), pl.ds(column, depth)]
        source = ready.at[slot, pl.ds(k * rows, rows), :]
        return pltpu.make_async_copy(source, target, out_sems.at[slot, k])

    def left(slot):
        for k in range(blocks):
            leave(slot, k, 0, 0, 0).wait()

    @pl.when(j == 0)
    def _():
        fetch(j, 0)

    @pl.when(j + 1 < n)
    def _():
        fetch(j + 1, (j + 1) % 2)

    slot = j % 2
    for p in range(parts):
        copy(0, p, slot).wait()

    @pl.when(j >= 2)
    def _():
        left(slot)

    for s in range(blocks * rows // SEQ):
        span = slice(s * SEQ, (s + 1) * SEQ)
        total = nt(lefts[0][span, :], held[slot, 0])
        for p in range(1, parts):
            total += nt(lefts[p][span, :], held[slot, p])
        ready[slot, span, :] = total.astype(BF16)
    column = pl.multiple_of(j % (n // 2) * depth, 128)
    for h in range(2):

        @pl.when((j >= n // 2) == (h == 1))
        def _():
            for k, (array, first) in enumerate(targets[h]):
                leave(slot, k, array, first, column).start()

    @pl.when(j == n - 1)
    def _():
        left(1 - slot)
        left(slot)


def times_trans(chain, parts, group):
    weights = [weight for _, weight in parts]
    n, depth, width = len(weights[0].pieces), weights[0].rows, weights[0].width
    rows = parts[0][0].shape[0]
    half = weights[0].model // 2
    size = rows // group.size
    messages = group.messages()
    shapes = [((size, half), BF16)] * 2
    targets = [{0: (0, 0)}, {0: (1, 0)}]
    for h in range(2):
        for keys in messages[h]:
            for i, k in enumerate(keys):
                targets[h][k] = (len(shapes), i * size)
            shapes.append(((len(keys) * size, half), BF16))
    targets = [[t[k] for k in range(group.size)] for t in targets]
    anywhere = pl.BlockSpec(memory_space=pl.ANY)
    outs = chain.call(
        functools.partial(trans_body, n, [weight.start for weight in weights], targets),
        (n,),
        [whole((rows, width))] * len(parts) + [anywhere] * (n * len(parts)),
        [anywhere] * len(shapes),
        shapes,
        flops=4 * rows * half * width * len(parts),
        scratch=[
            pltpu.VMEM((2, len(parts), depth, width), BF16),
            pltpu.VMEM((2, rows, depth), BF16),
            pltpu.SemaphoreType.DMA((2, len(parts))),
            pltpu.SemaphoreType.DMA((2, group.size)),
        ],
        moved=2 * (2 * rows * half + len(parts) * (rows + 2 * half) * width),
    )(*[left for left, _ in parts], *[piece for weight in weights for piece in weight.pieces])
    m = group.bits
    return outs[:2], [outs[2 : 2 + m], outs[2 + m :]]


def grad_body(parts, got, blocks, steps, *refs):
    lefts, refs = refs[:blocks], refs[blocks:]
    rights, refs = refs[:parts], refs[parts:]
    got_ref = refs[0] if got else None
    outs, turned = refs[got:-1], refs[-1]
    j = pl.program_id(0)

    @pl.when(j == 0)
    def _():
        rows = turned.shape[1] // blocks
        for k in range(blocks):
            turned[:, cut(rows, k)] = lefts[k][...].T

    for i in range(parts):

        @pl.when((j >= i * steps) & (j < (i + 1) * steps))
        def _():
            total = nn(turned[...], rights[i][...])
            if got:
                total += got_ref[...].astype(F32)
            total = total.astype(BF16)
            first = 0
            for out_ref in outs:
                count = out_ref.shape[0]
                out_ref[...] = total[first : first + count]
                first += count


def weight_grads(chain, left, which, rights, got=None, bits=0):
    rows, width = rights[0].shape
    parts = len(rights)
    tile = min(512, width)
    steps = width // tile
    if isinstance(left, list):
        lefts = [block[0] if len(block) == 1 else block[which] for block in left]
        half = left[0][0].shape[1] // 2
        places = [which if len(block) == 1 else 0 for block in left]
    else:
        lefts, places, half = [left], [which], left.shape[1] // 2
    blocks = len(lefts)
    ins = [
        pl.BlockSpec((rows // blocks, half), functools.partial(lambda at, j: (0, at), at))
        for at in places
    ]
    for i in range(parts):
        ins.append(
            pl.BlockSpec(
                (rows, tile),
                functools.partial(
                    lambda first, j: (0, jnp.clip(j - first, 0, steps - 1)), i * steps
                ),
            )
        )
    column = lambda j: (0, j)
    more = [] if got is None else [got]
    sizes = [half >> bits]
    for p in range(bits):
        sizes += [sizes[0], ((1 << p) - 1) * sizes[0]] if p else [sizes[0]]
    return chain.call(
        functools.partial(grad_body, parts, len(more), blocks, steps),
        (parts * steps,),
        ins + [pl.BlockSpec((half, tile), column)] * len(more),
        [pl.BlockSpec((size, tile), column) for size in sizes],
        [((size, parts * width), BF16) for size in sizes],
        flops=2 * rows * half * width * parts,
        scratch=[pltpu.VMEM((half, rows), BF16)],
        moved=2 * (rows * half + parts * (rows + half) * width),
    )(*lefts, *rights, *more)


def causal(scores):
    past = scores.shape[0] - HALF_SEQ
    key = lax.broadcasted_iota(jnp.int32, (HALF_SEQ, HALF_SEQ), 0)
    query = lax.broadcasted_iota(jnp.int32, (HALF_SEQ, HALF_SEQ), 1)
    last = jnp.where(key <= query, scores[past:], -1e30)
    return last if past == 0 else jnp.concatenate([scores[:past], last], axis=0)


def head_of(h):
    return slice(h * HEAD_DIM, (h + 1) * HEAD_DIM)


def span_of(b):
    return slice(b * HALF_SEQ, (b + 1) * HALF_SEQ)


def in_place(shift_ref, ref, count):
    rows = SEQ // count
    spans = [pl.ds(pl.multiple_of((i ^ shift_ref[0]) * rows, rows), rows) for i in range(count)]
    return jnp.concatenate([ref[span, :] for span in spans], axis=0)


def put_back(shift_ref, ref, count, values):
    rows = SEQ // count
    for i in range(count):
        ref[pl.ds(pl.multiple_of((i ^ shift_ref[0]) * rows, rows), rows), :] = values[cut(rows, i)]


def one_head(values, h):
    lane = lax.broadcasted_iota(jnp.int32, values.shape, 1)
    return jnp.where(lane // HEAD_DIM == h, values, jnp.zeros_like(values))


def attend_body(count, shift_ref, q_ref, k_ref, v_ref, out_ref, sum_ref):
    queries, keys = in_place(shift_ref, q_ref, count), in_place(shift_ref, k_ref, count)
    values = in_place(shift_ref, v_ref, count).astype(F32).T.astype(BF16)
    heads = []
    for h in range(2):
        blocks = []
        for b in range(2):
            reach = (b + 1) * HALF_SEQ
            query = one_head(queries[span_of(b)] * BF16(FACTOR), h)
            scores = causal(nt(keys[:reach], query))
            top = jnp.max(scores, axis=0, keepdims=True)
            expo = jnp.exp(scores - top)
            total = jnp.sum(expo, axis=0, keepdims=True)
            mixed = nn(values[head_of(h), :reach], expo.astype(BF16))
            blocks.append(mixed * (1.0 / total))
            sum_ref[0, 0, h : h + 1, span_of(b)] = top + jnp.log(total)
        heads.append(jnp.concatenate(blocks, axis=1))
    put_back(shift_ref, out_ref, count, jnp.concatenate(heads, axis=0).T.astype(BF16))


def attend(chain, shift, count, query, key, value):
    rows, width = query.shape
    seqs, pairs = rows // SEQ, width // PAIR
    tile = pl.BlockSpec((SEQ, PAIR), lambda s, p, _: (s, p))
    return chain.call(
        functools.partial(attend_body, count),
        (seqs, pairs),
        [tile] * 3,
        [tile, pl.BlockSpec((1, 1, 2, SEQ), lambda s, p, _: (s, p, 0, 0))],
        [((rows, width), BF16), ((seqs, pairs, 2, SEQ), F32)],
        flops=16 * rows * width * SEQ,
        prefetch=1,
        moved=8 * rows * width,
    )(shift, query, key, value)


def attend_back_body(
    count, shift_ref, q_ref, k_ref, v_ref, g_ref, sum_ref, cos_ref, sin_ref, dq_ref, dk_ref, dv_ref
):
    queries, keys, values, grads = (
        in_place(shift_ref, ref, count) for ref in (q_ref, k_ref, v_ref, g_ref)
    )
    turned = keys.astype(F32).T.astype(BF16)
    dq_heads = []
    dk, dv = [], []
    for b in range(2):
        reach = (b + 1) * HALF_SEQ
        dq = []
        for h in range(2):
            query = one_head(queries[span_of(b)], h)
            grad = one_head(grads[span_of(b)], h)
            scores = causal(nt(keys[:reach], query * BF16(FACTOR)))
            probs = jnp.exp(scores - sum_ref[0, 0, h : h + 1, span_of(b)])
            probs_grad = nt(values[:reach], grad)
            inner = jnp.sum(probs * probs_grad, axis=0, keepdims=True)
            score_grad = (probs * (probs_grad - inner)).astype(BF16)
            dv.append(nn(probs.astype(BF16), grad))
            dk.append(nn(score_grad, query))
            dq.append(nn(turned[head_of(h), :reach], score_grad))
        dq_heads.append(jnp.concatenate(dq, axis=0))

    def whole_rows(parts):
        early, late = parts[0] + parts[1], parts[2] + parts[3]
        return jnp.concatenate([late[:HALF_SEQ] + early, late[HALF_SEQ:]], axis=0)

    dq = jnp.concatenate(dq_heads, axis=1).T * FACTOR
    dk = whole_rows(dk) * FACTOR
    dv = whole_rows(dv).astype(BF16)
    cosine, sine = cos_ref[...], sin_ref[...]
    put_back(shift_ref, dq_ref, count, (dq * cosine - turn(dq) * sine).astype(BF16))
    put_back(shift_ref, dk_ref, count, (dk * cosine - turn(dk) * sine).astype(BF16))
    put_back(shift_ref, dv_ref, count, dv)


def attend_back(chain, shift, count, query, key, value, grad, logsum, tables):
    rows, width = query.shape
    seqs, pairs = rows // SEQ, width // PAIR
    tile = pl.BlockSpec((SEQ, PAIR), lambda s, p, _: (s, p))
    return chain.call(
        functools.partial(attend_back_body, count),
        (seqs, pairs),
        [tile] * 4
        + [pl.BlockSpec((1, 1, 2, SEQ), lambda s, p, _: (s, p, 0, 0))]
        + [whole((SEQ, PAIR))] * 2,
        [tile] * 3,
        [((rows, width), BF16)] * 3,
        flops=40 * rows * width * SEQ,
        prefetch=1,
        moved=14 * rows * width,
    )(shift, query, key, value, grad, logsum, *tables)


def local(
    chips,
    group,
    tokens,
    attn_gain,
    query_weight,
    key_weight,
    value_weight,
    output_weight,
    ffn_gain,
    gate_weight,
    up_weight,
    down_weight,
    cotangent,
):
    line = jnp.asarray(chips.table)[lax.axis_index("dp")]
    rows, model = tokens.shape
    count = SEQ // rows
    shift = lax.axis_index("tensor") % count
    row = jnp.arange(SEQ, dtype=jnp.int32)
    places = rope_tables(row)
    tables = rope_tables((row // rows ^ shift) * rows + row % rows)
    shift = jnp.reshape(shift, (1,)).astype(jnp.int32)
    early = (*places, *tables, line, shift)
    depth, own = query_weight.shape
    hidden_units = gate_weight.shape[1]
    chain = Chain()

    def gather(piece):
        return Gather(chips, chain, chain.join(piece)[0])

    def spread_of(values):
        return Spread(group, chain, chain.join(values)[0])

    def fold_of(part):
        own_part, sent = part
        sent = chain.join(*sent[0], *sent[1])
        return Fold(group, chain, own_part, [sent[: group.bits], sent[group.bits :]])

    def grads_of(left, rights):
        got = [None]
        chain.ask(weight_grads(chain, left, 1, rights)[0], got, 0, chips.other)

        def mine(**how):
            if got[0] is None:
                chain.flush()
            blocks = weight_grads(chain, left, 0, rights, got[0], chips.bits)
            return Sums(chips, chain, blocks, **how)

        return mine

    extra = jnp.concatenate([attn_gain, ffn_gain, jnp.zeros((4 * own - 2 * depth,), BF16)])
    attn = jnp.concatenate([query_weight, key_weight, value_weight, output_weight.T], axis=1)
    attn = gather(jnp.concatenate([attn, jnp.broadcast_to(extra, (16, 4 * own))], axis=0))
    spread = spread_of(tokens)
    grads_spread = spread_of(cotangent)
    grads_spread.later = []
    down_turned, *early = chain.join(down_weight.T, *early)
    places, tables, line, shift = early[:2], early[2:4], early[4], early[5]
    chain.end(attn, spread, grads_spread)
    chain.end(attn, spread)
    all_tokens = spread.blocks()
    attn = attn.pieces()
    pair = gather(jnp.concatenate([gate_weight, up_weight], axis=1))
    w_query, w_key, w_value, w_output = [Weight(attn, depth, i * own, own) for i in range(4)]
    gains = jnp.concatenate(
        [piece[depth : depth + 1, : 2 * depth].reshape(2, depth) for piece in attn], axis=1
    ).astype(F32)

    group_one = ordered(chain, norm_body, line, gains, all_tokens)
    grads_spread.resume()
    query, key, value = project(chain, group_one, tables, w_query, w_key, w_value)
    mixed, logsum = attend(chain, shift, count, query, key, value)
    out_part = times_trans(chain, [(mixed, w_output)], group)
    fold = fold_of(out_part)
    chain.end(fold, pair, grads_spread)
    grad_rows = ordered(chain, order_body, line, gains, grads_spread.blocks())
    chain.end(fold)
    attended = fold.total()
    middle, second = by_rows(
        chain, middle_body, line, tokens, gains, attended, [], [F32, BF16]
    )
    spread = spread_of(second)
    chain.end(spread, pair)
    pair = pair.pieces()
    down = gather(down_turned)
    chain.end(spread)
    group_two = spread.blocks()
    w_gate = Weight(pair, depth, 0, hidden_units)
    w_up = Weight(pair, depth, hidden_units, hidden_units)
    hidden, slope, silu = gate_up(chain, group_two, w_gate, w_up)

    mine = grads_of(grad_rows, [hidden])
    chain.end(down)
    chain.flush()
    down_sum = mine()
    w_down = Weight(down.pieces(), depth, 0, hidden_units)
    gate_grad, up_grad = hidden_back(chain, grad_rows, w_down, slope, silu)
    mine_gate = grads_of(group_two, [gate_grad])
    chain.end(down_sum)
    second_part = times_trans(chain, [(gate_grad, w_gate), (up_grad, w_up)], group)
    mine_up = grads_of(group_two, [up_grad])
    gate_sum = mine_gate(hold=True)
    chain.end(down_sum)
    fold = fold_of(second_part)
    up_sum = mine_up(apart=True)
    chain.end(gate_sum, fold)
    result_part = times_trans(chain, [(hidden, w_down)], group)
    chain.end(fold)
    second_grad = fold.total()
    middle_grad, low_grad = by_rows(
        chain, second_back_body, line, cotangent, gains, second_grad, [middle], [F32, BF16]
    )
    spread = spread_of(low_grad)
    chain.end(up_sum)
    gate_sum.resume()
    (down_sum,) = finish(chain, down_sum.terms())
    chain.end(spread)
    attn_grads = spread.blocks()

    mixed_grad = mixed_back(chain, attn_grads, w_output)
    mine_out = grads_of(attn_grads, [mixed])
    chain.end(gate_sum)
    up_sum.send_half(0)
    fold = fold_of(result_part)
    query_back, key_back, value_back = attend_back(
        chain, shift, count, query, key, value, mixed_grad, logsum, places
    )
    mine_qkv = grads_of(group_one, [query_back, key_back, value_back])
    out_sum = mine_out(hold=True)
    chain.end(up_sum, fold)
    up_sum.send_half(1)
    qkv_sum = mine_qkv(cut_in_two=True)
    chain.end(fold, out_sum)
    result_part = fold.total()
    first_part = times_trans(
        chain, [(query_back, w_query), (key_back, w_key), (value_back, w_value)], group
    )
    chain.end(up_sum, qkv_sum)
    fold = fold_of(first_part)
    out_sum.resume()
    up_sum, up_inner = finish(chain, up_sum.terms(), [up_weight])
    gate_sum, gate_inner = finish(chain, gate_sum.terms(), [gate_weight])
    (layer_out,) = by_rows(chain, result_body, line, middle, gains, result_part, [], [BF16])
    chain.end(fold)
    chain.end(fold)
    chain.end(qkv_sum)
    query_sum, key_sum, value_sum, qkv_inner = finish(
        chain, qkv_sum.terms(), [query_weight, key_weight, value_weight]
    )
    gain_parts = jnp.stack(
        [qkv_inner / attn_gain.astype(F32), (gate_inner + up_inner) / ffn_gain.astype(F32)]
    )
    (gain_parts,) = chain.join(gain_parts)
    first_grad = fold.total()
    (input_grad,) = by_rows(
        chain, first_back_body, line, tokens, gains, first_grad, [middle_grad], [F32]
    )
    (out_sum,) = finish(chain, out_sum.terms())
    gain_totals = gain_parts
    for k in range(1, group.size):
        pairs = [(i, i ^ k) for i in range(group.size)]
        gain_totals += lax.ppermute(gain_parts, "tensor", pairs)
    gain_one_total, gain_two_total = gain_totals[0], gain_totals[1]
    return (
        layer_out,
        input_grad,
        gain_one_total,
        query_sum,
        key_sum,
        value_sum,
        out_sum,
        gain_two_total,
        gate_sum,
        up_sum,
        down_sum,
    )


def solution(mesh):
    in_specs = (
        P(("dp", "tensor"), None),
        P("dp"),
        P("dp", "tensor"),
        P("dp", "tensor"),
        P("dp", "tensor"),
        P("tensor", "dp"),
        P("dp"),
        P("dp", "tensor"),
        P("dp", "tensor"),
        P("tensor", "dp"),
        P(("dp", "tensor"), None),
    )
    out_specs = (
        P(("dp", "tensor"), None),
        P(("dp", "tensor"), None),
        P("dp"),
        P("dp", "tensor"),
        P("dp", "tensor"),
        P("dp", "tensor"),
        P("tensor", "dp"),
        P("dp"),
        P("dp", "tensor"),
        P("dp", "tensor"),
        P("tensor", "dp"),
    )
    chips = Chips(mesh.shape["dp"])
    size = mesh.shape["tensor"]
    links = [[(i, i ^ 1 << b) for i in range(size)] for b in range(size.bit_length() - 1)]
    group = Group(links, "tensor")

    def run(*arrays):
        return local(chips, group, *arrays)

    return jax.shard_map(run, mesh=mesh, in_specs=in_specs, out_specs=out_specs, check_vma=False)
```

```python
import functools

import jax
import jax.numpy as jnp
import numpy as np
from jax import lax
from jax.experimental import pallas as pl
from jax.experimental.pallas import tpu as pltpu
from jax.sharding import PartitionSpec as P

HEAD_DIM = 64
SEQ = 512
EPS = 1e-05
THETA = 130000.0
BF16 = jnp.bfloat16
F32 = jnp.float32
FACTOR = HEAD_DIM**-0.5
PAIR = 2 * HEAD_DIM
HALF_SEQ = SEQ // 2
VMEM_LIMIT = 58 << 20
COST_SHARE = 4096


class Chain:
    def __init__(self):
        self.token = jnp.zeros((8, 128), F32)
        self.swaps, self.asked = [], []

    def join(self, *values):
        *values, self.token = lax.optimization_barrier((*values, self.token))
        return values

    def gate(self, *values):
        swaps, self.swaps = self.swaps, []
        asked, self.asked = self.asked, []
        joined = self.join(
            *values, *[held[i] for held, i in swaps], *[source for source, _, _, _ in asked]
        )
        for (held, i), value in zip(swaps, joined[len(values) :]):
            held[i] = value
        for (_, held, i, swap), value in zip(asked, joined[len(values) + len(swaps) :]):
            held[i] = swap(value)
            self.swaps.append((held, i))
        return joined[: len(values)]

    def end(self, *transfers):
        counts = [len(t.flying) for t in transfers]
        got = self.gate(*[value for t in transfers for value in t.flying])
        for t, count in zip(transfers, counts):
            if count:
                t.go_on(got[:count])
            got = got[count:]

    def ask(self, source, held, i, swap):
        self.asked.append((source, held, i, swap))

    def flush(self):
        for source, held, i, swap in self.asked:
            held[i] = swap(source)
        self.asked = []

    def call(self, body, grid, ins, outs, shapes, flops, scratch=(), prefetch=0, moved=0):
        first = prefetch + len(ins)
        second = first + 1 + len(outs)
        anywhere = pl.BlockSpec(memory_space=pl.ANY)

        def wrapped(*refs):
            body(*refs[:first], *refs[first + 1 : second], *refs[second + 1 :])

        run = pl.pallas_call(
            wrapped,
            grid_spec=pltpu.PrefetchScalarGridSpec(
                num_scalar_prefetch=prefetch,
                grid=grid,
                in_specs=[*ins, anywhere],
                out_specs=[*outs, anywhere],
                scratch_shapes=list(scratch),
            ),
            out_shape=[jax.ShapeDtypeStruct(s, t) for s, t in [*shapes, ((8, 128), F32)]],
            compiler_params=pltpu.CompilerParams(
                vmem_limit_bytes=VMEM_LIMIT, dimension_semantics=("arbitrary",) * len(grid)
            ),
            cost_estimate=pl.CostEstimate(
                flops=flops // COST_SHARE, bytes_accessed=moved // COST_SHARE, transcendentals=0
            ),
        )

        def with_token(*args):
            *results, self.token = run(*args, self.token)
            return results

        return with_token


class Chips:
    def __init__(self, size):
        self.bits = (size // 2).bit_length() - 1
        self.size = size
        self.swap = [(i, i ^ 1) for i in range(size)]
        self.links = [
            [(i, i ^ 2 << self.bits - 1 - p) for i in range(size)] for p in range(self.bits)
        ]
        flips = [
            sum(1 << self.bits - 1 - p for p in range(self.bits) if v >> p & 1)
            for v in range(1 << self.bits)
        ]
        table = [[i ^ 2 * f for f in flips] + [i ^ 2 * f ^ 1 for f in flips] for i in range(size)]
        self.table = np.array(table, np.int32)

    def send(self, value, p):
        return lax.ppermute(value, "dp", self.links[p])

    def other(self, value):
        return lax.ppermute(value, "dp", self.swap)


class Gather:
    def __init__(self, chips, chain, piece):
        self.chips, self.chain = chips, chain
        self.own = [piece] + [None] * (2**chips.bits - 1)
        self.others = list(self.own)
        self.ask(0)
        self.keys = [1 << p for p in range(chips.bits)]
        self.flying = [chips.send(piece, p) for p in range(chips.bits)]

    def ask(self, v):
        self.chain.ask(self.own[v], self.others, v, self.chips.other)

    def go_on(self, got):
        keys, self.keys, self.flying = self.keys, [], []
        for v, piece in zip(keys, got):
            self.own[v] = piece
            for p in range(v.bit_length(), self.chips.bits):
                self.keys.append(v | 1 << p)
                self.flying.append(self.chips.send(piece, p))
        for v in keys:
            self.ask(v)

    def pieces(self):
        while self.flying:
            self.chain.end(self)
        self.chain.flush()
        return self.own + self.others


class Sums:
    def __init__(self, chips, chain, mine, apart=False, hold=False, cut_in_two=False):
        self.chips, self.chain, self.apart, self.hold = chips, chain, apart, hold
        self.todo = []
        self.cut_in_two = cut_in_two and chips.bits == 2
        self.parts = [mine[0]]
        mine = list(mine[1:])
        self.direct, self.passed = [], []
        for p in range(chips.bits):
            self.direct.append(mine.pop(0))
            self.passed.append(mine.pop(0) if p else None)
        self.p = chips.bits - 1
        if self.cut_in_two:
            self.kinds = [0, 1]
            self.flying = [chips.send(half, 1) for half in self.in_two(self.passed[1])]
            return
        self.kinds = [self.p]
        self.flying = [chips.send(self.passed[self.p], self.p)]

    def in_two(self, values):
        width = values.shape[1] // 2
        return values[:, :width], values[:, width:]

    def go_on(self, got):
        rows = self.parts[0].shape[0]
        kinds, self.kinds, self.flying = self.kinds, [], []
        if self.p == 0:
            self.parts += got
            return
        if self.cut_in_two:
            self.p = 0
            total = self.direct[0].astype(F32) + jnp.concatenate(got, axis=1).astype(F32)
            self.todo = [(None, self.direct[1], 1), (None, total.astype(BF16), 0)]
            self.resume()
            return
        for kind, block in zip(kinds, got):
            if kind is None:
                self.parts.append(block)
                continue
            add = lambda held, first: (
                held.astype(F32) + block[first * rows : first * rows + held.shape[0]].astype(F32)
            ).astype(BF16)
            for q in range(kind):
                self.direct[q] = add(self.direct[q], (1 << q) - 1)
                if q:
                    self.passed[q] = add(self.passed[q], 1 << q)
        p, self.p = self.p, self.p - 1
        if p > 0:
            self.todo.append((None, self.direct[p], p))
        if p > 1:
            self.todo.append((p - 1, self.passed[p - 1], p - 1))
        if p == 1 and not self.apart:
            self.todo.append((None, self.direct[0], 0))
        if not self.hold:
            self.resume()

    def resume(self):
        todo, self.todo = self.todo, []
        values = self.chain.join(*[value for _, value, _ in todo])
        for (kind, _, p), value in zip(todo, values):
            self.kinds.append(kind)
            self.flying.append(self.chips.send(value, p))

    def send_half(self, i):
        while self.p > 0:
            self.chain.end(self)
        width = self.direct[0].shape[1] // 2
        (value,) = self.chain.join(self.direct[0][:, i * width : (i + 1) * width])
        self.kinds.append(None)
        self.flying.append(self.chips.send(value, 0))

    def terms(self):
        while self.flying or self.todo:
            if self.todo:
                self.resume()
            self.chain.end(self)
        return sorted(self.parts, key=lambda part: -part.shape[1])


class Group:
    def __init__(self, links, axes):
        self.links, self.axes = links, axes
        self.bits = len(links)
        self.size = 1 << self.bits
        self.orders = (list(range(self.bits)), list(range(self.bits))[::-1])

    def send(self, value, bit):
        return lax.ppermute(value, self.axes, self.links[bit])

    def messages(self):
        found = []
        for order in self.orders:
            found.append([])
            for top in reversed(range(self.bits)):
                found[-1].append(
                    [
                        1 << order[top] | sum(1 << order[p] for p in range(top) if v >> p & 1)
                        for v in range(1 << top)
                    ]
                )
        return found


class Spread:
    def __init__(self, group, chain, rows):
        self.group, self.chain = group, chain
        self.held = {0: [rows]}
        self.later = None
        self.keys = [(1 << b, None) for b in range(group.bits)]
        self.flying = [group.send(rows, b) for b in range(group.bits)]

    def go_on(self, got):
        fresh = list(zip(self.keys, got))
        self.keys, self.flying = [], []
        for (k, h), block in fresh:
            if h is None:
                self.held[k] = [block]
            else:
                self.held.setdefault(k, [None, None])[h] = block
        for (k, h), block in fresh:
            for way, order in enumerate(self.group.orders):
                if h is not None and h != way:
                    continue
                half = block.shape[1] // 2
                top = max(i for i, bit in enumerate(order) if k >> bit & 1)
                for i in range(top + 1, len(order)):
                    part = block if h is not None else block[:, way * half : (way + 1) * half]
                    self.keys.append((k | 1 << order[i], way))
                    if self.later is not None:
                        self.later.append((part, order[i]))
                    else:
                        self.flying.append(self.group.send(part, order[i]))

        if self.later:
            parts = self.chain.join(*[part for part, _ in self.later])
            self.later = [(part, bit) for part, (_, bit) in zip(parts, self.later)]

    def resume(self):
        later, self.later = self.later, None
        parts = self.chain.join(*[part for part, _ in later])
        self.flying = [self.group.send(part, bit) for part, (_, bit) in zip(parts, later)]

    def blocks(self):
        while self.flying:
            self.chain.end(self)
        return [self.held[k] for k in range(self.group.size)]


class Fold:
    def __init__(self, group, chain, own, sent):
        self.group, self.chain = group, chain
        self.rows = own[0].shape[0]
        self.sent = [list(half) for half in sent]
        self.parts = [[half] for half in own]
        self.wave = 0
        self.start()

    def start(self):
        self.flying = [
            self.group.send(self.sent[h][self.wave], order[self.group.bits - 1 - self.wave])
            for h, order in enumerate(self.group.orders)
        ]

    def go_on(self, got):
        self.wave += 1
        self.flying = []
        for h, block in enumerate(got):
            self.parts[h].append(block)
        for wave in range(self.wave, self.group.bits):
            sums = add_rows(self.chain, [sent[wave] for sent in self.sent], got)
            for sent, value in zip(self.sent, sums):
                sent[wave] = value
        if self.wave < self.group.bits:
            self.start()

    def total(self):
        while self.flying:
            self.chain.end(self)
        return self.parts


class Weight:
    def __init__(self, pieces, rows, start, width):
        self.pieces, self.rows, self.start, self.width = pieces, rows, start, width
        self.model = len(pieces) * rows

    def tiles(self, tile):
        first = self.start // tile
        return [pl.BlockSpec((self.rows, tile), lambda j: (0, first + j))] * len(self.pieces)


def nn(left, right):
    return lax.dot_general(left, right, (((1,), (0,)), ((), ())), preferred_element_type=F32)


def nt(left, right):
    return lax.dot_general(left, right, (((1,), (1,)), ((), ())), preferred_element_type=F32)


def tn(left, right):
    return lax.dot_general(left, right, (((0,), (0,)), ((), ())), preferred_element_type=F32)


def whole(shape):
    return pl.BlockSpec(shape, lambda *_: (0,) * len(shape))


def place(line_ref, j, width):
    return pl.ds(pl.multiple_of(line_ref[j] * width, 128), width)


def cut(width, j):
    return slice(j * width, (j + 1) * width)


def scale_of(values):
    return lax.rsqrt(jnp.mean(values * values, axis=-1, keepdims=True) + EPS)


def fetch_blocks(counts, refs, held, sems, k, slot, wait):
    first = 0
    for i, count in enumerate(counts):
        copies = []
        half = held.shape[2] // count
        for h in range(count):
            target = held.at[slot, :, pl.ds(h * half, half)]
            copies.append(pltpu.make_async_copy(refs[first + h], target, sems.at[slot, h]))
        first += count

        @pl.when(k == i)
        def _():
            for copy in copies:
                copy.wait() if wait else copy.start()


def fetched(counts, refs, held, sems):
    k = pl.program_id(0)

    @pl.when(k == 0)
    def _():
        fetch_blocks(counts, refs, held, sems, k, 0, False)

    fetch_blocks(counts, refs, held, sems, k + 1, (k + 1) % 2, False)
    fetch_blocks(counts, refs, held, sems, k, k % 2, True)
    return held.at[k % 2]


def norm_body(blocks, counts, line_ref, gain_ref, *refs):
    out_ref, held, sems = refs[sum(counts) :]
    x_ref = fetched(counts, refs, held, sems)
    width = out_ref.shape[1] // blocks
    scale = scale_of(x_ref[...].astype(F32))
    for j in range(blocks):
        part = x_ref[:, place(line_ref, j, width)].astype(F32)
        gain = gain_ref[0:1, cut(width, j)]
        out_ref[:, cut(width, j)] = (part * scale * gain).astype(BF16)


def order_body(blocks, counts, line_ref, gain_ref, *refs):
    out_ref, held, sems = refs[sum(counts) :]
    x_ref = fetched(counts, refs, held, sems)
    width = out_ref.shape[1] // blocks
    for j in range(blocks):
        out_ref[:, cut(width, j)] = x_ref[:, place(line_ref, j, width)]


def ordered(chain, body, line, gains, held):
    counts = [len(block) for block in held]
    rows, model = held[0][0].shape
    n = len(held)
    return chain.call(
        functools.partial(body, line.shape[0], counts),
        (n,),
        [whole(gains.shape)] + [pl.BlockSpec(memory_space=pl.ANY)] * sum(counts),
        [pl.BlockSpec((rows, model), lambda k, *_: (k, 0))],
        [((n * rows, model), BF16)],
        flops=20 * n * rows * model,
        scratch=[pltpu.VMEM((2, rows, model), BF16), pltpu.SemaphoreType.DMA((2, 2))],
        prefetch=1,
        moved=4 * n * rows * model,
    )(line, gains, *[array for block in held for array in block])[0]


def added(refs, span):
    total = refs[0][span, :].astype(F32)
    for ref in refs[1:]:
        total += ref[span, :].astype(F32)
    return total


def middle_body(blocks, m, line_ref, x_ref, gain_ref, *refs):
    middle_ref, out_ref = refs[2 * m :]
    width = x_ref.shape[1] // blocks
    half = x_ref.shape[1] // 2
    span = slice(None)
    middle_ref[:, :half] = added(refs[:m], span)
    middle_ref[:, half:] = added(refs[m : 2 * m], span)
    for j in range(blocks):
        here = x_ref[:, place(line_ref, j, width)].astype(F32)
        middle_ref[:, cut(width, j)] += here
    middle = middle_ref[...]
    out_ref[...] = (middle * scale_of(middle) * gain_ref[1:2, :]).astype(BF16)


def result_body(blocks, m, line_ref, middle_ref, gain_ref, *refs):
    out_ref = refs[2 * m]
    width = middle_ref.shape[1] // blocks
    span = slice(None)
    total = middle_ref[...] + jnp.concatenate(
        [added(refs[:m], span), added(refs[m : 2 * m], span)], axis=1
    )
    for j in range(blocks):
        out_ref[:, place(line_ref, j, width)] = total[:, cut(width, j)].astype(BF16)


def second_back_body(blocks, m, line_ref, dy_ref, gain_ref, *refs):
    middle_ref, out_ref, low_ref = refs[2 * m :]
    width = dy_ref.shape[1] // blocks
    span = slice(None)
    grad = jnp.concatenate([added(refs[:m], span), added(refs[m : 2 * m], span)], axis=1)
    middle = middle_ref[...]
    scale = scale_of(middle)
    normed = middle * scale
    scaled = grad * gain_ref[1:2, :]
    out_ref[...] = scale * (scaled - normed * jnp.mean(scaled * normed, axis=-1, keepdims=True))
    for j in range(blocks):
        out_ref[:, cut(width, j)] += dy_ref[:, place(line_ref, j, width)].astype(F32)
    low_ref[...] = out_ref[...].astype(BF16)


def first_back_body(blocks, m, line_ref, x_ref, gain_ref, *refs):
    above_ref, out_ref = refs[2 * m :]
    width = x_ref.shape[1] // blocks
    span = slice(None)
    scale = scale_of(x_ref[...].astype(F32))
    normed = jnp.concatenate(
        [x_ref[:, place(line_ref, j, width)].astype(F32) for j in range(blocks)], axis=1
    ) * scale
    grad = jnp.concatenate([added(refs[:m], span), added(refs[m : 2 * m], span)], axis=1)
    scaled = grad * gain_ref[0:1, :]
    back = scale * (scaled - normed * jnp.mean(scaled * normed, axis=-1, keepdims=True))
    total = above_ref[...] + back
    for j in range(blocks):
        out_ref[:, place(line_ref, j, width)] = total[:, cut(width, j)]


def by_rows(chain, body, line, first, gains, parts, more, kinds):
    rows, model = first.shape
    half = model // 2
    tile = min(256, rows)
    row = pl.BlockSpec((tile, model), lambda i, *_: (i, 0))
    slim = pl.BlockSpec((tile, half), lambda i, *_: (i, 0))
    m = len(parts[0])
    return chain.call(
        functools.partial(body, line.shape[0], m),
        (rows // tile,),
        [row, whole(gains.shape)] + [slim] * (2 * m) + [row] * len(more),
        [row] * len(kinds),
        [((rows, model), kind) for kind in kinds],
        flops=20 * rows * model,
        prefetch=1,
        moved=rows * model * (2 * m + 4 * len(kinds)),
    )(line, first, gains, *parts[0], *parts[1], *more)


def add_rows_body(count, *refs):
    for i in range(count):
        total = refs[i][...].astype(F32) + refs[count + i][...].astype(F32)
        refs[2 * count + i][...] = total.astype(BF16)


def add_rows(chain, helds, blocks):
    rows, columns = helds[0].shape
    tile = min(256, rows)
    steps = rows // tile
    count = len(helds)
    here = pl.BlockSpec((tile, columns), lambda i: (i, 0))
    return chain.call(
        functools.partial(add_rows_body, count),
        (steps,),
        [here] * count + [pl.BlockSpec((tile, columns), lambda i: (steps + i, 0))] * count,
        [here] * count,
        [((rows, columns), BF16)] * count,
        flops=count * rows * columns,
        moved=6 * count * rows * columns,
    )(*helds, *blocks)


def finish_body(m, halves, n, *refs):
    total = added(refs[:m], slice(None))
    if halves:
        total += jnp.concatenate([ref[...].astype(F32) for ref in refs[m : m + halves]], axis=1)
    m += halves
    weights, outs = refs[m : m + n], refs[m + n :]
    if not n:
        outs[0][...] = total.T
        return
    width = weights[0].shape[1]
    inner = jnp.zeros((total.shape[0], 1), F32)
    for i in range(n):
        part = total[:, cut(width, i)]
        outs[i][...] = part
        inner += jnp.sum(weights[i][...].astype(F32) * part, axis=1, keepdims=True)
    outs[n][...] = jnp.broadcast_to(inner, outs[n].shape)


def finish(chain, terms, weights=()):
    rows, columns = terms[0].shape
    tile = min(256 if weights else 128, rows)
    row = pl.BlockSpec((tile, columns), lambda i: (i, 0))
    n = len(weights)
    halves = sum(1 for term in terms if term.shape[1] < columns)
    half = [pl.BlockSpec((tile, columns // 2), lambda i: (i, 0))] * halves
    if n:
        slim = pl.BlockSpec((tile, columns // n), lambda i: (i, 0))
        outs = [slim] * n + [pl.BlockSpec((tile, 128), lambda i: (i, 0))]
        shapes = [((rows, columns // n), F32)] * n + [((rows, 128), F32)]
    else:
        slim = None
        outs = [pl.BlockSpec((columns, tile), lambda i: (0, i))]
        shapes = [((columns, rows), F32)]
    results = chain.call(
        functools.partial(finish_body, len(terms) - halves, halves, n),
        (rows // tile,),
        [row] * (len(terms) - halves) + half + [slim] * n,
        outs,
        shapes,
        flops=4 * rows * columns,
        moved=rows * columns * 12,
    )(*terms, *weights)
    if n:
        results[n] = results[n][:, 0]
    return results


def rope_tables(place):
    half = HEAD_DIM // 2
    freq = THETA ** (-2.0 * jnp.arange(half, dtype=F32) / HEAD_DIM)
    angle = place.astype(F32)[:, None] * freq[None, :]
    cosine, sine = jnp.cos(angle), jnp.sin(angle)
    return (
        jnp.concatenate([cosine] * (PAIR // half), axis=1),
        jnp.concatenate([-sine, sine] * (PAIR // HEAD_DIM), axis=1),
    )


def turn(values):
    half = HEAD_DIM // 2
    width = values.shape[-1]
    lane = lax.broadcasted_iota(jnp.int32, values.shape, 1) % HEAD_DIM
    return jnp.where(
        lane < half, pltpu.roll(values, width - half, 1), pltpu.roll(values, half, 1)
    )


def joined(refs):
    return jnp.concatenate([r[...] for r in refs], axis=0)


def qkv_body(n, x_ref, cos_ref, sin_ref, *refs):
    weights, outs = refs[: 3 * n], refs[3 * n :]
    rows = x_ref.shape[0]
    tile = outs[0].shape[1]
    for i in range(3):
        weight = joined(weights[i * n : (i + 1) * n])
        for s in range(rows // SEQ):
            span = slice(s * SEQ, (s + 1) * SEQ)
            product = nn(x_ref[span, :], weight)
            if i == 2:
                outs[i][span, :] = product.astype(BF16)
                continue
            for t in range(tile // PAIR):
                here = product[:, t * PAIR : (t + 1) * PAIR]
                turned = here * cos_ref[...] + turn(here) * sin_ref[...]
                outs[i][span, t * PAIR : (t + 1) * PAIR] = turned.astype(BF16)


def project(chain, x, tables, query, key, value):
    rows, model = x.shape
    n, width = len(query.pieces), query.width
    tile = min(256, width)
    out = pl.BlockSpec((rows, tile), lambda j: (0, j))
    return chain.call(
        functools.partial(qkv_body, n),
        (width // tile,),
        [whole(x.shape), whole((SEQ, PAIR)), whole((SEQ, PAIR))]
        + query.tiles(tile)
        + key.tiles(tile)
        + value.tiles(tile),
        [out] * 3,
        [((rows, width), BF16)] * 3,
        flops=6 * rows * model * width,
        moved=2 * (rows * model + 3 * model * width + 3 * rows * width),
    )(x, *tables, *query.pieces, *key.pieces, *value.pieces)


def collect(counts, refs, held, sems):
    rows = held.shape[0] // len(counts)
    copies = []
    for k, count in enumerate(counts):
        half = held.shape[1] // count
        for h in range(count):
            target = held.at[pl.ds(k * rows, rows), pl.ds(h * half, half)]
            i = len(copies)
            copies.append(pltpu.make_async_copy(refs[i], target, sems.at[i]))
    for copy in copies:
        copy.start()
    for copy in copies:
        copy.wait()


def gate_body(n, counts, *refs):
    m = sum(counts)
    gate_w, up_w = refs[m : m + n], refs[m + n : m + 2 * n]
    hidden_ref, slope_ref, silu_ref, x_ref, sems = refs[m + 2 * n :]

    @pl.when(pl.program_id(0) == 0)
    def _():
        collect(counts, refs, x_ref, sems)

    gate_weight, up_weight = joined(gate_w), joined(up_w)
    for s in range(x_ref.shape[0] // SEQ):
        span = slice(s * SEQ, (s + 1) * SEQ)
        gate = nn(x_ref[span, :], gate_weight)
        up = nn(x_ref[span, :], up_weight)
        sigm = jax.nn.sigmoid(gate)
        silu = gate * sigm
        hidden_ref[span, :] = (silu * up).astype(BF16)
        silu_ref[span, :] = silu.astype(BF16)
        slope_ref[span, :] = (up * sigm * (1.0 + gate * (1.0 - sigm))).astype(BF16)


def collected(held):
    counts = [len(block) for block in held]
    rows, model = held[0][0].shape
    scratch = [
        pltpu.VMEM((len(held) * rows, model), BF16),
        pltpu.SemaphoreType.DMA((sum(counts),)),
    ]
    arrays = [array for block in held for array in block]
    return counts, arrays, [pl.BlockSpec(memory_space=pl.ANY)] * len(arrays), scratch


def gate_up(chain, held, gate, up):
    counts, arrays, specs, scratch = collected(held)
    rows, model = scratch[0].shape
    n, width = len(gate.pieces), gate.width
    tile = min(256, width)
    out = pl.BlockSpec((rows, tile), lambda j: (0, j))
    return chain.call(
        functools.partial(gate_body, n, counts),
        (width // tile,),
        specs + gate.tiles(tile) + up.tiles(tile),
        [out] * 3,
        [((rows, width), BF16)] * 3,
        flops=4 * rows * model * width,
        scratch=scratch,
        moved=2 * (rows * model + 2 * model * width + 3 * rows * width),
    )(*arrays, *gate.pieces, *up.pieces)


def hidden_back_body(n, g_ref, *refs):
    weight = joined(refs[:n])
    slope_ref, silu_ref, gate_ref, up_ref = refs[n:]
    for s in range(g_ref.shape[0] // SEQ):
        span = slice(s * SEQ, (s + 1) * SEQ)
        grad = nn(g_ref[span, :], weight)
        gate_ref[span, :] = (grad * slope_ref[span, :].astype(F32)).astype(BF16)
        up_ref[span, :] = (grad * silu_ref[span, :].astype(F32)).astype(BF16)


def hidden_back(chain, grads, down, slope, silu):
    rows, model = grads.shape
    n, width = len(down.pieces), down.width
    tile = min(256, width)
    out = pl.BlockSpec((rows, tile), lambda j: (0, j))
    return chain.call(
        functools.partial(hidden_back_body, n),
        (width // tile,),
        [whole(grads.shape)] + down.tiles(tile) + [out] * 2,
        [out] * 2,
        [((rows, width), BF16)] * 2,
        flops=2 * rows * model * width,
        moved=2 * (rows * model + model * width + 4 * rows * width),
    )(grads, *down.pieces, slope, silu)


def mixed_back_body(n, counts, *refs):
    m = sum(counts)
    out_ref, x_ref, sems = refs[m + n :]

    @pl.when(pl.program_id(0) == 0)
    def _():
        collect(counts, refs, x_ref, sems)

    out_ref[...] = nn(x_ref[...], joined(refs[m : m + n])).astype(BF16)


def mixed_back(chain, held, out):
    counts, arrays, specs, scratch = collected(held)
    rows, model = scratch[0].shape
    n, width = len(out.pieces), out.width
    tile = min(256, width)
    return chain.call(
        functools.partial(mixed_back_body, n, counts),
        (width // tile,),
        specs + out.tiles(tile),
        [pl.BlockSpec((rows, tile), lambda j: (0, j))],
        [((rows, width), BF16)],
        flops=2 * rows * model * width,
        scratch=scratch,
        moved=2 * (rows * model + model * width + rows * width),
    )(*arrays, *out.pieces)[0]


def trans_body(n, starts, targets, *refs):
    parts, blocks = len(starts), len(targets[0])
    lefts = refs[:parts]
    pieces = refs[parts : parts * (n + 1)]
    outs = refs[parts * (n + 1) : -4]
    held, ready, sems, out_sems = refs[-4:]
    j = pl.program_id(0)
    depth, width = held.shape[2:]
    rows = ready.shape[1] // blocks

    def copy(i, p, slot):
        source = pieces[p * n + i].at[pl.ds(0, depth), pl.ds(starts[p], width)]
        return pltpu.make_async_copy(source, held.at[slot, p], sems.at[slot, p])

    def fetch(step, slot):
        for i in range(n):

            @pl.when(step == i)
            def _():
                for p in range(parts):
                    copy(i, p, slot).start()

    def leave(slot, k, array, first, column):
        target = outs[array].at[pl.ds(first, rows), pl.ds(column, depth)]
        source = ready.at[slot, pl.ds(k * rows, rows), :]
        return pltpu.make_async_copy(source, target, out_sems.at[slot, k])

    def left(slot):
        for k in range(blocks):
            leave(slot, k, 0, 0, 0).wait()

    @pl.when(j == 0)
    def _():
        fetch(j, 0)

    @pl.when(j + 1 < n)
    def _():
        fetch(j + 1, (j + 1) % 2)

    slot = j % 2
    for p in range(parts):
        copy(0, p, slot).wait()

    @pl.when(j >= 2)
    def _():
        left(slot)

    for s in range(blocks * rows // SEQ):
        span = slice(s * SEQ, (s + 1) * SEQ)
        total = nt(lefts[0][span, :], held[slot, 0])
        for p in range(1, parts):
            total += nt(lefts[p][span, :], held[slot, p])
        ready[slot, span, :] = total.astype(BF16)
    column = pl.multiple_of(j % (n // 2) * depth, 128)
    for h in range(2):

        @pl.when((j >= n // 2) == (h == 1))
        def _():
            for k, (array, first) in enumerate(targets[h]):
                leave(slot, k, array, first, column).start()

    @pl.when(j == n - 1)
    def _():
        left(1 - slot)
        left(slot)


def times_trans(chain, parts, group):
    weights = [weight for _, weight in parts]
    n, depth, width = len(weights[0].pieces), weights[0].rows, weights[0].width
    rows = parts[0][0].shape[0]
    half = weights[0].model // 2
    size = rows // group.size
    messages = group.messages()
    shapes = [((size, half), BF16)] * 2
    targets = [{0: (0, 0)}, {0: (1, 0)}]
    for h in range(2):
        for keys in messages[h]:
            for i, k in enumerate(keys):
                targets[h][k] = (len(shapes), i * size)
            shapes.append(((len(keys) * size, half), BF16))
    targets = [[t[k] for k in range(group.size)] for t in targets]
    anywhere = pl.BlockSpec(memory_space=pl.ANY)
    outs = chain.call(
        functools.partial(trans_body, n, [weight.start for weight in weights], targets),
        (n,),
        [whole((rows, width))] * len(parts) + [anywhere] * (n * len(parts)),
        [anywhere] * len(shapes),
        shapes,
        flops=4 * rows * half * width * len(parts),
        scratch=[
            pltpu.VMEM((2, len(parts), depth, width), BF16),
            pltpu.VMEM((2, rows, depth), BF16),
            pltpu.SemaphoreType.DMA((2, len(parts))),
            pltpu.SemaphoreType.DMA((2, group.size)),
        ],
        moved=2 * (2 * rows * half + len(parts) * (rows + 2 * half) * width),
    )(*[left for left, _ in parts], *[piece for weight in weights for piece in weight.pieces])
    m = group.bits
    return outs[:2], [outs[2 : 2 + m], outs[2 + m :]]


def grad_body(parts, got, blocks, steps, *refs):
    lefts, refs = refs[:blocks], refs[blocks:]
    rights, refs = refs[:parts], refs[parts:]
    got_ref = refs[0] if got else None
    outs, turned = refs[got:-1], refs[-1]
    j = pl.program_id(0)

    @pl.when(j == 0)
    def _():
        rows = turned.shape[1] // blocks
        for k in range(blocks):
            turned[:, cut(rows, k)] = lefts[k][...].T

    for i in range(parts):

        @pl.when((j >= i * steps) & (j < (i + 1) * steps))
        def _():
            total = nn(turned[...], rights[i][...])
            if got:
                total += got_ref[...].astype(F32)
            total = total.astype(BF16)
            first = 0
            for out_ref in outs:
                count = out_ref.shape[0]
                out_ref[...] = total[first : first + count]
                first += count


def weight_grads(chain, left, which, rights, got=None, bits=0):
    rows, width = rights[0].shape
    parts = len(rights)
    tile = min(512, width)
    steps = width // tile
    if isinstance(left, list):
        lefts = [block[0] if len(block) == 1 else block[which] for block in left]
        half = left[0][0].shape[1] // 2
        places = [which if len(block) == 1 else 0 for block in left]
    else:
        lefts, places, half = [left], [which], left.shape[1] // 2
    blocks = len(lefts)
    ins = [
        pl.BlockSpec((rows // blocks, half), functools.partial(lambda at, j: (0, at), at))
        for at in places
    ]
    for i in range(parts):
        ins.append(
            pl.BlockSpec(
                (rows, tile),
                functools.partial(
                    lambda first, j: (0, jnp.clip(j - first, 0, steps - 1)), i * steps
                ),
            )
        )
    column = lambda j: (0, j)
    more = [] if got is None else [got]
    sizes = [half >> bits]
    for p in range(bits):
        sizes += [sizes[0], ((1 << p) - 1) * sizes[0]] if p else [sizes[0]]
    return chain.call(
        functools.partial(grad_body, parts, len(more), blocks, steps),
        (parts * steps,),
        ins + [pl.BlockSpec((half, tile), column)] * len(more),
        [pl.BlockSpec((size, tile), column) for size in sizes],
        [((size, parts * width), BF16) for size in sizes],
        flops=2 * rows * half * width * parts,
        scratch=[pltpu.VMEM((half, rows), BF16)],
        moved=2 * (rows * half + parts * (rows + half) * width),
    )(*lefts, *rights, *more)


def causal(scores):
    past = scores.shape[0] - HALF_SEQ
    key = lax.broadcasted_iota(jnp.int32, (HALF_SEQ, HALF_SEQ), 0)
    query = lax.broadcasted_iota(jnp.int32, (HALF_SEQ, HALF_SEQ), 1)
    last = jnp.where(key <= query, scores[past:], -1e30)
    return last if past == 0 else jnp.concatenate([scores[:past], last], axis=0)


def head_of(h):
    return slice(h * HEAD_DIM, (h + 1) * HEAD_DIM)


def span_of(b):
    return slice(b * HALF_SEQ, (b + 1) * HALF_SEQ)


def in_place(shift_ref, ref, count):
    rows = SEQ // count
    spans = [pl.ds(pl.multiple_of((i ^ shift_ref[0]) * rows, rows), rows) for i in range(count)]
    return jnp.concatenate([ref[span, :] for span in spans], axis=0)


def put_back(shift_ref, ref, count, values):
    rows = SEQ // count
    for i in range(count):
        ref[pl.ds(pl.multiple_of((i ^ shift_ref[0]) * rows, rows), rows), :] = values[cut(rows, i)]


def one_head(values, h):
    lane = lax.broadcasted_iota(jnp.int32, values.shape, 1)
    return jnp.where(lane // HEAD_DIM == h, values, jnp.zeros_like(values))


def attend_body(count, shift_ref, q_ref, k_ref, v_ref, out_ref, sum_ref):
    queries, keys = in_place(shift_ref, q_ref, count), in_place(shift_ref, k_ref, count)
    values = in_place(shift_ref, v_ref, count).astype(F32).T.astype(BF16)
    heads = []
    for h in range(q_ref.shape[1] // HEAD_DIM):
        blocks = []
        for b in range(2):
            reach = (b + 1) * HALF_SEQ
            query = one_head(queries[span_of(b)] * BF16(FACTOR), h)
            scores = causal(nt(keys[:reach], query))
            top = jnp.max(scores, axis=0, keepdims=True)
            expo = jnp.exp(scores - top)
            total = jnp.sum(expo, axis=0, keepdims=True)
            mixed = nn(values[head_of(h), :reach], expo.astype(BF16))
            blocks.append(mixed * (1.0 / total))
            sum_ref[0, 0, h : h + 1, span_of(b)] = top + jnp.log(total)
        heads.append(jnp.concatenate(blocks, axis=1))
    put_back(shift_ref, out_ref, count, jnp.concatenate(heads, axis=0).T.astype(BF16))


def attention_specs(rows, width):
    wide = min(256, width)
    tile = pl.BlockSpec((SEQ, wide), lambda s, p, _: (s, p))
    sums = pl.BlockSpec((1, 1, wide // HEAD_DIM, SEQ), lambda s, p, _: (s, p, 0, 0))
    grid = (rows // SEQ, width // wide)
    return grid, tile, sums, (*grid, wide // HEAD_DIM, SEQ)


def attend(chain, shift, count, query, key, value):
    rows, width = query.shape
    grid, tile, sums, shape = attention_specs(rows, width)
    return chain.call(
        functools.partial(attend_body, count),
        grid,
        [tile] * 3,
        [tile, sums],
        [((rows, width), BF16), (shape, F32)],
        flops=16 * rows * width * SEQ,
        prefetch=1,
        moved=8 * rows * width,
    )(shift, query, key, value)


def attend_back_body(
    count, shift_ref, q_ref, k_ref, v_ref, g_ref, sum_ref, cos_ref, sin_ref, dq_ref, dk_ref, dv_ref
):
    queries, keys, values, grads = (
        in_place(shift_ref, ref, count) for ref in (q_ref, k_ref, v_ref, g_ref)
    )
    turned = keys.astype(F32).T.astype(BF16)
    dq_heads = []
    dk, dv = [], []
    for b in range(2):
        reach = (b + 1) * HALF_SEQ
        dq, dk_sum, dv_sum = [], None, None
        for h in range(q_ref.shape[1] // HEAD_DIM):
            query = one_head(queries[span_of(b)], h)
            grad = one_head(grads[span_of(b)], h)
            scores = causal(nt(keys[:reach], query * BF16(FACTOR)))
            probs = jnp.exp(scores - sum_ref[0, 0, h : h + 1, span_of(b)])
            probs_grad = nt(values[:reach], grad)
            inner = jnp.sum(probs * probs_grad, axis=0, keepdims=True)
            score_grad = (probs * (probs_grad - inner)).astype(BF16)
            dv_part, dk_part = nn(probs.astype(BF16), grad), nn(score_grad, query)
            dv_sum = dv_part if dv_sum is None else dv_sum + dv_part
            dk_sum = dk_part if dk_sum is None else dk_sum + dk_part
            dq.append(nn(turned[head_of(h), :reach], score_grad))
        dq_heads.append(jnp.concatenate(dq, axis=0))
        dk.append(dk_sum)
        dv.append(dv_sum)

    def whole_rows(parts):
        early, late = parts
        return jnp.concatenate([late[:HALF_SEQ] + early, late[HALF_SEQ:]], axis=0)

    dq = jnp.concatenate(dq_heads, axis=1).T * FACTOR
    dk = whole_rows(dk) * FACTOR
    dv = whole_rows(dv).astype(BF16)
    copies = dq.shape[1] // PAIR
    cosine = jnp.concatenate([cos_ref[...]] * copies, axis=1)
    sine = jnp.concatenate([sin_ref[...]] * copies, axis=1)
    put_back(shift_ref, dq_ref, count, (dq * cosine - turn(dq) * sine).astype(BF16))
    put_back(shift_ref, dk_ref, count, (dk * cosine - turn(dk) * sine).astype(BF16))
    put_back(shift_ref, dv_ref, count, dv)


def attend_back(chain, shift, count, query, key, value, grad, logsum, tables):
    rows, width = query.shape
    grid, tile, sums, _ = attention_specs(rows, width)
    return chain.call(
        functools.partial(attend_back_body, count),
        grid,
        [tile] * 4 + [sums] + [whole((SEQ, PAIR))] * 2,
        [tile] * 3,
        [((rows, width), BF16)] * 3,
        flops=40 * rows * width * SEQ,
        prefetch=1,
        moved=14 * rows * width,
    )(shift, query, key, value, grad, logsum, *tables)


def local(
    chips,
    group,
    tokens,
    attn_gain,
    query_weight,
    key_weight,
    value_weight,
    output_weight,
    ffn_gain,
    gate_weight,
    up_weight,
    down_weight,
    cotangent,
):
    line = jnp.asarray(chips.table)[lax.axis_index("dp")]
    rows, model = tokens.shape
    count = SEQ // rows
    shift = lax.axis_index("tensor") % count
    row = jnp.arange(SEQ, dtype=jnp.int32)
    places = rope_tables(row)
    tables = rope_tables((row // rows ^ shift) * rows + row % rows)
    shift = jnp.reshape(shift, (1,)).astype(jnp.int32)
    early = (*places, *tables, line, shift)
    depth, own = query_weight.shape
    hidden_units = gate_weight.shape[1]
    chain = Chain()

    def gather(piece):
        return Gather(chips, chain, chain.join(piece)[0])

    def spread_of(values):
        return Spread(group, chain, chain.join(values)[0])

    def fold_of(part):
        own_part, sent = part
        sent = chain.join(*sent[0], *sent[1])
        return Fold(group, chain, own_part, [sent[: group.bits], sent[group.bits :]])

    def grads_of(left, rights):
        got = [None]
        chain.ask(weight_grads(chain, left, 1, rights)[0], got, 0, chips.other)

        def mine(**how):
            if got[0] is None:
                chain.flush()
            blocks = weight_grads(chain, left, 0, rights, got[0], chips.bits)
            return Sums(chips, chain, blocks, **how)

        return mine

    extra = jnp.concatenate([attn_gain, ffn_gain, jnp.zeros((4 * own - 2 * depth,), BF16)])
    attn = jnp.concatenate([query_weight, key_weight, value_weight, output_weight.T], axis=1)
    attn = gather(jnp.concatenate([attn, jnp.broadcast_to(extra, (16, 4 * own))], axis=0))
    spread = spread_of(tokens)
    grads_spread = spread_of(cotangent)
    grads_spread.later = []
    down_turned, *early = chain.join(down_weight.T, *early)
    places, tables, line, shift = early[:2], early[2:4], early[4], early[5]
    chain.end(attn, spread, grads_spread)
    chain.end(attn, spread)
    all_tokens = spread.blocks()
    attn = attn.pieces()
    pair = gather(jnp.concatenate([gate_weight, up_weight], axis=1))
    w_query, w_key, w_value, w_output = [Weight(attn, depth, i * own, own) for i in range(4)]
    gains = jnp.concatenate(
        [piece[depth : depth + 1, : 2 * depth].reshape(2, depth) for piece in attn], axis=1
    ).astype(F32)

    group_one = ordered(chain, norm_body, line, gains, all_tokens)
    grads_spread.resume()
    query, key, value = project(chain, group_one, tables, w_query, w_key, w_value)
    mixed, logsum = attend(chain, shift, count, query, key, value)
    out_part = times_trans(chain, [(mixed, w_output)], group)
    fold = fold_of(out_part)
    chain.end(fold, pair, grads_spread)
    grad_rows = ordered(chain, order_body, line, gains, grads_spread.blocks())
    chain.end(fold)
    attended = fold.total()
    middle, second = by_rows(
        chain, middle_body, line, tokens, gains, attended, [], [F32, BF16]
    )
    spread = spread_of(second)
    chain.end(spread, pair)
    pair = pair.pieces()
    down = gather(down_turned)
    chain.end(spread)
    group_two = spread.blocks()
    w_gate = Weight(pair, depth, 0, hidden_units)
    w_up = Weight(pair, depth, hidden_units, hidden_units)
    hidden, slope, silu = gate_up(chain, group_two, w_gate, w_up)

    mine = grads_of(grad_rows, [hidden])
    chain.end(down)
    chain.flush()
    down_sum = mine()
    w_down = Weight(down.pieces(), depth, 0, hidden_units)
    gate_grad, up_grad = hidden_back(chain, grad_rows, w_down, slope, silu)
    mine_gate = grads_of(group_two, [gate_grad])
    chain.end(down_sum)
    second_part = times_trans(chain, [(gate_grad, w_gate), (up_grad, w_up)], group)
    mine_up = grads_of(group_two, [up_grad])
    gate_sum = mine_gate(hold=True)
    chain.end(down_sum)
    fold = fold_of(second_part)
    up_sum = mine_up(apart=True)
    chain.end(gate_sum, fold)
    result_part = times_trans(chain, [(hidden, w_down)], group)
    chain.end(fold)
    second_grad = fold.total()
    middle_grad, low_grad = by_rows(
        chain, second_back_body, line, cotangent, gains, second_grad, [middle], [F32, BF16]
    )
    spread = spread_of(low_grad)
    chain.end(up_sum)
    gate_sum.resume()
    (down_sum,) = finish(chain, down_sum.terms())
    chain.end(spread)
    attn_grads = spread.blocks()

    mixed_grad = mixed_back(chain, attn_grads, w_output)
    mine_out = grads_of(attn_grads, [mixed])
    chain.end(gate_sum)
    up_sum.send_half(0)
    fold = fold_of(result_part)
    query_back, key_back, value_back = attend_back(
        chain, shift, count, query, key, value, mixed_grad, logsum, places
    )
    mine_qkv = grads_of(group_one, [query_back, key_back, value_back])
    out_sum = mine_out(hold=True)
    chain.end(up_sum, fold)
    up_sum.send_half(1)
    qkv_sum = mine_qkv(cut_in_two=True)
    chain.end(fold, out_sum)
    result_part = fold.total()
    first_part = times_trans(
        chain, [(query_back, w_query), (key_back, w_key), (value_back, w_value)], group
    )
    chain.end(up_sum, qkv_sum)
    fold = fold_of(first_part)
    out_sum.resume()
    up_sum, up_inner = finish(chain, up_sum.terms(), [up_weight])
    gate_sum, gate_inner = finish(chain, gate_sum.terms(), [gate_weight])
    (layer_out,) = by_rows(chain, result_body, line, middle, gains, result_part, [], [BF16])
    chain.end(fold)
    chain.end(fold)
    chain.end(qkv_sum)
    query_sum, key_sum, value_sum, qkv_inner = finish(
        chain, qkv_sum.terms(), [query_weight, key_weight, value_weight]
    )
    gain_parts = jnp.stack(
        [qkv_inner / attn_gain.astype(F32), (gate_inner + up_inner) / ffn_gain.astype(F32)]
    )
    (gain_parts,) = chain.join(gain_parts)
    first_grad = fold.total()
    (input_grad,) = by_rows(
        chain, first_back_body, line, tokens, gains, first_grad, [middle_grad], [F32]
    )
    (out_sum,) = finish(chain, out_sum.terms())
    gain_totals = gain_parts
    for k in range(1, group.size):
        pairs = [(i, i ^ k) for i in range(group.size)]
        gain_totals += lax.ppermute(gain_parts, "tensor", pairs)
    gain_one_total, gain_two_total = gain_totals[0], gain_totals[1]
    return (
        layer_out,
        input_grad,
        gain_one_total,
        query_sum,
        key_sum,
        value_sum,
        out_sum,
        gain_two_total,
        gate_sum,
        up_sum,
        down_sum,
    )


def solution(mesh):
    in_specs = (
        P(("dp", "tensor"), None),
        P("dp"),
        P("dp", "tensor"),
        P("dp", "tensor"),
        P("dp", "tensor"),
        P("tensor", "dp"),
        P("dp"),
        P("dp", "tensor"),
        P("dp", "tensor"),
        P("tensor", "dp"),
        P(("dp", "tensor"), None),
    )
    out_specs = (
        P(("dp", "tensor"), None),
        P(("dp", "tensor"), None),
        P("dp"),
        P("dp", "tensor"),
        P("dp", "tensor"),
        P("dp", "tensor"),
        P("tensor", "dp"),
        P("dp"),
        P("dp", "tensor"),
        P("dp", "tensor"),
        P("tensor", "dp"),
    )
    chips = Chips(mesh.shape["dp"])
    size = mesh.shape["tensor"]
    links = [[(i, i ^ 1 << b) for i in range(size)] for b in range(size.bit_length() - 1)]
    group = Group(links, "tensor")

    def run(*arrays):
        return local(chips, group, *arrays)

    return jax.shard_map(run, mesh=mesh, in_specs=in_specs, out_specs=out_specs, check_vma=False)
```

```python
import functools

import jax
import jax.numpy as jnp
import numpy as np
from jax import lax
from jax.experimental import pallas as pl
from jax.experimental.pallas import tpu as pltpu
from jax.sharding import PartitionSpec as P

HEAD_DIM = 64
SEQ = 512
EPS = 1e-05
THETA = 130000.0
BF16 = jnp.bfloat16
F32 = jnp.float32
FACTOR = HEAD_DIM**-0.5
PAIR = 2 * HEAD_DIM
HALF_SEQ = SEQ // 2
VMEM_LIMIT = 58 << 20
COST_SHARE = 4096


class Chain:
    def __init__(self):
        self.token = jnp.zeros((8, 128), F32)
        self.swaps, self.asked = [], []

    def join(self, *values):
        *values, self.token = lax.optimization_barrier((*values, self.token))
        return values

    def gate(self, *values):
        swaps, self.swaps = self.swaps, []
        asked, self.asked = self.asked, []
        joined = self.join(
            *values, *[held[i] for held, i in swaps], *[source for source, _, _, _ in asked]
        )
        for (held, i), value in zip(swaps, joined[len(values) :]):
            held[i] = value
        for (_, held, i, swap), value in zip(asked, joined[len(values) + len(swaps) :]):
            held[i] = swap(value)
            self.swaps.append((held, i))
        return joined[: len(values)]

    def end(self, *transfers):
        counts = [len(t.flying) for t in transfers]
        got = self.gate(*[value for t in transfers for value in t.flying])
        for t, count in zip(transfers, counts):
            if count:
                t.go_on(got[:count])
            got = got[count:]

    def ask(self, source, held, i, swap):
        self.asked.append((source, held, i, swap))

    def flush(self):
        for source, held, i, swap in self.asked:
            held[i] = swap(source)
        self.asked = []

    def call(self, body, grid, ins, outs, shapes, flops, scratch=(), prefetch=0, moved=0):
        first = prefetch + len(ins)
        second = first + 1 + len(outs)
        anywhere = pl.BlockSpec(memory_space=pl.ANY)

        def wrapped(*refs):
            body(*refs[:first], *refs[first + 1 : second], *refs[second + 1 :])

        run = pl.pallas_call(
            wrapped,
            grid_spec=pltpu.PrefetchScalarGridSpec(
                num_scalar_prefetch=prefetch,
                grid=grid,
                in_specs=[*ins, anywhere],
                out_specs=[*outs, anywhere],
                scratch_shapes=list(scratch),
            ),
            out_shape=[jax.ShapeDtypeStruct(s, t) for s, t in [*shapes, ((8, 128), F32)]],
            compiler_params=pltpu.CompilerParams(
                vmem_limit_bytes=VMEM_LIMIT, dimension_semantics=("arbitrary",) * len(grid)
            ),
            cost_estimate=pl.CostEstimate(
                flops=flops // COST_SHARE, bytes_accessed=moved // COST_SHARE, transcendentals=0
            ),
        )

        def with_token(*args):
            *results, self.token = run(*args, self.token)
            return results

        return with_token


class Chips:
    def __init__(self, size):
        self.bits = (size // 2).bit_length() - 1
        self.size = size
        self.swap = [(i, i ^ 1) for i in range(size)]
        self.links = [
            [(i, i ^ 2 << self.bits - 1 - p) for i in range(size)] for p in range(self.bits)
        ]
        flips = [
            sum(1 << self.bits - 1 - p for p in range(self.bits) if v >> p & 1)
            for v in range(1 << self.bits)
        ]
        table = [[i ^ 2 * f for f in flips] + [i ^ 2 * f ^ 1 for f in flips] for i in range(size)]
        self.table = np.array(table, np.int32)

    def send(self, value, p):
        return lax.ppermute(value, "dp", self.links[p])

    def other(self, value):
        return lax.ppermute(value, "dp", self.swap)


class Gather:
    def __init__(self, chips, chain, piece):
        self.chips, self.chain = chips, chain
        self.own = [piece] + [None] * (2**chips.bits - 1)
        self.others = list(self.own)
        self.ask(0)
        self.keys = [1 << p for p in range(chips.bits)]
        self.flying = [chips.send(piece, p) for p in range(chips.bits)]

    def ask(self, v):
        self.chain.ask(self.own[v], self.others, v, self.chips.other)

    def go_on(self, got):
        keys, self.keys, self.flying = self.keys, [], []
        for v, piece in zip(keys, got):
            self.own[v] = piece
            for p in range(v.bit_length(), self.chips.bits):
                self.keys.append(v | 1 << p)
                self.flying.append(self.chips.send(piece, p))
        for v in keys:
            self.ask(v)

    def pieces(self):
        while self.flying:
            self.chain.end(self)
        self.chain.flush()
        return self.own + self.others


class Sums:
    def __init__(self, chips, chain, mine, apart=False, hold=False, cut_in_two=False):
        self.chips, self.chain, self.apart, self.hold = chips, chain, apart, hold
        self.todo = []
        self.cut_in_two = cut_in_two and chips.bits == 2
        self.parts = [mine[0]]
        mine = list(mine[1:])
        self.direct, self.passed = [], []
        for p in range(chips.bits):
            self.direct.append(mine.pop(0))
            self.passed.append(mine.pop(0) if p else None)
        self.p = chips.bits - 1
        if self.cut_in_two:
            self.kinds = [0, 1]
            self.flying = [chips.send(half, 1) for half in self.in_two(self.passed[1])]
            return
        self.kinds = [self.p]
        self.flying = [chips.send(self.passed[self.p], self.p)]

    def in_two(self, values):
        width = values.shape[1] // 2
        return values[:, :width], values[:, width:]

    def go_on(self, got):
        rows = self.parts[0].shape[0]
        kinds, self.kinds, self.flying = self.kinds, [], []
        if self.p == 0:
            self.parts += got
            return
        if self.cut_in_two:
            self.p = 0
            total = self.direct[0].astype(F32) + jnp.concatenate(got, axis=1).astype(F32)
            self.todo = [(None, self.direct[1], 1), (None, total.astype(BF16), 0)]
            self.resume()
            return
        for kind, block in zip(kinds, got):
            if kind is None:
                self.parts.append(block)
                continue
            add = lambda held, first: (
                held.astype(F32) + block[first * rows : first * rows + held.shape[0]].astype(F32)
            ).astype(BF16)
            for q in range(kind):
                self.direct[q] = add(self.direct[q], (1 << q) - 1)
                if q:
                    self.passed[q] = add(self.passed[q], 1 << q)
        p, self.p = self.p, self.p - 1
        if p > 0:
            self.todo.append((None, self.direct[p], p))
        if p > 1:
            self.todo.append((p - 1, self.passed[p - 1], p - 1))
        if p == 1 and not self.apart:
            self.todo.append((None, self.direct[0], 0))
        if not self.hold:
            self.resume()

    def resume(self):
        todo, self.todo = self.todo, []
        values = self.chain.join(*[value for _, value, _ in todo])
        for (kind, _, p), value in zip(todo, values):
            self.kinds.append(kind)
            self.flying.append(self.chips.send(value, p))

    def send_half(self, i):
        while self.p > 0:
            self.chain.end(self)
        width = self.direct[0].shape[1] // 2
        (value,) = self.chain.join(self.direct[0][:, i * width : (i + 1) * width])
        self.kinds.append(None)
        self.flying.append(self.chips.send(value, 0))

    def terms(self):
        while self.flying or self.todo:
            if self.todo:
                self.resume()
            self.chain.end(self)
        return sorted(self.parts, key=lambda part: -part.shape[1])


class Group:
    def __init__(self, links, axes):
        self.links, self.axes = links, axes
        self.bits = len(links)
        self.size = 1 << self.bits
        self.orders = (list(range(self.bits)), list(range(self.bits))[::-1])

    def send(self, value, bit):
        return lax.ppermute(value, self.axes, self.links[bit])

    def messages(self):
        found = []
        for order in self.orders:
            found.append([])
            for top in reversed(range(self.bits)):
                found[-1].append(
                    [
                        1 << order[top] | sum(1 << order[p] for p in range(top) if v >> p & 1)
                        for v in range(1 << top)
                    ]
                )
        return found


class Spread:
    def __init__(self, group, chain, rows):
        self.group, self.chain = group, chain
        self.held = {0: [rows]}
        self.later = None
        self.keys = [(1 << b, None) for b in range(group.bits)]
        self.flying = [group.send(rows, b) for b in range(group.bits)]

    def go_on(self, got):
        fresh = list(zip(self.keys, got))
        self.keys, self.flying = [], []
        for (k, h), block in fresh:
            if h is None:
                self.held[k] = [block]
            else:
                self.held.setdefault(k, [None, None])[h] = block
        for (k, h), block in fresh:
            for way, order in enumerate(self.group.orders):
                if h is not None and h != way:
                    continue
                half = block.shape[1] // 2
                top = max(i for i, bit in enumerate(order) if k >> bit & 1)
                for i in range(top + 1, len(order)):
                    part = block if h is not None else block[:, way * half : (way + 1) * half]
                    self.keys.append((k | 1 << order[i], way))
                    if self.later is not None:
                        self.later.append((part, order[i]))
                    else:
                        self.flying.append(self.group.send(part, order[i]))

        if self.later:
            parts = self.chain.join(*[part for part, _ in self.later])
            self.later = [(part, bit) for part, (_, bit) in zip(parts, self.later)]

    def resume(self):
        later, self.later = self.later, None
        parts = self.chain.join(*[part for part, _ in later])
        self.flying = [self.group.send(part, bit) for part, (_, bit) in zip(parts, later)]

    def blocks(self):
        while self.flying:
            self.chain.end(self)
        return [self.held[k] for k in range(self.group.size)]


class Fold:
    def __init__(self, group, chain, own, sent):
        self.group, self.chain = group, chain
        self.rows = own[0].shape[0]
        self.sent = [list(half) for half in sent]
        self.parts = [[half] for half in own]
        self.wave = 0
        self.start()

    def start(self):
        self.flying = [
            self.group.send(self.sent[h][self.wave], order[self.group.bits - 1 - self.wave])
            for h, order in enumerate(self.group.orders)
        ]

    def go_on(self, got):
        self.wave += 1
        self.flying = []
        for h, block in enumerate(got):
            self.parts[h].append(block)
        for wave in range(self.wave, self.group.bits):
            sums = add_rows(self.chain, [sent[wave] for sent in self.sent], got)
            for sent, value in zip(self.sent, sums):
                sent[wave] = value
        if self.wave < self.group.bits:
            self.start()

    def total(self):
        while self.flying:
            self.chain.end(self)
        return self.parts


class Weight:
    def __init__(self, pieces, rows, start, width):
        self.pieces, self.rows, self.start, self.width = pieces, rows, start, width
        self.model = len(pieces) * rows

    def tiles(self, tile):
        first = self.start // tile
        return [pl.BlockSpec((self.rows, tile), lambda j: (0, first + j))] * len(self.pieces)


def nn(left, right):
    return lax.dot_general(left, right, (((1,), (0,)), ((), ())), preferred_element_type=F32)


def nt(left, right):
    return lax.dot_general(left, right, (((1,), (1,)), ((), ())), preferred_element_type=F32)


def tn(left, right):
    return lax.dot_general(left, right, (((0,), (0,)), ((), ())), preferred_element_type=F32)


def whole(shape):
    return pl.BlockSpec(shape, lambda *_: (0,) * len(shape))


def place(line_ref, j, width):
    return pl.ds(pl.multiple_of(line_ref[j] * width, 128), width)


def cut(width, j):
    return slice(j * width, (j + 1) * width)


def scale_of(values):
    return lax.rsqrt(jnp.mean(values * values, axis=-1, keepdims=True) + EPS)


def fetch_blocks(counts, refs, held, sems, k, slot, wait):
    first = 0
    for i, count in enumerate(counts):
        copies = []
        half = held.shape[2] // count
        for h in range(count):
            target = held.at[slot, :, pl.ds(h * half, half)]
            copies.append(pltpu.make_async_copy(refs[first + h], target, sems.at[slot, h]))
        first += count

        @pl.when(k == i)
        def _():
            for copy in copies:
                copy.wait() if wait else copy.start()


def fetched(counts, refs, held, sems):
    k = pl.program_id(0)

    @pl.when(k == 0)
    def _():
        fetch_blocks(counts, refs, held, sems, k, 0, False)

    fetch_blocks(counts, refs, held, sems, k + 1, (k + 1) % 2, False)
    fetch_blocks(counts, refs, held, sems, k, k % 2, True)
    return held.at[k % 2]


def norm_body(blocks, counts, line_ref, gain_ref, *refs):
    out_ref, held, sems = refs[sum(counts) :]
    x_ref = fetched(counts, refs, held, sems)
    width = out_ref.shape[1] // blocks
    scale = scale_of(x_ref[...].astype(F32))
    for j in range(blocks):
        part = x_ref[:, place(line_ref, j, width)].astype(F32)
        gain = gain_ref[0:1, cut(width, j)]
        out_ref[:, cut(width, j)] = (part * scale * gain).astype(BF16)


def order_body(blocks, counts, line_ref, gain_ref, *refs):
    out_ref, held, sems = refs[sum(counts) :]
    x_ref = fetched(counts, refs, held, sems)
    width = out_ref.shape[1] // blocks
    for j in range(blocks):
        out_ref[:, cut(width, j)] = x_ref[:, place(line_ref, j, width)]


def ordered(chain, body, line, gains, held):
    counts = [len(block) for block in held]
    rows, model = held[0][0].shape
    n = len(held)
    return chain.call(
        functools.partial(body, line.shape[0], counts),
        (n,),
        [whole(gains.shape)] + [pl.BlockSpec(memory_space=pl.ANY)] * sum(counts),
        [pl.BlockSpec((rows, model), lambda k, *_: (k, 0))],
        [((n * rows, model), BF16)],
        flops=20 * n * rows * model,
        scratch=[pltpu.VMEM((2, rows, model), BF16), pltpu.SemaphoreType.DMA((2, 2))],
        prefetch=1,
        moved=4 * n * rows * model,
    )(line, gains, *[array for block in held for array in block])[0]


def added(refs, span):
    total = refs[0][span, :].astype(F32)
    for ref in refs[1:]:
        total += ref[span, :].astype(F32)
    return total


def middle_body(blocks, m, line_ref, x_ref, gain_ref, *refs):
    middle_ref, out_ref = refs[2 * m :]
    width = x_ref.shape[1] // blocks
    half = x_ref.shape[1] // 2
    span = slice(None)
    middle_ref[:, :half] = added(refs[:m], span)
    middle_ref[:, half:] = added(refs[m : 2 * m], span)
    for j in range(blocks):
        here = x_ref[:, place(line_ref, j, width)].astype(F32)
        middle_ref[:, cut(width, j)] += here
    middle = middle_ref[...]
    out_ref[...] = (middle * scale_of(middle) * gain_ref[1:2, :]).astype(BF16)


def result_body(blocks, m, line_ref, middle_ref, gain_ref, *refs):
    out_ref = refs[2 * m]
    width = middle_ref.shape[1] // blocks
    span = slice(None)
    total = middle_ref[...] + jnp.concatenate(
        [added(refs[:m], span), added(refs[m : 2 * m], span)], axis=1
    )
    for j in range(blocks):
        out_ref[:, place(line_ref, j, width)] = total[:, cut(width, j)].astype(BF16)


def second_back_body(blocks, m, line_ref, dy_ref, gain_ref, *refs):
    middle_ref, out_ref, low_ref = refs[2 * m :]
    width = dy_ref.shape[1] // blocks
    span = slice(None)
    grad = jnp.concatenate([added(refs[:m], span), added(refs[m : 2 * m], span)], axis=1)
    middle = middle_ref[...]
    scale = scale_of(middle)
    normed = middle * scale
    scaled = grad * gain_ref[1:2, :]
    out_ref[...] = scale * (scaled - normed * jnp.mean(scaled * normed, axis=-1, keepdims=True))
    for j in range(blocks):
        out_ref[:, cut(width, j)] += dy_ref[:, place(line_ref, j, width)].astype(F32)
    low_ref[...] = out_ref[...].astype(BF16)


def first_back_body(blocks, m, line_ref, x_ref, gain_ref, *refs):
    above_ref, out_ref = refs[2 * m :]
    width = x_ref.shape[1] // blocks
    span = slice(None)
    scale = scale_of(x_ref[...].astype(F32))
    normed = jnp.concatenate(
        [x_ref[:, place(line_ref, j, width)].astype(F32) for j in range(blocks)], axis=1
    ) * scale
    grad = jnp.concatenate([added(refs[:m], span), added(refs[m : 2 * m], span)], axis=1)
    scaled = grad * gain_ref[0:1, :]
    back = scale * (scaled - normed * jnp.mean(scaled * normed, axis=-1, keepdims=True))
    total = above_ref[...] + back
    for j in range(blocks):
        out_ref[:, place(line_ref, j, width)] = total[:, cut(width, j)]


def by_rows(chain, body, line, first, gains, parts, more, kinds):
    rows, model = first.shape
    half = model // 2
    tile = min(128, rows)
    row = pl.BlockSpec((tile, model), lambda i, *_: (i, 0))
    slim = pl.BlockSpec((tile, half), lambda i, *_: (i, 0))
    m = len(parts[0])
    return chain.call(
        functools.partial(body, line.shape[0], m),
        (rows // tile,),
        [row, whole(gains.shape)] + [slim] * (2 * m) + [row] * len(more),
        [row] * len(kinds),
        [((rows, model), kind) for kind in kinds],
        flops=20 * rows * model,
        prefetch=1,
        moved=rows * model * (2 * m + 4 * len(kinds)),
    )(line, first, gains, *parts[0], *parts[1], *more)


def add_rows_body(count, *refs):
    for i in range(count):
        total = refs[i][...].astype(F32) + refs[count + i][...].astype(F32)
        refs[2 * count + i][...] = total.astype(BF16)


def add_rows(chain, helds, blocks):
    rows, columns = helds[0].shape
    tile = min(128, rows)
    steps = rows // tile
    count = len(helds)
    here = pl.BlockSpec((tile, columns), lambda i: (i, 0))
    return chain.call(
        functools.partial(add_rows_body, count),
        (steps,),
        [here] * count + [pl.BlockSpec((tile, columns), lambda i: (steps + i, 0))] * count,
        [here] * count,
        [((rows, columns), BF16)] * count,
        flops=count * rows * columns,
        moved=6 * count * rows * columns,
    )(*helds, *blocks)


def finish_body(m, halves, n, *refs):
    total = added(refs[:m], slice(None))
    if halves:
        total += jnp.concatenate([ref[...].astype(F32) for ref in refs[m : m + halves]], axis=1)
    m += halves
    weights, outs = refs[m : m + n], refs[m + n :]
    if not n:
        outs[0][...] = total.T
        return
    width = weights[0].shape[1]
    inner = jnp.zeros((total.shape[0], 1), F32)
    for i in range(n):
        part = total[:, cut(width, i)]
        outs[i][...] = part
        inner += jnp.sum(weights[i][...].astype(F32) * part, axis=1, keepdims=True)
    outs[n][...] = jnp.broadcast_to(inner, outs[n].shape)


def finish(chain, terms, weights=()):
    rows, columns = terms[0].shape
    tile = min(128, rows)
    row = pl.BlockSpec((tile, columns), lambda i: (i, 0))
    n = len(weights)
    halves = sum(1 for term in terms if term.shape[1] < columns)
    half = [pl.BlockSpec((tile, columns // 2), lambda i: (i, 0))] * halves
    if n:
        slim = pl.BlockSpec((tile, columns // n), lambda i: (i, 0))
        outs = [slim] * n + [pl.BlockSpec((tile, 128), lambda i: (i, 0))]
        shapes = [((rows, columns // n), F32)] * n + [((rows, 128), F32)]
    else:
        slim = None
        outs = [pl.BlockSpec((columns, tile), lambda i: (0, i))]
        shapes = [((columns, rows), F32)]
    results = chain.call(
        functools.partial(finish_body, len(terms) - halves, halves, n),
        (rows // tile,),
        [row] * (len(terms) - halves) + half + [slim] * n,
        outs,
        shapes,
        flops=4 * rows * columns,
        moved=rows * columns * 12,
    )(*terms, *weights)
    if n:
        results[n] = results[n][:, 0]
    return results


def rope_tables(place):
    half = HEAD_DIM // 2
    freq = THETA ** (-2.0 * jnp.arange(half, dtype=F32) / HEAD_DIM)
    angle = place.astype(F32)[:, None] * freq[None, :]
    cosine, sine = jnp.cos(angle), jnp.sin(angle)
    return (
        jnp.concatenate([cosine] * (PAIR // half), axis=1),
        jnp.concatenate([-sine, sine] * (PAIR // HEAD_DIM), axis=1),
    )


def turn(values):
    half = HEAD_DIM // 2
    width = values.shape[-1]
    lane = lax.broadcasted_iota(jnp.int32, values.shape, 1) % HEAD_DIM
    return jnp.where(
        lane < half, pltpu.roll(values, width - half, 1), pltpu.roll(values, half, 1)
    )


def joined(refs):
    return jnp.concatenate([r[...] for r in refs], axis=0)


def qkv_body(n, x_ref, cos_ref, sin_ref, *refs):
    weights, outs = refs[: 3 * n], refs[3 * n :]
    rows = x_ref.shape[0]
    tile = outs[0].shape[1]
    for i in range(3):
        weight = joined(weights[i * n : (i + 1) * n])
        for s in range(rows // SEQ):
            span = slice(s * SEQ, (s + 1) * SEQ)
            product = nn(x_ref[span, :], weight)
            if i == 2:
                outs[i][span, :] = product.astype(BF16)
                continue
            for t in range(tile // PAIR):
                here = product[:, t * PAIR : (t + 1) * PAIR]
                turned = here * cos_ref[...] + turn(here) * sin_ref[...]
                outs[i][span, t * PAIR : (t + 1) * PAIR] = turned.astype(BF16)


def project(chain, x, tables, query, key, value):
    rows, model = x.shape
    n, width = len(query.pieces), query.width
    tile = min(256, width)
    out = pl.BlockSpec((rows, tile), lambda j: (0, j))
    return chain.call(
        functools.partial(qkv_body, n),
        (width // tile,),
        [whole(x.shape), whole((SEQ, PAIR)), whole((SEQ, PAIR))]
        + query.tiles(tile)
        + key.tiles(tile)
        + value.tiles(tile),
        [out] * 3,
        [((rows, width), BF16)] * 3,
        flops=6 * rows * model * width,
        moved=2 * (rows * model + 3 * model * width + 3 * rows * width),
    )(x, *tables, *query.pieces, *key.pieces, *value.pieces)


def collect(counts, refs, held, sems):
    rows = held.shape[0] // len(counts)
    copies = []
    for k, count in enumerate(counts):
        half = held.shape[1] // count
        for h in range(count):
            target = held.at[pl.ds(k * rows, rows), pl.ds(h * half, half)]
            i = len(copies)
            copies.append(pltpu.make_async_copy(refs[i], target, sems.at[i]))
    for copy in copies:
        copy.start()
    for copy in copies:
        copy.wait()


def gate_body(n, counts, *refs):
    m = sum(counts)
    gate_w, up_w = refs[m : m + n], refs[m + n : m + 2 * n]
    left_ref, hidden_ref, slope_ref, silu_ref, theirs_ref, x_ref, turned, sems = refs[m + 2 * n :]

    @pl.when(pl.program_id(0) == 0)
    def _():
        collect(counts, refs, x_ref, sems)
        turned[...] = left_ref[...].T

    gate_weight, up_weight = joined(gate_w), joined(up_w)
    for s in range(x_ref.shape[0] // SEQ):
        span = slice(s * SEQ, (s + 1) * SEQ)
        gate = nn(x_ref[span, :], gate_weight)
        up = nn(x_ref[span, :], up_weight)
        sigm = jax.nn.sigmoid(gate)
        silu = gate * sigm
        hidden_ref[span, :] = (silu * up).astype(BF16)
        silu_ref[span, :] = silu.astype(BF16)
        slope_ref[span, :] = (up * sigm * (1.0 + gate * (1.0 - sigm))).astype(BF16)
    theirs_ref[...] = nn(turned[...], hidden_ref[...]).astype(BF16)


def collected(held):
    counts = [len(block) for block in held]
    rows, model = held[0][0].shape
    scratch = [
        pltpu.VMEM((len(held) * rows, model), BF16),
        pltpu.SemaphoreType.DMA((sum(counts),)),
    ]
    arrays = [array for block in held for array in block]
    return counts, arrays, [pl.BlockSpec(memory_space=pl.ANY)] * len(arrays), scratch


def gate_up(chain, held, gate, up, grads):
    counts, arrays, specs, scratch = collected(held)
    rows, model = scratch[0].shape
    n, width = len(gate.pieces), gate.width
    tile = min(256, width)
    out = pl.BlockSpec((rows, tile), lambda j: (0, j))
    half = model // 2
    return chain.call(
        functools.partial(gate_body, n, counts),
        (width // tile,),
        specs
        + gate.tiles(tile)
        + up.tiles(tile)
        + [pl.BlockSpec((rows, half), lambda j: (0, 1))],
        [out] * 3 + [pl.BlockSpec((half, tile), lambda j: (0, j))],
        [((rows, width), BF16)] * 3 + [((half, width), BF16)],
        flops=6 * rows * model * width,
        scratch=[scratch[0], pltpu.VMEM((half, rows), BF16), scratch[1]],
        moved=2 * (rows * model + 2 * model * width + 3 * rows * width),
    )(*arrays, *gate.pieces, *up.pieces, grads)


def half_blocks(left, which):
    lefts = [block[0] if len(block) == 1 else block[which] for block in left]
    rows, half = lefts[0].shape[0], left[0][0].shape[1] // 2
    places = [which if len(block) == 1 else 0 for block in left]
    return lefts, [
        pl.BlockSpec((rows, half), functools.partial(lambda at, j: (0, at), at)) for at in places
    ]


def hidden_back_body(n, blocks, g_ref, *refs):
    weights, slope_ref, silu_ref = refs[:n], refs[n], refs[n + 1]
    lefts, refs = refs[n + 2 : n + 2 + blocks], refs[n + 2 + blocks :]
    gate_ref, up_ref, gate_theirs, up_theirs, turned = refs
    rows = turned.shape[1] // blocks

    @pl.when(pl.program_id(0) == 0)
    def _():
        for k in range(blocks):
            turned[:, cut(rows, k)] = lefts[k][...].T

    weight = joined(weights)
    for s in range(g_ref.shape[0] // SEQ):
        span = slice(s * SEQ, (s + 1) * SEQ)
        grad = nn(g_ref[span, :], weight)
        gate_ref[span, :] = (grad * slope_ref[span, :].astype(F32)).astype(BF16)
        up_ref[span, :] = (grad * silu_ref[span, :].astype(F32)).astype(BF16)
    gate_theirs[...] = nn(turned[...], gate_ref[...]).astype(BF16)
    up_theirs[...] = nn(turned[...], up_ref[...]).astype(BF16)


def hidden_back(chain, grads, down, slope, silu, left):
    rows, model = grads.shape
    n, width = len(down.pieces), down.width
    tile = min(256, width)
    out = pl.BlockSpec((rows, tile), lambda j: (0, j))
    lefts, specs = half_blocks(left, 1)
    half = model // 2
    return chain.call(
        functools.partial(hidden_back_body, n, len(lefts)),
        (width // tile,),
        [whole(grads.shape)] + down.tiles(tile) + [out] * 2 + specs,
        [out] * 2 + [pl.BlockSpec((half, tile), lambda j: (0, j))] * 2,
        [((rows, width), BF16)] * 2 + [((half, width), BF16)] * 2,
        flops=4 * rows * model * width,
        scratch=[pltpu.VMEM((half, rows), BF16)],
        moved=2 * (rows * model + model * width + 4 * rows * width),
    )(grads, *down.pieces, slope, silu, *lefts)


def mixed_back_body(n, counts, *refs):
    m = sum(counts)
    out_ref, x_ref, sems = refs[m + n :]

    @pl.when(pl.program_id(0) == 0)
    def _():
        collect(counts, refs, x_ref, sems)

    out_ref[...] = nn(x_ref[...], joined(refs[m : m + n])).astype(BF16)


def mixed_back(chain, held, out):
    counts, arrays, specs, scratch = collected(held)
    rows, model = scratch[0].shape
    n, width = len(out.pieces), out.width
    tile = min(256, width)
    return chain.call(
        functools.partial(mixed_back_body, n, counts),
        (width // tile,),
        specs + out.tiles(tile),
        [pl.BlockSpec((rows, tile), lambda j: (0, j))],
        [((rows, width), BF16)],
        flops=2 * rows * model * width,
        scratch=scratch,
        moved=2 * (rows * model + model * width + rows * width),
    )(*arrays, *out.pieces)[0]


def trans_body(n, starts, targets, *refs):
    parts, blocks = len(starts), len(targets[0])
    lefts = refs[:parts]
    pieces = refs[parts : parts * (n + 1)]
    outs = refs[parts * (n + 1) : -4]
    held, ready, sems, out_sems = refs[-4:]
    j = pl.program_id(0)
    depth, width = held.shape[2:]
    rows = ready.shape[1] // blocks

    def copy(i, p, slot):
        source = pieces[p * n + i].at[pl.ds(0, depth), pl.ds(starts[p], width)]
        return pltpu.make_async_copy(source, held.at[slot, p], sems.at[slot, p])

    def fetch(step, slot):
        for i in range(n):

            @pl.when(step == i)
            def _():
                for p in range(parts):
                    copy(i, p, slot).start()

    def leave(slot, k, array, first, column):
        target = outs[array].at[pl.ds(first, rows), pl.ds(column, depth)]
        source = ready.at[slot, pl.ds(k * rows, rows), :]
        return pltpu.make_async_copy(source, target, out_sems.at[slot, k])

    def left(slot):
        for k in range(blocks):
            leave(slot, k, 0, 0, 0).wait()

    @pl.when(j == 0)
    def _():
        fetch(j, 0)

    @pl.when(j + 1 < n)
    def _():
        fetch(j + 1, (j + 1) % 2)

    slot = j % 2
    for p in range(parts):
        copy(0, p, slot).wait()

    @pl.when(j >= 2)
    def _():
        left(slot)

    for s in range(blocks * rows // SEQ):
        span = slice(s * SEQ, (s + 1) * SEQ)
        total = nt(lefts[0][span, :], held[slot, 0])
        for p in range(1, parts):
            total += nt(lefts[p][span, :], held[slot, p])
        ready[slot, span, :] = total.astype(BF16)
    column = pl.multiple_of(j % (n // 2) * depth, 128)
    for h in range(2):

        @pl.when((j >= n // 2) == (h == 1))
        def _():
            for k, (array, first) in enumerate(targets[h]):
                leave(slot, k, array, first, column).start()

    @pl.when(j == n - 1)
    def _():
        left(1 - slot)
        left(slot)


def times_trans(chain, parts, group):
    weights = [weight for _, weight in parts]
    n, depth, width = len(weights[0].pieces), weights[0].rows, weights[0].width
    rows = parts[0][0].shape[0]
    half = weights[0].model // 2
    size = rows // group.size
    messages = group.messages()
    shapes = [((size, half), BF16)] * 2
    targets = [{0: (0, 0)}, {0: (1, 0)}]
    for h in range(2):
        for keys in messages[h]:
            for i, k in enumerate(keys):
                targets[h][k] = (len(shapes), i * size)
            shapes.append(((len(keys) * size, half), BF16))
    targets = [[t[k] for k in range(group.size)] for t in targets]
    anywhere = pl.BlockSpec(memory_space=pl.ANY)
    outs = chain.call(
        functools.partial(trans_body, n, [weight.start for weight in weights], targets),
        (n,),
        [whole((rows, width))] * len(parts) + [anywhere] * (n * len(parts)),
        [anywhere] * len(shapes),
        shapes,
        flops=4 * rows * half * width * len(parts),
        scratch=[
            pltpu.VMEM((2, len(parts), depth, width), BF16),
            pltpu.VMEM((2, rows, depth), BF16),
            pltpu.SemaphoreType.DMA((2, len(parts))),
            pltpu.SemaphoreType.DMA((2, group.size)),
        ],
        moved=2 * (2 * rows * half + len(parts) * (rows + 2 * half) * width),
    )(*[left for left, _ in parts], *[piece for weight in weights for piece in weight.pieces])
    m = group.bits
    return outs[:2], [outs[2 : 2 + m], outs[2 + m :]]


def grad_body(parts, got, blocks, steps, *refs):
    lefts, refs = refs[:blocks], refs[blocks:]
    rights, refs = refs[:parts], refs[parts:]
    got_ref = refs[0] if got else None
    outs, turned = refs[got:-1], refs[-1]
    j = pl.program_id(0)

    @pl.when(j == 0)
    def _():
        rows = turned.shape[1] // blocks
        for k in range(blocks):
            turned[:, cut(rows, k)] = lefts[k][...].T

    for i in range(parts):

        @pl.when((j >= i * steps) & (j < (i + 1) * steps))
        def _():
            total = nn(turned[...], rights[i][...])
            if got:
                total += got_ref[...].astype(F32)
            total = total.astype(BF16)
            first = 0
            for out_ref in outs:
                count = out_ref.shape[0]
                out_ref[...] = total[first : first + count]
                first += count


def weight_grads(chain, left, which, rights, got=None, bits=0):
    rows, width = rights[0].shape
    parts = len(rights)
    tile = min(512, width)
    steps = width // tile
    lefts, ins = half_blocks(left if isinstance(left, list) else [[left]], which)
    blocks, half = len(lefts), ins[0].block_shape[1]
    for i in range(parts):
        ins.append(
            pl.BlockSpec(
                (rows, tile),
                functools.partial(
                    lambda first, j: (0, jnp.clip(j - first, 0, steps - 1)), i * steps
                ),
            )
        )
    column = lambda j: (0, j)
    more = [] if got is None else [got]
    sizes = [half >> bits]
    for p in range(bits):
        sizes += [sizes[0], ((1 << p) - 1) * sizes[0]] if p else [sizes[0]]
    return chain.call(
        functools.partial(grad_body, parts, len(more), blocks, steps),
        (parts * steps,),
        ins + [pl.BlockSpec((half, tile), column)] * len(more),
        [pl.BlockSpec((size, tile), column) for size in sizes],
        [((size, parts * width), BF16) for size in sizes],
        flops=2 * rows * half * width * parts,
        scratch=[pltpu.VMEM((half, rows), BF16)],
        moved=2 * (rows * half + parts * (rows + half) * width),
    )(*lefts, *rights, *more)


def causal(scores):
    past = scores.shape[0] - HALF_SEQ
    key = lax.broadcasted_iota(jnp.int32, (HALF_SEQ, HALF_SEQ), 0)
    query = lax.broadcasted_iota(jnp.int32, (HALF_SEQ, HALF_SEQ), 1)
    last = jnp.where(key <= query, scores[past:], -1e30)
    return last if past == 0 else jnp.concatenate([scores[:past], last], axis=0)


def head_of(h):
    return slice(h * HEAD_DIM, (h + 1) * HEAD_DIM)


def span_of(b):
    return slice(b * HALF_SEQ, (b + 1) * HALF_SEQ)


def in_place(shift_ref, ref, count):
    rows = SEQ // count
    spans = [pl.ds(pl.multiple_of((i ^ shift_ref[0]) * rows, rows), rows) for i in range(count)]
    return jnp.concatenate([ref[span, :] for span in spans], axis=0)


def put_back(shift_ref, ref, count, values):
    rows = SEQ // count
    for i in range(count):
        ref[pl.ds(pl.multiple_of((i ^ shift_ref[0]) * rows, rows), rows), :] = values[cut(rows, i)]


def one_head(values, h):
    lane = lax.broadcasted_iota(jnp.int32, values.shape, 1)
    return jnp.where(lane // HEAD_DIM == h, values, jnp.zeros_like(values))


def attend_body(count, shift_ref, q_ref, k_ref, v_ref, out_ref, sum_ref):
    queries, keys = in_place(shift_ref, q_ref, count), in_place(shift_ref, k_ref, count)
    values = in_place(shift_ref, v_ref, count).astype(F32).T.astype(BF16)
    heads = []
    for h in range(q_ref.shape[1] // HEAD_DIM):
        blocks = []
        for b in range(2):
            reach = (b + 1) * HALF_SEQ
            query = one_head(queries[span_of(b)] * BF16(FACTOR), h)
            scores = causal(nt(keys[:reach], query))
            top = jnp.max(scores, axis=0, keepdims=True)
            expo = jnp.exp(scores - top)
            total = jnp.sum(expo, axis=0, keepdims=True)
            mixed = nn(values[head_of(h), :reach], expo.astype(BF16))
            blocks.append(mixed * (1.0 / total))
            sum_ref[0, h, :, span_of(b)] = top + jnp.log(total)
        heads.append(jnp.concatenate(blocks, axis=1))
    put_back(shift_ref, out_ref, count, jnp.concatenate(heads, axis=0).T.astype(BF16))


def attention_specs(rows, width, wide):
    wide = min(wide, width)
    tile = pl.BlockSpec((SEQ, wide), lambda s, p, _: (s, p))
    sums = pl.BlockSpec((1, wide // HEAD_DIM, 1, SEQ), lambda s, p, _: (s, p, 0, 0))
    return (rows // SEQ, width // wide), tile, sums


def attend(chain, shift, count, query, key, value):
    rows, width = query.shape
    grid, tile, sums = attention_specs(rows, width, 256)
    return chain.call(
        functools.partial(attend_body, count),
        grid,
        [tile] * 3,
        [tile, sums],
        [((rows, width), BF16), ((rows // SEQ, width // HEAD_DIM, 1, SEQ), F32)],
        flops=16 * rows * width * SEQ,
        prefetch=1,
        moved=8 * rows * width,
    )(shift, query, key, value)


def attend_back_body(
    count, shift_ref, q_ref, k_ref, v_ref, g_ref, sum_ref, cos_ref, sin_ref, dq_ref, dk_ref, dv_ref
):
    queries, keys, values, grads = (
        in_place(shift_ref, ref, count) for ref in (q_ref, k_ref, v_ref, g_ref)
    )
    turned = keys.astype(F32).T.astype(BF16)
    dq_heads = []
    dk, dv = [], []
    for b in range(2):
        reach = (b + 1) * HALF_SEQ
        dq, dk_sum, dv_sum = [], None, None
        for h in range(q_ref.shape[1] // HEAD_DIM):
            query = one_head(queries[span_of(b)], h)
            grad = one_head(grads[span_of(b)], h)
            scores = causal(nt(keys[:reach], query * BF16(FACTOR)))
            probs = jnp.exp(scores - sum_ref[0, h, :, span_of(b)])
            probs_grad = nt(values[:reach], grad)
            inner = jnp.sum(probs * probs_grad, axis=0, keepdims=True)
            score_grad = (probs * (probs_grad - inner)).astype(BF16)
            dv_part, dk_part = nn(probs.astype(BF16), grad), nn(score_grad, query)
            dv_sum = dv_part if dv_sum is None else dv_sum + dv_part
            dk_sum = dk_part if dk_sum is None else dk_sum + dk_part
            dq.append(nn(turned[head_of(h), :reach], score_grad))
        dq_heads.append(jnp.concatenate(dq, axis=0))
        dk.append(dk_sum)
        dv.append(dv_sum)

    def whole_rows(parts):
        early, late = parts
        return jnp.concatenate([late[:HALF_SEQ] + early, late[HALF_SEQ:]], axis=0)

    dq = jnp.concatenate(dq_heads, axis=1).T * FACTOR
    dk = whole_rows(dk) * FACTOR
    dv = whole_rows(dv).astype(BF16)
    copies = dq.shape[1] // PAIR
    cosine = jnp.concatenate([cos_ref[...]] * copies, axis=1)
    sine = jnp.concatenate([sin_ref[...]] * copies, axis=1)
    put_back(shift_ref, dq_ref, count, (dq * cosine - turn(dq) * sine).astype(BF16))
    put_back(shift_ref, dk_ref, count, (dk * cosine - turn(dk) * sine).astype(BF16))
    put_back(shift_ref, dv_ref, count, dv)


def attend_back(chain, shift, count, query, key, value, grad, logsum, tables):
    rows, width = query.shape
    grid, tile, sums = attention_specs(rows, width, PAIR)
    return chain.call(
        functools.partial(attend_back_body, count),
        grid,
        [tile] * 4 + [sums] + [whole((SEQ, PAIR))] * 2,
        [tile] * 3,
        [((rows, width), BF16)] * 3,
        flops=40 * rows * width * SEQ,
        prefetch=1,
        moved=14 * rows * width,
    )(shift, query, key, value, grad, logsum, *tables)


def local(
    chips,
    group,
    tokens,
    attn_gain,
    query_weight,
    key_weight,
    value_weight,
    output_weight,
    ffn_gain,
    gate_weight,
    up_weight,
    down_weight,
    cotangent,
):
    line = jnp.asarray(chips.table)[lax.axis_index("dp")]
    rows, model = tokens.shape
    count = SEQ // rows
    shift = lax.axis_index("tensor") % count
    row = jnp.arange(SEQ, dtype=jnp.int32)
    places = rope_tables(row)
    tables = rope_tables((row // rows ^ shift) * rows + row % rows)
    shift = jnp.reshape(shift, (1,)).astype(jnp.int32)
    early = (*places, *tables, line, shift)
    depth, own = query_weight.shape
    hidden_units = gate_weight.shape[1]
    chain = Chain()

    def gather(piece):
        return Gather(chips, chain, chain.join(piece)[0])

    def spread_of(values):
        return Spread(group, chain, chain.join(values)[0])

    def fold_of(part):
        own_part, sent = part
        sent = chain.join(*sent[0], *sent[1])
        return Fold(group, chain, own_part, [sent[: group.bits], sent[group.bits :]])

    def grads_of(left, rights, theirs=None):
        if theirs is None:
            (theirs,) = weight_grads(chain, left, 1, rights)
        got = [None]
        chain.ask(theirs, got, 0, chips.other)

        def mine(**how):
            if got[0] is None:
                chain.flush()
            blocks = weight_grads(chain, left, 0, rights, got[0], chips.bits)
            return Sums(chips, chain, blocks, **how)

        return mine

    extra = jnp.concatenate([attn_gain, ffn_gain, jnp.zeros((4 * own - 2 * depth,), BF16)])
    attn = jnp.concatenate([query_weight, key_weight, value_weight, output_weight.T], axis=1)
    attn = gather(jnp.concatenate([attn, jnp.broadcast_to(extra, (16, 4 * own))], axis=0))
    spread = spread_of(tokens)
    grads_spread = spread_of(cotangent)
    grads_spread.later = []
    down_turned, *early = chain.join(down_weight.T, *early)
    places, tables, line, shift = early[:2], early[2:4], early[4], early[5]
    chain.end(attn, spread, grads_spread)
    chain.end(attn, spread)
    all_tokens = spread.blocks()
    attn = attn.pieces()
    pair = gather(jnp.concatenate([gate_weight, up_weight], axis=1))
    w_query, w_key, w_value, w_output = [Weight(attn, depth, i * own, own) for i in range(4)]
    gains = jnp.concatenate(
        [piece[depth : depth + 1, : 2 * depth].reshape(2, depth) for piece in attn], axis=1
    ).astype(F32)

    group_one = ordered(chain, norm_body, line, gains, all_tokens)
    grads_spread.resume()
    query, key, value = project(chain, group_one, tables, w_query, w_key, w_value)
    mixed, logsum = attend(chain, shift, count, query, key, value)
    out_part = times_trans(chain, [(mixed, w_output)], group)
    fold = fold_of(out_part)
    chain.end(fold, pair, grads_spread)
    grad_rows = ordered(chain, order_body, line, gains, grads_spread.blocks())
    chain.end(fold)
    attended = fold.total()
    middle, second = by_rows(
        chain, middle_body, line, tokens, gains, attended, [], [F32, BF16]
    )
    spread = spread_of(second)
    chain.end(spread, pair)
    pair = pair.pieces()
    down = gather(down_turned)
    chain.end(spread)
    group_two = spread.blocks()
    w_gate = Weight(pair, depth, 0, hidden_units)
    w_up = Weight(pair, depth, hidden_units, hidden_units)
    hidden, slope, silu, theirs = gate_up(chain, group_two, w_gate, w_up, grad_rows)

    mine = grads_of(grad_rows, [hidden], theirs)
    chain.end(down)
    chain.flush()
    down_sum = mine()
    w_down = Weight(down.pieces(), depth, 0, hidden_units)
    gate_grad, up_grad, gate_theirs, up_theirs = hidden_back(
        chain, grad_rows, w_down, slope, silu, group_two
    )
    mine_gate = grads_of(group_two, [gate_grad], gate_theirs)
    mine_up = grads_of(group_two, [up_grad], up_theirs)
    chain.end(down_sum)
    second_part = times_trans(chain, [(gate_grad, w_gate), (up_grad, w_up)], group)
    gate_sum = mine_gate(hold=True)
    up_sum = mine_up(apart=True)
    chain.end(down_sum)
    fold = fold_of(second_part)
    result_part = times_trans(chain, [(hidden, w_down)], group)
    chain.end(gate_sum, fold)
    chain.end(fold)
    second_grad = fold.total()
    middle_grad, low_grad = by_rows(
        chain, second_back_body, line, cotangent, gains, second_grad, [middle], [F32, BF16]
    )
    spread = spread_of(low_grad)
    chain.end(up_sum)
    gate_sum.resume()
    (down_sum,) = finish(chain, down_sum.terms())
    chain.end(spread)
    attn_grads = spread.blocks()

    mixed_grad = mixed_back(chain, attn_grads, w_output)
    mine_out = grads_of(attn_grads, [mixed])
    chain.end(gate_sum)
    up_sum.send_half(0)
    fold = fold_of(result_part)
    query_back, key_back, value_back = attend_back(
        chain, shift, count, query, key, value, mixed_grad, logsum, places
    )
    mine_qkv = grads_of(group_one, [query_back, key_back, value_back])
    out_sum = mine_out(hold=True)
    chain.end(up_sum, fold)
    up_sum.send_half(1)
    qkv_sum = mine_qkv(cut_in_two=True)
    chain.end(fold, out_sum)
    result_part = fold.total()
    first_part = times_trans(
        chain, [(query_back, w_query), (key_back, w_key), (value_back, w_value)], group
    )
    chain.end(up_sum, qkv_sum)
    fold = fold_of(first_part)
    out_sum.resume()
    up_sum, up_inner = finish(chain, up_sum.terms(), [up_weight])
    gate_sum, gate_inner = finish(chain, gate_sum.terms(), [gate_weight])
    (layer_out,) = by_rows(chain, result_body, line, middle, gains, result_part, [], [BF16])
    chain.end(fold)
    chain.end(fold)
    chain.end(qkv_sum)
    query_sum, key_sum, value_sum, qkv_inner = finish(
        chain, qkv_sum.terms(), [query_weight, key_weight, value_weight]
    )
    gain_parts = jnp.stack(
        [qkv_inner / attn_gain.astype(F32), (gate_inner + up_inner) / ffn_gain.astype(F32)]
    )
    (gain_parts,) = chain.join(gain_parts)
    first_grad = fold.total()
    (input_grad,) = by_rows(
        chain, first_back_body, line, tokens, gains, first_grad, [middle_grad], [F32]
    )
    (out_sum,) = finish(chain, out_sum.terms())
    gain_totals = gain_parts
    for k in range(1, group.size):
        pairs = [(i, i ^ k) for i in range(group.size)]
        gain_totals += lax.ppermute(gain_parts, "tensor", pairs)
    gain_one_total, gain_two_total = gain_totals[0], gain_totals[1]
    return (
        layer_out,
        input_grad,
        gain_one_total,
        query_sum,
        key_sum,
        value_sum,
        out_sum,
        gain_two_total,
        gate_sum,
        up_sum,
        down_sum,
    )


def solution(mesh):
    in_specs = (
        P(("dp", "tensor"), None),
        P("dp"),
        P("dp", "tensor"),
        P("dp", "tensor"),
        P("dp", "tensor"),
        P("tensor", "dp"),
        P("dp"),
        P("dp", "tensor"),
        P("dp", "tensor"),
        P("tensor", "dp"),
        P(("dp", "tensor"), None),
    )
    out_specs = (
        P(("dp", "tensor"), None),
        P(("dp", "tensor"), None),
        P("dp"),
        P("dp", "tensor"),
        P("dp", "tensor"),
        P("dp", "tensor"),
        P("tensor", "dp"),
        P("dp"),
        P("dp", "tensor"),
        P("dp", "tensor"),
        P("tensor", "dp"),
    )
    chips = Chips(mesh.shape["dp"])
    size = mesh.shape["tensor"]
    links = [[(i, i ^ 1 << b) for i in range(size)] for b in range(size.bit_length() - 1)]
    group = Group(links, "tensor")

    def run(*arrays):
        return local(chips, group, *arrays)

    return jax.shard_map(run, mesh=mesh, in_specs=in_specs, out_specs=out_specs, check_vma=False)
```

```python
import functools

import jax
import jax.numpy as jnp
import numpy as np
from jax import lax
from jax.experimental import pallas as pl
from jax.experimental.pallas import tpu as pltpu
from jax.sharding import PartitionSpec as P

HEAD_DIM = 64
SEQ = 512
EPS = 1e-05
THETA = 130000.0
BF16 = jnp.bfloat16
F32 = jnp.float32
FACTOR = HEAD_DIM**-0.5
PAIR = 2 * HEAD_DIM
HALF_SEQ = SEQ // 2
VMEM_LIMIT = 58 << 20
COST_SHARE = 4096


class Chain:
    def __init__(self):
        self.token = jnp.zeros((8, 128), F32)
        self.swaps, self.asked = [], []

    def join(self, *values):
        *values, self.token = lax.optimization_barrier((*values, self.token))
        return values

    def gate(self, *values):
        swaps, self.swaps = self.swaps, []
        asked, self.asked = self.asked, []
        joined = self.join(
            *values, *[held[i] for held, i in swaps], *[source for source, _, _, _ in asked]
        )
        for (held, i), value in zip(swaps, joined[len(values) :]):
            held[i] = value
        for (_, held, i, swap), value in zip(asked, joined[len(values) + len(swaps) :]):
            held[i] = swap(value)
            self.swaps.append((held, i))
        return joined[: len(values)]

    def end(self, *transfers):
        counts = [len(t.flying) for t in transfers]
        got = self.gate(*[value for t in transfers for value in t.flying])
        for t, count in zip(transfers, counts):
            if count:
                t.go_on(got[:count])
            got = got[count:]

    def ask(self, source, held, i, swap):
        self.asked.append((source, held, i, swap))

    def flush(self):
        for source, held, i, swap in self.asked:
            held[i] = swap(source)
        self.asked = []

    def call(self, body, grid, ins, outs, shapes, flops, scratch=(), prefetch=0, moved=0):
        first = prefetch + len(ins)
        second = first + 1 + len(outs)
        anywhere = pl.BlockSpec(memory_space=pl.ANY)

        def wrapped(*refs):
            body(*refs[:first], *refs[first + 1 : second], *refs[second + 1 :])

        run = pl.pallas_call(
            wrapped,
            grid_spec=pltpu.PrefetchScalarGridSpec(
                num_scalar_prefetch=prefetch,
                grid=grid,
                in_specs=[*ins, anywhere],
                out_specs=[*outs, anywhere],
                scratch_shapes=list(scratch),
            ),
            out_shape=[jax.ShapeDtypeStruct(s, t) for s, t in [*shapes, ((8, 128), F32)]],
            compiler_params=pltpu.CompilerParams(
                vmem_limit_bytes=VMEM_LIMIT, dimension_semantics=("arbitrary",) * len(grid)
            ),
            cost_estimate=pl.CostEstimate(
                flops=flops // COST_SHARE, bytes_accessed=moved // COST_SHARE, transcendentals=0
            ),
        )

        def with_token(*args):
            *results, self.token = run(*args, self.token)
            return results

        return with_token


class Chips:
    def __init__(self, size):
        self.bits = (size // 2).bit_length() - 1
        self.size = size
        self.swap = [(i, i ^ 1) for i in range(size)]
        self.links = [
            [(i, i ^ 2 << self.bits - 1 - p) for i in range(size)] for p in range(self.bits)
        ]
        flips = [
            sum(1 << self.bits - 1 - p for p in range(self.bits) if v >> p & 1)
            for v in range(1 << self.bits)
        ]
        table = [[i ^ 2 * f for f in flips] + [i ^ 2 * f ^ 1 for f in flips] for i in range(size)]
        self.table = np.array(table, np.int32)

    def send(self, value, p):
        return lax.ppermute(value, "dp", self.links[p])

    def other(self, value):
        return lax.ppermute(value, "dp", self.swap)


class Gather:
    def __init__(self, chips, chain, piece):
        self.chips, self.chain = chips, chain
        self.own = [piece] + [None] * (2**chips.bits - 1)
        self.others = list(self.own)
        self.ask(0)
        self.keys = [1 << p for p in range(chips.bits)]
        self.flying = [chips.send(piece, p) for p in range(chips.bits)]

    def ask(self, v):
        self.chain.ask(self.own[v], self.others, v, self.chips.other)

    def go_on(self, got):
        keys, self.keys, self.flying = self.keys, [], []
        for v, piece in zip(keys, got):
            self.own[v] = piece
            for p in range(v.bit_length(), self.chips.bits):
                self.keys.append(v | 1 << p)
                self.flying.append(self.chips.send(piece, p))
        for v in keys:
            self.ask(v)

    def pieces(self):
        while self.flying:
            self.chain.end(self)
        self.chain.flush()
        return self.own + self.others


class Sums:
    def __init__(self, chips, chain, mine, apart=False, hold=False, cut_in_two=False):
        self.chips, self.chain, self.apart, self.hold = chips, chain, apart, hold
        self.todo = []
        self.cut_in_two = cut_in_two and chips.bits == 2
        self.parts = [mine[0]]
        mine = list(mine[1:])
        self.direct, self.passed = [], []
        for p in range(chips.bits):
            self.direct.append(mine.pop(0))
            self.passed.append(mine.pop(0) if p else None)
        self.p = chips.bits - 1
        if self.cut_in_two:
            self.kinds = [0, 1]
            self.flying = [chips.send(half, 1) for half in self.in_two(self.passed[1])]
            return
        self.kinds = [self.p]
        self.flying = [chips.send(self.passed[self.p], self.p)]

    def in_two(self, values):
        width = values.shape[1] // 2
        return values[:, :width], values[:, width:]

    def go_on(self, got):
        rows = self.parts[0].shape[0]
        kinds, self.kinds, self.flying = self.kinds, [], []
        if self.p == 0:
            self.parts += got
            return
        if self.cut_in_two:
            self.p = 0
            total = self.direct[0].astype(F32) + jnp.concatenate(got, axis=1).astype(F32)
            self.todo = [(None, self.direct[1], 1), (None, total.astype(BF16), 0)]
            self.resume()
            return
        for kind, block in zip(kinds, got):
            if kind is None:
                self.parts.append(block)
                continue
            add = lambda held, first: (
                held.astype(F32) + block[first * rows : first * rows + held.shape[0]].astype(F32)
            ).astype(BF16)
            for q in range(kind):
                self.direct[q] = add(self.direct[q], (1 << q) - 1)
                if q:
                    self.passed[q] = add(self.passed[q], 1 << q)
        p, self.p = self.p, self.p - 1
        if p > 0:
            self.todo.append((None, self.direct[p], p))
        if p > 1:
            self.todo.append((p - 1, self.passed[p - 1], p - 1))
        if p == 1 and not self.apart:
            self.todo.append((None, self.direct[0], 0))
        if not self.hold:
            self.resume()

    def resume(self):
        todo, self.todo = self.todo, []
        values = self.chain.join(*[value for _, value, _ in todo])
        for (kind, _, p), value in zip(todo, values):
            self.kinds.append(kind)
            self.flying.append(self.chips.send(value, p))

    def send_half(self, i):
        while self.p > 0:
            self.chain.end(self)
        width = self.direct[0].shape[1] // 2
        (value,) = self.chain.join(self.direct[0][:, i * width : (i + 1) * width])
        self.kinds.append(None)
        self.flying.append(self.chips.send(value, 0))

    def terms(self):
        while self.flying or self.todo:
            if self.todo:
                self.resume()
            self.chain.end(self)
        return sorted(self.parts, key=lambda part: -part.shape[1])


class Group:
    def __init__(self, links, axes):
        self.links, self.axes = links, axes
        self.bits = len(links)
        self.size = 1 << self.bits
        self.orders = (list(range(self.bits)), list(range(self.bits))[::-1])

    def send(self, value, bit):
        return lax.ppermute(value, self.axes, self.links[bit])

    def messages(self):
        found = []
        for order in self.orders:
            found.append([])
            for top in reversed(range(self.bits)):
                found[-1].append(
                    [
                        1 << order[top] | sum(1 << order[p] for p in range(top) if v >> p & 1)
                        for v in range(1 << top)
                    ]
                )
        return found


class Spread:
    def __init__(self, group, chain, rows):
        self.group, self.chain = group, chain
        self.held = {0: [rows]}
        self.later = None
        self.keys = [(1 << b, None) for b in range(group.bits)]
        self.flying = [group.send(rows, b) for b in range(group.bits)]

    def go_on(self, got):
        fresh = list(zip(self.keys, got))
        self.keys, self.flying = [], []
        for (k, h), block in fresh:
            if h is None:
                self.held[k] = [block]
            else:
                self.held.setdefault(k, [None, None])[h] = block
        for (k, h), block in fresh:
            for way, order in enumerate(self.group.orders):
                if h is not None and h != way:
                    continue
                half = block.shape[1] // 2
                top = max(i for i, bit in enumerate(order) if k >> bit & 1)
                for i in range(top + 1, len(order)):
                    part = block if h is not None else block[:, way * half : (way + 1) * half]
                    self.keys.append((k | 1 << order[i], way))
                    if self.later is not None:
                        self.later.append((part, order[i]))
                    else:
                        self.flying.append(self.group.send(part, order[i]))

        if self.later:
            parts = self.chain.join(*[part for part, _ in self.later])
            self.later = [(part, bit) for part, (_, bit) in zip(parts, self.later)]

    def resume(self):
        later, self.later = self.later, None
        parts = self.chain.join(*[part for part, _ in later])
        self.flying = [self.group.send(part, bit) for part, (_, bit) in zip(parts, later)]

    def blocks(self):
        while self.flying:
            self.chain.end(self)
        return [self.held[k] for k in range(self.group.size)]


class Fold:
    def __init__(self, group, chain, own, sent):
        self.group, self.chain = group, chain
        self.rows = own[0].shape[0]
        self.sent = [list(half) for half in sent]
        self.parts = [[half] for half in own]
        self.wave = 0
        self.start()

    def start(self):
        self.flying = [
            self.group.send(self.sent[h][self.wave], order[self.group.bits - 1 - self.wave])
            for h, order in enumerate(self.group.orders)
        ]

    def go_on(self, got):
        self.wave += 1
        self.flying = []
        for h, block in enumerate(got):
            self.parts[h].append(block)
        for wave in range(self.wave, self.group.bits):
            sums = add_rows(self.chain, [sent[wave] for sent in self.sent], got)
            for sent, value in zip(self.sent, sums):
                sent[wave] = value
        if self.wave < self.group.bits:
            self.start()

    def total(self):
        while self.flying:
            self.chain.end(self)
        return self.parts


class Weight:
    def __init__(self, pieces, rows, start, width):
        self.pieces, self.rows, self.start, self.width = pieces, rows, start, width
        self.model = len(pieces) * rows

    def tiles(self, tile):
        first = self.start // tile
        return [pl.BlockSpec((self.rows, tile), lambda j: (0, first + j))] * len(self.pieces)


def nn(left, right):
    return lax.dot_general(left, right, (((1,), (0,)), ((), ())), preferred_element_type=F32)


def nt(left, right):
    return lax.dot_general(left, right, (((1,), (1,)), ((), ())), preferred_element_type=F32)


def tn(left, right):
    return lax.dot_general(left, right, (((0,), (0,)), ((), ())), preferred_element_type=F32)


def whole(shape):
    return pl.BlockSpec(shape, lambda *_: (0,) * len(shape))


def place(line_ref, j, width):
    return pl.ds(pl.multiple_of(line_ref[j] * width, 128), width)


def cut(width, j):
    return slice(j * width, (j + 1) * width)


def scale_of(values):
    return lax.rsqrt(jnp.mean(values * values, axis=-1, keepdims=True) + EPS)


def fetch_blocks(counts, refs, held, sems, k, slot, wait):
    first = 0
    for i, count in enumerate(counts):
        copies = []
        half = held.shape[2] // count
        for h in range(count):
            target = held.at[slot, :, pl.ds(h * half, half)]
            copies.append(pltpu.make_async_copy(refs[first + h], target, sems.at[slot, h]))
        first += count

        @pl.when(k == i)
        def _():
            for copy in copies:
                copy.wait() if wait else copy.start()


def fetched(counts, refs, held, sems):
    k = pl.program_id(0)

    @pl.when(k == 0)
    def _():
        fetch_blocks(counts, refs, held, sems, k, 0, False)

    fetch_blocks(counts, refs, held, sems, k + 1, (k + 1) % 2, False)
    fetch_blocks(counts, refs, held, sems, k, k % 2, True)
    return held.at[k % 2]


def norm_body(blocks, counts, line_ref, gain_ref, *refs):
    out_ref, held, sems = refs[sum(counts) :]
    x_ref = fetched(counts, refs, held, sems)
    width = out_ref.shape[1] // blocks
    scale = scale_of(x_ref[...].astype(F32))
    for j in range(blocks):
        part = x_ref[:, place(line_ref, j, width)].astype(F32)
        gain = gain_ref[0:1, cut(width, j)]
        out_ref[:, cut(width, j)] = (part * scale * gain).astype(BF16)


def order_body(blocks, counts, line_ref, gain_ref, *refs):
    out_ref, held, sems = refs[sum(counts) :]
    x_ref = fetched(counts, refs, held, sems)
    width = out_ref.shape[1] // blocks
    for j in range(blocks):
        out_ref[:, cut(width, j)] = x_ref[:, place(line_ref, j, width)]


def ordered(chain, body, line, gains, held):
    counts = [len(block) for block in held]
    rows, model = held[0][0].shape
    n = len(held)
    return chain.call(
        functools.partial(body, line.shape[0], counts),
        (n,),
        [whole(gains.shape)] + [pl.BlockSpec(memory_space=pl.ANY)] * sum(counts),
        [pl.BlockSpec((rows, model), lambda k, *_: (k, 0))],
        [((n * rows, model), BF16)],
        flops=20 * n * rows * model,
        scratch=[pltpu.VMEM((2, rows, model), BF16), pltpu.SemaphoreType.DMA((2, 2))],
        prefetch=1,
        moved=4 * n * rows * model,
    )(line, gains, *[array for block in held for array in block])[0]


def added(refs, span):
    total = refs[0][span, :].astype(F32)
    for ref in refs[1:]:
        total += ref[span, :].astype(F32)
    return total


def middle_body(blocks, m, line_ref, x_ref, gain_ref, *refs):
    middle_ref, out_ref = refs[2 * m :]
    width = x_ref.shape[1] // blocks
    half = x_ref.shape[1] // 2
    span = slice(None)
    middle_ref[:, :half] = added(refs[:m], span)
    middle_ref[:, half:] = added(refs[m : 2 * m], span)
    for j in range(blocks):
        here = x_ref[:, place(line_ref, j, width)].astype(F32)
        middle_ref[:, cut(width, j)] += here
    middle = middle_ref[...]
    out_ref[...] = (middle * scale_of(middle) * gain_ref[1:2, :]).astype(BF16)


def result_body(blocks, m, line_ref, middle_ref, gain_ref, *refs):
    out_ref = refs[2 * m]
    width = middle_ref.shape[1] // blocks
    span = slice(None)
    total = middle_ref[...] + jnp.concatenate(
        [added(refs[:m], span), added(refs[m : 2 * m], span)], axis=1
    )
    for j in range(blocks):
        out_ref[:, place(line_ref, j, width)] = total[:, cut(width, j)].astype(BF16)


def second_back_body(blocks, m, line_ref, dy_ref, gain_ref, *refs):
    middle_ref, out_ref, low_ref = refs[2 * m :]
    width = dy_ref.shape[1] // blocks
    span = slice(None)
    grad = jnp.concatenate([added(refs[:m], span), added(refs[m : 2 * m], span)], axis=1)
    middle = middle_ref[...]
    scale = scale_of(middle)
    normed = middle * scale
    scaled = grad * gain_ref[1:2, :]
    out_ref[...] = scale * (scaled - normed * jnp.mean(scaled * normed, axis=-1, keepdims=True))
    for j in range(blocks):
        out_ref[:, cut(width, j)] += dy_ref[:, place(line_ref, j, width)].astype(F32)
    low_ref[...] = out_ref[...].astype(BF16)


def first_back_body(blocks, m, line_ref, x_ref, gain_ref, *refs):
    above_ref, out_ref = refs[2 * m :]
    width = x_ref.shape[1] // blocks
    span = slice(None)
    scale = scale_of(x_ref[...].astype(F32))
    normed = jnp.concatenate(
        [x_ref[:, place(line_ref, j, width)].astype(F32) for j in range(blocks)], axis=1
    ) * scale
    grad = jnp.concatenate([added(refs[:m], span), added(refs[m : 2 * m], span)], axis=1)
    scaled = grad * gain_ref[0:1, :]
    back = scale * (scaled - normed * jnp.mean(scaled * normed, axis=-1, keepdims=True))
    total = above_ref[...] + back
    for j in range(blocks):
        out_ref[:, place(line_ref, j, width)] = total[:, cut(width, j)]


def by_rows(chain, body, line, first, gains, parts, more, kinds):
    rows, model = first.shape
    half = model // 2
    tile = min(128, rows)
    row = pl.BlockSpec((tile, model), lambda i, *_: (i, 0))
    slim = pl.BlockSpec((tile, half), lambda i, *_: (i, 0))
    m = len(parts[0])
    return chain.call(
        functools.partial(body, line.shape[0], m),
        (rows // tile,),
        [row, whole(gains.shape)] + [slim] * (2 * m) + [row] * len(more),
        [row] * len(kinds),
        [((rows, model), kind) for kind in kinds],
        flops=20 * rows * model,
        prefetch=1,
        moved=rows * model * (2 * m + 4 * len(kinds)),
    )(line, first, gains, *parts[0], *parts[1], *more)


def add_rows_body(count, *refs):
    for i in range(count):
        total = refs[i][...].astype(F32) + refs[count + i][...].astype(F32)
        refs[2 * count + i][...] = total.astype(BF16)


def add_rows(chain, helds, blocks):
    rows, columns = helds[0].shape
    tile = min(128, rows)
    steps = rows // tile
    count = len(helds)
    here = pl.BlockSpec((tile, columns), lambda i: (i, 0))
    return chain.call(
        functools.partial(add_rows_body, count),
        (steps,),
        [here] * count + [pl.BlockSpec((tile, columns), lambda i: (steps + i, 0))] * count,
        [here] * count,
        [((rows, columns), BF16)] * count,
        flops=count * rows * columns,
        moved=6 * count * rows * columns,
    )(*helds, *blocks)


def finish_body(m, halves, n, *refs):
    total = added(refs[:m], slice(None))
    if halves:
        total += jnp.concatenate([ref[...].astype(F32) for ref in refs[m : m + halves]], axis=1)
    m += halves
    weights, outs = refs[m : m + n], refs[m + n :]
    if not n:
        outs[0][...] = total.T
        return
    width = weights[0].shape[1]
    inner = jnp.zeros((total.shape[0], 1), F32)
    for i in range(n):
        part = total[:, cut(width, i)]
        outs[i][...] = part
        inner += jnp.sum(weights[i][...].astype(F32) * part, axis=1, keepdims=True)
    outs[n][...] = jnp.broadcast_to(inner, outs[n].shape)


def finish(chain, terms, weights=()):
    rows, columns = terms[0].shape
    tile = min(128, rows)
    row = pl.BlockSpec((tile, columns), lambda i: (i, 0))
    n = len(weights)
    halves = sum(1 for term in terms if term.shape[1] < columns)
    half = [pl.BlockSpec((tile, columns // 2), lambda i: (i, 0))] * halves
    if n:
        slim = pl.BlockSpec((tile, columns // n), lambda i: (i, 0))
        outs = [slim] * n + [pl.BlockSpec((tile, 128), lambda i: (i, 0))]
        shapes = [((rows, columns // n), F32)] * n + [((rows, 128), F32)]
    else:
        slim = None
        outs = [pl.BlockSpec((columns, tile), lambda i: (0, i))]
        shapes = [((columns, rows), F32)]
    results = chain.call(
        functools.partial(finish_body, len(terms) - halves, halves, n),
        (rows // tile,),
        [row] * (len(terms) - halves) + half + [slim] * n,
        outs,
        shapes,
        flops=4 * rows * columns,
        moved=rows * columns * 12,
    )(*terms, *weights)
    if n:
        results[n] = results[n][:, 0]
    return results


def rope_tables(place):
    half = HEAD_DIM // 2
    freq = THETA ** (-2.0 * jnp.arange(half, dtype=F32) / HEAD_DIM)
    angle = place.astype(F32)[:, None] * freq[None, :]
    cosine, sine = jnp.cos(angle), jnp.sin(angle)
    return (
        jnp.concatenate([cosine] * (PAIR // half), axis=1),
        jnp.concatenate([-sine, sine] * (PAIR // HEAD_DIM), axis=1),
    )


def turn(values):
    half = HEAD_DIM // 2
    width = values.shape[-1]
    lane = lax.broadcasted_iota(jnp.int32, values.shape, 1) % HEAD_DIM
    return jnp.where(
        lane < half, pltpu.roll(values, width - half, 1), pltpu.roll(values, half, 1)
    )


def joined(refs):
    return jnp.concatenate([r[...] for r in refs], axis=0)


def qkv_body(n, x_ref, cos_ref, sin_ref, *refs):
    weights, outs = refs[: 3 * n], refs[3 * n :]
    rows = x_ref.shape[0]
    tile = outs[0].shape[1]
    for i in range(3):
        weight = joined(weights[i * n : (i + 1) * n])
        for s in range(rows // SEQ):
            span = slice(s * SEQ, (s + 1) * SEQ)
            product = nn(x_ref[span, :], weight)
            if i == 2:
                outs[i][span, :] = product.astype(BF16)
                continue
            for t in range(tile // PAIR):
                here = product[:, t * PAIR : (t + 1) * PAIR]
                turned = here * cos_ref[...] + turn(here) * sin_ref[...]
                outs[i][span, t * PAIR : (t + 1) * PAIR] = turned.astype(BF16)


def project(chain, x, tables, query, key, value):
    rows, model = x.shape
    n, width = len(query.pieces), query.width
    tile = min(256, width)
    out = pl.BlockSpec((rows, tile), lambda j: (0, j))
    return chain.call(
        functools.partial(qkv_body, n),
        (width // tile,),
        [whole(x.shape), whole((SEQ, PAIR)), whole((SEQ, PAIR))]
        + query.tiles(tile)
        + key.tiles(tile)
        + value.tiles(tile),
        [out] * 3,
        [((rows, width), BF16)] * 3,
        flops=6 * rows * model * width,
        moved=2 * (rows * model + 3 * model * width + 3 * rows * width),
    )(x, *tables, *query.pieces, *key.pieces, *value.pieces)


def collect(counts, refs, held, sems):
    rows = held.shape[0] // len(counts)
    copies = []
    for k, count in enumerate(counts):
        half = held.shape[1] // count
        for h in range(count):
            target = held.at[pl.ds(k * rows, rows), pl.ds(h * half, half)]
            i = len(copies)
            copies.append(pltpu.make_async_copy(refs[i], target, sems.at[i]))
    for copy in copies:
        copy.start()
    for copy in copies:
        copy.wait()


def gate_body(n, counts, *refs):
    m = sum(counts)
    gate_w, up_w = refs[m : m + n], refs[m + n : m + 2 * n]
    left_ref, hidden_ref, slope_ref, silu_ref, theirs_ref, x_ref, turned, sems = refs[m + 2 * n :]

    @pl.when(pl.program_id(0) == 0)
    def _():
        collect(counts, refs, x_ref, sems)
        turned[...] = left_ref[...].T

    gate_weight, up_weight = joined(gate_w), joined(up_w)
    for s in range(x_ref.shape[0] // SEQ):
        span = slice(s * SEQ, (s + 1) * SEQ)
        gate = nn(x_ref[span, :], gate_weight)
        up = nn(x_ref[span, :], up_weight)
        sigm = jax.nn.sigmoid(gate)
        silu = gate * sigm
        hidden_ref[span, :] = (silu * up).astype(BF16)
        silu_ref[span, :] = silu.astype(BF16)
        slope_ref[span, :] = (up * sigm * (1.0 + gate * (1.0 - sigm))).astype(BF16)
    theirs_ref[...] = nn(turned[...], hidden_ref[...]).astype(BF16)


def collected(held):
    counts = [len(block) for block in held]
    rows, model = held[0][0].shape
    scratch = [
        pltpu.VMEM((len(held) * rows, model), BF16),
        pltpu.SemaphoreType.DMA((sum(counts),)),
    ]
    arrays = [array for block in held for array in block]
    return counts, arrays, [pl.BlockSpec(memory_space=pl.ANY)] * len(arrays), scratch


def gate_up(chain, held, gate, up, grads):
    counts, arrays, specs, scratch = collected(held)
    rows, model = scratch[0].shape
    n, width = len(gate.pieces), gate.width
    tile = min(256, width)
    out = pl.BlockSpec((rows, tile), lambda j: (0, j))
    half = model // 2
    return chain.call(
        functools.partial(gate_body, n, counts),
        (width // tile,),
        specs
        + gate.tiles(tile)
        + up.tiles(tile)
        + [pl.BlockSpec((rows, half), lambda j: (0, 1))],
        [out] * 3 + [pl.BlockSpec((half, tile), lambda j: (0, j))],
        [((rows, width), BF16)] * 3 + [((half, width), BF16)],
        flops=6 * rows * model * width,
        scratch=[scratch[0], pltpu.VMEM((half, rows), BF16), scratch[1]],
        moved=2 * (rows * model + 2 * model * width + 3 * rows * width),
    )(*arrays, *gate.pieces, *up.pieces, grads)


def half_blocks(left, which):
    lefts = [block[0] if len(block) == 1 else block[which] for block in left]
    rows, half = lefts[0].shape[0], left[0][0].shape[1] // 2
    places = [which if len(block) == 1 else 0 for block in left]
    return lefts, [
        pl.BlockSpec((rows, half), functools.partial(lambda at, j: (0, at), at)) for at in places
    ]


def hidden_back_body(n, blocks, g_ref, *refs):
    weights, slope_ref, silu_ref = refs[:n], refs[n], refs[n + 1]
    lefts, refs = refs[n + 2 : n + 2 + blocks], refs[n + 2 + blocks :]
    gate_ref, up_ref, gate_theirs, up_theirs, turned = refs
    rows = turned.shape[1] // blocks

    @pl.when(pl.program_id(0) == 0)
    def _():
        for k in range(blocks):
            turned[:, cut(rows, k)] = lefts[k][...].T

    weight = joined(weights)
    for s in range(g_ref.shape[0] // SEQ):
        span = slice(s * SEQ, (s + 1) * SEQ)
        grad = nn(g_ref[span, :], weight)
        gate_ref[span, :] = (grad * slope_ref[span, :].astype(F32)).astype(BF16)
        up_ref[span, :] = (grad * silu_ref[span, :].astype(F32)).astype(BF16)
    gate_theirs[...] = nn(turned[...], gate_ref[...]).astype(BF16)
    up_theirs[...] = nn(turned[...], up_ref[...]).astype(BF16)


def hidden_back(chain, grads, down, slope, silu, left):
    rows, model = grads.shape
    n, width = len(down.pieces), down.width
    tile = min(256, width)
    out = pl.BlockSpec((rows, tile), lambda j: (0, j))
    lefts, specs = half_blocks(left, 1)
    half = model // 2
    return chain.call(
        functools.partial(hidden_back_body, n, len(lefts)),
        (width // tile,),
        [whole(grads.shape)] + down.tiles(tile) + [out] * 2 + specs,
        [out] * 2 + [pl.BlockSpec((half, tile), lambda j: (0, j))] * 2,
        [((rows, width), BF16)] * 2 + [((half, width), BF16)] * 2,
        flops=4 * rows * model * width,
        scratch=[pltpu.VMEM((half, rows), BF16)],
        moved=2 * (rows * model + model * width + 4 * rows * width),
    )(grads, *down.pieces, slope, silu, *lefts)


def mixed_back_body(n, counts, *refs):
    m = sum(counts)
    out_ref, x_ref, sems = refs[m + n :]

    @pl.when(pl.program_id(0) == 0)
    def _():
        collect(counts, refs, x_ref, sems)

    out_ref[...] = nn(x_ref[...], joined(refs[m : m + n])).astype(BF16)


def mixed_back(chain, held, out):
    counts, arrays, specs, scratch = collected(held)
    rows, model = scratch[0].shape
    n, width = len(out.pieces), out.width
    tile = min(256, width)
    return chain.call(
        functools.partial(mixed_back_body, n, counts),
        (width // tile,),
        specs + out.tiles(tile),
        [pl.BlockSpec((rows, tile), lambda j: (0, j))],
        [((rows, width), BF16)],
        flops=2 * rows * model * width,
        scratch=scratch,
        moved=2 * (rows * model + model * width + rows * width),
    )(*arrays, *out.pieces)[0]


def trans_body(n, starts, targets, *refs):
    parts, blocks = len(starts), len(targets[0])
    lefts = refs[:parts]
    pieces = refs[parts : parts * (n + 1)]
    outs = refs[parts * (n + 1) : -4]
    held, ready, sems, out_sems = refs[-4:]
    j = pl.program_id(0)
    depth, width = held.shape[2:]
    rows = ready.shape[1] // blocks

    def copy(i, p, slot):
        source = pieces[p * n + i].at[pl.ds(0, depth), pl.ds(starts[p], width)]
        return pltpu.make_async_copy(source, held.at[slot, p], sems.at[slot, p])

    def fetch(step, slot):
        for i in range(n):

            @pl.when(step == i)
            def _():
                for p in range(parts):
                    copy(i, p, slot).start()

    def leave(slot, k, array, first, column):
        target = outs[array].at[pl.ds(first, rows), pl.ds(column, depth)]
        source = ready.at[slot, pl.ds(k * rows, rows), :]
        return pltpu.make_async_copy(source, target, out_sems.at[slot, k])

    def left(slot):
        for k in range(blocks):
            leave(slot, k, 0, 0, 0).wait()

    @pl.when(j == 0)
    def _():
        fetch(j, 0)

    @pl.when(j + 1 < n)
    def _():
        fetch(j + 1, (j + 1) % 2)

    slot = j % 2
    for p in range(parts):
        copy(0, p, slot).wait()

    @pl.when(j >= 2)
    def _():
        left(slot)

    for s in range(blocks * rows // SEQ):
        span = slice(s * SEQ, (s + 1) * SEQ)
        total = nt(lefts[0][span, :], held[slot, 0])
        for p in range(1, parts):
            total += nt(lefts[p][span, :], held[slot, p])
        ready[slot, span, :] = total.astype(BF16)
    column = pl.multiple_of(j % (n // 2) * depth, 128)
    for h in range(2):

        @pl.when((j >= n // 2) == (h == 1))
        def _():
            for k, (array, first) in enumerate(targets[h]):
                leave(slot, k, array, first, column).start()

    @pl.when(j == n - 1)
    def _():
        left(1 - slot)
        left(slot)


def times_trans(chain, parts, group):
    weights = [weight for _, weight in parts]
    n, depth, width = len(weights[0].pieces), weights[0].rows, weights[0].width
    rows = parts[0][0].shape[0]
    half = weights[0].model // 2
    size = rows // group.size
    messages = group.messages()
    shapes = [((size, half), BF16)] * 2
    targets = [{0: (0, 0)}, {0: (1, 0)}]
    for h in range(2):
        for keys in messages[h]:
            for i, k in enumerate(keys):
                targets[h][k] = (len(shapes), i * size)
            shapes.append(((len(keys) * size, half), BF16))
    targets = [[t[k] for k in range(group.size)] for t in targets]
    anywhere = pl.BlockSpec(memory_space=pl.ANY)
    outs = chain.call(
        functools.partial(trans_body, n, [weight.start for weight in weights], targets),
        (n,),
        [whole((rows, width))] * len(parts) + [anywhere] * (n * len(parts)),
        [anywhere] * len(shapes),
        shapes,
        flops=4 * rows * half * width * len(parts),
        scratch=[
            pltpu.VMEM((2, len(parts), depth, width), BF16),
            pltpu.VMEM((2, rows, depth), BF16),
            pltpu.SemaphoreType.DMA((2, len(parts))),
            pltpu.SemaphoreType.DMA((2, group.size)),
        ],
        moved=2 * (2 * rows * half + len(parts) * (rows + 2 * half) * width),
    )(*[left for left, _ in parts], *[piece for weight in weights for piece in weight.pieces])
    m = group.bits
    return outs[:2], [outs[2 : 2 + m], outs[2 + m :]]


def grad_body(parts, got, blocks, steps, *refs):
    lefts, refs = refs[:blocks], refs[blocks:]
    rights, refs = refs[:parts], refs[parts:]
    got_ref = refs[0] if got else None
    outs, turned = refs[got:-1], refs[-1]
    j = pl.program_id(0)

    @pl.when(j == 0)
    def _():
        rows = turned.shape[1] // blocks
        for k in range(blocks):
            turned[:, cut(rows, k)] = lefts[k][...].T

    for i in range(parts):

        @pl.when((j >= i * steps) & (j < (i + 1) * steps))
        def _():
            total = nn(turned[...], rights[i][...])
            if got:
                total += got_ref[...].astype(F32)
            total = total.astype(BF16)
            first = 0
            for out_ref in outs:
                count = out_ref.shape[0]
                out_ref[...] = total[first : first + count]
                first += count


def weight_grads(chain, left, which, rights, got=None, bits=0):
    rows, width = rights[0].shape
    parts = len(rights)
    tile = min(512, width)
    steps = width // tile
    lefts, ins = half_blocks(left if isinstance(left, list) else [[left]], which)
    blocks, half = len(lefts), ins[0].block_shape[1]
    for i in range(parts):
        ins.append(
            pl.BlockSpec(
                (rows, tile),
                functools.partial(
                    lambda first, j: (0, jnp.clip(j - first, 0, steps - 1)), i * steps
                ),
            )
        )
    column = lambda j: (0, j)
    more = [] if got is None else [got]
    sizes = [half >> bits]
    for p in range(bits):
        sizes += [sizes[0], ((1 << p) - 1) * sizes[0]] if p else [sizes[0]]
    return chain.call(
        functools.partial(grad_body, parts, len(more), blocks, steps),
        (parts * steps,),
        ins + [pl.BlockSpec((half, tile), column)] * len(more),
        [pl.BlockSpec((size, tile), column) for size in sizes],
        [((size, parts * width), BF16) for size in sizes],
        flops=2 * rows * half * width * parts,
        scratch=[pltpu.VMEM((half, rows), BF16)],
        moved=2 * (rows * half + parts * (rows + half) * width),
    )(*lefts, *rights, *more)


def causal(scores):
    past = scores.shape[0] - HALF_SEQ
    key = lax.broadcasted_iota(jnp.int32, (HALF_SEQ, HALF_SEQ), 0)
    query = lax.broadcasted_iota(jnp.int32, (HALF_SEQ, HALF_SEQ), 1)
    last = jnp.where(key <= query, scores[past:], -1e30)
    return last if past == 0 else jnp.concatenate([scores[:past], last], axis=0)


def head_of(h):
    return slice(h * HEAD_DIM, (h + 1) * HEAD_DIM)


def span_of(b):
    return slice(b * HALF_SEQ, (b + 1) * HALF_SEQ)


def in_place(shift_ref, ref, count):
    rows = SEQ // count
    spans = [pl.ds(pl.multiple_of((i ^ shift_ref[0]) * rows, rows), rows) for i in range(count)]
    return jnp.concatenate([ref[span, :] for span in spans], axis=0)


def put_back(shift_ref, ref, count, values):
    rows = SEQ // count
    for i in range(count):
        ref[pl.ds(pl.multiple_of((i ^ shift_ref[0]) * rows, rows), rows), :] = values[cut(rows, i)]


def one_head(values, h):
    lane = lax.broadcasted_iota(jnp.int32, values.shape, 1)
    return jnp.where(lane // HEAD_DIM == h, values, jnp.zeros_like(values))


def attend_body(count, shift_ref, q_ref, k_ref, v_ref, out_ref, sum_ref):
    queries, keys = in_place(shift_ref, q_ref, count), in_place(shift_ref, k_ref, count)
    values = in_place(shift_ref, v_ref, count).astype(F32).T.astype(BF16)
    heads = []
    for h in range(q_ref.shape[1] // HEAD_DIM):
        blocks = []
        for b in range(2):
            reach = (b + 1) * HALF_SEQ
            query = one_head(queries[span_of(b)] * BF16(FACTOR), h)
            scores = causal(nt(keys[:reach], query))
            top = jnp.max(scores, axis=0, keepdims=True)
            expo = jnp.exp(scores - top)
            total = jnp.sum(expo, axis=0, keepdims=True)
            mixed = nn(values[head_of(h), :reach], expo.astype(BF16))
            blocks.append(mixed * (1.0 / total))
            sum_ref[0, h, :, span_of(b)] = top + jnp.log(total)
        heads.append(jnp.concatenate(blocks, axis=1))
    put_back(shift_ref, out_ref, count, jnp.concatenate(heads, axis=0).T.astype(BF16))


def attention_specs(rows, width, wide):
    wide = min(wide, width)
    tile = pl.BlockSpec((SEQ, wide), lambda s, p, _: (s, p))
    sums = pl.BlockSpec((1, wide // HEAD_DIM, 1, SEQ), lambda s, p, _: (s, p, 0, 0))
    return (rows // SEQ, width // wide), tile, sums


def attend(chain, shift, count, query, key, value):
    rows, width = query.shape
    grid, tile, sums = attention_specs(rows, width, 256)
    return chain.call(
        functools.partial(attend_body, count),
        grid,
        [tile] * 3,
        [tile, sums],
        [((rows, width), BF16), ((rows // SEQ, width // HEAD_DIM, 1, SEQ), F32)],
        flops=16 * rows * width * SEQ,
        prefetch=1,
        moved=8 * rows * width,
    )(shift, query, key, value)


def attend_back_body(
    count, shift_ref, q_ref, k_ref, v_ref, g_ref, sum_ref, cos_ref, sin_ref, dq_ref, dk_ref, dv_ref
):
    queries, keys, values, grads = (
        in_place(shift_ref, ref, count) for ref in (q_ref, k_ref, v_ref, g_ref)
    )
    turned = keys.astype(F32).T.astype(BF16)
    dq_heads = []
    dk, dv = [], []
    for b in range(2):
        reach = (b + 1) * HALF_SEQ
        dq, dk_sum, dv_sum = [], None, None
        for h in range(q_ref.shape[1] // HEAD_DIM):
            query = one_head(queries[span_of(b)], h)
            grad = one_head(grads[span_of(b)], h)
            scores = causal(nt(keys[:reach], query * BF16(FACTOR)))
            probs = jnp.exp(scores - sum_ref[0, h, :, span_of(b)])
            probs_grad = nt(values[:reach], grad)
            inner = jnp.sum(probs * probs_grad, axis=0, keepdims=True)
            score_grad = (probs * (probs_grad - inner)).astype(BF16)
            dv_part, dk_part = nn(probs.astype(BF16), grad), nn(score_grad, query)
            dv_sum = dv_part if dv_sum is None else dv_sum + dv_part
            dk_sum = dk_part if dk_sum is None else dk_sum + dk_part
            dq.append(nn(turned[head_of(h), :reach], score_grad))
        dq_heads.append(jnp.concatenate(dq, axis=0))
        dk.append(dk_sum)
        dv.append(dv_sum)

    def whole_rows(parts):
        early, late = parts
        return jnp.concatenate([late[:HALF_SEQ] + early, late[HALF_SEQ:]], axis=0)

    dq = jnp.concatenate(dq_heads, axis=1).T * FACTOR
    dk = whole_rows(dk) * FACTOR
    dv = whole_rows(dv).astype(BF16)
    copies = dq.shape[1] // PAIR
    cosine = jnp.concatenate([cos_ref[...]] * copies, axis=1)
    sine = jnp.concatenate([sin_ref[...]] * copies, axis=1)
    put_back(shift_ref, dq_ref, count, (dq * cosine - turn(dq) * sine).astype(BF16))
    put_back(shift_ref, dk_ref, count, (dk * cosine - turn(dk) * sine).astype(BF16))
    put_back(shift_ref, dv_ref, count, dv)


def attend_back(chain, shift, count, query, key, value, grad, logsum, tables):
    rows, width = query.shape
    grid, tile, sums = attention_specs(rows, width, PAIR)
    return chain.call(
        functools.partial(attend_back_body, count),
        grid,
        [tile] * 4 + [sums] + [whole((SEQ, PAIR))] * 2,
        [tile] * 3,
        [((rows, width), BF16)] * 3,
        flops=40 * rows * width * SEQ,
        prefetch=1,
        moved=14 * rows * width,
    )(shift, query, key, value, grad, logsum, *tables)


def local(
    chips,
    group,
    tokens,
    attn_gain,
    query_weight,
    key_weight,
    value_weight,
    output_weight,
    ffn_gain,
    gate_weight,
    up_weight,
    down_weight,
    cotangent,
):
    line = jnp.asarray(chips.table)[lax.axis_index("dp")]
    rows, model = tokens.shape
    count = SEQ // rows
    shift = lax.axis_index("tensor") % count
    row = jnp.arange(SEQ, dtype=jnp.int32)
    places = rope_tables(row)
    tables = rope_tables((row // rows ^ shift) * rows + row % rows)
    shift = jnp.reshape(shift, (1,)).astype(jnp.int32)
    early = (*places, *tables, line, shift)
    depth, own = query_weight.shape
    hidden_units = gate_weight.shape[1]
    chain = Chain()

    def gather(piece):
        return Gather(chips, chain, chain.join(piece)[0])

    def spread_of(values):
        return Spread(group, chain, chain.join(values)[0])

    def fold_of(part):
        own_part, sent = part
        sent = chain.join(*sent[0], *sent[1])
        return Fold(group, chain, own_part, [sent[: group.bits], sent[group.bits :]])

    def grads_of(left, rights, theirs=None):
        if theirs is None:
            (theirs,) = weight_grads(chain, left, 1, rights)
        got = [None]
        chain.ask(theirs, got, 0, chips.other)

        def mine(**how):
            if got[0] is None:
                chain.flush()
            blocks = weight_grads(chain, left, 0, rights, got[0], chips.bits)
            return Sums(chips, chain, blocks, **how)

        return mine

    extra = jnp.concatenate([attn_gain, ffn_gain, jnp.zeros((4 * own - 2 * depth,), BF16)])
    attn = jnp.concatenate([query_weight, key_weight, value_weight, output_weight.T], axis=1)
    attn = gather(jnp.concatenate([attn, jnp.broadcast_to(extra, (16, 4 * own))], axis=0))
    spread = spread_of(tokens)
    grads_spread = spread_of(cotangent)
    grads_spread.later = []
    down_turned, *early = chain.join(down_weight.T, *early)
    places, tables, line, shift = early[:2], early[2:4], early[4], early[5]
    chain.end(attn, spread, grads_spread)
    chain.end(attn, spread)
    all_tokens = spread.blocks()
    attn = attn.pieces()
    pair = gather(jnp.concatenate([gate_weight, up_weight], axis=1))
    w_query, w_key, w_value, w_output = [Weight(attn, depth, i * own, own) for i in range(4)]
    gains = jnp.concatenate(
        [piece[depth : depth + 1, : 2 * depth].reshape(2, depth) for piece in attn], axis=1
    ).astype(F32)

    group_one = ordered(chain, norm_body, line, gains, all_tokens)
    grads_spread.resume()
    query, key, value = project(chain, group_one, tables, w_query, w_key, w_value)
    mixed, logsum = attend(chain, shift, count, query, key, value)
    out_part = times_trans(chain, [(mixed, w_output)], group)
    fold = fold_of(out_part)
    chain.end(fold, pair, grads_spread)
    grad_rows = ordered(chain, order_body, line, gains, grads_spread.blocks())
    chain.end(fold)
    attended = fold.total()
    middle, second = by_rows(
        chain, middle_body, line, tokens, gains, attended, [], [F32, BF16]
    )
    spread = spread_of(second)
    chain.end(spread, pair)
    pair = pair.pieces()
    down = gather(down_turned)
    chain.end(spread)
    group_two = spread.blocks()
    w_gate = Weight(pair, depth, 0, hidden_units)
    w_up = Weight(pair, depth, hidden_units, hidden_units)
    hidden, slope, silu, theirs = gate_up(chain, group_two, w_gate, w_up, grad_rows)

    mine = grads_of(grad_rows, [hidden], theirs)
    chain.end(down)
    chain.flush()
    down_sum = mine()
    w_down = Weight(down.pieces(), depth, 0, hidden_units)
    gate_grad, up_grad, gate_theirs, up_theirs = hidden_back(
        chain, grad_rows, w_down, slope, silu, group_two
    )
    mine_gate = grads_of(group_two, [gate_grad], gate_theirs)
    chain.end(down_sum)
    second_part = times_trans(chain, [(gate_grad, w_gate), (up_grad, w_up)], group)
    fold = fold_of(second_part)
    gate_sum = mine_gate(hold=True)
    result_part = times_trans(chain, [(hidden, w_down)], group)
    chain.end(down_sum)
    (down_sum,) = finish(chain, down_sum.terms())
    mine_up = grads_of(group_two, [up_grad], up_theirs)
    chain.end(fold)
    up_sum = mine_up(hold=True)
    chain.end(fold)
    second_grad = fold.total()
    middle_grad, low_grad = by_rows(
        chain, second_back_body, line, cotangent, gains, second_grad, [middle], [F32, BF16]
    )
    spread = spread_of(low_grad)
    chain.end(gate_sum)
    gate_sum.resume()
    chain.end(up_sum, spread)
    chain.end(spread)
    attn_grads = spread.blocks()

    mixed_grad = mixed_back(chain, attn_grads, w_output)
    query_back, key_back, value_back = attend_back(
        chain, shift, count, query, key, value, mixed_grad, logsum, places
    )
    mine_qkv = grads_of(group_one, [query_back, key_back, value_back])
    mine_out = grads_of(attn_grads, [mixed])
    chain.end(gate_sum)
    up_sum.resume()
    fold = fold_of(result_part)
    qkv_sum = mine_qkv()
    first_part = times_trans(
        chain, [(query_back, w_query), (key_back, w_key), (value_back, w_value)], group
    )
    out_sum = mine_out(hold=True)
    gate_sum, gate_inner = finish(chain, gate_sum.terms(), [gate_weight])
    chain.end(up_sum, fold)
    chain.end(qkv_sum, out_sum, fold)
    result_part = fold.total()
    fold = fold_of(first_part)
    out_sum.resume()
    up_sum, up_inner = finish(chain, up_sum.terms(), [up_weight])
    (layer_out,) = by_rows(chain, result_body, line, middle, gains, result_part, [], [BF16])
    chain.end(fold)
    chain.end(fold)
    chain.end(qkv_sum)
    query_sum, key_sum, value_sum, qkv_inner = finish(
        chain, qkv_sum.terms(), [query_weight, key_weight, value_weight]
    )
    gain_parts = jnp.stack(
        [qkv_inner / attn_gain.astype(F32), (gate_inner + up_inner) / ffn_gain.astype(F32)]
    )
    (gain_parts,) = chain.join(gain_parts)
    first_grad = fold.total()
    (input_grad,) = by_rows(
        chain, first_back_body, line, tokens, gains, first_grad, [middle_grad], [F32]
    )
    (out_sum,) = finish(chain, out_sum.terms())
    gain_totals = gain_parts
    for k in range(1, group.size):
        pairs = [(i, i ^ k) for i in range(group.size)]
        gain_totals += lax.ppermute(gain_parts, "tensor", pairs)
    gain_one_total, gain_two_total = gain_totals[0], gain_totals[1]
    return (
        layer_out,
        input_grad,
        gain_one_total,
        query_sum,
        key_sum,
        value_sum,
        out_sum,
        gain_two_total,
        gate_sum,
        up_sum,
        down_sum,
    )


def solution(mesh):
    in_specs = (
        P(("dp", "tensor"), None),
        P("dp"),
        P("dp", "tensor"),
        P("dp", "tensor"),
        P("dp", "tensor"),
        P("tensor", "dp"),
        P("dp"),
        P("dp", "tensor"),
        P("dp", "tensor"),
        P("tensor", "dp"),
        P(("dp", "tensor"), None),
    )
    out_specs = (
        P(("dp", "tensor"), None),
        P(("dp", "tensor"), None),
        P("dp"),
        P("dp", "tensor"),
        P("dp", "tensor"),
        P("dp", "tensor"),
        P("tensor", "dp"),
        P("dp"),
        P("dp", "tensor"),
        P("dp", "tensor"),
        P("tensor", "dp"),
    )
    chips = Chips(mesh.shape["dp"])
    size = mesh.shape["tensor"]
    links = [[(i, i ^ 1 << b) for i in range(size)] for b in range(size.bit_length() - 1)]
    group = Group(links, "tensor")

    def run(*arrays):
        return local(chips, group, *arrays)

    return jax.shard_map(run, mesh=mesh, in_specs=in_specs, out_specs=out_specs, check_vma=False)
```

```python
import functools

import jax
import jax.numpy as jnp
import numpy as np
from jax import lax
from jax.experimental import pallas as pl
from jax.experimental.pallas import tpu as pltpu
from jax.sharding import PartitionSpec as P

HEAD_DIM = 64
SEQ = 512
EPS = 1e-05
THETA = 130000.0
BF16 = jnp.bfloat16
F32 = jnp.float32
FACTOR = HEAD_DIM**-0.5
PAIR = 2 * HEAD_DIM
HALF_SEQ = SEQ // 2
VMEM_LIMIT = 58 << 20
COST_SHARE = 4096


class Chain:
    def __init__(self):
        self.token = jnp.zeros((8, 128), F32)
        self.swaps, self.asked = [], []

    def join(self, *values):
        *values, self.token = lax.optimization_barrier((*values, self.token))
        return values

    def gate(self, *values):
        swaps, self.swaps = self.swaps, []
        asked, self.asked = self.asked, []
        joined = self.join(
            *values, *[held[i] for held, i in swaps], *[source for source, _, _, _ in asked]
        )
        for (held, i), value in zip(swaps, joined[len(values) :]):
            held[i] = value
        for (_, held, i, swap), value in zip(asked, joined[len(values) + len(swaps) :]):
            held[i] = swap(value)
            self.swaps.append((held, i))
        return joined[: len(values)]

    def end(self, *transfers):
        counts = [len(t.flying) for t in transfers]
        got = self.gate(*[value for t in transfers for value in t.flying])
        for t, count in zip(transfers, counts):
            if count:
                t.go_on(got[:count])
            got = got[count:]

    def ask(self, source, held, i, swap):
        self.asked.append((source, held, i, swap))

    def flush(self):
        for source, held, i, swap in self.asked:
            held[i] = swap(source)
        self.asked = []

    def call(self, body, grid, ins, outs, shapes, flops, scratch=(), prefetch=0, moved=0):
        first = prefetch + len(ins)
        second = first + 1 + len(outs)
        anywhere = pl.BlockSpec(memory_space=pl.ANY)

        def wrapped(*refs):
            body(*refs[:first], *refs[first + 1 : second], *refs[second + 1 :])

        run = pl.pallas_call(
            wrapped,
            grid_spec=pltpu.PrefetchScalarGridSpec(
                num_scalar_prefetch=prefetch,
                grid=grid,
                in_specs=[*ins, anywhere],
                out_specs=[*outs, anywhere],
                scratch_shapes=list(scratch),
            ),
            out_shape=[jax.ShapeDtypeStruct(s, t) for s, t in [*shapes, ((8, 128), F32)]],
            compiler_params=pltpu.CompilerParams(
                vmem_limit_bytes=VMEM_LIMIT, dimension_semantics=("arbitrary",) * len(grid)
            ),
            cost_estimate=pl.CostEstimate(
                flops=flops // COST_SHARE, bytes_accessed=moved // COST_SHARE, transcendentals=0
            ),
        )

        def with_token(*args):
            *results, self.token = run(*args, self.token)
            return results

        return with_token


class Chips:
    def __init__(self, size):
        self.bits = (size // 2).bit_length() - 1
        self.size = size
        self.swap = [(i, i ^ 1) for i in range(size)]
        self.links = [
            [(i, i ^ 2 << self.bits - 1 - p) for i in range(size)] for p in range(self.bits)
        ]
        flips = [
            sum(1 << self.bits - 1 - p for p in range(self.bits) if v >> p & 1)
            for v in range(1 << self.bits)
        ]
        table = [[i ^ 2 * f for f in flips] + [i ^ 2 * f ^ 1 for f in flips] for i in range(size)]
        self.table = np.array(table, np.int32)

    def send(self, value, p):
        return lax.ppermute(value, "dp", self.links[p])

    def other(self, value):
        return lax.ppermute(value, "dp", self.swap)


class Gather:
    def __init__(self, chips, chain, piece):
        self.chips, self.chain = chips, chain
        self.own = [piece] + [None] * (2**chips.bits - 1)
        self.others = list(self.own)
        self.ask(0)
        self.keys = [1 << p for p in range(chips.bits)]
        self.flying = [chips.send(piece, p) for p in range(chips.bits)]

    def ask(self, v):
        self.chain.ask(self.own[v], self.others, v, self.chips.other)

    def go_on(self, got):
        keys, self.keys, self.flying = self.keys, [], []
        for v, piece in zip(keys, got):
            self.own[v] = piece
            for p in range(v.bit_length(), self.chips.bits):
                self.keys.append(v | 1 << p)
                self.flying.append(self.chips.send(piece, p))
        for v in keys:
            self.ask(v)

    def pieces(self):
        while self.flying:
            self.chain.end(self)
        self.chain.flush()
        return self.own + self.others


class Sums:
    def __init__(self, chips, chain, mine, apart=False, hold=False, cut_in_two=False):
        self.chips, self.chain, self.apart, self.hold = chips, chain, apart, hold
        self.todo = []
        self.cut_in_two = cut_in_two and chips.bits == 2
        self.parts = [mine[0]]
        mine = list(mine[1:])
        self.direct, self.passed = [], []
        for p in range(chips.bits):
            self.direct.append(mine.pop(0))
            self.passed.append(mine.pop(0) if p else None)
        self.p = chips.bits - 1
        if self.cut_in_two:
            self.kinds = [0, 1]
            self.flying = [chips.send(half, 1) for half in self.in_two(self.passed[1])]
            return
        self.kinds = [self.p]
        self.flying = [chips.send(self.passed[self.p], self.p)]

    def in_two(self, values):
        width = values.shape[1] // 2
        return values[:, :width], values[:, width:]

    def go_on(self, got):
        rows = self.parts[0].shape[0]
        kinds, self.kinds, self.flying = self.kinds, [], []
        if self.p == 0:
            self.parts += got
            return
        if self.cut_in_two:
            self.p = 0
            total = self.direct[0].astype(F32) + jnp.concatenate(got, axis=1).astype(F32)
            self.todo = [(None, self.direct[1], 1), (None, total.astype(BF16), 0)]
            self.resume()
            return
        for kind, block in zip(kinds, got):
            if kind is None:
                self.parts.append(block)
                continue
            add = lambda held, first: (
                held.astype(F32) + block[first * rows : first * rows + held.shape[0]].astype(F32)
            ).astype(BF16)
            for q in range(kind):
                self.direct[q] = add(self.direct[q], (1 << q) - 1)
                if q:
                    self.passed[q] = add(self.passed[q], 1 << q)
        p, self.p = self.p, self.p - 1
        if p > 0:
            self.todo.append((None, self.direct[p], p))
        if p > 1:
            self.todo.append((p - 1, self.passed[p - 1], p - 1))
        if p == 1 and not self.apart:
            self.todo.append((None, self.direct[0], 0))
        if not self.hold:
            self.resume()

    def resume(self):
        todo, self.todo = self.todo, []
        values = self.chain.join(*[value for _, value, _ in todo])
        for (kind, _, p), value in zip(todo, values):
            self.kinds.append(kind)
            self.flying.append(self.chips.send(value, p))

    def send_half(self, i):
        while self.p > 0:
            self.chain.end(self)
        width = self.direct[0].shape[1] // 2
        (value,) = self.chain.join(self.direct[0][:, i * width : (i + 1) * width])
        self.kinds.append(None)
        self.flying.append(self.chips.send(value, 0))

    def terms(self):
        while self.flying or self.todo:
            if self.todo:
                self.resume()
            self.chain.end(self)
        return sorted(self.parts, key=lambda part: -part.shape[1])


class Group:
    def __init__(self, links, axes):
        self.links, self.axes = links, axes
        self.bits = len(links)
        self.size = 1 << self.bits
        self.orders = (list(range(self.bits)), list(range(self.bits))[::-1])

    def send(self, value, bit):
        return lax.ppermute(value, self.axes, self.links[bit])

    def messages(self):
        found = []
        for order in self.orders:
            found.append([])
            for top in reversed(range(self.bits)):
                found[-1].append(
                    [
                        1 << order[top] | sum(1 << order[p] for p in range(top) if v >> p & 1)
                        for v in range(1 << top)
                    ]
                )
        return found


class Spread:
    def __init__(self, group, chain, rows):
        self.group, self.chain = group, chain
        self.held = {0: [rows]}
        self.later = None
        self.keys = [(1 << b, None) for b in range(group.bits)]
        self.flying = [group.send(rows, b) for b in range(group.bits)]

    def go_on(self, got):
        fresh = list(zip(self.keys, got))
        self.keys, self.flying = [], []
        for (k, h), block in fresh:
            if h is None:
                self.held[k] = [block]
            else:
                self.held.setdefault(k, [None, None])[h] = block
        for (k, h), block in fresh:
            for way, order in enumerate(self.group.orders):
                if h is not None and h != way:
                    continue
                half = block.shape[1] // 2
                top = max(i for i, bit in enumerate(order) if k >> bit & 1)
                for i in range(top + 1, len(order)):
                    part = block if h is not None else block[:, way * half : (way + 1) * half]
                    self.keys.append((k | 1 << order[i], way))
                    if self.later is not None:
                        self.later.append((part, order[i]))
                    else:
                        self.flying.append(self.group.send(part, order[i]))

        if self.later:
            parts = self.chain.join(*[part for part, _ in self.later])
            self.later = [(part, bit) for part, (_, bit) in zip(parts, self.later)]

    def resume(self):
        later, self.later = self.later, None
        parts = self.chain.join(*[part for part, _ in later])
        self.flying = [self.group.send(part, bit) for part, (_, bit) in zip(parts, later)]

    def blocks(self):
        while self.flying:
            self.chain.end(self)
        return [self.held[k] for k in range(self.group.size)]


class Fold:
    def __init__(self, group, chain, own, sent):
        self.group, self.chain = group, chain
        self.rows = own[0].shape[0]
        self.sent = [list(half) for half in sent]
        self.parts = [[half] for half in own]
        self.wave = 0
        self.start()

    def start(self):
        self.flying = [
            self.group.send(self.sent[h][self.wave], order[self.group.bits - 1 - self.wave])
            for h, order in enumerate(self.group.orders)
        ]

    def go_on(self, got):
        self.wave += 1
        self.flying = []
        for h, block in enumerate(got):
            self.parts[h].append(block)
        for wave in range(self.wave, self.group.bits):
            sums = add_rows(self.chain, [sent[wave] for sent in self.sent], got)
            for sent, value in zip(self.sent, sums):
                sent[wave] = value
        if self.wave < self.group.bits:
            self.start()

    def total(self):
        while self.flying:
            self.chain.end(self)
        return self.parts


class Weight:
    def __init__(self, pieces, rows, start, width):
        self.pieces, self.rows, self.start, self.width = pieces, rows, start, width
        self.model = len(pieces) * rows

    def tiles(self, tile):
        first = self.start // tile
        return [pl.BlockSpec((self.rows, tile), lambda j: (0, first + j))] * len(self.pieces)


def nn(left, right):
    return lax.dot_general(left, right, (((1,), (0,)), ((), ())), preferred_element_type=F32)


def nt(left, right):
    return lax.dot_general(left, right, (((1,), (1,)), ((), ())), preferred_element_type=F32)


def tn(left, right):
    return lax.dot_general(left, right, (((0,), (0,)), ((), ())), preferred_element_type=F32)


def whole(shape):
    return pl.BlockSpec(shape, lambda *_: (0,) * len(shape))


def place(line_ref, j, width):
    return pl.ds(pl.multiple_of(line_ref[j] * width, 128), width)


def cut(width, j):
    return slice(j * width, (j + 1) * width)


def scale_of(values):
    return lax.rsqrt(jnp.mean(values * values, axis=-1, keepdims=True) + EPS)


def fetch_blocks(counts, refs, held, sems, k, slot, wait):
    first = 0
    for i, count in enumerate(counts):
        copies = []
        half = held.shape[2] // count
        for h in range(count):
            target = held.at[slot, :, pl.ds(h * half, half)]
            copies.append(pltpu.make_async_copy(refs[first + h], target, sems.at[slot, h]))
        first += count

        @pl.when(k == i)
        def _():
            for copy in copies:
                copy.wait() if wait else copy.start()


def fetched(counts, refs, held, sems):
    k = pl.program_id(0)

    @pl.when(k == 0)
    def _():
        fetch_blocks(counts, refs, held, sems, k, 0, False)

    fetch_blocks(counts, refs, held, sems, k + 1, (k + 1) % 2, False)
    fetch_blocks(counts, refs, held, sems, k, k % 2, True)
    return held.at[k % 2]


def norm_body(blocks, counts, line_ref, gain_ref, *refs):
    out_ref, held, sems = refs[sum(counts) :]
    x_ref = fetched(counts, refs, held, sems)
    width = out_ref.shape[1] // blocks
    scale = scale_of(x_ref[...].astype(F32))
    for j in range(blocks):
        part = x_ref[:, place(line_ref, j, width)].astype(F32)
        gain = gain_ref[0:1, cut(width, j)]
        out_ref[:, cut(width, j)] = (part * scale * gain).astype(BF16)


def order_body(blocks, counts, line_ref, gain_ref, *refs):
    out_ref, held, sems = refs[sum(counts) :]
    x_ref = fetched(counts, refs, held, sems)
    width = out_ref.shape[1] // blocks
    for j in range(blocks):
        out_ref[:, cut(width, j)] = x_ref[:, place(line_ref, j, width)]


def ordered(chain, body, line, gains, held):
    counts = [len(block) for block in held]
    rows, model = held[0][0].shape
    n = len(held)
    return chain.call(
        functools.partial(body, line.shape[0], counts),
        (n,),
        [whole(gains.shape)] + [pl.BlockSpec(memory_space=pl.ANY)] * sum(counts),
        [pl.BlockSpec((rows, model), lambda k, *_: (k, 0))],
        [((n * rows, model), BF16)],
        flops=20 * n * rows * model,
        scratch=[pltpu.VMEM((2, rows, model), BF16), pltpu.SemaphoreType.DMA((2, 2))],
        prefetch=1,
        moved=4 * n * rows * model,
    )(line, gains, *[array for block in held for array in block])[0]


def added(refs, span):
    total = refs[0][span, :].astype(F32)
    for ref in refs[1:]:
        total += ref[span, :].astype(F32)
    return total


def middle_body(blocks, m, line_ref, x_ref, gain_ref, *refs):
    middle_ref, out_ref = refs[2 * m :]
    width = x_ref.shape[1] // blocks
    half = x_ref.shape[1] // 2
    span = slice(None)
    middle_ref[:, :half] = added(refs[:m], span)
    middle_ref[:, half:] = added(refs[m : 2 * m], span)
    for j in range(blocks):
        here = x_ref[:, place(line_ref, j, width)].astype(F32)
        middle_ref[:, cut(width, j)] += here
    middle = middle_ref[...]
    out_ref[...] = (middle * scale_of(middle) * gain_ref[1:2, :]).astype(BF16)


def result_body(blocks, m, line_ref, middle_ref, gain_ref, *refs):
    out_ref = refs[2 * m]
    width = middle_ref.shape[1] // blocks
    span = slice(None)
    total = middle_ref[...] + jnp.concatenate(
        [added(refs[:m], span), added(refs[m : 2 * m], span)], axis=1
    )
    for j in range(blocks):
        out_ref[:, place(line_ref, j, width)] = total[:, cut(width, j)].astype(BF16)


def second_back_body(blocks, m, line_ref, dy_ref, gain_ref, *refs):
    middle_ref, out_ref, low_ref = refs[2 * m :]
    width = dy_ref.shape[1] // blocks
    span = slice(None)
    grad = jnp.concatenate([added(refs[:m], span), added(refs[m : 2 * m], span)], axis=1)
    middle = middle_ref[...]
    scale = scale_of(middle)
    normed = middle * scale
    scaled = grad * gain_ref[1:2, :]
    out_ref[...] = scale * (scaled - normed * jnp.mean(scaled * normed, axis=-1, keepdims=True))
    for j in range(blocks):
        out_ref[:, cut(width, j)] += dy_ref[:, place(line_ref, j, width)].astype(F32)
    low_ref[...] = out_ref[...].astype(BF16)


def first_back_body(blocks, m, line_ref, x_ref, gain_ref, *refs):
    above_ref, out_ref = refs[2 * m :]
    width = x_ref.shape[1] // blocks
    span = slice(None)
    scale = scale_of(x_ref[...].astype(F32))
    normed = jnp.concatenate(
        [x_ref[:, place(line_ref, j, width)].astype(F32) for j in range(blocks)], axis=1
    ) * scale
    grad = jnp.concatenate([added(refs[:m], span), added(refs[m : 2 * m], span)], axis=1)
    scaled = grad * gain_ref[0:1, :]
    back = scale * (scaled - normed * jnp.mean(scaled * normed, axis=-1, keepdims=True))
    total = above_ref[...] + back
    for j in range(blocks):
        out_ref[:, place(line_ref, j, width)] = total[:, cut(width, j)]


def by_rows(chain, body, line, first, gains, parts, more, kinds):
    rows, model = first.shape
    half = model // 2
    tile = min(128, rows)
    row = pl.BlockSpec((tile, model), lambda i, *_: (i, 0))
    slim = pl.BlockSpec((tile, half), lambda i, *_: (i, 0))
    m = len(parts[0])
    return chain.call(
        functools.partial(body, line.shape[0], m),
        (rows // tile,),
        [row, whole(gains.shape)] + [slim] * (2 * m) + [row] * len(more),
        [row] * len(kinds),
        [((rows, model), kind) for kind in kinds],
        flops=20 * rows * model,
        prefetch=1,
        moved=rows * model * (2 * m + 4 * len(kinds)),
    )(line, first, gains, *parts[0], *parts[1], *more)


def add_rows_body(count, *refs):
    for i in range(count):
        total = refs[i][...].astype(F32) + refs[count + i][...].astype(F32)
        refs[2 * count + i][...] = total.astype(BF16)


def add_rows(chain, helds, blocks):
    rows, columns = helds[0].shape
    tile = min(128, rows)
    steps = rows // tile
    count = len(helds)
    here = pl.BlockSpec((tile, columns), lambda i: (i, 0))
    return chain.call(
        functools.partial(add_rows_body, count),
        (steps,),
        [here] * count + [pl.BlockSpec((tile, columns), lambda i: (steps + i, 0))] * count,
        [here] * count,
        [((rows, columns), BF16)] * count,
        flops=count * rows * columns,
        moved=6 * count * rows * columns,
    )(*helds, *blocks)


def finish_body(m, halves, n, *refs):
    total = added(refs[:m], slice(None))
    if halves:
        total += jnp.concatenate([ref[...].astype(F32) for ref in refs[m : m + halves]], axis=1)
    m += halves
    weights, outs = refs[m : m + n], refs[m + n :]
    if not n:
        outs[0][...] = total.T
        return
    width = weights[0].shape[1]
    inner = jnp.zeros((total.shape[0], 1), F32)
    for i in range(n):
        part = total[:, cut(width, i)]
        outs[i][...] = part
        inner += jnp.sum(weights[i][...].astype(F32) * part, axis=1, keepdims=True)
    outs[n][...] = jnp.broadcast_to(inner, outs[n].shape)


def finish(chain, terms, weights=()):
    rows, columns = terms[0].shape
    tile = min(128, rows)
    row = pl.BlockSpec((tile, columns), lambda i: (i, 0))
    n = len(weights)
    halves = sum(1 for term in terms if term.shape[1] < columns)
    half = [pl.BlockSpec((tile, columns // 2), lambda i: (i, 0))] * halves
    if n:
        slim = pl.BlockSpec((tile, columns // n), lambda i: (i, 0))
        outs = [slim] * n + [pl.BlockSpec((tile, 128), lambda i: (i, 0))]
        shapes = [((rows, columns // n), F32)] * n + [((rows, 128), F32)]
    else:
        slim = None
        outs = [pl.BlockSpec((columns, tile), lambda i: (0, i))]
        shapes = [((columns, rows), F32)]
    results = chain.call(
        functools.partial(finish_body, len(terms) - halves, halves, n),
        (rows // tile,),
        [row] * (len(terms) - halves) + half + [slim] * n,
        outs,
        shapes,
        flops=4 * rows * columns,
        moved=rows * columns * 12,
    )(*terms, *weights)
    if n:
        results[n] = results[n][:, 0]
    return results


def rope_tables(place):
    half = HEAD_DIM // 2
    freq = THETA ** (-2.0 * jnp.arange(half, dtype=F32) / HEAD_DIM)
    angle = place.astype(F32)[:, None] * freq[None, :]
    cosine, sine = jnp.cos(angle), jnp.sin(angle)
    return (
        jnp.concatenate([cosine] * (PAIR // half), axis=1),
        jnp.concatenate([-sine, sine] * (PAIR // HEAD_DIM), axis=1),
    )


def turn(values):
    half = HEAD_DIM // 2
    width = values.shape[-1]
    lane = lax.broadcasted_iota(jnp.int32, values.shape, 1) % HEAD_DIM
    return jnp.where(
        lane < half, pltpu.roll(values, width - half, 1), pltpu.roll(values, half, 1)
    )


def joined(refs):
    return jnp.concatenate([r[...] for r in refs], axis=0)


def qkv_body(n, x_ref, cos_ref, sin_ref, *refs):
    weights, outs = refs[: 3 * n], refs[3 * n :]
    rows = x_ref.shape[0]
    tile = outs[0].shape[1]
    for i in range(3):
        weight = joined(weights[i * n : (i + 1) * n])
        for s in range(rows // SEQ):
            span = slice(s * SEQ, (s + 1) * SEQ)
            product = nn(x_ref[span, :], weight)
            if i == 2:
                outs[i][span, :] = product.astype(BF16)
                continue
            for t in range(tile // PAIR):
                here = product[:, t * PAIR : (t + 1) * PAIR]
                turned = here * cos_ref[...] + turn(here) * sin_ref[...]
                outs[i][span, t * PAIR : (t + 1) * PAIR] = turned.astype(BF16)


def project(chain, x, tables, query, key, value):
    rows, model = x.shape
    n, width = len(query.pieces), query.width
    tile = min(256, width)
    out = pl.BlockSpec((rows, tile), lambda j: (0, j))
    return chain.call(
        functools.partial(qkv_body, n),
        (width // tile,),
        [whole(x.shape), whole((SEQ, PAIR)), whole((SEQ, PAIR))]
        + query.tiles(tile)
        + key.tiles(tile)
        + value.tiles(tile),
        [out] * 3,
        [((rows, width), BF16)] * 3,
        flops=6 * rows * model * width,
        moved=2 * (rows * model + 3 * model * width + 3 * rows * width),
    )(x, *tables, *query.pieces, *key.pieces, *value.pieces)


def collect(counts, refs, held, sems):
    rows = held.shape[0] // len(counts)
    copies = []
    for k, count in enumerate(counts):
        half = held.shape[1] // count
        for h in range(count):
            target = held.at[pl.ds(k * rows, rows), pl.ds(h * half, half)]
            i = len(copies)
            copies.append(pltpu.make_async_copy(refs[i], target, sems.at[i]))
    for copy in copies:
        copy.start()
    for copy in copies:
        copy.wait()


def gate_body(n, counts, *refs):
    m = sum(counts)
    gate_w, up_w = refs[m : m + n], refs[m + n : m + 2 * n]
    left_ref, hidden_ref, slope_ref, silu_ref, theirs_ref, x_ref, turned, sems = refs[m + 2 * n :]

    @pl.when(pl.program_id(0) == 0)
    def _():
        collect(counts, refs, x_ref, sems)
        turned[...] = left_ref[...].T

    gate_weight, up_weight = joined(gate_w), joined(up_w)
    for s in range(x_ref.shape[0] // SEQ):
        span = slice(s * SEQ, (s + 1) * SEQ)
        gate = nn(x_ref[span, :], gate_weight)
        up = nn(x_ref[span, :], up_weight)
        sigm = jax.nn.sigmoid(gate)
        silu = gate * sigm
        hidden_ref[span, :] = (silu * up).astype(BF16)
        silu_ref[span, :] = silu.astype(BF16)
        slope_ref[span, :] = (up * sigm * (1.0 + gate * (1.0 - sigm))).astype(BF16)
    theirs_ref[...] = nn(turned[...], hidden_ref[...]).astype(BF16)


def collected(held):
    counts = [len(block) for block in held]
    rows, model = held[0][0].shape
    scratch = [
        pltpu.VMEM((len(held) * rows, model), BF16),
        pltpu.SemaphoreType.DMA((sum(counts),)),
    ]
    arrays = [array for block in held for array in block]
    return counts, arrays, [pl.BlockSpec(memory_space=pl.ANY)] * len(arrays), scratch


def gate_up(chain, held, gate, up, grads):
    counts, arrays, specs, scratch = collected(held)
    rows, model = scratch[0].shape
    n, width = len(gate.pieces), gate.width
    tile = min(256, width)
    out = pl.BlockSpec((rows, tile), lambda j: (0, j))
    half = model // 2
    return chain.call(
        functools.partial(gate_body, n, counts),
        (width // tile,),
        specs
        + gate.tiles(tile)
        + up.tiles(tile)
        + [pl.BlockSpec((rows, half), lambda j: (0, 1))],
        [out] * 3 + [pl.BlockSpec((half, tile), lambda j: (0, j))],
        [((rows, width), BF16)] * 3 + [((half, width), BF16)],
        flops=6 * rows * model * width,
        scratch=[scratch[0], pltpu.VMEM((half, rows), BF16), scratch[1]],
        moved=2 * (rows * model + 2 * model * width + 3 * rows * width),
    )(*arrays, *gate.pieces, *up.pieces, grads)


def half_blocks(left, which):
    lefts = [block[0] if len(block) == 1 else block[which] for block in left]
    rows, half = lefts[0].shape[0], left[0][0].shape[1] // 2
    places = [which if len(block) == 1 else 0 for block in left]
    return lefts, [
        pl.BlockSpec((rows, half), functools.partial(lambda at, j: (0, at), at)) for at in places
    ]


def hidden_back_body(n, blocks, g_ref, *refs):
    weights, slope_ref, silu_ref = refs[:n], refs[n], refs[n + 1]
    lefts, refs = refs[n + 2 : n + 2 + blocks], refs[n + 2 + blocks :]
    gate_ref, up_ref, gate_theirs, up_theirs, turned = refs
    rows = turned.shape[1] // blocks

    @pl.when(pl.program_id(0) == 0)
    def _():
        for k in range(blocks):
            turned[:, cut(rows, k)] = lefts[k][...].T

    weight = joined(weights)
    for s in range(g_ref.shape[0] // SEQ):
        span = slice(s * SEQ, (s + 1) * SEQ)
        grad = nn(g_ref[span, :], weight)
        gate_ref[span, :] = (grad * slope_ref[span, :].astype(F32)).astype(BF16)
        up_ref[span, :] = (grad * silu_ref[span, :].astype(F32)).astype(BF16)
    gate_theirs[...] = nn(turned[...], gate_ref[...]).astype(BF16)
    up_theirs[...] = nn(turned[...], up_ref[...]).astype(BF16)


def hidden_back(chain, grads, down, slope, silu, left):
    rows, model = grads.shape
    n, width = len(down.pieces), down.width
    tile = min(256, width)
    out = pl.BlockSpec((rows, tile), lambda j: (0, j))
    lefts, specs = half_blocks(left, 1)
    half = model // 2
    return chain.call(
        functools.partial(hidden_back_body, n, len(lefts)),
        (width // tile,),
        [whole(grads.shape)] + down.tiles(tile) + [out] * 2 + specs,
        [out] * 2 + [pl.BlockSpec((half, tile), lambda j: (0, j))] * 2,
        [((rows, width), BF16)] * 2 + [((half, width), BF16)] * 2,
        flops=4 * rows * model * width,
        scratch=[pltpu.VMEM((half, rows), BF16)],
        moved=2 * (rows * model + model * width + 4 * rows * width),
    )(grads, *down.pieces, slope, silu, *lefts)


def mixed_back_body(n, counts, *refs):
    m = sum(counts)
    out_ref, x_ref, sems = refs[m + n :]

    @pl.when(pl.program_id(0) == 0)
    def _():
        collect(counts, refs, x_ref, sems)

    out_ref[...] = nn(x_ref[...], joined(refs[m : m + n])).astype(BF16)


def mixed_back(chain, held, out):
    counts, arrays, specs, scratch = collected(held)
    rows, model = scratch[0].shape
    n, width = len(out.pieces), out.width
    tile = min(256, width)
    return chain.call(
        functools.partial(mixed_back_body, n, counts),
        (width // tile,),
        specs + out.tiles(tile),
        [pl.BlockSpec((rows, tile), lambda j: (0, j))],
        [((rows, width), BF16)],
        flops=2 * rows * model * width,
        scratch=scratch,
        moved=2 * (rows * model + model * width + rows * width),
    )(*arrays, *out.pieces)[0]


def trans_body(n, starts, targets, *refs):
    parts, blocks = len(starts), len(targets[0])
    lefts = refs[:parts]
    pieces = refs[parts : parts * (n + 1)]
    outs = refs[parts * (n + 1) : -4]
    held, ready, sems, out_sems = refs[-4:]
    j = pl.program_id(0)
    depth, width = held.shape[2:]
    rows = ready.shape[1] // blocks

    def copy(i, p, slot):
        source = pieces[p * n + i].at[pl.ds(0, depth), pl.ds(starts[p], width)]
        return pltpu.make_async_copy(source, held.at[slot, p], sems.at[slot, p])

    def fetch(step, slot):
        for i in range(n):

            @pl.when(step == i)
            def _():
                for p in range(parts):
                    copy(i, p, slot).start()

    def leave(slot, k, array, first, column):
        target = outs[array].at[pl.ds(first, rows), pl.ds(column, depth)]
        source = ready.at[slot, pl.ds(k * rows, rows), :]
        return pltpu.make_async_copy(source, target, out_sems.at[slot, k])

    def left(slot):
        for k in range(blocks):
            leave(slot, k, 0, 0, 0).wait()

    @pl.when(j == 0)
    def _():
        fetch(j, 0)

    @pl.when(j + 1 < n)
    def _():
        fetch(j + 1, (j + 1) % 2)

    slot = j % 2
    for p in range(parts):
        copy(0, p, slot).wait()

    @pl.when(j >= 2)
    def _():
        left(slot)

    for s in range(blocks * rows // SEQ):
        span = slice(s * SEQ, (s + 1) * SEQ)
        total = nt(lefts[0][span, :], held[slot, 0])
        for p in range(1, parts):
            total += nt(lefts[p][span, :], held[slot, p])
        ready[slot, span, :] = total.astype(BF16)
    column = pl.multiple_of(j % (n // 2) * depth, 128)
    for h in range(2):

        @pl.when((j >= n // 2) == (h == 1))
        def _():
            for k, (array, first) in enumerate(targets[h]):
                leave(slot, k, array, first, column).start()

    @pl.when(j == n - 1)
    def _():
        left(1 - slot)
        left(slot)


def times_trans(chain, parts, group):
    weights = [weight for _, weight in parts]
    n, depth, width = len(weights[0].pieces), weights[0].rows, weights[0].width
    rows = parts[0][0].shape[0]
    half = weights[0].model // 2
    size = rows // group.size
    messages = group.messages()
    shapes = [((size, half), BF16)] * 2
    targets = [{0: (0, 0)}, {0: (1, 0)}]
    for h in range(2):
        for keys in messages[h]:
            for i, k in enumerate(keys):
                targets[h][k] = (len(shapes), i * size)
            shapes.append(((len(keys) * size, half), BF16))
    targets = [[t[k] for k in range(group.size)] for t in targets]
    anywhere = pl.BlockSpec(memory_space=pl.ANY)
    outs = chain.call(
        functools.partial(trans_body, n, [weight.start for weight in weights], targets),
        (n,),
        [whole((rows, width))] * len(parts) + [anywhere] * (n * len(parts)),
        [anywhere] * len(shapes),
        shapes,
        flops=4 * rows * half * width * len(parts),
        scratch=[
            pltpu.VMEM((2, len(parts), depth, width), BF16),
            pltpu.VMEM((2, rows, depth), BF16),
            pltpu.SemaphoreType.DMA((2, len(parts))),
            pltpu.SemaphoreType.DMA((2, group.size)),
        ],
        moved=2 * (2 * rows * half + len(parts) * (rows + 2 * half) * width),
    )(*[left for left, _ in parts], *[piece for weight in weights for piece in weight.pieces])
    m = group.bits
    return outs[:2], [outs[2 : 2 + m], outs[2 + m :]]


def grad_body(parts, got, blocks, steps, *refs):
    lefts, refs = refs[:blocks], refs[blocks:]
    rights, refs = refs[:parts], refs[parts:]
    got_ref = refs[0] if got else None
    outs, turned = refs[got:-1], refs[-1]
    j = pl.program_id(0)

    @pl.when(j == 0)
    def _():
        rows = turned.shape[1] // blocks
        for k in range(blocks):
            turned[:, cut(rows, k)] = lefts[k][...].T

    for i in range(parts):

        @pl.when((j >= i * steps) & (j < (i + 1) * steps))
        def _():
            total = nn(turned[...], rights[i][...])
            if got:
                total += got_ref[...].astype(F32)
            total = total.astype(BF16)
            first = 0
            for out_ref in outs:
                count = out_ref.shape[0]
                out_ref[...] = total[first : first + count]
                first += count


def weight_grads(chain, left, which, rights, got=None, bits=0):
    rows, width = rights[0].shape
    parts = len(rights)
    tile = min(512, width)
    steps = width // tile
    lefts, ins = half_blocks(left if isinstance(left, list) else [[left]], which)
    blocks, half = len(lefts), ins[0].block_shape[1]
    for i in range(parts):
        ins.append(
            pl.BlockSpec(
                (rows, tile),
                functools.partial(
                    lambda first, j: (0, jnp.clip(j - first, 0, steps - 1)), i * steps
                ),
            )
        )
    column = lambda j: (0, j)
    more = [] if got is None else [got]
    sizes = [half >> bits]
    for p in range(bits):
        sizes += [sizes[0], ((1 << p) - 1) * sizes[0]] if p else [sizes[0]]
    return chain.call(
        functools.partial(grad_body, parts, len(more), blocks, steps),
        (parts * steps,),
        ins + [pl.BlockSpec((half, tile), column)] * len(more),
        [pl.BlockSpec((size, tile), column) for size in sizes],
        [((size, parts * width), BF16) for size in sizes],
        flops=2 * rows * half * width * parts,
        scratch=[pltpu.VMEM((half, rows), BF16)],
        moved=2 * (rows * half + parts * (rows + half) * width),
    )(*lefts, *rights, *more)


def causal(scores):
    past = scores.shape[0] - HALF_SEQ
    key = lax.broadcasted_iota(jnp.int32, (HALF_SEQ, HALF_SEQ), 0)
    query = lax.broadcasted_iota(jnp.int32, (HALF_SEQ, HALF_SEQ), 1)
    last = jnp.where(key <= query, scores[past:], -1e30)
    return last if past == 0 else jnp.concatenate([scores[:past], last], axis=0)


def head_of(h):
    return slice(h * HEAD_DIM, (h + 1) * HEAD_DIM)


def span_of(b):
    return slice(b * HALF_SEQ, (b + 1) * HALF_SEQ)


def in_place(shift_ref, ref, count):
    rows = SEQ // count
    spans = [pl.ds(pl.multiple_of((i ^ shift_ref[0]) * rows, rows), rows) for i in range(count)]
    return jnp.concatenate([ref[span, :] for span in spans], axis=0)


def put_back(shift_ref, ref, count, values):
    rows = SEQ // count
    for i in range(count):
        ref[pl.ds(pl.multiple_of((i ^ shift_ref[0]) * rows, rows), rows), :] = values[cut(rows, i)]


def one_head(values, h):
    lane = lax.broadcasted_iota(jnp.int32, values.shape, 1)
    return jnp.where(lane // HEAD_DIM == h, values, jnp.zeros_like(values))


def attend_body(count, shift_ref, q_ref, k_ref, v_ref, out_ref, sum_ref):
    queries, keys = in_place(shift_ref, q_ref, count), in_place(shift_ref, k_ref, count)
    values = in_place(shift_ref, v_ref, count).astype(F32).T.astype(BF16)
    heads = []
    for h in range(q_ref.shape[1] // HEAD_DIM):
        blocks = []
        for b in range(2):
            reach = (b + 1) * HALF_SEQ
            query = one_head(queries[span_of(b)] * BF16(FACTOR), h)
            scores = causal(nt(keys[:reach], query))
            top = jnp.max(scores, axis=0, keepdims=True)
            expo = jnp.exp(scores - top)
            total = jnp.sum(expo, axis=0, keepdims=True)
            mixed = nn(values[head_of(h), :reach], expo.astype(BF16))
            blocks.append(mixed * (1.0 / total))
            sum_ref[0, h, :, span_of(b)] = top + jnp.log(total)
        heads.append(jnp.concatenate(blocks, axis=1))
    put_back(shift_ref, out_ref, count, jnp.concatenate(heads, axis=0).T.astype(BF16))


def attention_specs(rows, width, wide):
    wide = min(wide, width)
    tile = pl.BlockSpec((SEQ, wide), lambda s, p, _: (s, p))
    sums = pl.BlockSpec((1, wide // HEAD_DIM, 1, SEQ), lambda s, p, _: (s, p, 0, 0))
    return (rows // SEQ, width // wide), tile, sums


def attend(chain, shift, count, query, key, value):
    rows, width = query.shape
    grid, tile, sums = attention_specs(rows, width, 256)
    return chain.call(
        functools.partial(attend_body, count),
        grid,
        [tile] * 3,
        [tile, sums],
        [((rows, width), BF16), ((rows // SEQ, width // HEAD_DIM, 1, SEQ), F32)],
        flops=16 * rows * width * SEQ,
        prefetch=1,
        moved=8 * rows * width,
    )(shift, query, key, value)


def attend_back_body(
    count, shift_ref, q_ref, k_ref, v_ref, g_ref, sum_ref, cos_ref, sin_ref, dq_ref, dk_ref, dv_ref
):
    queries, keys, values, grads = (
        in_place(shift_ref, ref, count) for ref in (q_ref, k_ref, v_ref, g_ref)
    )
    turned = keys.astype(F32).T.astype(BF16)
    dq_heads = []
    dk, dv = [], []
    for b in range(2):
        reach = (b + 1) * HALF_SEQ
        dq, dk_sum, dv_sum = [], None, None
        for h in range(q_ref.shape[1] // HEAD_DIM):
            query = one_head(queries[span_of(b)], h)
            grad = one_head(grads[span_of(b)], h)
            scores = causal(nt(keys[:reach], query * BF16(FACTOR)))
            probs = jnp.exp(scores - sum_ref[0, h, :, span_of(b)])
            probs_grad = nt(values[:reach], grad)
            inner = jnp.sum(probs * probs_grad, axis=0, keepdims=True)
            score_grad = (probs * (probs_grad - inner)).astype(BF16)
            dv_part, dk_part = nn(probs.astype(BF16), grad), nn(score_grad, query)
            dv_sum = dv_part if dv_sum is None else dv_sum + dv_part
            dk_sum = dk_part if dk_sum is None else dk_sum + dk_part
            dq.append(nn(turned[head_of(h), :reach], score_grad))
        dq_heads.append(jnp.concatenate(dq, axis=0))
        dk.append(dk_sum)
        dv.append(dv_sum)

    def whole_rows(parts):
        early, late = parts
        return jnp.concatenate([late[:HALF_SEQ] + early, late[HALF_SEQ:]], axis=0)

    dq = jnp.concatenate(dq_heads, axis=1).T * FACTOR
    dk = whole_rows(dk) * FACTOR
    dv = whole_rows(dv).astype(BF16)
    copies = dq.shape[1] // PAIR
    cosine = jnp.concatenate([cos_ref[...]] * copies, axis=1)
    sine = jnp.concatenate([sin_ref[...]] * copies, axis=1)
    put_back(shift_ref, dq_ref, count, (dq * cosine - turn(dq) * sine).astype(BF16))
    put_back(shift_ref, dk_ref, count, (dk * cosine - turn(dk) * sine).astype(BF16))
    put_back(shift_ref, dv_ref, count, dv)


def attend_back(chain, shift, count, query, key, value, grad, logsum, tables):
    rows, width = query.shape
    grid, tile, sums = attention_specs(rows, width, PAIR)
    return chain.call(
        functools.partial(attend_back_body, count),
        grid,
        [tile] * 4 + [sums] + [whole((SEQ, PAIR))] * 2,
        [tile] * 3,
        [((rows, width), BF16)] * 3,
        flops=40 * rows * width * SEQ,
        prefetch=1,
        moved=14 * rows * width,
    )(shift, query, key, value, grad, logsum, *tables)


def local(
    chips,
    group,
    tokens,
    attn_gain,
    query_weight,
    key_weight,
    value_weight,
    output_weight,
    ffn_gain,
    gate_weight,
    up_weight,
    down_weight,
    cotangent,
):
    line = jnp.asarray(chips.table)[lax.axis_index("dp")]
    rows, model = tokens.shape
    count = SEQ // rows
    shift = lax.axis_index("tensor") % count
    row = jnp.arange(SEQ, dtype=jnp.int32)
    places = rope_tables(row)
    tables = rope_tables((row // rows ^ shift) * rows + row % rows)
    shift = jnp.reshape(shift, (1,)).astype(jnp.int32)
    early = (*places, *tables, line, shift)
    depth, own = query_weight.shape
    hidden_units = gate_weight.shape[1]
    chain = Chain()

    def gather(piece):
        return Gather(chips, chain, chain.join(piece)[0])

    def spread_of(values):
        return Spread(group, chain, chain.join(values)[0])

    def fold_of(part):
        own_part, sent = part
        sent = chain.join(*sent[0], *sent[1])
        return Fold(group, chain, own_part, [sent[: group.bits], sent[group.bits :]])

    def grads_of(left, rights, theirs=None):
        if theirs is None:
            (theirs,) = weight_grads(chain, left, 1, rights)
        got = [None]
        chain.ask(theirs, got, 0, chips.other)

        def mine(**how):
            if got[0] is None:
                chain.flush()
            blocks = weight_grads(chain, left, 0, rights, got[0], chips.bits)
            return Sums(chips, chain, blocks, **how)

        return mine

    extra = jnp.concatenate([attn_gain, ffn_gain, jnp.zeros((4 * own - 2 * depth,), BF16)])
    attn = jnp.concatenate([query_weight, key_weight, value_weight, output_weight.T], axis=1)
    attn = gather(jnp.concatenate([attn, jnp.broadcast_to(extra, (16, 4 * own))], axis=0))
    spread = spread_of(tokens)
    grads_spread = spread_of(cotangent)
    grads_spread.later = []
    down_turned, *early = chain.join(down_weight.T, *early)
    places, tables, line, shift = early[:2], early[2:4], early[4], early[5]
    chain.end(attn, spread, grads_spread)
    chain.end(attn, spread)
    all_tokens = spread.blocks()
    attn = attn.pieces()
    pair = gather(jnp.concatenate([gate_weight, up_weight], axis=1))
    w_query, w_key, w_value, w_output = [Weight(attn, depth, i * own, own) for i in range(4)]
    gains = jnp.concatenate(
        [piece[depth : depth + 1, : 2 * depth].reshape(2, depth) for piece in attn], axis=1
    ).astype(F32)

    group_one = ordered(chain, norm_body, line, gains, all_tokens)
    grads_spread.resume()
    query, key, value = project(chain, group_one, tables, w_query, w_key, w_value)
    mixed, logsum = attend(chain, shift, count, query, key, value)
    out_part = times_trans(chain, [(mixed, w_output)], group)
    fold = fold_of(out_part)
    chain.end(fold, pair, grads_spread)
    grad_rows = ordered(chain, order_body, line, gains, grads_spread.blocks())
    chain.end(fold)
    attended = fold.total()
    middle, second = by_rows(
        chain, middle_body, line, tokens, gains, attended, [], [F32, BF16]
    )
    spread = spread_of(second)
    chain.end(spread, pair)
    pair = pair.pieces()
    down = gather(down_turned)
    chain.end(spread)
    group_two = spread.blocks()
    w_gate = Weight(pair, depth, 0, hidden_units)
    w_up = Weight(pair, depth, hidden_units, hidden_units)
    hidden, slope, silu, theirs = gate_up(chain, group_two, w_gate, w_up, grad_rows)

    mine = grads_of(grad_rows, [hidden], theirs)
    chain.end(down)
    chain.flush()
    down_sum = mine()
    w_down = Weight(down.pieces(), depth, 0, hidden_units)
    gate_grad, up_grad, gate_theirs, up_theirs = hidden_back(
        chain, grad_rows, w_down, slope, silu, group_two
    )
    mine_gate = grads_of(group_two, [gate_grad], gate_theirs)
    chain.end(down_sum)
    second_part = times_trans(chain, [(gate_grad, w_gate), (up_grad, w_up)], group)
    fold = fold_of(second_part)
    gate_sum = mine_gate(hold=True)
    result_part = times_trans(chain, [(hidden, w_down)], group)
    chain.end(down_sum)
    (down_sum,) = finish(chain, down_sum.terms())
    mine_up = grads_of(group_two, [up_grad], up_theirs)
    chain.end(fold)
    up_sum = mine_up(hold=True)
    chain.end(fold)
    second_grad = fold.total()
    middle_grad, low_grad = by_rows(
        chain, second_back_body, line, cotangent, gains, second_grad, [middle], [F32, BF16]
    )
    spread = spread_of(low_grad)
    chain.end(gate_sum)
    gate_sum.resume()
    chain.end(spread)
    chain.end(spread)
    attn_grads = spread.blocks()

    mixed_grad = mixed_back(chain, attn_grads, w_output)
    query_back, key_back, value_back = attend_back(
        chain, shift, count, query, key, value, mixed_grad, logsum, places
    )
    mine_qkv = grads_of(group_one, [query_back, key_back, value_back])
    mine_out = grads_of(attn_grads, [mixed])
    chain.end(gate_sum, up_sum)
    up_sum.resume()
    fold = fold_of(result_part)
    qkv_sum = mine_qkv()
    first_part = times_trans(
        chain, [(query_back, w_query), (key_back, w_key), (value_back, w_value)], group
    )
    out_sum = mine_out(hold=True)
    gate_sum, gate_inner = finish(chain, gate_sum.terms(), [gate_weight])
    chain.end(up_sum, out_sum, fold)
    chain.end(qkv_sum, fold)
    result_part = fold.total()
    fold = fold_of(first_part)
    out_sum.resume()
    up_sum, up_inner = finish(chain, up_sum.terms(), [up_weight])
    (layer_out,) = by_rows(chain, result_body, line, middle, gains, result_part, [], [BF16])
    chain.end(fold)
    chain.end(fold)
    chain.end(qkv_sum)
    query_sum, key_sum, value_sum, qkv_inner = finish(
        chain, qkv_sum.terms(), [query_weight, key_weight, value_weight]
    )
    gain_parts = jnp.stack(
        [qkv_inner / attn_gain.astype(F32), (gate_inner + up_inner) / ffn_gain.astype(F32)]
    )
    (gain_parts,) = chain.join(gain_parts)
    first_grad = fold.total()
    (input_grad,) = by_rows(
        chain, first_back_body, line, tokens, gains, first_grad, [middle_grad], [F32]
    )
    (out_sum,) = finish(chain, out_sum.terms())
    gain_totals = gain_parts
    for k in range(1, group.size):
        pairs = [(i, i ^ k) for i in range(group.size)]
        gain_totals += lax.ppermute(gain_parts, "tensor", pairs)
    gain_one_total, gain_two_total = gain_totals[0], gain_totals[1]
    return (
        layer_out,
        input_grad,
        gain_one_total,
        query_sum,
        key_sum,
        value_sum,
        out_sum,
        gain_two_total,
        gate_sum,
        up_sum,
        down_sum,
    )


def solution(mesh):
    in_specs = (
        P(("dp", "tensor"), None),
        P("dp"),
        P("dp", "tensor"),
        P("dp", "tensor"),
        P("dp", "tensor"),
        P("tensor", "dp"),
        P("dp"),
        P("dp", "tensor"),
        P("dp", "tensor"),
        P("tensor", "dp"),
        P(("dp", "tensor"), None),
    )
    out_specs = (
        P(("dp", "tensor"), None),
        P(("dp", "tensor"), None),
        P("dp"),
        P("dp", "tensor"),
        P("dp", "tensor"),
        P("dp", "tensor"),
        P("tensor", "dp"),
        P("dp"),
        P("dp", "tensor"),
        P("dp", "tensor"),
        P("tensor", "dp"),
    )
    chips = Chips(mesh.shape["dp"])
    size = mesh.shape["tensor"]
    links = [[(i, i ^ 1 << b) for i in range(size)] for b in range(size.bit_length() - 1)]
    group = Group(links, "tensor")

    def run(*arrays):
        return local(chips, group, *arrays)

    return jax.shard_map(run, mesh=mesh, in_specs=in_specs, out_specs=out_specs, check_vma=False)
```

```python
import functools

import jax
import jax.numpy as jnp
import numpy as np
from jax import lax
from jax.experimental import pallas as pl
from jax.experimental.pallas import tpu as pltpu
from jax.sharding import PartitionSpec as P

HEAD_DIM = 64
SEQ = 512
EPS = 1e-05
THETA = 130000.0
BF16 = jnp.bfloat16
F32 = jnp.float32
FACTOR = HEAD_DIM**-0.5
PAIR = 2 * HEAD_DIM
HALF_SEQ = SEQ // 2
VMEM_LIMIT = 58 << 20
COST_SHARE = 4096


class Chain:
    def __init__(self):
        self.token = jnp.zeros((8, 128), F32)
        self.swaps, self.asked = [], []

    def join(self, *values):
        *values, self.token = lax.optimization_barrier((*values, self.token))
        return values

    def gate(self, *values):
        swaps, self.swaps = self.swaps, []
        asked, self.asked = self.asked, []
        joined = self.join(
            *values, *[held[i] for held, i in swaps], *[source for source, _, _, _ in asked]
        )
        for (held, i), value in zip(swaps, joined[len(values) :]):
            held[i] = value
        for (_, held, i, swap), value in zip(asked, joined[len(values) + len(swaps) :]):
            held[i] = swap(value)
            self.swaps.append((held, i))
        return joined[: len(values)]

    def end(self, *transfers):
        counts = [len(t.flying) for t in transfers]
        got = self.gate(*[value for t in transfers for value in t.flying])
        for t, count in zip(transfers, counts):
            if count:
                t.go_on(got[:count])
            got = got[count:]

    def ask(self, source, held, i, swap):
        self.asked.append((source, held, i, swap))

    def flush(self):
        for source, held, i, swap in self.asked:
            held[i] = swap(source)
        self.asked = []

    def call(self, body, grid, ins, outs, shapes, flops, scratch=(), prefetch=0, moved=0):
        first = prefetch + len(ins)
        second = first + 1 + len(outs)
        anywhere = pl.BlockSpec(memory_space=pl.ANY)

        def wrapped(*refs):
            body(*refs[:first], *refs[first + 1 : second], *refs[second + 1 :])

        run = pl.pallas_call(
            wrapped,
            grid_spec=pltpu.PrefetchScalarGridSpec(
                num_scalar_prefetch=prefetch,
                grid=grid,
                in_specs=[*ins, anywhere],
                out_specs=[*outs, anywhere],
                scratch_shapes=list(scratch),
            ),
            out_shape=[jax.ShapeDtypeStruct(s, t) for s, t in [*shapes, ((8, 128), F32)]],
            compiler_params=pltpu.CompilerParams(
                vmem_limit_bytes=VMEM_LIMIT, dimension_semantics=("arbitrary",) * len(grid)
            ),
            cost_estimate=pl.CostEstimate(
                flops=flops // COST_SHARE, bytes_accessed=moved // COST_SHARE, transcendentals=0
            ),
        )

        def with_token(*args):
            *results, self.token = run(*args, self.token)
            return results

        return with_token


class Chips:
    def __init__(self, size):
        self.bits = (size // 2).bit_length() - 1
        self.size = size
        self.swap = [(i, i ^ 1) for i in range(size)]
        self.links = [
            [(i, i ^ 2 << self.bits - 1 - p) for i in range(size)] for p in range(self.bits)
        ]
        flips = [
            sum(1 << self.bits - 1 - p for p in range(self.bits) if v >> p & 1)
            for v in range(1 << self.bits)
        ]
        table = [[i ^ 2 * f for f in flips] + [i ^ 2 * f ^ 1 for f in flips] for i in range(size)]
        self.table = np.array(table, np.int32)

    def send(self, value, p):
        return lax.ppermute(value, "dp", self.links[p])

    def other(self, value):
        return lax.ppermute(value, "dp", self.swap)


class Gather:
    def __init__(self, chips, chain, piece):
        self.chips, self.chain = chips, chain
        self.own = [piece] + [None] * (2**chips.bits - 1)
        self.others = list(self.own)
        self.ask(0)
        self.keys = [1 << p for p in range(chips.bits)]
        self.flying = [chips.send(piece, p) for p in range(chips.bits)]

    def ask(self, v):
        self.chain.ask(self.own[v], self.others, v, self.chips.other)

    def go_on(self, got):
        keys, self.keys, self.flying = self.keys, [], []
        for v, piece in zip(keys, got):
            self.own[v] = piece
            for p in range(v.bit_length(), self.chips.bits):
                self.keys.append(v | 1 << p)
                self.flying.append(self.chips.send(piece, p))
        for v in keys:
            self.ask(v)

    def pieces(self):
        while self.flying:
            self.chain.end(self)
        self.chain.flush()
        return self.own + self.others


class Sums:
    def __init__(self, chips, chain, mine, apart=False, hold=False, cut_in_two=False):
        self.chips, self.chain, self.apart, self.hold = chips, chain, apart, hold
        self.todo = []
        self.cut_in_two = cut_in_two and chips.bits == 2
        self.parts = [mine[0]]
        mine = list(mine[1:])
        self.direct, self.passed = [], []
        for p in range(chips.bits):
            self.direct.append(mine.pop(0))
            self.passed.append(mine.pop(0) if p else None)
        self.p = chips.bits - 1
        if self.cut_in_two:
            self.kinds = [0, 1]
            self.flying = [chips.send(half, 1) for half in self.in_two(self.passed[1])]
            return
        self.kinds = [self.p]
        self.flying = [chips.send(self.passed[self.p], self.p)]

    def in_two(self, values):
        width = values.shape[1] // 2
        return values[:, :width], values[:, width:]

    def go_on(self, got):
        rows = self.parts[0].shape[0]
        kinds, self.kinds, self.flying = self.kinds, [], []
        if self.p == 0:
            self.parts += got
            return
        if self.cut_in_two:
            self.p = 0
            total = self.direct[0].astype(F32) + jnp.concatenate(got, axis=1).astype(F32)
            self.todo = [(None, self.direct[1], 1), (None, total.astype(BF16), 0)]
            self.resume()
            return
        for kind, block in zip(kinds, got):
            if kind is None:
                self.parts.append(block)
                continue
            add = lambda held, first: (
                held.astype(F32) + block[first * rows : first * rows + held.shape[0]].astype(F32)
            ).astype(BF16)
            for q in range(kind):
                self.direct[q] = add(self.direct[q], (1 << q) - 1)
                if q:
                    self.passed[q] = add(self.passed[q], 1 << q)
        p, self.p = self.p, self.p - 1
        if p > 0:
            self.todo.append((None, self.direct[p], p))
        if p > 1:
            self.todo.append((p - 1, self.passed[p - 1], p - 1))
        if p == 1 and not self.apart:
            self.todo.append((None, self.direct[0], 0))
        if not self.hold:
            self.resume()

    def resume(self):
        todo, self.todo = self.todo, []
        values = self.chain.join(*[value for _, value, _ in todo])
        for (kind, _, p), value in zip(todo, values):
            self.kinds.append(kind)
            self.flying.append(self.chips.send(value, p))

    def send_half(self, i):
        while self.p > 0:
            self.chain.end(self)
        width = self.direct[0].shape[1] // 2
        (value,) = self.chain.join(self.direct[0][:, i * width : (i + 1) * width])
        self.kinds.append(None)
        self.flying.append(self.chips.send(value, 0))

    def terms(self):
        while self.flying or self.todo:
            if self.todo:
                self.resume()
            self.chain.end(self)
        return sorted(self.parts, key=lambda part: -part.shape[1])


class Group:
    def __init__(self, links, axes):
        self.links, self.axes = links, axes
        self.bits = len(links)
        self.size = 1 << self.bits
        self.orders = (list(range(self.bits)), list(range(self.bits))[::-1])

    def send(self, value, bit):
        return lax.ppermute(value, self.axes, self.links[bit])

    def messages(self):
        found = []
        for order in self.orders:
            found.append([])
            for top in reversed(range(self.bits)):
                found[-1].append(
                    [
                        1 << order[top] | sum(1 << order[p] for p in range(top) if v >> p & 1)
                        for v in range(1 << top)
                    ]
                )
        return found


class Spread:
    def __init__(self, group, chain, rows):
        self.group, self.chain = group, chain
        self.held = {0: [rows]}
        self.later = None
        self.keys = [(1 << b, None) for b in range(group.bits)]
        self.flying = [group.send(rows, b) for b in range(group.bits)]

    def go_on(self, got):
        fresh = list(zip(self.keys, got))
        self.keys, self.flying = [], []
        for (k, h), block in fresh:
            if h is None:
                self.held[k] = [block]
            else:
                self.held.setdefault(k, [None, None])[h] = block
        for (k, h), block in fresh:
            for way, order in enumerate(self.group.orders):
                if h is not None and h != way:
                    continue
                half = block.shape[1] // 2
                top = max(i for i, bit in enumerate(order) if k >> bit & 1)
                for i in range(top + 1, len(order)):
                    part = block if h is not None else block[:, way * half : (way + 1) * half]
                    self.keys.append((k | 1 << order[i], way))
                    if self.later is not None:
                        self.later.append((part, order[i]))
                    else:
                        self.flying.append(self.group.send(part, order[i]))

        if self.later:
            parts = self.chain.join(*[part for part, _ in self.later])
            self.later = [(part, bit) for part, (_, bit) in zip(parts, self.later)]

    def resume(self):
        later, self.later = self.later, None
        parts = self.chain.join(*[part for part, _ in later])
        self.flying = [self.group.send(part, bit) for part, (_, bit) in zip(parts, later)]

    def blocks(self):
        while self.flying:
            self.chain.end(self)
        return [self.held[k] for k in range(self.group.size)]


class Fold:
    def __init__(self, group, chain, own, sent):
        self.group, self.chain = group, chain
        self.rows = own[0].shape[0]
        self.sent = [list(half) for half in sent]
        self.parts = [[half] for half in own]
        self.wave = 0
        self.start()

    def start(self):
        self.flying = [
            self.group.send(self.sent[h][self.wave], order[self.group.bits - 1 - self.wave])
            for h, order in enumerate(self.group.orders)
        ]

    def go_on(self, got):
        self.wave += 1
        self.flying = []
        for h, block in enumerate(got):
            self.parts[h].append(block)
        for wave in range(self.wave, self.group.bits):
            sums = add_rows(self.chain, [sent[wave] for sent in self.sent], got)
            for sent, value in zip(self.sent, sums):
                sent[wave] = value
        if self.wave < self.group.bits:
            self.start()

    def total(self):
        while self.flying:
            self.chain.end(self)
        return self.parts


class Weight:
    def __init__(self, pieces, rows, start, width):
        self.pieces, self.rows, self.start, self.width = pieces, rows, start, width
        self.model = len(pieces) * rows

    def tiles(self, tile):
        first = self.start // tile
        return [pl.BlockSpec((self.rows, tile), lambda j: (0, first + j))] * len(self.pieces)


def nn(left, right):
    return lax.dot_general(left, right, (((1,), (0,)), ((), ())), preferred_element_type=F32)


def nt(left, right):
    return lax.dot_general(left, right, (((1,), (1,)), ((), ())), preferred_element_type=F32)


def tn(left, right):
    return lax.dot_general(left, right, (((0,), (0,)), ((), ())), preferred_element_type=F32)


def whole(shape):
    return pl.BlockSpec(shape, lambda *_: (0,) * len(shape))


def place(line_ref, j, width):
    return pl.ds(pl.multiple_of(line_ref[j] * width, 128), width)


def cut(width, j):
    return slice(j * width, (j + 1) * width)


def scale_of(values):
    return lax.rsqrt(jnp.mean(values * values, axis=-1, keepdims=True) + EPS)


def fetch_blocks(counts, refs, held, sems, k, slot, wait):
    first = 0
    for i, count in enumerate(counts):
        copies = []
        half = held.shape[2] // count
        for h in range(count):
            target = held.at[slot, :, pl.ds(h * half, half)]
            copies.append(pltpu.make_async_copy(refs[first + h], target, sems.at[slot, h]))
        first += count

        @pl.when(k == i)
        def _():
            for copy in copies:
                copy.wait() if wait else copy.start()


def fetched(counts, refs, held, sems):
    k = pl.program_id(0)

    @pl.when(k == 0)
    def _():
        fetch_blocks(counts, refs, held, sems, k, 0, False)

    fetch_blocks(counts, refs, held, sems, k + 1, (k + 1) % 2, False)
    fetch_blocks(counts, refs, held, sems, k, k % 2, True)
    return held.at[k % 2]


def norm_body(blocks, counts, line_ref, gain_ref, *refs):
    out_ref, held, sems = refs[sum(counts) :]
    x_ref = fetched(counts, refs, held, sems)
    width = out_ref.shape[1] // blocks
    scale = scale_of(x_ref[...].astype(F32))
    for j in range(blocks):
        part = x_ref[:, place(line_ref, j, width)].astype(F32)
        gain = gain_ref[0:1, cut(width, j)]
        out_ref[:, cut(width, j)] = (part * scale * gain).astype(BF16)


def order_body(blocks, counts, line_ref, gain_ref, *refs):
    out_ref, held, sems = refs[sum(counts) :]
    x_ref = fetched(counts, refs, held, sems)
    width = out_ref.shape[1] // blocks
    for j in range(blocks):
        out_ref[:, cut(width, j)] = x_ref[:, place(line_ref, j, width)]


def ordered(chain, body, line, gains, held):
    counts = [len(block) for block in held]
    rows, model = held[0][0].shape
    n = len(held)
    return chain.call(
        functools.partial(body, line.shape[0], counts),
        (n,),
        [whole(gains.shape)] + [pl.BlockSpec(memory_space=pl.ANY)] * sum(counts),
        [pl.BlockSpec((rows, model), lambda k, *_: (k, 0))],
        [((n * rows, model), BF16)],
        flops=20 * n * rows * model,
        scratch=[pltpu.VMEM((2, rows, model), BF16), pltpu.SemaphoreType.DMA((2, 2))],
        prefetch=1,
        moved=4 * n * rows * model,
    )(line, gains, *[array for block in held for array in block])[0]


def added(refs, span):
    total = refs[0][span, :].astype(F32)
    for ref in refs[1:]:
        total += ref[span, :].astype(F32)
    return total


def middle_body(blocks, m, line_ref, x_ref, gain_ref, *refs):
    middle_ref, out_ref = refs[2 * m :]
    width = x_ref.shape[1] // blocks
    half = x_ref.shape[1] // 2
    span = slice(None)
    middle_ref[:, :half] = added(refs[:m], span)
    middle_ref[:, half:] = added(refs[m : 2 * m], span)
    for j in range(blocks):
        here = x_ref[:, place(line_ref, j, width)].astype(F32)
        middle_ref[:, cut(width, j)] += here
    middle = middle_ref[...]
    out_ref[...] = (middle * scale_of(middle) * gain_ref[1:2, :]).astype(BF16)


def result_body(blocks, m, line_ref, middle_ref, gain_ref, *refs):
    out_ref = refs[2 * m]
    width = middle_ref.shape[1] // blocks
    span = slice(None)
    total = middle_ref[...] + jnp.concatenate(
        [added(refs[:m], span), added(refs[m : 2 * m], span)], axis=1
    )
    for j in range(blocks):
        out_ref[:, place(line_ref, j, width)] = total[:, cut(width, j)].astype(BF16)


def second_back_body(blocks, m, line_ref, dy_ref, gain_ref, *refs):
    middle_ref, out_ref, low_ref = refs[2 * m :]
    width = dy_ref.shape[1] // blocks
    span = slice(None)
    grad = jnp.concatenate([added(refs[:m], span), added(refs[m : 2 * m], span)], axis=1)
    middle = middle_ref[...]
    scale = scale_of(middle)
    normed = middle * scale
    scaled = grad * gain_ref[1:2, :]
    out_ref[...] = scale * (scaled - normed * jnp.mean(scaled * normed, axis=-1, keepdims=True))
    for j in range(blocks):
        out_ref[:, cut(width, j)] += dy_ref[:, place(line_ref, j, width)].astype(F32)
    low_ref[...] = out_ref[...].astype(BF16)


def first_back_body(blocks, m, line_ref, x_ref, gain_ref, *refs):
    above_ref, out_ref = refs[2 * m :]
    width = x_ref.shape[1] // blocks
    span = slice(None)
    scale = scale_of(x_ref[...].astype(F32))
    normed = jnp.concatenate(
        [x_ref[:, place(line_ref, j, width)].astype(F32) for j in range(blocks)], axis=1
    ) * scale
    grad = jnp.concatenate([added(refs[:m], span), added(refs[m : 2 * m], span)], axis=1)
    scaled = grad * gain_ref[0:1, :]
    back = scale * (scaled - normed * jnp.mean(scaled * normed, axis=-1, keepdims=True))
    total = above_ref[...] + back
    for j in range(blocks):
        out_ref[:, place(line_ref, j, width)] = total[:, cut(width, j)]


def by_rows(chain, body, line, first, gains, parts, more, kinds):
    rows, model = first.shape
    half = model // 2
    tile = min(128, rows)
    row = pl.BlockSpec((tile, model), lambda i, *_: (i, 0))
    slim = pl.BlockSpec((tile, half), lambda i, *_: (i, 0))
    m = len(parts[0])
    return chain.call(
        functools.partial(body, line.shape[0], m),
        (rows // tile,),
        [row, whole(gains.shape)] + [slim] * (2 * m) + [row] * len(more),
        [row] * len(kinds),
        [((rows, model), kind) for kind in kinds],
        flops=20 * rows * model,
        prefetch=1,
        moved=rows * model * (2 * m + 4 * len(kinds)),
    )(line, first, gains, *parts[0], *parts[1], *more)


def add_rows_body(count, *refs):
    for i in range(count):
        total = refs[i][...].astype(F32) + refs[count + i][...].astype(F32)
        refs[2 * count + i][...] = total.astype(BF16)


def add_rows(chain, helds, blocks):
    rows, columns = helds[0].shape
    tile = min(128, rows)
    steps = rows // tile
    count = len(helds)
    here = pl.BlockSpec((tile, columns), lambda i: (i, 0))
    return chain.call(
        functools.partial(add_rows_body, count),
        (steps,),
        [here] * count + [pl.BlockSpec((tile, columns), lambda i: (steps + i, 0))] * count,
        [here] * count,
        [((rows, columns), BF16)] * count,
        flops=count * rows * columns,
        moved=6 * count * rows * columns,
    )(*helds, *blocks)


def finish_body(m, halves, n, *refs):
    total = added(refs[:m], slice(None))
    if halves:
        total += jnp.concatenate([ref[...].astype(F32) for ref in refs[m : m + halves]], axis=1)
    m += halves
    weights, outs = refs[m : m + n], refs[m + n :]
    if not n:
        outs[0][...] = total.T
        return
    width = weights[0].shape[1]
    inner = jnp.zeros((total.shape[0], 1), F32)
    for i in range(n):
        part = total[:, cut(width, i)]
        outs[i][...] = part
        inner += jnp.sum(weights[i][...].astype(F32) * part, axis=1, keepdims=True)
    outs[n][...] = jnp.broadcast_to(inner, outs[n].shape)


def finish(chain, terms, weights=()):
    rows, columns = terms[0].shape
    tile = min(128, rows)
    row = pl.BlockSpec((tile, columns), lambda i: (i, 0))
    n = len(weights)
    halves = sum(1 for term in terms if term.shape[1] < columns)
    half = [pl.BlockSpec((tile, columns // 2), lambda i: (i, 0))] * halves
    if n:
        slim = pl.BlockSpec((tile, columns // n), lambda i: (i, 0))
        outs = [slim] * n + [pl.BlockSpec((tile, 128), lambda i: (i, 0))]
        shapes = [((rows, columns // n), F32)] * n + [((rows, 128), F32)]
    else:
        slim = None
        outs = [pl.BlockSpec((columns, tile), lambda i: (0, i))]
        shapes = [((columns, rows), F32)]
    results = chain.call(
        functools.partial(finish_body, len(terms) - halves, halves, n),
        (rows // tile,),
        [row] * (len(terms) - halves) + half + [slim] * n,
        outs,
        shapes,
        flops=4 * rows * columns,
        moved=rows * columns * 12,
    )(*terms, *weights)
    if n:
        results[n] = results[n][:, 0]
    return results


def rope_tables(place):
    half = HEAD_DIM // 2
    freq = THETA ** (-2.0 * jnp.arange(half, dtype=F32) / HEAD_DIM)
    angle = place.astype(F32)[:, None] * freq[None, :]
    cosine, sine = jnp.cos(angle), jnp.sin(angle)
    return (
        jnp.concatenate([cosine] * (PAIR // half), axis=1),
        jnp.concatenate([-sine, sine] * (PAIR // HEAD_DIM), axis=1),
    )


def turn(values):
    half = HEAD_DIM // 2
    width = values.shape[-1]
    lane = lax.broadcasted_iota(jnp.int32, values.shape, 1) % HEAD_DIM
    return jnp.where(
        lane < half, pltpu.roll(values, width - half, 1), pltpu.roll(values, half, 1)
    )


def joined(refs):
    return jnp.concatenate([r[...] for r in refs], axis=0)


def qkv_body(n, x_ref, cos_ref, sin_ref, *refs):
    weights, outs = refs[: 3 * n], refs[3 * n :]
    rows = x_ref.shape[0]
    tile = outs[0].shape[1]
    for i in range(3):
        weight = joined(weights[i * n : (i + 1) * n])
        for s in range(rows // SEQ):
            span = slice(s * SEQ, (s + 1) * SEQ)
            product = nn(x_ref[span, :], weight)
            if i == 2:
                outs[i][span, :] = product.astype(BF16)
                continue
            for t in range(tile // PAIR):
                here = product[:, t * PAIR : (t + 1) * PAIR]
                turned = here * cos_ref[...] + turn(here) * sin_ref[...]
                outs[i][span, t * PAIR : (t + 1) * PAIR] = turned.astype(BF16)


def project(chain, x, tables, query, key, value):
    rows, model = x.shape
    n, width = len(query.pieces), query.width
    tile = min(256, width)
    out = pl.BlockSpec((rows, tile), lambda j: (0, j))
    return chain.call(
        functools.partial(qkv_body, n),
        (width // tile,),
        [whole(x.shape), whole((SEQ, PAIR)), whole((SEQ, PAIR))]
        + query.tiles(tile)
        + key.tiles(tile)
        + value.tiles(tile),
        [out] * 3,
        [((rows, width), BF16)] * 3,
        flops=6 * rows * model * width,
        moved=2 * (rows * model + 3 * model * width + 3 * rows * width),
    )(x, *tables, *query.pieces, *key.pieces, *value.pieces)


def collect(counts, refs, held, sems):
    rows = held.shape[0] // len(counts)
    copies = []
    for k, count in enumerate(counts):
        half = held.shape[1] // count
        for h in range(count):
            target = held.at[pl.ds(k * rows, rows), pl.ds(h * half, half)]
            i = len(copies)
            copies.append(pltpu.make_async_copy(refs[i], target, sems.at[i]))
    for copy in copies:
        copy.start()
    for copy in copies:
        copy.wait()


def gate_body(n, counts, *refs):
    m = sum(counts)
    gate_w, up_w = refs[m : m + n], refs[m + n : m + 2 * n]
    left_ref, hidden_ref, slope_ref, silu_ref, theirs_ref, x_ref, turned, sems = refs[m + 2 * n :]

    @pl.when(pl.program_id(0) == 0)
    def _():
        collect(counts, refs, x_ref, sems)
        turned[...] = left_ref[...].T

    gate_weight, up_weight = joined(gate_w), joined(up_w)
    for s in range(x_ref.shape[0] // SEQ):
        span = slice(s * SEQ, (s + 1) * SEQ)
        gate = nn(x_ref[span, :], gate_weight)
        up = nn(x_ref[span, :], up_weight)
        sigm = jax.nn.sigmoid(gate)
        silu = gate * sigm
        hidden_ref[span, :] = (silu * up).astype(BF16)
        silu_ref[span, :] = silu.astype(BF16)
        slope_ref[span, :] = (up * sigm * (1.0 + gate * (1.0 - sigm))).astype(BF16)
    theirs_ref[...] = nn(turned[...], hidden_ref[...]).astype(BF16)


def collected(held):
    counts = [len(block) for block in held]
    rows, model = held[0][0].shape
    scratch = [
        pltpu.VMEM((len(held) * rows, model), BF16),
        pltpu.SemaphoreType.DMA((sum(counts),)),
    ]
    arrays = [array for block in held for array in block]
    return counts, arrays, [pl.BlockSpec(memory_space=pl.ANY)] * len(arrays), scratch


def gate_up(chain, held, gate, up, grads):
    counts, arrays, specs, scratch = collected(held)
    rows, model = scratch[0].shape
    n, width = len(gate.pieces), gate.width
    tile = min(256, width)
    out = pl.BlockSpec((rows, tile), lambda j: (0, j))
    half = model // 2
    return chain.call(
        functools.partial(gate_body, n, counts),
        (width // tile,),
        specs
        + gate.tiles(tile)
        + up.tiles(tile)
        + [pl.BlockSpec((rows, half), lambda j: (0, 1))],
        [out] * 3 + [pl.BlockSpec((half, tile), lambda j: (0, j))],
        [((rows, width), BF16)] * 3 + [((half, width), BF16)],
        flops=6 * rows * model * width,
        scratch=[scratch[0], pltpu.VMEM((half, rows), BF16), scratch[1]],
        moved=2 * (rows * model + 2 * model * width + 3 * rows * width),
    )(*arrays, *gate.pieces, *up.pieces, grads)


def half_blocks(left, which):
    lefts = [block[0] if len(block) == 1 else block[which] for block in left]
    rows, half = lefts[0].shape[0], left[0][0].shape[1] // 2
    places = [which if len(block) == 1 else 0 for block in left]
    return lefts, [
        pl.BlockSpec((rows, half), functools.partial(lambda at, j: (0, at), at)) for at in places
    ]


def hidden_back_body(n, blocks, g_ref, *refs):
    weights, slope_ref, silu_ref = refs[:n], refs[n], refs[n + 1]
    lefts, refs = refs[n + 2 : n + 2 + blocks], refs[n + 2 + blocks :]
    gate_ref, up_ref, gate_theirs, up_theirs, turned = refs
    rows = turned.shape[1] // blocks

    @pl.when(pl.program_id(0) == 0)
    def _():
        for k in range(blocks):
            turned[:, cut(rows, k)] = lefts[k][...].T

    weight = joined(weights)
    for s in range(g_ref.shape[0] // SEQ):
        span = slice(s * SEQ, (s + 1) * SEQ)
        grad = nn(g_ref[span, :], weight)
        gate_ref[span, :] = (grad * slope_ref[span, :].astype(F32)).astype(BF16)
        up_ref[span, :] = (grad * silu_ref[span, :].astype(F32)).astype(BF16)
    gate_theirs[...] = nn(turned[...], gate_ref[...]).astype(BF16)
    up_theirs[...] = nn(turned[...], up_ref[...]).astype(BF16)


def hidden_back(chain, grads, down, slope, silu, left):
    rows, model = grads.shape
    n, width = len(down.pieces), down.width
    tile = min(256, width)
    out = pl.BlockSpec((rows, tile), lambda j: (0, j))
    lefts, specs = half_blocks(left, 1)
    half = model // 2
    return chain.call(
        functools.partial(hidden_back_body, n, len(lefts)),
        (width // tile,),
        [whole(grads.shape)] + down.tiles(tile) + [out] * 2 + specs,
        [out] * 2 + [pl.BlockSpec((half, tile), lambda j: (0, j))] * 2,
        [((rows, width), BF16)] * 2 + [((half, width), BF16)] * 2,
        flops=4 * rows * model * width,
        scratch=[pltpu.VMEM((half, rows), BF16)],
        moved=2 * (rows * model + model * width + 4 * rows * width),
    )(grads, *down.pieces, slope, silu, *lefts)


def mixed_back_body(n, counts, *refs):
    m = sum(counts)
    out_ref, x_ref, sems = refs[m + n :]

    @pl.when(pl.program_id(0) == 0)
    def _():
        collect(counts, refs, x_ref, sems)

    out_ref[...] = nn(x_ref[...], joined(refs[m : m + n])).astype(BF16)


def mixed_back(chain, held, out):
    counts, arrays, specs, scratch = collected(held)
    rows, model = scratch[0].shape
    n, width = len(out.pieces), out.width
    tile = min(256, width)
    return chain.call(
        functools.partial(mixed_back_body, n, counts),
        (width // tile,),
        specs + out.tiles(tile),
        [pl.BlockSpec((rows, tile), lambda j: (0, j))],
        [((rows, width), BF16)],
        flops=2 * rows * model * width,
        scratch=scratch,
        moved=2 * (rows * model + model * width + rows * width),
    )(*arrays, *out.pieces)[0]


def trans_body(n, starts, targets, *refs):
    parts, blocks = len(starts), len(targets[0])
    lefts = refs[:parts]
    pieces = refs[parts : parts * (n + 1)]
    outs = refs[parts * (n + 1) : -4]
    held, ready, sems, out_sems = refs[-4:]
    j = pl.program_id(0)
    depth, width = held.shape[2:]
    rows = ready.shape[1] // blocks

    def copy(i, p, slot):
        source = pieces[p * n + i].at[pl.ds(0, depth), pl.ds(starts[p], width)]
        return pltpu.make_async_copy(source, held.at[slot, p], sems.at[slot, p])

    def fetch(step, slot):
        for i in range(n):

            @pl.when(step == i)
            def _():
                for p in range(parts):
                    copy(i, p, slot).start()

    def leave(slot, k, array, first, column):
        target = outs[array].at[pl.ds(first, rows), pl.ds(column, depth)]
        source = ready.at[slot, pl.ds(k * rows, rows), :]
        return pltpu.make_async_copy(source, target, out_sems.at[slot, k])

    def left(slot):
        for k in range(blocks):
            leave(slot, k, 0, 0, 0).wait()

    @pl.when(j == 0)
    def _():
        fetch(j, 0)

    @pl.when(j + 1 < n)
    def _():
        fetch(j + 1, (j + 1) % 2)

    slot = j % 2
    for p in range(parts):
        copy(0, p, slot).wait()

    @pl.when(j >= 2)
    def _():
        left(slot)

    for s in range(blocks * rows // SEQ):
        span = slice(s * SEQ, (s + 1) * SEQ)
        total = nt(lefts[0][span, :], held[slot, 0])
        for p in range(1, parts):
            total += nt(lefts[p][span, :], held[slot, p])
        ready[slot, span, :] = total.astype(BF16)
    column = pl.multiple_of(j % (n // 2) * depth, 128)
    for h in range(2):

        @pl.when((j >= n // 2) == (h == 1))
        def _():
            for k, (array, first) in enumerate(targets[h]):
                leave(slot, k, array, first, column).start()

    @pl.when(j == n - 1)
    def _():
        left(1 - slot)
        left(slot)


def times_trans(chain, parts, group):
    weights = [weight for _, weight in parts]
    n, depth, width = len(weights[0].pieces), weights[0].rows, weights[0].width
    rows = parts[0][0].shape[0]
    half = weights[0].model // 2
    size = rows // group.size
    messages = group.messages()
    shapes = [((size, half), BF16)] * 2
    targets = [{0: (0, 0)}, {0: (1, 0)}]
    for h in range(2):
        for keys in messages[h]:
            for i, k in enumerate(keys):
                targets[h][k] = (len(shapes), i * size)
            shapes.append(((len(keys) * size, half), BF16))
    targets = [[t[k] for k in range(group.size)] for t in targets]
    anywhere = pl.BlockSpec(memory_space=pl.ANY)
    outs = chain.call(
        functools.partial(trans_body, n, [weight.start for weight in weights], targets),
        (n,),
        [whole((rows, width))] * len(parts) + [anywhere] * (n * len(parts)),
        [anywhere] * len(shapes),
        shapes,
        flops=4 * rows * half * width * len(parts),
        scratch=[
            pltpu.VMEM((2, len(parts), depth, width), BF16),
            pltpu.VMEM((2, rows, depth), BF16),
            pltpu.SemaphoreType.DMA((2, len(parts))),
            pltpu.SemaphoreType.DMA((2, group.size)),
        ],
        moved=2 * (2 * rows * half + len(parts) * (rows + 2 * half) * width),
    )(*[left for left, _ in parts], *[piece for weight in weights for piece in weight.pieces])
    m = group.bits
    return outs[:2], [outs[2 : 2 + m], outs[2 + m :]]


def grad_body(parts, got, blocks, steps, *refs):
    lefts, refs = refs[:blocks], refs[blocks:]
    rights, refs = refs[:parts], refs[parts:]
    got_ref = refs[0] if got else None
    outs, turned = refs[got:-1], refs[-1]
    j = pl.program_id(0)

    @pl.when(j == 0)
    def _():
        rows = turned.shape[1] // blocks
        for k in range(blocks):
            turned[:, cut(rows, k)] = lefts[k][...].T

    for i in range(parts):

        @pl.when((j >= i * steps) & (j < (i + 1) * steps))
        def _():
            total = nn(turned[...], rights[i][...])
            if got:
                total += got_ref[...].astype(F32)
            total = total.astype(BF16)
            first = 0
            for out_ref in outs:
                count = out_ref.shape[0]
                out_ref[...] = total[first : first + count]
                first += count


def weight_grads(chain, left, which, rights, got=None, bits=0):
    rows, width = rights[0].shape
    parts = len(rights)
    tile = min(512, width)
    steps = width // tile
    lefts, ins = half_blocks(left if isinstance(left, list) else [[left]], which)
    blocks, half = len(lefts), ins[0].block_shape[1]
    for i in range(parts):
        ins.append(
            pl.BlockSpec(
                (rows, tile),
                functools.partial(
                    lambda first, j: (0, jnp.clip(j - first, 0, steps - 1)), i * steps
                ),
            )
        )
    column = lambda j: (0, j)
    more = [] if got is None else [got]
    sizes = [half >> bits]
    for p in range(bits):
        sizes += [sizes[0], ((1 << p) - 1) * sizes[0]] if p else [sizes[0]]
    return chain.call(
        functools.partial(grad_body, parts, len(more), blocks, steps),
        (parts * steps,),
        ins + [pl.BlockSpec((half, tile), column)] * len(more),
        [pl.BlockSpec((size, tile), column) for size in sizes],
        [((size, parts * width), BF16) for size in sizes],
        flops=2 * rows * half * width * parts,
        scratch=[pltpu.VMEM((half, rows), BF16)],
        moved=2 * (rows * half + parts * (rows + half) * width),
    )(*lefts, *rights, *more)


def causal(scores):
    past = scores.shape[0] - HALF_SEQ
    key = lax.broadcasted_iota(jnp.int32, (HALF_SEQ, HALF_SEQ), 0)
    query = lax.broadcasted_iota(jnp.int32, (HALF_SEQ, HALF_SEQ), 1)
    last = jnp.where(key <= query, scores[past:], -1e30)
    return last if past == 0 else jnp.concatenate([scores[:past], last], axis=0)


def head_of(h):
    return slice(h * HEAD_DIM, (h + 1) * HEAD_DIM)


def span_of(b):
    return slice(b * HALF_SEQ, (b + 1) * HALF_SEQ)


def in_place(shift_ref, ref, count):
    rows = SEQ // count
    spans = [pl.ds(pl.multiple_of((i ^ shift_ref[0]) * rows, rows), rows) for i in range(count)]
    return jnp.concatenate([ref[span, :] for span in spans], axis=0)


def put_back(shift_ref, ref, count, values):
    rows = SEQ // count
    for i in range(count):
        ref[pl.ds(pl.multiple_of((i ^ shift_ref[0]) * rows, rows), rows), :] = values[cut(rows, i)]


def one_head(values, h):
    lane = lax.broadcasted_iota(jnp.int32, values.shape, 1)
    return jnp.where(lane // HEAD_DIM == h, values, jnp.zeros_like(values))


def attend_body(count, shift_ref, q_ref, k_ref, v_ref, out_ref, sum_ref):
    queries, keys = in_place(shift_ref, q_ref, count), in_place(shift_ref, k_ref, count)
    values = in_place(shift_ref, v_ref, count).astype(F32).T.astype(BF16)
    heads = []
    for h in range(q_ref.shape[1] // HEAD_DIM):
        blocks = []
        for b in range(2):
            reach = (b + 1) * HALF_SEQ
            query = one_head(queries[span_of(b)] * BF16(FACTOR), h)
            scores = causal(nt(keys[:reach], query))
            top = jnp.max(scores, axis=0, keepdims=True)
            expo = jnp.exp(scores - top)
            total = jnp.sum(expo, axis=0, keepdims=True)
            mixed = nn(values[head_of(h), :reach], expo.astype(BF16))
            blocks.append(mixed * (1.0 / total))
            sum_ref[0, h, :, span_of(b)] = top + jnp.log(total)
        heads.append(jnp.concatenate(blocks, axis=1))
    put_back(shift_ref, out_ref, count, jnp.concatenate(heads, axis=0).T.astype(BF16))


def attention_specs(rows, width, wide):
    wide = min(wide, width)
    tile = pl.BlockSpec((SEQ, wide), lambda s, p, _: (s, p))
    sums = pl.BlockSpec((1, wide // HEAD_DIM, 1, SEQ), lambda s, p, _: (s, p, 0, 0))
    return (rows // SEQ, width // wide), tile, sums


def attend(chain, shift, count, query, key, value):
    rows, width = query.shape
    grid, tile, sums = attention_specs(rows, width, 256)
    return chain.call(
        functools.partial(attend_body, count),
        grid,
        [tile] * 3,
        [tile, sums],
        [((rows, width), BF16), ((rows // SEQ, width // HEAD_DIM, 1, SEQ), F32)],
        flops=16 * rows * width * SEQ,
        prefetch=1,
        moved=8 * rows * width,
    )(shift, query, key, value)


def attend_back_body(
    count, shift_ref, q_ref, k_ref, v_ref, g_ref, sum_ref, cos_ref, sin_ref, dq_ref, dk_ref, dv_ref
):
    queries, keys, values, grads = (
        in_place(shift_ref, ref, count) for ref in (q_ref, k_ref, v_ref, g_ref)
    )
    turned = keys.astype(F32).T.astype(BF16)
    dq_heads = []
    dk, dv = [], []
    for b in range(2):
        reach = (b + 1) * HALF_SEQ
        dq, dk_sum, dv_sum = [], None, None
        for h in range(q_ref.shape[1] // HEAD_DIM):
            query = one_head(queries[span_of(b)], h)
            grad = one_head(grads[span_of(b)], h)
            scores = causal(nt(keys[:reach], query * BF16(FACTOR)))
            probs = jnp.exp(scores - sum_ref[0, h, :, span_of(b)])
            probs_grad = nt(values[:reach], grad)
            inner = jnp.sum(probs * probs_grad, axis=0, keepdims=True)
            score_grad = (probs * (probs_grad - inner)).astype(BF16)
            dv_part, dk_part = nn(probs.astype(BF16), grad), nn(score_grad, query)
            dv_sum = dv_part if dv_sum is None else dv_sum + dv_part
            dk_sum = dk_part if dk_sum is None else dk_sum + dk_part
            dq.append(nn(turned[head_of(h), :reach], score_grad))
        dq_heads.append(jnp.concatenate(dq, axis=0))
        dk.append(dk_sum)
        dv.append(dv_sum)

    def whole_rows(parts):
        early, late = parts
        return jnp.concatenate([late[:HALF_SEQ] + early, late[HALF_SEQ:]], axis=0)

    dq = jnp.concatenate(dq_heads, axis=1).T * FACTOR
    dk = whole_rows(dk) * FACTOR
    dv = whole_rows(dv).astype(BF16)
    copies = dq.shape[1] // PAIR
    cosine = jnp.concatenate([cos_ref[...]] * copies, axis=1)
    sine = jnp.concatenate([sin_ref[...]] * copies, axis=1)
    put_back(shift_ref, dq_ref, count, (dq * cosine - turn(dq) * sine).astype(BF16))
    put_back(shift_ref, dk_ref, count, (dk * cosine - turn(dk) * sine).astype(BF16))
    put_back(shift_ref, dv_ref, count, dv)


def attend_back(chain, shift, count, query, key, value, grad, logsum, tables):
    rows, width = query.shape
    grid, tile, sums = attention_specs(rows, width, PAIR)
    return chain.call(
        functools.partial(attend_back_body, count),
        grid,
        [tile] * 4 + [sums] + [whole((SEQ, PAIR))] * 2,
        [tile] * 3,
        [((rows, width), BF16)] * 3,
        flops=40 * rows * width * SEQ,
        prefetch=1,
        moved=14 * rows * width,
    )(shift, query, key, value, grad, logsum, *tables)


def local(
    chips,
    group,
    tokens,
    attn_gain,
    query_weight,
    key_weight,
    value_weight,
    output_weight,
    ffn_gain,
    gate_weight,
    up_weight,
    down_weight,
    cotangent,
):
    line = jnp.asarray(chips.table)[lax.axis_index("dp")]
    rows, model = tokens.shape
    count = SEQ // rows
    shift = lax.axis_index("tensor") % count
    row = jnp.arange(SEQ, dtype=jnp.int32)
    places = rope_tables(row)
    tables = rope_tables((row // rows ^ shift) * rows + row % rows)
    shift = jnp.reshape(shift, (1,)).astype(jnp.int32)
    early = (*places, *tables, line, shift)
    depth, own = query_weight.shape
    hidden_units = gate_weight.shape[1]
    chain = Chain()

    def gather(piece):
        return Gather(chips, chain, chain.join(piece)[0])

    def spread_of(values):
        return Spread(group, chain, chain.join(values)[0])

    def fold_of(part):
        own_part, sent = part
        sent = chain.join(*sent[0], *sent[1])
        return Fold(group, chain, own_part, [sent[: group.bits], sent[group.bits :]])

    def grads_of(left, rights, theirs=None):
        if theirs is None:
            (theirs,) = weight_grads(chain, left, 1, rights)
        got = [None]
        chain.ask(theirs, got, 0, chips.other)

        def mine(**how):
            if got[0] is None:
                chain.flush()
            blocks = weight_grads(chain, left, 0, rights, got[0], chips.bits)
            return Sums(chips, chain, blocks, **how)

        return mine

    extra = jnp.concatenate([attn_gain, ffn_gain, jnp.zeros((4 * own - 2 * depth,), BF16)])
    attn = jnp.concatenate([query_weight, key_weight, value_weight, output_weight.T], axis=1)
    attn = gather(jnp.concatenate([attn, jnp.broadcast_to(extra, (16, 4 * own))], axis=0))
    spread = spread_of(tokens)
    grads_spread = spread_of(cotangent)
    grads_spread.later = []
    down_turned, *early = chain.join(down_weight.T, *early)
    places, tables, line, shift = early[:2], early[2:4], early[4], early[5]
    chain.end(attn, spread, grads_spread)
    chain.end(attn, spread)
    all_tokens = spread.blocks()
    attn = attn.pieces()
    pair = gather(jnp.concatenate([gate_weight, up_weight], axis=1))
    w_query, w_key, w_value, w_output = [Weight(attn, depth, i * own, own) for i in range(4)]
    gains = jnp.concatenate(
        [piece[depth : depth + 1, : 2 * depth].reshape(2, depth) for piece in attn], axis=1
    ).astype(F32)

    group_one = ordered(chain, norm_body, line, gains, all_tokens)
    grads_spread.resume()
    query, key, value = project(chain, group_one, tables, w_query, w_key, w_value)
    mixed, logsum = attend(chain, shift, count, query, key, value)
    out_part = times_trans(chain, [(mixed, w_output)], group)
    fold = fold_of(out_part)
    chain.end(fold, pair, grads_spread)
    grad_rows = ordered(chain, order_body, line, gains, grads_spread.blocks())
    chain.end(fold)
    attended = fold.total()
    middle, second = by_rows(
        chain, middle_body, line, tokens, gains, attended, [], [F32, BF16]
    )
    spread = spread_of(second)
    chain.end(spread, pair)
    pair = pair.pieces()
    down = gather(down_turned)
    chain.end(spread)
    group_two = spread.blocks()
    w_gate = Weight(pair, depth, 0, hidden_units)
    w_up = Weight(pair, depth, hidden_units, hidden_units)
    hidden, slope, silu, theirs = gate_up(chain, group_two, w_gate, w_up, grad_rows)

    mine = grads_of(grad_rows, [hidden], theirs)
    chain.end(down)
    chain.flush()
    down_sum = mine()
    w_down = Weight(down.pieces(), depth, 0, hidden_units)
    gate_grad, up_grad, gate_theirs, up_theirs = hidden_back(
        chain, grad_rows, w_down, slope, silu, group_two
    )
    mine_gate = grads_of(group_two, [gate_grad], gate_theirs)
    chain.end(down_sum)
    second_part = times_trans(chain, [(gate_grad, w_gate), (up_grad, w_up)], group)
    fold = fold_of(second_part)
    gate_sum = mine_gate(hold=True)
    chain.end(down_sum)
    (down_sum,) = finish(chain, down_sum.terms())
    mine_up = grads_of(group_two, [up_grad], up_theirs)
    chain.end(fold)
    up_sum = mine_up(hold=True)
    chain.end(fold)
    second_grad = fold.total()
    middle_grad, low_grad = by_rows(
        chain, second_back_body, line, cotangent, gains, second_grad, [middle], [F32, BF16]
    )
    spread = spread_of(low_grad)
    chain.end(gate_sum)
    gate_sum.resume()
    result_part = times_trans(chain, [(hidden, w_down)], group)
    chain.end(spread)
    chain.end(spread)
    attn_grads = spread.blocks()

    mixed_grad = mixed_back(chain, attn_grads, w_output)
    query_back, key_back, value_back = attend_back(
        chain, shift, count, query, key, value, mixed_grad, logsum, places
    )
    mine_qkv = grads_of(group_one, [query_back, key_back, value_back])
    mine_out = grads_of(attn_grads, [mixed])
    chain.end(gate_sum, up_sum)
    up_sum.resume()
    fold = fold_of(result_part)
    qkv_sum = mine_qkv()
    first_part = times_trans(
        chain, [(query_back, w_query), (key_back, w_key), (value_back, w_value)], group
    )
    out_sum = mine_out(hold=True)
    chain.end(fold)
    gate_sum, gate_inner = finish(chain, gate_sum.terms(), [gate_weight])
    chain.end(up_sum, out_sum, fold)
    result_part = fold.total()
    fold = fold_of(first_part)
    (layer_out,) = by_rows(chain, result_body, line, middle, gains, result_part, [], [BF16])
    up_sum, up_inner = finish(chain, up_sum.terms(), [up_weight])
    chain.end(qkv_sum)
    out_sum.resume()
    chain.end(fold)
    chain.end(fold)
    first_grad = fold.total()
    (input_grad,) = by_rows(
        chain, first_back_body, line, tokens, gains, first_grad, [middle_grad], [F32]
    )
    chain.end(qkv_sum)
    query_sum, key_sum, value_sum, qkv_inner = finish(
        chain, qkv_sum.terms(), [query_weight, key_weight, value_weight]
    )
    gain_parts = jnp.stack(
        [qkv_inner / attn_gain.astype(F32), (gate_inner + up_inner) / ffn_gain.astype(F32)]
    )
    (gain_parts,) = chain.join(gain_parts)
    (out_sum,) = finish(chain, out_sum.terms())
    gain_totals = gain_parts
    for k in range(1, group.size):
        pairs = [(i, i ^ k) for i in range(group.size)]
        gain_totals += lax.ppermute(gain_parts, "tensor", pairs)
    gain_one_total, gain_two_total = gain_totals[0], gain_totals[1]
    return (
        layer_out,
        input_grad,
        gain_one_total,
        query_sum,
        key_sum,
        value_sum,
        out_sum,
        gain_two_total,
        gate_sum,
        up_sum,
        down_sum,
    )


def solution(mesh):
    in_specs = (
        P(("dp", "tensor"), None),
        P("dp"),
        P("dp", "tensor"),
        P("dp", "tensor"),
        P("dp", "tensor"),
        P("tensor", "dp"),
        P("dp"),
        P("dp", "tensor"),
        P("dp", "tensor"),
        P("tensor", "dp"),
        P(("dp", "tensor"), None),
    )
    out_specs = (
        P(("dp", "tensor"), None),
        P(("dp", "tensor"), None),
        P("dp"),
        P("dp", "tensor"),
        P("dp", "tensor"),
        P("dp", "tensor"),
        P("tensor", "dp"),
        P("dp"),
        P("dp", "tensor"),
        P("dp", "tensor"),
        P("tensor", "dp"),
    )
    chips = Chips(mesh.shape["dp"])
    size = mesh.shape["tensor"]
    links = [[(i, i ^ 1 << b) for i in range(size)] for b in range(size.bit_length() - 1)]
    group = Group(links, "tensor")

    def run(*arrays):
        return local(chips, group, *arrays)

    return jax.shard_map(run, mesh=mesh, in_specs=in_specs, out_specs=out_specs, check_vma=False)
```

```python
import functools

import jax
import jax.numpy as jnp
import numpy as np
from jax import lax
from jax.experimental import pallas as pl
from jax.experimental.pallas import tpu as pltpu
from jax.sharding import PartitionSpec as P

HEAD_DIM = 64
SEQ = 512
EPS = 1e-05
THETA = 130000.0
BF16 = jnp.bfloat16
F32 = jnp.float32
FACTOR = HEAD_DIM**-0.5
PAIR = 2 * HEAD_DIM
HALF_SEQ = SEQ // 2
VMEM_LIMIT = 58 << 20
COST_SHARE = 4096


class Chain:
    def __init__(self):
        self.token = jnp.zeros((8, 128), F32)
        self.swaps, self.asked = [], []

    def join(self, *values):
        *values, self.token = lax.optimization_barrier((*values, self.token))
        return values

    def gate(self, *values):
        swaps, self.swaps = self.swaps, []
        asked, self.asked = self.asked, []
        joined = self.join(
            *values, *[held[i] for held, i in swaps], *[source for source, _, _, _ in asked]
        )
        for (held, i), value in zip(swaps, joined[len(values) :]):
            held[i] = value
        for (_, held, i, swap), value in zip(asked, joined[len(values) + len(swaps) :]):
            held[i] = swap(value)
            self.swaps.append((held, i))
        return joined[: len(values)]

    def end(self, *transfers):
        counts = [len(t.flying) for t in transfers]
        got = self.gate(*[value for t in transfers for value in t.flying])
        for t, count in zip(transfers, counts):
            if count:
                t.go_on(got[:count])
            got = got[count:]

    def ask(self, source, held, i, swap):
        self.asked.append((source, held, i, swap))

    def flush(self):
        for source, held, i, swap in self.asked:
            held[i] = swap(source)
        self.asked = []

    def call(self, body, grid, ins, outs, shapes, flops, scratch=(), prefetch=0, moved=0):
        first = prefetch + len(ins)
        second = first + 1 + len(outs)
        anywhere = pl.BlockSpec(memory_space=pl.ANY)

        def wrapped(*refs):
            body(*refs[:first], *refs[first + 1 : second], *refs[second + 1 :])

        run = pl.pallas_call(
            wrapped,
            grid_spec=pltpu.PrefetchScalarGridSpec(
                num_scalar_prefetch=prefetch,
                grid=grid,
                in_specs=[*ins, anywhere],
                out_specs=[*outs, anywhere],
                scratch_shapes=list(scratch),
            ),
            out_shape=[jax.ShapeDtypeStruct(s, t) for s, t in [*shapes, ((8, 128), F32)]],
            compiler_params=pltpu.CompilerParams(
                vmem_limit_bytes=VMEM_LIMIT, dimension_semantics=("arbitrary",) * len(grid)
            ),
            cost_estimate=pl.CostEstimate(
                flops=flops // COST_SHARE, bytes_accessed=moved // COST_SHARE, transcendentals=0
            ),
        )

        def with_token(*args):
            *results, self.token = run(*args, self.token)
            return results

        return with_token


class Chips:
    def __init__(self, size):
        self.bits = (size // 2).bit_length() - 1
        self.size = size
        self.swap = [(i, i ^ 1) for i in range(size)]
        self.links = [
            [(i, i ^ 2 << self.bits - 1 - p) for i in range(size)] for p in range(self.bits)
        ]
        flips = [
            sum(1 << self.bits - 1 - p for p in range(self.bits) if v >> p & 1)
            for v in range(1 << self.bits)
        ]
        table = [[i ^ 2 * f for f in flips] + [i ^ 2 * f ^ 1 for f in flips] for i in range(size)]
        self.table = np.array(table, np.int32)

    def send(self, value, p):
        return lax.ppermute(value, "dp", self.links[p])

    def other(self, value):
        return lax.ppermute(value, "dp", self.swap)


class Gather:
    def __init__(self, chips, chain, piece):
        self.chips, self.chain = chips, chain
        self.own = [piece] + [None] * (2**chips.bits - 1)
        self.others = list(self.own)
        self.ask(0)
        self.keys = [1 << p for p in range(chips.bits)]
        self.flying = [chips.send(piece, p) for p in range(chips.bits)]

    def ask(self, v):
        self.chain.ask(self.own[v], self.others, v, self.chips.other)

    def go_on(self, got):
        keys, self.keys, self.flying = self.keys, [], []
        for v, piece in zip(keys, got):
            self.own[v] = piece
            for p in range(v.bit_length(), self.chips.bits):
                self.keys.append(v | 1 << p)
                self.flying.append(self.chips.send(piece, p))
        for v in keys:
            self.ask(v)

    def pieces(self):
        while self.flying:
            self.chain.end(self)
        self.chain.flush()
        return self.own + self.others


class Sums:
    def __init__(self, chips, chain, mine, apart=False, hold=False, cut_in_two=False):
        self.chips, self.chain, self.apart, self.hold = chips, chain, apart, hold
        self.todo = []
        self.cut_in_two = cut_in_two and chips.bits == 2
        self.parts = [mine[0]]
        mine = list(mine[1:])
        self.direct, self.passed = [], []
        for p in range(chips.bits):
            self.direct.append(mine.pop(0))
            self.passed.append(mine.pop(0) if p else None)
        self.p = chips.bits - 1
        if self.cut_in_two:
            self.kinds = [0, 1]
            self.flying = [chips.send(half, 1) for half in self.in_two(self.passed[1])]
            return
        self.kinds = [self.p]
        self.flying = [chips.send(self.passed[self.p], self.p)]

    def in_two(self, values):
        width = values.shape[1] // 2
        return values[:, :width], values[:, width:]

    def go_on(self, got):
        rows = self.parts[0].shape[0]
        kinds, self.kinds, self.flying = self.kinds, [], []
        if self.p == 0:
            self.parts += got
            return
        if self.cut_in_two:
            self.p = 0
            total = self.direct[0].astype(F32) + jnp.concatenate(got, axis=1).astype(F32)
            self.todo = [(None, self.direct[1], 1), (None, total.astype(BF16), 0)]
            self.resume()
            return
        for kind, block in zip(kinds, got):
            if kind is None:
                self.parts.append(block)
                continue
            add = lambda held, first: (
                held.astype(F32) + block[first * rows : first * rows + held.shape[0]].astype(F32)
            ).astype(BF16)
            for q in range(kind):
                self.direct[q] = add(self.direct[q], (1 << q) - 1)
                if q:
                    self.passed[q] = add(self.passed[q], 1 << q)
        p, self.p = self.p, self.p - 1
        if p > 0:
            self.todo.append((None, self.direct[p], p))
        if p > 1:
            self.todo.append((p - 1, self.passed[p - 1], p - 1))
        if p == 1 and not self.apart:
            self.todo.append((None, self.direct[0], 0))
        if not self.hold:
            self.resume()

    def resume(self):
        todo, self.todo = self.todo, []
        values = self.chain.join(*[value for _, value, _ in todo])
        for (kind, _, p), value in zip(todo, values):
            self.kinds.append(kind)
            self.flying.append(self.chips.send(value, p))

    def send_half(self, i):
        while self.p > 0:
            self.chain.end(self)
        width = self.direct[0].shape[1] // 2
        (value,) = self.chain.join(self.direct[0][:, i * width : (i + 1) * width])
        self.kinds.append(None)
        self.flying.append(self.chips.send(value, 0))

    def terms(self):
        while self.flying or self.todo:
            if self.todo:
                self.resume()
            self.chain.end(self)
        return sorted(self.parts, key=lambda part: -part.shape[1])


class Group:
    def __init__(self, links, axes):
        self.links, self.axes = links, axes
        self.bits = len(links)
        self.size = 1 << self.bits
        self.orders = (list(range(self.bits)), list(range(self.bits))[::-1])

    def send(self, value, bit):
        return lax.ppermute(value, self.axes, self.links[bit])

    def messages(self):
        found = []
        for order in self.orders:
            found.append([])
            for top in reversed(range(self.bits)):
                found[-1].append(
                    [
                        1 << order[top] | sum(1 << order[p] for p in range(top) if v >> p & 1)
                        for v in range(1 << top)
                    ]
                )
        return found


class Spread:
    def __init__(self, group, chain, rows):
        self.group, self.chain = group, chain
        self.held = {0: [rows]}
        self.later = None
        self.keys = [(1 << b, None) for b in range(group.bits)]
        self.flying = [group.send(rows, b) for b in range(group.bits)]

    def go_on(self, got):
        fresh = list(zip(self.keys, got))
        self.keys, self.flying = [], []
        for (k, h), block in fresh:
            if h is None:
                self.held[k] = [block]
            else:
                self.held.setdefault(k, [None, None])[h] = block
        for (k, h), block in fresh:
            for way, order in enumerate(self.group.orders):
                if h is not None and h != way:
                    continue
                half = block.shape[1] // 2
                top = max(i for i, bit in enumerate(order) if k >> bit & 1)
                for i in range(top + 1, len(order)):
                    part = block if h is not None else block[:, way * half : (way + 1) * half]
                    self.keys.append((k | 1 << order[i], way))
                    if self.later is not None:
                        self.later.append((part, order[i]))
                    else:
                        self.flying.append(self.group.send(part, order[i]))

        if self.later:
            parts = self.chain.join(*[part for part, _ in self.later])
            self.later = [(part, bit) for part, (_, bit) in zip(parts, self.later)]

    def resume(self):
        later, self.later = self.later, None
        parts = self.chain.join(*[part for part, _ in later])
        self.flying = [self.group.send(part, bit) for part, (_, bit) in zip(parts, later)]

    def blocks(self):
        while self.flying:
            self.chain.end(self)
        return [self.held[k] for k in range(self.group.size)]


class Fold:
    def __init__(self, group, chain, own, sent):
        self.group, self.chain = group, chain
        self.rows = own[0].shape[0]
        self.sent = [list(half) for half in sent]
        self.parts = [[half] for half in own]
        self.wave = 0
        self.start()

    def start(self):
        self.flying = [
            self.group.send(self.sent[h][self.wave], order[self.group.bits - 1 - self.wave])
            for h, order in enumerate(self.group.orders)
        ]

    def go_on(self, got):
        self.wave += 1
        self.flying = []
        for h, block in enumerate(got):
            self.parts[h].append(block)
        for wave in range(self.wave, self.group.bits):
            sums = add_rows(self.chain, [sent[wave] for sent in self.sent], got)
            for sent, value in zip(self.sent, sums):
                sent[wave] = value
        if self.wave < self.group.bits:
            self.start()

    def total(self):
        while self.flying:
            self.chain.end(self)
        return self.parts


class Weight:
    def __init__(self, pieces, rows, start, width):
        self.pieces, self.rows, self.start, self.width = pieces, rows, start, width
        self.model = len(pieces) * rows

    def tiles(self, tile):
        first = self.start // tile
        return [pl.BlockSpec((self.rows, tile), lambda j: (0, first + j))] * len(self.pieces)


def nn(left, right):
    return lax.dot_general(left, right, (((1,), (0,)), ((), ())), preferred_element_type=F32)


def nt(left, right):
    return lax.dot_general(left, right, (((1,), (1,)), ((), ())), preferred_element_type=F32)


def tn(left, right):
    return lax.dot_general(left, right, (((0,), (0,)), ((), ())), preferred_element_type=F32)


def whole(shape):
    return pl.BlockSpec(shape, lambda *_: (0,) * len(shape))


def place(line_ref, j, width):
    return pl.ds(pl.multiple_of(line_ref[j] * width, 128), width)


def cut(width, j):
    return slice(j * width, (j + 1) * width)


def scale_of(values):
    return lax.rsqrt(jnp.mean(values * values, axis=-1, keepdims=True) + EPS)


def fetch_blocks(counts, refs, held, sems, k, slot, wait):
    first = 0
    for i, count in enumerate(counts):
        copies = []
        half = held.shape[2] // count
        for h in range(count):
            target = held.at[slot, :, pl.ds(h * half, half)]
            copies.append(pltpu.make_async_copy(refs[first + h], target, sems.at[slot, h]))
        first += count

        @pl.when(k == i)
        def _():
            for copy in copies:
                copy.wait() if wait else copy.start()


def fetched(counts, refs, held, sems):
    k = pl.program_id(0)

    @pl.when(k == 0)
    def _():
        fetch_blocks(counts, refs, held, sems, k, 0, False)

    fetch_blocks(counts, refs, held, sems, k + 1, (k + 1) % 2, False)
    fetch_blocks(counts, refs, held, sems, k, k % 2, True)
    return held.at[k % 2]


def norm_body(blocks, counts, line_ref, gain_ref, *refs):
    out_ref, held, sems = refs[sum(counts) :]
    x_ref = fetched(counts, refs, held, sems)
    width = out_ref.shape[1] // blocks
    scale = scale_of(x_ref[...].astype(F32))
    for j in range(blocks):
        part = x_ref[:, place(line_ref, j, width)].astype(F32)
        gain = gain_ref[0:1, cut(width, j)]
        out_ref[:, cut(width, j)] = (part * scale * gain).astype(BF16)


def order_body(blocks, counts, line_ref, gain_ref, *refs):
    out_ref, held, sems = refs[sum(counts) :]
    x_ref = fetched(counts, refs, held, sems)
    width = out_ref.shape[1] // blocks
    for j in range(blocks):
        out_ref[:, cut(width, j)] = x_ref[:, place(line_ref, j, width)]


def ordered(chain, body, line, gains, held):
    counts = [len(block) for block in held]
    rows, model = held[0][0].shape
    n = len(held)
    return chain.call(
        functools.partial(body, line.shape[0], counts),
        (n,),
        [whole(gains.shape)] + [pl.BlockSpec(memory_space=pl.ANY)] * sum(counts),
        [pl.BlockSpec((rows, model), lambda k, *_: (k, 0))],
        [((n * rows, model), BF16)],
        flops=20 * n * rows * model,
        scratch=[pltpu.VMEM((2, rows, model), BF16), pltpu.SemaphoreType.DMA((2, 2))],
        prefetch=1,
        moved=4 * n * rows * model,
    )(line, gains, *[array for block in held for array in block])[0]


def added(refs, span):
    total = refs[0][span, :].astype(F32)
    for ref in refs[1:]:
        total += ref[span, :].astype(F32)
    return total


def middle_body(blocks, m, line_ref, x_ref, gain_ref, *refs):
    middle_ref, out_ref = refs[2 * m :]
    width = x_ref.shape[1] // blocks
    half = x_ref.shape[1] // 2
    span = slice(None)
    middle_ref[:, :half] = added(refs[:m], span)
    middle_ref[:, half:] = added(refs[m : 2 * m], span)
    for j in range(blocks):
        here = x_ref[:, place(line_ref, j, width)].astype(F32)
        middle_ref[:, cut(width, j)] += here
    middle = middle_ref[...]
    out_ref[...] = (middle * scale_of(middle) * gain_ref[1:2, :]).astype(BF16)


def result_body(blocks, m, line_ref, middle_ref, gain_ref, *refs):
    out_ref = refs[2 * m]
    width = middle_ref.shape[1] // blocks
    span = slice(None)
    total = middle_ref[...] + jnp.concatenate(
        [added(refs[:m], span), added(refs[m : 2 * m], span)], axis=1
    )
    for j in range(blocks):
        out_ref[:, place(line_ref, j, width)] = total[:, cut(width, j)].astype(BF16)


def second_back_body(blocks, m, line_ref, dy_ref, gain_ref, *refs):
    middle_ref, out_ref, low_ref = refs[2 * m :]
    width = dy_ref.shape[1] // blocks
    span = slice(None)
    grad = jnp.concatenate([added(refs[:m], span), added(refs[m : 2 * m], span)], axis=1)
    middle = middle_ref[...]
    scale = scale_of(middle)
    normed = middle * scale
    scaled = grad * gain_ref[1:2, :]
    out_ref[...] = scale * (scaled - normed * jnp.mean(scaled * normed, axis=-1, keepdims=True))
    for j in range(blocks):
        out_ref[:, cut(width, j)] += dy_ref[:, place(line_ref, j, width)].astype(F32)
    low_ref[...] = out_ref[...].astype(BF16)


def first_back_body(blocks, m, line_ref, x_ref, gain_ref, *refs):
    above_ref, out_ref = refs[2 * m :]
    width = x_ref.shape[1] // blocks
    span = slice(None)
    scale = scale_of(x_ref[...].astype(F32))
    normed = jnp.concatenate(
        [x_ref[:, place(line_ref, j, width)].astype(F32) for j in range(blocks)], axis=1
    ) * scale
    grad = jnp.concatenate([added(refs[:m], span), added(refs[m : 2 * m], span)], axis=1)
    scaled = grad * gain_ref[0:1, :]
    back = scale * (scaled - normed * jnp.mean(scaled * normed, axis=-1, keepdims=True))
    total = above_ref[...] + back
    for j in range(blocks):
        out_ref[:, place(line_ref, j, width)] = total[:, cut(width, j)]


def by_rows(chain, body, line, first, gains, parts, more, kinds):
    rows, model = first.shape
    half = model // 2
    tile = min(128, rows)
    row = pl.BlockSpec((tile, model), lambda i, *_: (i, 0))
    slim = pl.BlockSpec((tile, half), lambda i, *_: (i, 0))
    m = len(parts[0])
    return chain.call(
        functools.partial(body, line.shape[0], m),
        (rows // tile,),
        [row, whole(gains.shape)] + [slim] * (2 * m) + [row] * len(more),
        [row] * len(kinds),
        [((rows, model), kind) for kind in kinds],
        flops=20 * rows * model,
        prefetch=1,
        moved=rows * model * (2 * m + 4 * len(kinds)),
    )(line, first, gains, *parts[0], *parts[1], *more)


def add_rows_body(count, *refs):
    for i in range(count):
        total = refs[i][...].astype(F32) + refs[count + i][...].astype(F32)
        refs[2 * count + i][...] = total.astype(BF16)


def add_rows(chain, helds, blocks):
    rows, columns = helds[0].shape
    tile = min(128, rows)
    steps = rows // tile
    count = len(helds)
    here = pl.BlockSpec((tile, columns), lambda i: (i, 0))
    return chain.call(
        functools.partial(add_rows_body, count),
        (steps,),
        [here] * count + [pl.BlockSpec((tile, columns), lambda i: (steps + i, 0))] * count,
        [here] * count,
        [((rows, columns), BF16)] * count,
        flops=count * rows * columns,
        moved=6 * count * rows * columns,
    )(*helds, *blocks)


def finish_body(m, halves, n, *refs):
    total = added(refs[:m], slice(None))
    if halves:
        total += jnp.concatenate([ref[...].astype(F32) for ref in refs[m : m + halves]], axis=1)
    m += halves
    weights, outs = refs[m : m + n], refs[m + n :]
    if not n:
        outs[0][...] = total.T
        return
    width = weights[0].shape[1]
    inner = jnp.zeros((total.shape[0], 1), F32)
    for i in range(n):
        part = total[:, cut(width, i)]
        outs[i][...] = part
        inner += jnp.sum(weights[i][...].astype(F32) * part, axis=1, keepdims=True)
    outs[n][...] = jnp.broadcast_to(inner, outs[n].shape)


def finish(chain, terms, weights=()):
    rows, columns = terms[0].shape
    tile = min(128, rows)
    row = pl.BlockSpec((tile, columns), lambda i: (i, 0))
    n = len(weights)
    halves = sum(1 for term in terms if term.shape[1] < columns)
    half = [pl.BlockSpec((tile, columns // 2), lambda i: (i, 0))] * halves
    if n:
        slim = pl.BlockSpec((tile, columns // n), lambda i: (i, 0))
        outs = [slim] * n + [pl.BlockSpec((tile, 128), lambda i: (i, 0))]
        shapes = [((rows, columns // n), F32)] * n + [((rows, 128), F32)]
    else:
        slim = None
        outs = [pl.BlockSpec((columns, tile), lambda i: (0, i))]
        shapes = [((columns, rows), F32)]
    results = chain.call(
        functools.partial(finish_body, len(terms) - halves, halves, n),
        (rows // tile,),
        [row] * (len(terms) - halves) + half + [slim] * n,
        outs,
        shapes,
        flops=4 * rows * columns,
        moved=rows * columns * 12,
    )(*terms, *weights)
    if n:
        results[n] = results[n][:, 0]
    return results


def rope_tables(place):
    half = HEAD_DIM // 2
    freq = THETA ** (-2.0 * jnp.arange(half, dtype=F32) / HEAD_DIM)
    angle = place.astype(F32)[:, None] * freq[None, :]
    cosine, sine = jnp.cos(angle), jnp.sin(angle)
    return (
        jnp.concatenate([cosine] * (PAIR // half), axis=1),
        jnp.concatenate([-sine, sine] * (PAIR // HEAD_DIM), axis=1),
    )


def turn(values):
    half = HEAD_DIM // 2
    width = values.shape[-1]
    lane = lax.broadcasted_iota(jnp.int32, values.shape, 1) % HEAD_DIM
    return jnp.where(
        lane < half, pltpu.roll(values, width - half, 1), pltpu.roll(values, half, 1)
    )


def joined(refs):
    return jnp.concatenate([r[...] for r in refs], axis=0)


def qkv_body(n, x_ref, cos_ref, sin_ref, *refs):
    weights, outs = refs[: 3 * n], refs[3 * n :]
    rows = x_ref.shape[0]
    tile = outs[0].shape[1]
    for i in range(3):
        weight = joined(weights[i * n : (i + 1) * n])
        for s in range(rows // SEQ):
            span = slice(s * SEQ, (s + 1) * SEQ)
            product = nn(x_ref[span, :], weight)
            if i == 2:
                outs[i][span, :] = product.astype(BF16)
                continue
            for t in range(tile // PAIR):
                here = product[:, t * PAIR : (t + 1) * PAIR]
                turned = here * cos_ref[...] + turn(here) * sin_ref[...]
                outs[i][span, t * PAIR : (t + 1) * PAIR] = turned.astype(BF16)


def project(chain, x, tables, query, key, value):
    rows, model = x.shape
    n, width = len(query.pieces), query.width
    tile = min(256, width)
    out = pl.BlockSpec((rows, tile), lambda j: (0, j))
    return chain.call(
        functools.partial(qkv_body, n),
        (width // tile,),
        [whole(x.shape), whole((SEQ, PAIR)), whole((SEQ, PAIR))]
        + query.tiles(tile)
        + key.tiles(tile)
        + value.tiles(tile),
        [out] * 3,
        [((rows, width), BF16)] * 3,
        flops=6 * rows * model * width,
        moved=2 * (rows * model + 3 * model * width + 3 * rows * width),
    )(x, *tables, *query.pieces, *key.pieces, *value.pieces)


def collect(counts, refs, held, sems):
    rows = held.shape[0] // len(counts)
    copies = []
    for k, count in enumerate(counts):
        half = held.shape[1] // count
        for h in range(count):
            target = held.at[pl.ds(k * rows, rows), pl.ds(h * half, half)]
            i = len(copies)
            copies.append(pltpu.make_async_copy(refs[i], target, sems.at[i]))
    for copy in copies:
        copy.start()
    for copy in copies:
        copy.wait()


def gate_body(n, counts, *refs):
    m = sum(counts)
    gate_w, up_w = refs[m : m + n], refs[m + n : m + 2 * n]
    left_ref, hidden_ref, slope_ref, silu_ref, theirs_ref, x_ref, turned, sems = refs[m + 2 * n :]

    @pl.when(pl.program_id(0) == 0)
    def _():
        collect(counts, refs, x_ref, sems)
        turned[...] = left_ref[...].T

    gate_weight, up_weight = joined(gate_w), joined(up_w)
    for s in range(x_ref.shape[0] // SEQ):
        span = slice(s * SEQ, (s + 1) * SEQ)
        gate = nn(x_ref[span, :], gate_weight)
        up = nn(x_ref[span, :], up_weight)
        sigm = jax.nn.sigmoid(gate)
        silu = gate * sigm
        hidden_ref[span, :] = (silu * up).astype(BF16)
        silu_ref[span, :] = silu.astype(BF16)
        slope_ref[span, :] = (up * sigm * (1.0 + gate * (1.0 - sigm))).astype(BF16)
    theirs_ref[...] = nn(turned[...], hidden_ref[...]).astype(BF16)


def collected(held):
    counts = [len(block) for block in held]
    rows, model = held[0][0].shape
    scratch = [
        pltpu.VMEM((len(held) * rows, model), BF16),
        pltpu.SemaphoreType.DMA((sum(counts),)),
    ]
    arrays = [array for block in held for array in block]
    return counts, arrays, [pl.BlockSpec(memory_space=pl.ANY)] * len(arrays), scratch


def gate_up(chain, held, gate, up, grads):
    counts, arrays, specs, scratch = collected(held)
    rows, model = scratch[0].shape
    n, width = len(gate.pieces), gate.width
    tile = min(256, width)
    out = pl.BlockSpec((rows, tile), lambda j: (0, j))
    half = model // 2
    return chain.call(
        functools.partial(gate_body, n, counts),
        (width // tile,),
        specs
        + gate.tiles(tile)
        + up.tiles(tile)
        + [pl.BlockSpec((rows, half), lambda j: (0, 1))],
        [out] * 3 + [pl.BlockSpec((half, tile), lambda j: (0, j))],
        [((rows, width), BF16)] * 3 + [((half, width), BF16)],
        flops=6 * rows * model * width,
        scratch=[scratch[0], pltpu.VMEM((half, rows), BF16), scratch[1]],
        moved=2 * (rows * model + 2 * model * width + 3 * rows * width),
    )(*arrays, *gate.pieces, *up.pieces, grads)


def half_blocks(left, which):
    lefts = [block[0] if len(block) == 1 else block[which] for block in left]
    rows, half = lefts[0].shape[0], left[0][0].shape[1] // 2
    places = [which if len(block) == 1 else 0 for block in left]
    return lefts, [
        pl.BlockSpec((rows, half), functools.partial(lambda at, j: (0, at), at)) for at in places
    ]


def hidden_back_body(n, blocks, g_ref, *refs):
    weights, slope_ref, silu_ref = refs[:n], refs[n], refs[n + 1]
    lefts, refs = refs[n + 2 : n + 2 + blocks], refs[n + 2 + blocks :]
    gate_ref, up_ref, gate_theirs, up_theirs, turned = refs
    rows = turned.shape[1] // blocks

    @pl.when(pl.program_id(0) == 0)
    def _():
        for k in range(blocks):
            turned[:, cut(rows, k)] = lefts[k][...].T

    weight = joined(weights)
    for s in range(g_ref.shape[0] // SEQ):
        span = slice(s * SEQ, (s + 1) * SEQ)
        grad = nn(g_ref[span, :], weight)
        gate_ref[span, :] = (grad * slope_ref[span, :].astype(F32)).astype(BF16)
        up_ref[span, :] = (grad * silu_ref[span, :].astype(F32)).astype(BF16)
    gate_theirs[...] = nn(turned[...], gate_ref[...]).astype(BF16)
    up_theirs[...] = nn(turned[...], up_ref[...]).astype(BF16)


def hidden_back(chain, grads, down, slope, silu, left):
    rows, model = grads.shape
    n, width = len(down.pieces), down.width
    tile = min(256, width)
    out = pl.BlockSpec((rows, tile), lambda j: (0, j))
    lefts, specs = half_blocks(left, 1)
    half = model // 2
    return chain.call(
        functools.partial(hidden_back_body, n, len(lefts)),
        (width // tile,),
        [whole(grads.shape)] + down.tiles(tile) + [out] * 2 + specs,
        [out] * 2 + [pl.BlockSpec((half, tile), lambda j: (0, j))] * 2,
        [((rows, width), BF16)] * 2 + [((half, width), BF16)] * 2,
        flops=4 * rows * model * width,
        scratch=[pltpu.VMEM((half, rows), BF16)],
        moved=2 * (rows * model + model * width + 4 * rows * width),
    )(grads, *down.pieces, slope, silu, *lefts)


def mixed_back_body(n, counts, *refs):
    m = sum(counts)
    out_ref, x_ref, sems = refs[m + n :]

    @pl.when(pl.program_id(0) == 0)
    def _():
        collect(counts, refs, x_ref, sems)

    out_ref[...] = nn(x_ref[...], joined(refs[m : m + n])).astype(BF16)


def mixed_back(chain, held, out):
    counts, arrays, specs, scratch = collected(held)
    rows, model = scratch[0].shape
    n, width = len(out.pieces), out.width
    tile = min(256, width)
    return chain.call(
        functools.partial(mixed_back_body, n, counts),
        (width // tile,),
        specs + out.tiles(tile),
        [pl.BlockSpec((rows, tile), lambda j: (0, j))],
        [((rows, width), BF16)],
        flops=2 * rows * model * width,
        scratch=scratch,
        moved=2 * (rows * model + model * width + rows * width),
    )(*arrays, *out.pieces)[0]


def trans_body(n, starts, targets, *refs):
    parts, blocks = len(starts), len(targets[0])
    lefts = refs[:parts]
    pieces = refs[parts : parts * (n + 1)]
    outs = refs[parts * (n + 1) : -4]
    held, ready, sems, out_sems = refs[-4:]
    j = pl.program_id(0)
    depth, width = held.shape[2:]
    rows = ready.shape[1] // blocks

    def copy(i, p, slot):
        source = pieces[p * n + i].at[pl.ds(0, depth), pl.ds(starts[p], width)]
        return pltpu.make_async_copy(source, held.at[slot, p], sems.at[slot, p])

    def fetch(step, slot):
        for i in range(n):

            @pl.when(step == i)
            def _():
                for p in range(parts):
                    copy(i, p, slot).start()

    def leave(slot, k, array, first, column):
        target = outs[array].at[pl.ds(first, rows), pl.ds(column, depth)]
        source = ready.at[slot, pl.ds(k * rows, rows), :]
        return pltpu.make_async_copy(source, target, out_sems.at[slot, k])

    def left(slot):
        for k in range(blocks):
            leave(slot, k, 0, 0, 0).wait()

    @pl.when(j == 0)
    def _():
        fetch(j, 0)

    @pl.when(j + 1 < n)
    def _():
        fetch(j + 1, (j + 1) % 2)

    slot = j % 2
    for p in range(parts):
        copy(0, p, slot).wait()

    @pl.when(j >= 2)
    def _():
        left(slot)

    for s in range(blocks * rows // SEQ):
        span = slice(s * SEQ, (s + 1) * SEQ)
        total = nt(lefts[0][span, :], held[slot, 0])
        for p in range(1, parts):
            total += nt(lefts[p][span, :], held[slot, p])
        ready[slot, span, :] = total.astype(BF16)
    column = pl.multiple_of(j % (n // 2) * depth, 128)
    for h in range(2):

        @pl.when((j >= n // 2) == (h == 1))
        def _():
            for k, (array, first) in enumerate(targets[h]):
                leave(slot, k, array, first, column).start()

    @pl.when(j == n - 1)
    def _():
        left(1 - slot)
        left(slot)


def times_trans(chain, parts, group):
    weights = [weight for _, weight in parts]
    n, depth, width = len(weights[0].pieces), weights[0].rows, weights[0].width
    rows = parts[0][0].shape[0]
    half = weights[0].model // 2
    size = rows // group.size
    messages = group.messages()
    shapes = [((size, half), BF16)] * 2
    targets = [{0: (0, 0)}, {0: (1, 0)}]
    for h in range(2):
        for keys in messages[h]:
            for i, k in enumerate(keys):
                targets[h][k] = (len(shapes), i * size)
            shapes.append(((len(keys) * size, half), BF16))
    targets = [[t[k] for k in range(group.size)] for t in targets]
    anywhere = pl.BlockSpec(memory_space=pl.ANY)
    outs = chain.call(
        functools.partial(trans_body, n, [weight.start for weight in weights], targets),
        (n,),
        [whole((rows, width))] * len(parts) + [anywhere] * (n * len(parts)),
        [anywhere] * len(shapes),
        shapes,
        flops=4 * rows * half * width * len(parts),
        scratch=[
            pltpu.VMEM((2, len(parts), depth, width), BF16),
            pltpu.VMEM((2, rows, depth), BF16),
            pltpu.SemaphoreType.DMA((2, len(parts))),
            pltpu.SemaphoreType.DMA((2, group.size)),
        ],
        moved=2 * (2 * rows * half + len(parts) * (rows + 2 * half) * width),
    )(*[left for left, _ in parts], *[piece for weight in weights for piece in weight.pieces])
    m = group.bits
    return outs[:2], [outs[2 : 2 + m], outs[2 + m :]]


def grad_body(parts, got, blocks, steps, *refs):
    lefts, refs = refs[:blocks], refs[blocks:]
    rights, refs = refs[:parts], refs[parts:]
    got_ref = refs[0] if got else None
    outs, turned = refs[got:-1], refs[-1]
    j = pl.program_id(0)

    @pl.when(j == 0)
    def _():
        rows = turned.shape[1] // blocks
        for k in range(blocks):
            turned[:, cut(rows, k)] = lefts[k][...].T

    for i in range(parts):

        @pl.when((j >= i * steps) & (j < (i + 1) * steps))
        def _():
            total = nn(turned[...], rights[i][...])
            if got:
                total += got_ref[...].astype(F32)
            total = total.astype(BF16)
            first = 0
            for out_ref in outs:
                count = out_ref.shape[0]
                out_ref[...] = total[first : first + count]
                first += count


def weight_grads(chain, left, which, rights, got=None, bits=0):
    rows, width = rights[0].shape
    parts = len(rights)
    tile = min(512, width)
    steps = width // tile
    lefts, ins = half_blocks(left if isinstance(left, list) else [[left]], which)
    blocks, half = len(lefts), ins[0].block_shape[1]
    for i in range(parts):
        ins.append(
            pl.BlockSpec(
                (rows, tile),
                functools.partial(
                    lambda first, j: (0, jnp.clip(j - first, 0, steps - 1)), i * steps
                ),
            )
        )
    column = lambda j: (0, j)
    more = [] if got is None else [got]
    sizes = [half >> bits]
    for p in range(bits):
        sizes += [sizes[0], ((1 << p) - 1) * sizes[0]] if p else [sizes[0]]
    return chain.call(
        functools.partial(grad_body, parts, len(more), blocks, steps),
        (parts * steps,),
        ins + [pl.BlockSpec((half, tile), column)] * len(more),
        [pl.BlockSpec((size, tile), column) for size in sizes],
        [((size, parts * width), BF16) for size in sizes],
        flops=2 * rows * half * width * parts,
        scratch=[pltpu.VMEM((half, rows), BF16)],
        moved=2 * (rows * half + parts * (rows + half) * width),
    )(*lefts, *rights, *more)


def causal(scores):
    past = scores.shape[0] - HALF_SEQ
    key = lax.broadcasted_iota(jnp.int32, (HALF_SEQ, HALF_SEQ), 0)
    query = lax.broadcasted_iota(jnp.int32, (HALF_SEQ, HALF_SEQ), 1)
    last = jnp.where(key <= query, scores[past:], -1e30)
    return last if past == 0 else jnp.concatenate([scores[:past], last], axis=0)


def head_of(h):
    return slice(h * HEAD_DIM, (h + 1) * HEAD_DIM)


def span_of(b):
    return slice(b * HALF_SEQ, (b + 1) * HALF_SEQ)


def in_place(shift_ref, ref, count):
    rows = SEQ // count
    spans = [pl.ds(pl.multiple_of((i ^ shift_ref[0]) * rows, rows), rows) for i in range(count)]
    return jnp.concatenate([ref[span, :] for span in spans], axis=0)


def put_back(shift_ref, ref, count, values):
    rows = SEQ // count
    for i in range(count):
        ref[pl.ds(pl.multiple_of((i ^ shift_ref[0]) * rows, rows), rows), :] = values[cut(rows, i)]


def one_head(values, h):
    lane = lax.broadcasted_iota(jnp.int32, values.shape, 1)
    return jnp.where(lane // HEAD_DIM == h, values, jnp.zeros_like(values))


def attend_body(count, shift_ref, q_ref, k_ref, v_ref, out_ref, sum_ref):
    queries, keys = in_place(shift_ref, q_ref, count), in_place(shift_ref, k_ref, count)
    values = in_place(shift_ref, v_ref, count).astype(F32).T.astype(BF16)
    heads = []
    for h in range(q_ref.shape[1] // HEAD_DIM):
        blocks = []
        for b in range(2):
            reach = (b + 1) * HALF_SEQ
            query = one_head(queries[span_of(b)] * BF16(FACTOR), h)
            scores = causal(nt(keys[:reach], query))
            top = jnp.max(scores, axis=0, keepdims=True)
            expo = jnp.exp(scores - top)
            total = jnp.sum(expo, axis=0, keepdims=True)
            mixed = nn(values[head_of(h), :reach], expo.astype(BF16))
            blocks.append(mixed * (1.0 / total))
            sum_ref[0, h, :, span_of(b)] = top + jnp.log(total)
        heads.append(jnp.concatenate(blocks, axis=1))
    put_back(shift_ref, out_ref, count, jnp.concatenate(heads, axis=0).T.astype(BF16))


def attention_specs(rows, width, wide):
    wide = min(wide, width)
    tile = pl.BlockSpec((SEQ, wide), lambda s, p, _: (s, p))
    sums = pl.BlockSpec((1, wide // HEAD_DIM, 1, SEQ), lambda s, p, _: (s, p, 0, 0))
    return (rows // SEQ, width // wide), tile, sums


def attend(chain, shift, count, query, key, value):
    rows, width = query.shape
    grid, tile, sums = attention_specs(rows, width, 256)
    return chain.call(
        functools.partial(attend_body, count),
        grid,
        [tile] * 3,
        [tile, sums],
        [((rows, width), BF16), ((rows // SEQ, width // HEAD_DIM, 1, SEQ), F32)],
        flops=16 * rows * width * SEQ,
        prefetch=1,
        moved=8 * rows * width,
    )(shift, query, key, value)


def attend_back_body(
    count, shift_ref, q_ref, k_ref, v_ref, g_ref, sum_ref, cos_ref, sin_ref, dq_ref, dk_ref, dv_ref
):
    queries, keys, values, grads = (
        in_place(shift_ref, ref, count) for ref in (q_ref, k_ref, v_ref, g_ref)
    )
    turned = keys.astype(F32).T.astype(BF16)
    dq_heads = []
    dk, dv = [], []
    for b in range(2):
        reach = (b + 1) * HALF_SEQ
        dq, dk_sum, dv_sum = [], None, None
        for h in range(q_ref.shape[1] // HEAD_DIM):
            query = one_head(queries[span_of(b)], h)
            grad = one_head(grads[span_of(b)], h)
            scores = causal(nt(keys[:reach], query * BF16(FACTOR)))
            probs = jnp.exp(scores - sum_ref[0, h, :, span_of(b)])
            probs_grad = nt(values[:reach], grad)
            inner = jnp.sum(probs * probs_grad, axis=0, keepdims=True)
            score_grad = (probs * (probs_grad - inner)).astype(BF16)
            dv_part, dk_part = nn(probs.astype(BF16), grad), nn(score_grad, query)
            dv_sum = dv_part if dv_sum is None else dv_sum + dv_part
            dk_sum = dk_part if dk_sum is None else dk_sum + dk_part
            dq.append(nn(turned[head_of(h), :reach], score_grad))
        dq_heads.append(jnp.concatenate(dq, axis=0))
        dk.append(dk_sum)
        dv.append(dv_sum)

    def whole_rows(parts):
        early, late = parts
        return jnp.concatenate([late[:HALF_SEQ] + early, late[HALF_SEQ:]], axis=0)

    dq = jnp.concatenate(dq_heads, axis=1).T * FACTOR
    dk = whole_rows(dk) * FACTOR
    dv = whole_rows(dv).astype(BF16)
    copies = dq.shape[1] // PAIR
    cosine = jnp.concatenate([cos_ref[...]] * copies, axis=1)
    sine = jnp.concatenate([sin_ref[...]] * copies, axis=1)
    put_back(shift_ref, dq_ref, count, (dq * cosine - turn(dq) * sine).astype(BF16))
    put_back(shift_ref, dk_ref, count, (dk * cosine - turn(dk) * sine).astype(BF16))
    put_back(shift_ref, dv_ref, count, dv)


def attend_back(chain, shift, count, query, key, value, grad, logsum, tables):
    rows, width = query.shape
    grid, tile, sums = attention_specs(rows, width, PAIR)
    return chain.call(
        functools.partial(attend_back_body, count),
        grid,
        [tile] * 4 + [sums] + [whole((SEQ, PAIR))] * 2,
        [tile] * 3,
        [((rows, width), BF16)] * 3,
        flops=40 * rows * width * SEQ,
        prefetch=1,
        moved=14 * rows * width,
    )(shift, query, key, value, grad, logsum, *tables)


def local(
    chips,
    group,
    tokens,
    attn_gain,
    query_weight,
    key_weight,
    value_weight,
    output_weight,
    ffn_gain,
    gate_weight,
    up_weight,
    down_weight,
    cotangent,
):
    line = jnp.asarray(chips.table)[lax.axis_index("dp")]
    rows, model = tokens.shape
    count = SEQ // rows
    shift = lax.axis_index("tensor") % count
    row = jnp.arange(SEQ, dtype=jnp.int32)
    places = rope_tables(row)
    tables = rope_tables((row // rows ^ shift) * rows + row % rows)
    shift = jnp.reshape(shift, (1,)).astype(jnp.int32)
    early = (*places, *tables, line, shift)
    depth, own = query_weight.shape
    hidden_units = gate_weight.shape[1]
    chain = Chain()

    def gather(piece):
        return Gather(chips, chain, chain.join(piece)[0])

    def spread_of(values):
        return Spread(group, chain, chain.join(values)[0])

    def fold_of(part):
        own_part, sent = part
        sent = chain.join(*sent[0], *sent[1])
        return Fold(group, chain, own_part, [sent[: group.bits], sent[group.bits :]])

    def grads_of(left, rights, theirs=None):
        if theirs is None:
            (theirs,) = weight_grads(chain, left, 1, rights)
        got = [None]
        chain.ask(theirs, got, 0, chips.other)

        def mine(**how):
            if got[0] is None:
                chain.flush()
            blocks = weight_grads(chain, left, 0, rights, got[0], chips.bits)
            return Sums(chips, chain, blocks, **how)

        return mine

    extra = jnp.concatenate([attn_gain, ffn_gain, jnp.zeros((4 * own - 2 * depth,), BF16)])
    attn = jnp.concatenate([query_weight, key_weight, value_weight, output_weight.T], axis=1)
    attn = gather(jnp.concatenate([attn, jnp.broadcast_to(extra, (16, 4 * own))], axis=0))
    spread = spread_of(tokens)
    grads_spread = spread_of(cotangent)
    grads_spread.later = []
    down_turned, *early = chain.join(down_weight.T, *early)
    places, tables, line, shift = early[:2], early[2:4], early[4], early[5]
    chain.end(attn, spread, grads_spread)
    chain.end(attn, spread)
    all_tokens = spread.blocks()
    attn = attn.pieces()
    pair = gather(jnp.concatenate([gate_weight, up_weight], axis=1))
    w_query, w_key, w_value, w_output = [Weight(attn, depth, i * own, own) for i in range(4)]
    gains = jnp.concatenate(
        [piece[depth : depth + 1, : 2 * depth].reshape(2, depth) for piece in attn], axis=1
    ).astype(F32)

    group_one = ordered(chain, norm_body, line, gains, all_tokens)
    grads_spread.resume()
    query, key, value = project(chain, group_one, tables, w_query, w_key, w_value)
    mixed, logsum = attend(chain, shift, count, query, key, value)
    out_part = times_trans(chain, [(mixed, w_output)], group)
    fold = fold_of(out_part)
    chain.end(fold, pair, grads_spread)
    grad_rows = ordered(chain, order_body, line, gains, grads_spread.blocks())
    chain.end(fold)
    attended = fold.total()
    middle, second = by_rows(
        chain, middle_body, line, tokens, gains, attended, [], [F32, BF16]
    )
    spread = spread_of(second)
    chain.end(spread, pair)
    pair = pair.pieces()
    down = gather(down_turned)
    chain.end(spread)
    group_two = spread.blocks()
    w_gate = Weight(pair, depth, 0, hidden_units)
    w_up = Weight(pair, depth, hidden_units, hidden_units)
    hidden, slope, silu, theirs = gate_up(chain, group_two, w_gate, w_up, grad_rows)

    mine = grads_of(grad_rows, [hidden], theirs)
    chain.end(down)
    chain.flush()
    down_sum = mine()
    w_down = Weight(down.pieces(), depth, 0, hidden_units)
    gate_grad, up_grad, gate_theirs, up_theirs = hidden_back(
        chain, grad_rows, w_down, slope, silu, group_two
    )
    mine_gate = grads_of(group_two, [gate_grad], gate_theirs)
    chain.end(down_sum)
    second_part = times_trans(chain, [(gate_grad, w_gate), (up_grad, w_up)], group)
    fold = fold_of(second_part)
    gate_sum = mine_gate(hold=True)
    chain.end(down_sum)
    (down_sum,) = finish(chain, down_sum.terms())
    mine_up = grads_of(group_two, [up_grad], up_theirs)
    chain.end(fold)
    up_sum = mine_up(hold=True)
    chain.end(fold)
    second_grad = fold.total()
    middle_grad, low_grad = by_rows(
        chain, second_back_body, line, cotangent, gains, second_grad, [middle], [F32, BF16]
    )
    spread = spread_of(low_grad)
    chain.end(gate_sum)
    gate_sum.resume()
    result_part = times_trans(chain, [(hidden, w_down)], group)
    chain.end(spread)
    chain.end(spread)
    attn_grads = spread.blocks()

    mixed_grad = mixed_back(chain, attn_grads, w_output)
    query_back, key_back, value_back = attend_back(
        chain, shift, count, query, key, value, mixed_grad, logsum, places
    )
    mine_qkv = grads_of(group_one, [query_back, key_back, value_back])
    mine_out = grads_of(attn_grads, [mixed])
    chain.end(gate_sum, up_sum)
    up_sum.resume()
    fold = fold_of(result_part)
    qkv_sum = mine_qkv()
    first_part = times_trans(
        chain, [(query_back, w_query), (key_back, w_key), (value_back, w_value)], group
    )
    out_sum = mine_out(hold=True)
    chain.end(fold)
    gate_sum, gate_inner = finish(chain, gate_sum.terms(), [gate_weight])
    chain.end(fold)
    result_part = fold.total()
    (layer_out,) = by_rows(chain, result_body, line, middle, gains, result_part, [], [BF16])
    fold = fold_of(first_part)
    chain.end(up_sum, out_sum)
    chain.end(qkv_sum)
    out_sum.resume()
    up_sum, up_inner = finish(chain, up_sum.terms(), [up_weight])
    chain.end(fold)
    chain.end(fold)
    first_grad = fold.total()
    (input_grad,) = by_rows(
        chain, first_back_body, line, tokens, gains, first_grad, [middle_grad], [F32]
    )
    chain.end(qkv_sum)
    query_sum, key_sum, value_sum, qkv_inner = finish(
        chain, qkv_sum.terms(), [query_weight, key_weight, value_weight]
    )
    gain_parts = jnp.stack(
        [qkv_inner / attn_gain.astype(F32), (gate_inner + up_inner) / ffn_gain.astype(F32)]
    )
    (gain_parts,) = chain.join(gain_parts)
    (out_sum,) = finish(chain, out_sum.terms())
    gain_totals = gain_parts
    for k in range(1, group.size):
        pairs = [(i, i ^ k) for i in range(group.size)]
        gain_totals += lax.ppermute(gain_parts, "tensor", pairs)
    gain_one_total, gain_two_total = gain_totals[0], gain_totals[1]
    return (
        layer_out,
        input_grad,
        gain_one_total,
        query_sum,
        key_sum,
        value_sum,
        out_sum,
        gain_two_total,
        gate_sum,
        up_sum,
        down_sum,
    )


def solution(mesh):
    in_specs = (
        P(("dp", "tensor"), None),
        P("dp"),
        P("dp", "tensor"),
        P("dp", "tensor"),
        P("dp", "tensor"),
        P("tensor", "dp"),
        P("dp"),
        P("dp", "tensor"),
        P("dp", "tensor"),
        P("tensor", "dp"),
        P(("dp", "tensor"), None),
    )
    out_specs = (
        P(("dp", "tensor"), None),
        P(("dp", "tensor"), None),
        P("dp"),
        P("dp", "tensor"),
        P("dp", "tensor"),
        P("dp", "tensor"),
        P("tensor", "dp"),
        P("dp"),
        P("dp", "tensor"),
        P("dp", "tensor"),
        P("tensor", "dp"),
    )
    chips = Chips(mesh.shape["dp"])
    size = mesh.shape["tensor"]
    links = [[(i, i ^ 1 << b) for i in range(size)] for b in range(size.bit_length() - 1)]
    group = Group(links, "tensor")

    def run(*arrays):
        return local(chips, group, *arrays)

    return jax.shard_map(run, mesh=mesh, in_specs=in_specs, out_specs=out_specs, check_vma=False)
```

```python
import functools

import jax
import jax.numpy as jnp
import numpy as np
from jax import lax
from jax.experimental import pallas as pl
from jax.experimental.pallas import tpu as pltpu
from jax.sharding import PartitionSpec as P

HEAD_DIM = 64
SEQ = 512
EPS = 1e-05
THETA = 130000.0
BF16 = jnp.bfloat16
F32 = jnp.float32
FACTOR = HEAD_DIM**-0.5
PAIR = 2 * HEAD_DIM
HALF_SEQ = SEQ // 2
VMEM_LIMIT = 58 << 20
COST_SHARE = 4096


class Chain:
    def __init__(self):
        self.token = jnp.zeros((8, 128), F32)
        self.swaps, self.asked = [], []

    def join(self, *values):
        *values, self.token = lax.optimization_barrier((*values, self.token))
        return values

    def gate(self, *values):
        swaps, self.swaps = self.swaps, []
        asked, self.asked = self.asked, []
        joined = self.join(
            *values, *[held[i] for held, i in swaps], *[source for source, _, _, _ in asked]
        )
        for (held, i), value in zip(swaps, joined[len(values) :]):
            held[i] = value
        for (_, held, i, swap), value in zip(asked, joined[len(values) + len(swaps) :]):
            held[i] = swap(value)
            self.swaps.append((held, i))
        return joined[: len(values)]

    def end(self, *transfers):
        counts = [len(t.flying) for t in transfers]
        got = self.gate(*[value for t in transfers for value in t.flying])
        for t, count in zip(transfers, counts):
            if count:
                t.go_on(got[:count])
            got = got[count:]

    def ask(self, source, held, i, swap):
        self.asked.append((source, held, i, swap))

    def flush(self):
        for source, held, i, swap in self.asked:
            held[i] = swap(source)
        self.asked = []

    def call(self, body, grid, ins, outs, shapes, flops, scratch=(), prefetch=0, moved=0):
        first = prefetch + len(ins)
        second = first + 1 + len(outs)
        anywhere = pl.BlockSpec(memory_space=pl.ANY)

        def wrapped(*refs):
            body(*refs[:first], *refs[first + 1 : second], *refs[second + 1 :])

        run = pl.pallas_call(
            wrapped,
            grid_spec=pltpu.PrefetchScalarGridSpec(
                num_scalar_prefetch=prefetch,
                grid=grid,
                in_specs=[*ins, anywhere],
                out_specs=[*outs, anywhere],
                scratch_shapes=list(scratch),
            ),
            out_shape=[jax.ShapeDtypeStruct(s, t) for s, t in [*shapes, ((8, 128), F32)]],
            compiler_params=pltpu.CompilerParams(
                vmem_limit_bytes=VMEM_LIMIT, dimension_semantics=("arbitrary",) * len(grid)
            ),
            cost_estimate=pl.CostEstimate(
                flops=flops // COST_SHARE, bytes_accessed=moved // COST_SHARE, transcendentals=0
            ),
        )

        def with_token(*args):
            *results, self.token = run(*args, self.token)
            return results

        return with_token


class Chips:
    def __init__(self, size):
        self.bits = (size // 2).bit_length() - 1
        self.size = size
        self.swap = [(i, i ^ 1) for i in range(size)]
        self.links = [
            [(i, i ^ 2 << self.bits - 1 - p) for i in range(size)] for p in range(self.bits)
        ]
        flips = [
            sum(1 << self.bits - 1 - p for p in range(self.bits) if v >> p & 1)
            for v in range(1 << self.bits)
        ]
        table = [[i ^ 2 * f for f in flips] + [i ^ 2 * f ^ 1 for f in flips] for i in range(size)]
        self.table = np.array(table, np.int32)

    def send(self, value, p):
        return lax.ppermute(value, "dp", self.links[p])

    def other(self, value):
        return lax.ppermute(value, "dp", self.swap)


class Gather:
    def __init__(self, chips, chain, piece):
        self.chips, self.chain = chips, chain
        self.own = [piece] + [None] * (2**chips.bits - 1)
        self.others = list(self.own)
        self.ask(0)
        self.keys = [1 << p for p in range(chips.bits)]
        self.flying = [chips.send(piece, p) for p in range(chips.bits)]

    def ask(self, v):
        self.chain.ask(self.own[v], self.others, v, self.chips.other)

    def go_on(self, got):
        keys, self.keys, self.flying = self.keys, [], []
        for v, piece in zip(keys, got):
            self.own[v] = piece
            for p in range(v.bit_length(), self.chips.bits):
                self.keys.append(v | 1 << p)
                self.flying.append(self.chips.send(piece, p))
        for v in keys:
            self.ask(v)

    def pieces(self):
        while self.flying:
            self.chain.end(self)
        self.chain.flush()
        return self.own + self.others


class Sums:
    def __init__(self, chips, chain, mine, apart=False, hold=False, cut_in_two=False):
        self.chips, self.chain, self.apart, self.hold = chips, chain, apart, hold
        self.todo = []
        self.cut_in_two = cut_in_two and chips.bits == 2
        self.parts = [mine[0]]
        mine = list(mine[1:])
        self.direct, self.passed = [], []
        for p in range(chips.bits):
            self.direct.append(mine.pop(0))
            self.passed.append(mine.pop(0) if p else None)
        self.p = chips.bits - 1
        if self.cut_in_two:
            self.kinds = [0, 1]
            self.flying = [chips.send(half, 1) for half in self.in_two(self.passed[1])]
            return
        self.kinds = [self.p]
        self.flying = [chips.send(self.passed[self.p], self.p)]

    def in_two(self, values):
        width = values.shape[1] // 2
        return values[:, :width], values[:, width:]

    def go_on(self, got):
        rows = self.parts[0].shape[0]
        kinds, self.kinds, self.flying = self.kinds, [], []
        if self.p == 0:
            self.parts += got
            return
        if self.cut_in_two:
            self.p = 0
            total = self.direct[0].astype(F32) + jnp.concatenate(got, axis=1).astype(F32)
            self.todo = [(None, self.direct[1], 1), (None, total.astype(BF16), 0)]
            self.resume()
            return
        for kind, block in zip(kinds, got):
            if kind is None:
                self.parts.append(block)
                continue
            add = lambda held, first: (
                held.astype(F32) + block[first * rows : first * rows + held.shape[0]].astype(F32)
            ).astype(BF16)
            for q in range(kind):
                self.direct[q] = add(self.direct[q], (1 << q) - 1)
                if q:
                    self.passed[q] = add(self.passed[q], 1 << q)
        p, self.p = self.p, self.p - 1
        if p > 0:
            self.todo.append((None, self.direct[p], p))
        if p > 1:
            self.todo.append((p - 1, self.passed[p - 1], p - 1))
        if p == 1 and not self.apart:
            self.todo.append((None, self.direct[0], 0))
        if not self.hold:
            self.resume()

    def resume(self):
        todo, self.todo = self.todo, []
        values = self.chain.join(*[value for _, value, _ in todo])
        for (kind, _, p), value in zip(todo, values):
            self.kinds.append(kind)
            self.flying.append(self.chips.send(value, p))

    def send_half(self, i):
        while self.p > 0:
            self.chain.end(self)
        width = self.direct[0].shape[1] // 2
        (value,) = self.chain.join(self.direct[0][:, i * width : (i + 1) * width])
        self.kinds.append(None)
        self.flying.append(self.chips.send(value, 0))

    def terms(self):
        while self.flying or self.todo:
            if self.todo:
                self.resume()
            self.chain.end(self)
        return sorted(self.parts, key=lambda part: -part.shape[1])


class Group:
    def __init__(self, links, axes):
        self.links, self.axes = links, axes
        self.bits = len(links)
        self.size = 1 << self.bits
        self.orders = (list(range(self.bits)), list(range(self.bits))[::-1])

    def send(self, value, bit):
        return lax.ppermute(value, self.axes, self.links[bit])

    def messages(self):
        found = []
        for order in self.orders:
            found.append([])
            for top in reversed(range(self.bits)):
                found[-1].append(
                    [
                        1 << order[top] | sum(1 << order[p] for p in range(top) if v >> p & 1)
                        for v in range(1 << top)
                    ]
                )
        return found


class Spread:
    def __init__(self, group, chain, rows):
        self.group, self.chain = group, chain
        self.held = {0: [rows]}
        self.later = None
        self.keys = [(1 << b, None) for b in range(group.bits)]
        self.flying = [group.send(rows, b) for b in range(group.bits)]

    def go_on(self, got):
        fresh = list(zip(self.keys, got))
        self.keys, self.flying = [], []
        for (k, h), block in fresh:
            if h is None:
                self.held[k] = [block]
            else:
                self.held.setdefault(k, [None, None])[h] = block
        for (k, h), block in fresh:
            for way, order in enumerate(self.group.orders):
                if h is not None and h != way:
                    continue
                half = block.shape[1] // 2
                top = max(i for i, bit in enumerate(order) if k >> bit & 1)
                for i in range(top + 1, len(order)):
                    part = block if h is not None else block[:, way * half : (way + 1) * half]
                    self.keys.append((k | 1 << order[i], way))
                    if self.later is not None:
                        self.later.append((part, order[i]))
                    else:
                        self.flying.append(self.group.send(part, order[i]))

        if self.later:
            parts = self.chain.join(*[part for part, _ in self.later])
            self.later = [(part, bit) for part, (_, bit) in zip(parts, self.later)]

    def resume(self):
        later, self.later = self.later, None
        parts = self.chain.join(*[part for part, _ in later])
        self.flying = [self.group.send(part, bit) for part, (_, bit) in zip(parts, later)]

    def blocks(self):
        while self.flying:
            self.chain.end(self)
        return [self.held[k] for k in range(self.group.size)]


class Fold:
    def __init__(self, group, chain, own, sent):
        self.group, self.chain = group, chain
        self.rows = own[0].shape[0]
        self.sent = [list(half) for half in sent]
        self.parts = [[half] for half in own]
        self.wave = 0
        self.start()

    def start(self):
        self.flying = [
            self.group.send(self.sent[h][self.wave], order[self.group.bits - 1 - self.wave])
            for h, order in enumerate(self.group.orders)
        ]

    def go_on(self, got):
        self.wave += 1
        self.flying = []
        for h, block in enumerate(got):
            self.parts[h].append(block)
        for wave in range(self.wave, self.group.bits):
            sums = add_rows(self.chain, [sent[wave] for sent in self.sent], got)
            for sent, value in zip(self.sent, sums):
                sent[wave] = value
        if self.wave < self.group.bits:
            self.start()

    def total(self):
        while self.flying:
            self.chain.end(self)
        return self.parts


class Weight:
    def __init__(self, pieces, rows, start, width):
        self.pieces, self.rows, self.start, self.width = pieces, rows, start, width
        self.model = len(pieces) * rows

    def tiles(self, tile):
        first = self.start // tile
        return [pl.BlockSpec((self.rows, tile), lambda j: (0, first + j))] * len(self.pieces)


def nn(left, right):
    return lax.dot_general(left, right, (((1,), (0,)), ((), ())), preferred_element_type=F32)


def nt(left, right):
    return lax.dot_general(left, right, (((1,), (1,)), ((), ())), preferred_element_type=F32)


def tn(left, right):
    return lax.dot_general(left, right, (((0,), (0,)), ((), ())), preferred_element_type=F32)


def whole(shape):
    return pl.BlockSpec(shape, lambda *_: (0,) * len(shape))


def place(line_ref, j, width):
    return pl.ds(pl.multiple_of(line_ref[j] * width, 128), width)


def cut(width, j):
    return slice(j * width, (j + 1) * width)


def scale_of(values):
    return lax.rsqrt(jnp.mean(values * values, axis=-1, keepdims=True) + EPS)


def fetch_blocks(counts, refs, held, sems, k, slot, wait):
    first = 0
    for i, count in enumerate(counts):
        copies = []
        half = held.shape[2] // count
        for h in range(count):
            target = held.at[slot, :, pl.ds(h * half, half)]
            copies.append(pltpu.make_async_copy(refs[first + h], target, sems.at[slot, h]))
        first += count

        @pl.when(k == i)
        def _():
            for copy in copies:
                copy.wait() if wait else copy.start()


def fetched(counts, refs, held, sems):
    k = pl.program_id(0)

    @pl.when(k == 0)
    def _():
        fetch_blocks(counts, refs, held, sems, k, 0, False)

    fetch_blocks(counts, refs, held, sems, k + 1, (k + 1) % 2, False)
    fetch_blocks(counts, refs, held, sems, k, k % 2, True)
    return held.at[k % 2]


def norm_body(blocks, counts, line_ref, gain_ref, *refs):
    out_ref, held, sems = refs[sum(counts) :]
    x_ref = fetched(counts, refs, held, sems)
    width = out_ref.shape[1] // blocks
    scale = scale_of(x_ref[...].astype(F32))
    for j in range(blocks):
        part = x_ref[:, place(line_ref, j, width)].astype(F32)
        gain = gain_ref[0:1, cut(width, j)]
        out_ref[:, cut(width, j)] = (part * scale * gain).astype(BF16)


def order_body(blocks, counts, line_ref, gain_ref, *refs):
    out_ref, held, sems = refs[sum(counts) :]
    x_ref = fetched(counts, refs, held, sems)
    width = out_ref.shape[1] // blocks
    for j in range(blocks):
        out_ref[:, cut(width, j)] = x_ref[:, place(line_ref, j, width)]


def ordered(chain, body, line, gains, held):
    counts = [len(block) for block in held]
    rows, model = held[0][0].shape
    n = len(held)
    return chain.call(
        functools.partial(body, line.shape[0], counts),
        (n,),
        [whole(gains.shape)] + [pl.BlockSpec(memory_space=pl.ANY)] * sum(counts),
        [pl.BlockSpec((rows, model), lambda k, *_: (k, 0))],
        [((n * rows, model), BF16)],
        flops=20 * n * rows * model,
        scratch=[pltpu.VMEM((2, rows, model), BF16), pltpu.SemaphoreType.DMA((2, 2))],
        prefetch=1,
        moved=4 * n * rows * model,
    )(line, gains, *[array for block in held for array in block])[0]


def added(refs, span):
    total = refs[0][span, :].astype(F32)
    for ref in refs[1:]:
        total += ref[span, :].astype(F32)
    return total


def middle_body(blocks, m, line_ref, x_ref, gain_ref, *refs):
    middle_ref, out_ref = refs[2 * m :]
    width = x_ref.shape[1] // blocks
    half = x_ref.shape[1] // 2
    span = slice(None)
    middle_ref[:, :half] = added(refs[:m], span)
    middle_ref[:, half:] = added(refs[m : 2 * m], span)
    for j in range(blocks):
        here = x_ref[:, place(line_ref, j, width)].astype(F32)
        middle_ref[:, cut(width, j)] += here
    middle = middle_ref[...]
    out_ref[...] = (middle * scale_of(middle) * gain_ref[1:2, :]).astype(BF16)


def result_body(blocks, m, line_ref, middle_ref, gain_ref, *refs):
    out_ref = refs[2 * m]
    width = middle_ref.shape[1] // blocks
    span = slice(None)
    total = middle_ref[...] + jnp.concatenate(
        [added(refs[:m], span), added(refs[m : 2 * m], span)], axis=1
    )
    for j in range(blocks):
        out_ref[:, place(line_ref, j, width)] = total[:, cut(width, j)].astype(BF16)


def second_back_body(blocks, m, line_ref, dy_ref, gain_ref, *refs):
    middle_ref, out_ref, low_ref = refs[2 * m :]
    width = dy_ref.shape[1] // blocks
    span = slice(None)
    grad = jnp.concatenate([added(refs[:m], span), added(refs[m : 2 * m], span)], axis=1)
    middle = middle_ref[...]
    scale = scale_of(middle)
    normed = middle * scale
    scaled = grad * gain_ref[1:2, :]
    out_ref[...] = scale * (scaled - normed * jnp.mean(scaled * normed, axis=-1, keepdims=True))
    for j in range(blocks):
        out_ref[:, cut(width, j)] += dy_ref[:, place(line_ref, j, width)].astype(F32)
    low_ref[...] = out_ref[...].astype(BF16)


def first_back_body(blocks, m, line_ref, x_ref, gain_ref, *refs):
    above_ref, out_ref = refs[2 * m :]
    width = x_ref.shape[1] // blocks
    span = slice(None)
    scale = scale_of(x_ref[...].astype(F32))
    normed = jnp.concatenate(
        [x_ref[:, place(line_ref, j, width)].astype(F32) for j in range(blocks)], axis=1
    ) * scale
    grad = jnp.concatenate([added(refs[:m], span), added(refs[m : 2 * m], span)], axis=1)
    scaled = grad * gain_ref[0:1, :]
    back = scale * (scaled - normed * jnp.mean(scaled * normed, axis=-1, keepdims=True))
    total = above_ref[...] + back
    for j in range(blocks):
        out_ref[:, place(line_ref, j, width)] = total[:, cut(width, j)]


def by_rows(chain, body, line, first, gains, parts, more, kinds):
    rows, model = first.shape
    half = model // 2
    tile = min(128, rows)
    row = pl.BlockSpec((tile, model), lambda i, *_: (i, 0))
    slim = pl.BlockSpec((tile, half), lambda i, *_: (i, 0))
    m = len(parts[0])
    return chain.call(
        functools.partial(body, line.shape[0], m),
        (rows // tile,),
        [row, whole(gains.shape)] + [slim] * (2 * m) + [row] * len(more),
        [row] * len(kinds),
        [((rows, model), kind) for kind in kinds],
        flops=20 * rows * model,
        prefetch=1,
        moved=rows * model * (2 * m + 4 * len(kinds)),
    )(line, first, gains, *parts[0], *parts[1], *more)


def add_rows_body(count, *refs):
    for i in range(count):
        total = refs[i][...].astype(F32) + refs[count + i][...].astype(F32)
        refs[2 * count + i][...] = total.astype(BF16)


def add_rows(chain, helds, blocks):
    rows, columns = helds[0].shape
    tile = min(128, rows)
    steps = rows // tile
    count = len(helds)
    here = pl.BlockSpec((tile, columns), lambda i: (i, 0))
    return chain.call(
        functools.partial(add_rows_body, count),
        (steps,),
        [here] * count + [pl.BlockSpec((tile, columns), lambda i: (steps + i, 0))] * count,
        [here] * count,
        [((rows, columns), BF16)] * count,
        flops=count * rows * columns,
        moved=6 * count * rows * columns,
    )(*helds, *blocks)


def finish_body(m, halves, n, *refs):
    total = added(refs[:m], slice(None))
    if halves:
        total += jnp.concatenate([ref[...].astype(F32) for ref in refs[m : m + halves]], axis=1)
    m += halves
    weights, outs = refs[m : m + n], refs[m + n :]
    if not n:
        outs[0][...] = total.T
        return
    width = weights[0].shape[1]
    inner = jnp.zeros((total.shape[0], 1), F32)
    for i in range(n):
        part = total[:, cut(width, i)]
        outs[i][...] = part
        inner += jnp.sum(weights[i][...].astype(F32) * part, axis=1, keepdims=True)
    outs[n][...] = jnp.broadcast_to(inner, outs[n].shape)


def finish(chain, terms, weights=()):
    rows, columns = terms[0].shape
    tile = min(128, rows)
    row = pl.BlockSpec((tile, columns), lambda i: (i, 0))
    n = len(weights)
    halves = sum(1 for term in terms if term.shape[1] < columns)
    half = [pl.BlockSpec((tile, columns // 2), lambda i: (i, 0))] * halves
    if n:
        slim = pl.BlockSpec((tile, columns // n), lambda i: (i, 0))
        outs = [slim] * n + [pl.BlockSpec((tile, 128), lambda i: (i, 0))]
        shapes = [((rows, columns // n), F32)] * n + [((rows, 128), F32)]
    else:
        slim = None
        outs = [pl.BlockSpec((columns, tile), lambda i: (0, i))]
        shapes = [((columns, rows), F32)]
    results = chain.call(
        functools.partial(finish_body, len(terms) - halves, halves, n),
        (rows // tile,),
        [row] * (len(terms) - halves) + half + [slim] * n,
        outs,
        shapes,
        flops=4 * rows * columns,
        moved=rows * columns * 12,
    )(*terms, *weights)
    if n:
        results[n] = results[n][:, 0]
    return results


def rope_tables(place):
    half = HEAD_DIM // 2
    freq = THETA ** (-2.0 * jnp.arange(half, dtype=F32) / HEAD_DIM)
    angle = place.astype(F32)[:, None] * freq[None, :]
    cosine, sine = jnp.cos(angle), jnp.sin(angle)
    return (
        jnp.concatenate([cosine] * (PAIR // half), axis=1),
        jnp.concatenate([-sine, sine] * (PAIR // HEAD_DIM), axis=1),
    )


def turn(values):
    half = HEAD_DIM // 2
    width = values.shape[-1]
    lane = lax.broadcasted_iota(jnp.int32, values.shape, 1) % HEAD_DIM
    return jnp.where(
        lane < half, pltpu.roll(values, width - half, 1), pltpu.roll(values, half, 1)
    )


def joined(refs):
    return jnp.concatenate([r[...] for r in refs], axis=0)


def qkv_body(n, x_ref, cos_ref, sin_ref, *refs):
    weights, outs = refs[: 3 * n], refs[3 * n :]
    rows = x_ref.shape[0]
    tile = outs[0].shape[1]
    for i in range(3):
        weight = joined(weights[i * n : (i + 1) * n])
        for s in range(rows // SEQ):
            span = slice(s * SEQ, (s + 1) * SEQ)
            product = nn(x_ref[span, :], weight)
            if i == 2:
                outs[i][span, :] = product.astype(BF16)
                continue
            for t in range(tile // PAIR):
                here = product[:, t * PAIR : (t + 1) * PAIR]
                turned = here * cos_ref[...] + turn(here) * sin_ref[...]
                outs[i][span, t * PAIR : (t + 1) * PAIR] = turned.astype(BF16)


def project(chain, x, tables, query, key, value):
    rows, model = x.shape
    n, width = len(query.pieces), query.width
    tile = min(256, width)
    out = pl.BlockSpec((rows, tile), lambda j: (0, j))
    return chain.call(
        functools.partial(qkv_body, n),
        (width // tile,),
        [whole(x.shape), whole((SEQ, PAIR)), whole((SEQ, PAIR))]
        + query.tiles(tile)
        + key.tiles(tile)
        + value.tiles(tile),
        [out] * 3,
        [((rows, width), BF16)] * 3,
        flops=6 * rows * model * width,
        moved=2 * (rows * model + 3 * model * width + 3 * rows * width),
    )(x, *tables, *query.pieces, *key.pieces, *value.pieces)


def collect(counts, refs, held, sems):
    rows = held.shape[0] // len(counts)
    copies = []
    for k, count in enumerate(counts):
        half = held.shape[1] // count
        for h in range(count):
            target = held.at[pl.ds(k * rows, rows), pl.ds(h * half, half)]
            i = len(copies)
            copies.append(pltpu.make_async_copy(refs[i], target, sems.at[i]))
    for copy in copies:
        copy.start()
    for copy in copies:
        copy.wait()


def gate_body(n, counts, *refs):
    m = sum(counts)
    gate_w, up_w = refs[m : m + n], refs[m + n : m + 2 * n]
    left_ref, hidden_ref, slope_ref, silu_ref, theirs_ref, x_ref, turned, sems = refs[m + 2 * n :]

    @pl.when(pl.program_id(0) == 0)
    def _():
        collect(counts, refs, x_ref, sems)
        turned[...] = left_ref[...].T

    gate_weight, up_weight = joined(gate_w), joined(up_w)
    for s in range(x_ref.shape[0] // SEQ):
        span = slice(s * SEQ, (s + 1) * SEQ)
        gate = nn(x_ref[span, :], gate_weight)
        up = nn(x_ref[span, :], up_weight)
        sigm = jax.nn.sigmoid(gate)
        silu = gate * sigm
        hidden_ref[span, :] = (silu * up).astype(BF16)
        silu_ref[span, :] = silu.astype(BF16)
        slope_ref[span, :] = (up * sigm * (1.0 + gate * (1.0 - sigm))).astype(BF16)
    theirs_ref[...] = nn(turned[...], hidden_ref[...]).astype(BF16)


def collected(held):
    counts = [len(block) for block in held]
    rows, model = held[0][0].shape
    scratch = [
        pltpu.VMEM((len(held) * rows, model), BF16),
        pltpu.SemaphoreType.DMA((sum(counts),)),
    ]
    arrays = [array for block in held for array in block]
    return counts, arrays, [pl.BlockSpec(memory_space=pl.ANY)] * len(arrays), scratch


def gate_up(chain, held, gate, up, grads):
    counts, arrays, specs, scratch = collected(held)
    rows, model = scratch[0].shape
    n, width = len(gate.pieces), gate.width
    tile = min(256, width)
    out = pl.BlockSpec((rows, tile), lambda j: (0, j))
    half = model // 2
    return chain.call(
        functools.partial(gate_body, n, counts),
        (width // tile,),
        specs
        + gate.tiles(tile)
        + up.tiles(tile)
        + [pl.BlockSpec((rows, half), lambda j: (0, 1))],
        [out] * 3 + [pl.BlockSpec((half, tile), lambda j: (0, j))],
        [((rows, width), BF16)] * 3 + [((half, width), BF16)],
        flops=6 * rows * model * width,
        scratch=[scratch[0], pltpu.VMEM((half, rows), BF16), scratch[1]],
        moved=2 * (rows * model + 2 * model * width + 3 * rows * width),
    )(*arrays, *gate.pieces, *up.pieces, grads)


def half_blocks(left, which):
    lefts = [block[0] if len(block) == 1 else block[which] for block in left]
    rows, half = lefts[0].shape[0], left[0][0].shape[1] // 2
    places = [which if len(block) == 1 else 0 for block in left]
    return lefts, [
        pl.BlockSpec((rows, half), functools.partial(lambda at, j: (0, at), at)) for at in places
    ]


def hidden_back_body(n, blocks, g_ref, *refs):
    weights, slope_ref, silu_ref = refs[:n], refs[n], refs[n + 1]
    lefts, refs = refs[n + 2 : n + 2 + blocks], refs[n + 2 + blocks :]
    gate_ref, up_ref, theirs_ref, turned = refs
    rows = turned.shape[1] // blocks

    @pl.when(pl.program_id(0) == 0)
    def _():
        for k in range(blocks):
            turned[:, cut(rows, k)] = lefts[k][...].T

    weight = joined(weights)
    for s in range(g_ref.shape[0] // SEQ):
        span = slice(s * SEQ, (s + 1) * SEQ)
        grad = nn(g_ref[span, :], weight)
        gate_ref[span, :] = (grad * slope_ref[span, :].astype(F32)).astype(BF16)
        up_ref[span, :] = (grad * silu_ref[span, :].astype(F32)).astype(BF16)
    theirs_ref[...] = nn(turned[...], gate_ref[...]).astype(BF16)


def hidden_back(chain, grads, down, slope, silu, left):
    rows, model = grads.shape
    n, width = len(down.pieces), down.width
    tile = min(256, width)
    out = pl.BlockSpec((rows, tile), lambda j: (0, j))
    lefts, specs = half_blocks(left, 1)
    half = model // 2
    return chain.call(
        functools.partial(hidden_back_body, n, len(lefts)),
        (width // tile,),
        [whole(grads.shape)] + down.tiles(tile) + [out] * 2 + specs,
        [out] * 2 + [pl.BlockSpec((half, tile), lambda j: (0, j))],
        [((rows, width), BF16)] * 2 + [((half, width), BF16)],
        flops=3 * rows * model * width,
        scratch=[pltpu.VMEM((half, rows), BF16)],
        moved=2 * (rows * model + model * width + 4 * rows * width),
    )(grads, *down.pieces, slope, silu, *lefts)


def mixed_back_body(n, counts, *refs):
    m = sum(counts)
    out_ref, x_ref, sems = refs[m + n :]

    @pl.when(pl.program_id(0) == 0)
    def _():
        collect(counts, refs, x_ref, sems)

    out_ref[...] = nn(x_ref[...], joined(refs[m : m + n])).astype(BF16)


def mixed_back(chain, held, out):
    counts, arrays, specs, scratch = collected(held)
    rows, model = scratch[0].shape
    n, width = len(out.pieces), out.width
    tile = min(256, width)
    return chain.call(
        functools.partial(mixed_back_body, n, counts),
        (width // tile,),
        specs + out.tiles(tile),
        [pl.BlockSpec((rows, tile), lambda j: (0, j))],
        [((rows, width), BF16)],
        flops=2 * rows * model * width,
        scratch=scratch,
        moved=2 * (rows * model + model * width + rows * width),
    )(*arrays, *out.pieces)[0]


def trans_body(n, starts, targets, *refs):
    parts, blocks = len(starts), len(targets[0])
    lefts = refs[:parts]
    pieces = refs[parts : parts * (n + 1)]
    outs = refs[parts * (n + 1) : -4]
    held, ready, sems, out_sems = refs[-4:]
    j = pl.program_id(0)
    depth, width = held.shape[2:]
    rows = ready.shape[1] // blocks

    def copy(i, p, slot):
        source = pieces[p * n + i].at[pl.ds(0, depth), pl.ds(starts[p], width)]
        return pltpu.make_async_copy(source, held.at[slot, p], sems.at[slot, p])

    def fetch(step, slot):
        for i in range(n):

            @pl.when(step == i)
            def _():
                for p in range(parts):
                    copy(i, p, slot).start()

    def leave(slot, k, array, first, column):
        target = outs[array].at[pl.ds(first, rows), pl.ds(column, depth)]
        source = ready.at[slot, pl.ds(k * rows, rows), :]
        return pltpu.make_async_copy(source, target, out_sems.at[slot, k])

    def left(slot):
        for k in range(blocks):
            leave(slot, k, 0, 0, 0).wait()

    @pl.when(j == 0)
    def _():
        fetch(j, 0)

    @pl.when(j + 1 < n)
    def _():
        fetch(j + 1, (j + 1) % 2)

    slot = j % 2
    for p in range(parts):
        copy(0, p, slot).wait()

    @pl.when(j >= 2)
    def _():
        left(slot)

    for s in range(blocks * rows // SEQ):
        span = slice(s * SEQ, (s + 1) * SEQ)
        total = nt(lefts[0][span, :], held[slot, 0])
        for p in range(1, parts):
            total += nt(lefts[p][span, :], held[slot, p])
        ready[slot, span, :] = total.astype(BF16)
    column = pl.multiple_of(j % (n // 2) * depth, 128)
    for h in range(2):

        @pl.when((j >= n // 2) == (h == 1))
        def _():
            for k, (array, first) in enumerate(targets[h]):
                leave(slot, k, array, first, column).start()

    @pl.when(j == n - 1)
    def _():
        left(1 - slot)
        left(slot)


def times_trans(chain, parts, group):
    weights = [weight for _, weight in parts]
    n, depth, width = len(weights[0].pieces), weights[0].rows, weights[0].width
    rows = parts[0][0].shape[0]
    half = weights[0].model // 2
    size = rows // group.size
    messages = group.messages()
    shapes = [((size, half), BF16)] * 2
    targets = [{0: (0, 0)}, {0: (1, 0)}]
    for h in range(2):
        for keys in messages[h]:
            for i, k in enumerate(keys):
                targets[h][k] = (len(shapes), i * size)
            shapes.append(((len(keys) * size, half), BF16))
    targets = [[t[k] for k in range(group.size)] for t in targets]
    anywhere = pl.BlockSpec(memory_space=pl.ANY)
    outs = chain.call(
        functools.partial(trans_body, n, [weight.start for weight in weights], targets),
        (n,),
        [whole((rows, width))] * len(parts) + [anywhere] * (n * len(parts)),
        [anywhere] * len(shapes),
        shapes,
        flops=4 * rows * half * width * len(parts),
        scratch=[
            pltpu.VMEM((2, len(parts), depth, width), BF16),
            pltpu.VMEM((2, rows, depth), BF16),
            pltpu.SemaphoreType.DMA((2, len(parts))),
            pltpu.SemaphoreType.DMA((2, group.size)),
        ],
        moved=2 * (2 * rows * half + len(parts) * (rows + 2 * half) * width),
    )(*[left for left, _ in parts], *[piece for weight in weights for piece in weight.pieces])
    m = group.bits
    return outs[:2], [outs[2 : 2 + m], outs[2 + m :]]


def grad_body(parts, got, blocks, steps, *refs):
    lefts, refs = refs[:blocks], refs[blocks:]
    rights, refs = refs[:parts], refs[parts:]
    got_ref = refs[0] if got else None
    outs, turned = refs[got:-1], refs[-1]
    j = pl.program_id(0)

    @pl.when(j == 0)
    def _():
        rows = turned.shape[1] // blocks
        for k in range(blocks):
            turned[:, cut(rows, k)] = lefts[k][...].T

    for i in range(parts):

        @pl.when((j >= i * steps) & (j < (i + 1) * steps))
        def _():
            total = nn(turned[...], rights[i][...])
            if got:
                total += got_ref[...].astype(F32)
            total = total.astype(BF16)
            first = 0
            for out_ref in outs:
                count = out_ref.shape[0]
                out_ref[...] = total[first : first + count]
                first += count


def weight_grads(chain, left, which, rights, got=None, bits=0):
    rows, width = rights[0].shape
    parts = len(rights)
    tile = min(512, width)
    steps = width // tile
    lefts, ins = half_blocks(left if isinstance(left, list) else [[left]], which)
    blocks, half = len(lefts), ins[0].block_shape[1]
    for i in range(parts):
        ins.append(
            pl.BlockSpec(
                (rows, tile),
                functools.partial(
                    lambda first, j: (0, jnp.clip(j - first, 0, steps - 1)), i * steps
                ),
            )
        )
    column = lambda j: (0, j)
    more = [] if got is None else [got]
    sizes = [half >> bits]
    for p in range(bits):
        sizes += [sizes[0], ((1 << p) - 1) * sizes[0]] if p else [sizes[0]]
    return chain.call(
        functools.partial(grad_body, parts, len(more), blocks, steps),
        (parts * steps,),
        ins + [pl.BlockSpec((half, tile), column)] * len(more),
        [pl.BlockSpec((size, tile), column) for size in sizes],
        [((size, parts * width), BF16) for size in sizes],
        flops=2 * rows * half * width * parts,
        scratch=[pltpu.VMEM((half, rows), BF16)],
        moved=2 * (rows * half + parts * (rows + half) * width),
    )(*lefts, *rights, *more)


def causal(scores):
    past = scores.shape[0] - HALF_SEQ
    key = lax.broadcasted_iota(jnp.int32, (HALF_SEQ, HALF_SEQ), 0)
    query = lax.broadcasted_iota(jnp.int32, (HALF_SEQ, HALF_SEQ), 1)
    last = jnp.where(key <= query, scores[past:], -1e30)
    return last if past == 0 else jnp.concatenate([scores[:past], last], axis=0)


def head_of(h):
    return slice(h * HEAD_DIM, (h + 1) * HEAD_DIM)


def span_of(b):
    return slice(b * HALF_SEQ, (b + 1) * HALF_SEQ)


def in_place(shift_ref, ref, count):
    rows = SEQ // count
    spans = [pl.ds(pl.multiple_of((i ^ shift_ref[0]) * rows, rows), rows) for i in range(count)]
    return jnp.concatenate([ref[span, :] for span in spans], axis=0)


def put_back(shift_ref, ref, count, values):
    rows = SEQ // count
    for i in range(count):
        ref[pl.ds(pl.multiple_of((i ^ shift_ref[0]) * rows, rows), rows), :] = values[cut(rows, i)]


def one_head(values, h):
    lane = lax.broadcasted_iota(jnp.int32, values.shape, 1)
    return jnp.where(lane // HEAD_DIM == h, values, jnp.zeros_like(values))


def attend_body(count, shift_ref, q_ref, k_ref, v_ref, out_ref, sum_ref):
    queries, keys = in_place(shift_ref, q_ref, count), in_place(shift_ref, k_ref, count)
    values = in_place(shift_ref, v_ref, count).astype(F32).T.astype(BF16)
    heads = []
    for h in range(q_ref.shape[1] // HEAD_DIM):
        blocks = []
        for b in range(2):
            reach = (b + 1) * HALF_SEQ
            query = one_head(queries[span_of(b)] * BF16(FACTOR), h)
            scores = causal(nt(keys[:reach], query))
            top = jnp.max(scores, axis=0, keepdims=True)
            expo = jnp.exp(scores - top)
            total = jnp.sum(expo, axis=0, keepdims=True)
            mixed = nn(values[head_of(h), :reach], expo.astype(BF16))
            blocks.append(mixed * (1.0 / total))
            sum_ref[0, h, :, span_of(b)] = top + jnp.log(total)
        heads.append(jnp.concatenate(blocks, axis=1))
    put_back(shift_ref, out_ref, count, jnp.concatenate(heads, axis=0).T.astype(BF16))


def attention_specs(rows, width, wide):
    wide = min(wide, width)
    tile = pl.BlockSpec((SEQ, wide), lambda s, p, _: (s, p))
    sums = pl.BlockSpec((1, wide // HEAD_DIM, 1, SEQ), lambda s, p, _: (s, p, 0, 0))
    return (rows // SEQ, width // wide), tile, sums


def attend(chain, shift, count, query, key, value):
    rows, width = query.shape
    grid, tile, sums = attention_specs(rows, width, 256)
    return chain.call(
        functools.partial(attend_body, count),
        grid,
        [tile] * 3,
        [tile, sums],
        [((rows, width), BF16), ((rows // SEQ, width // HEAD_DIM, 1, SEQ), F32)],
        flops=16 * rows * width * SEQ,
        prefetch=1,
        moved=8 * rows * width,
    )(shift, query, key, value)


def attend_back_body(
    count, shift_ref, q_ref, k_ref, v_ref, g_ref, sum_ref, cos_ref, sin_ref, dq_ref, dk_ref, dv_ref
):
    queries, keys, values, grads = (
        in_place(shift_ref, ref, count) for ref in (q_ref, k_ref, v_ref, g_ref)
    )
    turned = keys.astype(F32).T.astype(BF16)
    dq_heads = []
    dk, dv = [], []
    for b in range(2):
        reach = (b + 1) * HALF_SEQ
        dq, dk_sum, dv_sum = [], None, None
        for h in range(q_ref.shape[1] // HEAD_DIM):
            query = one_head(queries[span_of(b)], h)
            grad = one_head(grads[span_of(b)], h)
            scores = causal(nt(keys[:reach], query * BF16(FACTOR)))
            probs = jnp.exp(scores - sum_ref[0, h, :, span_of(b)])
            probs_grad = nt(values[:reach], grad)
            inner = jnp.sum(probs * probs_grad, axis=0, keepdims=True)
            score_grad = (probs * (probs_grad - inner)).astype(BF16)
            dv_part, dk_part = nn(probs.astype(BF16), grad), nn(score_grad, query)
            dv_sum = dv_part if dv_sum is None else dv_sum + dv_part
            dk_sum = dk_part if dk_sum is None else dk_sum + dk_part
            dq.append(nn(turned[head_of(h), :reach], score_grad))
        dq_heads.append(jnp.concatenate(dq, axis=0))
        dk.append(dk_sum)
        dv.append(dv_sum)

    def whole_rows(parts):
        early, late = parts
        return jnp.concatenate([late[:HALF_SEQ] + early, late[HALF_SEQ:]], axis=0)

    dq = jnp.concatenate(dq_heads, axis=1).T * FACTOR
    dk = whole_rows(dk) * FACTOR
    dv = whole_rows(dv).astype(BF16)
    copies = dq.shape[1] // PAIR
    cosine = jnp.concatenate([cos_ref[...]] * copies, axis=1)
    sine = jnp.concatenate([sin_ref[...]] * copies, axis=1)
    put_back(shift_ref, dq_ref, count, (dq * cosine - turn(dq) * sine).astype(BF16))
    put_back(shift_ref, dk_ref, count, (dk * cosine - turn(dk) * sine).astype(BF16))
    put_back(shift_ref, dv_ref, count, dv)


def attend_back(chain, shift, count, query, key, value, grad, logsum, tables):
    rows, width = query.shape
    grid, tile, sums = attention_specs(rows, width, PAIR)
    return chain.call(
        functools.partial(attend_back_body, count),
        grid,
        [tile] * 4 + [sums] + [whole((SEQ, PAIR))] * 2,
        [tile] * 3,
        [((rows, width), BF16)] * 3,
        flops=40 * rows * width * SEQ,
        prefetch=1,
        moved=14 * rows * width,
    )(shift, query, key, value, grad, logsum, *tables)


def local(
    chips,
    group,
    tokens,
    attn_gain,
    query_weight,
    key_weight,
    value_weight,
    output_weight,
    ffn_gain,
    gate_weight,
    up_weight,
    down_weight,
    cotangent,
):
    line = jnp.asarray(chips.table)[lax.axis_index("dp")]
    rows, model = tokens.shape
    count = SEQ // rows
    shift = lax.axis_index("tensor") % count
    row = jnp.arange(SEQ, dtype=jnp.int32)
    places = rope_tables(row)
    tables = rope_tables((row // rows ^ shift) * rows + row % rows)
    shift = jnp.reshape(shift, (1,)).astype(jnp.int32)
    early = (*places, *tables, line, shift)
    depth, own = query_weight.shape
    hidden_units = gate_weight.shape[1]
    chain = Chain()

    def gather(piece):
        return Gather(chips, chain, chain.join(piece)[0])

    def spread_of(values):
        return Spread(group, chain, chain.join(values)[0])

    def fold_of(part):
        own_part, sent = part
        sent = chain.join(*sent[0], *sent[1])
        return Fold(group, chain, own_part, [sent[: group.bits], sent[group.bits :]])

    def grads_of(left, rights, theirs=None):
        if theirs is None:
            (theirs,) = weight_grads(chain, left, 1, rights)
        got = [None]
        chain.ask(theirs, got, 0, chips.other)

        def mine(**how):
            if got[0] is None:
                chain.flush()
            blocks = weight_grads(chain, left, 0, rights, got[0], chips.bits)
            return Sums(chips, chain, blocks, **how)

        return mine

    extra = jnp.concatenate([attn_gain, ffn_gain, jnp.zeros((4 * own - 2 * depth,), BF16)])
    attn = jnp.concatenate([query_weight, key_weight, value_weight, output_weight.T], axis=1)
    attn = gather(jnp.concatenate([attn, jnp.broadcast_to(extra, (16, 4 * own))], axis=0))
    spread = spread_of(tokens)
    grads_spread = spread_of(cotangent)
    grads_spread.later = []
    down_turned, *early = chain.join(down_weight.T, *early)
    places, tables, line, shift = early[:2], early[2:4], early[4], early[5]
    chain.end(attn, spread, grads_spread)
    chain.end(attn, spread)
    all_tokens = spread.blocks()
    attn = attn.pieces()
    pair = gather(jnp.concatenate([gate_weight, up_weight], axis=1))
    w_query, w_key, w_value, w_output = [Weight(attn, depth, i * own, own) for i in range(4)]
    gains = jnp.concatenate(
        [piece[depth : depth + 1, : 2 * depth].reshape(2, depth) for piece in attn], axis=1
    ).astype(F32)

    group_one = ordered(chain, norm_body, line, gains, all_tokens)
    grads_spread.resume()
    query, key, value = project(chain, group_one, tables, w_query, w_key, w_value)
    mixed, logsum = attend(chain, shift, count, query, key, value)
    out_part = times_trans(chain, [(mixed, w_output)], group)
    fold = fold_of(out_part)
    chain.end(fold, pair, grads_spread)
    grad_rows = ordered(chain, order_body, line, gains, grads_spread.blocks())
    chain.end(fold)
    attended = fold.total()
    middle, second = by_rows(
        chain, middle_body, line, tokens, gains, attended, [], [F32, BF16]
    )
    spread = spread_of(second)
    chain.end(spread, pair)
    pair = pair.pieces()
    down = gather(down_turned)
    chain.end(spread)
    group_two = spread.blocks()
    w_gate = Weight(pair, depth, 0, hidden_units)
    w_up = Weight(pair, depth, hidden_units, hidden_units)
    hidden, slope, silu, theirs = gate_up(chain, group_two, w_gate, w_up, grad_rows)

    mine = grads_of(grad_rows, [hidden], theirs)
    chain.end(down)
    chain.flush()
    down_sum = mine()
    w_down = Weight(down.pieces(), depth, 0, hidden_units)
    gate_grad, up_grad, gate_theirs = hidden_back(
        chain, grad_rows, w_down, slope, silu, group_two
    )
    mine_gate = grads_of(group_two, [gate_grad], gate_theirs)
    chain.end(down_sum)
    second_part = times_trans(chain, [(gate_grad, w_gate), (up_grad, w_up)], group)
    fold = fold_of(second_part)
    gate_sum = mine_gate(hold=True)
    (up_theirs,) = weight_grads(chain, group_two, 1, [up_grad])
    chain.end(down_sum)
    (down_sum,) = finish(chain, down_sum.terms())
    mine_up = grads_of(group_two, [up_grad], up_theirs)
    chain.end(fold)
    up_sum = mine_up(hold=True)
    chain.end(fold)
    second_grad = fold.total()
    middle_grad, low_grad = by_rows(
        chain, second_back_body, line, cotangent, gains, second_grad, [middle], [F32, BF16]
    )
    spread = spread_of(low_grad)
    chain.end(gate_sum)
    gate_sum.resume()
    result_part = times_trans(chain, [(hidden, w_down)], group)
    chain.end(spread)
    chain.end(spread)
    attn_grads = spread.blocks()

    mixed_grad = mixed_back(chain, attn_grads, w_output)
    query_back, key_back, value_back = attend_back(
        chain, shift, count, query, key, value, mixed_grad, logsum, places
    )
    mine_qkv = grads_of(group_one, [query_back, key_back, value_back])
    mine_out = grads_of(attn_grads, [mixed])
    chain.end(gate_sum, up_sum)
    up_sum.resume()
    fold = fold_of(result_part)
    qkv_sum = mine_qkv()
    first_part = times_trans(
        chain, [(query_back, w_query), (key_back, w_key), (value_back, w_value)], group
    )
    out_sum = mine_out(hold=True)
    chain.end(fold)
    gate_sum, gate_inner = finish(chain, gate_sum.terms(), [gate_weight])
    chain.end(fold)
    result_part = fold.total()
    (layer_out,) = by_rows(chain, result_body, line, middle, gains, result_part, [], [BF16])
    fold = fold_of(first_part)
    chain.end(up_sum, out_sum)
    chain.end(qkv_sum)
    out_sum.resume()
    up_sum, up_inner = finish(chain, up_sum.terms(), [up_weight])
    chain.end(fold)
    chain.end(fold)
    first_grad = fold.total()
    (input_grad,) = by_rows(
        chain, first_back_body, line, tokens, gains, first_grad, [middle_grad], [F32]
    )
    chain.end(qkv_sum)
    query_sum, key_sum, value_sum, qkv_inner = finish(
        chain, qkv_sum.terms(), [query_weight, key_weight, value_weight]
    )
    gain_parts = jnp.stack(
        [qkv_inner / attn_gain.astype(F32), (gate_inner + up_inner) / ffn_gain.astype(F32)]
    )
    (gain_parts,) = chain.join(gain_parts)
    (out_sum,) = finish(chain, out_sum.terms())
    gain_totals = gain_parts
    for k in range(1, group.size):
        pairs = [(i, i ^ k) for i in range(group.size)]
        gain_totals += lax.ppermute(gain_parts, "tensor", pairs)
    gain_one_total, gain_two_total = gain_totals[0], gain_totals[1]
    return (
        layer_out,
        input_grad,
        gain_one_total,
        query_sum,
        key_sum,
        value_sum,
        out_sum,
        gain_two_total,
        gate_sum,
        up_sum,
        down_sum,
    )


def solution(mesh):
    in_specs = (
        P(("dp", "tensor"), None),
        P("dp"),
        P("dp", "tensor"),
        P("dp", "tensor"),
        P("dp", "tensor"),
        P("tensor", "dp"),
        P("dp"),
        P("dp", "tensor"),
        P("dp", "tensor"),
        P("tensor", "dp"),
        P(("dp", "tensor"), None),
    )
    out_specs = (
        P(("dp", "tensor"), None),
        P(("dp", "tensor"), None),
        P("dp"),
        P("dp", "tensor"),
        P("dp", "tensor"),
        P("dp", "tensor"),
        P("tensor", "dp"),
        P("dp"),
        P("dp", "tensor"),
        P("dp", "tensor"),
        P("tensor", "dp"),
    )
    chips = Chips(mesh.shape["dp"])
    size = mesh.shape["tensor"]
    links = [[(i, i ^ 1 << b) for i in range(size)] for b in range(size.bit_length() - 1)]
    group = Group(links, "tensor")

    def run(*arrays):
        return local(chips, group, *arrays)

    return jax.shard_map(run, mesh=mesh, in_specs=in_specs, out_specs=out_specs, check_vma=False)
```

```python
import functools

import jax
import jax.numpy as jnp
import numpy as np
from jax import lax
from jax.experimental import pallas as pl
from jax.experimental.pallas import tpu as pltpu
from jax.sharding import PartitionSpec as P

HEAD_DIM = 64
SEQ = 512
EPS = 1e-05
THETA = 130000.0
BF16 = jnp.bfloat16
F32 = jnp.float32
FACTOR = HEAD_DIM**-0.5
PAIR = 2 * HEAD_DIM
HALF_SEQ = SEQ // 2
VMEM_LIMIT = 58 << 20
COST_SHARE = 4096


class Chain:
    def __init__(self):
        self.token = jnp.zeros((8, 128), F32)
        self.swaps, self.asked = [], []

    def join(self, *values):
        *values, self.token = lax.optimization_barrier((*values, self.token))
        return values

    def gate(self, *values):
        swaps, self.swaps = self.swaps, []
        asked, self.asked = self.asked, []
        joined = self.join(
            *values, *[held[i] for held, i in swaps], *[source for source, _, _, _ in asked]
        )
        for (held, i), value in zip(swaps, joined[len(values) :]):
            held[i] = value
        for (_, held, i, swap), value in zip(asked, joined[len(values) + len(swaps) :]):
            held[i] = swap(value)
            self.swaps.append((held, i))
        return joined[: len(values)]

    def end(self, *transfers):
        counts = [len(t.flying) for t in transfers]
        got = self.gate(*[value for t in transfers for value in t.flying])
        for t, count in zip(transfers, counts):
            if count:
                t.go_on(got[:count])
            got = got[count:]

    def ask(self, source, held, i, swap):
        self.asked.append((source, held, i, swap))

    def flush(self):
        for source, held, i, swap in self.asked:
            held[i] = swap(source)
        self.asked = []

    def call(self, body, grid, ins, outs, shapes, flops, scratch=(), prefetch=0, moved=0):
        first = prefetch + len(ins)
        second = first + 1 + len(outs)
        anywhere = pl.BlockSpec(memory_space=pl.ANY)

        def wrapped(*refs):
            body(*refs[:first], *refs[first + 1 : second], *refs[second + 1 :])

        run = pl.pallas_call(
            wrapped,
            grid_spec=pltpu.PrefetchScalarGridSpec(
                num_scalar_prefetch=prefetch,
                grid=grid,
                in_specs=[*ins, anywhere],
                out_specs=[*outs, anywhere],
                scratch_shapes=list(scratch),
            ),
            out_shape=[jax.ShapeDtypeStruct(s, t) for s, t in [*shapes, ((8, 128), F32)]],
            compiler_params=pltpu.CompilerParams(
                vmem_limit_bytes=VMEM_LIMIT, dimension_semantics=("arbitrary",) * len(grid)
            ),
            cost_estimate=pl.CostEstimate(
                flops=flops // COST_SHARE, bytes_accessed=moved // COST_SHARE, transcendentals=0
            ),
        )

        def with_token(*args):
            *results, self.token = run(*args, self.token)
            return results

        return with_token


class Chips:
    def __init__(self, size):
        self.bits = (size // 2).bit_length() - 1
        self.size = size
        self.swap = [(i, i ^ 1) for i in range(size)]
        self.links = [
            [(i, i ^ 2 << self.bits - 1 - p) for i in range(size)] for p in range(self.bits)
        ]
        flips = [
            sum(1 << self.bits - 1 - p for p in range(self.bits) if v >> p & 1)
            for v in range(1 << self.bits)
        ]
        table = [[i ^ 2 * f for f in flips] + [i ^ 2 * f ^ 1 for f in flips] for i in range(size)]
        self.table = np.array(table, np.int32)

    def send(self, value, p):
        return lax.ppermute(value, "dp", self.links[p])

    def other(self, value):
        return lax.ppermute(value, "dp", self.swap)


class Gather:
    def __init__(self, chips, chain, piece):
        self.chips, self.chain = chips, chain
        self.own = [piece] + [None] * (2**chips.bits - 1)
        self.others = list(self.own)
        self.ask(0)
        self.keys = [1 << p for p in range(chips.bits)]
        self.flying = [chips.send(piece, p) for p in range(chips.bits)]

    def ask(self, v):
        self.chain.ask(self.own[v], self.others, v, self.chips.other)

    def go_on(self, got):
        keys, self.keys, self.flying = self.keys, [], []
        for v, piece in zip(keys, got):
            self.own[v] = piece
            for p in range(v.bit_length(), self.chips.bits):
                self.keys.append(v | 1 << p)
                self.flying.append(self.chips.send(piece, p))
        for v in keys:
            self.ask(v)

    def pieces(self):
        while self.flying:
            self.chain.end(self)
        self.chain.flush()
        return self.own + self.others


class Sums:
    def __init__(self, chips, chain, mine, apart=False, hold=False, cut_in_two=False):
        self.chips, self.chain, self.apart, self.hold = chips, chain, apart, hold
        self.todo = []
        self.cut_in_two = cut_in_two and chips.bits == 2
        self.parts = [mine[0]]
        mine = list(mine[1:])
        self.direct, self.passed = [], []
        for p in range(chips.bits):
            self.direct.append(mine.pop(0))
            self.passed.append(mine.pop(0) if p else None)
        self.p = chips.bits - 1
        if self.cut_in_two:
            self.kinds = [0, 1]
            self.flying = [chips.send(half, 1) for half in self.in_two(self.passed[1])]
            return
        self.kinds = [self.p]
        self.flying = [chips.send(self.passed[self.p], self.p)]

    def in_two(self, values):
        width = values.shape[1] // 2
        return values[:, :width], values[:, width:]

    def go_on(self, got):
        rows = self.parts[0].shape[0]
        kinds, self.kinds, self.flying = self.kinds, [], []
        if self.p == 0:
            self.parts += got
            return
        if self.cut_in_two:
            self.p = 0
            total = self.direct[0].astype(F32) + jnp.concatenate(got, axis=1).astype(F32)
            self.todo = [(None, self.direct[1], 1), (None, total.astype(BF16), 0)]
            self.resume()
            return
        for kind, block in zip(kinds, got):
            if kind is None:
                self.parts.append(block)
                continue
            add = lambda held, first: (
                held.astype(F32) + block[first * rows : first * rows + held.shape[0]].astype(F32)
            ).astype(BF16)
            for q in range(kind):
                self.direct[q] = add(self.direct[q], (1 << q) - 1)
                if q:
                    self.passed[q] = add(self.passed[q], 1 << q)
        p, self.p = self.p, self.p - 1
        if p > 0:
            self.todo.append((None, self.direct[p], p))
        if p > 1:
            self.todo.append((p - 1, self.passed[p - 1], p - 1))
        if p == 1 and not self.apart:
            self.todo.append((None, self.direct[0], 0))
        if not self.hold:
            self.resume()

    def resume(self):
        todo, self.todo = self.todo, []
        values = self.chain.join(*[value for _, value, _ in todo])
        for (kind, _, p), value in zip(todo, values):
            self.kinds.append(kind)
            self.flying.append(self.chips.send(value, p))

    def send_half(self, i):
        while self.p > 0:
            self.chain.end(self)
        width = self.direct[0].shape[1] // 2
        (value,) = self.chain.join(self.direct[0][:, i * width : (i + 1) * width])
        self.kinds.append(None)
        self.flying.append(self.chips.send(value, 0))

    def terms(self):
        while self.flying or self.todo:
            if self.todo:
                self.resume()
            self.chain.end(self)
        return sorted(self.parts, key=lambda part: -part.shape[1])


class Group:
    def __init__(self, links, axes):
        self.links, self.axes = links, axes
        self.bits = len(links)
        self.size = 1 << self.bits
        self.orders = (list(range(self.bits)), list(range(self.bits))[::-1])

    def send(self, value, bit):
        return lax.ppermute(value, self.axes, self.links[bit])

    def messages(self):
        found = []
        for order in self.orders:
            found.append([])
            for top in reversed(range(self.bits)):
                found[-1].append(
                    [
                        1 << order[top] | sum(1 << order[p] for p in range(top) if v >> p & 1)
                        for v in range(1 << top)
                    ]
                )
        return found


class Spread:
    def __init__(self, group, chain, rows):
        self.group, self.chain = group, chain
        self.held = {0: [rows]}
        self.later = None
        self.keys = [(1 << b, None) for b in range(group.bits)]
        self.flying = [group.send(rows, b) for b in range(group.bits)]

    def go_on(self, got):
        fresh = list(zip(self.keys, got))
        self.keys, self.flying = [], []
        for (k, h), block in fresh:
            if h is None:
                self.held[k] = [block]
            else:
                self.held.setdefault(k, [None, None])[h] = block
        for (k, h), block in fresh:
            for way, order in enumerate(self.group.orders):
                if h is not None and h != way:
                    continue
                half = block.shape[1] // 2
                top = max(i for i, bit in enumerate(order) if k >> bit & 1)
                for i in range(top + 1, len(order)):
                    part = block if h is not None else block[:, way * half : (way + 1) * half]
                    self.keys.append((k | 1 << order[i], way))
                    if self.later is not None:
                        self.later.append((part, order[i]))
                    else:
                        self.flying.append(self.group.send(part, order[i]))

        if self.later:
            parts = self.chain.join(*[part for part, _ in self.later])
            self.later = [(part, bit) for part, (_, bit) in zip(parts, self.later)]

    def resume(self):
        later, self.later = self.later, None
        parts = self.chain.join(*[part for part, _ in later])
        self.flying = [self.group.send(part, bit) for part, (_, bit) in zip(parts, later)]

    def blocks(self):
        while self.flying:
            self.chain.end(self)
        return [self.held[k] for k in range(self.group.size)]


class Fold:
    def __init__(self, group, chain, own, sent):
        self.group, self.chain = group, chain
        self.rows = own[0].shape[0]
        self.sent = [list(half) for half in sent]
        self.parts = [[half] for half in own]
        self.wave = 0
        self.start()

    def start(self):
        self.flying = [
            self.group.send(self.sent[h][self.wave], order[self.group.bits - 1 - self.wave])
            for h, order in enumerate(self.group.orders)
        ]

    def go_on(self, got):
        self.wave += 1
        self.flying = []
        for h, block in enumerate(got):
            self.parts[h].append(block)
        for wave in range(self.wave, self.group.bits):
            sums = add_rows(self.chain, [sent[wave] for sent in self.sent], got)
            for sent, value in zip(self.sent, sums):
                sent[wave] = value
        if self.wave < self.group.bits:
            self.start()

    def total(self):
        while self.flying:
            self.chain.end(self)
        return self.parts


class Weight:
    def __init__(self, pieces, rows, start, width):
        self.pieces, self.rows, self.start, self.width = pieces, rows, start, width
        self.model = len(pieces) * rows

    def tiles(self, tile):
        first = self.start // tile
        return [pl.BlockSpec((self.rows, tile), lambda j: (0, first + j))] * len(self.pieces)


def nn(left, right):
    return lax.dot_general(left, right, (((1,), (0,)), ((), ())), preferred_element_type=F32)


def nt(left, right):
    return lax.dot_general(left, right, (((1,), (1,)), ((), ())), preferred_element_type=F32)


def tn(left, right):
    return lax.dot_general(left, right, (((0,), (0,)), ((), ())), preferred_element_type=F32)


def whole(shape):
    return pl.BlockSpec(shape, lambda *_: (0,) * len(shape))


def place(line_ref, j, width):
    return pl.ds(pl.multiple_of(line_ref[j] * width, 128), width)


def cut(width, j):
    return slice(j * width, (j + 1) * width)


def scale_of(values):
    return lax.rsqrt(jnp.mean(values * values, axis=-1, keepdims=True) + EPS)


def fetch_blocks(counts, refs, held, sems, k, slot, wait):
    first = 0
    for i, count in enumerate(counts):
        copies = []
        half = held.shape[2] // count
        for h in range(count):
            target = held.at[slot, :, pl.ds(h * half, half)]
            copies.append(pltpu.make_async_copy(refs[first + h], target, sems.at[slot, h]))
        first += count

        @pl.when(k == i)
        def _():
            for copy in copies:
                copy.wait() if wait else copy.start()


def fetched(counts, refs, held, sems):
    k = pl.program_id(0)

    @pl.when(k == 0)
    def _():
        fetch_blocks(counts, refs, held, sems, k, 0, False)

    fetch_blocks(counts, refs, held, sems, k + 1, (k + 1) % 2, False)
    fetch_blocks(counts, refs, held, sems, k, k % 2, True)
    return held.at[k % 2]


def norm_body(blocks, counts, line_ref, gain_ref, *refs):
    out_ref, held, sems = refs[sum(counts) :]
    x_ref = fetched(counts, refs, held, sems)
    width = out_ref.shape[1] // blocks
    scale = scale_of(x_ref[...].astype(F32))
    for j in range(blocks):
        part = x_ref[:, place(line_ref, j, width)].astype(F32)
        gain = gain_ref[0:1, cut(width, j)]
        out_ref[:, cut(width, j)] = (part * scale * gain).astype(BF16)


def order_body(blocks, counts, line_ref, gain_ref, *refs):
    out_ref, held, sems = refs[sum(counts) :]
    x_ref = fetched(counts, refs, held, sems)
    width = out_ref.shape[1] // blocks
    for j in range(blocks):
        out_ref[:, cut(width, j)] = x_ref[:, place(line_ref, j, width)]


def ordered(chain, body, line, gains, held):
    counts = [len(block) for block in held]
    rows, model = held[0][0].shape
    n = len(held)
    return chain.call(
        functools.partial(body, line.shape[0], counts),
        (n,),
        [whole(gains.shape)] + [pl.BlockSpec(memory_space=pl.ANY)] * sum(counts),
        [pl.BlockSpec((rows, model), lambda k, *_: (k, 0))],
        [((n * rows, model), BF16)],
        flops=20 * n * rows * model,
        scratch=[pltpu.VMEM((2, rows, model), BF16), pltpu.SemaphoreType.DMA((2, 2))],
        prefetch=1,
        moved=4 * n * rows * model,
    )(line, gains, *[array for block in held for array in block])[0]


def added(refs, span):
    total = refs[0][span, :].astype(F32)
    for ref in refs[1:]:
        total += ref[span, :].astype(F32)
    return total


def middle_body(blocks, m, line_ref, x_ref, gain_ref, *refs):
    middle_ref, out_ref = refs[2 * m :]
    width = x_ref.shape[1] // blocks
    half = x_ref.shape[1] // 2
    span = slice(None)
    middle_ref[:, :half] = added(refs[:m], span)
    middle_ref[:, half:] = added(refs[m : 2 * m], span)
    for j in range(blocks):
        here = x_ref[:, place(line_ref, j, width)].astype(F32)
        middle_ref[:, cut(width, j)] += here
    middle = middle_ref[...]
    out_ref[...] = (middle * scale_of(middle) * gain_ref[1:2, :]).astype(BF16)


def result_body(blocks, m, line_ref, middle_ref, gain_ref, *refs):
    out_ref = refs[2 * m]
    width = middle_ref.shape[1] // blocks
    span = slice(None)
    total = middle_ref[...] + jnp.concatenate(
        [added(refs[:m], span), added(refs[m : 2 * m], span)], axis=1
    )
    for j in range(blocks):
        out_ref[:, place(line_ref, j, width)] = total[:, cut(width, j)].astype(BF16)


def second_back_body(blocks, m, line_ref, dy_ref, gain_ref, *refs):
    middle_ref, out_ref, low_ref = refs[2 * m :]
    width = dy_ref.shape[1] // blocks
    span = slice(None)
    grad = jnp.concatenate([added(refs[:m], span), added(refs[m : 2 * m], span)], axis=1)
    middle = middle_ref[...]
    scale = scale_of(middle)
    normed = middle * scale
    scaled = grad * gain_ref[1:2, :]
    out_ref[...] = scale * (scaled - normed * jnp.mean(scaled * normed, axis=-1, keepdims=True))
    for j in range(blocks):
        out_ref[:, cut(width, j)] += dy_ref[:, place(line_ref, j, width)].astype(F32)
    low_ref[...] = out_ref[...].astype(BF16)


def first_back_body(blocks, m, line_ref, x_ref, gain_ref, *refs):
    above_ref, out_ref = refs[2 * m :]
    width = x_ref.shape[1] // blocks
    span = slice(None)
    scale = scale_of(x_ref[...].astype(F32))
    normed = jnp.concatenate(
        [x_ref[:, place(line_ref, j, width)].astype(F32) for j in range(blocks)], axis=1
    ) * scale
    grad = jnp.concatenate([added(refs[:m], span), added(refs[m : 2 * m], span)], axis=1)
    scaled = grad * gain_ref[0:1, :]
    back = scale * (scaled - normed * jnp.mean(scaled * normed, axis=-1, keepdims=True))
    total = above_ref[...] + back
    for j in range(blocks):
        out_ref[:, place(line_ref, j, width)] = total[:, cut(width, j)]


def by_rows(chain, body, line, first, gains, parts, more, kinds):
    rows, model = first.shape
    half = model // 2
    tile = min(128, rows)
    row = pl.BlockSpec((tile, model), lambda i, *_: (i, 0))
    slim = pl.BlockSpec((tile, half), lambda i, *_: (i, 0))
    m = len(parts[0])
    return chain.call(
        functools.partial(body, line.shape[0], m),
        (rows // tile,),
        [row, whole(gains.shape)] + [slim] * (2 * m) + [row] * len(more),
        [row] * len(kinds),
        [((rows, model), kind) for kind in kinds],
        flops=20 * rows * model,
        prefetch=1,
        moved=rows * model * (2 * m + 4 * len(kinds)),
    )(line, first, gains, *parts[0], *parts[1], *more)


def add_rows_body(count, *refs):
    for i in range(count):
        total = refs[i][...].astype(F32) + refs[count + i][...].astype(F32)
        refs[2 * count + i][...] = total.astype(BF16)


def add_rows(chain, helds, blocks):
    rows, columns = helds[0].shape
    tile = min(128, rows)
    steps = rows // tile
    count = len(helds)
    here = pl.BlockSpec((tile, columns), lambda i: (i, 0))
    return chain.call(
        functools.partial(add_rows_body, count),
        (steps,),
        [here] * count + [pl.BlockSpec((tile, columns), lambda i: (steps + i, 0))] * count,
        [here] * count,
        [((rows, columns), BF16)] * count,
        flops=count * rows * columns,
        moved=6 * count * rows * columns,
    )(*helds, *blocks)


def finish_body(m, halves, n, *refs):
    total = added(refs[:m], slice(None))
    if halves:
        total += jnp.concatenate([ref[...].astype(F32) for ref in refs[m : m + halves]], axis=1)
    m += halves
    weights, outs = refs[m : m + n], refs[m + n :]
    if not n:
        outs[0][...] = total.T
        return
    width = weights[0].shape[1]
    inner = jnp.zeros((total.shape[0], 1), F32)
    for i in range(n):
        part = total[:, cut(width, i)]
        outs[i][...] = part
        inner += jnp.sum(weights[i][...].astype(F32) * part, axis=1, keepdims=True)
    outs[n][...] = jnp.broadcast_to(inner, outs[n].shape)


def finish(chain, terms, weights=()):
    rows, columns = terms[0].shape
    tile = min(128, rows)
    row = pl.BlockSpec((tile, columns), lambda i: (i, 0))
    n = len(weights)
    halves = sum(1 for term in terms if term.shape[1] < columns)
    half = [pl.BlockSpec((tile, columns // 2), lambda i: (i, 0))] * halves
    if n:
        slim = pl.BlockSpec((tile, columns // n), lambda i: (i, 0))
        outs = [slim] * n + [pl.BlockSpec((tile, 128), lambda i: (i, 0))]
        shapes = [((rows, columns // n), F32)] * n + [((rows, 128), F32)]
    else:
        slim = None
        outs = [pl.BlockSpec((columns, tile), lambda i: (0, i))]
        shapes = [((columns, rows), F32)]
    results = chain.call(
        functools.partial(finish_body, len(terms) - halves, halves, n),
        (rows // tile,),
        [row] * (len(terms) - halves) + half + [slim] * n,
        outs,
        shapes,
        flops=4 * rows * columns,
        moved=rows * columns * 12,
    )(*terms, *weights)
    if n:
        results[n] = results[n][:, 0]
    return results


def rope_tables(place):
    half = HEAD_DIM // 2
    freq = THETA ** (-2.0 * jnp.arange(half, dtype=F32) / HEAD_DIM)
    angle = place.astype(F32)[:, None] * freq[None, :]
    cosine, sine = jnp.cos(angle), jnp.sin(angle)
    return (
        jnp.concatenate([cosine] * (PAIR // half), axis=1),
        jnp.concatenate([-sine, sine] * (PAIR // HEAD_DIM), axis=1),
    )


def turn(values):
    half = HEAD_DIM // 2
    width = values.shape[-1]
    lane = lax.broadcasted_iota(jnp.int32, values.shape, 1) % HEAD_DIM
    return jnp.where(
        lane < half, pltpu.roll(values, width - half, 1), pltpu.roll(values, half, 1)
    )


def joined(refs):
    return jnp.concatenate([r[...] for r in refs], axis=0)


def qkv_body(n, x_ref, cos_ref, sin_ref, *refs):
    weights, outs = refs[: 3 * n], refs[3 * n :]
    rows = x_ref.shape[0]
    tile = outs[0].shape[1]
    for i in range(3):
        weight = joined(weights[i * n : (i + 1) * n])
        for s in range(rows // SEQ):
            span = slice(s * SEQ, (s + 1) * SEQ)
            product = nn(x_ref[span, :], weight)
            if i == 2:
                outs[i][span, :] = product.astype(BF16)
                continue
            for t in range(tile // PAIR):
                here = product[:, t * PAIR : (t + 1) * PAIR]
                turned = here * cos_ref[...] + turn(here) * sin_ref[...]
                outs[i][span, t * PAIR : (t + 1) * PAIR] = turned.astype(BF16)


def project(chain, x, tables, query, key, value):
    rows, model = x.shape
    n, width = len(query.pieces), query.width
    tile = min(256, width)
    out = pl.BlockSpec((rows, tile), lambda j: (0, j))
    return chain.call(
        functools.partial(qkv_body, n),
        (width // tile,),
        [whole(x.shape), whole((SEQ, PAIR)), whole((SEQ, PAIR))]
        + query.tiles(tile)
        + key.tiles(tile)
        + value.tiles(tile),
        [out] * 3,
        [((rows, width), BF16)] * 3,
        flops=6 * rows * model * width,
        moved=2 * (rows * model + 3 * model * width + 3 * rows * width),
    )(x, *tables, *query.pieces, *key.pieces, *value.pieces)


def collect(counts, refs, held, sems):
    rows = held.shape[0] // len(counts)
    copies = []
    for k, count in enumerate(counts):
        half = held.shape[1] // count
        for h in range(count):
            target = held.at[pl.ds(k * rows, rows), pl.ds(h * half, half)]
            i = len(copies)
            copies.append(pltpu.make_async_copy(refs[i], target, sems.at[i]))
    for copy in copies:
        copy.start()
    for copy in copies:
        copy.wait()


def gate_body(n, counts, *refs):
    m = sum(counts)
    gate_w, up_w = refs[m : m + n], refs[m + n : m + 2 * n]
    left_ref, hidden_ref, slope_ref, silu_ref, theirs_ref, x_ref, turned, sems = refs[m + 2 * n :]

    @pl.when(pl.program_id(0) == 0)
    def _():
        collect(counts, refs, x_ref, sems)
        turned[...] = left_ref[...].T

    gate_weight, up_weight = joined(gate_w), joined(up_w)
    for s in range(x_ref.shape[0] // SEQ):
        span = slice(s * SEQ, (s + 1) * SEQ)
        gate = nn(x_ref[span, :], gate_weight)
        up = nn(x_ref[span, :], up_weight)
        sigm = jax.nn.sigmoid(gate)
        silu = gate * sigm
        hidden_ref[span, :] = (silu * up).astype(BF16)
        silu_ref[span, :] = silu.astype(BF16)
        slope_ref[span, :] = (up * sigm * (1.0 + gate * (1.0 - sigm))).astype(BF16)
    theirs_ref[...] = nn(turned[...], hidden_ref[...]).astype(BF16)


def collected(held):
    counts = [len(block) for block in held]
    rows, model = held[0][0].shape
    scratch = [
        pltpu.VMEM((len(held) * rows, model), BF16),
        pltpu.SemaphoreType.DMA((sum(counts),)),
    ]
    arrays = [array for block in held for array in block]
    return counts, arrays, [pl.BlockSpec(memory_space=pl.ANY)] * len(arrays), scratch


def gate_up(chain, held, gate, up, grads):
    counts, arrays, specs, scratch = collected(held)
    rows, model = scratch[0].shape
    n, width = len(gate.pieces), gate.width
    tile = min(256, width)
    out = pl.BlockSpec((rows, tile), lambda j: (0, j))
    half = model // 2
    return chain.call(
        functools.partial(gate_body, n, counts),
        (width // tile,),
        specs
        + gate.tiles(tile)
        + up.tiles(tile)
        + [pl.BlockSpec((rows, half), lambda j: (0, 1))],
        [out] * 3 + [pl.BlockSpec((half, tile), lambda j: (0, j))],
        [((rows, width), BF16)] * 3 + [((half, width), BF16)],
        flops=6 * rows * model * width,
        scratch=[scratch[0], pltpu.VMEM((half, rows), BF16), scratch[1]],
        moved=2 * (rows * model + 2 * model * width + 3 * rows * width),
    )(*arrays, *gate.pieces, *up.pieces, grads)


def half_blocks(left, which):
    lefts = [block[0] if len(block) == 1 else block[which] for block in left]
    rows, half = lefts[0].shape[0], left[0][0].shape[1] // 2
    places = [which if len(block) == 1 else 0 for block in left]
    return lefts, [
        pl.BlockSpec((rows, half), functools.partial(lambda at, j: (0, at), at)) for at in places
    ]


def hidden_back_body(n, blocks, g_ref, *refs):
    weights, slope_ref, silu_ref = refs[:n], refs[n], refs[n + 1]
    lefts, refs = refs[n + 2 : n + 2 + blocks], refs[n + 2 + blocks :]
    gate_ref, up_ref, theirs_ref, turned = refs
    rows = turned.shape[1] // blocks

    @pl.when(pl.program_id(0) == 0)
    def _():
        for k in range(blocks):
            turned[:, cut(rows, k)] = lefts[k][...].T

    weight = joined(weights)
    for s in range(g_ref.shape[0] // SEQ):
        span = slice(s * SEQ, (s + 1) * SEQ)
        grad = nn(g_ref[span, :], weight)
        gate_ref[span, :] = (grad * slope_ref[span, :].astype(F32)).astype(BF16)
        up_ref[span, :] = (grad * silu_ref[span, :].astype(F32)).astype(BF16)
    theirs_ref[...] = nn(turned[...], gate_ref[...]).astype(BF16)


def hidden_back(chain, grads, down, slope, silu, left):
    rows, model = grads.shape
    n, width = len(down.pieces), down.width
    tile = min(256, width)
    out = pl.BlockSpec((rows, tile), lambda j: (0, j))
    lefts, specs = half_blocks(left, 1)
    half = model // 2
    return chain.call(
        functools.partial(hidden_back_body, n, len(lefts)),
        (width // tile,),
        [whole(grads.shape)] + down.tiles(tile) + [out] * 2 + specs,
        [out] * 2 + [pl.BlockSpec((half, tile), lambda j: (0, j))],
        [((rows, width), BF16)] * 2 + [((half, width), BF16)],
        flops=3 * rows * model * width,
        scratch=[pltpu.VMEM((half, rows), BF16)],
        moved=2 * (rows * model + model * width + 4 * rows * width),
    )(grads, *down.pieces, slope, silu, *lefts)


def mixed_back_body(n, counts, *refs):
    m = sum(counts)
    out_ref, x_ref, sems = refs[m + n :]

    @pl.when(pl.program_id(0) == 0)
    def _():
        collect(counts, refs, x_ref, sems)

    out_ref[...] = nn(x_ref[...], joined(refs[m : m + n])).astype(BF16)


def mixed_back(chain, held, out):
    counts, arrays, specs, scratch = collected(held)
    rows, model = scratch[0].shape
    n, width = len(out.pieces), out.width
    tile = min(256, width)
    return chain.call(
        functools.partial(mixed_back_body, n, counts),
        (width // tile,),
        specs + out.tiles(tile),
        [pl.BlockSpec((rows, tile), lambda j: (0, j))],
        [((rows, width), BF16)],
        flops=2 * rows * model * width,
        scratch=scratch,
        moved=2 * (rows * model + model * width + rows * width),
    )(*arrays, *out.pieces)[0]


def trans_body(n, starts, targets, chunks, *refs):
    parts, blocks = len(starts), len(targets[0])
    arrays = refs[:parts]
    pieces, outs = refs[parts : parts * (n + 1)], refs[parts * (n + 1) : -6]
    lefts, held, ready, left_sems, sems, out_sems = refs[-6:]
    j = pl.program_id(0)
    depth, width = held.shape[2:]
    rows = ready.shape[1] // blocks
    chunk = width // chunks

    def left_copy(p, c):
        span = pl.ds(c * chunk, chunk)
        return pltpu.make_async_copy(
            arrays[p].at[:, span], lefts.at[p, :, span], left_sems.at[p, c]
        )

    def copy(i, p, slot):
        source = pieces[p * n + i].at[pl.ds(0, depth), pl.ds(starts[p], width)]
        return pltpu.make_async_copy(source, held.at[slot, p], sems.at[slot, p])

    def fetch(step, slot):
        for i in range(n):

            @pl.when(step == i)
            def _():
                for p in range(parts):
                    copy(i, p, slot).start()

    def leave(slot, k, array, first, column):
        target = outs[array].at[pl.ds(first, rows), pl.ds(column, depth)]
        source = ready.at[slot, pl.ds(k * rows, rows), :]
        return pltpu.make_async_copy(source, target, out_sems.at[slot, k])

    def left(slot):
        for k in range(blocks):
            leave(slot, k, 0, 0, 0).wait()

    @pl.when(j == 0)
    def _():
        fetch(j, 0)
        for c in range(chunks):
            for p in range(parts):
                left_copy(p, c).start()

    @pl.when(j + 1 < n)
    def _():
        fetch(j + 1, (j + 1) % 2)

    slot = j % 2
    for p in range(parts):
        copy(0, p, slot).wait()

    @pl.when(j >= 2)
    def _():
        left(slot)

    spans = [slice(s * SEQ, (s + 1) * SEQ) for s in range(blocks * rows // SEQ)]

    @pl.when(j == 0)
    def _():
        totals = [None] * len(spans)
        for c in range(chunks):
            for p in range(parts):
                left_copy(p, c).wait()
                for s, span in enumerate(spans):
                    part = nt(lefts[p, span, cut(chunk, c)], held[0, p, :, cut(chunk, c)])
                    totals[s] = part if totals[s] is None else totals[s] + part
        for total, span in zip(totals, spans):
            ready[0, span, :] = total.astype(BF16)

    @pl.when(j > 0)
    def _():
        for span in spans:
            total = nt(lefts[0, span, :], held[slot, 0])
            for p in range(1, parts):
                total += nt(lefts[p, span, :], held[slot, p])
            ready[slot, span, :] = total.astype(BF16)

    column = pl.multiple_of(j % (n // 2) * depth, 128)
    for h in range(2):

        @pl.when((j >= n // 2) == (h == 1))
        def _():
            for k, (array, first) in enumerate(targets[h]):
                leave(slot, k, array, first, column).start()

    @pl.when(j == n - 1)
    def _():
        left(1 - slot)
        left(slot)


def times_trans(chain, parts, group):
    weights = [weight for _, weight in parts]
    n, depth, width = len(weights[0].pieces), weights[0].rows, weights[0].width
    rows = parts[0][0].shape[0]
    half = weights[0].model // 2
    size = rows // group.size
    messages = group.messages()
    shapes = [((size, half), BF16)] * 2
    targets = [{0: (0, 0)}, {0: (1, 0)}]
    for h in range(2):
        for keys in messages[h]:
            for i, k in enumerate(keys):
                targets[h][k] = (len(shapes), i * size)
            shapes.append(((len(keys) * size, half), BF16))
    targets = [[t[k] for k in range(group.size)] for t in targets]
    anywhere = pl.BlockSpec(memory_space=pl.ANY)
    chunks = max(1, width // 512)
    outs = chain.call(
        functools.partial(trans_body, n, [weight.start for weight in weights], targets, chunks),
        (n,),
        [anywhere] * ((n + 1) * len(parts)),
        [anywhere] * len(shapes),
        shapes,
        flops=4 * rows * half * width * len(parts),
        scratch=[
            pltpu.VMEM((len(parts), rows, width), BF16),
            pltpu.VMEM((2, len(parts), depth, width), BF16),
            pltpu.VMEM((2, rows, depth), BF16),
            pltpu.SemaphoreType.DMA((len(parts), chunks)),
            pltpu.SemaphoreType.DMA((2, len(parts))),
            pltpu.SemaphoreType.DMA((2, group.size)),
        ],
        moved=2 * (2 * rows * half + len(parts) * (rows + 2 * half) * width),
    )(*[left for left, _ in parts], *[piece for weight in weights for piece in weight.pieces])
    m = group.bits
    return outs[:2], [outs[2 : 2 + m], outs[2 + m :]]


def grad_body(parts, got, blocks, steps, *refs):
    lefts, refs = refs[:blocks], refs[blocks:]
    rights, refs = refs[:parts], refs[parts:]
    got_ref = refs[0] if got else None
    outs, turned = refs[got:-1], refs[-1]
    j = pl.program_id(0)

    @pl.when(j == 0)
    def _():
        rows = turned.shape[1] // blocks
        for k in range(blocks):
            turned[:, cut(rows, k)] = lefts[k][...].T

    for i in range(parts):

        @pl.when((j >= i * steps) & (j < (i + 1) * steps))
        def _():
            total = nn(turned[...], rights[i][...])
            if got:
                total += got_ref[...].astype(F32)
            total = total.astype(BF16)
            first = 0
            for out_ref in outs:
                count = out_ref.shape[0]
                out_ref[...] = total[first : first + count]
                first += count


def weight_grads(chain, left, which, rights, got=None, bits=0):
    rows, width = rights[0].shape
    parts = len(rights)
    tile = min(512, width)
    steps = width // tile
    lefts, ins = half_blocks(left if isinstance(left, list) else [[left]], which)
    blocks, half = len(lefts), ins[0].block_shape[1]
    for i in range(parts):
        ins.append(
            pl.BlockSpec(
                (rows, tile),
                functools.partial(
                    lambda first, j: (0, jnp.clip(j - first, 0, steps - 1)), i * steps
                ),
            )
        )
    column = lambda j: (0, j)
    more = [] if got is None else [got]
    sizes = [half >> bits]
    for p in range(bits):
        sizes += [sizes[0], ((1 << p) - 1) * sizes[0]] if p else [sizes[0]]
    return chain.call(
        functools.partial(grad_body, parts, len(more), blocks, steps),
        (parts * steps,),
        ins + [pl.BlockSpec((half, tile), column)] * len(more),
        [pl.BlockSpec((size, tile), column) for size in sizes],
        [((size, parts * width), BF16) for size in sizes],
        flops=2 * rows * half * width * parts,
        scratch=[pltpu.VMEM((half, rows), BF16)],
        moved=2 * (rows * half + parts * (rows + half) * width),
    )(*lefts, *rights, *more)


def causal(scores):
    past = scores.shape[0] - HALF_SEQ
    key = lax.broadcasted_iota(jnp.int32, (HALF_SEQ, HALF_SEQ), 0)
    query = lax.broadcasted_iota(jnp.int32, (HALF_SEQ, HALF_SEQ), 1)
    last = jnp.where(key <= query, scores[past:], -1e30)
    return last if past == 0 else jnp.concatenate([scores[:past], last], axis=0)


def head_of(h):
    return slice(h * HEAD_DIM, (h + 1) * HEAD_DIM)


def span_of(b):
    return slice(b * HALF_SEQ, (b + 1) * HALF_SEQ)


def in_place(shift_ref, ref, count):
    rows = SEQ // count
    spans = [pl.ds(pl.multiple_of((i ^ shift_ref[0]) * rows, rows), rows) for i in range(count)]
    return jnp.concatenate([ref[span, :] for span in spans], axis=0)


def put_back(shift_ref, ref, count, values):
    rows = SEQ // count
    for i in range(count):
        ref[pl.ds(pl.multiple_of((i ^ shift_ref[0]) * rows, rows), rows), :] = values[cut(rows, i)]


def one_head(values, h):
    lane = lax.broadcasted_iota(jnp.int32, values.shape, 1)
    return jnp.where(lane // HEAD_DIM == h, values, jnp.zeros_like(values))


def attend_body(count, shift_ref, q_ref, k_ref, v_ref, out_ref, sum_ref):
    queries, keys = in_place(shift_ref, q_ref, count), in_place(shift_ref, k_ref, count)
    values = in_place(shift_ref, v_ref, count).astype(F32).T.astype(BF16)
    heads = []
    for h in range(q_ref.shape[1] // HEAD_DIM):
        blocks = []
        for b in range(2):
            reach = (b + 1) * HALF_SEQ
            query = one_head(queries[span_of(b)] * BF16(FACTOR), h)
            scores = causal(nt(keys[:reach], query))
            top = jnp.max(scores, axis=0, keepdims=True)
            expo = jnp.exp(scores - top)
            total = jnp.sum(expo, axis=0, keepdims=True)
            mixed = nn(values[head_of(h), :reach], expo.astype(BF16))
            blocks.append(mixed * (1.0 / total))
            sum_ref[0, h, :, span_of(b)] = top + jnp.log(total)
        heads.append(jnp.concatenate(blocks, axis=1))
    put_back(shift_ref, out_ref, count, jnp.concatenate(heads, axis=0).T.astype(BF16))


def attention_specs(rows, width, wide):
    wide = min(wide, width)
    tile = pl.BlockSpec((SEQ, wide), lambda s, p, _: (s, p))
    sums = pl.BlockSpec((1, wide // HEAD_DIM, 1, SEQ), lambda s, p, _: (s, p, 0, 0))
    return (rows // SEQ, width // wide), tile, sums


def attend(chain, shift, count, query, key, value):
    rows, width = query.shape
    grid, tile, sums = attention_specs(rows, width, 256)
    return chain.call(
        functools.partial(attend_body, count),
        grid,
        [tile] * 3,
        [tile, sums],
        [((rows, width), BF16), ((rows // SEQ, width // HEAD_DIM, 1, SEQ), F32)],
        flops=16 * rows * width * SEQ,
        prefetch=1,
        moved=8 * rows * width,
    )(shift, query, key, value)


def attend_back_body(
    count, shift_ref, q_ref, k_ref, v_ref, g_ref, sum_ref, cos_ref, sin_ref, dq_ref, dk_ref, dv_ref
):
    queries, keys, values, grads = (
        in_place(shift_ref, ref, count) for ref in (q_ref, k_ref, v_ref, g_ref)
    )
    turned = keys.astype(F32).T.astype(BF16)
    dq_heads = []
    dk, dv = [], []
    for b in range(2):
        reach = (b + 1) * HALF_SEQ
        dq, dk_sum, dv_sum = [], None, None
        for h in range(q_ref.shape[1] // HEAD_DIM):
            query = one_head(queries[span_of(b)], h)
            grad = one_head(grads[span_of(b)], h)
            scores = causal(nt(keys[:reach], query * BF16(FACTOR)))
            probs = jnp.exp(scores - sum_ref[0, h, :, span_of(b)])
            probs_grad = nt(values[:reach], grad)
            inner = jnp.sum(probs * probs_grad, axis=0, keepdims=True)
            score_grad = (probs * (probs_grad - inner)).astype(BF16)
            dv_part, dk_part = nn(probs.astype(BF16), grad), nn(score_grad, query)
            dv_sum = dv_part if dv_sum is None else dv_sum + dv_part
            dk_sum = dk_part if dk_sum is None else dk_sum + dk_part
            dq.append(nn(turned[head_of(h), :reach], score_grad))
        dq_heads.append(jnp.concatenate(dq, axis=0))
        dk.append(dk_sum)
        dv.append(dv_sum)

    def whole_rows(parts):
        early, late = parts
        return jnp.concatenate([late[:HALF_SEQ] + early, late[HALF_SEQ:]], axis=0)

    dq = jnp.concatenate(dq_heads, axis=1).T * FACTOR
    dk = whole_rows(dk) * FACTOR
    dv = whole_rows(dv).astype(BF16)
    copies = dq.shape[1] // PAIR
    cosine = jnp.concatenate([cos_ref[...]] * copies, axis=1)
    sine = jnp.concatenate([sin_ref[...]] * copies, axis=1)
    put_back(shift_ref, dq_ref, count, (dq * cosine - turn(dq) * sine).astype(BF16))
    put_back(shift_ref, dk_ref, count, (dk * cosine - turn(dk) * sine).astype(BF16))
    put_back(shift_ref, dv_ref, count, dv)


def attend_back(chain, shift, count, query, key, value, grad, logsum, tables):
    rows, width = query.shape
    grid, tile, sums = attention_specs(rows, width, PAIR)
    return chain.call(
        functools.partial(attend_back_body, count),
        grid,
        [tile] * 4 + [sums] + [whole((SEQ, PAIR))] * 2,
        [tile] * 3,
        [((rows, width), BF16)] * 3,
        flops=40 * rows * width * SEQ,
        prefetch=1,
        moved=14 * rows * width,
    )(shift, query, key, value, grad, logsum, *tables)


def local(
    chips,
    group,
    tokens,
    attn_gain,
    query_weight,
    key_weight,
    value_weight,
    output_weight,
    ffn_gain,
    gate_weight,
    up_weight,
    down_weight,
    cotangent,
):
    line = jnp.asarray(chips.table)[lax.axis_index("dp")]
    rows, model = tokens.shape
    count = SEQ // rows
    shift = lax.axis_index("tensor") % count
    row = jnp.arange(SEQ, dtype=jnp.int32)
    places = rope_tables(row)
    tables = rope_tables((row // rows ^ shift) * rows + row % rows)
    shift = jnp.reshape(shift, (1,)).astype(jnp.int32)
    early = (*places, *tables, line, shift)
    depth, own = query_weight.shape
    hidden_units = gate_weight.shape[1]
    chain = Chain()

    def gather(piece):
        return Gather(chips, chain, chain.join(piece)[0])

    def spread_of(values):
        return Spread(group, chain, chain.join(values)[0])

    def fold_of(part):
        own_part, sent = part
        sent = chain.join(*sent[0], *sent[1])
        return Fold(group, chain, own_part, [sent[: group.bits], sent[group.bits :]])

    def grads_of(left, rights, theirs=None):
        if theirs is None:
            (theirs,) = weight_grads(chain, left, 1, rights)
        got = [None]
        chain.ask(theirs, got, 0, chips.other)

        def mine(**how):
            if got[0] is None:
                chain.flush()
            blocks = weight_grads(chain, left, 0, rights, got[0], chips.bits)
            return Sums(chips, chain, blocks, **how)

        return mine

    extra = jnp.concatenate([attn_gain, ffn_gain, jnp.zeros((4 * own - 2 * depth,), BF16)])
    attn = jnp.concatenate([query_weight, key_weight, value_weight, output_weight.T], axis=1)
    attn = gather(jnp.concatenate([attn, jnp.broadcast_to(extra, (16, 4 * own))], axis=0))
    spread = spread_of(tokens)
    grads_spread = spread_of(cotangent)
    grads_spread.later = []
    down_turned, *early = chain.join(down_weight.T, *early)
    places, tables, line, shift = early[:2], early[2:4], early[4], early[5]
    chain.end(attn, spread, grads_spread)
    chain.end(attn, spread)
    all_tokens = spread.blocks()
    attn = attn.pieces()
    pair = gather(jnp.concatenate([gate_weight, up_weight], axis=1))
    w_query, w_key, w_value, w_output = [Weight(attn, depth, i * own, own) for i in range(4)]
    gains = jnp.concatenate(
        [piece[depth : depth + 1, : 2 * depth].reshape(2, depth) for piece in attn], axis=1
    ).astype(F32)

    group_one = ordered(chain, norm_body, line, gains, all_tokens)
    grads_spread.resume()
    query, key, value = project(chain, group_one, tables, w_query, w_key, w_value)
    mixed, logsum = attend(chain, shift, count, query, key, value)
    out_part = times_trans(chain, [(mixed, w_output)], group)
    fold = fold_of(out_part)
    chain.end(fold, pair, grads_spread)
    grad_rows = ordered(chain, order_body, line, gains, grads_spread.blocks())
    chain.end(fold)
    attended = fold.total()
    middle, second = by_rows(
        chain, middle_body, line, tokens, gains, attended, [], [F32, BF16]
    )
    spread = spread_of(second)
    chain.end(spread, pair)
    pair = pair.pieces()
    down = gather(down_turned)
    chain.end(spread)
    group_two = spread.blocks()
    w_gate = Weight(pair, depth, 0, hidden_units)
    w_up = Weight(pair, depth, hidden_units, hidden_units)
    hidden, slope, silu, theirs = gate_up(chain, group_two, w_gate, w_up, grad_rows)

    mine = grads_of(grad_rows, [hidden], theirs)
    chain.end(down)
    chain.flush()
    down_sum = mine()
    w_down = Weight(down.pieces(), depth, 0, hidden_units)
    gate_grad, up_grad, gate_theirs = hidden_back(
        chain, grad_rows, w_down, slope, silu, group_two
    )
    mine_gate = grads_of(group_two, [gate_grad], gate_theirs)
    chain.end(down_sum)
    second_part = times_trans(chain, [(gate_grad, w_gate), (up_grad, w_up)], group)
    fold = fold_of(second_part)
    gate_sum = mine_gate(hold=True)
    (up_theirs,) = weight_grads(chain, group_two, 1, [up_grad])
    chain.end(down_sum)
    mine_up = grads_of(group_two, [up_grad], up_theirs)
    chain.end(fold)
    up_sum = mine_up(hold=True)
    chain.end(fold)
    second_grad = fold.total()
    middle_grad, low_grad = by_rows(
        chain, second_back_body, line, cotangent, gains, second_grad, [middle], [F32, BF16]
    )
    spread = spread_of(low_grad)
    chain.end(gate_sum)
    gate_sum.resume()
    result_part = times_trans(chain, [(hidden, w_down)], group)
    chain.end(spread)
    (down_sum,) = finish(chain, down_sum.terms())
    chain.end(spread)
    attn_grads = spread.blocks()

    mixed_grad = mixed_back(chain, attn_grads, w_output)
    query_back, key_back, value_back = attend_back(
        chain, shift, count, query, key, value, mixed_grad, logsum, places
    )
    mine_qkv = grads_of(group_one, [query_back, key_back, value_back])
    mine_out = grads_of(attn_grads, [mixed])
    chain.end(gate_sum, up_sum)
    up_sum.resume()
    fold = fold_of(result_part)
    qkv_sum = mine_qkv()
    first_part = times_trans(
        chain, [(query_back, w_query), (key_back, w_key), (value_back, w_value)], group
    )
    out_sum = mine_out(hold=True)
    chain.end(fold)
    gate_sum, gate_inner = finish(chain, gate_sum.terms(), [gate_weight])
    chain.end(fold)
    result_part = fold.total()
    (layer_out,) = by_rows(chain, result_body, line, middle, gains, result_part, [], [BF16])
    fold = fold_of(first_part)
    chain.end(up_sum, out_sum)
    chain.end(qkv_sum)
    out_sum.resume()
    up_sum, up_inner = finish(chain, up_sum.terms(), [up_weight])
    chain.end(fold)
    chain.end(fold)
    first_grad = fold.total()
    (input_grad,) = by_rows(
        chain, first_back_body, line, tokens, gains, first_grad, [middle_grad], [F32]
    )
    chain.end(qkv_sum)
    query_sum, key_sum, value_sum, qkv_inner = finish(
        chain, qkv_sum.terms(), [query_weight, key_weight, value_weight]
    )
    gain_parts = jnp.stack(
        [qkv_inner / attn_gain.astype(F32), (gate_inner + up_inner) / ffn_gain.astype(F32)]
    )
    (gain_parts,) = chain.join(gain_parts)
    (out_sum,) = finish(chain, out_sum.terms())
    gain_totals = gain_parts
    for k in range(1, group.size):
        pairs = [(i, i ^ k) for i in range(group.size)]
        gain_totals += lax.ppermute(gain_parts, "tensor", pairs)
    gain_one_total, gain_two_total = gain_totals[0], gain_totals[1]
    return (
        layer_out,
        input_grad,
        gain_one_total,
        query_sum,
        key_sum,
        value_sum,
        out_sum,
        gain_two_total,
        gate_sum,
        up_sum,
        down_sum,
    )


def solution(mesh):
    in_specs = (
        P(("dp", "tensor"), None),
        P("dp"),
        P("dp", "tensor"),
        P("dp", "tensor"),
        P("dp", "tensor"),
        P("tensor", "dp"),
        P("dp"),
        P("dp", "tensor"),
        P("dp", "tensor"),
        P("tensor", "dp"),
        P(("dp", "tensor"), None),
    )
    out_specs = (
        P(("dp", "tensor"), None),
        P(("dp", "tensor"), None),
        P("dp"),
        P("dp", "tensor"),
        P("dp", "tensor"),
        P("dp", "tensor"),
        P("tensor", "dp"),
        P("dp"),
        P("dp", "tensor"),
        P("dp", "tensor"),
        P("tensor", "dp"),
    )
    chips = Chips(mesh.shape["dp"])
    size = mesh.shape["tensor"]
    links = [[(i, i ^ 1 << b) for i in range(size)] for b in range(size.bit_length() - 1)]
    group = Group(links, "tensor")

    def run(*arrays):
        return local(chips, group, *arrays)

    return jax.shard_map(run, mesh=mesh, in_specs=in_specs, out_specs=out_specs, check_vma=False)
```

```python
import functools

import jax
import jax.numpy as jnp
import numpy as np
from jax import lax
from jax.experimental import pallas as pl
from jax.experimental.pallas import tpu as pltpu
from jax.sharding import PartitionSpec as P

HEAD_DIM = 64
SEQ = 512
EPS = 1e-05
THETA = 130000.0
BF16 = jnp.bfloat16
F32 = jnp.float32
FACTOR = HEAD_DIM**-0.5
PAIR = 2 * HEAD_DIM
HALF_SEQ = SEQ // 2
VMEM_LIMIT = 58 << 20
COST_SHARE = 4096


class Chain:
    def __init__(self):
        self.token = jnp.zeros((8, 128), F32)
        self.swaps, self.asked = [], []

    def join(self, *values):
        *values, self.token = lax.optimization_barrier((*values, self.token))
        return values

    def gate(self, *values):
        swaps, self.swaps = self.swaps, []
        asked, self.asked = self.asked, []
        joined = self.join(
            *values, *[held[i] for held, i in swaps], *[source for source, _, _, _ in asked]
        )
        for (held, i), value in zip(swaps, joined[len(values) :]):
            held[i] = value
        for (_, held, i, swap), value in zip(asked, joined[len(values) + len(swaps) :]):
            held[i] = swap(value)
            self.swaps.append((held, i))
        return joined[: len(values)]

    def end(self, *transfers):
        counts = [len(t.flying) for t in transfers]
        got = self.gate(*[value for t in transfers for value in t.flying])
        for t, count in zip(transfers, counts):
            if count:
                t.go_on(got[:count])
            got = got[count:]

    def ask(self, source, held, i, swap):
        self.asked.append((source, held, i, swap))

    def flush(self):
        for source, held, i, swap in self.asked:
            held[i] = swap(source)
        self.asked = []

    def call(self, body, grid, ins, outs, shapes, flops, scratch=(), prefetch=0, moved=0):
        first = prefetch + len(ins)
        second = first + 1 + len(outs)
        anywhere = pl.BlockSpec(memory_space=pl.ANY)

        def wrapped(*refs):
            body(*refs[:first], *refs[first + 1 : second], *refs[second + 1 :])

        run = pl.pallas_call(
            wrapped,
            grid_spec=pltpu.PrefetchScalarGridSpec(
                num_scalar_prefetch=prefetch,
                grid=grid,
                in_specs=[*ins, anywhere],
                out_specs=[*outs, anywhere],
                scratch_shapes=list(scratch),
            ),
            out_shape=[jax.ShapeDtypeStruct(s, t) for s, t in [*shapes, ((8, 128), F32)]],
            compiler_params=pltpu.CompilerParams(
                vmem_limit_bytes=VMEM_LIMIT, dimension_semantics=("arbitrary",) * len(grid)
            ),
            cost_estimate=pl.CostEstimate(
                flops=flops // COST_SHARE, bytes_accessed=moved // COST_SHARE, transcendentals=0
            ),
        )

        def with_token(*args):
            *results, self.token = run(*args, self.token)
            return results

        return with_token


class Chips:
    def __init__(self, size):
        self.bits = (size // 2).bit_length() - 1
        self.size = size
        self.swap = [(i, i ^ 1) for i in range(size)]
        self.links = [
            [(i, i ^ 2 << self.bits - 1 - p) for i in range(size)] for p in range(self.bits)
        ]
        flips = [
            sum(1 << self.bits - 1 - p for p in range(self.bits) if v >> p & 1)
            for v in range(1 << self.bits)
        ]
        table = [[i ^ 2 * f for f in flips] + [i ^ 2 * f ^ 1 for f in flips] for i in range(size)]
        self.table = np.array(table, np.int32)

    def send(self, value, p):
        return lax.ppermute(value, "dp", self.links[p])

    def other(self, value):
        return lax.ppermute(value, "dp", self.swap)


class Gather:
    def __init__(self, chips, chain, piece):
        self.chips, self.chain = chips, chain
        self.own = [piece] + [None] * (2**chips.bits - 1)
        self.others = list(self.own)
        self.ask(0)
        self.keys = [1 << p for p in range(chips.bits)]
        self.flying = [chips.send(piece, p) for p in range(chips.bits)]

    def ask(self, v):
        self.chain.ask(self.own[v], self.others, v, self.chips.other)

    def go_on(self, got):
        keys, self.keys, self.flying = self.keys, [], []
        for v, piece in zip(keys, got):
            self.own[v] = piece
            for p in range(v.bit_length(), self.chips.bits):
                self.keys.append(v | 1 << p)
                self.flying.append(self.chips.send(piece, p))
        for v in keys:
            self.ask(v)

    def pieces(self):
        while self.flying:
            self.chain.end(self)
        self.chain.flush()
        return self.own + self.others


class Sums:
    def __init__(self, chips, chain, mine, apart=False, hold=False, cut_in_two=False):
        self.chips, self.chain, self.apart, self.hold = chips, chain, apart, hold
        self.todo = []
        self.cut_in_two = cut_in_two and chips.bits == 2
        self.parts = [mine[0]]
        mine = list(mine[1:])
        self.direct, self.passed = [], []
        for p in range(chips.bits):
            self.direct.append(mine.pop(0))
            self.passed.append(mine.pop(0) if p else None)
        self.p = chips.bits - 1
        if self.cut_in_two:
            self.kinds = [0, 1]
            self.flying = [chips.send(half, 1) for half in self.in_two(self.passed[1])]
            return
        self.kinds = [self.p]
        self.flying = [chips.send(self.passed[self.p], self.p)]

    def in_two(self, values):
        width = values.shape[1] // 2
        return values[:, :width], values[:, width:]

    def go_on(self, got):
        rows = self.parts[0].shape[0]
        kinds, self.kinds, self.flying = self.kinds, [], []
        if self.p == 0:
            self.parts += got
            return
        if self.cut_in_two:
            self.p = 0
            total = self.direct[0].astype(F32) + jnp.concatenate(got, axis=1).astype(F32)
            self.todo = [(None, self.direct[1], 1), (None, total.astype(BF16), 0)]
            self.resume()
            return
        for kind, block in zip(kinds, got):
            if kind is None:
                self.parts.append(block)
                continue
            add = lambda held, first: (
                held.astype(F32) + block[first * rows : first * rows + held.shape[0]].astype(F32)
            ).astype(BF16)
            for q in range(kind):
                self.direct[q] = add(self.direct[q], (1 << q) - 1)
                if q:
                    self.passed[q] = add(self.passed[q], 1 << q)
        p, self.p = self.p, self.p - 1
        if p > 0:
            self.todo.append((None, self.direct[p], p))
        if p > 1:
            self.todo.append((p - 1, self.passed[p - 1], p - 1))
        if p == 1 and not self.apart:
            self.todo.append((None, self.direct[0], 0))
        if not self.hold:
            self.resume()

    def resume(self):
        todo, self.todo = self.todo, []
        values = self.chain.join(*[value for _, value, _ in todo])
        for (kind, _, p), value in zip(todo, values):
            self.kinds.append(kind)
            self.flying.append(self.chips.send(value, p))

    def send_half(self, i):
        while self.p > 0:
            self.chain.end(self)
        width = self.direct[0].shape[1] // 2
        (value,) = self.chain.join(self.direct[0][:, i * width : (i + 1) * width])
        self.kinds.append(None)
        self.flying.append(self.chips.send(value, 0))

    def terms(self):
        while self.flying or self.todo:
            if self.todo:
                self.resume()
            self.chain.end(self)
        return sorted(self.parts, key=lambda part: -part.shape[1])


class Group:
    def __init__(self, links, axes):
        self.links, self.axes = links, axes
        self.bits = len(links)
        self.size = 1 << self.bits
        self.orders = (list(range(self.bits)), list(range(self.bits))[::-1])

    def send(self, value, bit):
        return lax.ppermute(value, self.axes, self.links[bit])

    def messages(self):
        found = []
        for order in self.orders:
            found.append([])
            for top in reversed(range(self.bits)):
                found[-1].append(
                    [
                        1 << order[top] | sum(1 << order[p] for p in range(top) if v >> p & 1)
                        for v in range(1 << top)
                    ]
                )
        return found


class Spread:
    def __init__(self, group, chain, rows):
        self.group, self.chain = group, chain
        self.held = {0: [rows]}
        self.later = None
        self.keys = [(1 << b, None) for b in range(group.bits)]
        self.flying = [group.send(rows, b) for b in range(group.bits)]

    def go_on(self, got):
        fresh = list(zip(self.keys, got))
        self.keys, self.flying = [], []
        for (k, h), block in fresh:
            if h is None:
                self.held[k] = [block]
            else:
                self.held.setdefault(k, [None, None])[h] = block
        for (k, h), block in fresh:
            for way, order in enumerate(self.group.orders):
                if h is not None and h != way:
                    continue
                half = block.shape[1] // 2
                top = max(i for i, bit in enumerate(order) if k >> bit & 1)
                for i in range(top + 1, len(order)):
                    part = block if h is not None else block[:, way * half : (way + 1) * half]
                    self.keys.append((k | 1 << order[i], way))
                    if self.later is not None:
                        self.later.append((part, order[i]))
                    else:
                        self.flying.append(self.group.send(part, order[i]))

        if self.later:
            parts = self.chain.join(*[part for part, _ in self.later])
            self.later = [(part, bit) for part, (_, bit) in zip(parts, self.later)]

    def resume(self):
        later, self.later = self.later, None
        parts = self.chain.join(*[part for part, _ in later])
        self.flying = [self.group.send(part, bit) for part, (_, bit) in zip(parts, later)]

    def blocks(self):
        while self.flying:
            self.chain.end(self)
        return [self.held[k] for k in range(self.group.size)]


class Fold:
    def __init__(self, group, chain, own, sent):
        self.group, self.chain = group, chain
        self.rows = own[0].shape[0]
        self.sent = [list(half) for half in sent]
        self.parts = [[half] for half in own]
        self.wave = 0
        self.start()

    def start(self):
        self.flying = [
            self.group.send(self.sent[h][self.wave], order[self.group.bits - 1 - self.wave])
            for h, order in enumerate(self.group.orders)
        ]

    def go_on(self, got):
        self.wave += 1
        self.flying = []
        for h, block in enumerate(got):
            self.parts[h].append(block)
        for wave in range(self.wave, self.group.bits):
            sums = add_rows(self.chain, [sent[wave] for sent in self.sent], got)
            for sent, value in zip(self.sent, sums):
                sent[wave] = value
        if self.wave < self.group.bits:
            self.start()

    def total(self):
        while self.flying:
            self.chain.end(self)
        return self.parts


class Weight:
    def __init__(self, pieces, rows, start, width):
        self.pieces, self.rows, self.start, self.width = pieces, rows, start, width
        self.model = len(pieces) * rows

    def tiles(self, tile):
        first = self.start // tile
        return [pl.BlockSpec((self.rows, tile), lambda j: (0, first + j))] * len(self.pieces)


def nn(left, right):
    return lax.dot_general(left, right, (((1,), (0,)), ((), ())), preferred_element_type=F32)


def nt(left, right):
    return lax.dot_general(left, right, (((1,), (1,)), ((), ())), preferred_element_type=F32)


def tn(left, right):
    return lax.dot_general(left, right, (((0,), (0,)), ((), ())), preferred_element_type=F32)


def whole(shape):
    return pl.BlockSpec(shape, lambda *_: (0,) * len(shape))


def place(line_ref, j, width):
    return pl.ds(pl.multiple_of(line_ref[j] * width, 128), width)


def cut(width, j):
    return slice(j * width, (j + 1) * width)


def scale_of(values):
    return lax.rsqrt(jnp.mean(values * values, axis=-1, keepdims=True) + EPS)


def fetch_blocks(counts, refs, held, sems, k, slot, wait):
    first = 0
    for i, count in enumerate(counts):
        copies = []
        half = held.shape[2] // count
        for h in range(count):
            target = held.at[slot, :, pl.ds(h * half, half)]
            copies.append(pltpu.make_async_copy(refs[first + h], target, sems.at[slot, h]))
        first += count

        @pl.when(k == i)
        def _():
            for copy in copies:
                copy.wait() if wait else copy.start()


def fetched(counts, refs, held, sems):
    k = pl.program_id(0)

    @pl.when(k == 0)
    def _():
        fetch_blocks(counts, refs, held, sems, k, 0, False)

    fetch_blocks(counts, refs, held, sems, k + 1, (k + 1) % 2, False)
    fetch_blocks(counts, refs, held, sems, k, k % 2, True)
    return held.at[k % 2]


def norm_body(blocks, counts, line_ref, gain_ref, *refs):
    out_ref, held, sems = refs[sum(counts) :]
    x_ref = fetched(counts, refs, held, sems)
    width = out_ref.shape[1] // blocks
    scale = scale_of(x_ref[...].astype(F32))
    for j in range(blocks):
        part = x_ref[:, place(line_ref, j, width)].astype(F32)
        gain = gain_ref[0:1, cut(width, j)]
        out_ref[:, cut(width, j)] = (part * scale * gain).astype(BF16)


def order_body(blocks, counts, line_ref, gain_ref, *refs):
    out_ref, held, sems = refs[sum(counts) :]
    x_ref = fetched(counts, refs, held, sems)
    width = out_ref.shape[1] // blocks
    for j in range(blocks):
        out_ref[:, cut(width, j)] = x_ref[:, place(line_ref, j, width)]


def ordered(chain, body, line, gains, held):
    counts = [len(block) for block in held]
    rows, model = held[0][0].shape
    n = len(held)
    return chain.call(
        functools.partial(body, line.shape[0], counts),
        (n,),
        [whole(gains.shape)] + [pl.BlockSpec(memory_space=pl.ANY)] * sum(counts),
        [pl.BlockSpec((rows, model), lambda k, *_: (k, 0))],
        [((n * rows, model), BF16)],
        flops=20 * n * rows * model,
        scratch=[pltpu.VMEM((2, rows, model), BF16), pltpu.SemaphoreType.DMA((2, 2))],
        prefetch=1,
        moved=4 * n * rows * model,
    )(line, gains, *[array for block in held for array in block])[0]


def added(refs, span):
    total = refs[0][span, :].astype(F32)
    for ref in refs[1:]:
        total += ref[span, :].astype(F32)
    return total


def middle_body(blocks, m, line_ref, x_ref, gain_ref, *refs):
    middle_ref, out_ref = refs[2 * m :]
    width = x_ref.shape[1] // blocks
    half = x_ref.shape[1] // 2
    span = slice(None)
    middle_ref[:, :half] = added(refs[:m], span)
    middle_ref[:, half:] = added(refs[m : 2 * m], span)
    for j in range(blocks):
        here = x_ref[:, place(line_ref, j, width)].astype(F32)
        middle_ref[:, cut(width, j)] += here
    middle = middle_ref[...]
    out_ref[...] = (middle * scale_of(middle) * gain_ref[1:2, :]).astype(BF16)


def result_body(blocks, m, line_ref, middle_ref, gain_ref, *refs):
    out_ref = refs[2 * m]
    width = middle_ref.shape[1] // blocks
    span = slice(None)
    total = middle_ref[...] + jnp.concatenate(
        [added(refs[:m], span), added(refs[m : 2 * m], span)], axis=1
    )
    for j in range(blocks):
        out_ref[:, place(line_ref, j, width)] = total[:, cut(width, j)].astype(BF16)


def second_back_body(blocks, m, line_ref, dy_ref, gain_ref, *refs):
    middle_ref, out_ref, low_ref = refs[2 * m :]
    width = dy_ref.shape[1] // blocks
    span = slice(None)
    grad = jnp.concatenate([added(refs[:m], span), added(refs[m : 2 * m], span)], axis=1)
    middle = middle_ref[...]
    scale = scale_of(middle)
    normed = middle * scale
    scaled = grad * gain_ref[1:2, :]
    out_ref[...] = scale * (scaled - normed * jnp.mean(scaled * normed, axis=-1, keepdims=True))
    for j in range(blocks):
        out_ref[:, cut(width, j)] += dy_ref[:, place(line_ref, j, width)].astype(F32)
    low_ref[...] = out_ref[...].astype(BF16)


def first_back_body(blocks, m, line_ref, x_ref, gain_ref, *refs):
    above_ref, out_ref = refs[2 * m :]
    width = x_ref.shape[1] // blocks
    span = slice(None)
    scale = scale_of(x_ref[...].astype(F32))
    normed = jnp.concatenate(
        [x_ref[:, place(line_ref, j, width)].astype(F32) for j in range(blocks)], axis=1
    ) * scale
    grad = jnp.concatenate([added(refs[:m], span), added(refs[m : 2 * m], span)], axis=1)
    scaled = grad * gain_ref[0:1, :]
    back = scale * (scaled - normed * jnp.mean(scaled * normed, axis=-1, keepdims=True))
    total = above_ref[...] + back
    for j in range(blocks):
        out_ref[:, place(line_ref, j, width)] = total[:, cut(width, j)]


def by_rows(chain, body, line, first, gains, parts, more, kinds):
    rows, model = first.shape
    half = model // 2
    tile = min(128, rows)
    row = pl.BlockSpec((tile, model), lambda i, *_: (i, 0))
    slim = pl.BlockSpec((tile, half), lambda i, *_: (i, 0))
    m = len(parts[0])
    return chain.call(
        functools.partial(body, line.shape[0], m),
        (rows // tile,),
        [row, whole(gains.shape)] + [slim] * (2 * m) + [row] * len(more),
        [row] * len(kinds),
        [((rows, model), kind) for kind in kinds],
        flops=20 * rows * model,
        prefetch=1,
        moved=rows * model * (2 * m + 4 * len(kinds)),
    )(line, first, gains, *parts[0], *parts[1], *more)


def add_rows_body(count, *refs):
    for i in range(count):
        total = refs[i][...].astype(F32) + refs[count + i][...].astype(F32)
        refs[2 * count + i][...] = total.astype(BF16)


def add_rows(chain, helds, blocks):
    rows, columns = helds[0].shape
    tile = min(128, rows)
    steps = rows // tile
    count = len(helds)
    here = pl.BlockSpec((tile, columns), lambda i: (i, 0))
    return chain.call(
        functools.partial(add_rows_body, count),
        (steps,),
        [here] * count + [pl.BlockSpec((tile, columns), lambda i: (steps + i, 0))] * count,
        [here] * count,
        [((rows, columns), BF16)] * count,
        flops=count * rows * columns,
        moved=6 * count * rows * columns,
    )(*helds, *blocks)


def finish_body(m, halves, n, *refs):
    total = added(refs[:m], slice(None))
    if halves:
        total += jnp.concatenate([ref[...].astype(F32) for ref in refs[m : m + halves]], axis=1)
    m += halves
    weights, outs = refs[m : m + n], refs[m + n :]
    if not n:
        outs[0][...] = total.T
        return
    width = weights[0].shape[1]
    inner = jnp.zeros((total.shape[0], 1), F32)
    for i in range(n):
        part = total[:, cut(width, i)]
        outs[i][...] = part
        inner += jnp.sum(weights[i][...].astype(F32) * part, axis=1, keepdims=True)
    outs[n][...] = jnp.broadcast_to(inner, outs[n].shape)


def finish(chain, terms, weights=()):
    rows, columns = terms[0].shape
    tile = min(128, rows)
    row = pl.BlockSpec((tile, columns), lambda i: (i, 0))
    n = len(weights)
    halves = sum(1 for term in terms if term.shape[1] < columns)
    half = [pl.BlockSpec((tile, columns // 2), lambda i: (i, 0))] * halves
    if n:
        slim = pl.BlockSpec((tile, columns // n), lambda i: (i, 0))
        outs = [slim] * n + [pl.BlockSpec((tile, 128), lambda i: (i, 0))]
        shapes = [((rows, columns // n), F32)] * n + [((rows, 128), F32)]
    else:
        slim = None
        outs = [pl.BlockSpec((columns, tile), lambda i: (0, i))]
        shapes = [((columns, rows), F32)]
    results = chain.call(
        functools.partial(finish_body, len(terms) - halves, halves, n),
        (rows // tile,),
        [row] * (len(terms) - halves) + half + [slim] * n,
        outs,
        shapes,
        flops=4 * rows * columns,
        moved=rows * columns * 12,
    )(*terms, *weights)
    if n:
        results[n] = results[n][:, 0]
    return results


def rope_tables(place):
    half = HEAD_DIM // 2
    freq = THETA ** (-2.0 * jnp.arange(half, dtype=F32) / HEAD_DIM)
    angle = place.astype(F32)[:, None] * freq[None, :]
    cosine, sine = jnp.cos(angle), jnp.sin(angle)
    return (
        jnp.concatenate([cosine] * (PAIR // half), axis=1),
        jnp.concatenate([-sine, sine] * (PAIR // HEAD_DIM), axis=1),
    )


def turn(values):
    half = HEAD_DIM // 2
    width = values.shape[-1]
    lane = lax.broadcasted_iota(jnp.int32, values.shape, 1) % HEAD_DIM
    return jnp.where(
        lane < half, pltpu.roll(values, width - half, 1), pltpu.roll(values, half, 1)
    )


def joined(refs):
    return jnp.concatenate([r[...] for r in refs], axis=0)


def qkv_body(n, x_ref, cos_ref, sin_ref, *refs):
    weights, outs = refs[: 3 * n], refs[3 * n :]
    rows = x_ref.shape[0]
    tile = outs[0].shape[1]
    for i in range(3):
        weight = joined(weights[i * n : (i + 1) * n])
        for s in range(rows // SEQ):
            span = slice(s * SEQ, (s + 1) * SEQ)
            product = nn(x_ref[span, :], weight)
            if i == 2:
                outs[i][span, :] = product.astype(BF16)
                continue
            for t in range(tile // PAIR):
                here = product[:, t * PAIR : (t + 1) * PAIR]
                turned = here * cos_ref[...] + turn(here) * sin_ref[...]
                outs[i][span, t * PAIR : (t + 1) * PAIR] = turned.astype(BF16)


def project(chain, x, tables, query, key, value):
    rows, model = x.shape
    n, width = len(query.pieces), query.width
    tile = min(256, width)
    out = pl.BlockSpec((rows, tile), lambda j: (0, j))
    return chain.call(
        functools.partial(qkv_body, n),
        (width // tile,),
        [whole(x.shape), whole((SEQ, PAIR)), whole((SEQ, PAIR))]
        + query.tiles(tile)
        + key.tiles(tile)
        + value.tiles(tile),
        [out] * 3,
        [((rows, width), BF16)] * 3,
        flops=6 * rows * model * width,
        moved=2 * (rows * model + 3 * model * width + 3 * rows * width),
    )(x, *tables, *query.pieces, *key.pieces, *value.pieces)


def collect(counts, refs, held, sems):
    rows = held.shape[0] // len(counts)
    copies = []
    for k, count in enumerate(counts):
        half = held.shape[1] // count
        for h in range(count):
            target = held.at[pl.ds(k * rows, rows), pl.ds(h * half, half)]
            i = len(copies)
            copies.append(pltpu.make_async_copy(refs[i], target, sems.at[i]))
    for copy in copies:
        copy.start()
    for copy in copies:
        copy.wait()


def gate_body(n, counts, *refs):
    m = sum(counts)
    gate_w, up_w = refs[m : m + n], refs[m + n : m + 2 * n]
    left_ref, hidden_ref, slope_ref, silu_ref, theirs_ref, x_ref, turned, sems = refs[m + 2 * n :]

    @pl.when(pl.program_id(0) == 0)
    def _():
        collect(counts, refs, x_ref, sems)
        turned[...] = left_ref[...].T

    gate_weight, up_weight = joined(gate_w), joined(up_w)
    for s in range(x_ref.shape[0] // SEQ):
        span = slice(s * SEQ, (s + 1) * SEQ)
        gate = nn(x_ref[span, :], gate_weight)
        up = nn(x_ref[span, :], up_weight)
        sigm = jax.nn.sigmoid(gate)
        silu = gate * sigm
        hidden_ref[span, :] = (silu * up).astype(BF16)
        silu_ref[span, :] = silu.astype(BF16)
        slope_ref[span, :] = (up * sigm * (1.0 + gate * (1.0 - sigm))).astype(BF16)
    theirs_ref[...] = nn(turned[...], hidden_ref[...]).astype(BF16)


def collected(held):
    counts = [len(block) for block in held]
    rows, model = held[0][0].shape
    scratch = [
        pltpu.VMEM((len(held) * rows, model), BF16),
        pltpu.SemaphoreType.DMA((sum(counts),)),
    ]
    arrays = [array for block in held for array in block]
    return counts, arrays, [pl.BlockSpec(memory_space=pl.ANY)] * len(arrays), scratch


def gate_up(chain, held, gate, up, grads):
    counts, arrays, specs, scratch = collected(held)
    rows, model = scratch[0].shape
    n, width = len(gate.pieces), gate.width
    tile = min(256, width)
    out = pl.BlockSpec((rows, tile), lambda j: (0, j))
    half = model // 2
    return chain.call(
        functools.partial(gate_body, n, counts),
        (width // tile,),
        specs
        + gate.tiles(tile)
        + up.tiles(tile)
        + [pl.BlockSpec((rows, half), lambda j: (0, 1))],
        [out] * 3 + [pl.BlockSpec((half, tile), lambda j: (0, j))],
        [((rows, width), BF16)] * 3 + [((half, width), BF16)],
        flops=6 * rows * model * width,
        scratch=[scratch[0], pltpu.VMEM((half, rows), BF16), scratch[1]],
        moved=2 * (rows * model + 2 * model * width + 3 * rows * width),
    )(*arrays, *gate.pieces, *up.pieces, grads)


def half_blocks(left, which):
    lefts = [block[0] if len(block) == 1 else block[which] for block in left]
    rows, half = lefts[0].shape[0], left[0][0].shape[1] // 2
    places = [which if len(block) == 1 else 0 for block in left]
    return lefts, [
        pl.BlockSpec((rows, half), functools.partial(lambda at, j: (0, at), at)) for at in places
    ]


def hidden_back_body(n, blocks, g_ref, *refs):
    weights, slope_ref, silu_ref = refs[:n], refs[n], refs[n + 1]
    lefts, refs = refs[n + 2 : n + 2 + blocks], refs[n + 2 + blocks :]
    gate_ref, up_ref, theirs_ref, turned = refs
    rows = turned.shape[1] // blocks

    @pl.when(pl.program_id(0) == 0)
    def _():
        for k in range(blocks):
            turned[:, cut(rows, k)] = lefts[k][...].T

    weight = joined(weights)
    for s in range(g_ref.shape[0] // SEQ):
        span = slice(s * SEQ, (s + 1) * SEQ)
        grad = nn(g_ref[span, :], weight)
        gate_ref[span, :] = (grad * slope_ref[span, :].astype(F32)).astype(BF16)
        up_ref[span, :] = (grad * silu_ref[span, :].astype(F32)).astype(BF16)
    theirs_ref[...] = nn(turned[...], gate_ref[...]).astype(BF16)


def hidden_back(chain, grads, down, slope, silu, left):
    rows, model = grads.shape
    n, width = len(down.pieces), down.width
    tile = min(256, width)
    out = pl.BlockSpec((rows, tile), lambda j: (0, j))
    lefts, specs = half_blocks(left, 1)
    half = model // 2
    return chain.call(
        functools.partial(hidden_back_body, n, len(lefts)),
        (width // tile,),
        [whole(grads.shape)] + down.tiles(tile) + [out] * 2 + specs,
        [out] * 2 + [pl.BlockSpec((half, tile), lambda j: (0, j))],
        [((rows, width), BF16)] * 2 + [((half, width), BF16)],
        flops=3 * rows * model * width,
        scratch=[pltpu.VMEM((half, rows), BF16)],
        moved=2 * (rows * model + model * width + 4 * rows * width),
    )(grads, *down.pieces, slope, silu, *lefts)


def mixed_back_body(n, counts, *refs):
    m = sum(counts)
    out_ref, x_ref, sems = refs[m + n :]
    rows = x_ref.shape[0] // len(counts)
    blocks, i = [], 0
    for k, count in enumerate(counts):
        half = x_ref.shape[1] // count
        blocks.append([])
        for h in range(count):
            target = x_ref.at[pl.ds(k * rows, rows), pl.ds(h * half, half)]
            blocks[-1].append(pltpu.make_async_copy(refs[i], target, sems.at[i]))
            blocks[-1][-1].start()
            i += 1
    weight = joined(refs[m : m + n])
    for k, copies in enumerate(blocks):
        for copy in copies:
            copy.wait()
        out_ref[cut(rows, k), :] = nn(x_ref[cut(rows, k), :], weight).astype(BF16)


def mixed_back(chain, held, out):
    counts, arrays, specs, scratch = collected(held)
    rows, model = scratch[0].shape
    n, width = len(out.pieces), out.width
    return chain.call(
        functools.partial(mixed_back_body, n, counts),
        (1,),
        specs + out.tiles(width),
        [whole((rows, width))],
        [((rows, width), BF16)],
        flops=2 * rows * model * width,
        scratch=scratch,
        moved=2 * (rows * model + model * width + rows * width),
    )(*arrays, *out.pieces)[0]


def trans_body(n, starts, targets, chunks, *refs):
    parts, blocks = len(starts), len(targets[0])
    arrays = refs[:parts]
    pieces, outs = refs[parts : parts * (n + 1)], refs[parts * (n + 1) : -6]
    lefts, held, ready, left_sems, sems, out_sems = refs[-6:]
    j = pl.program_id(0)
    depth, width = held.shape[2:]
    rows = ready.shape[1] // blocks
    chunk = width // chunks

    def left_copy(p, c):
        span = pl.ds(c * chunk, chunk)
        return pltpu.make_async_copy(
            arrays[p].at[:, span], lefts.at[p, :, span], left_sems.at[p, c]
        )

    def copy(i, p, slot):
        source = pieces[p * n + i].at[pl.ds(0, depth), pl.ds(starts[p], width)]
        return pltpu.make_async_copy(source, held.at[slot, p], sems.at[slot, p])

    def fetch(step, slot):
        for i in range(n):

            @pl.when(step == i)
            def _():
                for p in range(parts):
                    copy(i, p, slot).start()

    def leave(slot, k, array, first, column):
        target = outs[array].at[pl.ds(first, rows), pl.ds(column, depth)]
        source = ready.at[slot, pl.ds(k * rows, rows), :]
        return pltpu.make_async_copy(source, target, out_sems.at[slot, k])

    def left(slot):
        for k in range(blocks):
            leave(slot, k, 0, 0, 0).wait()

    @pl.when(j == 0)
    def _():
        fetch(j, 0)
        for c in range(chunks):
            for p in range(parts):
                left_copy(p, c).start()

    @pl.when(j + 1 < n)
    def _():
        fetch(j + 1, (j + 1) % 2)

    slot = j % 2
    for p in range(parts):
        copy(0, p, slot).wait()

    @pl.when(j >= 2)
    def _():
        left(slot)

    spans = [slice(s * SEQ, (s + 1) * SEQ) for s in range(blocks * rows // SEQ)]

    @pl.when(j == 0)
    def _():
        totals = [None] * len(spans)
        for c in range(chunks):
            for p in range(parts):
                left_copy(p, c).wait()
                for s, span in enumerate(spans):
                    part = nt(lefts[p, span, cut(chunk, c)], held[0, p, :, cut(chunk, c)])
                    totals[s] = part if totals[s] is None else totals[s] + part
        for total, span in zip(totals, spans):
            ready[0, span, :] = total.astype(BF16)

    @pl.when(j > 0)
    def _():
        for span in spans:
            total = nt(lefts[0, span, :], held[slot, 0])
            for p in range(1, parts):
                total += nt(lefts[p, span, :], held[slot, p])
            ready[slot, span, :] = total.astype(BF16)

    column = pl.multiple_of(j % (n // 2) * depth, 128)
    for h in range(2):

        @pl.when((j >= n // 2) == (h == 1))
        def _():
            for k, (array, first) in enumerate(targets[h]):
                leave(slot, k, array, first, column).start()

    @pl.when(j == n - 1)
    def _():
        left(1 - slot)
        left(slot)


def times_trans(chain, parts, group):
    weights = [weight for _, weight in parts]
    n, depth, width = len(weights[0].pieces), weights[0].rows, weights[0].width
    rows = parts[0][0].shape[0]
    half = weights[0].model // 2
    size = rows // group.size
    messages = group.messages()
    shapes = [((size, half), BF16)] * 2
    targets = [{0: (0, 0)}, {0: (1, 0)}]
    for h in range(2):
        for keys in messages[h]:
            for i, k in enumerate(keys):
                targets[h][k] = (len(shapes), i * size)
            shapes.append(((len(keys) * size, half), BF16))
    targets = [[t[k] for k in range(group.size)] for t in targets]
    anywhere = pl.BlockSpec(memory_space=pl.ANY)
    chunks = max(1, width // 512)
    outs = chain.call(
        functools.partial(trans_body, n, [weight.start for weight in weights], targets, chunks),
        (n,),
        [anywhere] * ((n + 1) * len(parts)),
        [anywhere] * len(shapes),
        shapes,
        flops=4 * rows * half * width * len(parts),
        scratch=[
            pltpu.VMEM((len(parts), rows, width), BF16),
            pltpu.VMEM((2, len(parts), depth, width), BF16),
            pltpu.VMEM((2, rows, depth), BF16),
            pltpu.SemaphoreType.DMA((len(parts), chunks)),
            pltpu.SemaphoreType.DMA((2, len(parts))),
            pltpu.SemaphoreType.DMA((2, group.size)),
        ],
        moved=2 * (2 * rows * half + len(parts) * (rows + 2 * half) * width),
    )(*[left for left, _ in parts], *[piece for weight in weights for piece in weight.pieces])
    m = group.bits
    return outs[:2], [outs[2 : 2 + m], outs[2 + m :]]


def grad_body(parts, got, blocks, steps, *refs):
    lefts, refs = refs[:blocks], refs[blocks:]
    rights, refs = refs[:parts], refs[parts:]
    got_ref = refs[0] if got else None
    outs, turned = refs[got:-1], refs[-1]
    j = pl.program_id(0)

    @pl.when(j == 0)
    def _():
        rows = turned.shape[1] // blocks
        for k in range(blocks):
            turned[:, cut(rows, k)] = lefts[k][...].T

    for i in range(parts):

        @pl.when((j >= i * steps) & (j < (i + 1) * steps))
        def _():
            total = nn(turned[...], rights[i][...])
            if got:
                total += got_ref[...].astype(F32)
            total = total.astype(BF16)
            first = 0
            for out_ref in outs:
                count = out_ref.shape[0]
                out_ref[...] = total[first : first + count]
                first += count


def weight_grads(chain, left, which, rights, got=None, bits=0):
    rows, width = rights[0].shape
    parts = len(rights)
    tile = min(512, width)
    steps = width // tile
    lefts, ins = half_blocks(left if isinstance(left, list) else [[left]], which)
    blocks, half = len(lefts), ins[0].block_shape[1]
    for i in range(parts):
        ins.append(
            pl.BlockSpec(
                (rows, tile),
                functools.partial(
                    lambda first, j: (0, jnp.clip(j - first, 0, steps - 1)), i * steps
                ),
            )
        )
    column = lambda j: (0, j)
    more = [] if got is None else [got]
    sizes = [half >> bits]
    for p in range(bits):
        sizes += [sizes[0], ((1 << p) - 1) * sizes[0]] if p else [sizes[0]]
    return chain.call(
        functools.partial(grad_body, parts, len(more), blocks, steps),
        (parts * steps,),
        ins + [pl.BlockSpec((half, tile), column)] * len(more),
        [pl.BlockSpec((size, tile), column) for size in sizes],
        [((size, parts * width), BF16) for size in sizes],
        flops=2 * rows * half * width * parts,
        scratch=[pltpu.VMEM((half, rows), BF16)],
        moved=2 * (rows * half + parts * (rows + half) * width),
    )(*lefts, *rights, *more)


def causal(scores):
    past = scores.shape[0] - HALF_SEQ
    key = lax.broadcasted_iota(jnp.int32, (HALF_SEQ, HALF_SEQ), 0)
    query = lax.broadcasted_iota(jnp.int32, (HALF_SEQ, HALF_SEQ), 1)
    last = jnp.where(key <= query, scores[past:], -1e30)
    return last if past == 0 else jnp.concatenate([scores[:past], last], axis=0)


def head_of(h):
    return slice(h * HEAD_DIM, (h + 1) * HEAD_DIM)


def span_of(b):
    return slice(b * HALF_SEQ, (b + 1) * HALF_SEQ)


def in_place(shift_ref, ref, count):
    rows = SEQ // count
    spans = [pl.ds(pl.multiple_of((i ^ shift_ref[0]) * rows, rows), rows) for i in range(count)]
    return jnp.concatenate([ref[span, :] for span in spans], axis=0)


def put_back(shift_ref, ref, count, values):
    rows = SEQ // count
    for i in range(count):
        ref[pl.ds(pl.multiple_of((i ^ shift_ref[0]) * rows, rows), rows), :] = values[cut(rows, i)]


def one_head(values, h):
    lane = lax.broadcasted_iota(jnp.int32, values.shape, 1)
    return jnp.where(lane // HEAD_DIM == h, values, jnp.zeros_like(values))


def attend_body(count, shift_ref, q_ref, k_ref, v_ref, out_ref, sum_ref):
    queries, keys = in_place(shift_ref, q_ref, count), in_place(shift_ref, k_ref, count)
    values = in_place(shift_ref, v_ref, count).astype(F32).T.astype(BF16)
    heads = []
    for h in range(q_ref.shape[1] // HEAD_DIM):
        blocks = []
        for b in range(2):
            reach = (b + 1) * HALF_SEQ
            query = one_head(queries[span_of(b)] * BF16(FACTOR), h)
            scores = causal(nt(keys[:reach], query))
            top = jnp.max(scores, axis=0, keepdims=True)
            expo = jnp.exp(scores - top)
            total = jnp.sum(expo, axis=0, keepdims=True)
            mixed = nn(values[head_of(h), :reach], expo.astype(BF16))
            blocks.append(mixed * (1.0 / total))
            sum_ref[0, h, :, span_of(b)] = top + jnp.log(total)
        heads.append(jnp.concatenate(blocks, axis=1))
    put_back(shift_ref, out_ref, count, jnp.concatenate(heads, axis=0).T.astype(BF16))


def attention_specs(rows, width, wide):
    wide = min(wide, width)
    tile = pl.BlockSpec((SEQ, wide), lambda s, p, _: (s, p))
    sums = pl.BlockSpec((1, wide // HEAD_DIM, 1, SEQ), lambda s, p, _: (s, p, 0, 0))
    return (rows // SEQ, width // wide), tile, sums


def attend(chain, shift, count, query, key, value):
    rows, width = query.shape
    grid, tile, sums = attention_specs(rows, width, 256)
    return chain.call(
        functools.partial(attend_body, count),
        grid,
        [tile] * 3,
        [tile, sums],
        [((rows, width), BF16), ((rows // SEQ, width // HEAD_DIM, 1, SEQ), F32)],
        flops=16 * rows * width * SEQ,
        prefetch=1,
        moved=8 * rows * width,
    )(shift, query, key, value)


def attend_back_body(
    count, shift_ref, q_ref, k_ref, v_ref, g_ref, sum_ref, cos_ref, sin_ref, dq_ref, dk_ref, dv_ref
):
    queries, keys, values, grads = (
        in_place(shift_ref, ref, count) for ref in (q_ref, k_ref, v_ref, g_ref)
    )
    turned = keys.astype(F32).T.astype(BF16)
    dq_heads = []
    dk, dv = [], []
    for b in range(2):
        reach = (b + 1) * HALF_SEQ
        dq, dk_sum, dv_sum = [], None, None
        for h in range(q_ref.shape[1] // HEAD_DIM):
            query = one_head(queries[span_of(b)], h)
            grad = one_head(grads[span_of(b)], h)
            scores = causal(nt(keys[:reach], query * BF16(FACTOR)))
            probs = jnp.exp(scores - sum_ref[0, h, :, span_of(b)])
            probs_grad = nt(values[:reach], grad)
            inner = jnp.sum(probs * probs_grad, axis=0, keepdims=True)
            score_grad = (probs * (probs_grad - inner)).astype(BF16)
            dv_part, dk_part = nn(probs.astype(BF16), grad), nn(score_grad, query)
            dv_sum = dv_part if dv_sum is None else dv_sum + dv_part
            dk_sum = dk_part if dk_sum is None else dk_sum + dk_part
            dq.append(nn(turned[head_of(h), :reach], score_grad))
        dq_heads.append(jnp.concatenate(dq, axis=0))
        dk.append(dk_sum)
        dv.append(dv_sum)

    def whole_rows(parts):
        early, late = parts
        return jnp.concatenate([late[:HALF_SEQ] + early, late[HALF_SEQ:]], axis=0)

    dq = jnp.concatenate(dq_heads, axis=1).T * FACTOR
    dk = whole_rows(dk) * FACTOR
    dv = whole_rows(dv).astype(BF16)
    copies = dq.shape[1] // PAIR
    cosine = jnp.concatenate([cos_ref[...]] * copies, axis=1)
    sine = jnp.concatenate([sin_ref[...]] * copies, axis=1)
    put_back(shift_ref, dq_ref, count, (dq * cosine - turn(dq) * sine).astype(BF16))
    put_back(shift_ref, dk_ref, count, (dk * cosine - turn(dk) * sine).astype(BF16))
    put_back(shift_ref, dv_ref, count, dv)


def attend_back(chain, shift, count, query, key, value, grad, logsum, tables):
    rows, width = query.shape
    grid, tile, sums = attention_specs(rows, width, PAIR)
    return chain.call(
        functools.partial(attend_back_body, count),
        grid,
        [tile] * 4 + [sums] + [whole((SEQ, PAIR))] * 2,
        [tile] * 3,
        [((rows, width), BF16)] * 3,
        flops=40 * rows * width * SEQ,
        prefetch=1,
        moved=14 * rows * width,
    )(shift, query, key, value, grad, logsum, *tables)


def local(
    chips,
    group,
    tokens,
    attn_gain,
    query_weight,
    key_weight,
    value_weight,
    output_weight,
    ffn_gain,
    gate_weight,
    up_weight,
    down_weight,
    cotangent,
):
    line = jnp.asarray(chips.table)[lax.axis_index("dp")]
    rows, model = tokens.shape
    count = SEQ // rows
    shift = lax.axis_index("tensor") % count
    row = jnp.arange(SEQ, dtype=jnp.int32)
    places = rope_tables(row)
    tables = rope_tables((row // rows ^ shift) * rows + row % rows)
    shift = jnp.reshape(shift, (1,)).astype(jnp.int32)
    early = (*places, *tables, line, shift)
    depth, own = query_weight.shape
    hidden_units = gate_weight.shape[1]
    chain = Chain()

    def gather(piece):
        return Gather(chips, chain, chain.join(piece)[0])

    def spread_of(values):
        return Spread(group, chain, chain.join(values)[0])

    def fold_of(part):
        own_part, sent = part
        sent = chain.join(*sent[0], *sent[1])
        return Fold(group, chain, own_part, [sent[: group.bits], sent[group.bits :]])

    def grads_of(left, rights, theirs=None):
        if theirs is None:
            (theirs,) = weight_grads(chain, left, 1, rights)
        got = [None]
        chain.ask(theirs, got, 0, chips.other)

        def mine(**how):
            if got[0] is None:
                chain.flush()
            blocks = weight_grads(chain, left, 0, rights, got[0], chips.bits)
            return Sums(chips, chain, blocks, **how)

        return mine

    extra = jnp.concatenate([attn_gain, ffn_gain, jnp.zeros((4 * own - 2 * depth,), BF16)])
    attn = jnp.concatenate([query_weight, key_weight, value_weight, output_weight.T], axis=1)
    attn = gather(jnp.concatenate([attn, jnp.broadcast_to(extra, (16, 4 * own))], axis=0))
    spread = spread_of(tokens)
    grads_spread = spread_of(cotangent)
    grads_spread.later = []
    down_turned, *early = chain.join(down_weight.T, *early)
    places, tables, line, shift = early[:2], early[2:4], early[4], early[5]
    chain.end(attn, spread, grads_spread)
    chain.end(attn, spread)
    all_tokens = spread.blocks()
    attn = attn.pieces()
    pair = gather(jnp.concatenate([gate_weight, up_weight], axis=1))
    w_query, w_key, w_value, w_output = [Weight(attn, depth, i * own, own) for i in range(4)]
    gains = jnp.concatenate(
        [piece[depth : depth + 1, : 2 * depth].reshape(2, depth) for piece in attn], axis=1
    ).astype(F32)

    group_one = ordered(chain, norm_body, line, gains, all_tokens)
    grads_spread.resume()
    query, key, value = project(chain, group_one, tables, w_query, w_key, w_value)
    mixed, logsum = attend(chain, shift, count, query, key, value)
    out_part = times_trans(chain, [(mixed, w_output)], group)
    fold = fold_of(out_part)
    chain.end(fold, pair, grads_spread)
    grad_rows = ordered(chain, order_body, line, gains, grads_spread.blocks())
    chain.end(fold)
    attended = fold.total()
    middle, second = by_rows(
        chain, middle_body, line, tokens, gains, attended, [], [F32, BF16]
    )
    spread = spread_of(second)
    chain.end(spread, pair)
    pair = pair.pieces()
    down = gather(down_turned)
    chain.end(spread)
    group_two = spread.blocks()
    w_gate = Weight(pair, depth, 0, hidden_units)
    w_up = Weight(pair, depth, hidden_units, hidden_units)
    hidden, slope, silu, theirs = gate_up(chain, group_two, w_gate, w_up, grad_rows)

    mine = grads_of(grad_rows, [hidden], theirs)
    chain.end(down)
    chain.flush()
    down_sum = mine()
    w_down = Weight(down.pieces(), depth, 0, hidden_units)
    gate_grad, up_grad, gate_theirs = hidden_back(
        chain, grad_rows, w_down, slope, silu, group_two
    )
    mine_gate = grads_of(group_two, [gate_grad], gate_theirs)
    chain.end(down_sum)
    second_part = times_trans(chain, [(gate_grad, w_gate), (up_grad, w_up)], group)
    fold = fold_of(second_part)
    gate_sum = mine_gate(hold=True)
    (up_theirs,) = weight_grads(chain, group_two, 1, [up_grad])
    chain.end(down_sum)
    mine_up = grads_of(group_two, [up_grad], up_theirs)
    chain.end(fold)
    up_sum = mine_up(hold=True)
    chain.end(fold)
    second_grad = fold.total()
    middle_grad, low_grad = by_rows(
        chain, second_back_body, line, cotangent, gains, second_grad, [middle], [F32, BF16]
    )
    spread = spread_of(low_grad)
    chain.end(gate_sum)
    gate_sum.resume()
    result_part = times_trans(chain, [(hidden, w_down)], group)
    chain.end(spread)
    (down_sum,) = finish(chain, down_sum.terms())
    chain.end(spread)
    attn_grads = spread.blocks()

    mixed_grad = mixed_back(chain, attn_grads, w_output)
    query_back, key_back, value_back = attend_back(
        chain, shift, count, query, key, value, mixed_grad, logsum, places
    )
    mine_qkv = grads_of(group_one, [query_back, key_back, value_back])
    mine_out = grads_of(attn_grads, [mixed])
    chain.end(gate_sum, up_sum)
    up_sum.resume()
    fold = fold_of(result_part)
    qkv_sum = mine_qkv()
    first_part = times_trans(
        chain, [(query_back, w_query), (key_back, w_key), (value_back, w_value)], group
    )
    out_sum = mine_out(hold=True)
    chain.end(fold)
    gate_sum, gate_inner = finish(chain, gate_sum.terms(), [gate_weight])
    chain.end(fold)
    result_part = fold.total()
    (layer_out,) = by_rows(chain, result_body, line, middle, gains, result_part, [], [BF16])
    fold = fold_of(first_part)
    chain.end(up_sum, out_sum)
    chain.end(qkv_sum)
    out_sum.resume()
    up_sum, up_inner = finish(chain, up_sum.terms(), [up_weight])
    chain.end(fold)
    chain.end(fold)
    first_grad = fold.total()
    (input_grad,) = by_rows(
        chain, first_back_body, line, tokens, gains, first_grad, [middle_grad], [F32]
    )
    chain.end(qkv_sum)
    query_sum, key_sum, value_sum, qkv_inner = finish(
        chain, qkv_sum.terms(), [query_weight, key_weight, value_weight]
    )
    gain_parts = jnp.stack(
        [qkv_inner / attn_gain.astype(F32), (gate_inner + up_inner) / ffn_gain.astype(F32)]
    )
    (gain_parts,) = chain.join(gain_parts)
    (out_sum,) = finish(chain, out_sum.terms())
    gain_totals = gain_parts
    for k in range(1, group.size):
        pairs = [(i, i ^ k) for i in range(group.size)]
        gain_totals += lax.ppermute(gain_parts, "tensor", pairs)
    gain_one_total, gain_two_total = gain_totals[0], gain_totals[1]
    return (
        layer_out,
        input_grad,
        gain_one_total,
        query_sum,
        key_sum,
        value_sum,
        out_sum,
        gain_two_total,
        gate_sum,
        up_sum,
        down_sum,
    )


def solution(mesh):
    in_specs = (
        P(("dp", "tensor"), None),
        P("dp"),
        P("dp", "tensor"),
        P("dp", "tensor"),
        P("dp", "tensor"),
        P("tensor", "dp"),
        P("dp"),
        P("dp", "tensor"),
        P("dp", "tensor"),
        P("tensor", "dp"),
        P(("dp", "tensor"), None),
    )
    out_specs = (
        P(("dp", "tensor"), None),
        P(("dp", "tensor"), None),
        P("dp"),
        P("dp", "tensor"),
        P("dp", "tensor"),
        P("dp", "tensor"),
        P("tensor", "dp"),
        P("dp"),
        P("dp", "tensor"),
        P("dp", "tensor"),
        P("tensor", "dp"),
    )
    chips = Chips(mesh.shape["dp"])
    size = mesh.shape["tensor"]
    links = [[(i, i ^ 1 << b) for i in range(size)] for b in range(size.bit_length() - 1)]
    group = Group(links, "tensor")

    def run(*arrays):
        return local(chips, group, *arrays)

    return jax.shard_map(run, mesh=mesh, in_specs=in_specs, out_specs=out_specs, check_vma=False)
```
